32 devices in a mesh: face: 2 (over x), blk: 16 (over z, y, core).
Axes of the slice: x: 2, y: 2, z: 4, core: 2. Of those that a mesh axis runs over, the one named last changes fastest.
Arguments:
- fields: float32 [3, 8, 8, 8192], P(None, None, None, ('face', 'blk')), may hold values from -6 to 6
- jacobian: float32 [8, 8, 8192], P(None, None, ('face', 'blk')), may hold values from 0.6 to 1.6
- water_depth: float32 [8, 8, 8192], P(None, None, ('face', 'blk')), may hold values from 0.4 to 2.5
- coriolis: float32 [8, 8, 8192], P(None, None, ('face', 'blk')), may hold values from -2 to 2
- tide_height: float32 [8, 8, 8192], P(None, None, ('face', 'blk')), may hold values from -4 to 4
- slot_of: int32 [32, 256], P(('face', 'blk')), may hold values from 0 to 255, each once within a row
- seam_rows: int32 [2, 256], replicated, may hold values from 0 to 255, as said below
Outputs:
- stepped: float32 [3, 8, 8, 8192], P(None, None, None, ('face', 'blk'))
The draws below stay inside these ranges and needn't reach their ends.
Inputs may be any that keep to these rules, and one draw needn't show every extreme that they name: For one seam k, drawn, seam_rows[k, y] = y; for the other, seam_rows[k, y] = 255 - y. `slot_of`: each row is a permutation of 0 to 255.
All inputs are finite; a program needn't handle non-finite values.
Results may differ from the reference program's by a relative error of at most 0.00005.
Values sent between devices are 32-bit elements; how exact they have to be, the bound alone decides.
No kernel may reach another device: no remote copies, remote signals or barrier semaphores. Data moves between devices by JAX's collectives and lax.ppermute only.
A program may use at most 64 MiB of HBM per device.

```python
import math
import jax
import jax.numpy as jnp
from jax import lax

NP = 8
BY = 16
GX = 16
GY = 16
E_DEV = 256
NX = 16
NY = 256
ELEMS = 8192
N_FACE = 2
N_BLK = 16


def draw_seam_rows(key, part):
    key = jax.random.fold_in(key, 7)
    which = jax.random.randint(key, (1,), 0, 2)
    reversed_flag = jnp.concatenate([which, 1 - which])[:, None]
    rows_along = jnp.arange(NY, dtype=jnp.int32)[None, :]
    return jnp.where(reversed_flag == 1, NY - 1 - rows_along, rows_along).astype(jnp.int32)


def level_of(stream_key, shape, shards, least, largest):
    def one(dim, blocks):
        draws = jax.random.uniform(jax.random.fold_in(jax.random.fold_in(stream_key, 6), dim), (blocks,), jnp.float32, least / len(shards), largest / len(shards))
        return jnp.repeat(jnp.exp(draws), shape[dim] // blocks).reshape((-1,) + (1,) * (len(shape) - dim - 1))

    level = one(*shards[0])
    for cut in shards[1:]:
        level = level * one(*cut)
    return level


def gaussian(own_key, shape, deviation, bound, cuts=(), kind=jnp.bfloat16):
    gain = level_of(own_key, shape, cuts, -0.22, 0.18) if cuts else 1.0
    values = jax.random.normal(own_key, shape, jnp.float32) * deviation * gain
    return jnp.minimum(jnp.maximum(values, -bound), bound).astype(kind)


def setup_inputs(seed: int = 0) -> dict:
    key_of = jax.random.split(jax.random.key(seed), 8)
    fields = gaussian(key_of[0], (3, NP, NP, ELEMS), 1.0, 6.0, ((3, 32),), jnp.float32)
    jacobian = jnp.clip(jnp.exp(math.log(1.6) - 0.98082923 * jax.random.uniform(key_of[1], (NP, NP, ELEMS), jnp.float32) ** level_of(key_of[1], (NP, NP, ELEMS), ((2, 32),), -0.2, 0.2)), 0.6, 1.6)
    water_depth = jnp.clip(jnp.exp(math.log(2.5) - 1.8325814 * jax.random.uniform(key_of[2], (NP, NP, ELEMS), jnp.float32) ** level_of(key_of[2], (NP, NP, ELEMS), ((2, 32),), -0.2, 0.2)), 0.4, 2.5)
    coriolis = jnp.clip(jax.random.uniform(key_of[3], (NP, NP, ELEMS), jnp.float32, -2.0, 2.0) * level_of(key_of[3], (NP, NP, ELEMS), ((2, 32),), -0.4, 0.0), -2.0, 2.0)
    tide_height = gaussian(key_of[4], (NP, NP, ELEMS), 1.0, 4.0, ((2, 32),), jnp.float32)
    slot_of = jax.vmap(lambda own: jax.random.permutation(own, E_DEV))(jax.random.split(key_of[5], (N_FACE * N_BLK))).reshape((N_FACE * N_BLK, E_DEV)).astype(jnp.int32)
    seam_rows = draw_seam_rows(jax.random.fold_in(key_of[7], 71), 0)
    return {"fields": fields, "jacobian": jacobian, "water_depth": water_depth, "coriolis": coriolis, "tide_height": tide_height, "slot_of": slot_of, "seam_rows": seam_rows}


time_step = 0.03
hyper_coeff = 0.0002

def legendre_pair(location, degree):
    lower_value = 1.0
    upper_value = location
    for polynomial_order in range(2, degree + 1):
        lower_value, upper_value = (upper_value, ((2 * polynomial_order - 1) * location * upper_value - (polynomial_order - 1) * lower_value) / polynomial_order)
    return (lower_value, upper_value)

def gll_tables(points):
    degree = points - 1
    locations = [-math.cos(math.pi * position / degree) for position in range(points)]
    for iteration in range(100):
        updated = []
        for location in locations:
            lower_value, upper_value = legendre_pair(location, degree)
            updated.append(location - (location * upper_value - lower_value) / ((degree + 1) * upper_value))
        locations = updated
    locations[0] = -1.0
    locations[degree] = 1.0
    legendre_at = [legendre_pair(location, degree)[1] for location in locations]
    weights = [2.0 / (degree * (degree + 1) * value * value) for value in legendre_at]
    corner_value = degree * (degree + 1) / 4.0
    derivative = []
    for row_index in range(points):
        row_values = []
        for column_index in range(points):
            if row_index != column_index:
                row_values.append(legendre_at[row_index] / (legendre_at[column_index] * (locations[row_index] - locations[column_index])))
            elif row_index == 0:
                row_values.append(-corner_value)
            elif row_index == degree:
                row_values.append(corner_value)
            else:
                row_values.append(0.0)
        derivative.append(row_values)
    return (jnp.asarray(weights, jnp.float32), jnp.asarray(derivative, jnp.float32))

def along_x(derivative, stacked):
    return jnp.einsum('ai,cijxy->cajxy', derivative, stacked, precision=lax.Precision.HIGHEST)

def along_y(derivative, stacked):
    return jnp.einsum('bj,cijxy->cibxy', derivative, stacked, precision=lax.Precision.HIGHEST)

def seam_parts(seam_rows):
    size_y = seam_rows.shape[1]
    flipped = (seam_rows[:, 1] - seam_rows[:, 0]) % size_y != 1
    inverse = jnp.zeros_like(seam_rows).at[jnp.arange(2)[:, None], seam_rows].set(jnp.broadcast_to(jnp.arange(size_y, dtype=jnp.int32)[None, :], seam_rows.shape))
    return (flipped, inverse)

def orient(values, flipped, flip_signs):
    return jnp.where(flipped, jnp.flip(values, 1) * flip_signs[:, None, None], values)

def x_pass(stacked, flip_signs, seam_rows, flipped, inverse):
    points = stacked.shape[1]
    width_x = stacked.shape[3]
    half_x = width_x // 2
    east_edge = stacked[:, points - 1]
    west_edge = stacked[:, 0]
    partner_east = jnp.roll(west_edge, -1, axis=2)
    partner_west = jnp.roll(east_edge, 1, axis=2)
    seam_zero_east = orient(west_edge[:, :, half_x][..., seam_rows[0]], flipped[0], flip_signs)
    seam_one_east = orient(west_edge[:, :, 0][..., seam_rows[1]], flipped[1], flip_signs)
    seam_zero_west = orient(east_edge[:, :, half_x - 1][..., inverse[0]], flipped[0], flip_signs)
    seam_one_west = orient(east_edge[:, :, width_x - 1][..., inverse[1]], flipped[1], flip_signs)
    partner_east = partner_east.at[:, :, half_x - 1].set(seam_zero_east).at[:, :, width_x - 1].set(seam_one_east)
    partner_west = partner_west.at[:, :, half_x].set(seam_zero_west).at[:, :, 0].set(seam_one_west)
    return stacked.at[:, points - 1].set(east_edge + partner_east).at[:, 0].set(west_edge + partner_west)

def y_pass(stacked):
    points = stacked.shape[1]
    north_edge = stacked[:, :, points - 1]
    south_edge = stacked[:, :, 0]
    partner_north = jnp.concatenate([south_edge[..., 1:], jnp.zeros_like(south_edge[..., :1])], 3)
    partner_south = jnp.concatenate([jnp.zeros_like(north_edge[..., :1]), north_edge[..., :-1]], 3)
    return stacked.at[:, :, points - 1].set(north_edge + partner_north).at[:, :, 0].set(south_edge + partner_south)

def reference(fields, jacobian, water_depth, coriolis, tide_height, slot_of, seam_rows):
    column_x = jnp.arange(N_FACE * NX, dtype=jnp.int32)[:, None]
    column_y = jnp.arange(NY, dtype=jnp.int32)[None, :]
    face_of = column_x // NX
    block_x = column_x % NX // GX
    device_of = face_of * N_BLK + block_x * BY + column_y // GY
    cell_of = column_x % GX * GY + column_y % GY
    column_of = (device_of * E_DEV + slot_of[device_of, cell_of]).astype(jnp.int32)
    weights, derivative = gll_tables(NP)
    area_grid = jacobian[:, :, column_of][None]
    depth_grid = water_depth[:, :, column_of][None]
    spin_grid = coriolis[:, :, column_of][None]
    tide_grid = tide_height[:, :, column_of][None]
    root_area = jnp.sqrt(area_grid)
    mass_grid = (weights[:, None] * weights[None, :])[None, :, :, None, None] * area_grid
    flipped, inverse = seam_parts(seam_rows)
    vector_signs = jnp.array([1.0, 1.0, -1.0], dtype=jnp.float32)
    scalar_signs = jnp.ones((1,), dtype=jnp.float32)

    def edge_sum(stacked, flip_signs):
        return y_pass(x_pass(stacked, flip_signs, seam_rows, flipped, inverse))
    mass_sum = edge_sum(mass_grid, scalar_signs)

    def average(stacked):
        return edge_sum(mass_grid * stacked, vector_signs) / mass_sum

    def tendency(current):
        height_diff = current[0:1] - tide_grid
        slopes_x = along_x(derivative, jnp.concatenate([height_diff, root_area * depth_grid * current[1:2]], 0))
        slopes_y = along_y(derivative, jnp.concatenate([height_diff, root_area * depth_grid * current[2:3]], 0))
        spread = (slopes_x[1:2] + slopes_y[1:2]) / area_grid
        return jnp.concatenate([-spread, -slopes_x[0:1] / root_area + spin_grid * current[2:3], -slopes_y[0:1] / root_area - spin_grid * current[1:2]], 0)

    def laplace(stacked):
        return (along_x(derivative, along_x(derivative, stacked)) + along_y(derivative, along_y(derivative, stacked))) / area_grid
    current = fields[:, :, :, column_of]
    section_one = current + time_step * average(tendency(current))
    section_two = 0.75 * current + 0.25 * (section_one + time_step * average(tendency(section_one)))
    section_three = current / 3.0 + 2.0 / 3.0 * (section_two + time_step * average(tendency(section_two)))
    biharmonic = average(laplace(average(laplace(section_three))))
    stepped = section_three - time_step * hyper_coeff * biharmonic
    return jnp.zeros_like(fields).at[:, :, :, column_of].set(stepped)
```

```python
import functools
import math

import jax
import jax.numpy as jnp
import ml_dtypes
import numpy as np
from jax import lax
from jax.experimental import pallas as pl
from jax.experimental.pallas import tpu as pltpu
from jax.sharding import PartitionSpec as P

BY = 16
GX = 16
GY = 16
NP = 8
NODES = NP * NP
ARRAYS = 7
ROWS = ARRAYS * NODES
EDGE_ROWS = 4 * NP
ALL_ROWS = ROWS + EDGE_ROWS
HALF_ROWS = ALL_ROWS // 2
RING_X = 4
RING_Y = 5
PITCH = GX + 2 * RING_X
MID = GY * PITCH
LANES = 128
EXT = MID + 2 * LANES
LEAD = LANES - RING_Y * PITCH
ELEMENTS = GX * GY

time_step = 0.03
hyper_coeff = 0.0002

f32 = jnp.float32
bf16 = jnp.bfloat16
i32 = jnp.int32


def legendre_pair(location, degree):
    lower_value = 1.0
    upper_value = location
    for polynomial_order in range(2, degree + 1):
        lower_value, upper_value = (
            upper_value,
            (
                (2 * polynomial_order - 1) * location * upper_value
                - (polynomial_order - 1) * lower_value
            )
            / polynomial_order,
        )
    return (lower_value, upper_value)


def gll_tables(points):
    degree = points - 1
    locations = [-math.cos(math.pi * position / degree) for position in range(points)]
    for iteration in range(100):
        updated = []
        for location in locations:
            lower_value, upper_value = legendre_pair(location, degree)
            updated.append(
                location - (location * upper_value - lower_value) / ((degree + 1) * upper_value)
            )
        locations = updated
    locations[0] = -1.0
    locations[degree] = 1.0
    legendre_at = [legendre_pair(location, degree)[1] for location in locations]
    weights = [2.0 / (degree * (degree + 1) * value * value) for value in legendre_at]
    corner_value = degree * (degree + 1) / 4.0
    derivative = []
    for row_index in range(points):
        row_values = []
        for column_index in range(points):
            if row_index != column_index:
                row_values.append(
                    legendre_at[row_index]
                    / (legendre_at[column_index] * (locations[row_index] - locations[column_index]))
                )
            elif row_index == 0:
                row_values.append(-corner_value)
            elif row_index == degree:
                row_values.append(corner_value)
            else:
                row_values.append(0.0)
        derivative.append(row_values)
    return np.asarray(weights, np.float64), np.asarray(derivative, np.float64)


def in_three(matrix):
    high = matrix.astype(ml_dtypes.bfloat16)
    low = (matrix - high.astype(np.float64)).astype(ml_dtypes.bfloat16)
    return np.concatenate([high, high, low], 1)


def operator_table():
    weights, derivative = gll_tables(NP)
    eye = np.eye(NP)
    node_weight = np.outer(weights, weights).reshape(NODES, 1)
    along_x = node_weight * np.kron(derivative, eye)
    along_y = node_weight * np.kron(eye, derivative)
    second = derivative @ derivative
    both = node_weight * (np.kron(second, eye) + np.kron(eye, second))
    table = np.zeros((4 * NODES, 6 * NODES), ml_dtypes.bfloat16)
    table[:NODES, : 3 * NODES] = in_three(along_x)
    table[NODES : 2 * NODES, : 3 * NODES] = in_three(along_y)
    table[2 * NODES : 3 * NODES, : 3 * NODES] = in_three(along_x)
    table[2 * NODES : 3 * NODES, 3 * NODES :] = in_three(along_y)
    table[3 * NODES :, : 3 * NODES] = in_three(both)
    spread = np.broadcast_to(node_weight, (NODES, LANES)).astype(np.float32)
    return table, np.ascontiguousarray(spread)


def lane_tables():
    table = np.zeros((24, MID), np.int32)
    for lane in range(MID):
        row, col = divmod(lane, PITCH)
        x = col - RING_X
        own = 0 <= x < GX
        table[0:8, lane] = x * GY + row if own else -1
        if not own:
            table[8:16, lane] = row * RING_X + (col if x < 0 else x - GX)
        table[16:24, lane] = 0 if own else (1 if x < 0 else 2)
    ext = np.zeros((8, EXT), np.int32)
    for lane in range(EXT):
        row, col = divmod(lane - LEAD, PITCH)
        y = row - RING_Y
        x = col - RING_X
        ext[0, lane] = x in (-RING_X, GX + RING_X - 1)
        ext[1, lane] = y == GY - 1
        ext[2, lane] = y == 0
        ext[3, lane] = 0 <= y < GY and 0 <= x < GX
    return table, ext


def exact_pieces(values):
    high = values.astype(bf16)
    rest = values - high.astype(f32)
    middle = rest.astype(bf16)
    low = (rest - middle.astype(f32)).astype(bf16)
    return high, middle, low


def dot(a, b):
    return jnp.dot(a, b, preferred_element_type=f32)


def dot_other(a, b):
    return lax.dot_general(a, b, (((1,), (1,)), ((), ())), preferred_element_type=f32)


def picked(values, one_hot, product=dot):
    high, middle, low = exact_pieces(values)
    return (product(high, one_hot) + product(middle, one_hot)) + product(low, one_hot)


def as_one_hot(row_of_lane, depth):
    index = lax.broadcasted_iota(i32, (depth, row_of_lane.shape[1]), 0)
    return jnp.where(index == row_of_lane[0:1], 1.0, 0.0).astype(bf16)


def high_low_high(values):
    high = values.astype(bf16)
    low = (values - high.astype(f32)).astype(bf16)
    return [high, low, high]


def by_slot(slot_ref, cell_of_lane):
    slots = jnp.broadcast_to(slot_ref[...], (8, ELEMENTS)).astype(f32).astype(bf16)
    chosen = dot(slots, as_one_hot(cell_of_lane, ELEMENTS))
    chosen = jnp.where(cell_of_lane >= 0, chosen, -1.0)
    index = lax.broadcasted_iota(i32, (ELEMENTS, cell_of_lane.shape[1]), 0).astype(f32)
    return jnp.where(index == chosen[0:1], 1.0, 0.0).astype(bf16)


def stored_rows(fields_ref, others):
    parts = [fields_ref[...].reshape(3 * NODES, ELEMENTS)]
    parts += [ref[...].reshape(NODES, ELEMENTS) for ref in others]
    return jnp.concatenate(parts, 0)


def mass_tendency(table, h, u, v, tide, area_depth, weighted_area, spin):
    p = high_low_high(h - tide)
    slopes = dot(table[: 2 * NODES, : 3 * NODES], jnp.concatenate(p, 0))
    flux = high_low_high(area_depth * u) + high_low_high(area_depth * v)
    spread = dot(table[2 * NODES : 3 * NODES], jnp.concatenate(flux, 0))
    return [
        -spread,
        spin * v - weighted_area * slopes[:NODES],
        -spin * u - weighted_area * slopes[NODES:],
    ]


def seam_flags(seam_ref, block_cols):
    size_y = seam_ref.shape[1]
    face = lax.axis_index("face")
    blk = lax.axis_index("blk")
    block_x = blk // BY

    def flipped(k):
        return jnp.where(lax.rem(seam_ref[k, 1] - seam_ref[k, 0] + size_y, size_y) != 1, 1, 0)

    first, second = flipped(0), flipped(1)
    east_flip = jnp.where(face == 0, first, second)
    west_flip = jnp.where(face == 0, second, first)
    if block_cols == 1:
        return 1 - east_flip, 0, east_flip, 1
    at_east = jnp.where(block_x == block_cols - 1, east_flip, 0)
    at_west = jnp.where(block_x == 0, west_flip, 0)
    return 1, at_east, 0, at_west


def strips_kernel(
    block_cols, seam_ref, slot_ref, fields_ref, area_ref, depth_ref, spin_ref, tide_ref,
    table_ref, weight_ref, out0_ref, out1_ref,
):
    east0, flip0, east1, flip1 = seam_flags(seam_ref, block_cols)
    lane = lax.broadcasted_iota(i32, (8, 2 * LANES), 1)
    second = (lane & 64) != 0
    place = lane & 63
    row = place >> 2
    row = jnp.where(jnp.where(second, flip1, flip0) != 0, GY - 1 - row, row)
    east = jnp.where(second, east1, east0) != 0
    col = jnp.where(east, GX - RING_X, 0) + (place & 3)
    col = jnp.where(lane >= LANES, jnp.where(east, GX - RING_X - 1, RING_X), col)
    one_hot = by_slot(slot_ref, col * GY + row)
    stored = stored_rows(fields_ref, (area_ref, depth_ref, spin_ref, tide_ref))
    both = picked(stored, one_hot)

    lane = lax.broadcasted_iota(i32, (1, LANES), 1)
    second = lane >= 64
    flip = jnp.where(second, flip1, flip0) != 0
    sign = jnp.where(flip, -1.0, 1.0)
    node = lax.broadcasted_iota(i32, (1, NP, 1), 1)

    def in_frame(values):
        shaped = values.reshape(-1, NP, LANES)
        turned = pltpu.roll(shaped, 4, 1)
        turned = jnp.where((node & 2) == 0, pltpu.roll(turned, 6, 1), pltpu.roll(turned, 2, 1))
        turned = jnp.where((node & 1) == 0, pltpu.roll(turned, 7, 1), pltpu.roll(turned, 1, 1))
        values = jnp.where(flip[None], turned, shaped).reshape(values.shape)
        parts = [values[k * NODES : (k + 1) * NODES] for k in range(ARRAYS)]
        parts[2] = parts[2] * sign
        parts[5] = parts[5] * sign
        return parts

    strip = in_frame(both[:, :LANES])
    h, u, v, area, depth, spin, tide = in_frame(both[:, LANES:])
    root = jnp.sqrt(area)
    mass = weight_ref[...] * area
    edges = mass_tendency(
        table_ref[...], h, u, v, tide, root * depth, root, mass * spin
    ) + [mass]
    east = jnp.where(second, east1, east0) != 0
    edges = [jnp.where(east, part[NODES - NP :], part[:NP]) for part in edges]
    whole = jnp.concatenate(strip + edges, 0)
    top, bottom = whole[:HALF_ROWS], whole[HALF_ROWS:]
    out0_ref[...] = jnp.where(second, pltpu.roll(bottom, 64, 1), top)
    out1_ref[...] = jnp.where(second, bottom, pltpu.roll(top, 64, 1))


def own_kernel(
    slot_ref, fields_ref, area_ref, depth_ref, spin_ref, tide_ref, lanes_ref, own_ref, hot_ref
):
    one_hot = by_slot(slot_ref, lanes_ref[0:8])
    stored = stored_rows(fields_ref, (area_ref, depth_ref, spin_ref, tide_ref))
    own_ref[...] = picked(stored, one_hot)
    hot_ref[...] = one_hot


def middle_kernel(
    block_cols, seam_ref, in0_ref, in1_ref, own_ref, lanes_ref, low_ref, centre_ref, high_ref
):
    east0, flip0, east1, flip1 = seam_flags(seam_ref, block_cols)
    second = lax.broadcasted_iota(i32, (1, LANES), 1) >= 64
    in0, in1 = in0_ref[...], in1_ref[...]
    top = jnp.where(second, pltpu.roll(in1, 64, 1), in0)
    bottom = jnp.where(second, in1, pltpu.roll(in0, 64, 1))
    whole = jnp.concatenate([top, bottom], 0)
    side = lanes_ref[16:24]
    first_at = jnp.where(side == 2, 64 * (1 - east0), 64 * east0)
    place = jnp.where(side == 0, -1, lanes_ref[8:16] + first_at)
    placed = picked(whole, as_one_hot(place, LANES))
    for k, ref in enumerate((low_ref, centre_ref, high_ref)):
        part = slice(k * LANES, (k + 1) * LANES)
        ref[:ROWS] = placed[:ROWS, part] + own_ref[:, part]
        ref[ROWS:] = placed[ROWS:, part]


def steps_kernel(
    below_ref, low_ref, centre_ref, high_ref, above_ref, hot_ref, table_ref, weight_ref,
    ext_ref, out_ref, sums,
):
    tiles = (below_ref, low_ref, centre_ref, high_ref, above_ref)
    block_y = lax.rem(lax.axis_index("blk"), BY)

    def rows_of(start, count):
        return jnp.concatenate([ref[start : start + count] for ref in tiles], 1)

    table = table_ref[...]
    weight = jnp.concatenate([weight_ref[...]] * len(tiles), 1)
    at_rim = ext_ref[0:1] != 0
    top_row = jnp.where(block_y == BY - 1, ext_ref[1:2], 0) != 0
    bottom_row = jnp.where(block_y == 0, ext_ref[2:3], 0) != 0

    def edge_sum(parts, rims=None):
        count = len(parts) * NP
        for c, part in enumerate(parts):
            west, east = part[:NP], part[NODES - NP :]
            at_east = pltpu.roll(west, EXT - 1, 1)
            at_west = pltpu.roll(east, 1, 1)
            if rims is not None:
                at_east = jnp.where(at_rim, rims[c], at_east)
                at_west = jnp.where(at_rim, rims[c], at_west)
            part = jnp.concatenate([west + at_west, part[NP : NODES - NP], east + at_east], 0)
            for k in range(len(tiles)):
                sums[k, c * NODES : (c + 1) * NODES] = part[:, k * LANES : (k + 1) * LANES]
        south_at, north_at = pl.ds(0, count, stride=NP), pl.ds(NP - 1, count, stride=NP)
        south = jnp.concatenate([sums[k, south_at] for k in range(len(tiles))], 1)
        north = jnp.concatenate([sums[k, north_at] for k in range(len(tiles))], 1)
        to_north = north + jnp.where(top_row, 0.0, pltpu.roll(south, EXT - PITCH, 1))
        to_south = south + jnp.where(bottom_row, 0.0, pltpu.roll(north, PITCH, 1))
        for k in range(len(tiles)):
            sums[k, south_at] = to_south[:, k * LANES : (k + 1) * LANES]
            sums[k, north_at] = to_north[:, k * LANES : (k + 1) * LANES]
        return [
            jnp.concatenate(
                [sums[k, c * NODES : (c + 1) * NODES] for k in range(len(tiles))], 1
            )
            for c in range(len(parts))
        ]

    start = [rows_of(c * NODES, NODES) for c in range(3)]
    area, depth, spin, tide = [rows_of(c * NODES, NODES) for c in range(3, ARRAYS)]
    root = jnp.sqrt(area)
    mass = weight * area
    mass_spin = mass * spin
    area_depth = root * depth
    per_mass = 1.0 / edge_sum([mass], [rows_of(ROWS + 3 * NP, NP)])[0]

    def average(parts, rims=None):
        return [part * per_mass for part in edge_sum(parts, rims)]

    def tendency(s):
        return mass_tendency(table, *s, tide, area_depth, root, mass_spin)

    def laplace(s):
        return [
            dot(table[3 * NODES :, : 3 * NODES], jnp.concatenate(high_low_high(part), 0))
            for part in s
        ]

    rims = [rows_of(ROWS + c * NP, NP) for c in range(3)]
    change = average(tendency(start), rims)
    one = [s + time_step * c for s, c in zip(start, change)]
    change = average(tendency(one))
    two = [0.75 * s + 0.25 * (o + time_step * c) for s, o, c in zip(start, one, change)]
    change = average(tendency(two))
    three = [s / 3.0 + 2.0 / 3.0 * (o + time_step * c) for s, o, c in zip(start, two, change)]
    biharmonic = average(laplace(average(laplace(three))))
    own = ext_ref[3:4, LANES : LANES + MID] != 0
    stepped = [
        jnp.where(
            own,
            (s - time_step * hyper_coeff * b)[:, LANES : LANES + MID],
            0.0,
        )
        for s, b in zip(three, biharmonic)
    ]
    stored = picked(jnp.concatenate(stepped, 0), hot_ref[...], dot_other)
    out_ref[...] = stored.reshape(out_ref.shape)


def on_device(fields, jacobian, water_depth, coriolis, tide_height, slot_of, seam_rows):
    block_cols = lax.axis_size("blk") // BY
    count = lax.axis_size("face") * lax.axis_size("blk")
    table, weight = operator_table()
    lanes, ext = lane_tables()
    table, weight, lanes, ext = (jnp.asarray(part) for part in (table, weight, lanes, ext))
    vmem = pl.BlockSpec(memory_space=pltpu.VMEM)
    smem = pl.BlockSpec(memory_space=pltpu.SMEM)
    params = pltpu.CompilerParams(vmem_limit_bytes=48 * 2**20)
    held = (fields, jacobian, water_depth, coriolis, tide_height)

    def call(kernel, ins, outs, cost, scratch=(), name=None):
        return pl.pallas_call(
            kernel,
            out_shape=[jax.ShapeDtypeStruct(*out) for out in outs],
            in_specs=[smem if spec is smem else vmem for spec, value in ins],
            out_specs=[vmem] * len(outs),
            scratch_shapes=list(scratch),
            compiler_params=params,
            cost_estimate=pl.CostEstimate(
                flops=cost, bytes_accessed=2 * 2**20, transcendentals=0
            ),
            name=name,
        )(*[value for spec, value in ins])

    strip = ((HALF_ROWS, LANES), f32)
    strip0, strip1 = call(
        functools.partial(strips_kernel, block_cols),
        [(smem, seam_rows)] + [(vmem, x) for x in (slot_of, *held, table, weight)],
        [strip, strip],
        10**8,
        name="strips",
    )
    span = block_cols * BY

    def rank(face, block_x, block_y):
        return face * span + block_x * BY + block_y

    both = ("face", "blk")
    places = [(f, x, y) for f in range(2) for x in range(block_cols) for y in range(BY)]
    if block_cols == 1:
        halo0 = lax.ppermute(
            strip0, both, [(rank(f, x, y), rank(1 - f, x, y)) for f, x, y in places]
        )
        halo1 = lax.ppermute(
            strip1, both, [(rank(f, x, y), rank(1 - f, x, BY - 1 - y)) for f, x, y in places]
        )
    else:
        last = block_cols - 1
        flipped = (seam_rows[:, 1] - seam_rows[:, 0]) % seam_rows.shape[1] != 1
        face = lax.axis_index("face")
        block_x = lax.axis_index("blk") // BY
        from_west = lax.ppermute(strip0, both, [(i, (i + BY) % count) for i in range(count)])
        from_east = lax.ppermute(strip1, both, [(i, (i - BY) % count) for i in range(count)])
        turned_west = lax.ppermute(
            strip0, both,
            [(rank(f, last, y), rank(1 - f, 0, BY - 1 - y)) for f in range(2) for y in range(BY)],
        )
        turned_east = lax.ppermute(
            strip1, both,
            [(rank(f, 0, y), rank(1 - f, last, BY - 1 - y)) for f in range(2) for y in range(BY)],
        )
        halo0 = jnp.where((block_x == last) & flipped[face], turned_east, from_east)
        halo1 = jnp.where((block_x == 0) & flipped[1 - face], turned_west, from_west)
    own, hot = call(
        own_kernel,
        [(vmem, x) for x in (slot_of, *held, lanes)],
        [((ROWS, MID), f32), ((ELEMENTS, MID), bf16)],
        3 * 10**8,
        name="own",
    )
    tile = ((ALL_ROWS, LANES), f32)
    low, centre, high = call(
        functools.partial(middle_kernel, block_cols),
        [(smem, seam_rows)] + [(vmem, x) for x in (halo0, halo1, own, lanes)],
        [tile, tile, tile],
        10**8,
        name="middle",
    )
    above = lax.ppermute(
        low, both, [(rank(f, x, y), rank(f, x, (y - 1) % BY)) for f, x, y in places]
    )
    below = lax.ppermute(
        high, both, [(rank(f, x, y), rank(f, x, (y + 1) % BY)) for f, x, y in places]
    )
    (stepped,) = call(
        steps_kernel,
        [(vmem, x) for x in (below, low, centre, high, above, hot, table, weight, ext)],
        [(fields.shape, f32)],
        10**9,
        scratch=[pltpu.VMEM((EXT // LANES, 3 * NODES, LANES), f32)],
        name="steps",
    )
    return stepped


def solution(mesh):
    return jax.shard_map(
        on_device,
        mesh=mesh,
        in_specs=(
            P(None, None, None, ("face", "blk")),
            P(None, None, ("face", "blk")),
            P(None, None, ("face", "blk")),
            P(None, None, ("face", "blk")),
            P(None, None, ("face", "blk")),
            P(("face", "blk"), None),
            P(),
        ),
        out_specs=P(None, None, None, ("face", "blk")),
        check_vma=False,
    )
```

```python
import functools
import math

import jax
import jax.numpy as jnp
import ml_dtypes
import numpy as np
from jax import lax
from jax.experimental import pallas as pl
from jax.experimental.pallas import tpu as pltpu
from jax.sharding import PartitionSpec as P

BY = 16
GX = 16
GY = 16
NP = 8
NODES = NP * NP
ARRAYS = 7
ROWS = ARRAYS * NODES
EDGE_ROWS = 4 * NP
ALL_ROWS = ROWS + EDGE_ROWS
HALF_ROWS = ALL_ROWS // 2
RING_X = 4
RING_Y = 5
PITCH = GX + 2 * RING_X
MID = GY * PITCH
LANES = 128
EXT = MID + 2 * LANES
LEAD = LANES - RING_Y * PITCH
ELEMENTS = GX * GY

time_step = 0.03
hyper_coeff = 0.0002

f32 = jnp.float32
bf16 = jnp.bfloat16
i32 = jnp.int32


def legendre_pair(location, degree):
    lower_value = 1.0
    upper_value = location
    for polynomial_order in range(2, degree + 1):
        lower_value, upper_value = (
            upper_value,
            (
                (2 * polynomial_order - 1) * location * upper_value
                - (polynomial_order - 1) * lower_value
            )
            / polynomial_order,
        )
    return (lower_value, upper_value)


def gll_tables(points):
    degree = points - 1
    locations = [-math.cos(math.pi * position / degree) for position in range(points)]
    for iteration in range(100):
        updated = []
        for location in locations:
            lower_value, upper_value = legendre_pair(location, degree)
            updated.append(
                location - (location * upper_value - lower_value) / ((degree + 1) * upper_value)
            )
        locations = updated
    locations[0] = -1.0
    locations[degree] = 1.0
    legendre_at = [legendre_pair(location, degree)[1] for location in locations]
    weights = [2.0 / (degree * (degree + 1) * value * value) for value in legendre_at]
    corner_value = degree * (degree + 1) / 4.0
    derivative = []
    for row_index in range(points):
        row_values = []
        for column_index in range(points):
            if row_index != column_index:
                row_values.append(
                    legendre_at[row_index]
                    / (legendre_at[column_index] * (locations[row_index] - locations[column_index]))
                )
            elif row_index == 0:
                row_values.append(-corner_value)
            elif row_index == degree:
                row_values.append(corner_value)
            else:
                row_values.append(0.0)
        derivative.append(row_values)
    return np.asarray(weights, np.float64), np.asarray(derivative, np.float64)


def in_three(matrix):
    high = matrix.astype(ml_dtypes.bfloat16)
    low = (matrix - high.astype(np.float64)).astype(ml_dtypes.bfloat16)
    return np.concatenate([high, high, low], 1)


def operator_table():
    weights, derivative = gll_tables(NP)
    eye = np.eye(NP)
    node_weight = np.outer(weights, weights).reshape(NODES, 1)
    along_x = node_weight * np.kron(derivative, eye)
    along_y = node_weight * np.kron(eye, derivative)
    second = derivative @ derivative
    both = node_weight * (np.kron(second, eye) + np.kron(eye, second))
    table = np.zeros((4 * NODES, 6 * NODES), ml_dtypes.bfloat16)
    table[:NODES, : 3 * NODES] = in_three(along_x)
    table[NODES : 2 * NODES, : 3 * NODES] = in_three(along_y)
    table[2 * NODES : 3 * NODES, : 3 * NODES] = in_three(along_x)
    table[2 * NODES : 3 * NODES, 3 * NODES :] = in_three(along_y)
    table[3 * NODES :, : 3 * NODES] = in_three(both)
    spread = np.broadcast_to(node_weight, (NODES, LANES)).astype(np.float32)
    return table.astype(np.float32), np.ascontiguousarray(spread)


def lane_tables():
    table = np.zeros((24, MID), np.int32)
    for lane in range(MID):
        row, col = divmod(lane, PITCH)
        x = col - RING_X
        own = 0 <= x < GX
        table[0:8, lane] = x * GY + row if own else -1
        if not own:
            table[8:16, lane] = row * RING_X + (col if x < 0 else x - GX)
        table[16:24, lane] = 0 if own else (1 if x < 0 else 2)
    ext = np.zeros((8, EXT), np.int32)
    for lane in range(EXT):
        row, col = divmod(lane - LEAD, PITCH)
        y = row - RING_Y
        x = col - RING_X
        ext[0, lane] = x in (-RING_X, GX + RING_X - 1)
        ext[1, lane] = y == GY - 1
        ext[2, lane] = y == 0
        ext[3, lane] = 0 <= y < GY and 0 <= x < GX
    return table, ext


def exact_pieces(values):
    high = values.astype(bf16)
    rest = values - high.astype(f32)
    middle = rest.astype(bf16)
    low = (rest - middle.astype(f32)).astype(bf16)
    return high, middle, low


def dot(a, b):
    return jnp.dot(a, b, preferred_element_type=f32)


def dot_other(a, b):
    return lax.dot_general(a, b, (((1,), (1,)), ((), ())), preferred_element_type=f32)


def picked(values, one_hot, product=dot):
    high, middle, low = exact_pieces(values)
    return (product(high, one_hot) + product(middle, one_hot)) + product(low, one_hot)


def as_one_hot(row_of_lane, depth):
    index = lax.broadcasted_iota(i32, (depth, row_of_lane.shape[1]), 0)
    return jnp.where(index == row_of_lane[0:1], 1.0, 0.0).astype(bf16)


def high_low_high(values):
    high = values.astype(bf16)
    low = (values - high.astype(f32)).astype(bf16)
    return [high, low, high]


def by_slot(slot_ref, cell_of_lane):
    slots = jnp.broadcast_to(slot_ref[...], (8, ELEMENTS)).astype(f32).astype(bf16)
    chosen = dot(slots, as_one_hot(cell_of_lane, ELEMENTS))
    chosen = jnp.where(cell_of_lane >= 0, chosen, -1.0)
    index = lax.broadcasted_iota(i32, (ELEMENTS, cell_of_lane.shape[1]), 0).astype(f32)
    return jnp.where(index == chosen[0:1], 1.0, 0.0).astype(bf16)


def brought(sources, buffers, sems):
    copies = [
        pltpu.make_async_copy(source, buffer, sems.at[k])
        for k, (source, buffer) in enumerate(zip(sources, buffers))
    ]
    for copy in copies:
        copy.start()
    for copy in copies:
        copy.wait()


def stored_rows(fields_ref, others):
    parts = [fields_ref[...].reshape(3 * NODES, ELEMENTS)]
    parts += [ref[...].reshape(NODES, ELEMENTS) for ref in others]
    return jnp.concatenate(parts, 0)


def mass_tendency(table, h, u, v, tide, area_depth, weighted_area, spin):
    p = high_low_high(h - tide)
    slopes = dot(table[: 2 * NODES, : 3 * NODES], jnp.concatenate(p, 0))
    flux = high_low_high(area_depth * u) + high_low_high(area_depth * v)
    spread = dot(table[2 * NODES : 3 * NODES], jnp.concatenate(flux, 0))
    return [
        -spread,
        spin * v - weighted_area * slopes[:NODES],
        -spin * u - weighted_area * slopes[NODES:],
    ]


def seam_flags(seam_ref, block_cols):
    size_y = seam_ref.shape[1]
    face = lax.axis_index("face")
    blk = lax.axis_index("blk")
    block_x = blk // BY

    def flipped(k):
        return jnp.where(lax.rem(seam_ref[k, 1] - seam_ref[k, 0] + size_y, size_y) != 1, 1, 0)

    first, second = flipped(0), flipped(1)
    east_flip = jnp.where(face == 0, first, second)
    west_flip = jnp.where(face == 0, second, first)
    if block_cols == 1:
        return 1 - east_flip, 0, east_flip, 1
    at_east = jnp.where(block_x == block_cols - 1, east_flip, 0)
    at_west = jnp.where(block_x == 0, west_flip, 0)
    return 1, at_east, 0, at_west


def strips_kernel(block_cols, *refs):
    sources, (out0_ref, out1_ref), buffers, sems = refs[:9], refs[9:11], refs[11:20], refs[20]
    brought(sources, buffers, sems)
    seam_ref, slot_ref, fields_ref, area_ref, depth_ref, spin_ref, tide_ref = buffers[:7]
    table_ref, weight_ref = buffers[7:]
    east0, flip0, east1, flip1 = seam_flags(seam_ref, block_cols)
    lane = lax.broadcasted_iota(i32, (8, 2 * LANES), 1)
    second = (lane & 64) != 0
    place = lane & 63
    row = place >> 2
    row = jnp.where(jnp.where(second, flip1, flip0) != 0, GY - 1 - row, row)
    east = jnp.where(second, east1, east0) != 0
    col = jnp.where(east, GX - RING_X, 0) + (place & 3)
    col = jnp.where(lane >= LANES, jnp.where(east, GX - RING_X - 1, RING_X), col)
    one_hot = by_slot(slot_ref, col * GY + row)
    stored = stored_rows(fields_ref, (area_ref, depth_ref, spin_ref, tide_ref))
    both = picked(stored, one_hot)

    lane = lax.broadcasted_iota(i32, (1, LANES), 1)
    second = lane >= 64
    flip = jnp.where(second, flip1, flip0) != 0
    sign = jnp.where(flip, -1.0, 1.0)
    node = lax.broadcasted_iota(i32, (1, NP, 1), 1)

    def in_frame(values):
        shaped = values.reshape(-1, NP, LANES)
        turned = pltpu.roll(shaped, 4, 1)
        turned = jnp.where((node & 2) == 0, pltpu.roll(turned, 6, 1), pltpu.roll(turned, 2, 1))
        turned = jnp.where((node & 1) == 0, pltpu.roll(turned, 7, 1), pltpu.roll(turned, 1, 1))
        values = jnp.where(flip[None], turned, shaped).reshape(values.shape)
        parts = [values[k * NODES : (k + 1) * NODES] for k in range(ARRAYS)]
        parts[2] = parts[2] * sign
        parts[5] = parts[5] * sign
        return parts

    strip = in_frame(both[:, :LANES])
    h, u, v, area, depth, spin, tide = in_frame(both[:, LANES:])
    root = jnp.sqrt(area)
    mass = weight_ref[...] * area
    edges = mass_tendency(
        table_ref[...].astype(bf16), h, u, v, tide, root * depth, root, mass * spin
    ) + [mass]
    east = jnp.where(second, east1, east0) != 0
    edges = [jnp.where(east, part[NODES - NP :], part[:NP]) for part in edges]
    whole = jnp.concatenate(strip + edges, 0)
    top, bottom = whole[:HALF_ROWS], whole[HALF_ROWS:]
    out0_ref[...] = jnp.where(second, pltpu.roll(bottom, 64, 1), top)
    out1_ref[...] = jnp.where(second, bottom, pltpu.roll(top, 64, 1))


def own_kernel(*refs):
    sources, (own_ref, hot_ref), buffers, sems = refs[:7], refs[7:9], refs[9:16], refs[16]
    brought(sources, buffers, sems)
    slot_ref, fields_ref, area_ref, depth_ref, spin_ref, tide_ref, lanes_ref = buffers
    one_hot = by_slot(slot_ref, lanes_ref[0:8])
    stored = stored_rows(fields_ref, (area_ref, depth_ref, spin_ref, tide_ref))
    own_ref[...] = picked(stored, one_hot)
    hot_ref[...] = one_hot


def middle_kernel(
    block_cols, seam_ref, in0_ref, in1_ref, own_ref, lanes_ref, low_ref, centre_ref, high_ref
):
    east0, flip0, east1, flip1 = seam_flags(seam_ref, block_cols)
    second = lax.broadcasted_iota(i32, (1, LANES), 1) >= 64
    in0, in1 = in0_ref[...], in1_ref[...]
    top = jnp.where(second, pltpu.roll(in1, 64, 1), in0)
    bottom = jnp.where(second, in1, pltpu.roll(in0, 64, 1))
    whole = jnp.concatenate([top, bottom], 0)
    side = lanes_ref[16:24]
    first_at = jnp.where(side == 2, 64 * (1 - east0), 64 * east0)
    place = jnp.where(side == 0, -1, lanes_ref[8:16] + first_at)
    placed = picked(whole, as_one_hot(place, LANES))
    for k, ref in enumerate((low_ref, centre_ref, high_ref)):
        part = slice(k * LANES, (k + 1) * LANES)
        ref[:ROWS] = placed[:ROWS, part] + own_ref[:, part]
        ref[ROWS:] = placed[ROWS:, part]


def steps_kernel(
    below_ref, low_ref, centre_ref, high_ref, above_ref, hot_ref, table_ref, weight_ref,
    ext_ref, out_ref, sums,
):
    tiles = (below_ref, low_ref, centre_ref, high_ref, above_ref)
    block_y = lax.rem(lax.axis_index("blk"), BY)

    def rows_of(start, count):
        return jnp.concatenate([ref[start : start + count] for ref in tiles], 1)

    table = table_ref[...].astype(bf16)
    weight = jnp.concatenate([weight_ref[...]] * len(tiles), 1)
    at_rim = ext_ref[0:1] != 0
    top_row = jnp.where(block_y == BY - 1, ext_ref[1:2], 0) != 0
    bottom_row = jnp.where(block_y == 0, ext_ref[2:3], 0) != 0

    def edge_sum(parts, rims=None):
        count = len(parts) * NP
        for c, part in enumerate(parts):
            west, east = part[:NP], part[NODES - NP :]
            at_east = pltpu.roll(west, EXT - 1, 1)
            at_west = pltpu.roll(east, 1, 1)
            if rims is not None:
                at_east = jnp.where(at_rim, rims[c], at_east)
                at_west = jnp.where(at_rim, rims[c], at_west)
            part = jnp.concatenate([west + at_west, part[NP : NODES - NP], east + at_east], 0)
            for k in range(len(tiles)):
                sums[k, c * NODES : (c + 1) * NODES] = part[:, k * LANES : (k + 1) * LANES]
        south_at, north_at = pl.ds(0, count, stride=NP), pl.ds(NP - 1, count, stride=NP)
        south = jnp.concatenate([sums[k, south_at] for k in range(len(tiles))], 1)
        north = jnp.concatenate([sums[k, north_at] for k in range(len(tiles))], 1)
        to_north = north + jnp.where(top_row, 0.0, pltpu.roll(south, EXT - PITCH, 1))
        to_south = south + jnp.where(bottom_row, 0.0, pltpu.roll(north, PITCH, 1))
        for k in range(len(tiles)):
            sums[k, south_at] = to_south[:, k * LANES : (k + 1) * LANES]
            sums[k, north_at] = to_north[:, k * LANES : (k + 1) * LANES]
        return [
            jnp.concatenate(
                [sums[k, c * NODES : (c + 1) * NODES] for k in range(len(tiles))], 1
            )
            for c in range(len(parts))
        ]

    start = [rows_of(c * NODES, NODES) for c in range(3)]
    area, depth, spin, tide = [rows_of(c * NODES, NODES) for c in range(3, ARRAYS)]
    area = jnp.where(area > 0.0, area, 1.0)
    root = jnp.sqrt(area)
    mass = weight * area
    mass_spin = mass * spin
    area_depth = root * depth
    per_mass = 1.0 / edge_sum([mass], [rows_of(ROWS + 3 * NP, NP)])[0]

    def average(parts, rims=None):
        return [part * per_mass for part in edge_sum(parts, rims)]

    def tendency(s):
        return mass_tendency(table, *s, tide, area_depth, root, mass_spin)

    def laplace(s):
        return [
            dot(table[3 * NODES :, : 3 * NODES], jnp.concatenate(high_low_high(part), 0))
            for part in s
        ]

    rims = [rows_of(ROWS + c * NP, NP) for c in range(3)]
    change = average(tendency(start), rims)
    one = [s + time_step * c for s, c in zip(start, change)]
    change = average(tendency(one))
    two = [0.75 * s + 0.25 * (o + time_step * c) for s, o, c in zip(start, one, change)]
    change = average(tendency(two))
    three = [s / 3.0 + 2.0 / 3.0 * (o + time_step * c) for s, o, c in zip(start, two, change)]
    biharmonic = average(laplace(average(laplace(three))))
    own = ext_ref[3:4, LANES : LANES + MID] != 0
    stepped = [
        jnp.where(
            own,
            (s - time_step * hyper_coeff * b)[:, LANES : LANES + MID],
            0.0,
        )
        for s, b in zip(three, biharmonic)
    ]
    stored = picked(jnp.concatenate(stepped, 0), hot_ref[...], dot_other)
    out_ref[...] = stored.reshape(out_ref.shape)


def on_device(fields, jacobian, water_depth, coriolis, tide_height, slot_of, seam_rows):
    block_cols = lax.axis_size("blk") // BY
    count = lax.axis_size("face") * lax.axis_size("blk")
    table, weight = operator_table()
    lanes, ext = lane_tables()
    table, weight, lanes, ext = (jnp.asarray(part) for part in (table, weight, lanes, ext))
    vmem = pl.BlockSpec(memory_space=pltpu.VMEM)
    smem = pl.BlockSpec(memory_space=pltpu.SMEM)
    hbm = pl.BlockSpec(memory_space=pltpu.HBM)
    params = pltpu.CompilerParams(vmem_limit_bytes=48 * 2**20)
    held = (fields, jacobian, water_depth, coriolis, tide_height)

    def call(kernel, ins, outs, cost, scratch=(), name=None):
        return pl.pallas_call(
            kernel,
            out_shape=[jax.ShapeDtypeStruct(*out) for out in outs],
            in_specs=[spec for spec, value in ins],
            out_specs=[vmem] * len(outs),
            scratch_shapes=list(scratch),
            compiler_params=params,
            cost_estimate=pl.CostEstimate(
                flops=cost, bytes_accessed=2 * 2**20, transcendentals=0
            ),
            name=name,
        )(
            *[
                pltpu.with_memory_space_constraint(value, pltpu.HBM) if spec is hbm else value
                for spec, value in ins
            ]
        )

    strip = ((HALF_ROWS, LANES), f32)
    def room(values, spaces=None):
        spaces = spaces or [pltpu.VMEM] * len(values)
        buffers = [space(x.shape, x.dtype) for space, x in zip(spaces, values)]
        return buffers + [pltpu.SemaphoreType.DMA((len(values),))]

    needed = (seam_rows, slot_of, *held, table, weight)
    strip0, strip1 = call(
        functools.partial(strips_kernel, block_cols),
        [(hbm, x) for x in needed],
        [strip, strip],
        10**8,
        scratch=room(needed, [pltpu.SMEM] + [pltpu.VMEM] * (len(needed) - 1)),
        name="strips",
    )
    span = block_cols * BY

    def rank(face, block_x, block_y):
        return face * span + block_x * BY + block_y

    both = ("face", "blk")
    places = [(f, x, y) for f in range(2) for x in range(block_cols) for y in range(BY)]
    if block_cols == 1:
        halo1 = lax.ppermute(
            strip1, both, [(rank(f, x, y), rank(1 - f, x, BY - 1 - y)) for f, x, y in places]
        )
        halo0 = lax.ppermute(
            strip0, both, [(rank(f, x, y), rank(1 - f, x, y)) for f, x, y in places]
        )
    else:
        last = block_cols - 1
        flipped = (seam_rows[:, 1] - seam_rows[:, 0]) % seam_rows.shape[1] != 1
        face = lax.axis_index("face")
        block_x = lax.axis_index("blk") // BY
        from_west = lax.ppermute(strip0, both, [(i, (i + BY) % count) for i in range(count)])
        from_east = lax.ppermute(strip1, both, [(i, (i - BY) % count) for i in range(count)])
        turned_west = lax.ppermute(
            strip0, both,
            [(rank(f, last, y), rank(1 - f, 0, BY - 1 - y)) for f in range(2) for y in range(BY)],
        )
        turned_east = lax.ppermute(
            strip1, both,
            [(rank(f, 0, y), rank(1 - f, last, BY - 1 - y)) for f in range(2) for y in range(BY)],
        )
        halo0 = jnp.where((block_x == last) & flipped[face], turned_east, from_east)
        halo1 = jnp.where((block_x == 0) & flipped[1 - face], turned_west, from_west)
    needed = (slot_of, *held, lanes)
    own, hot = call(
        own_kernel,
        [(hbm, x) for x in needed],
        [((ROWS, MID), f32), ((ELEMENTS, MID), bf16)],
        3 * 10**8,
        scratch=room(needed),
        name="own",
    )
    tile = ((ALL_ROWS, LANES), f32)
    low, centre, high = call(
        functools.partial(middle_kernel, block_cols),
        [(smem, seam_rows)] + [(vmem, x) for x in (halo0, halo1, own, lanes)],
        [tile, tile, tile],
        10**8,
        name="middle",
    )
    above = lax.ppermute(
        low, both, [(rank(f, x, y), rank(f, x, y - 1)) for f, x, y in places if y > 0]
    )
    below = lax.ppermute(
        high, both, [(rank(f, x, y), rank(f, x, y + 1)) for f, x, y in places if y < BY - 1]
    )
    (stepped,) = call(
        steps_kernel,
        [(vmem, x) for x in (below, low, centre, high, above, hot, table, weight, ext)],
        [(fields.shape, f32)],
        10**9,
        scratch=[pltpu.VMEM((EXT // LANES, 3 * NODES, LANES), f32)],
        name="steps",
    )
    return stepped


def solution(mesh):
    return jax.shard_map(
        on_device,
        mesh=mesh,
        in_specs=(
            P(None, None, None, ("face", "blk")),
            P(None, None, ("face", "blk")),
            P(None, None, ("face", "blk")),
            P(None, None, ("face", "blk")),
            P(None, None, ("face", "blk")),
            P(("face", "blk"), None),
            P(),
        ),
        out_specs=P(None, None, None, ("face", "blk")),
        check_vma=False,
    )
```

```python
import functools
import math

import jax
import jax.numpy as jnp
import ml_dtypes
import numpy as np
from jax import lax
from jax.experimental import pallas as pl
from jax.experimental.pallas import tpu as pltpu
from jax.sharding import PartitionSpec as P

BY = 16
GX = 16
GY = 16
NP = 8
NODES = NP * NP
ARRAYS = 7
ROWS = ARRAYS * NODES
EDGE_ROWS = 4 * NP
ALL_ROWS = ROWS + EDGE_ROWS
HALF_ROWS = ALL_ROWS // 2
RING = 4
RIM_ROWS = ROWS + 2 * EDGE_ROWS
PITCH = GX + 2 * RING
MID = GY * PITCH
LANES = 128
EXT = MID + 2 * LANES
LEAD = LANES - RING * PITCH
ELEMENTS = GX * GY

time_step = 0.03
hyper_coeff = 0.0002

f32 = jnp.float32
bf16 = jnp.bfloat16
i32 = jnp.int32


def legendre_pair(location, degree):
    lower_value = 1.0
    upper_value = location
    for polynomial_order in range(2, degree + 1):
        lower_value, upper_value = (
            upper_value,
            (
                (2 * polynomial_order - 1) * location * upper_value
                - (polynomial_order - 1) * lower_value
            )
            / polynomial_order,
        )
    return (lower_value, upper_value)


def gll_tables(points):
    degree = points - 1
    locations = [-math.cos(math.pi * position / degree) for position in range(points)]
    for iteration in range(100):
        updated = []
        for location in locations:
            lower_value, upper_value = legendre_pair(location, degree)
            updated.append(
                location - (location * upper_value - lower_value) / ((degree + 1) * upper_value)
            )
        locations = updated
    locations[0] = -1.0
    locations[degree] = 1.0
    legendre_at = [legendre_pair(location, degree)[1] for location in locations]
    weights = [2.0 / (degree * (degree + 1) * value * value) for value in legendre_at]
    corner_value = degree * (degree + 1) / 4.0
    derivative = []
    for row_index in range(points):
        row_values = []
        for column_index in range(points):
            if row_index != column_index:
                row_values.append(
                    legendre_at[row_index]
                    / (legendre_at[column_index] * (locations[row_index] - locations[column_index]))
                )
            elif row_index == 0:
                row_values.append(-corner_value)
            elif row_index == degree:
                row_values.append(corner_value)
            else:
                row_values.append(0.0)
        derivative.append(row_values)
    return np.asarray(weights, np.float64), np.asarray(derivative, np.float64)


def in_three(matrix):
    high = matrix.astype(ml_dtypes.bfloat16)
    low = (matrix - high.astype(np.float64)).astype(ml_dtypes.bfloat16)
    return np.concatenate([high, high, low], 1)


def operator_table():
    weights, derivative = gll_tables(NP)
    eye = np.eye(NP)
    node_weight = np.outer(weights, weights).reshape(NODES, 1)
    along_x = node_weight * np.kron(derivative, eye)
    along_y = node_weight * np.kron(eye, derivative)
    second = derivative @ derivative
    both = node_weight * (np.kron(second, eye) + np.kron(eye, second))
    table = np.zeros((4 * NODES, 6 * NODES), ml_dtypes.bfloat16)
    table[:NODES, : 3 * NODES] = in_three(along_x)
    table[NODES : 2 * NODES, : 3 * NODES] = in_three(along_y)
    table[2 * NODES : 3 * NODES, : 3 * NODES] = in_three(along_x)
    table[2 * NODES : 3 * NODES, 3 * NODES :] = in_three(along_y)
    table[3 * NODES :, : 3 * NODES] = in_three(both)
    spread = np.broadcast_to(node_weight, (NODES, LANES)).astype(np.float32)
    return table.astype(np.float32), np.ascontiguousarray(spread)


def lane_tables():
    table = np.zeros((24, MID), np.int32)
    for lane in range(MID):
        row, col = divmod(lane, PITCH)
        x = col - RING
        own = 0 <= x < GX
        table[0:8, lane] = x * GY + row if own else -1
        if not own:
            table[8:16, lane] = row * RING + (col if x < 0 else x - GX)
        table[16:24, lane] = 0 if own else (1 if x < 0 else 2)
    ext = np.zeros((8, EXT), np.int32)
    outer = np.zeros((24, 2 * LANES), np.int32)
    for lane in range(EXT):
        row, col = divmod(lane - LEAD, PITCH)
        y = row - RING
        x = col - RING
        inside = 0 <= row < GY + 2 * RING
        ext[0, lane] = x in (-RING, GX + RING - 1)
        ext[1, lane] = y == GY - 1
        ext[2, lane] = y == 0
        ext[3, lane] = 0 <= y < GY and 0 <= x < GX
        ext[4, lane] = y == -RING
        ext[5, lane] = y == GY + RING - 1
        if inside and not 0 <= y < GY:
            place = lane if y < 0 else lane - LANES - MID + LANES
            step = y + RING if y < 0 else y - GY
            if 0 <= x < GX:
                outer[0:8, place] = step * GX + x
                outer[8:16, place] = 1
            else:
                outer[0:8, place] = LANES + step * RING + (x + RING if x < 0 else x - GX)
                outer[8:16, place] = 2 if x < 0 else 3
            outer[16:24, place] = y > 0
    return table, ext, outer


def exact_pieces(values):
    high = values.astype(bf16)
    rest = values - high.astype(f32)
    middle = rest.astype(bf16)
    low = (rest - middle.astype(f32)).astype(bf16)
    return high, middle, low


def dot(a, b):
    return jnp.dot(a, b, preferred_element_type=f32)


def dot_other(a, b):
    return lax.dot_general(a, b, (((1,), (1,)), ((), ())), preferred_element_type=f32)


def picked(values, one_hot, product=dot):
    high, middle, low = exact_pieces(values)
    return (product(high, one_hot) + product(middle, one_hot)) + product(low, one_hot)


def as_one_hot(row_of_lane, depth):
    index = lax.broadcasted_iota(i32, (depth, row_of_lane.shape[1]), 0)
    return jnp.where(index == row_of_lane[0:1], 1.0, 0.0).astype(bf16)


def high_low_high(values):
    high = values.astype(bf16)
    low = (values - high.astype(f32)).astype(bf16)
    return [high, low, high]


def by_slot(slot_ref, cell_of_lane):
    slots = jnp.broadcast_to(slot_ref[...], (8, ELEMENTS)).astype(f32).astype(bf16)
    chosen = dot(slots, as_one_hot(cell_of_lane, ELEMENTS))
    chosen = jnp.where(cell_of_lane >= 0, chosen, -1.0)
    index = lax.broadcasted_iota(i32, (ELEMENTS, cell_of_lane.shape[1]), 0).astype(f32)
    return jnp.where(index == chosen[0:1], 1.0, 0.0).astype(bf16)


def brought(sources, buffers, sems):
    copies = [
        pltpu.make_async_copy(source, buffer, sems.at[k])
        for k, (source, buffer) in enumerate(zip(sources, buffers))
    ]
    for copy in copies:
        copy.start()
    for copy in copies:
        copy.wait()


def stored_rows(fields_ref, others):
    parts = [fields_ref[...].reshape(3 * NODES, ELEMENTS)]
    parts += [ref[...].reshape(NODES, ELEMENTS) for ref in others]
    return jnp.concatenate(parts, 0)


def mass_tendency(table, h, u, v, tide, area_depth, weighted_area, spin):
    p = high_low_high(h - tide)
    slopes = dot(table[: 2 * NODES, : 3 * NODES], jnp.concatenate(p, 0))
    flux = high_low_high(area_depth * u) + high_low_high(area_depth * v)
    spread = dot(table[2 * NODES : 3 * NODES], jnp.concatenate(flux, 0))
    return [
        -spread,
        spin * v - weighted_area * slopes[:NODES],
        -spin * u - weighted_area * slopes[NODES:],
    ]


def edge_values(table_ref, weight_ref, h, u, v, area, depth, spin, tide):
    root = jnp.sqrt(area)
    mass = weight_ref[...] * area
    table = table_ref[...].astype(bf16)
    return mass_tendency(table, h, u, v, tide, root * depth, root, mass * spin) + [mass]


def row_edges(sums):
    return sums[pl.ds(NP - 1, EDGE_ROWS, stride=NP)], sums[pl.ds(0, EDGE_ROWS, stride=NP)]


def packed(whole):
    second = lax.broadcasted_iota(i32, (1, LANES), 1) >= 64
    top, bottom = whole[:HALF_ROWS], whole[HALF_ROWS:]
    return (
        jnp.where(second, pltpu.roll(bottom, 64, 1), top),
        jnp.where(second, bottom, pltpu.roll(top, 64, 1)),
    )


def unpacked(in0, in1):
    second = lax.broadcasted_iota(i32, (1, LANES), 1) >= 64
    top = jnp.where(second, pltpu.roll(in1, 64, 1), in0)
    bottom = jnp.where(second, in1, pltpu.roll(in0, 64, 1))
    return jnp.concatenate([top, bottom], 0)


def seam_flags(seam_ref, block_cols):
    size_y = seam_ref.shape[1]
    face = lax.axis_index("face")
    blk = lax.axis_index("blk")
    block_x = blk // BY

    def flipped(k):
        return jnp.where(lax.rem(seam_ref[k, 1] - seam_ref[k, 0] + size_y, size_y) != 1, 1, 0)

    first, second = flipped(0), flipped(1)
    east_flip = jnp.where(face == 0, first, second)
    west_flip = jnp.where(face == 0, second, first)
    if block_cols == 1:
        return 1 - east_flip, 0, east_flip, 1
    at_east = jnp.where(block_x == block_cols - 1, east_flip, 0)
    at_west = jnp.where(block_x == 0, west_flip, 0)
    return 1, at_east, 0, at_west


def strips_kernel(block_cols, *refs):
    sources, (out0_ref, out1_ref, stored_ref) = refs[:9], refs[9:12]
    buffers, sems = refs[12:21], refs[21]
    brought(sources, buffers, sems)
    seam_ref, slot_ref, fields_ref, area_ref, depth_ref, spin_ref, tide_ref = buffers[:7]
    table_ref, weight_ref = buffers[7:]
    east0, flip0, east1, flip1 = seam_flags(seam_ref, block_cols)
    lane = lax.broadcasted_iota(i32, (8, 2 * LANES), 1)
    second = (lane & 64) != 0
    place = lane & 63
    row = place >> 2
    row = jnp.where(jnp.where(second, flip1, flip0) != 0, GY - 1 - row, row)
    east = jnp.where(second, east1, east0) != 0
    col = jnp.where(east, GX - RING, 0) + (place & 3)
    col = jnp.where(lane >= LANES, jnp.where(east, GX - RING - 1, RING), col)
    one_hot = by_slot(slot_ref, col * GY + row)
    stored = stored_rows(fields_ref, (area_ref, depth_ref, spin_ref, tide_ref))
    stored_ref[...] = stored
    both = picked(stored, one_hot)

    lane = lax.broadcasted_iota(i32, (1, LANES), 1)
    second = lane >= 64
    flip = jnp.where(second, flip1, flip0) != 0
    sign = jnp.where(flip, -1.0, 1.0)
    node = lax.broadcasted_iota(i32, (1, NP, 1), 1)

    def in_frame(values):
        shaped = values.reshape(-1, NP, LANES)
        turned = pltpu.roll(shaped, 4, 1)
        turned = jnp.where((node & 2) == 0, pltpu.roll(turned, 6, 1), pltpu.roll(turned, 2, 1))
        turned = jnp.where((node & 1) == 0, pltpu.roll(turned, 7, 1), pltpu.roll(turned, 1, 1))
        values = jnp.where(flip[None], turned, shaped).reshape(values.shape)
        parts = [values[k * NODES : (k + 1) * NODES] for k in range(ARRAYS)]
        parts[2] = parts[2] * sign
        parts[5] = parts[5] * sign
        return parts

    strip = in_frame(both[:, :LANES])
    h, u, v, area, depth, spin, tide = in_frame(both[:, LANES:])
    edges = edge_values(table_ref, weight_ref, h, u, v, area, depth, spin, tide)
    east = jnp.where(second, east1, east0) != 0
    edges = [jnp.where(east, part[NODES - NP :], part[:NP]) for part in edges]
    out0_ref[...], out1_ref[...] = packed(jnp.concatenate(strip + edges, 0))


def rows_kernel(stored_ref, slot_ref, table_ref, weight_ref, out0_ref, out1_ref, sums):
    odd = lax.axis_index("blk") & 1

    def goes_up(lane):
        return jnp.where((lane & 64) != 0, odd, 1 - odd) != 0

    lane = lax.broadcasted_iota(i32, (8, 2 * LANES), 1)
    up = goes_up(lane)
    row = jnp.where(up, GY - RING, 0) + ((lane & 63) >> 4)
    row = jnp.where(lane >= LANES, jnp.where(up, GY - RING - 1, RING), row)
    both = picked(stored_ref[...], by_slot(slot_ref, (lane & 15) * GY + row))
    h, u, v, area, depth, spin, tide = [
        both[k * NODES : (k + 1) * NODES, LANES:] for k in range(ARRAYS)
    ]
    edges = edge_values(table_ref, weight_ref, h, u, v, area, depth, spin, tide)
    sums[...] = jnp.concatenate(edges, 0)
    north, south = row_edges(sums)
    up = goes_up(lax.broadcasted_iota(i32, (1, LANES), 1))
    rim = jnp.where(up, north, south)
    out0_ref[...], out1_ref[...] = packed(jnp.concatenate([both[:, :LANES], rim], 0))


def corners_kernel(
    in0_ref, in1_ref, table_ref, weight_ref, out0_ref, out1_ref, sums
):
    odd = lax.axis_index("blk") & 1
    whole = unpacked(in0_ref[...], in1_ref[...])
    parts = [whole[k * NODES : (k + 1) * NODES] for k in range(ARRAYS)]
    sums[...] = jnp.concatenate(edge_values(table_ref, weight_ref, *parts), 0)
    north, south = row_edges(sums)
    lane = lax.broadcasted_iota(i32, (1, LANES), 1)

    def squeezed(values, shift):
        return jnp.where(
            lane < 16,
            pltpu.roll(values, shift, 1) if shift else values,
            pltpu.roll(values, (shift + 80) % LANES, 1),
        )

    up = squeezed(jnp.concatenate([whole, pltpu.roll(north, 4, 1)], 0), 80)
    down = squeezed(jnp.concatenate([whole, pltpu.roll(south, LANES - 4, 1)], 0), 0)

    def in_fours(values):
        parts = [values[k * LANES : (k + 1) * LANES] for k in range(4)]
        out = parts[0]
        for k in range(1, 4):
            out = jnp.where(lane >= 32 * k, pltpu.roll(parts[k], 32 * k, 1), out)
        return out

    up, down = in_fours(up), in_fours(down)
    out0_ref[...] = jnp.where(odd != 0, down, up)
    out1_ref[...] = jnp.where(odd != 0, up, down)


def own_kernel(stored_ref, slot_ref, lanes_ref, own_ref, hot_ref):
    one_hot = by_slot(slot_ref, lanes_ref[0:8])
    own_ref[...] = picked(stored_ref[...], one_hot)
    hot_ref[...] = one_hot


def middle_kernel(
    block_cols, seam_ref, in0_ref, in1_ref, own_ref, lanes_ref, low_ref, centre_ref, high_ref
):
    east0, flip0, east1, flip1 = seam_flags(seam_ref, block_cols)
    whole = unpacked(in0_ref[...], in1_ref[...])
    side = lanes_ref[16:24]
    first_at = jnp.where(side == 2, 64 * (1 - east0), 64 * east0)
    place = jnp.where(side == 0, -1, lanes_ref[8:16] + first_at)
    placed = picked(whole, as_one_hot(place, LANES))
    for k, ref in enumerate((low_ref, centre_ref, high_ref)):
        part = slice(k * LANES, (k + 1) * LANES)
        ref[:ROWS] = placed[:ROWS, part] + own_ref[:, part]
        ref[ROWS:] = placed[ROWS:, part]


def steps_kernel(
    block_cols, seam_ref, rows0_ref, rows1_ref, corner0_ref, corner1_ref, low_ref, centre_ref,
    high_ref, hot_ref, table_ref, weight_ref, ext_ref, outer_ref, out_ref, sums,
):
    east0, flip0, east1, flip1 = seam_flags(seam_ref, block_cols)
    odd = lax.axis_index("blk") & 1
    block_y = lax.rem(lax.axis_index("blk"), BY)

    lane = lax.broadcasted_iota(i32, (1, LANES), 1)
    strips = unpacked(rows0_ref[...], rows1_ref[...])
    strips = jnp.concatenate(
        [strips[:ROWS], jnp.zeros((EDGE_ROWS, LANES), f32), strips[ROWS:]], 0
    )
    corner0, corner1 = corner0_ref[...], corner1_ref[...]
    corners = []
    for k in range(4):
        first = pltpu.roll(corner0, LANES - 32 * k, 1) if k else corner0
        other = pltpu.roll(corner1, (LANES + 32 - 32 * k) % LANES, 1) if k != 1 else corner1
        corners.append(jnp.where(lane < 32, first, other))
    around = jnp.concatenate([strips, jnp.concatenate(corners, 0)], 1)
    kind = outer_ref[8:16]
    sender = jnp.where(outer_ref[16:24] != 0, odd, 1 - odd)
    strip_at = jnp.where(kind == 3, 16 * (1 - east0), 16 * east0)
    place = outer_ref[0:8] + jnp.where(kind == 1, 64 * sender, 32 * sender + strip_at)
    outer = picked(around, as_one_hot(jnp.where(kind == 0, -1, place), 2 * LANES))
    tiles = (outer[:, :LANES], low_ref, centre_ref, high_ref, outer[:, LANES:])

    def rows_of(start, count):
        return jnp.concatenate([ref[start : start + count] for ref in tiles], 1)

    table = table_ref[...].astype(bf16)
    weight = jnp.concatenate([weight_ref[...]] * len(tiles), 1)
    at_rim = ext_ref[0:1] != 0
    top_row = jnp.where(block_y == BY - 1, ext_ref[1:2], 0) != 0
    bottom_row = jnp.where(block_y == 0, ext_ref[2:3], 0) != 0

    first_row = ext_ref[4:5] != 0
    last_row = ext_ref[5:6] != 0

    def edge_sum(parts, rims=None, rows=None):
        count = len(parts) * NP
        for c, part in enumerate(parts):
            west, east = part[:NP], part[NODES - NP :]
            at_east = pltpu.roll(west, EXT - 1, 1)
            at_west = pltpu.roll(east, 1, 1)
            if rims is not None:
                at_east = jnp.where(at_rim, rims[c], at_east)
                at_west = jnp.where(at_rim, rims[c], at_west)
            part = jnp.concatenate([west + at_west, part[NP : NODES - NP], east + at_east], 0)
            for k in range(len(tiles)):
                sums[k, c * NODES : (c + 1) * NODES] = part[:, k * LANES : (k + 1) * LANES]
        south_at, north_at = pl.ds(0, count, stride=NP), pl.ds(NP - 1, count, stride=NP)
        south = jnp.concatenate([sums[k, south_at] for k in range(len(tiles))], 1)
        north = jnp.concatenate([sums[k, north_at] for k in range(len(tiles))], 1)
        at_north = jnp.where(top_row, 0.0, pltpu.roll(south, EXT - PITCH, 1))
        at_south = jnp.where(bottom_row, 0.0, pltpu.roll(north, PITCH, 1))
        if rows is not None:
            at_north = jnp.where(last_row, rows, at_north)
            at_south = jnp.where(first_row, rows, at_south)
        to_north, to_south = north + at_north, south + at_south
        for k in range(len(tiles)):
            sums[k, south_at] = to_south[:, k * LANES : (k + 1) * LANES]
            sums[k, north_at] = to_north[:, k * LANES : (k + 1) * LANES]
        return [
            jnp.concatenate(
                [sums[k, c * NODES : (c + 1) * NODES] for k in range(len(tiles))], 1
            )
            for c in range(len(parts))
        ]

    start = [rows_of(c * NODES, NODES) for c in range(3)]
    area, depth, spin, tide = [rows_of(c * NODES, NODES) for c in range(3, ARRAYS)]
    root = jnp.sqrt(area)
    mass = weight * area
    mass_spin = mass * spin
    area_depth = root * depth
    rims = [rows_of(ROWS + c * NP, NP) for c in range(4)]
    blank = jnp.zeros((EDGE_ROWS, MID), f32)
    rows = jnp.concatenate([tiles[0][ALL_ROWS:], blank, tiles[-1][ALL_ROWS:]], 1)
    node = lax.broadcasted_iota(i32, (1, NP, 1), 1)
    east = pltpu.roll(rows, EXT - 1, 1).reshape(4, NP, EXT)
    west = pltpu.roll(rows, 1, 1).reshape(4, NP, EXT)
    rows = (
        rows.reshape(4, NP, EXT)
        + jnp.where(node == NP - 1, pltpu.roll(east, NP - 1, 1), 0.0)
        + jnp.where(node == 0, pltpu.roll(west, 1, 1), 0.0)
    ).reshape(EDGE_ROWS, EXT)
    per_mass = 1.0 / edge_sum([mass], rims[3:], rows[3 * NP :])[0]

    def average(parts, rims=None, rows=None):
        return [part * per_mass for part in edge_sum(parts, rims, rows)]

    def tendency(s):
        return mass_tendency(table, *s, tide, area_depth, root, mass_spin)

    def laplace(s):
        return [
            dot(table[3 * NODES :, : 3 * NODES], jnp.concatenate(high_low_high(part), 0))
            for part in s
        ]

    change = average(tendency(start), rims[:3], rows[: 3 * NP])
    one = [s + time_step * c for s, c in zip(start, change)]
    change = average(tendency(one))
    two = [0.75 * s + 0.25 * (o + time_step * c) for s, o, c in zip(start, one, change)]
    change = average(tendency(two))
    three = [s / 3.0 + 2.0 / 3.0 * (o + time_step * c) for s, o, c in zip(start, two, change)]
    biharmonic = average(laplace(average(laplace(three))))
    own = ext_ref[3:4, LANES : LANES + MID] != 0
    stepped = [
        jnp.where(
            own,
            (s - time_step * hyper_coeff * b)[:, LANES : LANES + MID],
            0.0,
        )
        for s, b in zip(three, biharmonic)
    ]
    stored = picked(jnp.concatenate(stepped, 0), hot_ref[...], dot_other)
    out_ref[...] = stored.reshape(out_ref.shape)


def on_device(fields, jacobian, water_depth, coriolis, tide_height, slot_of, seam_rows):
    block_cols = lax.axis_size("blk") // BY
    count = lax.axis_size("face") * lax.axis_size("blk")
    table, weight = operator_table()
    table, weight, lanes, ext, outer = map(jnp.asarray, (table, weight, *lane_tables()))
    vmem = pl.BlockSpec(memory_space=pltpu.VMEM)
    smem = pl.BlockSpec(memory_space=pltpu.SMEM)
    hbm = pl.BlockSpec(memory_space=pltpu.HBM)
    params = pltpu.CompilerParams(vmem_limit_bytes=48 * 2**20)
    held = (fields, jacobian, water_depth, coriolis, tide_height)

    def call(kernel, ins, outs, cost, scratch=(), name=None):
        return pl.pallas_call(
            kernel,
            out_shape=[jax.ShapeDtypeStruct(*out) for out in outs],
            in_specs=[spec for spec, value in ins],
            out_specs=[vmem] * len(outs),
            scratch_shapes=list(scratch),
            compiler_params=params,
            cost_estimate=pl.CostEstimate(
                flops=cost, bytes_accessed=2 * 2**20, transcendentals=0
            ),
            name=name,
        )(
            *[
                pltpu.with_memory_space_constraint(value, pltpu.HBM) if spec is hbm else value
                for spec, value in ins
            ]
        )

    strip = ((HALF_ROWS, LANES), f32)
    def room(values, spaces=None):
        spaces = spaces or [pltpu.VMEM] * len(values)
        buffers = [space(x.shape, x.dtype) for space, x in zip(spaces, values)]
        return buffers + [pltpu.SemaphoreType.DMA((len(values),))]

    needed = (seam_rows, slot_of, *held, table, weight)
    strip0, strip1, stored = call(
        functools.partial(strips_kernel, block_cols),
        [(hbm, x) for x in needed],
        [strip, strip, ((ROWS, ELEMENTS), f32)],
        10**8,
        scratch=room(needed, [pltpu.SMEM] + [pltpu.VMEM] * (len(needed) - 1)),
        name="strips",
    )
    span = block_cols * BY

    def rank(face, block_x, block_y):
        return face * span + block_x * BY + block_y

    both = ("face", "blk")
    places = [(f, x, y) for f in range(2) for x in range(block_cols) for y in range(BY)]
    if block_cols == 1:
        halo1 = lax.ppermute(
            strip1, both, [(rank(f, x, y), rank(1 - f, x, BY - 1 - y)) for f, x, y in places]
        )
        halo0 = lax.ppermute(
            strip0, both, [(rank(f, x, y), rank(1 - f, x, y)) for f, x, y in places]
        )
    else:
        last = block_cols - 1
        flipped = (seam_rows[:, 1] - seam_rows[:, 0]) % seam_rows.shape[1] != 1
        face = lax.axis_index("face")
        block_x = lax.axis_index("blk") // BY
        from_west = lax.ppermute(strip0, both, [(i, (i + BY) % count) for i in range(count)])
        from_east = lax.ppermute(strip1, both, [(i, (i - BY) % count) for i in range(count)])
        turned_west = lax.ppermute(
            strip0, both,
            [(rank(f, last, y), rank(1 - f, 0, BY - 1 - y)) for f in range(2) for y in range(BY)],
        )
        turned_east = lax.ppermute(
            strip1, both,
            [(rank(f, 0, y), rank(1 - f, last, BY - 1 - y)) for f in range(2) for y in range(BY)],
        )
        halo0 = jnp.where((block_x == last) & flipped[face], turned_east, from_east)
        halo1 = jnp.where((block_x == 0) & flipped[1 - face], turned_west, from_west)
    sums = [pltpu.VMEM((4 * NODES, LANES), f32)]
    rows0, rows1 = call(
        rows_kernel,
        [(vmem, x) for x in (stored, slot_of, table, weight)],
        [strip, strip],
        10**8,
        scratch=sums,
        name="rows",
    )

    def in_pair(y):
        return y ^ 1

    def next_pair(y):
        other = y + 1 if y % 2 else y - 1
        return other if 0 <= other < BY else y

    def swapped(value, partner):
        return lax.ppermute(
            value, both, [(rank(f, x, y), rank(f, x, partner(y))) for f, x, y in places]
        )

    from_rows1 = swapped(rows1, next_pair)
    from_rows0 = swapped(rows0, in_pair)
    own, hot = call(
        own_kernel,
        [(vmem, x) for x in (stored, slot_of, lanes)],
        [((ROWS, MID), f32), ((ELEMENTS, MID), bf16)],
        3 * 10**8,
        name="own",
    )
    corner = ((RIM_ROWS // 4, LANES), f32)
    corner0, corner1 = call(
        corners_kernel,
        [(vmem, x) for x in (halo0, halo1, table, weight)],
        [corner, corner],
        10**8,
        scratch=sums,
        name="corners",
    )
    from_corner1 = swapped(corner1, next_pair)
    from_corner0 = swapped(corner0, in_pair)
    tile = ((ALL_ROWS, LANES), f32)
    low, centre, high = call(
        functools.partial(middle_kernel, block_cols),
        [(smem, seam_rows)] + [(vmem, x) for x in (halo0, halo1, own, lanes)],
        [tile, tile, tile],
        10**8,
        name="middle",
    )
    (stepped,) = call(
        functools.partial(steps_kernel, block_cols),
        [(smem, seam_rows)]
        + [
            (vmem, x)
            for x in (
                from_rows0, from_rows1, from_corner0, from_corner1, low, centre, high,
                hot, table, weight, ext, outer,
            )
        ],
        [(fields.shape, f32)],
        10**9,
        scratch=[pltpu.VMEM((EXT // LANES, 3 * NODES, LANES), f32)],
        name="steps",
    )
    return stepped


def solution(mesh):
    return jax.shard_map(
        on_device,
        mesh=mesh,
        in_specs=(
            P(None, None, None, ("face", "blk")),
            P(None, None, ("face", "blk")),
            P(None, None, ("face", "blk")),
            P(None, None, ("face", "blk")),
            P(None, None, ("face", "blk")),
            P(("face", "blk"), None),
            P(),
        ),
        out_specs=P(None, None, None, ("face", "blk")),
        check_vma=False,
    )
```

```python
import functools
import math

import jax
import jax.numpy as jnp
import ml_dtypes
import numpy as np
from jax import lax
from jax.experimental import pallas as pl
from jax.experimental.pallas import tpu as pltpu
from jax.sharding import PartitionSpec as P

BY = 16
GX = 16
GY = 16
NP = 8
NODES = NP * NP
ARRAYS = 7
ROWS = ARRAYS * NODES
EDGE_ROWS = 4 * NP
ALL_ROWS = ROWS + EDGE_ROWS
HALF_ROWS = ALL_ROWS // 2
RING = 4
RIM_ROWS = ROWS + 2 * EDGE_ROWS
CORNER_ROWS = RIM_ROWS // 8
PITCH = GX + 2 * RING
MID = GY * PITCH
LANES = 128
EXT = MID + 2 * LANES
LEAD = LANES - RING * PITCH
ELEMENTS = GX * GY

time_step = 0.03
hyper_coeff = 0.0002

f32 = jnp.float32
bf16 = jnp.bfloat16
i32 = jnp.int32


def legendre_pair(location, degree):
    lower_value = 1.0
    upper_value = location
    for polynomial_order in range(2, degree + 1):
        lower_value, upper_value = (
            upper_value,
            (
                (2 * polynomial_order - 1) * location * upper_value
                - (polynomial_order - 1) * lower_value
            )
            / polynomial_order,
        )
    return (lower_value, upper_value)


def gll_tables(points):
    degree = points - 1
    locations = [-math.cos(math.pi * position / degree) for position in range(points)]
    for iteration in range(100):
        updated = []
        for location in locations:
            lower_value, upper_value = legendre_pair(location, degree)
            updated.append(
                location - (location * upper_value - lower_value) / ((degree + 1) * upper_value)
            )
        locations = updated
    locations[0] = -1.0
    locations[degree] = 1.0
    legendre_at = [legendre_pair(location, degree)[1] for location in locations]
    weights = [2.0 / (degree * (degree + 1) * value * value) for value in legendre_at]
    corner_value = degree * (degree + 1) / 4.0
    derivative = []
    for row_index in range(points):
        row_values = []
        for column_index in range(points):
            if row_index != column_index:
                row_values.append(
                    legendre_at[row_index]
                    / (legendre_at[column_index] * (locations[row_index] - locations[column_index]))
                )
            elif row_index == 0:
                row_values.append(-corner_value)
            elif row_index == degree:
                row_values.append(corner_value)
            else:
                row_values.append(0.0)
        derivative.append(row_values)
    return np.asarray(weights, np.float64), np.asarray(derivative, np.float64)


def in_three(matrix):
    high = matrix.astype(ml_dtypes.bfloat16)
    low = (matrix - high.astype(np.float64)).astype(ml_dtypes.bfloat16)
    return np.concatenate([high, high, low], 1)


def operator_table():
    weights, derivative = gll_tables(NP)
    eye = np.eye(NP)
    node_weight = np.outer(weights, weights).reshape(NODES, 1)
    along_x = node_weight * np.kron(derivative, eye)
    along_y = node_weight * np.kron(eye, derivative)
    second = derivative @ derivative
    both = node_weight * (np.kron(second, eye) + np.kron(eye, second))
    table = np.zeros((4 * NODES, 6 * NODES), ml_dtypes.bfloat16)
    table[:NODES, : 3 * NODES] = in_three(along_x)
    table[NODES : 2 * NODES, : 3 * NODES] = in_three(along_y)
    table[2 * NODES : 3 * NODES, : 3 * NODES] = in_three(along_x)
    table[2 * NODES : 3 * NODES, 3 * NODES :] = in_three(along_y)
    table[3 * NODES :, : 3 * NODES] = in_three(both)
    spread = np.broadcast_to(node_weight, (NODES, LANES)).astype(np.float32)
    return table.astype(np.float32), np.ascontiguousarray(spread)


def lane_tables():
    table = np.zeros((24, MID), np.int32)
    for lane in range(MID):
        row, col = divmod(lane, PITCH)
        x = col - RING
        own = 0 <= x < GX
        table[0:8, lane] = x * GY + row if own else -1
        if not own:
            table[8:16, lane] = row * RING + (col if x < 0 else x - GX)
        table[16:24, lane] = 0 if own else (1 if x < 0 else 2)
    ext = np.zeros((8, EXT), np.int32)
    outer = np.zeros((24, 2 * LANES), np.int32)
    for lane in range(EXT):
        row, col = divmod(lane - LEAD, PITCH)
        y = row - RING
        x = col - RING
        inside = 0 <= row < GY + 2 * RING
        ext[0, lane] = x in (-RING, GX + RING - 1)
        ext[1, lane] = y == GY - 1
        ext[2, lane] = y == 0
        ext[3, lane] = 0 <= y < GY and 0 <= x < GX
        ext[4, lane] = y == -RING
        ext[5, lane] = y == GY + RING - 1
        if inside and not 0 <= y < GY:
            place = lane if y < 0 else lane - LANES - MID + LANES
            step = y + RING if y < 0 else y - GY
            if 0 <= x < GX:
                outer[0:8, place] = step * GX + x
                outer[8:16, place] = 1
            else:
                outer[0:8, place] = LANES + step * RING + (x + RING if x < 0 else x - GX)
                outer[8:16, place] = 2 if x < 0 else 3
            outer[16:24, place] = y > 0
    return table, ext, outer


def exact_pieces(values):
    high = values.astype(bf16)
    rest = values - high.astype(f32)
    middle = rest.astype(bf16)
    low = (rest - middle.astype(f32)).astype(bf16)
    return high, middle, low


def dot(a, b):
    return jnp.dot(a, b, preferred_element_type=f32)


def dot_other(a, b):
    return lax.dot_general(a, b, (((1,), (1,)), ((), ())), preferred_element_type=f32)


def picked(values, one_hot, product=dot):
    high, middle, low = exact_pieces(values)
    return (product(high, one_hot) + product(middle, one_hot)) + product(low, one_hot)


def as_one_hot(row_of_lane, depth):
    index = lax.broadcasted_iota(i32, (depth, row_of_lane.shape[1]), 0)
    return jnp.where(index == row_of_lane[0:1], 1.0, 0.0).astype(bf16)


def high_low_high(values):
    high = values.astype(bf16)
    low = (values - high.astype(f32)).astype(bf16)
    return [high, low, high]


def by_slot(slot_ref, cell_of_lane):
    slots = jnp.broadcast_to(slot_ref[...], (8, ELEMENTS)).astype(f32).astype(bf16)
    chosen = dot(slots, as_one_hot(cell_of_lane, ELEMENTS))
    chosen = jnp.where(cell_of_lane >= 0, chosen, -1.0)
    index = lax.broadcasted_iota(i32, (ELEMENTS, cell_of_lane.shape[1]), 0).astype(f32)
    return jnp.where(index == chosen[0:1], 1.0, 0.0).astype(bf16)


def brought(sources, buffers, sems):
    copies = [
        pltpu.make_async_copy(source, buffer, sems.at[k])
        for k, (source, buffer) in enumerate(zip(sources, buffers))
    ]
    for copy in copies:
        copy.start()
    for copy in copies:
        copy.wait()


def stored_rows(fields_ref, others):
    parts = [fields_ref[...].reshape(3 * NODES, ELEMENTS)]
    parts += [ref[...].reshape(NODES, ELEMENTS) for ref in others]
    return jnp.concatenate(parts, 0)


def mass_tendency(table, h, u, v, tide, area_depth, weighted_area, spin):
    p = high_low_high(h - tide)
    slopes = dot(table[: 2 * NODES, : 3 * NODES], jnp.concatenate(p, 0))
    flux = high_low_high(area_depth * u) + high_low_high(area_depth * v)
    spread = dot(table[2 * NODES : 3 * NODES], jnp.concatenate(flux, 0))
    return [
        -spread,
        spin * v - weighted_area * slopes[:NODES],
        -spin * u - weighted_area * slopes[NODES:],
    ]


def edge_values(table_ref, weight_ref, h, u, v, area, depth, spin, tide):
    root = jnp.sqrt(area)
    mass = jnp.concatenate([weight_ref[...]] * (area.shape[1] // LANES), 1) * area
    table = table_ref[...].astype(bf16)
    return mass_tendency(table, h, u, v, tide, root * depth, root, mass * spin) + [mass]


def row_edges(sums):
    return sums[pl.ds(NP - 1, EDGE_ROWS, stride=NP)], sums[pl.ds(0, EDGE_ROWS, stride=NP)]


def beside(left, right):
    return jnp.concatenate([left, right], 1)


def with_row_rim(whole, sums, top):
    north, south = row_edges(sums)
    rim = jnp.where(top, pltpu.roll(north, RING, 1), pltpu.roll(south, LANES - RING, 1))
    return jnp.concatenate([whole, rim], 0)


def corner_of(whole, start, top):
    lane = lax.broadcasted_iota(i32, (1, LANES), 1)
    base = LANES - start - jnp.where(top != 0, 48, 0)
    out = None
    for k in range(RIM_ROWS // CORNER_ROWS):
        part = whole[k * CORNER_ROWS : (k + 1) * CORNER_ROWS]
        part = pltpu.roll(part, (base + 16 * k) & (LANES - 1), 1)
        out = part if k == 0 else jnp.where(lane >= 16 * k, part, out)
    return out


def packed(whole):
    second = lax.broadcasted_iota(i32, (1, LANES), 1) >= 64
    top, bottom = whole[:HALF_ROWS], whole[HALF_ROWS:]
    return (
        jnp.where(second, pltpu.roll(bottom, 64, 1), top),
        jnp.where(second, bottom, pltpu.roll(top, 64, 1)),
    )


def unpacked(in0, in1):
    second = lax.broadcasted_iota(i32, (1, LANES), 1) >= 64
    top = jnp.where(second, pltpu.roll(in1, 64, 1), in0)
    bottom = jnp.where(second, in1, pltpu.roll(in0, 64, 1))
    return jnp.concatenate([top, bottom], 0)


def seam_flags(seam_ref, block_cols):
    size_y = seam_ref.shape[1]
    face = lax.axis_index("face")
    blk = lax.axis_index("blk")
    block_x = blk // BY

    def flipped(k):
        return jnp.where(lax.rem(seam_ref[k, 1] - seam_ref[k, 0] + size_y, size_y) != 1, 1, 0)

    first, second = flipped(0), flipped(1)
    east_flip = jnp.where(face == 0, first, second)
    west_flip = jnp.where(face == 0, second, first)
    if block_cols == 1:
        return 1 - east_flip, 0, east_flip, 1
    at_east = jnp.where(block_x == block_cols - 1, east_flip, 0)
    at_west = jnp.where(block_x == 0, west_flip, 0)
    return 1, at_east, 0, at_west


def strips_kernel(block_cols, *refs):
    sources, (out1_ref, far1_ref, out0_ref, far0_ref, stored_ref) = refs[:9], refs[9:14]
    buffers, sems, sums = refs[14:23], refs[23], refs[24]
    brought(sources, buffers, sems)
    seam_ref, slot_ref, fields_ref, area_ref, depth_ref, spin_ref, tide_ref = buffers[:7]
    table_ref, weight_ref = buffers[7:]
    east0, flip0, east1, flip1 = seam_flags(seam_ref, block_cols)
    lane = lax.broadcasted_iota(i32, (8, 2 * LANES), 1)
    second = (lane & 64) != 0
    place = lane & 63
    row = place >> 2
    row = jnp.where(jnp.where(second, flip1, flip0) != 0, GY - 1 - row, row)
    east = jnp.where(second, east1, east0) != 0
    col = jnp.where(east, GX - RING, 0) + (place & 3)
    col = jnp.where(lane >= LANES, jnp.where(east, GX - RING - 1, RING), col)
    one_hot = by_slot(slot_ref, col * GY + row)
    stored = stored_rows(fields_ref, (area_ref, depth_ref, spin_ref, tide_ref))
    stored_ref[...] = stored
    both = picked(stored, one_hot)

    lane = lax.broadcasted_iota(i32, (1, LANES), 1)
    second = lane >= 64
    flip = jnp.where(second, flip1, flip0) != 0
    sign = jnp.where(flip, -1.0, 1.0)
    node = lax.broadcasted_iota(i32, (1, NP, 1), 1)

    def in_frame(values):
        shaped = values.reshape(-1, NP, LANES)
        turned = pltpu.roll(shaped, 4, 1)
        turned = jnp.where((node & 2) == 0, pltpu.roll(turned, 6, 1), pltpu.roll(turned, 2, 1))
        turned = jnp.where((node & 1) == 0, pltpu.roll(turned, 7, 1), pltpu.roll(turned, 1, 1))
        values = jnp.where(flip[None], turned, shaped).reshape(values.shape)
        parts = [values[k * NODES : (k + 1) * NODES] for k in range(ARRAYS)]
        parts[2] = parts[2] * sign
        parts[5] = parts[5] * sign
        return parts

    strip, ring = in_frame(both[:, :LANES]), in_frame(both[:, LANES:])
    edges = edge_values(table_ref, weight_ref, *map(beside, strip, ring))
    east = jnp.where(second, east1, east0) != 0
    ends = [jnp.where(east, part[NODES - NP :, LANES:], part[:NP, LANES:]) for part in edges]
    whole = jnp.concatenate(strip + ends, 0)
    out0_ref[...], out1_ref[...] = packed(whole)
    odd = lax.axis_index("blk") & 1
    sums[...] = jnp.concatenate([part[:, :LANES] for part in edges], 0)
    top0, top1 = odd ^ flip0, odd ^ flip1
    whole = with_row_rim(whole, sums, jnp.where(second, top1, top0) != 0)
    far0_ref[...] = corner_of(whole, 0, top0)
    far1_ref[...] = corner_of(whole, 64, top1)


def rows_kernel(stored_ref, slot_ref, table_ref, weight_ref, out0_ref, out1_ref, sums):
    odd = lax.axis_index("blk") & 1

    def goes_up(lane):
        return jnp.where((lane & 64) != 0, odd, 1 - odd) != 0

    lane = lax.broadcasted_iota(i32, (8, 2 * LANES), 1)
    up = goes_up(lane)
    row = jnp.where(up, GY - RING, 0) + ((lane & 63) >> 4)
    row = jnp.where(lane >= LANES, jnp.where(up, GY - RING - 1, RING), row)
    both = picked(stored_ref[...], by_slot(slot_ref, (lane & 15) * GY + row))
    h, u, v, area, depth, spin, tide = [
        both[k * NODES : (k + 1) * NODES, LANES:] for k in range(ARRAYS)
    ]
    edges = edge_values(table_ref, weight_ref, h, u, v, area, depth, spin, tide)
    sums[...] = jnp.concatenate(edges, 0)
    north, south = row_edges(sums)
    up = goes_up(lax.broadcasted_iota(i32, (1, LANES), 1))
    rim = jnp.where(up, north, south)
    out0_ref[...], out1_ref[...] = packed(jnp.concatenate([both[:, :LANES], rim], 0))


def corners_kernel(in1_ref, in0_ref, table_ref, weight_ref, *refs):
    out_ref, sums = refs[-2:]
    top = 1 - (lax.axis_index("blk") & 1)
    whole = unpacked(in0_ref[...], in1_ref[...])
    parts = [whole[k * NODES : (k + 1) * NODES] for k in range(ARRAYS)]
    sums[...] = jnp.concatenate(edge_values(table_ref, weight_ref, *parts), 0)
    whole = with_row_rim(whole, sums, jnp.broadcast_to(top != 0, (1, LANES)))
    out_ref[:CORNER_ROWS] = corner_of(whole, 0, top)
    out_ref[CORNER_ROWS:] = corner_of(whole, 64, top)


def own_kernel(stored_ref, slot_ref, lanes_ref, own_ref, hot_ref):
    one_hot = by_slot(slot_ref, lanes_ref[0:8])
    own_ref[...] = picked(stored_ref[...], one_hot)
    hot_ref[...] = one_hot


def middle_kernel(
    block_cols, seam_ref, in0_ref, in1_ref, own_ref, lanes_ref, low_ref, centre_ref, high_ref
):
    east0, flip0, east1, flip1 = seam_flags(seam_ref, block_cols)
    whole = unpacked(in0_ref[...], in1_ref[...])
    side = lanes_ref[16:24]
    first_at = jnp.where(side == 2, 64 * (1 - east0), 64 * east0)
    place = jnp.where(side == 0, -1, lanes_ref[8:16] + first_at)
    placed = picked(whole, as_one_hot(place, LANES))
    for k, ref in enumerate((low_ref, centre_ref, high_ref)):
        part = slice(k * LANES, (k + 1) * LANES)
        ref[:ROWS] = placed[:ROWS, part] + own_ref[:, part]
        ref[ROWS:] = placed[ROWS:, part]


def steps_kernel(
    block_cols, seam_ref, rows0_ref, rows1_ref, near_ref, far0_ref, far1_ref, low_ref,
    centre_ref, high_ref, hot_ref, table_ref, weight_ref, ext_ref, outer_ref, out_ref, sums,
):
    east0, flip0, east1, flip1 = seam_flags(seam_ref, block_cols)
    odd = lax.axis_index("blk") & 1
    block_y = lax.rem(lax.axis_index("blk"), BY)

    lane = lax.broadcasted_iota(i32, (1, LANES), 1)
    strips = unpacked(rows0_ref[...], rows1_ref[...])
    strips = jnp.concatenate(
        [strips[:ROWS], jnp.zeros((EDGE_ROWS, LANES), f32), strips[ROWS:]], 0
    )
    near = near_ref[...]
    sources = (near[:CORNER_ROWS], near[CORNER_ROWS:], far0_ref[...], far1_ref[...])
    corners = []
    for k in range(RIM_ROWS // CORNER_ROWS):
        rows = None
        for n, source in enumerate(sources):
            shift = 16 * (n - k) % LANES
            part = pltpu.roll(source, shift, 1) if shift else source
            rows = part if n == 0 else jnp.where(lane >= 16 * n, part, rows)
        corners.append(rows)
    around = jnp.concatenate([strips, jnp.concatenate(corners, 0)], 1)
    kind = outer_ref[8:16]
    sender = jnp.where(outer_ref[16:24] != 0, odd, 1 - odd)
    strip_at = jnp.where(kind == 3, 16 * (1 - east0), 16 * east0)
    place = outer_ref[0:8] + jnp.where(kind == 1, 64 * sender, 32 * sender + strip_at)
    outer = picked(around, as_one_hot(jnp.where(kind == 0, -1, place), 2 * LANES))
    tiles = (outer[:, :LANES], low_ref, centre_ref, high_ref, outer[:, LANES:])

    def rows_of(start, count):
        return jnp.concatenate([ref[start : start + count] for ref in tiles], 1)

    table = table_ref[...].astype(bf16)
    weight = jnp.concatenate([weight_ref[...]] * len(tiles), 1)
    at_rim = ext_ref[0:1] != 0
    top_row = jnp.where(block_y == BY - 1, ext_ref[1:2], 0) != 0
    bottom_row = jnp.where(block_y == 0, ext_ref[2:3], 0) != 0

    first_row = ext_ref[4:5] != 0
    last_row = ext_ref[5:6] != 0

    def edge_sum(parts, rims=None, rows=None):
        count = len(parts) * NP
        for c, part in enumerate(parts):
            west, east = part[:NP], part[NODES - NP :]
            at_east = pltpu.roll(west, EXT - 1, 1)
            at_west = pltpu.roll(east, 1, 1)
            if rims is not None:
                at_east = jnp.where(at_rim, rims[c], at_east)
                at_west = jnp.where(at_rim, rims[c], at_west)
            part = jnp.concatenate([west + at_west, part[NP : NODES - NP], east + at_east], 0)
            for k in range(len(tiles)):
                sums[k, c * NODES : (c + 1) * NODES] = part[:, k * LANES : (k + 1) * LANES]
        south_at, north_at = pl.ds(0, count, stride=NP), pl.ds(NP - 1, count, stride=NP)
        south = jnp.concatenate([sums[k, south_at] for k in range(len(tiles))], 1)
        north = jnp.concatenate([sums[k, north_at] for k in range(len(tiles))], 1)
        at_north = jnp.where(top_row, 0.0, pltpu.roll(south, EXT - PITCH, 1))
        at_south = jnp.where(bottom_row, 0.0, pltpu.roll(north, PITCH, 1))
        if rows is not None:
            at_north = jnp.where(last_row, rows, at_north)
            at_south = jnp.where(first_row, rows, at_south)
        to_north, to_south = north + at_north, south + at_south
        for k in range(len(tiles)):
            sums[k, south_at] = to_south[:, k * LANES : (k + 1) * LANES]
            sums[k, north_at] = to_north[:, k * LANES : (k + 1) * LANES]
        return [
            jnp.concatenate(
                [sums[k, c * NODES : (c + 1) * NODES] for k in range(len(tiles))], 1
            )
            for c in range(len(parts))
        ]

    start = [rows_of(c * NODES, NODES) for c in range(3)]
    area, depth, spin, tide = [rows_of(c * NODES, NODES) for c in range(3, ARRAYS)]
    root = jnp.sqrt(area)
    mass = weight * area
    mass_spin = mass * spin
    area_depth = root * depth
    rims = [rows_of(ROWS + c * NP, NP) for c in range(4)]
    blank = jnp.zeros((EDGE_ROWS, MID), f32)
    rows = jnp.concatenate([tiles[0][ALL_ROWS:], blank, tiles[-1][ALL_ROWS:]], 1)
    node = lax.broadcasted_iota(i32, (1, NP, 1), 1)
    east = pltpu.roll(rows, EXT - 1, 1).reshape(4, NP, EXT)
    west = pltpu.roll(rows, 1, 1).reshape(4, NP, EXT)
    rows = (
        rows.reshape(4, NP, EXT)
        + jnp.where(node == NP - 1, pltpu.roll(east, NP - 1, 1), 0.0)
        + jnp.where(node == 0, pltpu.roll(west, 1, 1), 0.0)
    ).reshape(EDGE_ROWS, EXT)
    per_mass = 1.0 / edge_sum([mass], rims[3:], rows[3 * NP :])[0]

    def average(parts, rims=None, rows=None):
        return [part * per_mass for part in edge_sum(parts, rims, rows)]

    def tendency(s):
        return mass_tendency(table, *s, tide, area_depth, root, mass_spin)

    def laplace(s):
        return [
            dot(table[3 * NODES :, : 3 * NODES], jnp.concatenate(high_low_high(part), 0))
            for part in s
        ]

    change = average(tendency(start), rims[:3], rows[: 3 * NP])
    one = [s + time_step * c for s, c in zip(start, change)]
    change = average(tendency(one))
    two = [0.75 * s + 0.25 * (o + time_step * c) for s, o, c in zip(start, one, change)]
    change = average(tendency(two))
    three = [s / 3.0 + 2.0 / 3.0 * (o + time_step * c) for s, o, c in zip(start, two, change)]
    biharmonic = average(laplace(average(laplace(three))))
    own = ext_ref[3:4, LANES : LANES + MID] != 0
    stepped = [
        jnp.where(
            own,
            (s - time_step * hyper_coeff * b)[:, LANES : LANES + MID],
            0.0,
        )
        for s, b in zip(three, biharmonic)
    ]
    stored = picked(jnp.concatenate(stepped, 0), hot_ref[...], dot_other)
    out_ref[...] = stored.reshape(out_ref.shape)


def on_device(fields, jacobian, water_depth, coriolis, tide_height, slot_of, seam_rows):
    block_cols = lax.axis_size("blk") // BY
    table, weight = operator_table()
    table, weight, lanes, ext, outer = map(jnp.asarray, (table, weight, *lane_tables()))
    vmem = pl.BlockSpec(memory_space=pltpu.VMEM)
    smem = pl.BlockSpec(memory_space=pltpu.SMEM)
    hbm = pl.BlockSpec(memory_space=pltpu.HBM)
    params = pltpu.CompilerParams(vmem_limit_bytes=48 * 2**20)
    held = (fields, jacobian, water_depth, coriolis, tide_height)

    def call(kernel, ins, outs, cost, scratch=(), name=None):
        return pl.pallas_call(
            kernel,
            out_shape=[jax.ShapeDtypeStruct(*out) for out in outs],
            in_specs=[spec for spec, value in ins],
            out_specs=[vmem] * len(outs),
            scratch_shapes=list(scratch),
            compiler_params=params,
            cost_estimate=pl.CostEstimate(
                flops=cost, bytes_accessed=2 * 2**20, transcendentals=0
            ),
            name=name,
        )(
            *[
                pltpu.with_memory_space_constraint(value, pltpu.HBM) if spec is hbm else value
                for spec, value in ins
            ]
        )

    strip = ((HALF_ROWS, LANES), f32)
    def room(values, spaces=None):
        spaces = spaces or [pltpu.VMEM] * len(values)
        buffers = [space(x.shape, x.dtype) for space, x in zip(spaces, values)]
        return buffers + [pltpu.SemaphoreType.DMA((len(values),))]

    needed = (seam_rows, slot_of, *held, table, weight)
    corner = ((CORNER_ROWS, LANES), f32)
    sums = [pltpu.VMEM((4 * NODES, LANES), f32)]
    strip1, corner1, strip0, corner0, stored = call(
        functools.partial(strips_kernel, block_cols),
        [(hbm, x) for x in needed],
        [strip, corner, strip, corner, ((ROWS, ELEMENTS), f32)],
        10**8,
        scratch=room(needed, [pltpu.SMEM] + [pltpu.VMEM] * (len(needed) - 1)) + sums,
        name="strips",
    )
    span = block_cols * BY
    both = ("face", "blk")
    places = [(f, x, y) for f in range(2) for x in range(block_cols) for y in range(BY)]

    def rank(face, block_x, block_y):
        return face * span + block_x * BY + block_y

    def same(y):
        return y

    def in_pair(y):
        return y ^ 1

    def next_pair(y):
        other = y + 1 if y % 2 else y - 1
        return other if 0 <= other < BY else y

    def swapped(value, partner):
        return lax.ppermute(
            value, both, [(rank(f, x, y), rank(f, x, partner(y))) for f, x, y in places]
        )

    def across(value0, value1, partner):
        last = block_cols - 1
        straight = {
            (f, x, y): (f, x + 1, partner(y)) if x < last else (1 - f, 0, partner(y))
            for f, x, y in places
        }
        turned = {
            (f, last, y): (1 - f, 0, BY - 1 - partner(y)) for f in range(2) for y in range(BY)
        }

        def eastward(value, pairs):
            return lax.ppermute(value, both, [(rank(*a), rank(*b)) for a, b in pairs.items()])

        def westward(value, pairs):
            return lax.ppermute(value, both, [(rank(*b), rank(*a)) for a, b in pairs.items()])

        if block_cols == 1:
            return eastward(value0, straight), eastward(value1, turned)
        flipped = (seam_rows[:, 1] - seam_rows[:, 0]) % seam_rows.shape[1] != 1
        face = lax.axis_index("face")
        block_x = lax.axis_index("blk") // BY
        return (
            jnp.where(
                (block_x == last) & flipped[face],
                westward(value1, turned),
                westward(value1, straight),
            ),
            jnp.where(
                (block_x == 0) & flipped[1 - face],
                eastward(value0, turned),
                eastward(value0, straight),
            ),
        )

    halo0, halo1 = across(strip0, strip1, same)
    far0, far1 = across(corner0, corner1, next_pair)
    rows0, rows1 = call(
        rows_kernel,
        [(vmem, x) for x in (stored, slot_of, table, weight)],
        [strip, strip],
        10**8,
        scratch=sums,
        name="rows",
    )
    from_rows1 = swapped(rows1, next_pair)
    from_rows0 = swapped(rows0, in_pair)
    own, hot = call(
        own_kernel,
        [(vmem, x) for x in (stored, slot_of, lanes)],
        [((ROWS, MID), f32), ((ELEMENTS, MID), bf16)],
        3 * 10**8,
        name="own",
    )
    (near,) = call(
        corners_kernel,
        [(vmem, x) for x in (halo1, halo0, table, weight, hot, far1, far0)],
        [((2 * CORNER_ROWS, LANES), f32)],
        10**8,
        scratch=sums,
        name="corners",
    )
    near = swapped(near, in_pair)
    tile = ((ALL_ROWS, LANES), f32)
    low, centre, high = call(
        functools.partial(middle_kernel, block_cols),
        [(smem, seam_rows)] + [(vmem, x) for x in (halo0, halo1, own, lanes)],
        [tile, tile, tile],
        10**8,
        name="middle",
    )
    (stepped,) = call(
        functools.partial(steps_kernel, block_cols),
        [(smem, seam_rows)]
        + [
            (vmem, x)
            for x in (
                from_rows0, from_rows1, near, far0, far1, low, centre, high,
                hot, table, weight, ext, outer,
            )
        ],
        [(fields.shape, f32)],
        10**9,
        scratch=[pltpu.VMEM((EXT // LANES, 3 * NODES, LANES), f32)],
        name="steps",
    )
    return stepped


def solution(mesh):
    return jax.shard_map(
        on_device,
        mesh=mesh,
        in_specs=(
            P(None, None, None, ("face", "blk")),
            P(None, None, ("face", "blk")),
            P(None, None, ("face", "blk")),
            P(None, None, ("face", "blk")),
            P(None, None, ("face", "blk")),
            P(("face", "blk"), None),
            P(),
        ),
        out_specs=P(None, None, None, ("face", "blk")),
        check_vma=False,
    )
```

```python
import functools
import math

import jax
import jax.numpy as jnp
import ml_dtypes
import numpy as np
from jax import lax
from jax.experimental import pallas as pl
from jax.experimental.pallas import tpu as pltpu
from jax.sharding import PartitionSpec as P

BY = 16
GX = 16
GY = 16
NP = 8
NODES = NP * NP
ARRAYS = 7
ROWS = ARRAYS * NODES
EDGE_ROWS = 4 * NP
ALL_ROWS = ROWS + EDGE_ROWS
HALF_ROWS = ALL_ROWS // 2
RING = 4
RIM_ROWS = ROWS + 2 * EDGE_ROWS
CORNER_ROWS = RIM_ROWS // 8
PITCH = GX + 2 * RING
MID = GY * PITCH
LANES = 128
EXT = MID + 2 * LANES
LEAD = LANES - RING * PITCH
ELEMENTS = GX * GY

time_step = 0.03
hyper_coeff = 0.0002

f32 = jnp.float32
bf16 = jnp.bfloat16
i32 = jnp.int32


def legendre_pair(location, degree):
    lower_value = 1.0
    upper_value = location
    for polynomial_order in range(2, degree + 1):
        lower_value, upper_value = (
            upper_value,
            (
                (2 * polynomial_order - 1) * location * upper_value
                - (polynomial_order - 1) * lower_value
            )
            / polynomial_order,
        )
    return (lower_value, upper_value)


def gll_tables(points):
    degree = points - 1
    locations = [-math.cos(math.pi * position / degree) for position in range(points)]
    for iteration in range(100):
        updated = []
        for location in locations:
            lower_value, upper_value = legendre_pair(location, degree)
            updated.append(
                location - (location * upper_value - lower_value) / ((degree + 1) * upper_value)
            )
        locations = updated
    locations[0] = -1.0
    locations[degree] = 1.0
    legendre_at = [legendre_pair(location, degree)[1] for location in locations]
    weights = [2.0 / (degree * (degree + 1) * value * value) for value in legendre_at]
    corner_value = degree * (degree + 1) / 4.0
    derivative = []
    for row_index in range(points):
        row_values = []
        for column_index in range(points):
            if row_index != column_index:
                row_values.append(
                    legendre_at[row_index]
                    / (legendre_at[column_index] * (locations[row_index] - locations[column_index]))
                )
            elif row_index == 0:
                row_values.append(-corner_value)
            elif row_index == degree:
                row_values.append(corner_value)
            else:
                row_values.append(0.0)
        derivative.append(row_values)
    return np.asarray(weights, np.float64), np.asarray(derivative, np.float64)


def in_three(matrix):
    high = matrix.astype(ml_dtypes.bfloat16)
    low = (matrix - high.astype(np.float64)).astype(ml_dtypes.bfloat16)
    return np.concatenate([high, high, low], 1)


def operator_table():
    weights, derivative = gll_tables(NP)
    eye = np.eye(NP)
    node_weight = np.outer(weights, weights).reshape(NODES, 1)
    along_x = node_weight * np.kron(derivative, eye)
    along_y = node_weight * np.kron(eye, derivative)
    second = derivative @ derivative
    both = node_weight * (np.kron(second, eye) + np.kron(eye, second))
    table = np.zeros((4 * NODES, 6 * NODES), ml_dtypes.bfloat16)
    table[:NODES, : 3 * NODES] = in_three(along_x)
    table[NODES : 2 * NODES, : 3 * NODES] = in_three(along_y)
    table[2 * NODES : 3 * NODES, : 3 * NODES] = in_three(along_x)
    table[2 * NODES : 3 * NODES, 3 * NODES :] = in_three(along_y)
    table[3 * NODES :, : 3 * NODES] = in_three(both)
    spread = np.broadcast_to(node_weight, (NODES, LANES)).astype(np.float32)
    return table.astype(np.float32), np.ascontiguousarray(spread)


def lane_tables():
    table = np.zeros((24, MID), np.int32)
    for lane in range(MID):
        row, col = divmod(lane, PITCH)
        x = col - RING
        own = 0 <= x < GX
        table[0:8, lane] = x * GY + row if own else -1
        if not own:
            table[8:16, lane] = row * RING + (col if x < 0 else x - GX)
        table[16:24, lane] = 0 if own else (1 if x < 0 else 2)
    ext = np.zeros((8, EXT), np.int32)
    outer = np.zeros((24, 2 * LANES), np.int32)
    for lane in range(EXT):
        row, col = divmod(lane - LEAD, PITCH)
        y = row - RING
        x = col - RING
        inside = 0 <= row < GY + 2 * RING
        ext[0, lane] = x in (-RING, GX + RING - 1)
        ext[1, lane] = y == GY - 1
        ext[2, lane] = y == 0
        ext[3, lane] = 0 <= y < GY and 0 <= x < GX
        ext[4, lane] = y == -RING
        ext[5, lane] = y == GY + RING - 1
        if inside and not 0 <= y < GY:
            place = lane if y < 0 else lane - LANES - MID + LANES
            step = y + RING if y < 0 else y - GY
            if 0 <= x < GX:
                outer[0:8, place] = step * GX + x
                outer[8:16, place] = 1
            else:
                outer[0:8, place] = LANES + step * RING + (x + RING if x < 0 else x - GX)
                outer[8:16, place] = 2 if x < 0 else 3
            outer[16:24, place] = y > 0
    return table, ext, outer


def exact_pieces(values):
    high = values.astype(bf16)
    rest = values - high.astype(f32)
    middle = rest.astype(bf16)
    low = (rest - middle.astype(f32)).astype(bf16)
    return high, middle, low


def dot(a, b):
    return jnp.dot(a, b, preferred_element_type=f32)


def dot_other(a, b):
    return lax.dot_general(a, b, (((1,), (1,)), ((), ())), preferred_element_type=f32)


def picked(values, one_hot, product=dot):
    high, middle, low = exact_pieces(values)
    return (product(high, one_hot) + product(middle, one_hot)) + product(low, one_hot)


def as_one_hot(row_of_lane, depth):
    index = lax.broadcasted_iota(i32, (depth, row_of_lane.shape[1]), 0)
    return jnp.where(index == row_of_lane[0:1], 1.0, 0.0).astype(bf16)


def high_low_high(values):
    high = values.astype(bf16)
    low = (values - high.astype(f32)).astype(bf16)
    return [high, low, high]


def by_slot(slot_ref, cell_of_lane):
    slots = jnp.broadcast_to(slot_ref[...], (8, ELEMENTS)).astype(f32).astype(bf16)
    chosen = dot(slots, as_one_hot(cell_of_lane, ELEMENTS))
    chosen = jnp.where(cell_of_lane >= 0, chosen, -1.0)
    index = lax.broadcasted_iota(i32, (ELEMENTS, cell_of_lane.shape[1]), 0).astype(f32)
    return jnp.where(index == chosen[0:1], 1.0, 0.0).astype(bf16)


def brought(sources, buffers, sems):
    copies = [
        pltpu.make_async_copy(source, buffer, sems.at[k])
        for k, (source, buffer) in enumerate(zip(sources, buffers))
    ]
    for copy in copies:
        copy.start()
    for copy in copies:
        copy.wait()


def stored_rows(fields_ref, others):
    parts = [fields_ref[...].reshape(3 * NODES, ELEMENTS)]
    parts += [ref[...].reshape(NODES, ELEMENTS) for ref in others]
    return jnp.concatenate(parts, 0)


def mass_tendency(table, h, u, v, tide, area_depth, weighted_area, spin):
    p = high_low_high(h - tide)
    slopes = dot(table[: 2 * NODES, : 3 * NODES], jnp.concatenate(p, 0))
    flux = high_low_high(area_depth * u) + high_low_high(area_depth * v)
    spread = dot(table[2 * NODES : 3 * NODES], jnp.concatenate(flux, 0))
    return [
        -spread,
        spin * v - weighted_area * slopes[:NODES],
        -spin * u - weighted_area * slopes[NODES:],
    ]


def edge_values(table_ref, weight_ref, h, u, v, area, depth, spin, tide):
    root = jnp.sqrt(area)
    mass = jnp.concatenate([weight_ref[...]] * (area.shape[1] // LANES), 1) * area
    table = table_ref[...].astype(bf16)
    return mass_tendency(table, h, u, v, tide, root * depth, root, mass * spin) + [mass]


def row_edges(sums, tile):
    return tuple(sums[tile, pl.ds(j, EDGE_ROWS, stride=NP)] for j in (NP - 1, 0))


def beside(left, right):
    return jnp.concatenate([left, right], 1)


def with_row_rim(whole, sums, top):
    north, south = row_edges(sums, 0)
    rim = jnp.where(top, pltpu.roll(north, RING, 1), pltpu.roll(south, LANES - RING, 1))
    return jnp.concatenate([whole, rim], 0)


def corner_of(whole, start, top):
    lane = lax.broadcasted_iota(i32, (1, LANES), 1)
    base = LANES - start - jnp.where(top != 0, 48, 0)
    out = None
    for k in range(RIM_ROWS // CORNER_ROWS):
        part = whole[k * CORNER_ROWS : (k + 1) * CORNER_ROWS]
        part = pltpu.roll(part, (base + 16 * k) & (LANES - 1), 1)
        out = part if k == 0 else jnp.where(lane >= 16 * k, part, out)
    return out


def packed(whole):
    second = lax.broadcasted_iota(i32, (1, LANES), 1) >= 64
    top, bottom = whole[:HALF_ROWS], whole[HALF_ROWS:]
    return (
        jnp.where(second, pltpu.roll(bottom, 64, 1), top),
        jnp.where(second, bottom, pltpu.roll(top, 64, 1)),
    )


def unpacked(in0, in1):
    second = lax.broadcasted_iota(i32, (1, LANES), 1) >= 64
    top = jnp.where(second, pltpu.roll(in1, 64, 1), in0)
    bottom = jnp.where(second, in1, pltpu.roll(in0, 64, 1))
    return jnp.concatenate([top, bottom], 0)


def seam_flags(seam_ref, block_cols):
    size_y = seam_ref.shape[1]
    face = lax.axis_index("face")
    blk = lax.axis_index("blk")
    block_x = blk // BY

    def flipped(k):
        return jnp.where(lax.rem(seam_ref[k, 1] - seam_ref[k, 0] + size_y, size_y) != 1, 1, 0)

    first, second = flipped(0), flipped(1)
    east_flip = jnp.where(face == 0, first, second)
    west_flip = jnp.where(face == 0, second, first)
    if block_cols == 1:
        return 1 - east_flip, 0, east_flip, 1
    at_east = jnp.where(block_x == block_cols - 1, east_flip, 0)
    at_west = jnp.where(block_x == 0, west_flip, 0)
    return 1, at_east, 0, at_west


def strips_kernel(block_cols, *refs):
    sources, (out1_ref, out0_ref, stored_ref) = refs[:9], refs[9:12]
    buffers, sems = refs[12:21], refs[21]
    brought(sources, buffers, sems)
    seam_ref, slot_ref, fields_ref, area_ref, depth_ref, spin_ref, tide_ref = buffers[:7]
    table_ref, weight_ref = buffers[7:]
    east0, flip0, east1, flip1 = seam_flags(seam_ref, block_cols)
    lane = lax.broadcasted_iota(i32, (8, 2 * LANES), 1)
    second = (lane & 64) != 0
    place = lane & 63
    row = place >> 2
    row = jnp.where(jnp.where(second, flip1, flip0) != 0, GY - 1 - row, row)
    east = jnp.where(second, east1, east0) != 0
    col = jnp.where(east, GX - RING, 0) + (place & 3)
    col = jnp.where(lane >= LANES, jnp.where(east, GX - RING - 1, RING), col)
    one_hot = by_slot(slot_ref, col * GY + row)
    stored = stored_rows(fields_ref, (area_ref, depth_ref, spin_ref, tide_ref))
    stored_ref[...] = stored
    both = picked(stored, one_hot)

    lane = lax.broadcasted_iota(i32, (1, LANES), 1)
    second = lane >= 64
    flip = jnp.where(second, flip1, flip0) != 0
    sign = jnp.where(flip, -1.0, 1.0)
    node = lax.broadcasted_iota(i32, (1, NP, 1), 1)

    def in_frame(values):
        shaped = values.reshape(-1, NP, LANES)
        turned = pltpu.roll(shaped, 4, 1)
        turned = jnp.where((node & 2) == 0, pltpu.roll(turned, 6, 1), pltpu.roll(turned, 2, 1))
        turned = jnp.where((node & 1) == 0, pltpu.roll(turned, 7, 1), pltpu.roll(turned, 1, 1))
        values = jnp.where(flip[None], turned, shaped).reshape(values.shape)
        parts = [values[k * NODES : (k + 1) * NODES] for k in range(ARRAYS)]
        parts[2] = parts[2] * sign
        parts[5] = parts[5] * sign
        return parts

    strip, ring = in_frame(both[:, :LANES]), in_frame(both[:, LANES:])
    edges = edge_values(table_ref, weight_ref, *ring)
    east = jnp.where(second, east1, east0) != 0
    ends = [jnp.where(east, part[NODES - NP :], part[:NP]) for part in edges]
    out0_ref[...], out1_ref[...] = packed(jnp.concatenate(strip + ends, 0))


def rows_kernel(
    block_cols, seam_ref, stored_ref, strip1_ref, strip0_ref, slot_ref, table_ref, weight_ref,
    far1_ref, far0_ref, next_ref, pair_ref, sums,
):
    east0, flip0, east1, flip1 = seam_flags(seam_ref, block_cols)
    odd = lax.axis_index("blk") & 1

    def goes_up(lane):
        return jnp.where((lane & 64) != 0, odd, 1 - odd) != 0

    lane = lax.broadcasted_iota(i32, (8, 2 * LANES), 1)
    up = goes_up(lane)
    row = jnp.where(up, GY - RING, 0) + ((lane & 63) >> 4)
    row = jnp.where(lane >= LANES, jnp.where(up, GY - RING - 1, RING), row)
    both = picked(stored_ref[...], by_slot(slot_ref, (lane & 15) * GY + row))
    whole = unpacked(strip0_ref[...], strip1_ref[...])
    parts = [
        beside(whole[k * NODES : (k + 1) * NODES], both[k * NODES : (k + 1) * NODES, LANES:])
        for k in range(ARRAYS)
    ]
    edges = jnp.concatenate(edge_values(table_ref, weight_ref, *parts), 0)
    sums[0], sums[1] = edges[:, :LANES], edges[:, LANES:]
    lane = lax.broadcasted_iota(i32, (1, LANES), 1)
    top0, top1 = odd ^ flip0, odd ^ flip1
    whole = with_row_rim(whole, sums, jnp.where(lane >= 64, top1, top0) != 0)
    far0_ref[...] = corner_of(whole, 0, top0)
    far1_ref[...] = corner_of(whole, 64, top1)
    rim = jnp.where(goes_up(lane), *row_edges(sums, 1))
    pair_ref[...], next_ref[...] = packed(jnp.concatenate([both[:, :LANES], rim], 0))


def corners_kernel(in1_ref, in0_ref, pair_ref, table_ref, weight_ref, *refs):
    out_ref, sums = refs[-2:]
    top = 1 - (lax.axis_index("blk") & 1)
    whole = unpacked(in0_ref[...], in1_ref[...])
    parts = [whole[k * NODES : (k + 1) * NODES] for k in range(ARRAYS)]
    sums[0] = jnp.concatenate(edge_values(table_ref, weight_ref, *parts), 0)
    whole = with_row_rim(whole, sums, jnp.broadcast_to(top != 0, (1, LANES)))
    out_ref[:HALF_ROWS] = pair_ref[...]
    out_ref[HALF_ROWS : HALF_ROWS + CORNER_ROWS] = corner_of(whole, 0, top)
    out_ref[HALF_ROWS + CORNER_ROWS :] = corner_of(whole, 64, top)


def own_kernel(stored_ref, slot_ref, lanes_ref, own_ref, hot_ref):
    one_hot = by_slot(slot_ref, lanes_ref[0:8])
    own_ref[...] = picked(stored_ref[...], one_hot)
    hot_ref[...] = one_hot


def middle_kernel(
    block_cols, seam_ref, in0_ref, in1_ref, own_ref, lanes_ref, low_ref, centre_ref, high_ref
):
    east0, flip0, east1, flip1 = seam_flags(seam_ref, block_cols)
    whole = unpacked(in0_ref[...], in1_ref[...])
    side = lanes_ref[16:24]
    first_at = jnp.where(side == 2, 64 * (1 - east0), 64 * east0)
    place = jnp.where(side == 0, -1, lanes_ref[8:16] + first_at)
    placed = picked(whole, as_one_hot(place, LANES))
    for k, ref in enumerate((low_ref, centre_ref, high_ref)):
        part = slice(k * LANES, (k + 1) * LANES)
        ref[:ROWS] = placed[:ROWS, part] + own_ref[:, part]
        ref[ROWS:] = placed[ROWS:, part]


def steps_kernel(
    block_cols, seam_ref, pair_ref, next_ref, far0_ref, far1_ref, low_ref, centre_ref,
    high_ref, hot_ref, table_ref, weight_ref, ext_ref, outer_ref, out_ref, sums,
):
    east0, flip0, east1, flip1 = seam_flags(seam_ref, block_cols)
    odd = lax.axis_index("blk") & 1
    block_y = lax.rem(lax.axis_index("blk"), BY)

    lane = lax.broadcasted_iota(i32, (1, LANES), 1)
    pair = pair_ref[...]
    strips = unpacked(pair[:HALF_ROWS], next_ref[...])
    strips = jnp.concatenate(
        [strips[:ROWS], jnp.zeros((EDGE_ROWS, LANES), f32), strips[ROWS:]], 0
    )
    near = pair[HALF_ROWS:]
    sources = (near[:CORNER_ROWS], near[CORNER_ROWS:], far0_ref[...], far1_ref[...])
    corners = []
    for k in range(RIM_ROWS // CORNER_ROWS):
        rows = None
        for n, source in enumerate(sources):
            shift = 16 * (n - k) % LANES
            part = pltpu.roll(source, shift, 1) if shift else source
            rows = part if n == 0 else jnp.where(lane >= 16 * n, part, rows)
        corners.append(rows)
    around = jnp.concatenate([strips, jnp.concatenate(corners, 0)], 1)
    kind = outer_ref[8:16]
    sender = jnp.where(outer_ref[16:24] != 0, odd, 1 - odd)
    strip_at = jnp.where(kind == 3, 16 * (1 - east0), 16 * east0)
    place = outer_ref[0:8] + jnp.where(kind == 1, 64 * sender, 32 * sender + strip_at)
    outer = picked(around, as_one_hot(jnp.where(kind == 0, -1, place), 2 * LANES))
    tiles = (outer[:, :LANES], low_ref, centre_ref, high_ref, outer[:, LANES:])

    def rows_of(start, count):
        return jnp.concatenate([ref[start : start + count] for ref in tiles], 1)

    table = table_ref[...].astype(bf16)
    weight = jnp.concatenate([weight_ref[...]] * len(tiles), 1)
    at_rim = ext_ref[0:1] != 0
    top_row = jnp.where(block_y == BY - 1, ext_ref[1:2], 0) != 0
    bottom_row = jnp.where(block_y == 0, ext_ref[2:3], 0) != 0

    first_row = ext_ref[4:5] != 0
    last_row = ext_ref[5:6] != 0

    def edge_sum(parts, rims=None, rows=None):
        count = len(parts) * NP
        for c, part in enumerate(parts):
            west, east = part[:NP], part[NODES - NP :]
            at_east = pltpu.roll(west, EXT - 1, 1)
            at_west = pltpu.roll(east, 1, 1)
            if rims is not None:
                at_east = jnp.where(at_rim, rims[c], at_east)
                at_west = jnp.where(at_rim, rims[c], at_west)
            part = jnp.concatenate([west + at_west, part[NP : NODES - NP], east + at_east], 0)
            for k in range(len(tiles)):
                sums[k, c * NODES : (c + 1) * NODES] = part[:, k * LANES : (k + 1) * LANES]
        south_at, north_at = pl.ds(0, count, stride=NP), pl.ds(NP - 1, count, stride=NP)
        south = jnp.concatenate([sums[k, south_at] for k in range(len(tiles))], 1)
        north = jnp.concatenate([sums[k, north_at] for k in range(len(tiles))], 1)
        at_north = jnp.where(top_row, 0.0, pltpu.roll(south, EXT - PITCH, 1))
        at_south = jnp.where(bottom_row, 0.0, pltpu.roll(north, PITCH, 1))
        if rows is not None:
            at_north = jnp.where(last_row, rows, at_north)
            at_south = jnp.where(first_row, rows, at_south)
        to_north, to_south = north + at_north, south + at_south
        for k in range(len(tiles)):
            sums[k, south_at] = to_south[:, k * LANES : (k + 1) * LANES]
            sums[k, north_at] = to_north[:, k * LANES : (k + 1) * LANES]
        return [
            jnp.concatenate(
                [sums[k, c * NODES : (c + 1) * NODES] for k in range(len(tiles))], 1
            )
            for c in range(len(parts))
        ]

    start = [rows_of(c * NODES, NODES) for c in range(3)]
    area, depth, spin, tide = [rows_of(c * NODES, NODES) for c in range(3, ARRAYS)]
    root = jnp.sqrt(area)
    mass = weight * area
    mass_spin = mass * spin
    area_depth = root * depth
    rims = [rows_of(ROWS + c * NP, NP) for c in range(4)]
    blank = jnp.zeros((EDGE_ROWS, MID), f32)
    rows = jnp.concatenate([tiles[0][ALL_ROWS:], blank, tiles[-1][ALL_ROWS:]], 1)
    node = lax.broadcasted_iota(i32, (1, NP, 1), 1)
    east = pltpu.roll(rows, EXT - 1, 1).reshape(4, NP, EXT)
    west = pltpu.roll(rows, 1, 1).reshape(4, NP, EXT)
    rows = (
        rows.reshape(4, NP, EXT)
        + jnp.where(node == NP - 1, pltpu.roll(east, NP - 1, 1), 0.0)
        + jnp.where(node == 0, pltpu.roll(west, 1, 1), 0.0)
    ).reshape(EDGE_ROWS, EXT)
    per_mass = 1.0 / edge_sum([mass], rims[3:], rows[3 * NP :])[0]

    def average(parts, rims=None, rows=None):
        return [part * per_mass for part in edge_sum(parts, rims, rows)]

    def tendency(s):
        return mass_tendency(table, *s, tide, area_depth, root, mass_spin)

    def laplace(s):
        return [
            dot(table[3 * NODES :, : 3 * NODES], jnp.concatenate(high_low_high(part), 0))
            for part in s
        ]

    change = average(tendency(start), rims[:3], rows[: 3 * NP])
    one = [s + time_step * c for s, c in zip(start, change)]
    change = average(tendency(one))
    two = [0.75 * s + 0.25 * (o + time_step * c) for s, o, c in zip(start, one, change)]
    change = average(tendency(two))
    three = [s / 3.0 + 2.0 / 3.0 * (o + time_step * c) for s, o, c in zip(start, two, change)]
    biharmonic = average(laplace(average(laplace(three))))
    own = ext_ref[3:4, LANES : LANES + MID] != 0
    stepped = [
        jnp.where(
            own,
            (s - time_step * hyper_coeff * b)[:, LANES : LANES + MID],
            0.0,
        )
        for s, b in zip(three, biharmonic)
    ]
    stored = picked(jnp.concatenate(stepped, 0), hot_ref[...], dot_other)
    out_ref[...] = stored.reshape(out_ref.shape)


def on_device(fields, jacobian, water_depth, coriolis, tide_height, slot_of, seam_rows):
    block_cols = lax.axis_size("blk") // BY
    table, weight = operator_table()
    table, weight, lanes, ext, outer = map(jnp.asarray, (table, weight, *lane_tables()))
    vmem = pl.BlockSpec(memory_space=pltpu.VMEM)
    smem = pl.BlockSpec(memory_space=pltpu.SMEM)
    hbm = pl.BlockSpec(memory_space=pltpu.HBM)
    params = pltpu.CompilerParams(vmem_limit_bytes=48 * 2**20)
    held = (fields, jacobian, water_depth, coriolis, tide_height)

    def call(kernel, ins, outs, cost, scratch=(), name=None):
        return pl.pallas_call(
            kernel,
            out_shape=[jax.ShapeDtypeStruct(*out) for out in outs],
            in_specs=[spec for spec, value in ins],
            out_specs=[vmem] * len(outs),
            scratch_shapes=list(scratch),
            compiler_params=params,
            cost_estimate=pl.CostEstimate(
                flops=cost, bytes_accessed=2 * 2**20, transcendentals=0
            ),
            name=name,
        )(
            *[
                pltpu.with_memory_space_constraint(value, pltpu.HBM) if spec is hbm else value
                for spec, value in ins
            ]
        )

    strip = ((HALF_ROWS, LANES), f32)
    def room(values, spaces=None):
        spaces = spaces or [pltpu.VMEM] * len(values)
        buffers = [space(x.shape, x.dtype) for space, x in zip(spaces, values)]
        return buffers + [pltpu.SemaphoreType.DMA((len(values),))]

    needed = (seam_rows, slot_of, *held, table, weight)
    corner = ((CORNER_ROWS, LANES), f32)
    strip1, strip0, stored = call(
        functools.partial(strips_kernel, block_cols),
        [(hbm, x) for x in needed],
        [strip, strip, ((ROWS, ELEMENTS), f32)],
        10**8,
        scratch=room(needed, [pltpu.SMEM] + [pltpu.VMEM] * (len(needed) - 1)),
        name="strips",
    )
    span = block_cols * BY
    both = ("face", "blk")
    places = [(f, x, y) for f in range(2) for x in range(block_cols) for y in range(BY)]

    def rank(face, block_x, block_y):
        return face * span + block_x * BY + block_y

    def same(y):
        return y

    def in_pair(y):
        return y ^ 1

    def next_pair(y):
        other = y + 1 if y % 2 else y - 1
        return other if 0 <= other < BY else y

    def swapped(value, partner):
        return lax.ppermute(
            value, both, [(rank(f, x, y), rank(f, x, partner(y))) for f, x, y in places]
        )

    def across(value0, value1, partner):
        last = block_cols - 1
        straight = {
            (f, x, y): (f, x + 1, partner(y)) if x < last else (1 - f, 0, partner(y))
            for f, x, y in places
        }
        turned = {
            (f, last, y): (1 - f, 0, BY - 1 - partner(y)) for f in range(2) for y in range(BY)
        }

        def eastward(value, pairs):
            return lax.ppermute(value, both, [(rank(*a), rank(*b)) for a, b in pairs.items()])

        def westward(value, pairs):
            return lax.ppermute(value, both, [(rank(*b), rank(*a)) for a, b in pairs.items()])

        if block_cols == 1:
            return eastward(value0, straight), eastward(value1, turned)
        flipped = (seam_rows[:, 1] - seam_rows[:, 0]) % seam_rows.shape[1] != 1
        face = lax.axis_index("face")
        block_x = lax.axis_index("blk") // BY
        return (
            jnp.where(
                (block_x == last) & flipped[face],
                westward(value1, turned),
                westward(value1, straight),
            ),
            jnp.where(
                (block_x == 0) & flipped[1 - face],
                eastward(value0, turned),
                eastward(value0, straight),
            ),
        )

    halo0, halo1 = across(strip0, strip1, same)
    far1, far0, to_next, to_pair = call(
        functools.partial(rows_kernel, block_cols),
        [(smem, seam_rows)]
        + [(vmem, x) for x in (stored, strip1, strip0, slot_of, table, weight)],
        [corner, corner, strip, strip],
        10**8,
        scratch=[pltpu.VMEM((2, 4 * NODES, LANES), f32)],
        name="rows",
    )
    far0, far1 = across(far0, far1, next_pair)
    from_next = swapped(to_next, next_pair)
    own, hot = call(
        own_kernel,
        [(vmem, x) for x in (stored, slot_of, lanes)],
        [((ROWS, MID), f32), ((ELEMENTS, MID), bf16)],
        3 * 10**8,
        name="own",
    )
    (to_pair,) = call(
        corners_kernel,
        [(vmem, x) for x in (halo1, halo0, to_pair, table, weight, hot, far1, far0, from_next)],
        [((HALF_ROWS + 2 * CORNER_ROWS, LANES), f32)],
        10**8,
        scratch=[pltpu.VMEM((1, 4 * NODES, LANES), f32)],
        name="corners",
    )
    from_pair = swapped(to_pair, in_pair)
    tile = ((ALL_ROWS, LANES), f32)
    low, centre, high = call(
        functools.partial(middle_kernel, block_cols),
        [(smem, seam_rows)] + [(vmem, x) for x in (halo0, halo1, own, lanes)],
        [tile, tile, tile],
        10**8,
        name="middle",
    )
    (stepped,) = call(
        functools.partial(steps_kernel, block_cols),
        [(smem, seam_rows)]
        + [
            (vmem, x)
            for x in (
                from_pair, from_next, far0, far1, low, centre, high,
                hot, table, weight, ext, outer,
            )
        ],
        [(fields.shape, f32)],
        10**9,
        scratch=[pltpu.VMEM((EXT // LANES, 3 * NODES, LANES), f32)],
        name="steps",
    )
    return stepped


def solution(mesh):
    return jax.shard_map(
        on_device,
        mesh=mesh,
        in_specs=(
            P(None, None, None, ("face", "blk")),
            P(None, None, ("face", "blk")),
            P(None, None, ("face", "blk")),
            P(None, None, ("face", "blk")),
            P(None, None, ("face", "blk")),
            P(("face", "blk"), None),
            P(),
        ),
        out_specs=P(None, None, None, ("face", "blk")),
        check_vma=False,
    )
```

```python
import functools
import math

import jax
import jax.numpy as jnp
import ml_dtypes
import numpy as np
from jax import lax
from jax.experimental import pallas as pl
from jax.experimental.pallas import tpu as pltpu
from jax.sharding import PartitionSpec as P

BY = 16
GX = 16
GY = 16
NP = 8
NODES = NP * NP
ARRAYS = 7
ROWS = ARRAYS * NODES
EDGE_ROWS = 4 * NP
ALL_ROWS = ROWS + EDGE_ROWS
HALF_ROWS = ALL_ROWS // 2
RING = 4
RIM_ROWS = ROWS + 2 * EDGE_ROWS
CORNER_ROWS = RIM_ROWS // 8
PITCH = GX + 2 * RING
MID = GY * PITCH
LANES = 128
EXT = MID + 2 * LANES
LEAD = LANES - RING * PITCH
ELEMENTS = GX * GY

time_step = 0.03
hyper_coeff = 0.0002

f32 = jnp.float32
bf16 = jnp.bfloat16
i32 = jnp.int32


def legendre_pair(location, degree):
    lower_value = 1.0
    upper_value = location
    for polynomial_order in range(2, degree + 1):
        lower_value, upper_value = (
            upper_value,
            (
                (2 * polynomial_order - 1) * location * upper_value
                - (polynomial_order - 1) * lower_value
            )
            / polynomial_order,
        )
    return (lower_value, upper_value)


def gll_tables(points):
    degree = points - 1
    locations = [-math.cos(math.pi * position / degree) for position in range(points)]
    for iteration in range(100):
        updated = []
        for location in locations:
            lower_value, upper_value = legendre_pair(location, degree)
            updated.append(
                location - (location * upper_value - lower_value) / ((degree + 1) * upper_value)
            )
        locations = updated
    locations[0] = -1.0
    locations[degree] = 1.0
    legendre_at = [legendre_pair(location, degree)[1] for location in locations]
    weights = [2.0 / (degree * (degree + 1) * value * value) for value in legendre_at]
    corner_value = degree * (degree + 1) / 4.0
    derivative = []
    for row_index in range(points):
        row_values = []
        for column_index in range(points):
            if row_index != column_index:
                row_values.append(
                    legendre_at[row_index]
                    / (legendre_at[column_index] * (locations[row_index] - locations[column_index]))
                )
            elif row_index == 0:
                row_values.append(-corner_value)
            elif row_index == degree:
                row_values.append(corner_value)
            else:
                row_values.append(0.0)
        derivative.append(row_values)
    return np.asarray(weights, np.float64), np.asarray(derivative, np.float64)


def in_three(matrix):
    high = matrix.astype(ml_dtypes.bfloat16)
    low = (matrix - high.astype(np.float64)).astype(ml_dtypes.bfloat16)
    return np.concatenate([high, high, low], 1)


def operator_table():
    weights, derivative = gll_tables(NP)
    eye = np.eye(NP)
    node_weight = np.outer(weights, weights).reshape(NODES, 1)
    along_x = node_weight * np.kron(derivative, eye)
    along_y = node_weight * np.kron(eye, derivative)
    second = derivative @ derivative
    both = node_weight * (np.kron(second, eye) + np.kron(eye, second))
    table = np.zeros((4 * NODES, 6 * NODES), ml_dtypes.bfloat16)
    table[:NODES, : 3 * NODES] = in_three(along_x)
    table[NODES : 2 * NODES, : 3 * NODES] = in_three(along_y)
    table[2 * NODES : 3 * NODES, : 3 * NODES] = in_three(along_x)
    table[2 * NODES : 3 * NODES, 3 * NODES :] = in_three(along_y)
    table[3 * NODES :, : 3 * NODES] = in_three(both)
    spread = np.broadcast_to(node_weight, (NODES, LANES)).astype(np.float32)
    return table.astype(np.float32), np.ascontiguousarray(spread)


def lane_tables():
    table = np.zeros((24, MID), np.int32)
    for lane in range(MID):
        row, col = divmod(lane, PITCH)
        x = col - RING
        own = 0 <= x < GX
        table[0:8, lane] = x * GY + row if own else -1
        if not own:
            table[8:16, lane] = row * RING + (col if x < 0 else x - GX)
        table[16:24, lane] = 0 if own else (1 if x < 0 else 2)
    ext = np.zeros((8, EXT), np.int32)
    outer = np.zeros((24, 2 * LANES), np.int32)
    for lane in range(EXT):
        row, col = divmod(lane - LEAD, PITCH)
        y = row - RING
        x = col - RING
        inside = 0 <= row < GY + 2 * RING
        ext[0, lane] = x in (-RING, GX + RING - 1)
        ext[1, lane] = y == GY - 1
        ext[2, lane] = y == 0
        ext[3, lane] = 0 <= y < GY and 0 <= x < GX
        ext[4, lane] = y == -RING
        ext[5, lane] = y == GY + RING - 1
        if inside and not 0 <= y < GY:
            place = lane if y < 0 else lane - LANES - MID + LANES
            step = y + RING if y < 0 else y - GY
            if 0 <= x < GX:
                outer[0:8, place] = step * GX + x
                outer[8:16, place] = 1
            else:
                outer[0:8, place] = LANES + step * RING + (x + RING if x < 0 else x - GX)
                outer[8:16, place] = 2 if x < 0 else 3
            outer[16:24, place] = y > 0
    return table, ext, outer


def exact_pieces(values):
    high = values.astype(bf16)
    rest = values - high.astype(f32)
    middle = rest.astype(bf16)
    low = (rest - middle.astype(f32)).astype(bf16)
    return high, middle, low


def dot(a, b):
    return jnp.dot(a, b, preferred_element_type=f32)


def dot_other(a, b):
    return lax.dot_general(a, b, (((1,), (1,)), ((), ())), preferred_element_type=f32)


def picked(values, one_hot, product=dot):
    high, middle, low = exact_pieces(values)
    return (product(high, one_hot) + product(middle, one_hot)) + product(low, one_hot)


def as_one_hot(row_of_lane, depth):
    index = lax.broadcasted_iota(i32, (depth, row_of_lane.shape[1]), 0)
    return jnp.where(index == row_of_lane[0:1], 1.0, 0.0).astype(bf16)


def high_low_high(values):
    high = values.astype(bf16)
    low = (values - high.astype(f32)).astype(bf16)
    return [high, low, high]


def by_slot(slot_ref, cell_of_lane):
    slots = jnp.broadcast_to(slot_ref[...], (8, ELEMENTS)).astype(f32).astype(bf16)
    chosen = dot(slots, as_one_hot(cell_of_lane, ELEMENTS))
    chosen = jnp.where(cell_of_lane >= 0, chosen, -1.0)
    index = lax.broadcasted_iota(i32, (ELEMENTS, cell_of_lane.shape[1]), 0).astype(f32)
    return jnp.where(index == chosen[0:1], 1.0, 0.0).astype(bf16)


def brought(sources, buffers, sems):
    copies = [
        pltpu.make_async_copy(source, buffer, sems.at[k])
        for k, (source, buffer) in enumerate(zip(sources, buffers))
    ]
    for copy in copies:
        copy.start()
    for copy in copies:
        copy.wait()


def stored_rows(fields_ref, others):
    parts = [fields_ref[...].reshape(3 * NODES, ELEMENTS)]
    parts += [ref[...].reshape(NODES, ELEMENTS) for ref in others]
    return jnp.concatenate(parts, 0)


def mass_tendency(table, h, u, v, tide, area_depth, weighted_area, spin):
    p = high_low_high(h - tide)
    slopes = dot(table[: 2 * NODES, : 3 * NODES], jnp.concatenate(p, 0))
    flux = high_low_high(area_depth * u) + high_low_high(area_depth * v)
    spread = dot(table[2 * NODES : 3 * NODES], jnp.concatenate(flux, 0))
    return [
        -spread,
        spin * v - weighted_area * slopes[:NODES],
        -spin * u - weighted_area * slopes[NODES:],
    ]


def edge_values(table_ref, weight_ref, h, u, v, area, depth, spin, tide):
    root = jnp.sqrt(area)
    mass = jnp.concatenate([weight_ref[...]] * (area.shape[1] // LANES), 1) * area
    table = table_ref[...].astype(bf16)
    return mass_tendency(table, h, u, v, tide, root * depth, root, mass * spin) + [mass]


def row_edges(sums):
    return tuple(sums[0, pl.ds(j, EDGE_ROWS, stride=NP)] for j in (NP - 1, 0))


def beside(left, right):
    return jnp.concatenate([left, right], 1)


def with_row_rim(whole, sums, top):
    north, south = row_edges(sums)
    rim = jnp.where(top, pltpu.roll(north, RING, 1), pltpu.roll(south, LANES - RING, 1))
    return jnp.concatenate([whole, rim], 0)


def corner_of(whole, start, top):
    lane = lax.broadcasted_iota(i32, (1, LANES), 1)
    base = LANES - start - jnp.where(top != 0, 48, 0)
    out = None
    for k in range(RIM_ROWS // CORNER_ROWS):
        part = whole[k * CORNER_ROWS : (k + 1) * CORNER_ROWS]
        part = pltpu.roll(part, (base + 16 * k) & (LANES - 1), 1)
        out = part if k == 0 else jnp.where(lane >= 16 * k, part, out)
    return out


def packed(whole):
    second = lax.broadcasted_iota(i32, (1, LANES), 1) >= 64
    top, bottom = whole[:HALF_ROWS], whole[HALF_ROWS:]
    return (
        jnp.where(second, pltpu.roll(bottom, 64, 1), top),
        jnp.where(second, bottom, pltpu.roll(top, 64, 1)),
    )


def unpacked(in0, in1):
    second = lax.broadcasted_iota(i32, (1, LANES), 1) >= 64
    top = jnp.where(second, pltpu.roll(in1, 64, 1), in0)
    bottom = jnp.where(second, in1, pltpu.roll(in0, 64, 1))
    return jnp.concatenate([top, bottom], 0)


def seam_flags(seam_ref, block_cols):
    size_y = seam_ref.shape[1]
    face = lax.axis_index("face")
    blk = lax.axis_index("blk")
    block_x = blk // BY

    def flipped(k):
        return jnp.where(lax.rem(seam_ref[k, 1] - seam_ref[k, 0] + size_y, size_y) != 1, 1, 0)

    first, second = flipped(0), flipped(1)
    east_flip = jnp.where(face == 0, first, second)
    west_flip = jnp.where(face == 0, second, first)
    if block_cols == 1:
        return 1 - east_flip, 0, east_flip, 1
    at_east = jnp.where(block_x == block_cols - 1, east_flip, 0)
    at_west = jnp.where(block_x == 0, west_flip, 0)
    return 1, at_east, 0, at_west


def strips_kernel(block_cols, *refs):
    sources = refs[:9]
    out1_ref, far1_ref, out0_ref, far0_ref, next_ref, pair_ref, stored_ref = refs[9:16]
    buffers, sems, sums = refs[16:25], refs[25], refs[26]
    brought(sources, buffers, sems)
    seam_ref, slot_ref, fields_ref, area_ref, depth_ref, spin_ref, tide_ref = buffers[:7]
    table_ref, weight_ref = buffers[7:]
    east0, flip0, east1, flip1 = seam_flags(seam_ref, block_cols)
    lane = lax.broadcasted_iota(i32, (8, 2 * LANES), 1)
    second = (lane & 64) != 0
    place = lane & 63
    row = place >> 2
    row = jnp.where(jnp.where(second, flip1, flip0) != 0, GY - 1 - row, row)
    east = jnp.where(second, east1, east0) != 0
    col = jnp.where(east, GX - RING, 0) + (place & 3)
    col = jnp.where(lane >= LANES, jnp.where(east, GX - RING - 1, RING), col)
    cells = col * GY + row
    odd = lax.axis_index("blk") & 1

    def goes_up(lane):
        return jnp.where((lane & 64) != 0, odd, 1 - odd) != 0

    up = goes_up(lane)
    row = jnp.where(up, GY - RING, 0) + ((lane & 63) >> 4)
    row = jnp.where(lane >= LANES, jnp.where(up, GY - RING - 1, RING), row)
    one_hot = by_slot(slot_ref, beside(cells, (lane & 15) * GY + row))
    stored = stored_rows(fields_ref, (area_ref, depth_ref, spin_ref, tide_ref))
    stored_ref[...] = stored
    both = picked(stored, one_hot)

    lane = lax.broadcasted_iota(i32, (1, LANES), 1)
    second = lane >= 64
    flip = jnp.where(second, flip1, flip0) != 0
    sign = jnp.where(flip, -1.0, 1.0)
    node = lax.broadcasted_iota(i32, (1, NP, 1), 1)

    def in_frame(values):
        shaped = values.reshape(-1, NP, LANES)
        turned = pltpu.roll(shaped, 4, 1)
        turned = jnp.where((node & 2) == 0, pltpu.roll(turned, 6, 1), pltpu.roll(turned, 2, 1))
        turned = jnp.where((node & 1) == 0, pltpu.roll(turned, 7, 1), pltpu.roll(turned, 1, 1))
        values = jnp.where(flip[None], turned, shaped).reshape(values.shape)
        parts = [values[k * NODES : (k + 1) * NODES] for k in range(ARRAYS)]
        parts[2] = parts[2] * sign
        parts[5] = parts[5] * sign
        return parts

    strip, ring = in_frame(both[:, :LANES]), in_frame(both[:, LANES : 2 * LANES])
    rows = both[:, 3 * LANES :]
    rows = [rows[k * NODES : (k + 1) * NODES] for k in range(ARRAYS)]
    edges = edge_values(
        table_ref, weight_ref, *(jnp.concatenate(parts, 1) for parts in zip(strip, ring, rows))
    )
    east = jnp.where(second, east1, east0) != 0
    ends = [part[:, LANES : 2 * LANES] for part in edges]
    ends = [jnp.where(east, part[NODES - NP :], part[:NP]) for part in ends]
    whole = jnp.concatenate(strip + ends, 0)
    out0_ref[...], out1_ref[...] = packed(whole)
    sums[0] = jnp.concatenate([part[:, :LANES] for part in edges], 0)
    top0, top1 = odd ^ flip0, odd ^ flip1
    whole = with_row_rim(whole, sums, jnp.where(second, top1, top0) != 0)
    far0_ref[...] = corner_of(whole, 0, top0)
    far1_ref[...] = corner_of(whole, 64, top1)
    sums[0] = jnp.concatenate([part[:, 2 * LANES :] for part in edges], 0)
    rim = jnp.where(goes_up(lane), *row_edges(sums))
    rows = jnp.concatenate([both[:, 2 * LANES : 3 * LANES], rim], 0)
    pair_ref[...], next_ref[...] = packed(rows)


def corners_kernel(in1_ref, in0_ref, pair_ref, table_ref, weight_ref, *refs):
    out_ref, sums = refs[-2:]
    top = 1 - (lax.axis_index("blk") & 1)
    whole = unpacked(in0_ref[...], in1_ref[...])
    parts = [whole[k * NODES : (k + 1) * NODES] for k in range(ARRAYS)]
    sums[0] = jnp.concatenate(edge_values(table_ref, weight_ref, *parts), 0)
    whole = with_row_rim(whole, sums, jnp.broadcast_to(top != 0, (1, LANES)))
    out_ref[:HALF_ROWS] = pair_ref[...]
    out_ref[HALF_ROWS : HALF_ROWS + CORNER_ROWS] = corner_of(whole, 0, top)
    out_ref[HALF_ROWS + CORNER_ROWS :] = corner_of(whole, 64, top)


def own_kernel(stored_ref, slot_ref, lanes_ref, own_ref, hot_ref):
    one_hot = by_slot(slot_ref, lanes_ref[0:8])
    own_ref[...] = picked(stored_ref[...], one_hot)
    hot_ref[...] = one_hot


def middle_kernel(
    block_cols, seam_ref, in0_ref, in1_ref, own_ref, lanes_ref, low_ref, centre_ref, high_ref
):
    east0, flip0, east1, flip1 = seam_flags(seam_ref, block_cols)
    whole = unpacked(in0_ref[...], in1_ref[...])
    side = lanes_ref[16:24]
    first_at = jnp.where(side == 2, 64 * (1 - east0), 64 * east0)
    place = jnp.where(side == 0, -1, lanes_ref[8:16] + first_at)
    placed = picked(whole, as_one_hot(place, LANES))
    for k, ref in enumerate((low_ref, centre_ref, high_ref)):
        part = slice(k * LANES, (k + 1) * LANES)
        ref[:ROWS] = placed[:ROWS, part] + own_ref[:, part]
        ref[ROWS:] = placed[ROWS:, part]


def steps_kernel(
    block_cols, seam_ref, pair_ref, next_ref, far0_ref, far1_ref, low_ref, centre_ref,
    high_ref, hot_ref, table_ref, weight_ref, ext_ref, outer_ref, out_ref, sums,
):
    east0, flip0, east1, flip1 = seam_flags(seam_ref, block_cols)
    odd = lax.axis_index("blk") & 1
    block_y = lax.rem(lax.axis_index("blk"), BY)

    lane = lax.broadcasted_iota(i32, (1, LANES), 1)
    pair = pair_ref[...]
    strips = unpacked(pair[:HALF_ROWS], next_ref[...])
    strips = jnp.concatenate(
        [strips[:ROWS], jnp.zeros((EDGE_ROWS, LANES), f32), strips[ROWS:]], 0
    )
    near = pair[HALF_ROWS:]
    sources = (near[:CORNER_ROWS], near[CORNER_ROWS:], far0_ref[...], far1_ref[...])
    corners = []
    for k in range(RIM_ROWS // CORNER_ROWS):
        rows = None
        for n, source in enumerate(sources):
            shift = 16 * (n - k) % LANES
            part = pltpu.roll(source, shift, 1) if shift else source
            rows = part if n == 0 else jnp.where(lane >= 16 * n, part, rows)
        corners.append(rows)
    around = jnp.concatenate([strips, jnp.concatenate(corners, 0)], 1)
    kind = outer_ref[8:16]
    sender = jnp.where(outer_ref[16:24] != 0, odd, 1 - odd)
    strip_at = jnp.where(kind == 3, 16 * (1 - east0), 16 * east0)
    place = outer_ref[0:8] + jnp.where(kind == 1, 64 * sender, 32 * sender + strip_at)
    outer = picked(around, as_one_hot(jnp.where(kind == 0, -1, place), 2 * LANES))
    tiles = (outer[:, :LANES], low_ref, centre_ref, high_ref, outer[:, LANES:])

    def rows_of(start, count):
        return jnp.concatenate([ref[start : start + count] for ref in tiles], 1)

    table = table_ref[...].astype(bf16)
    weight = jnp.concatenate([weight_ref[...]] * len(tiles), 1)
    at_rim = ext_ref[0:1] != 0
    top_row = jnp.where(block_y == BY - 1, ext_ref[1:2], 0) != 0
    bottom_row = jnp.where(block_y == 0, ext_ref[2:3], 0) != 0

    first_row = ext_ref[4:5] != 0
    last_row = ext_ref[5:6] != 0

    def edge_sum(parts, rims=None, rows=None):
        count = len(parts) * NP
        for c, part in enumerate(parts):
            west, east = part[:NP], part[NODES - NP :]
            at_east = pltpu.roll(west, EXT - 1, 1)
            at_west = pltpu.roll(east, 1, 1)
            if rims is not None:
                at_east = jnp.where(at_rim, rims[c], at_east)
                at_west = jnp.where(at_rim, rims[c], at_west)
            part = jnp.concatenate([west + at_west, part[NP : NODES - NP], east + at_east], 0)
            for k in range(len(tiles)):
                sums[k, c * NODES : (c + 1) * NODES] = part[:, k * LANES : (k + 1) * LANES]
        south_at, north_at = pl.ds(0, count, stride=NP), pl.ds(NP - 1, count, stride=NP)
        south = jnp.concatenate([sums[k, south_at] for k in range(len(tiles))], 1)
        north = jnp.concatenate([sums[k, north_at] for k in range(len(tiles))], 1)
        at_north = jnp.where(top_row, 0.0, pltpu.roll(south, EXT - PITCH, 1))
        at_south = jnp.where(bottom_row, 0.0, pltpu.roll(north, PITCH, 1))
        if rows is not None:
            at_north = jnp.where(last_row, rows, at_north)
            at_south = jnp.where(first_row, rows, at_south)
        to_north, to_south = north + at_north, south + at_south
        for k in range(len(tiles)):
            sums[k, south_at] = to_south[:, k * LANES : (k + 1) * LANES]
            sums[k, north_at] = to_north[:, k * LANES : (k + 1) * LANES]
        return [
            jnp.concatenate(
                [sums[k, c * NODES : (c + 1) * NODES] for k in range(len(tiles))], 1
            )
            for c in range(len(parts))
        ]

    start = [rows_of(c * NODES, NODES) for c in range(3)]
    area, depth, spin, tide = [rows_of(c * NODES, NODES) for c in range(3, ARRAYS)]
    root = jnp.sqrt(area)
    mass = weight * area
    mass_spin = mass * spin
    area_depth = root * depth
    rims = [rows_of(ROWS + c * NP, NP) for c in range(4)]
    blank = jnp.zeros((EDGE_ROWS, MID), f32)
    rows = jnp.concatenate([tiles[0][ALL_ROWS:], blank, tiles[-1][ALL_ROWS:]], 1)
    node = lax.broadcasted_iota(i32, (1, NP, 1), 1)
    east = pltpu.roll(rows, EXT - 1, 1).reshape(4, NP, EXT)
    west = pltpu.roll(rows, 1, 1).reshape(4, NP, EXT)
    rows = (
        rows.reshape(4, NP, EXT)
        + jnp.where(node == NP - 1, pltpu.roll(east, NP - 1, 1), 0.0)
        + jnp.where(node == 0, pltpu.roll(west, 1, 1), 0.0)
    ).reshape(EDGE_ROWS, EXT)
    per_mass = 1.0 / edge_sum([mass], rims[3:], rows[3 * NP :])[0]

    def average(parts, rims=None, rows=None):
        return [part * per_mass for part in edge_sum(parts, rims, rows)]

    def tendency(s):
        return mass_tendency(table, *s, tide, area_depth, root, mass_spin)

    def laplace(s):
        return [
            dot(table[3 * NODES :, : 3 * NODES], jnp.concatenate(high_low_high(part), 0))
            for part in s
        ]

    change = average(tendency(start), rims[:3], rows[: 3 * NP])
    one = [s + time_step * c for s, c in zip(start, change)]
    change = average(tendency(one))
    two = [0.75 * s + 0.25 * (o + time_step * c) for s, o, c in zip(start, one, change)]
    change = average(tendency(two))
    three = [s / 3.0 + 2.0 / 3.0 * (o + time_step * c) for s, o, c in zip(start, two, change)]
    biharmonic = average(laplace(average(laplace(three))))
    own = ext_ref[3:4, LANES : LANES + MID] != 0
    stepped = [
        jnp.where(
            own,
            (s - time_step * hyper_coeff * b)[:, LANES : LANES + MID],
            0.0,
        )
        for s, b in zip(three, biharmonic)
    ]
    stored = picked(jnp.concatenate(stepped, 0), hot_ref[...], dot_other)
    out_ref[...] = stored.reshape(out_ref.shape)


def on_device(fields, jacobian, water_depth, coriolis, tide_height, slot_of, seam_rows):
    block_cols = lax.axis_size("blk") // BY
    table, weight = operator_table()
    table, weight, lanes, ext, outer = map(jnp.asarray, (table, weight, *lane_tables()))
    vmem = pl.BlockSpec(memory_space=pltpu.VMEM)
    smem = pl.BlockSpec(memory_space=pltpu.SMEM)
    hbm = pl.BlockSpec(memory_space=pltpu.HBM)
    params = pltpu.CompilerParams(vmem_limit_bytes=48 * 2**20)
    held = (fields, jacobian, water_depth, coriolis, tide_height)

    def call(kernel, ins, outs, cost, scratch=(), name=None):
        return pl.pallas_call(
            kernel,
            out_shape=[jax.ShapeDtypeStruct(*out) for out in outs],
            in_specs=[spec for spec, value in ins],
            out_specs=[vmem] * len(outs),
            scratch_shapes=list(scratch),
            compiler_params=params,
            cost_estimate=pl.CostEstimate(
                flops=cost, bytes_accessed=2 * 2**20, transcendentals=0
            ),
            name=name,
        )(
            *[
                pltpu.with_memory_space_constraint(value, pltpu.HBM) if spec is hbm else value
                for spec, value in ins
            ]
        )

    strip = ((HALF_ROWS, LANES), f32)
    def room(values, spaces=None):
        spaces = spaces or [pltpu.VMEM] * len(values)
        buffers = [space(x.shape, x.dtype) for space, x in zip(spaces, values)]
        return buffers + [pltpu.SemaphoreType.DMA((len(values),))]

    needed = (seam_rows, slot_of, *held, table, weight)
    corner = ((CORNER_ROWS, LANES), f32)
    scratch = [pltpu.VMEM((1, 4 * NODES, LANES), f32)]
    strip1, far1, strip0, far0, to_next, to_pair, stored = call(
        functools.partial(strips_kernel, block_cols),
        [(hbm, x) for x in needed],
        [strip, corner, strip, corner, strip, strip, ((ROWS, ELEMENTS), f32)],
        10**8,
        scratch=room(needed, [pltpu.SMEM] + [pltpu.VMEM] * (len(needed) - 1)) + scratch,
        name="strips",
    )
    span = block_cols * BY
    both = ("face", "blk")
    places = [(f, x, y) for f in range(2) for x in range(block_cols) for y in range(BY)]

    def rank(face, block_x, block_y):
        return face * span + block_x * BY + block_y

    def same(y):
        return y

    def in_pair(y):
        return y ^ 1

    def next_pair(y):
        other = y + 1 if y % 2 else y - 1
        return other if 0 <= other < BY else y

    def swapped(value, partner):
        return lax.ppermute(
            value, both, [(rank(f, x, y), rank(f, x, partner(y))) for f, x, y in places]
        )

    def across(value0, value1, partner):
        last = block_cols - 1
        straight = {
            (f, x, y): (f, x + 1, partner(y)) if x < last else (1 - f, 0, partner(y))
            for f, x, y in places
        }
        turned = {
            (f, last, y): (1 - f, 0, BY - 1 - partner(y)) for f in range(2) for y in range(BY)
        }

        def eastward(value, pairs):
            return lax.ppermute(value, both, [(rank(*a), rank(*b)) for a, b in pairs.items()])

        def westward(value, pairs):
            return lax.ppermute(value, both, [(rank(*b), rank(*a)) for a, b in pairs.items()])

        if block_cols == 1:
            return eastward(value0, straight), eastward(value1, turned)
        flipped = (seam_rows[:, 1] - seam_rows[:, 0]) % seam_rows.shape[1] != 1
        face = lax.axis_index("face")
        block_x = lax.axis_index("blk") // BY
        return (
            jnp.where(
                (block_x == last) & flipped[face],
                westward(value1, turned),
                westward(value1, straight),
            ),
            jnp.where(
                (block_x == 0) & flipped[1 - face],
                eastward(value0, turned),
                eastward(value0, straight),
            ),
        )

    halo0, halo1 = across(strip0, strip1, same)
    far0, far1 = across(far0, far1, next_pair)
    from_next = swapped(to_next, next_pair)
    own, hot = call(
        own_kernel,
        [(vmem, x) for x in (stored, slot_of, lanes)],
        [((ROWS, MID), f32), ((ELEMENTS, MID), bf16)],
        10**8,
        name="own",
    )
    (to_pair,) = call(
        corners_kernel,
        [(vmem, x) for x in (halo1, halo0, to_pair, table, weight, hot, far1, far0, from_next)],
        [((HALF_ROWS + 2 * CORNER_ROWS, LANES), f32)],
        10**8,
        scratch=scratch,
        name="corners",
    )
    from_pair = swapped(to_pair, in_pair)
    tile = ((ALL_ROWS, LANES), f32)
    low, centre, high = call(
        functools.partial(middle_kernel, block_cols),
        [(smem, seam_rows)] + [(vmem, x) for x in (halo0, halo1, own, lanes)],
        [tile, tile, tile],
        10**8,
        name="middle",
    )
    (stepped,) = call(
        functools.partial(steps_kernel, block_cols),
        [(smem, seam_rows)]
        + [
            (vmem, x)
            for x in (
                from_pair, from_next, far0, far1, low, centre, high,
                hot, table, weight, ext, outer,
            )
        ],
        [(fields.shape, f32)],
        10**8,
        scratch=[pltpu.VMEM((EXT // LANES, 3 * NODES, LANES), f32)],
        name="steps",
    )
    return stepped


def solution(mesh):
    return jax.shard_map(
        on_device,
        mesh=mesh,
        in_specs=(
            P(None, None, None, ("face", "blk")),
            P(None, None, ("face", "blk")),
            P(None, None, ("face", "blk")),
            P(None, None, ("face", "blk")),
            P(None, None, ("face", "blk")),
            P(("face", "blk"), None),
            P(),
        ),
        out_specs=P(None, None, None, ("face", "blk")),
        check_vma=False,
    )
```

```python
import functools
import math

import jax
import jax.numpy as jnp
import ml_dtypes
import numpy as np
from jax import lax
from jax.experimental import pallas as pl
from jax.experimental.pallas import tpu as pltpu
from jax.sharding import PartitionSpec as P

BY = 16
GX = 16
GY = 16
NP = 8
NODES = NP * NP
ARRAYS = 7
ROWS = ARRAYS * NODES
EDGE_ROWS = 4 * NP
ALL_ROWS = ROWS + EDGE_ROWS
HALF_ROWS = ALL_ROWS // 2
RING = 4
RIM_ROWS = ROWS + 2 * EDGE_ROWS
CORNER_ROWS = RIM_ROWS // 8
PITCH = GX + 2 * RING
MID = GY * PITCH
LANES = 128
EXT = MID + 2 * LANES
LEAD = LANES - RING * PITCH
ELEMENTS = GX * GY

time_step = 0.03
hyper_coeff = 0.0002

f32 = jnp.float32
bf16 = jnp.bfloat16
i32 = jnp.int32


def legendre_pair(location, degree):
    lower_value = 1.0
    upper_value = location
    for polynomial_order in range(2, degree + 1):
        lower_value, upper_value = (
            upper_value,
            (
                (2 * polynomial_order - 1) * location * upper_value
                - (polynomial_order - 1) * lower_value
            )
            / polynomial_order,
        )
    return (lower_value, upper_value)


def gll_tables(points):
    degree = points - 1
    locations = [-math.cos(math.pi * position / degree) for position in range(points)]
    for iteration in range(100):
        updated = []
        for location in locations:
            lower_value, upper_value = legendre_pair(location, degree)
            updated.append(
                location - (location * upper_value - lower_value) / ((degree + 1) * upper_value)
            )
        locations = updated
    locations[0] = -1.0
    locations[degree] = 1.0
    legendre_at = [legendre_pair(location, degree)[1] for location in locations]
    weights = [2.0 / (degree * (degree + 1) * value * value) for value in legendre_at]
    corner_value = degree * (degree + 1) / 4.0
    derivative = []
    for row_index in range(points):
        row_values = []
        for column_index in range(points):
            if row_index != column_index:
                row_values.append(
                    legendre_at[row_index]
                    / (legendre_at[column_index] * (locations[row_index] - locations[column_index]))
                )
            elif row_index == 0:
                row_values.append(-corner_value)
            elif row_index == degree:
                row_values.append(corner_value)
            else:
                row_values.append(0.0)
        derivative.append(row_values)
    return np.asarray(weights, np.float64), np.asarray(derivative, np.float64)


def in_three(matrix):
    high = matrix.astype(ml_dtypes.bfloat16)
    low = (matrix - high.astype(np.float64)).astype(ml_dtypes.bfloat16)
    return np.concatenate([high, high, low], 1)


def operator_table():
    weights, derivative = gll_tables(NP)
    eye = np.eye(NP)
    node_weight = np.outer(weights, weights).reshape(NODES, 1)
    along_x = node_weight * np.kron(derivative, eye)
    along_y = node_weight * np.kron(eye, derivative)
    second = derivative @ derivative
    both = node_weight * (np.kron(second, eye) + np.kron(eye, second))
    table = np.zeros((4 * NODES, 6 * NODES), ml_dtypes.bfloat16)
    table[:NODES, : 3 * NODES] = in_three(along_x)
    table[NODES : 2 * NODES, : 3 * NODES] = in_three(along_y)
    table[2 * NODES : 3 * NODES, : 3 * NODES] = in_three(along_x)
    table[2 * NODES : 3 * NODES, 3 * NODES :] = in_three(along_y)
    table[3 * NODES :, : 3 * NODES] = in_three(both)
    spread = np.broadcast_to(node_weight, (NODES, LANES)).astype(np.float32)
    return table.astype(np.float32), np.ascontiguousarray(spread)


def lane_tables():
    table = np.zeros((24, MID), np.int32)
    for lane in range(MID):
        row, col = divmod(lane, PITCH)
        x = col - RING
        own = 0 <= x < GX
        table[0:8, lane] = x * GY + row if own else -1
        if not own:
            table[8:16, lane] = row * RING + (col if x < 0 else x - GX)
        table[16:24, lane] = 0 if own else (1 if x < 0 else 2)
    ext = np.zeros((8, EXT), np.int32)
    outer = np.zeros((24, 2 * LANES), np.int32)
    for lane in range(EXT):
        row, col = divmod(lane - LEAD, PITCH)
        y = row - RING
        x = col - RING
        inside = 0 <= row < GY + 2 * RING
        ext[0, lane] = x in (-RING, GX + RING - 1)
        ext[1, lane] = y == GY - 1
        ext[2, lane] = y == 0
        ext[3, lane] = 0 <= y < GY and 0 <= x < GX
        ext[4, lane] = y == -RING
        ext[5, lane] = y == GY + RING - 1
        if inside and not 0 <= y < GY:
            place = lane if y < 0 else lane - LANES - MID + LANES
            step = y + RING if y < 0 else y - GY
            if 0 <= x < GX:
                outer[0:8, place] = step * GX + x
                outer[8:16, place] = 1
            else:
                outer[0:8, place] = LANES + step * RING + (x + RING if x < 0 else x - GX)
                outer[8:16, place] = 2 if x < 0 else 3
            outer[16:24, place] = y > 0
    return table, ext, outer


def exact_pieces(values):
    high = values.astype(bf16)
    rest = values - high.astype(f32)
    middle = rest.astype(bf16)
    low = (rest - middle.astype(f32)).astype(bf16)
    return high, middle, low


def dot(a, b):
    return jnp.dot(a, b, preferred_element_type=f32)


def dot_other(a, b):
    return lax.dot_general(a, b, (((1,), (1,)), ((), ())), preferred_element_type=f32)


def picked(values, one_hot, product=dot):
    high, middle, low = exact_pieces(values)
    return (product(high, one_hot) + product(middle, one_hot)) + product(low, one_hot)


def as_one_hot(row_of_lane, depth):
    index = lax.broadcasted_iota(i32, (depth, row_of_lane.shape[1]), 0)
    return jnp.where(index == row_of_lane[0:1], 1.0, 0.0).astype(bf16)


def high_low_high(values):
    high = values.astype(bf16)
    low = (values - high.astype(f32)).astype(bf16)
    return [high, low, high]


def by_slot(slot_ref, cell_of_lane):
    slots = jnp.broadcast_to(slot_ref[...], (8, ELEMENTS)).astype(f32).astype(bf16)
    chosen = dot(slots, as_one_hot(cell_of_lane, ELEMENTS))
    chosen = jnp.where(cell_of_lane >= 0, chosen, -1.0)
    index = lax.broadcasted_iota(i32, (ELEMENTS, cell_of_lane.shape[1]), 0).astype(f32)
    return jnp.where(index == chosen[0:1], 1.0, 0.0).astype(bf16)


def brought(sources, buffers, sems):
    copies = [
        pltpu.make_async_copy(source, buffer, sems.at[k])
        for k, (source, buffer) in enumerate(zip(sources, buffers))
    ]
    for copy in copies:
        copy.start()
    for copy in copies:
        copy.wait()


def stored_rows(fields_ref, others):
    parts = [fields_ref[...].reshape(3 * NODES, ELEMENTS)]
    parts += [ref[...].reshape(NODES, ELEMENTS) for ref in others]
    return jnp.concatenate(parts, 0)


def mass_tendency(table, h, u, v, tide, area_depth, weighted_area, spin):
    p = high_low_high(h - tide)
    slopes = dot(table[: 2 * NODES, : 3 * NODES], jnp.concatenate(p, 0))
    flux = high_low_high(area_depth * u) + high_low_high(area_depth * v)
    spread = dot(table[2 * NODES : 3 * NODES], jnp.concatenate(flux, 0))
    return [
        -spread,
        spin * v - weighted_area * slopes[:NODES],
        -spin * u - weighted_area * slopes[NODES:],
    ]


def edge_values(table_ref, weight_ref, h, u, v, area, depth, spin, tide):
    root = jnp.sqrt(area)
    mass = jnp.concatenate([weight_ref[...]] * (area.shape[1] // LANES), 1) * area
    table = table_ref[...].astype(bf16)
    return mass_tendency(table, h, u, v, tide, root * depth, root, mass * spin) + [mass]


def row_edges(sums):
    return tuple(sums[0, pl.ds(j, EDGE_ROWS, stride=NP)] for j in (NP - 1, 0))


def beside(left, right):
    return jnp.concatenate([left, right], 1)


def corner_of(whole, start, top):
    lane = lax.broadcasted_iota(i32, (1, LANES), 1)
    base = LANES - start - jnp.where(top != 0, 48, 0)
    out = None
    for k in range(RIM_ROWS // CORNER_ROWS):
        part = whole[k * CORNER_ROWS : (k + 1) * CORNER_ROWS]
        part = pltpu.roll(part, (base + 16 * k) & (LANES - 1), 1)
        out = part if k == 0 else jnp.where(lane >= 16 * k, part, out)
    return out


def packed(whole):
    second = lax.broadcasted_iota(i32, (1, LANES), 1) >= 64
    top, bottom = whole[:HALF_ROWS], whole[HALF_ROWS:]
    return (
        jnp.where(second, pltpu.roll(bottom, 64, 1), top),
        jnp.where(second, bottom, pltpu.roll(top, 64, 1)),
    )


def unpacked(in0, in1):
    second = lax.broadcasted_iota(i32, (1, LANES), 1) >= 64
    top = jnp.where(second, pltpu.roll(in1, 64, 1), in0)
    bottom = jnp.where(second, in1, pltpu.roll(in0, 64, 1))
    return jnp.concatenate([top, bottom], 0)


def seam_flags(seam_ref, block_cols):
    size_y = seam_ref.shape[1]
    face = lax.axis_index("face")
    blk = lax.axis_index("blk")
    block_x = blk // BY

    def flipped(k):
        return jnp.where(lax.rem(seam_ref[k, 1] - seam_ref[k, 0] + size_y, size_y) != 1, 1, 0)

    first, second = flipped(0), flipped(1)
    east_flip = jnp.where(face == 0, first, second)
    west_flip = jnp.where(face == 0, second, first)
    if block_cols == 1:
        return 1 - east_flip, 0, east_flip, 1
    at_east = jnp.where(block_x == block_cols - 1, east_flip, 0)
    at_west = jnp.where(block_x == 0, west_flip, 0)
    return 1, at_east, 0, at_west


def strips_kernel(block_cols, *refs):
    sources = refs[:9]
    out1_ref, out0_ref, next_ref, pair_ref, stored_ref = refs[9:14]
    buffers, sems, sums = refs[14:23], refs[23], refs[24]
    brought(sources, buffers, sems)
    seam_ref, slot_ref, fields_ref, area_ref, depth_ref, spin_ref, tide_ref = buffers[:7]
    table_ref, weight_ref = buffers[7:]
    east0, flip0, east1, flip1 = seam_flags(seam_ref, block_cols)
    lane = lax.broadcasted_iota(i32, (8, 2 * LANES), 1)
    second = (lane & 64) != 0
    place = lane & 63
    row = place >> 2
    row = jnp.where(jnp.where(second, flip1, flip0) != 0, GY - 1 - row, row)
    east = jnp.where(second, east1, east0) != 0
    col = jnp.where(east, GX - RING, 0) + (place & 3)
    col = jnp.where(lane >= LANES, jnp.where(east, GX - RING - 1, RING), col)
    cells = col * GY + row
    odd = lax.axis_index("blk") & 1

    def goes_up(lane):
        return jnp.where((lane & 64) != 0, odd, 1 - odd) != 0

    up = goes_up(lane)
    row = jnp.where(up, GY - RING, 0) + ((lane & 63) >> 4)
    row = jnp.where(lane >= LANES, jnp.where(up, GY - RING - 1, RING), row)
    one_hot = by_slot(slot_ref, beside(cells, (lane & 15) * GY + row))
    stored = stored_rows(fields_ref, (area_ref, depth_ref, spin_ref, tide_ref))
    stored_ref[...] = stored
    both = picked(stored, one_hot)

    lane = lax.broadcasted_iota(i32, (1, LANES), 1)
    second = lane >= 64
    flip = jnp.where(second, flip1, flip0) != 0
    sign = jnp.where(flip, -1.0, 1.0)
    node = lax.broadcasted_iota(i32, (1, NP, 1), 1)

    def in_frame(values):
        shaped = values.reshape(-1, NP, LANES)
        turned = pltpu.roll(shaped, 4, 1)
        turned = jnp.where((node & 2) == 0, pltpu.roll(turned, 6, 1), pltpu.roll(turned, 2, 1))
        turned = jnp.where((node & 1) == 0, pltpu.roll(turned, 7, 1), pltpu.roll(turned, 1, 1))
        values = jnp.where(flip[None], turned, shaped).reshape(values.shape)
        parts = [values[k * NODES : (k + 1) * NODES] for k in range(ARRAYS)]
        parts[2] = parts[2] * sign
        parts[5] = parts[5] * sign
        return parts

    strip, ring = in_frame(both[:, :LANES]), in_frame(both[:, LANES : 2 * LANES])
    rows = both[:, 3 * LANES :]
    rows = [rows[k * NODES : (k + 1) * NODES] for k in range(ARRAYS)]
    edges = edge_values(table_ref, weight_ref, *map(beside, ring, rows))
    east = jnp.where(second, east1, east0) != 0
    ends = [jnp.where(east, part[NODES - NP :, :LANES], part[:NP, :LANES]) for part in edges]
    out0_ref[...], out1_ref[...] = packed(jnp.concatenate(strip + ends, 0))
    sums[0] = jnp.concatenate([part[:, LANES:] for part in edges], 0)
    rim = jnp.where(goes_up(lane), *row_edges(sums))
    rows = jnp.concatenate([both[:, 2 * LANES : 3 * LANES], rim], 0)
    pair_ref[...], next_ref[...] = packed(rows)


def corners_kernel(in1_ref, in0_ref, table_ref, weight_ref, _, next_ref, pair_ref, sums):
    odd = lax.axis_index("blk") & 1
    whole = unpacked(in0_ref[...], in1_ref[...])
    parts = [whole[k * NODES : (k + 1) * NODES] for k in range(ARRAYS)]
    sums[0] = jnp.concatenate(edge_values(table_ref, weight_ref, *parts), 0)
    north, south = row_edges(sums)
    north, south = pltpu.roll(north, RING, 1), pltpu.roll(south, LANES - RING, 1)
    for ref, top in ((next_ref, odd), (pair_ref, 1 - odd)):
        rim = jnp.where(jnp.broadcast_to(top != 0, (1, LANES)), north, south)
        rimmed = jnp.concatenate([whole, rim], 0)
        ref[:CORNER_ROWS] = corner_of(rimmed, 0, top)
        ref[CORNER_ROWS:] = corner_of(rimmed, 64, top)


def own_kernel(stored_ref, slot_ref, lanes_ref, own_ref, hot_ref):
    one_hot = by_slot(slot_ref, lanes_ref[0:8])
    own_ref[...] = picked(stored_ref[...], one_hot)
    hot_ref[...] = one_hot


def middle_kernel(
    block_cols, seam_ref, in0_ref, in1_ref, own_ref, lanes_ref, low_ref, centre_ref, high_ref
):
    east0, flip0, east1, flip1 = seam_flags(seam_ref, block_cols)
    whole = unpacked(in0_ref[...], in1_ref[...])
    side = lanes_ref[16:24]
    first_at = jnp.where(side == 2, 64 * (1 - east0), 64 * east0)
    place = jnp.where(side == 0, -1, lanes_ref[8:16] + first_at)
    placed = picked(whole, as_one_hot(place, LANES))
    for k, ref in enumerate((low_ref, centre_ref, high_ref)):
        part = slice(k * LANES, (k + 1) * LANES)
        ref[:ROWS] = placed[:ROWS, part] + own_ref[:, part]
        ref[ROWS:] = placed[ROWS:, part]


def steps_kernel(
    block_cols, seam_ref, next_ref, pair_ref, far_ref, near_ref, low_ref, centre_ref,
    high_ref, hot_ref, table_ref, weight_ref, ext_ref, outer_ref, out_ref, sums,
):
    east0, flip0, east1, flip1 = seam_flags(seam_ref, block_cols)
    odd = lax.axis_index("blk") & 1
    block_y = lax.rem(lax.axis_index("blk"), BY)

    lane = lax.broadcasted_iota(i32, (1, LANES), 1)
    strips = unpacked(pair_ref[...], next_ref[...])
    strips = jnp.concatenate(
        [strips[:ROWS], jnp.zeros((EDGE_ROWS, LANES), f32), strips[ROWS:]], 0
    )
    near, far = near_ref[...], far_ref[...]
    sources = (near[:CORNER_ROWS], near[CORNER_ROWS:], far[:CORNER_ROWS], far[CORNER_ROWS:])
    corners = []
    for k in range(RIM_ROWS // CORNER_ROWS):
        rows = None
        for n, source in enumerate(sources):
            shift = 16 * (n - k) % LANES
            part = pltpu.roll(source, shift, 1) if shift else source
            rows = part if n == 0 else jnp.where(lane >= 16 * n, part, rows)
        corners.append(rows)
    around = jnp.concatenate([strips, jnp.concatenate(corners, 0)], 1)
    kind = outer_ref[8:16]
    sender = jnp.where(outer_ref[16:24] != 0, odd, 1 - odd)
    strip_at = jnp.where(kind == 3, 16 * (1 - east0), 16 * east0)
    place = outer_ref[0:8] + jnp.where(kind == 1, 64 * sender, 32 * sender + strip_at)
    outer = picked(around, as_one_hot(jnp.where(kind == 0, -1, place), 2 * LANES))
    tiles = (outer[:, :LANES], low_ref, centre_ref, high_ref, outer[:, LANES:])

    def rows_of(start, count):
        return jnp.concatenate([ref[start : start + count] for ref in tiles], 1)

    table = table_ref[...].astype(bf16)
    weight = jnp.concatenate([weight_ref[...]] * len(tiles), 1)
    at_rim = ext_ref[0:1] != 0
    top_row = jnp.where(block_y == BY - 1, ext_ref[1:2], 0) != 0
    bottom_row = jnp.where(block_y == 0, ext_ref[2:3], 0) != 0

    first_row = ext_ref[4:5] != 0
    last_row = ext_ref[5:6] != 0

    def edge_sum(parts, rims=None, rows=None):
        count = len(parts) * NP
        for c, part in enumerate(parts):
            west, east = part[:NP], part[NODES - NP :]
            at_east = pltpu.roll(west, EXT - 1, 1)
            at_west = pltpu.roll(east, 1, 1)
            if rims is not None:
                at_east = jnp.where(at_rim, rims[c], at_east)
                at_west = jnp.where(at_rim, rims[c], at_west)
            part = jnp.concatenate([west + at_west, part[NP : NODES - NP], east + at_east], 0)
            for k in range(len(tiles)):
                sums[k, c * NODES : (c + 1) * NODES] = part[:, k * LANES : (k + 1) * LANES]
        south_at, north_at = pl.ds(0, count, stride=NP), pl.ds(NP - 1, count, stride=NP)
        south = jnp.concatenate([sums[k, south_at] for k in range(len(tiles))], 1)
        north = jnp.concatenate([sums[k, north_at] for k in range(len(tiles))], 1)
        at_north = jnp.where(top_row, 0.0, pltpu.roll(south, EXT - PITCH, 1))
        at_south = jnp.where(bottom_row, 0.0, pltpu.roll(north, PITCH, 1))
        if rows is not None:
            at_north = jnp.where(last_row, rows, at_north)
            at_south = jnp.where(first_row, rows, at_south)
        to_north, to_south = north + at_north, south + at_south
        for k in range(len(tiles)):
            sums[k, south_at] = to_south[:, k * LANES : (k + 1) * LANES]
            sums[k, north_at] = to_north[:, k * LANES : (k + 1) * LANES]
        return [
            jnp.concatenate(
                [sums[k, c * NODES : (c + 1) * NODES] for k in range(len(tiles))], 1
            )
            for c in range(len(parts))
        ]

    start = [rows_of(c * NODES, NODES) for c in range(3)]
    area, depth, spin, tide = [rows_of(c * NODES, NODES) for c in range(3, ARRAYS)]
    root = jnp.sqrt(area)
    mass = weight * area
    mass_spin = mass * spin
    area_depth = root * depth
    rims = [rows_of(ROWS + c * NP, NP) for c in range(4)]
    blank = jnp.zeros((EDGE_ROWS, MID), f32)
    rows = jnp.concatenate([tiles[0][ALL_ROWS:], blank, tiles[-1][ALL_ROWS:]], 1)
    node = lax.broadcasted_iota(i32, (1, NP, 1), 1)
    east = pltpu.roll(rows, EXT - 1, 1).reshape(4, NP, EXT)
    west = pltpu.roll(rows, 1, 1).reshape(4, NP, EXT)
    rows = (
        rows.reshape(4, NP, EXT)
        + jnp.where(node == NP - 1, pltpu.roll(east, NP - 1, 1), 0.0)
        + jnp.where(node == 0, pltpu.roll(west, 1, 1), 0.0)
    ).reshape(EDGE_ROWS, EXT)
    per_mass = 1.0 / edge_sum([mass], rims[3:], rows[3 * NP :])[0]

    def average(parts, rims=None, rows=None):
        return [part * per_mass for part in edge_sum(parts, rims, rows)]

    def tendency(s):
        return mass_tendency(table, *s, tide, area_depth, root, mass_spin)

    def laplace(s):
        return [
            dot(table[3 * NODES :, : 3 * NODES], jnp.concatenate(high_low_high(part), 0))
            for part in s
        ]

    change = average(tendency(start), rims[:3], rows[: 3 * NP])
    one = [s + time_step * c for s, c in zip(start, change)]
    change = average(tendency(one))
    two = [0.75 * s + 0.25 * (o + time_step * c) for s, o, c in zip(start, one, change)]
    change = average(tendency(two))
    three = [s / 3.0 + 2.0 / 3.0 * (o + time_step * c) for s, o, c in zip(start, two, change)]
    biharmonic = average(laplace(average(laplace(three))))
    own = ext_ref[3:4, LANES : LANES + MID] != 0
    stepped = [
        jnp.where(
            own,
            (s - time_step * hyper_coeff * b)[:, LANES : LANES + MID],
            0.0,
        )
        for s, b in zip(three, biharmonic)
    ]
    stored = picked(jnp.concatenate(stepped, 0), hot_ref[...], dot_other)
    out_ref[...] = stored.reshape(out_ref.shape)


def on_device(fields, jacobian, water_depth, coriolis, tide_height, slot_of, seam_rows):
    block_cols = lax.axis_size("blk") // BY
    table, weight = operator_table()
    table, weight, lanes, ext, outer = map(jnp.asarray, (table, weight, *lane_tables()))
    vmem = pl.BlockSpec(memory_space=pltpu.VMEM)
    smem = pl.BlockSpec(memory_space=pltpu.SMEM)
    hbm = pl.BlockSpec(memory_space=pltpu.HBM)
    params = pltpu.CompilerParams(vmem_limit_bytes=48 * 2**20)
    held = (fields, jacobian, water_depth, coriolis, tide_height)

    def call(kernel, ins, outs, cost, scratch=(), name=None):
        return pl.pallas_call(
            kernel,
            out_shape=[jax.ShapeDtypeStruct(*out) for out in outs],
            in_specs=[spec for spec, value in ins],
            out_specs=[vmem] * len(outs),
            scratch_shapes=list(scratch),
            compiler_params=params,
            cost_estimate=pl.CostEstimate(
                flops=cost, bytes_accessed=2 * 2**20, transcendentals=0
            ),
            name=name,
        )(
            *[
                pltpu.with_memory_space_constraint(value, pltpu.HBM) if spec is hbm else value
                for spec, value in ins
            ]
        )

    strip = ((HALF_ROWS, LANES), f32)
    def room(values, spaces=None):
        spaces = spaces or [pltpu.VMEM] * len(values)
        buffers = [space(x.shape, x.dtype) for space, x in zip(spaces, values)]
        return buffers + [pltpu.SemaphoreType.DMA((len(values),))]

    needed = (seam_rows, slot_of, *held, table, weight)
    corner = ((2 * CORNER_ROWS, LANES), f32)
    scratch = [pltpu.VMEM((1, 4 * NODES, LANES), f32)]
    strip1, strip0, to_next, to_pair, stored = call(
        functools.partial(strips_kernel, block_cols),
        [(hbm, x) for x in needed],
        [strip, strip, strip, strip, ((ROWS, ELEMENTS), f32)],
        10**8,
        scratch=room(needed, [pltpu.SMEM] + [pltpu.VMEM] * (len(needed) - 1)) + scratch,
        name="strips",
    )
    span = block_cols * BY
    both = ("face", "blk")
    places = [(f, x, y) for f in range(2) for x in range(block_cols) for y in range(BY)]

    def rank(face, block_x, block_y):
        return face * span + block_x * BY + block_y

    def in_pair(y):
        return y ^ 1

    def next_pair(y):
        other = y + 1 if y % 2 else y - 1
        return other if 0 <= other < BY else y

    def swapped(value, partner):
        return lax.ppermute(
            value, both, [(rank(f, x, y), rank(f, x, partner(y))) for f, x, y in places]
        )

    def across(value0, value1):
        last = block_cols - 1
        straight = {
            (f, x, y): (f, x + 1, y) if x < last else (1 - f, 0, y)
            for f, x, y in places
        }
        turned = {
            (f, last, y): (1 - f, 0, BY - 1 - y) for f in range(2) for y in range(BY)
        }

        def eastward(value, pairs):
            return lax.ppermute(value, both, [(rank(*a), rank(*b)) for a, b in pairs.items()])

        def westward(value, pairs):
            return lax.ppermute(value, both, [(rank(*b), rank(*a)) for a, b in pairs.items()])

        if block_cols == 1:
            return eastward(value0, straight), eastward(value1, turned)
        flipped = (seam_rows[:, 1] - seam_rows[:, 0]) % seam_rows.shape[1] != 1
        face = lax.axis_index("face")
        block_x = lax.axis_index("blk") // BY
        return (
            jnp.where(
                (block_x == last) & flipped[face],
                westward(value1, turned),
                westward(value1, straight),
            ),
            jnp.where(
                (block_x == 0) & flipped[1 - face],
                eastward(value0, turned),
                eastward(value0, straight),
            ),
        )

    halo0, halo1 = across(strip0, strip1)
    from_next = swapped(to_next, next_pair)
    from_pair = swapped(to_pair, in_pair)
    own, hot = call(
        own_kernel,
        [(vmem, x) for x in (stored, slot_of, lanes)],
        [((ROWS, MID), f32), ((ELEMENTS, MID), bf16)],
        10**8,
        name="own",
    )
    far, near = call(
        corners_kernel,
        [(vmem, x) for x in (halo1, halo0, table, weight, hot)],
        [corner, corner],
        10**8,
        scratch=scratch,
        name="corners",
    )
    far = swapped(far, next_pair)
    near = swapped(near, in_pair)
    tile = ((ALL_ROWS, LANES), f32)
    low, centre, high = call(
        functools.partial(middle_kernel, block_cols),
        [(smem, seam_rows)] + [(vmem, x) for x in (halo0, halo1, own, lanes)],
        [tile, tile, tile],
        10**8,
        name="middle",
    )
    (stepped,) = call(
        functools.partial(steps_kernel, block_cols),
        [(smem, seam_rows)]
        + [
            (vmem, x)
            for x in (
                from_next, from_pair, far, near, low, centre, high,
                hot, table, weight, ext, outer,
            )
        ],
        [(fields.shape, f32)],
        10**8,
        scratch=[pltpu.VMEM((EXT // LANES, 3 * NODES, LANES), f32)],
        name="steps",
    )
    return stepped


def solution(mesh):
    return jax.shard_map(
        on_device,
        mesh=mesh,
        in_specs=(
            P(None, None, None, ("face", "blk")),
            P(None, None, ("face", "blk")),
            P(None, None, ("face", "blk")),
            P(None, None, ("face", "blk")),
            P(None, None, ("face", "blk")),
            P(("face", "blk"), None),
            P(),
        ),
        out_specs=P(None, None, None, ("face", "blk")),
        check_vma=False,
    )
```

```python
import functools
import math

import jax
import jax.numpy as jnp
import ml_dtypes
import numpy as np
from jax import lax
from jax.experimental import pallas as pl
from jax.experimental.pallas import tpu as pltpu
from jax.sharding import PartitionSpec as P

BY = 16
GX = 16
GY = 16
NP = 8
NODES = NP * NP
ARRAYS = 7
ROWS = ARRAYS * NODES
EDGE_ROWS = 4 * NP
ALL_ROWS = ROWS + EDGE_ROWS
HALF_ROWS = ALL_ROWS // 2
RING = 4
RIM_ROWS = ROWS + 2 * EDGE_ROWS
CORNER_ROWS = RIM_ROWS // 8
PITCH = GX + 2 * RING
MID = GY * PITCH
LANES = 128
EXT = MID + 2 * LANES
LEAD = LANES - RING * PITCH
ELEMENTS = GX * GY

time_step = 0.03
hyper_coeff = 0.0002

f32 = jnp.float32
bf16 = jnp.bfloat16
i32 = jnp.int32


def legendre_pair(location, degree):
    lower_value = 1.0
    upper_value = location
    for polynomial_order in range(2, degree + 1):
        lower_value, upper_value = (
            upper_value,
            (
                (2 * polynomial_order - 1) * location * upper_value
                - (polynomial_order - 1) * lower_value
            )
            / polynomial_order,
        )
    return (lower_value, upper_value)


def gll_tables(points):
    degree = points - 1
    locations = [-math.cos(math.pi * position / degree) for position in range(points)]
    for iteration in range(100):
        updated = []
        for location in locations:
            lower_value, upper_value = legendre_pair(location, degree)
            updated.append(
                location - (location * upper_value - lower_value) / ((degree + 1) * upper_value)
            )
        locations = updated
    locations[0] = -1.0
    locations[degree] = 1.0
    legendre_at = [legendre_pair(location, degree)[1] for location in locations]
    weights = [2.0 / (degree * (degree + 1) * value * value) for value in legendre_at]
    corner_value = degree * (degree + 1) / 4.0
    derivative = []
    for row_index in range(points):
        row_values = []
        for column_index in range(points):
            if row_index != column_index:
                row_values.append(
                    legendre_at[row_index]
                    / (legendre_at[column_index] * (locations[row_index] - locations[column_index]))
                )
            elif row_index == 0:
                row_values.append(-corner_value)
            elif row_index == degree:
                row_values.append(corner_value)
            else:
                row_values.append(0.0)
        derivative.append(row_values)
    return np.asarray(weights, np.float64), np.asarray(derivative, np.float64)


def in_three(matrix):
    high = matrix.astype(ml_dtypes.bfloat16)
    low = (matrix - high.astype(np.float64)).astype(ml_dtypes.bfloat16)
    return np.concatenate([high, high, low], 1)


def operator_table():
    weights, derivative = gll_tables(NP)
    eye = np.eye(NP)
    node_weight = np.outer(weights, weights).reshape(NODES, 1)
    along_x = node_weight * np.kron(derivative, eye)
    along_y = node_weight * np.kron(eye, derivative)
    second = derivative @ derivative
    both = node_weight * (np.kron(second, eye) + np.kron(eye, second))
    table = np.zeros((4 * NODES, 6 * NODES), ml_dtypes.bfloat16)
    table[:NODES, : 3 * NODES] = in_three(along_x)
    table[NODES : 2 * NODES, : 3 * NODES] = in_three(along_y)
    table[2 * NODES : 3 * NODES, : 3 * NODES] = in_three(along_x)
    table[2 * NODES : 3 * NODES, 3 * NODES :] = in_three(along_y)
    table[3 * NODES :, : 3 * NODES] = in_three(both)
    spread = np.broadcast_to(node_weight, (NODES, LANES)).astype(np.float32)
    return table.astype(np.float32), np.ascontiguousarray(spread)


def lane_tables():
    table = np.zeros((24, MID), np.int32)
    for lane in range(MID):
        row, col = divmod(lane, PITCH)
        x = col - RING
        own = 0 <= x < GX
        table[0:8, lane] = x * GY + row if own else -1
        if not own:
            table[8:16, lane] = row * RING + (col if x < 0 else x - GX)
        table[16:24, lane] = 0 if own else (1 if x < 0 else 2)
    ext = np.zeros((8, EXT), np.int32)
    outer = np.zeros((24, 2 * LANES), np.int32)
    for lane in range(EXT):
        row, col = divmod(lane - LEAD, PITCH)
        y = row - RING
        x = col - RING
        inside = 0 <= row < GY + 2 * RING
        ext[0, lane] = x in (-RING, GX + RING - 1)
        ext[1, lane] = y == GY - 1
        ext[2, lane] = y == 0
        ext[3, lane] = 0 <= y < GY and 0 <= x < GX
        ext[4, lane] = y == -RING
        ext[5, lane] = y == GY + RING - 1
        if inside and not 0 <= y < GY:
            place = lane if y < 0 else lane - LANES - MID + LANES
            step = y + RING if y < 0 else y - GY
            if 0 <= x < GX:
                outer[0:8, place] = step * GX + x
                outer[8:16, place] = 1
            else:
                outer[0:8, place] = LANES + step * RING + (x + RING if x < 0 else x - GX)
                outer[8:16, place] = 2 if x < 0 else 3
            outer[16:24, place] = y > 0
    return table, ext, outer


def exact_pieces(values):
    high = values.astype(bf16)
    rest = values - high.astype(f32)
    middle = rest.astype(bf16)
    low = (rest - middle.astype(f32)).astype(bf16)
    return high, middle, low


def dot(a, b):
    return jnp.dot(a, b, preferred_element_type=f32)


def dot_other(a, b):
    return lax.dot_general(a, b, (((1,), (1,)), ((), ())), preferred_element_type=f32)


def picked(values, one_hot, product=dot):
    high, middle, low = exact_pieces(values)
    return (product(high, one_hot) + product(middle, one_hot)) + product(low, one_hot)


def as_one_hot(row_of_lane, depth):
    index = lax.broadcasted_iota(i32, (depth, row_of_lane.shape[1]), 0)
    return jnp.where(index == row_of_lane[0:1], 1.0, 0.0).astype(bf16)


def high_low_high(values):
    high = values.astype(bf16)
    low = (values - high.astype(f32)).astype(bf16)
    return [high, low, high]


def by_slot(slot_ref, cell_of_lane):
    slots = jnp.broadcast_to(slot_ref[...], (8, ELEMENTS)).astype(f32).astype(bf16)
    chosen = dot(slots, as_one_hot(cell_of_lane, ELEMENTS))
    chosen = jnp.where(cell_of_lane >= 0, chosen, -1.0)
    index = lax.broadcasted_iota(i32, (ELEMENTS, cell_of_lane.shape[1]), 0).astype(f32)
    return jnp.where(index == chosen[0:1], 1.0, 0.0).astype(bf16)


def brought(sources, buffers, sems):
    copies = [
        pltpu.make_async_copy(source, buffer, sems.at[k])
        for k, (source, buffer) in enumerate(zip(sources, buffers))
    ]
    for copy in copies:
        copy.start()
    for copy in copies:
        copy.wait()


def stored_rows(fields_ref, others):
    parts = [fields_ref[...].reshape(3 * NODES, ELEMENTS)]
    parts += [ref[...].reshape(NODES, ELEMENTS) for ref in others]
    return jnp.concatenate(parts, 0)


def mass_tendency(table, h, u, v, tide, area_depth, weighted_area, spin):
    p = high_low_high(h - tide)
    slopes = dot(table[: 2 * NODES, : 3 * NODES], jnp.concatenate(p, 0))
    flux = high_low_high(area_depth * u) + high_low_high(area_depth * v)
    spread = dot(table[2 * NODES : 3 * NODES], jnp.concatenate(flux, 0))
    return [
        -spread,
        spin * v - weighted_area * slopes[:NODES],
        -spin * u - weighted_area * slopes[NODES:],
    ]


def edge_values(table_ref, weight_ref, h, u, v, area, depth, spin, tide):
    root = jnp.sqrt(area)
    mass = jnp.concatenate([weight_ref[...]] * (area.shape[1] // LANES), 1) * area
    table = table_ref[...].astype(bf16)
    return mass_tendency(table, h, u, v, tide, root * depth, root, mass * spin) + [mass]


def row_edges(sums):
    return tuple(sums[0, pl.ds(j, EDGE_ROWS, stride=NP)] for j in (NP - 1, 0))


def beside(left, right):
    return jnp.concatenate([left, right], 1)


def with_row_rim(whole, sums, top):
    north, south = row_edges(sums)
    rim = jnp.where(top, pltpu.roll(north, RING, 1), pltpu.roll(south, LANES - RING, 1))
    return jnp.concatenate([whole, rim], 0)


def corner_of(whole, start, top):
    lane = lax.broadcasted_iota(i32, (1, LANES), 1)
    base = LANES - start - jnp.where(top != 0, 48, 0)
    out = None
    for k in range(RIM_ROWS // CORNER_ROWS):
        part = whole[k * CORNER_ROWS : (k + 1) * CORNER_ROWS]
        part = pltpu.roll(part, (base + 16 * k) & (LANES - 1), 1)
        out = part if k == 0 else jnp.where(lane >= 16 * k, part, out)
    return out


def packed(whole):
    second = lax.broadcasted_iota(i32, (1, LANES), 1) >= 64
    top, bottom = whole[:HALF_ROWS], whole[HALF_ROWS:]
    return (
        jnp.where(second, pltpu.roll(bottom, 64, 1), top),
        jnp.where(second, bottom, pltpu.roll(top, 64, 1)),
    )


def unpacked(in0, in1):
    second = lax.broadcasted_iota(i32, (1, LANES), 1) >= 64
    top = jnp.where(second, pltpu.roll(in1, 64, 1), in0)
    bottom = jnp.where(second, in1, pltpu.roll(in0, 64, 1))
    return jnp.concatenate([top, bottom], 0)


def seam_flags(seam_ref, block_cols):
    size_y = seam_ref.shape[1]
    face = lax.axis_index("face")
    blk = lax.axis_index("blk")
    block_x = blk // BY

    def flipped(k):
        return jnp.where(lax.rem(seam_ref[k, 1] - seam_ref[k, 0] + size_y, size_y) != 1, 1, 0)

    first, second = flipped(0), flipped(1)
    east_flip = jnp.where(face == 0, first, second)
    west_flip = jnp.where(face == 0, second, first)
    if block_cols == 1:
        return 1 - east_flip, 0, east_flip, 1
    at_east = jnp.where(block_x == block_cols - 1, east_flip, 0)
    at_west = jnp.where(block_x == 0, west_flip, 0)
    return 1, at_east, 0, at_west


def strips_kernel(block_cols, *refs):
    sources = refs[:9]
    out1_ref, far1_ref, out0_ref, far0_ref, next_ref, pair_ref, stored_ref = refs[9:16]
    buffers, sems, sums = refs[16:25], refs[25], refs[26]
    brought(sources, buffers, sems)
    seam_ref, slot_ref, fields_ref, area_ref, depth_ref, spin_ref, tide_ref = buffers[:7]
    table_ref, weight_ref = buffers[7:]
    east0, flip0, east1, flip1 = seam_flags(seam_ref, block_cols)
    lane = lax.broadcasted_iota(i32, (8, 2 * LANES), 1)
    second = (lane & 64) != 0
    place = lane & 63
    row = place >> 2
    row = jnp.where(jnp.where(second, flip1, flip0) != 0, GY - 1 - row, row)
    east = jnp.where(second, east1, east0) != 0
    col = jnp.where(east, GX - RING, 0) + (place & 3)
    col = jnp.where(lane >= LANES, jnp.where(east, GX - RING - 1, RING), col)
    cells = col * GY + row
    odd = lax.axis_index("blk") & 1

    def goes_up(lane):
        return jnp.where((lane & 64) != 0, odd, 1 - odd) != 0

    up = goes_up(lane)
    row = jnp.where(up, GY - RING, 0) + ((lane & 63) >> 4)
    row = jnp.where(lane >= LANES, jnp.where(up, GY - RING - 1, RING), row)
    one_hot = by_slot(slot_ref, beside(cells, (lane & 15) * GY + row))
    stored = stored_rows(fields_ref, (area_ref, depth_ref, spin_ref, tide_ref))
    stored_ref[...] = stored
    both = picked(stored, one_hot)

    lane = lax.broadcasted_iota(i32, (1, LANES), 1)
    second = lane >= 64
    flip = jnp.where(second, flip1, flip0) != 0
    sign = jnp.where(flip, -1.0, 1.0)
    node = lax.broadcasted_iota(i32, (1, NP, 1), 1)

    def in_frame(values):
        shaped = values.reshape(-1, NP, LANES)
        turned = pltpu.roll(shaped, 4, 1)
        turned = jnp.where((node & 2) == 0, pltpu.roll(turned, 6, 1), pltpu.roll(turned, 2, 1))
        turned = jnp.where((node & 1) == 0, pltpu.roll(turned, 7, 1), pltpu.roll(turned, 1, 1))
        values = jnp.where(flip[None], turned, shaped).reshape(values.shape)
        parts = [values[k * NODES : (k + 1) * NODES] for k in range(ARRAYS)]
        parts[2] = parts[2] * sign
        parts[5] = parts[5] * sign
        return parts

    strip, ring = in_frame(both[:, :LANES]), in_frame(both[:, LANES : 2 * LANES])
    rows = both[:, 3 * LANES :]
    rows = [rows[k * NODES : (k + 1) * NODES] for k in range(ARRAYS)]
    edges = edge_values(
        table_ref, weight_ref, *(jnp.concatenate(parts, 1) for parts in zip(strip, ring, rows))
    )
    east = jnp.where(second, east1, east0) != 0
    ends = [part[:, LANES : 2 * LANES] for part in edges]
    ends = [jnp.where(east, part[NODES - NP :], part[:NP]) for part in ends]
    whole = jnp.concatenate(strip + ends, 0)
    out0_ref[...], out1_ref[...] = packed(whole)
    sums[0] = jnp.concatenate([part[:, :LANES] for part in edges], 0)
    top0, top1 = odd ^ flip0, odd ^ flip1
    whole = with_row_rim(whole, sums, jnp.where(second, top1, top0) != 0)
    far0_ref[...] = corner_of(whole, 0, top0)
    far1_ref[...] = corner_of(whole, 64, top1)
    sums[0] = jnp.concatenate([part[:, 2 * LANES :] for part in edges], 0)
    rim = jnp.where(goes_up(lane), *row_edges(sums))
    rows = jnp.concatenate([both[:, 2 * LANES : 3 * LANES], rim], 0)
    pair_ref[...], next_ref[...] = packed(rows)


def corners_kernel(_, in1_ref, in0_ref, pair_ref, table_ref, weight_ref, *refs):
    out_ref, sums = refs[-2:]
    top = 1 - (lax.axis_index("blk") & 1)
    whole = unpacked(in0_ref[...], in1_ref[...])
    parts = [whole[k * NODES : (k + 1) * NODES] for k in range(ARRAYS)]
    sums[0] = jnp.concatenate(edge_values(table_ref, weight_ref, *parts), 0)
    whole = with_row_rim(whole, sums, jnp.broadcast_to(top != 0, (1, LANES)))
    out_ref[:HALF_ROWS] = pair_ref[...]
    out_ref[HALF_ROWS : HALF_ROWS + CORNER_ROWS] = corner_of(whole, 0, top)
    out_ref[HALF_ROWS + CORNER_ROWS :] = corner_of(whole, 64, top)


def own_kernel(stored_ref, slot_ref, lanes_ref, own_ref, hot_ref):
    one_hot = by_slot(slot_ref, lanes_ref[0:8])
    own_ref[...] = picked(stored_ref[...], one_hot)
    hot_ref[...] = one_hot


def middle_kernel(
    block_cols, seam_ref, in0_ref, in1_ref, own_ref, lanes_ref, low_ref, centre_ref, high_ref
):
    east0, flip0, east1, flip1 = seam_flags(seam_ref, block_cols)
    whole = unpacked(in0_ref[...], in1_ref[...])
    side = lanes_ref[16:24]
    first_at = jnp.where(side == 2, 64 * (1 - east0), 64 * east0)
    place = jnp.where(side == 0, -1, lanes_ref[8:16] + first_at)
    placed = picked(whole, as_one_hot(place, LANES))
    for k, ref in enumerate((low_ref, centre_ref, high_ref)):
        part = slice(k * LANES, (k + 1) * LANES)
        ref[:ROWS] = placed[:ROWS, part] + own_ref[:, part]
        ref[ROWS:] = placed[ROWS:, part]


def steps_kernel(
    block_cols, seam_ref, pair_ref, next_ref, far0_ref, far1_ref, low_ref, centre_ref,
    high_ref, hot_ref, table_ref, weight_ref, ext_ref, outer_ref, out_ref, sums,
):
    east0, flip0, east1, flip1 = seam_flags(seam_ref, block_cols)
    odd = lax.axis_index("blk") & 1
    block_y = lax.rem(lax.axis_index("blk"), BY)

    lane = lax.broadcasted_iota(i32, (1, LANES), 1)
    pair = pair_ref[...]
    strips = unpacked(pair[:HALF_ROWS], next_ref[...])
    strips = jnp.concatenate(
        [strips[:ROWS], jnp.zeros((EDGE_ROWS, LANES), f32), strips[ROWS:]], 0
    )
    near = pair[HALF_ROWS:]
    sources = (near[:CORNER_ROWS], near[CORNER_ROWS:], far0_ref[...], far1_ref[...])
    corners = []
    for k in range(RIM_ROWS // CORNER_ROWS):
        rows = None
        for n, source in enumerate(sources):
            shift = 16 * (n - k) % LANES
            part = pltpu.roll(source, shift, 1) if shift else source
            rows = part if n == 0 else jnp.where(lane >= 16 * n, part, rows)
        corners.append(rows)
    around = jnp.concatenate([strips, jnp.concatenate(corners, 0)], 1)
    kind = outer_ref[8:16]
    sender = jnp.where(outer_ref[16:24] != 0, odd, 1 - odd)
    strip_at = jnp.where(kind == 3, 16 * (1 - east0), 16 * east0)
    place = outer_ref[0:8] + jnp.where(kind == 1, 64 * sender, 32 * sender + strip_at)
    outer = picked(around, as_one_hot(jnp.where(kind == 0, -1, place), 2 * LANES))
    tiles = (outer[:, :LANES], low_ref, centre_ref, high_ref, outer[:, LANES:])

    def rows_of(start, count):
        return jnp.concatenate([ref[start : start + count] for ref in tiles], 1)

    table = table_ref[...].astype(bf16)
    weight = jnp.concatenate([weight_ref[...]] * len(tiles), 1)
    at_rim = ext_ref[0:1] != 0
    top_row = jnp.where(block_y == BY - 1, ext_ref[1:2], 0) != 0
    bottom_row = jnp.where(block_y == 0, ext_ref[2:3], 0) != 0

    first_row = ext_ref[4:5] != 0
    last_row = ext_ref[5:6] != 0

    def edge_sum(parts, rims=None, rows=None):
        count = len(parts) * NP
        for c, part in enumerate(parts):
            west, east = part[:NP], part[NODES - NP :]
            at_east = pltpu.roll(west, EXT - 1, 1)
            at_west = pltpu.roll(east, 1, 1)
            if rims is not None:
                at_east = jnp.where(at_rim, rims[c], at_east)
                at_west = jnp.where(at_rim, rims[c], at_west)
            part = jnp.concatenate([west + at_west, part[NP : NODES - NP], east + at_east], 0)
            for k in range(len(tiles)):
                sums[k, c * NODES : (c + 1) * NODES] = part[:, k * LANES : (k + 1) * LANES]
        south_at, north_at = pl.ds(0, count, stride=NP), pl.ds(NP - 1, count, stride=NP)
        south = jnp.concatenate([sums[k, south_at] for k in range(len(tiles))], 1)
        north = jnp.concatenate([sums[k, north_at] for k in range(len(tiles))], 1)
        at_north = jnp.where(top_row, 0.0, pltpu.roll(south, EXT - PITCH, 1))
        at_south = jnp.where(bottom_row, 0.0, pltpu.roll(north, PITCH, 1))
        if rows is not None:
            at_north = jnp.where(last_row, rows, at_north)
            at_south = jnp.where(first_row, rows, at_south)
        to_north, to_south = north + at_north, south + at_south
        for k in range(len(tiles)):
            sums[k, south_at] = to_south[:, k * LANES : (k + 1) * LANES]
            sums[k, north_at] = to_north[:, k * LANES : (k + 1) * LANES]
        return [
            jnp.concatenate(
                [sums[k, c * NODES : (c + 1) * NODES] for k in range(len(tiles))], 1
            )
            for c in range(len(parts))
        ]

    start = [rows_of(c * NODES, NODES) for c in range(3)]
    area, depth, spin, tide = [rows_of(c * NODES, NODES) for c in range(3, ARRAYS)]
    root = jnp.sqrt(area)
    mass = weight * area
    mass_spin = mass * spin
    area_depth = root * depth
    rims = [rows_of(ROWS + c * NP, NP) for c in range(4)]
    blank = jnp.zeros((EDGE_ROWS, MID), f32)
    rows = jnp.concatenate([tiles[0][ALL_ROWS:], blank, tiles[-1][ALL_ROWS:]], 1)
    node = lax.broadcasted_iota(i32, (1, NP, 1), 1)
    east = pltpu.roll(rows, EXT - 1, 1).reshape(4, NP, EXT)
    west = pltpu.roll(rows, 1, 1).reshape(4, NP, EXT)
    rows = (
        rows.reshape(4, NP, EXT)
        + jnp.where(node == NP - 1, pltpu.roll(east, NP - 1, 1), 0.0)
        + jnp.where(node == 0, pltpu.roll(west, 1, 1), 0.0)
    ).reshape(EDGE_ROWS, EXT)
    per_mass = 1.0 / edge_sum([mass], rims[3:], rows[3 * NP :])[0]

    def average(parts, rims=None, rows=None):
        return [part * per_mass for part in edge_sum(parts, rims, rows)]

    def tendency(s):
        return mass_tendency(table, *s, tide, area_depth, root, mass_spin)

    def laplace(s):
        return [
            dot(table[3 * NODES :, : 3 * NODES], jnp.concatenate(high_low_high(part), 0))
            for part in s
        ]

    change = average(tendency(start), rims[:3], rows[: 3 * NP])
    one = [s + time_step * c for s, c in zip(start, change)]
    change = average(tendency(one))
    two = [0.75 * s + 0.25 * (o + time_step * c) for s, o, c in zip(start, one, change)]
    change = average(tendency(two))
    three = [s / 3.0 + 2.0 / 3.0 * (o + time_step * c) for s, o, c in zip(start, two, change)]
    biharmonic = average(laplace(average(laplace(three))))
    own = ext_ref[3:4, LANES : LANES + MID] != 0
    stepped = [
        jnp.where(
            own,
            (s - time_step * hyper_coeff * b)[:, LANES : LANES + MID],
            0.0,
        )
        for s, b in zip(three, biharmonic)
    ]
    stored = picked(jnp.concatenate(stepped, 0), hot_ref[...], dot_other)
    out_ref[...] = stored.reshape(out_ref.shape)


def on_device(fields, jacobian, water_depth, coriolis, tide_height, slot_of, seam_rows):
    block_cols = lax.axis_size("blk") // BY
    table, weight = operator_table()
    table, weight, lanes, ext, outer = map(jnp.asarray, (table, weight, *lane_tables()))
    vmem = pl.BlockSpec(memory_space=pltpu.VMEM)
    smem = pl.BlockSpec(memory_space=pltpu.SMEM)
    hbm = pl.BlockSpec(memory_space=pltpu.HBM)
    params = pltpu.CompilerParams(vmem_limit_bytes=48 * 2**20)
    held = (fields, jacobian, water_depth, coriolis, tide_height)

    def call(kernel, ins, outs, cost, scratch=(), name=None):
        return pl.pallas_call(
            kernel,
            out_shape=[jax.ShapeDtypeStruct(*out) for out in outs],
            in_specs=[spec for spec, value in ins],
            out_specs=[vmem] * len(outs),
            scratch_shapes=list(scratch),
            compiler_params=params,
            cost_estimate=pl.CostEstimate(
                flops=cost, bytes_accessed=2 * 2**20, transcendentals=0
            ),
            name=name,
        )(
            *[
                pltpu.with_memory_space_constraint(value, pltpu.HBM) if spec is hbm else value
                for spec, value in ins
            ]
        )

    strip = ((HALF_ROWS, LANES), f32)
    def room(values, spaces=None):
        spaces = spaces or [pltpu.VMEM] * len(values)
        buffers = [space(x.shape, x.dtype) for space, x in zip(spaces, values)]
        return buffers + [pltpu.SemaphoreType.DMA((len(values),))]

    needed = (seam_rows, slot_of, *held, table, weight)
    corner = ((CORNER_ROWS, LANES), f32)
    scratch = [pltpu.VMEM((1, 4 * NODES, LANES), f32)]
    strip1, far1, strip0, far0, to_next, to_pair, stored = call(
        functools.partial(strips_kernel, block_cols),
        [(hbm, x) for x in needed],
        [strip, corner, strip, corner, strip, strip, ((ROWS, ELEMENTS), f32)],
        10**8,
        scratch=room(needed, [pltpu.SMEM] + [pltpu.VMEM] * (len(needed) - 1)) + scratch,
        name="strips",
    )
    span = block_cols * BY
    both = ("face", "blk")
    places = [(f, x, y) for f in range(2) for x in range(block_cols) for y in range(BY)]

    def rank(face, block_x, block_y):
        return face * span + block_x * BY + block_y

    def same(y):
        return y

    def in_pair(y):
        return y ^ 1

    def next_pair(y):
        other = y + 1 if y % 2 else y - 1
        return other if 0 <= other < BY else y

    def swapped(value, partner):
        return lax.ppermute(
            value, both, [(rank(f, x, y), rank(f, x, partner(y))) for f, x, y in places]
        )

    def across(value0, value1, partner):
        last = block_cols - 1
        straight = {
            (f, x, y): (f, x + 1, partner(y)) if x < last else (1 - f, 0, partner(y))
            for f, x, y in places
        }
        turned = {
            (f, last, y): (1 - f, 0, BY - 1 - partner(y)) for f in range(2) for y in range(BY)
        }

        def eastward(value, pairs):
            return lax.ppermute(value, both, [(rank(*a), rank(*b)) for a, b in pairs.items()])

        def westward(value, pairs):
            return lax.ppermute(value, both, [(rank(*b), rank(*a)) for a, b in pairs.items()])

        if block_cols == 1:
            return eastward(value0, straight), eastward(value1, turned)
        flipped = (seam_rows[:, 1] - seam_rows[:, 0]) % seam_rows.shape[1] != 1
        face = lax.axis_index("face")
        block_x = lax.axis_index("blk") // BY
        return (
            jnp.where(
                (block_x == last) & flipped[face],
                westward(value1, turned),
                westward(value1, straight),
            ),
            jnp.where(
                (block_x == 0) & flipped[1 - face],
                eastward(value0, turned),
                eastward(value0, straight),
            ),
        )

    halo0, halo1 = across(strip0, strip1, same)
    far0, far1 = across(far0, far1, next_pair)
    from_next = swapped(to_next, next_pair)
    own, hot = call(
        own_kernel,
        [(vmem, x) for x in (stored, slot_of, lanes)],
        [((ROWS, MID), f32), ((ELEMENTS, MID), bf16)],
        10**8,
        name="own",
    )
    (to_pair,) = call(
        corners_kernel,
        [(vmem, x) for x in (from_next, halo1, halo0, to_pair, table, weight, hot, far1, far0)],
        [((HALF_ROWS + 2 * CORNER_ROWS, LANES), f32)],
        10**8,
        scratch=scratch,
        name="corners",
    )
    from_pair = swapped(to_pair, in_pair)
    tile = ((ALL_ROWS, LANES), f32)
    low, centre, high = call(
        functools.partial(middle_kernel, block_cols),
        [(smem, seam_rows)] + [(vmem, x) for x in (halo0, halo1, own, lanes)],
        [tile, tile, tile],
        10**8,
        name="middle",
    )
    (stepped,) = call(
        functools.partial(steps_kernel, block_cols),
        [(smem, seam_rows)]
        + [
            (vmem, x)
            for x in (
                from_pair, from_next, far0, far1, low, centre, high,
                hot, table, weight, ext, outer,
            )
        ],
        [(fields.shape, f32)],
        10**8,
        scratch=[pltpu.VMEM((EXT // LANES, 3 * NODES, LANES), f32)],
        name="steps",
    )
    return stepped


def solution(mesh):
    return jax.shard_map(
        on_device,
        mesh=mesh,
        in_specs=(
            P(None, None, None, ("face", "blk")),
            P(None, None, ("face", "blk")),
            P(None, None, ("face", "blk")),
            P(None, None, ("face", "blk")),
            P(None, None, ("face", "blk")),
            P(("face", "blk"), None),
            P(),
        ),
        out_specs=P(None, None, None, ("face", "blk")),
        check_vma=False,
    )
```

```python
import functools
import math

import jax
import jax.numpy as jnp
import ml_dtypes
import numpy as np
from jax import lax
from jax.experimental import pallas as pl
from jax.experimental.pallas import tpu as pltpu
from jax.sharding import PartitionSpec as P

BY = 16
GX = 16
GY = 16
NP = 8
NODES = NP * NP
ARRAYS = 7
ROWS = ARRAYS * NODES
MOVED = 6 * NODES
EDGE_ROWS = 4 * NP
ALL_ROWS = ROWS + EDGE_ROWS
HALF_ROWS = (MOVED + NODES // 2 + 2 * NP) // 2
RING = 4
RIM_ROWS = ROWS + 2 * EDGE_ROWS
CORNER_ROWS = (MOVED + NODES // 2 + 4 * NP) // 8
PITCH = GX + 2 * RING
MID = GY * PITCH
LANES = 128
EXT = MID + 2 * LANES
LEAD = LANES - RING * PITCH
ELEMENTS = GX * GY

time_step = 0.03
hyper_coeff = 0.0002

f32 = jnp.float32
bf16 = jnp.bfloat16
i32 = jnp.int32


def legendre_pair(location, degree):
    lower_value = 1.0
    upper_value = location
    for polynomial_order in range(2, degree + 1):
        lower_value, upper_value = (
            upper_value,
            (
                (2 * polynomial_order - 1) * location * upper_value
                - (polynomial_order - 1) * lower_value
            )
            / polynomial_order,
        )
    return (lower_value, upper_value)


def gll_tables(points):
    degree = points - 1
    locations = [-math.cos(math.pi * position / degree) for position in range(points)]
    for iteration in range(100):
        updated = []
        for location in locations:
            lower_value, upper_value = legendre_pair(location, degree)
            updated.append(
                location - (location * upper_value - lower_value) / ((degree + 1) * upper_value)
            )
        locations = updated
    locations[0] = -1.0
    locations[degree] = 1.0
    legendre_at = [legendre_pair(location, degree)[1] for location in locations]
    weights = [2.0 / (degree * (degree + 1) * value * value) for value in legendre_at]
    corner_value = degree * (degree + 1) / 4.0
    derivative = []
    for row_index in range(points):
        row_values = []
        for column_index in range(points):
            if row_index != column_index:
                row_values.append(
                    legendre_at[row_index]
                    / (legendre_at[column_index] * (locations[row_index] - locations[column_index]))
                )
            elif row_index == 0:
                row_values.append(-corner_value)
            elif row_index == degree:
                row_values.append(corner_value)
            else:
                row_values.append(0.0)
        derivative.append(row_values)
    return np.asarray(weights, np.float64), np.asarray(derivative, np.float64)


def in_three(matrix):
    high = matrix.astype(ml_dtypes.bfloat16)
    low = (matrix - high.astype(np.float64)).astype(ml_dtypes.bfloat16)
    return np.concatenate([high, high, low], 1)


def operator_table():
    weights, derivative = gll_tables(NP)
    eye = np.eye(NP)
    node_weight = np.outer(weights, weights).reshape(NODES, 1)
    along_x = node_weight * np.kron(derivative, eye)
    along_y = node_weight * np.kron(eye, derivative)
    second = derivative @ derivative
    both = node_weight * (np.kron(second, eye) + np.kron(eye, second))
    table = np.zeros((4 * NODES, 6 * NODES), ml_dtypes.bfloat16)
    table[:NODES, : 3 * NODES] = in_three(along_x)
    table[NODES : 2 * NODES, : 3 * NODES] = in_three(along_y)
    table[2 * NODES : 3 * NODES, : 3 * NODES] = in_three(along_x)
    table[2 * NODES : 3 * NODES, 3 * NODES :] = in_three(along_y)
    table[3 * NODES :, : 3 * NODES] = in_three(both)
    spread = np.broadcast_to(node_weight, (NODES, LANES)).astype(np.float32)
    return table.astype(np.float32), np.ascontiguousarray(spread)


def lane_tables():
    table = np.zeros((24, MID), np.int32)
    for lane in range(MID):
        row, col = divmod(lane, PITCH)
        x = col - RING
        own = 0 <= x < GX
        table[0:8, lane] = x * GY + row if own else -1
        if not own:
            table[8:16, lane] = row * RING + (col if x < 0 else x - GX)
        table[16:24, lane] = 0 if own else (1 if x < 0 else 2)
    ext = np.zeros((8, EXT), np.int32)
    outer = np.zeros((24, 2 * LANES), np.int32)
    for lane in range(EXT):
        row, col = divmod(lane - LEAD, PITCH)
        y = row - RING
        x = col - RING
        inside = 0 <= row < GY + 2 * RING
        ext[0, lane] = x in (-RING, GX + RING - 1)
        ext[1, lane] = y == GY - 1
        ext[2, lane] = y == 0
        ext[3, lane] = 0 <= y < GY and 0 <= x < GX
        ext[4, lane] = y == -RING
        ext[5, lane] = y == GY + RING - 1
        if inside and not 0 <= y < GY:
            place = lane if y < 0 else lane - LANES - MID + LANES
            step = y + RING if y < 0 else y - GY
            if 0 <= x < GX:
                outer[0:8, place] = step * GX + x
                outer[8:16, place] = 1
            else:
                outer[0:8, place] = LANES + step * RING + (x + RING if x < 0 else x - GX)
                outer[8:16, place] = 2 if x < 0 else 3
            outer[16:24, place] = y > 0
    return table, ext, outer


def dot(a, b):
    return jnp.dot(a, b, preferred_element_type=f32)


def dot_other(a, b):
    return lax.dot_general(a, b, (((1,), (1,)), ((), ())), preferred_element_type=f32)


def picked(values, one_hot, product=dot):
    high = values.astype(bf16)
    low = (values - high.astype(f32)).astype(bf16)
    return product(high, one_hot) + product(low, one_hot)


def as_one_hot(row_of_lane, depth):
    index = lax.broadcasted_iota(i32, (depth, row_of_lane.shape[1]), 0)
    return jnp.where(index == row_of_lane[0:1], 1.0, 0.0).astype(bf16)


def high_low_high(values):
    high = values.astype(bf16)
    low = (values - high.astype(f32)).astype(bf16)
    return [high, low, high]


def by_slot(slot_ref, cell_of_lane):
    slots = jnp.broadcast_to(slot_ref[...], (8, ELEMENTS)).astype(f32).astype(bf16)
    chosen = dot(slots, as_one_hot(cell_of_lane, ELEMENTS))
    chosen = jnp.where(cell_of_lane >= 0, chosen, -1.0)
    index = lax.broadcasted_iota(i32, (ELEMENTS, cell_of_lane.shape[1]), 0).astype(f32)
    return jnp.where(index == chosen[0:1], 1.0, 0.0).astype(bf16)


def brought(sources, buffers, sems):
    copies = [
        pltpu.make_async_copy(source, buffer, sems.at[k])
        for k, (source, buffer) in enumerate(zip(sources, buffers))
    ]
    for copy in copies:
        copy.start()
    for copy in copies:
        copy.wait()


def stored_rows(fields_ref, others):
    fields = fields_ref[...].reshape(3 * NODES, ELEMENTS)
    others = [ref[...].reshape(NODES, ELEMENTS) for ref in others]
    return jnp.concatenate([fields[:NODES] - others[-1], fields[NODES:]] + others, 0)


def mass_tendency(table, p, u, v, area_depth, weighted_area, spin):
    slopes = dot(table[: 2 * NODES, : 3 * NODES], jnp.concatenate(high_low_high(p), 0))
    flux = high_low_high(area_depth * u) + high_low_high(area_depth * v)
    spread = dot(table[2 * NODES : 3 * NODES], jnp.concatenate(flux, 0))
    return [
        -spread,
        spin * v - weighted_area * slopes[:NODES],
        -spin * u - weighted_area * slopes[NODES:],
    ]


def edge_values(table_ref, weight_ref, p, u, v, area, depth, spin):
    root = jnp.sqrt(area)
    mass = jnp.concatenate([weight_ref[...]] * (area.shape[1] // LANES), 1) * area
    table = table_ref[...].astype(bf16)
    return mass_tendency(table, p, u, v, root * depth, root, mass * spin) + [mass]


def row_edges(sums):
    return tuple(sums[0, pl.ds(j, EDGE_ROWS, stride=NP)] for j in (NP - 1, 0))


def beside(left, right):
    return jnp.concatenate([left, right], 1)


def one_of_four(parts, index):
    out = parts[0]
    for k in range(1, 4):
        out = jnp.where(index == k, parts[k], out)
    return out


def folded(tide, kept, late, step):
    half = NODES // 2
    back = pltpu.roll(tide[half:], LANES - step, 1)
    onward = pltpu.roll(tide[half:], step, 1)
    return jnp.where(kept, tide[:half], jnp.where(late, back, onward))


def unfolded(rows, late, step):
    back = pltpu.roll(rows, LANES - step, 1)
    onward = pltpu.roll(rows, step, 1)
    return jnp.concatenate([rows, jnp.where(late, onward, back)], 0)


def strip_rows(parts, late, shift, rims):
    lane = lax.broadcasted_iota(i32, (1, LANES), 1)
    index = (lane >> shift) & 3
    kept = jnp.where(late, index // 2, 1 - index // 2) != 0
    tide = folded(parts[6], kept, late, 2 << shift)
    rim = one_of_four(rims, index)
    return jnp.concatenate(parts[:6] + [tide, rim, jnp.zeros_like(rim)], 0)


def placed_rows(whole, late, shift):
    half = NODES // 2
    tide = unfolded(whole[MOVED : MOVED + half], late, 2 << shift)
    rim = whole[MOVED + half : MOVED + half + NP]
    return jnp.concatenate([whole[:MOVED], tide] + spread_out(rim, late, shift), 0)


def spread_out(rim, late, shift):
    parts = []
    for k in range(4):
        first = pltpu.roll(rim, (LANES - (k << shift)) % LANES, 1) if k else rim
        last = pltpu.roll(rim, (3 - k) << shift, 1) if k < 3 else rim
        parts.append(jnp.where(late, first, last))
    return parts


def with_row_rim(whole, sums, top):
    north, south = row_edges(sums)
    rim = jnp.where(top, pltpu.roll(north, RING, 1), pltpu.roll(south, LANES - RING, 1))
    parts = [rim[k * NP : (k + 1) * NP] for k in range(4)]
    lane = lax.broadcasted_iota(i32, (1, LANES), 1)
    spots = []
    for k, part in enumerate(parts):
        first = pltpu.roll(part, k * RING, 1) if k else part
        last = pltpu.roll(part, (LANES - (3 - k) * RING) % LANES, 1) if k < 3 else part
        spots.append(jnp.where(top, first, last))
    rim = one_of_four(spots, (lane >> 2) & 3)
    return jnp.concatenate([whole[: MOVED + NODES // 2 + NP], rim], 0)


def corner_of(whole, start, top):
    lane = lax.broadcasted_iota(i32, (1, LANES), 1)
    base = LANES - start - jnp.where(top != 0, 48, 0)
    whole = jnp.concatenate([whole, jnp.zeros((8 * CORNER_ROWS - whole.shape[0], LANES), f32)], 0)
    out = None
    for k in range(8):
        part = whole[k * CORNER_ROWS : (k + 1) * CORNER_ROWS]
        part = pltpu.roll(part, (base + 16 * k) & (LANES - 1), 1)
        out = part if k == 0 else jnp.where(lane >= 16 * k, part, out)
    return out


def packed(whole):
    second = lax.broadcasted_iota(i32, (1, LANES), 1) >= 64
    top, bottom = whole[:HALF_ROWS], whole[HALF_ROWS:]
    return (
        jnp.where(second, pltpu.roll(bottom, 64, 1), top),
        jnp.where(second, bottom, pltpu.roll(top, 64, 1)),
    )


def unpacked(in0, in1):
    second = lax.broadcasted_iota(i32, (1, LANES), 1) >= 64
    top = jnp.where(second, pltpu.roll(in1, 64, 1), in0)
    bottom = jnp.where(second, in1, pltpu.roll(in0, 64, 1))
    return jnp.concatenate([top, bottom], 0)


def seam_flags(seam_ref, block_cols):
    size_y = seam_ref.shape[1]
    face = lax.axis_index("face")
    blk = lax.axis_index("blk")
    block_x = blk // BY

    def flipped(k):
        return jnp.where(lax.rem(seam_ref[k, 1] - seam_ref[k, 0] + size_y, size_y) != 1, 1, 0)

    first, second = flipped(0), flipped(1)
    east_flip = jnp.where(face == 0, first, second)
    west_flip = jnp.where(face == 0, second, first)
    if block_cols == 1:
        return 1 - east_flip, 0, east_flip, 1
    at_east = jnp.where(block_x == block_cols - 1, east_flip, 0)
    at_west = jnp.where(block_x == 0, west_flip, 0)
    return 1, at_east, 0, at_west


def strips_kernel(block_cols, *refs):
    sources = refs[:9]
    out1_ref, far1_ref, out0_ref, far0_ref, next_ref, pair_ref, stored_ref = refs[9:16]
    buffers, sems, sums = refs[16:25], refs[25], refs[26]
    brought(sources, buffers, sems)
    seam_ref, slot_ref, fields_ref, area_ref, depth_ref, spin_ref, tide_ref = buffers[:7]
    table_ref, weight_ref = buffers[7:]
    east0, flip0, east1, flip1 = seam_flags(seam_ref, block_cols)
    lane = lax.broadcasted_iota(i32, (8, 2 * LANES), 1)
    second = (lane & 64) != 0
    place = lane & 63
    row = place >> 2
    row = jnp.where(jnp.where(second, flip1, flip0) != 0, GY - 1 - row, row)
    east = jnp.where(second, east1, east0) != 0
    col = jnp.where(east, GX - RING, 0) + (place & 3)
    col = jnp.where(lane >= LANES, jnp.where(east, GX - RING - 1, RING), col)
    cells = col * GY + row
    odd = lax.axis_index("blk") & 1

    def goes_up(lane):
        return jnp.where((lane & 64) != 0, odd, 1 - odd) != 0

    up = goes_up(lane)
    row = jnp.where(up, GY - RING, 0) + ((lane & 63) >> 4)
    row = jnp.where(lane >= LANES, jnp.where(up, GY - RING - 1, RING), row)
    one_hot = by_slot(slot_ref, beside(cells, (lane & 15) * GY + row))
    stored = stored_rows(fields_ref, (area_ref, depth_ref, spin_ref, tide_ref))
    stored_ref[...] = stored
    both = picked(stored, one_hot)

    lane = lax.broadcasted_iota(i32, (1, LANES), 1)
    second = lane >= 64
    flip = jnp.where(second, flip1, flip0) != 0
    sign = jnp.where(flip, -1.0, 1.0)
    node = lax.broadcasted_iota(i32, (1, NP, 1), 1)

    def in_frame(values):
        shaped = values.reshape(-1, NP, LANES)
        turned = pltpu.roll(shaped, 4, 1)
        turned = jnp.where((node & 2) == 0, pltpu.roll(turned, 6, 1), pltpu.roll(turned, 2, 1))
        turned = jnp.where((node & 1) == 0, pltpu.roll(turned, 7, 1), pltpu.roll(turned, 1, 1))
        values = jnp.where(flip[None], turned, shaped).reshape(values.shape)
        parts = [values[k * NODES : (k + 1) * NODES] for k in range(ARRAYS)]
        parts[2] = parts[2] * sign
        parts[5] = parts[5] * sign
        return parts

    strip, ring = in_frame(both[:, :LANES]), in_frame(both[:, LANES : 2 * LANES])
    rows, behind = (
        [part[k * NODES : (k + 1) * NODES] for k in range(ARRAYS)]
        for part in (both[:, 2 * LANES : 3 * LANES], both[:, 3 * LANES :])
    )
    edges = edge_values(
        table_ref,
        weight_ref,
        *(jnp.concatenate(parts, 1) for parts in zip(strip[:6], ring[:6], behind[:6])),
    )
    east = jnp.where(second, east1, east0) != 0
    ends = [part[:, LANES : 2 * LANES] for part in edges]
    ends = [jnp.where(east, part[NODES - NP :], part[:NP]) for part in ends]
    whole = strip_rows(strip, east, 0, ends)
    out0_ref[...], out1_ref[...] = packed(whole)
    sums[0] = jnp.concatenate([part[:, :LANES] for part in edges], 0)
    top0, top1 = odd ^ flip0, odd ^ flip1
    whole = with_row_rim(whole, sums, jnp.where(second, top1, top0) != 0)
    far0_ref[...] = corner_of(whole, 0, top0)
    far1_ref[...] = corner_of(whole, 64, top1)
    sums[0] = jnp.concatenate([part[:, 2 * LANES :] for part in edges], 0)
    up = goes_up(lane)
    rim = jnp.where(up, *row_edges(sums))
    rim = [rim[k * NP : (k + 1) * NP] for k in range(4)]
    pair_ref[...], next_ref[...] = packed(strip_rows(rows, up, 4, rim))


def corners_kernel(in1_ref, in0_ref, pair_ref, table_ref, weight_ref, *refs):
    out_ref, sums = refs[-2:]
    top = 1 - (lax.axis_index("blk") & 1)
    whole = unpacked(in0_ref[...], in1_ref[...])
    parts = [whole[k * NODES : (k + 1) * NODES] for k in range(6)]
    sums[0] = jnp.concatenate(edge_values(table_ref, weight_ref, *parts), 0)
    whole = with_row_rim(whole, sums, jnp.broadcast_to(top != 0, (1, LANES)))
    out_ref[:HALF_ROWS] = pair_ref[...]
    out_ref[HALF_ROWS : HALF_ROWS + CORNER_ROWS] = corner_of(whole, 0, top)
    out_ref[HALF_ROWS + CORNER_ROWS :] = corner_of(whole, 64, top)


def own_kernel(stored_ref, slot_ref, lanes_ref, own_ref, hot_ref):
    one_hot = by_slot(slot_ref, lanes_ref[0:8])
    own_ref[...] = picked(stored_ref[...], one_hot)
    hot_ref[...] = one_hot


def middle_kernel(
    block_cols, seam_ref, in0_ref, in1_ref, own_ref, lanes_ref, low_ref, centre_ref, high_ref
):
    east0, flip0, east1, flip1 = seam_flags(seam_ref, block_cols)
    second = lax.broadcasted_iota(i32, (1, LANES), 1) >= 64
    late = jnp.where(second, east1, east0) == 0
    whole = placed_rows(unpacked(in0_ref[...], in1_ref[...]), late, 0)
    side = lanes_ref[16:24]
    first_at = jnp.where(side == 2, 64 * (1 - east0), 64 * east0)
    place = jnp.where(side == 0, -1, lanes_ref[8:16] + first_at)
    placed = picked(whole, as_one_hot(place, LANES))
    for k, ref in enumerate((low_ref, centre_ref, high_ref)):
        part = slice(k * LANES, (k + 1) * LANES)
        ref[:ROWS] = placed[:ROWS, part] + own_ref[:, part]
        ref[ROWS:] = placed[ROWS:, part]


def steps_kernel(
    block_cols, seam_ref, pair_ref, next_ref, far0_ref, far1_ref, low_ref, centre_ref,
    high_ref, hot_ref, table_ref, weight_ref, ext_ref, outer_ref, out_ref, sums,
):
    east0, flip0, east1, flip1 = seam_flags(seam_ref, block_cols)
    odd = lax.axis_index("blk") & 1
    block_y = lax.rem(lax.axis_index("blk"), BY)

    lane = lax.broadcasted_iota(i32, (1, LANES), 1)
    pair = pair_ref[...]
    late = jnp.where(lane < 64, odd, 1 - odd) != 0
    strips = placed_rows(unpacked(pair[:HALF_ROWS], next_ref[...]), late, 4)
    strips = jnp.concatenate(
        [strips[:ROWS], jnp.zeros((EDGE_ROWS, LANES), f32), strips[ROWS:]], 0
    )
    near = pair[HALF_ROWS:]
    sources = (near[:CORNER_ROWS], near[CORNER_ROWS:], far0_ref[...], far1_ref[...])
    corners = []
    for k in range(8):
        rows = None
        for n, source in enumerate(sources):
            shift = 16 * (n - k) % LANES
            part = pltpu.roll(source, shift, 1) if shift else source
            rows = part if n == 0 else jnp.where(lane >= 16 * n, part, rows)
        corners.append(rows)
    corners = jnp.concatenate(corners, 0)
    rim = MOVED + NODES // 2 + NP
    late = jnp.where((lane & 16) != 0, east1, east0) == 0
    below = jnp.where((lane & 32) != 0, 1 - odd, odd) != 0
    corners = jnp.concatenate(
        [placed_rows(corners, late, 0)] + spread_out(corners[rim : rim + NP], below, 2), 0
    )
    around = jnp.concatenate([strips, corners], 1)
    kind = outer_ref[8:16]
    sender = jnp.where(outer_ref[16:24] != 0, odd, 1 - odd)
    strip_at = jnp.where(kind == 3, 16 * (1 - east0), 16 * east0)
    place = outer_ref[0:8] + jnp.where(kind == 1, 64 * sender, 32 * sender + strip_at)
    outer = picked(around, as_one_hot(jnp.where(kind == 0, -1, place), 2 * LANES))
    tiles = (outer[:, :LANES], low_ref, centre_ref, high_ref, outer[:, LANES:])

    def rows_of(start, count):
        return jnp.concatenate([ref[start : start + count] for ref in tiles], 1)

    table = table_ref[...].astype(bf16)
    weight = jnp.concatenate([weight_ref[...]] * len(tiles), 1)
    at_rim = ext_ref[0:1] != 0
    top_row = jnp.where(block_y == BY - 1, ext_ref[1:2], 0) != 0
    bottom_row = jnp.where(block_y == 0, ext_ref[2:3], 0) != 0

    first_row = ext_ref[4:5] != 0
    last_row = ext_ref[5:6] != 0

    def edge_sum(parts, rims=None, rows=None):
        count = len(parts) * NP
        for c, part in enumerate(parts):
            west, east = part[:NP], part[NODES - NP :]
            at_east = pltpu.roll(west, EXT - 1, 1)
            at_west = pltpu.roll(east, 1, 1)
            if rims is not None:
                at_east = jnp.where(at_rim, rims[c], at_east)
                at_west = jnp.where(at_rim, rims[c], at_west)
            part = jnp.concatenate([west + at_west, part[NP : NODES - NP], east + at_east], 0)
            for k in range(len(tiles)):
                sums[k, c * NODES : (c + 1) * NODES] = part[:, k * LANES : (k + 1) * LANES]
        south_at, north_at = pl.ds(0, count, stride=NP), pl.ds(NP - 1, count, stride=NP)
        south = jnp.concatenate([sums[k, south_at] for k in range(len(tiles))], 1)
        north = jnp.concatenate([sums[k, north_at] for k in range(len(tiles))], 1)
        at_north = jnp.where(top_row, 0.0, pltpu.roll(south, EXT - PITCH, 1))
        at_south = jnp.where(bottom_row, 0.0, pltpu.roll(north, PITCH, 1))
        if rows is not None:
            at_north = jnp.where(last_row, rows, at_north)
            at_south = jnp.where(first_row, rows, at_south)
        to_north, to_south = north + at_north, south + at_south
        for k in range(len(tiles)):
            sums[k, south_at] = to_south[:, k * LANES : (k + 1) * LANES]
            sums[k, north_at] = to_north[:, k * LANES : (k + 1) * LANES]
        return [
            jnp.concatenate(
                [sums[k, c * NODES : (c + 1) * NODES] for k in range(len(tiles))], 1
            )
            for c in range(len(parts))
        ]

    start = [rows_of(c * NODES, NODES) for c in range(3)]
    area, depth, spin, tide = [rows_of(c * NODES, NODES) for c in range(3, ARRAYS)]
    root = jnp.sqrt(area)
    mass = weight * area
    mass_spin = mass * spin
    area_depth = root * depth
    rims = [rows_of(ROWS + c * NP, NP) for c in range(4)]
    blank = jnp.zeros((EDGE_ROWS, MID), f32)
    rows = jnp.concatenate([tiles[0][ALL_ROWS:], blank, tiles[-1][ALL_ROWS:]], 1)
    node = lax.broadcasted_iota(i32, (1, NP, 1), 1)
    east = pltpu.roll(rows, EXT - 1, 1).reshape(4, NP, EXT)
    west = pltpu.roll(rows, 1, 1).reshape(4, NP, EXT)
    rows = (
        rows.reshape(4, NP, EXT)
        + jnp.where(node == NP - 1, pltpu.roll(east, NP - 1, 1), 0.0)
        + jnp.where(node == 0, pltpu.roll(west, 1, 1), 0.0)
    ).reshape(EDGE_ROWS, EXT)
    per_mass = 1.0 / edge_sum([mass], rims[3:], rows[3 * NP :])[0]

    def average(parts, rims=None, rows=None):
        return [part * per_mass for part in edge_sum(parts, rims, rows)]

    def tendency(s):
        return mass_tendency(table, *s, area_depth, root, mass_spin)

    def laplace(s):
        return [
            dot(table[3 * NODES :, : 3 * NODES], jnp.concatenate(high_low_high(part), 0))
            for part in s
        ]

    change = average(tendency(start), rims[:3], rows[: 3 * NP])
    one = [s + time_step * c for s, c in zip(start, change)]
    change = average(tendency(one))
    two = [0.75 * s + 0.25 * (o + time_step * c) for s, o, c in zip(start, one, change)]
    change = average(tendency(two))
    three = [s / 3.0 + 2.0 / 3.0 * (o + time_step * c) for s, o, c in zip(start, two, change)]
    three[0] = three[0] + tide
    biharmonic = average(laplace(average(laplace(three))))
    own = ext_ref[3:4, LANES : LANES + MID] != 0
    stepped = [
        jnp.where(
            own,
            (s - time_step * hyper_coeff * b)[:, LANES : LANES + MID],
            0.0,
        )
        for s, b in zip(three, biharmonic)
    ]
    stored = picked(jnp.concatenate(stepped, 0), hot_ref[...], dot_other)
    out_ref[...] = stored.reshape(out_ref.shape)


def on_device(fields, jacobian, water_depth, coriolis, tide_height, slot_of, seam_rows):
    block_cols = lax.axis_size("blk") // BY
    table, weight = operator_table()
    table, weight, lanes, ext, outer = map(jnp.asarray, (table, weight, *lane_tables()))
    vmem = pl.BlockSpec(memory_space=pltpu.VMEM)
    smem = pl.BlockSpec(memory_space=pltpu.SMEM)
    hbm = pl.BlockSpec(memory_space=pltpu.HBM)
    params = pltpu.CompilerParams(vmem_limit_bytes=48 * 2**20)
    held = (fields, jacobian, water_depth, coriolis, tide_height)

    def call(kernel, ins, outs, cost, scratch=(), name=None):
        return pl.pallas_call(
            kernel,
            out_shape=[jax.ShapeDtypeStruct(*out) for out in outs],
            in_specs=[spec for spec, value in ins],
            out_specs=[vmem] * len(outs),
            scratch_shapes=list(scratch),
            compiler_params=params,
            cost_estimate=pl.CostEstimate(
                flops=cost, bytes_accessed=2 * 2**20, transcendentals=0
            ),
            name=name,
        )(
            *[
                pltpu.with_memory_space_constraint(value, pltpu.HBM) if spec is hbm else value
                for spec, value in ins
            ]
        )

    strip = ((HALF_ROWS, LANES), f32)
    def room(values, spaces=None):
        spaces = spaces or [pltpu.VMEM] * len(values)
        buffers = [space(x.shape, x.dtype) for space, x in zip(spaces, values)]
        return buffers + [pltpu.SemaphoreType.DMA((len(values),))]

    needed = (seam_rows, slot_of, *held, table, weight)
    corner = ((CORNER_ROWS, LANES), f32)
    scratch = [pltpu.VMEM((1, 4 * NODES, LANES), f32)]
    strip1, far1, strip0, far0, to_next, to_pair, stored = call(
        functools.partial(strips_kernel, block_cols),
        [(hbm, x) for x in needed],
        [strip, corner, strip, corner, strip, strip, ((ROWS, ELEMENTS), f32)],
        10**8,
        scratch=room(needed, [pltpu.SMEM] + [pltpu.VMEM] * (len(needed) - 1)) + scratch,
        name="strips",
    )
    span = block_cols * BY
    both = ("face", "blk")
    places = [(f, x, y) for f in range(2) for x in range(block_cols) for y in range(BY)]

    def rank(face, block_x, block_y):
        return face * span + block_x * BY + block_y

    def same(y):
        return y

    def in_pair(y):
        return y ^ 1

    def next_pair(y):
        other = y + 1 if y % 2 else y - 1
        return other if 0 <= other < BY else y

    def swapped(value, partner):
        return lax.ppermute(
            value, both, [(rank(f, x, y), rank(f, x, partner(y))) for f, x, y in places]
        )

    def across(value0, value1, partner):
        last = block_cols - 1
        straight = {
            (f, x, y): (f, x + 1, partner(y)) if x < last else (1 - f, 0, partner(y))
            for f, x, y in places
        }
        turned = {
            (f, last, y): (1 - f, 0, BY - 1 - partner(y)) for f in range(2) for y in range(BY)
        }

        def eastward(value, pairs):
            return lax.ppermute(value, both, [(rank(*a), rank(*b)) for a, b in pairs.items()])

        def westward(value, pairs):
            return lax.ppermute(value, both, [(rank(*b), rank(*a)) for a, b in pairs.items()])

        if block_cols == 1:
            return eastward(value0, straight), eastward(value1, turned)
        flipped = (seam_rows[:, 1] - seam_rows[:, 0]) % seam_rows.shape[1] != 1
        face = lax.axis_index("face")
        block_x = lax.axis_index("blk") // BY
        return (
            jnp.where(
                (block_x == last) & flipped[face],
                westward(value1, turned),
                westward(value1, straight),
            ),
            jnp.where(
                (block_x == 0) & flipped[1 - face],
                eastward(value0, turned),
                eastward(value0, straight),
            ),
        )

    halo0, halo1 = across(strip0, strip1, same)
    far0, far1 = across(far0, far1, next_pair)
    from_next = swapped(to_next, next_pair)
    own, hot = call(
        own_kernel,
        [(vmem, x) for x in (stored, slot_of, lanes)],
        [((ROWS, MID), f32), ((ELEMENTS, MID), bf16)],
        10**8,
        name="own",
    )
    (to_pair,) = call(
        corners_kernel,
        [(vmem, x) for x in (halo1, halo0, to_pair, table, weight, hot, far1, far0, from_next)],
        [((HALF_ROWS + 2 * CORNER_ROWS, LANES), f32)],
        10**8,
        scratch=scratch,
        name="corners",
    )
    from_pair = swapped(to_pair, in_pair)
    tile = ((ALL_ROWS, LANES), f32)
    low, centre, high = call(
        functools.partial(middle_kernel, block_cols),
        [(smem, seam_rows)] + [(vmem, x) for x in (halo0, halo1, own, lanes)],
        [tile, tile, tile],
        10**8,
        name="middle",
    )
    (stepped,) = call(
        functools.partial(steps_kernel, block_cols),
        [(smem, seam_rows)]
        + [
            (vmem, x)
            for x in (
                from_pair, from_next, far0, far1, low, centre, high,
                hot, table, weight, ext, outer,
            )
        ],
        [(fields.shape, f32)],
        10**8,
        scratch=[pltpu.VMEM((EXT // LANES, 3 * NODES, LANES), f32)],
        name="steps",
    )
    return stepped


def solution(mesh):
    return jax.shard_map(
        on_device,
        mesh=mesh,
        in_specs=(
            P(None, None, None, ("face", "blk")),
            P(None, None, ("face", "blk")),
            P(None, None, ("face", "blk")),
            P(None, None, ("face", "blk")),
            P(None, None, ("face", "blk")),
            P(("face", "blk"), None),
            P(),
        ),
        out_specs=P(None, None, None, ("face", "blk")),
        check_vma=False,
    )
```

```python
import functools
import math

import jax
import jax.numpy as jnp
import ml_dtypes
import numpy as np
from jax import lax
from jax.experimental import pallas as pl
from jax.experimental.pallas import tpu as pltpu
from jax.sharding import PartitionSpec as P

BY = 16
GX = 16
GY = 16
NP = 8
NODES = NP * NP
ARRAYS = 7
ROWS = ARRAYS * NODES
MOVED = 6 * NODES
EDGE_ROWS = 4 * NP
ALL_ROWS = ROWS + EDGE_ROWS
HALF_ROWS = (MOVED + NODES // 2 + 2 * NP) // 2
RING = 4
RIM_ROWS = ROWS + 2 * EDGE_ROWS
CORNER_ROWS = (MOVED + NODES // 2 + 4 * NP) // 8
PITCH = GX + 2 * RING
MID = GY * PITCH
LANES = 128
EXT = MID + 2 * LANES
LEAD = LANES - RING * PITCH
ELEMENTS = GX * GY

time_step = 0.03
hyper_coeff = 0.0002

f32 = jnp.float32
bf16 = jnp.bfloat16
i32 = jnp.int32


def legendre_pair(location, degree):
    lower_value = 1.0
    upper_value = location
    for polynomial_order in range(2, degree + 1):
        lower_value, upper_value = (
            upper_value,
            (
                (2 * polynomial_order - 1) * location * upper_value
                - (polynomial_order - 1) * lower_value
            )
            / polynomial_order,
        )
    return (lower_value, upper_value)


def gll_tables(points):
    degree = points - 1
    locations = [-math.cos(math.pi * position / degree) for position in range(points)]
    for iteration in range(100):
        updated = []
        for location in locations:
            lower_value, upper_value = legendre_pair(location, degree)
            updated.append(
                location - (location * upper_value - lower_value) / ((degree + 1) * upper_value)
            )
        locations = updated
    locations[0] = -1.0
    locations[degree] = 1.0
    legendre_at = [legendre_pair(location, degree)[1] for location in locations]
    weights = [2.0 / (degree * (degree + 1) * value * value) for value in legendre_at]
    corner_value = degree * (degree + 1) / 4.0
    derivative = []
    for row_index in range(points):
        row_values = []
        for column_index in range(points):
            if row_index != column_index:
                row_values.append(
                    legendre_at[row_index]
                    / (legendre_at[column_index] * (locations[row_index] - locations[column_index]))
                )
            elif row_index == 0:
                row_values.append(-corner_value)
            elif row_index == degree:
                row_values.append(corner_value)
            else:
                row_values.append(0.0)
        derivative.append(row_values)
    return np.asarray(weights, np.float64), np.asarray(derivative, np.float64)


def in_three(matrix):
    high = matrix.astype(ml_dtypes.bfloat16)
    low = (matrix - high.astype(np.float64)).astype(ml_dtypes.bfloat16)
    return np.concatenate([high, high, low], 1)


def operator_table():
    weights, derivative = gll_tables(NP)
    eye = np.eye(NP)
    node_weight = np.outer(weights, weights).reshape(NODES, 1)
    along_x = node_weight * np.kron(derivative, eye)
    along_y = node_weight * np.kron(eye, derivative)
    second = derivative @ derivative
    both = node_weight * (np.kron(second, eye) + np.kron(eye, second))
    table = np.zeros((4 * NODES, 6 * NODES), ml_dtypes.bfloat16)
    table[:NODES, : 3 * NODES] = in_three(along_x)
    table[NODES : 2 * NODES, : 3 * NODES] = in_three(along_y)
    table[2 * NODES : 3 * NODES, : 3 * NODES] = in_three(along_x)
    table[2 * NODES : 3 * NODES, 3 * NODES :] = in_three(along_y)
    table[3 * NODES :, : 3 * NODES] = in_three(both)
    spread = np.broadcast_to(node_weight, (NODES, LANES)).astype(np.float32)
    return table.astype(np.float32), np.ascontiguousarray(spread)


def lane_tables():
    table = np.zeros((24, MID), np.int32)
    for lane in range(MID):
        row, col = divmod(lane, PITCH)
        x = col - RING
        own = 0 <= x < GX
        table[0:8, lane] = x * GY + row if own else -1
        if not own:
            table[8:16, lane] = row * RING + (col if x < 0 else x - GX)
        table[16:24, lane] = 0 if own else (1 if x < 0 else 2)
    ext = np.zeros((8, EXT), np.int32)
    outer = np.zeros((24, 2 * LANES), np.int32)
    for lane in range(EXT):
        row, col = divmod(lane - LEAD, PITCH)
        y = row - RING
        x = col - RING
        inside = 0 <= row < GY + 2 * RING
        ext[0, lane] = x in (-RING, GX + RING - 1)
        ext[1, lane] = y == GY - 1
        ext[2, lane] = y == 0
        ext[3, lane] = 0 <= y < GY and 0 <= x < GX
        ext[4, lane] = y == -RING
        ext[5, lane] = y == GY + RING - 1
        if inside and not 0 <= y < GY:
            place = lane if y < 0 else lane - LANES - MID + LANES
            step = y + RING if y < 0 else y - GY
            if 0 <= x < GX:
                outer[0:8, place] = step * GX + x
                outer[8:16, place] = 1
            else:
                outer[0:8, place] = LANES + step * RING + (x + RING if x < 0 else x - GX)
                outer[8:16, place] = 2 if x < 0 else 3
            outer[16:24, place] = y > 0
    return table, ext, outer


def dot(a, b):
    return jnp.dot(a, b, preferred_element_type=f32)


def dot_other(a, b):
    return lax.dot_general(a, b, (((1,), (1,)), ((), ())), preferred_element_type=f32)


def picked(values, one_hot, product=dot):
    high = values.astype(bf16)
    low = (values - high.astype(f32)).astype(bf16)
    return product(high, one_hot) + product(low, one_hot)


def as_one_hot(row_of_lane, depth):
    index = lax.broadcasted_iota(i32, (depth, row_of_lane.shape[1]), 0)
    return jnp.where(index == row_of_lane[0:1], 1.0, 0.0).astype(bf16)


def high_low_high(values):
    high = values.astype(bf16)
    low = (values - high.astype(f32)).astype(bf16)
    return [high, low, high]


def by_slot(slot_ref, cell_of_lane):
    slots = jnp.broadcast_to(slot_ref[...], (8, ELEMENTS)).astype(f32).astype(bf16)
    chosen = dot(slots, as_one_hot(cell_of_lane, ELEMENTS))
    chosen = jnp.where(cell_of_lane >= 0, chosen, -1.0)
    index = lax.broadcasted_iota(i32, (ELEMENTS, cell_of_lane.shape[1]), 0).astype(f32)
    return jnp.where(index == chosen[0:1], 1.0, 0.0).astype(bf16)


def brought(sources, buffers, sems):
    copies = [
        pltpu.make_async_copy(source, buffer, sems.at[k])
        for k, (source, buffer) in enumerate(zip(sources, buffers))
    ]
    for copy in copies:
        copy.start()
    for copy in copies:
        copy.wait()


def stored_rows(fields_ref, others):
    fields = fields_ref[...].reshape(3 * NODES, ELEMENTS)
    others = [ref[...].reshape(NODES, ELEMENTS) for ref in others]
    return jnp.concatenate([fields[:NODES] - others[-1], fields[NODES:]] + others, 0)


def mass_tendency(table, p, u, v, area_depth, weighted_area, spin):
    slopes = dot(table[: 2 * NODES, : 3 * NODES], jnp.concatenate(high_low_high(p), 0))
    flux = high_low_high(area_depth * u) + high_low_high(area_depth * v)
    spread = dot(table[2 * NODES : 3 * NODES], jnp.concatenate(flux, 0))
    return [
        -spread,
        spin * v - weighted_area * slopes[:NODES],
        -spin * u - weighted_area * slopes[NODES:],
    ]


def edge_values(table_ref, weight_ref, p, u, v, area, depth, spin):
    root = jnp.sqrt(area)
    mass = jnp.concatenate([weight_ref[...]] * (area.shape[1] // LANES), 1) * area
    table = table_ref[...].astype(bf16)
    return mass_tendency(table, p, u, v, root * depth, root, mass * spin) + [mass]


def row_edges(sums):
    return tuple(sums[0, pl.ds(j, EDGE_ROWS, stride=NP)] for j in (NP - 1, 0))


def beside(left, right):
    return jnp.concatenate([left, right], 1)


def one_of_four(parts, index):
    out = parts[0]
    for k in range(1, 4):
        out = jnp.where(index == k, parts[k], out)
    return out


def folded(tide, kept, late, step):
    half = NODES // 2
    back = pltpu.roll(tide[half:], LANES - step, 1)
    onward = pltpu.roll(tide[half:], step, 1)
    return jnp.where(kept, tide[:half], jnp.where(late, back, onward))


def unfolded(rows, late, step):
    back = pltpu.roll(rows, LANES - step, 1)
    onward = pltpu.roll(rows, step, 1)
    return jnp.concatenate([rows, jnp.where(late, onward, back)], 0)


def strip_rows(parts, late, shift, rims):
    lane = lax.broadcasted_iota(i32, (1, LANES), 1)
    index = (lane >> shift) & 3
    kept = jnp.where(late, index // 2, 1 - index // 2) != 0
    tide = folded(parts[6], kept, late, 2 << shift)
    rim = one_of_four(rims, index)
    return jnp.concatenate(parts[:6] + [tide, rim, jnp.zeros_like(rim)], 0)


def placed_rows(whole, late, shift):
    half = NODES // 2
    tide = unfolded(whole[MOVED : MOVED + half], late, 2 << shift)
    rim = whole[MOVED + half : MOVED + half + NP]
    return jnp.concatenate([whole[:MOVED], tide] + spread_out(rim, late, shift), 0)


def spread_out(rim, late, shift):
    parts = []
    for k in range(4):
        first = pltpu.roll(rim, (LANES - (k << shift)) % LANES, 1) if k else rim
        last = pltpu.roll(rim, (3 - k) << shift, 1) if k < 3 else rim
        parts.append(jnp.where(late, first, last))
    return parts


def with_row_rim(whole, sums, top):
    north, south = row_edges(sums)
    rim = jnp.where(top, pltpu.roll(north, RING, 1), pltpu.roll(south, LANES - RING, 1))
    parts = [rim[k * NP : (k + 1) * NP] for k in range(4)]
    lane = lax.broadcasted_iota(i32, (1, LANES), 1)
    spots = []
    for k, part in enumerate(parts):
        first = pltpu.roll(part, k * RING, 1) if k else part
        last = pltpu.roll(part, (LANES - (3 - k) * RING) % LANES, 1) if k < 3 else part
        spots.append(jnp.where(top, first, last))
    rim = one_of_four(spots, (lane >> 2) & 3)
    return jnp.concatenate([whole[: MOVED + NODES // 2 + NP], rim], 0)


def corner_of(whole, start, top):
    lane = lax.broadcasted_iota(i32, (1, LANES), 1)
    base = LANES - start - jnp.where(top != 0, 48, 0)
    whole = jnp.concatenate([whole, jnp.zeros((8 * CORNER_ROWS - whole.shape[0], LANES), f32)], 0)
    out = None
    for k in range(8):
        part = whole[k * CORNER_ROWS : (k + 1) * CORNER_ROWS]
        part = pltpu.roll(part, (base + 16 * k) & (LANES - 1), 1)
        out = part if k == 0 else jnp.where(lane >= 16 * k, part, out)
    return out


def packed(whole):
    second = lax.broadcasted_iota(i32, (1, LANES), 1) >= 64
    top, bottom = whole[:HALF_ROWS], whole[HALF_ROWS:]
    return (
        jnp.where(second, pltpu.roll(bottom, 64, 1), top),
        jnp.where(second, bottom, pltpu.roll(top, 64, 1)),
    )


def unpacked(in0, in1):
    second = lax.broadcasted_iota(i32, (1, LANES), 1) >= 64
    top = jnp.where(second, pltpu.roll(in1, 64, 1), in0)
    bottom = jnp.where(second, in1, pltpu.roll(in0, 64, 1))
    return jnp.concatenate([top, bottom], 0)


def seam_flags(seam_ref, block_cols):
    size_y = seam_ref.shape[1]
    face = lax.axis_index("face")
    blk = lax.axis_index("blk")
    block_x = blk // BY

    def flipped(k):
        return jnp.where(lax.rem(seam_ref[k, 1] - seam_ref[k, 0] + size_y, size_y) != 1, 1, 0)

    first, second = flipped(0), flipped(1)
    east_flip = jnp.where(face == 0, first, second)
    west_flip = jnp.where(face == 0, second, first)
    if block_cols == 1:
        return 1 - east_flip, 0, east_flip, 1
    at_east = jnp.where(block_x == block_cols - 1, east_flip, 0)
    at_west = jnp.where(block_x == 0, west_flip, 0)
    return 1, at_east, 0, at_west


def strips_kernel(block_cols, *refs):
    sources = refs[:9]
    out1_ref, far1_ref, out0_ref, far0_ref, next_ref, pair_ref, stored_ref = refs[9:16]
    buffers, sems, sums = refs[16:25], refs[25], refs[26]
    brought(sources, buffers, sems)
    seam_ref, slot_ref, fields_ref, area_ref, depth_ref, spin_ref, tide_ref = buffers[:7]
    table_ref, weight_ref = buffers[7:]
    east0, flip0, east1, flip1 = seam_flags(seam_ref, block_cols)
    lane = lax.broadcasted_iota(i32, (8, 2 * LANES), 1)
    second = (lane & 64) != 0
    place = lane & 63
    row = place >> 2
    row = jnp.where(jnp.where(second, flip1, flip0) != 0, GY - 1 - row, row)
    east = jnp.where(second, east1, east0) != 0
    col = jnp.where(east, GX - RING, 0) + (place & 3)
    col = jnp.where(lane >= LANES, jnp.where(east, GX - RING - 1, RING), col)
    cells = col * GY + row
    odd = lax.axis_index("blk") & 1

    def goes_up(lane):
        return jnp.where((lane & 64) != 0, odd, 1 - odd) != 0

    up = goes_up(lane)
    row = jnp.where(up, GY - RING, 0) + ((lane & 63) >> 4)
    row = jnp.where(lane >= LANES, jnp.where(up, GY - RING - 1, RING), row)
    one_hot = by_slot(slot_ref, beside(cells, (lane & 15) * GY + row))
    stored = stored_rows(fields_ref, (area_ref, depth_ref, spin_ref, tide_ref))
    stored_ref[...] = stored
    both = picked(stored, one_hot)

    lane = lax.broadcasted_iota(i32, (1, LANES), 1)
    second = lane >= 64
    flip = jnp.where(second, flip1, flip0) != 0
    sign = jnp.where(flip, -1.0, 1.0)
    node = lax.broadcasted_iota(i32, (1, NP, 1), 1)

    def in_frame(values):
        shaped = values.reshape(-1, NP, LANES)
        turned = pltpu.roll(shaped, 4, 1)
        turned = jnp.where((node & 2) == 0, pltpu.roll(turned, 6, 1), pltpu.roll(turned, 2, 1))
        turned = jnp.where((node & 1) == 0, pltpu.roll(turned, 7, 1), pltpu.roll(turned, 1, 1))
        values = jnp.where(flip[None], turned, shaped).reshape(values.shape)
        parts = [values[k * NODES : (k + 1) * NODES] for k in range(ARRAYS)]
        parts[2] = parts[2] * sign
        parts[5] = parts[5] * sign
        return parts

    strip, ring = in_frame(both[:, :LANES]), in_frame(both[:, LANES : 2 * LANES])
    rows, behind = (
        [part[k * NODES : (k + 1) * NODES] for k in range(ARRAYS)]
        for part in (both[:, 2 * LANES : 3 * LANES], both[:, 3 * LANES :])
    )
    edges = edge_values(
        table_ref,
        weight_ref,
        *(jnp.concatenate(parts, 1) for parts in zip(strip[:6], ring[:6], behind[:6])),
    )
    east = jnp.where(second, east1, east0) != 0
    ends = [part[:, LANES : 2 * LANES] for part in edges]
    ends = [jnp.where(east, part[NODES - NP :], part[:NP]) for part in ends]
    whole = strip_rows(strip, east, 0, ends)
    out0_ref[...], out1_ref[...] = packed(whole)
    sums[0] = jnp.concatenate([part[:, :LANES] for part in edges], 0)
    top0, top1 = odd ^ flip0, odd ^ flip1
    whole = with_row_rim(whole, sums, jnp.where(second, top1, top0) != 0)
    far0_ref[...] = corner_of(whole, 0, top0)
    far1_ref[...] = corner_of(whole, 64, top1)
    sums[0] = jnp.concatenate([part[:, 2 * LANES :] for part in edges], 0)
    up = goes_up(lane)
    rim = jnp.where(up, *row_edges(sums))
    rim = [rim[k * NP : (k + 1) * NP] for k in range(4)]
    pair_ref[...], next_ref[...] = packed(strip_rows(rows, up, 4, rim))


def corners_kernel(in1_ref, in0_ref, pair_ref, table_ref, weight_ref, *refs):
    out_ref, sums = refs[-2:]
    top = 1 - (lax.axis_index("blk") & 1)
    whole = unpacked(in0_ref[...], in1_ref[...])
    parts = [whole[k * NODES : (k + 1) * NODES] for k in range(6)]
    sums[0] = jnp.concatenate(edge_values(table_ref, weight_ref, *parts), 0)
    whole = with_row_rim(whole, sums, jnp.broadcast_to(top != 0, (1, LANES)))
    out_ref[:HALF_ROWS] = pair_ref[...]
    out_ref[HALF_ROWS : HALF_ROWS + CORNER_ROWS] = corner_of(whole, 0, top)
    out_ref[HALF_ROWS + CORNER_ROWS :] = corner_of(whole, 64, top)


def own_kernel(stored_ref, slot_ref, lanes_ref, own_ref, hot_ref):
    one_hot = by_slot(slot_ref, lanes_ref[0:8])
    own_ref[...] = picked(stored_ref[...], one_hot)
    hot_ref[...] = one_hot


def middle_kernel(
    block_cols, seam_ref, in0_ref, in1_ref, own_ref, lanes_ref, low_ref, centre_ref, high_ref
):
    east0, flip0, east1, flip1 = seam_flags(seam_ref, block_cols)
    second = lax.broadcasted_iota(i32, (1, LANES), 1) >= 64
    late = jnp.where(second, east1, east0) == 0
    whole = placed_rows(unpacked(in0_ref[...], in1_ref[...]), late, 0)
    side = lanes_ref[16:24]
    first_at = jnp.where(side == 2, 64 * (1 - east0), 64 * east0)
    place = jnp.where(side == 0, -1, lanes_ref[8:16] + first_at)
    placed = picked(whole, as_one_hot(place, LANES))
    for k, ref in enumerate((low_ref, centre_ref, high_ref)):
        part = slice(k * LANES, (k + 1) * LANES)
        ref[:ROWS] = placed[:ROWS, part] + own_ref[:, part]
        ref[ROWS:] = placed[ROWS:, part]


def steps_kernel(
    block_cols, seam_ref, pair_ref, next_ref, far0_ref, far1_ref, low_ref, centre_ref,
    high_ref, hot_ref, table_ref, weight_ref, ext_ref, outer_ref, out_ref, sums,
):
    east0, flip0, east1, flip1 = seam_flags(seam_ref, block_cols)
    odd = lax.axis_index("blk") & 1
    block_y = lax.rem(lax.axis_index("blk"), BY)

    lane = lax.broadcasted_iota(i32, (1, LANES), 1)
    pair = pair_ref[...]
    late = jnp.where(lane < 64, odd, 1 - odd) != 0
    strips = placed_rows(unpacked(pair[:HALF_ROWS], next_ref[...]), late, 4)
    strips = jnp.concatenate(
        [strips[:ROWS], jnp.zeros((EDGE_ROWS, LANES), f32), strips[ROWS:]], 0
    )
    near = pair[HALF_ROWS:]
    sources = (near[:CORNER_ROWS], near[CORNER_ROWS:], far0_ref[...], far1_ref[...])
    corners = []
    for k in range(8):
        rows = None
        for n, source in enumerate(sources):
            shift = 16 * (n - k) % LANES
            part = pltpu.roll(source, shift, 1) if shift else source
            rows = part if n == 0 else jnp.where(lane >= 16 * n, part, rows)
        corners.append(rows)
    corners = jnp.concatenate(corners, 0)
    rim = MOVED + NODES // 2 + NP
    late = jnp.where((lane & 16) != 0, east1, east0) == 0
    below = jnp.where((lane & 32) != 0, 1 - odd, odd) != 0
    corners = jnp.concatenate(
        [placed_rows(corners, late, 0)] + spread_out(corners[rim : rim + NP], below, 2), 0
    )
    around = jnp.concatenate([strips, corners], 1)
    kind = outer_ref[8:16]
    sender = jnp.where(outer_ref[16:24] != 0, odd, 1 - odd)
    strip_at = jnp.where(kind == 3, 16 * (1 - east0), 16 * east0)
    place = outer_ref[0:8] + jnp.where(kind == 1, 64 * sender, 32 * sender + strip_at)
    outer = picked(around, as_one_hot(jnp.where(kind == 0, -1, place), 2 * LANES))
    tiles = (outer[:, :LANES], low_ref, centre_ref, high_ref, outer[:, LANES:])

    def rows_of(start, count):
        return jnp.concatenate([ref[start : start + count] for ref in tiles], 1)

    table = table_ref[...].astype(bf16)
    weight = jnp.concatenate([weight_ref[...]] * len(tiles), 1)
    at_rim = ext_ref[0:1] != 0
    top_row = jnp.where(block_y == BY - 1, ext_ref[1:2], 0) != 0
    bottom_row = jnp.where(block_y == 0, ext_ref[2:3], 0) != 0

    first_row = ext_ref[4:5] != 0
    last_row = ext_ref[5:6] != 0

    def edge_sum(parts, rims=None, rows=None):
        count = len(parts) * NP
        for c, part in enumerate(parts):
            west, east = part[:NP], part[NODES - NP :]
            at_east = pltpu.roll(west, EXT - 1, 1)
            at_west = pltpu.roll(east, 1, 1)
            if rims is not None:
                at_east = jnp.where(at_rim, rims[c], at_east)
                at_west = jnp.where(at_rim, rims[c], at_west)
            part = jnp.concatenate([west + at_west, part[NP : NODES - NP], east + at_east], 0)
            for k in range(len(tiles)):
                sums[k, c * NODES : (c + 1) * NODES] = part[:, k * LANES : (k + 1) * LANES]
        south_at, north_at = pl.ds(0, count, stride=NP), pl.ds(NP - 1, count, stride=NP)
        south = jnp.concatenate([sums[k, south_at] for k in range(len(tiles))], 1)
        north = jnp.concatenate([sums[k, north_at] for k in range(len(tiles))], 1)
        at_north = jnp.where(top_row, 0.0, pltpu.roll(south, EXT - PITCH, 1))
        at_south = jnp.where(bottom_row, 0.0, pltpu.roll(north, PITCH, 1))
        if rows is not None:
            at_north = jnp.where(last_row, rows, at_north)
            at_south = jnp.where(first_row, rows, at_south)
        to_north, to_south = north + at_north, south + at_south
        for k in range(len(tiles)):
            sums[k, south_at] = to_south[:, k * LANES : (k + 1) * LANES]
            sums[k, north_at] = to_north[:, k * LANES : (k + 1) * LANES]
        return [
            jnp.concatenate(
                [sums[k, c * NODES : (c + 1) * NODES] for k in range(len(tiles))], 1
            )
            for c in range(len(parts))
        ]

    start = [rows_of(c * NODES, NODES) for c in range(3)]
    area, depth, spin, tide = [rows_of(c * NODES, NODES) for c in range(3, ARRAYS)]
    root = jnp.sqrt(area)
    mass = weight * area
    mass_spin = mass * spin
    area_depth = root * depth
    rims = [rows_of(ROWS + c * NP, NP) for c in range(4)]
    blank = jnp.zeros((EDGE_ROWS, MID), f32)
    rows = jnp.concatenate([tiles[0][ALL_ROWS:], blank, tiles[-1][ALL_ROWS:]], 1)
    node = lax.broadcasted_iota(i32, (1, NP, 1), 1)
    east = pltpu.roll(rows, EXT - 1, 1).reshape(4, NP, EXT)
    west = pltpu.roll(rows, 1, 1).reshape(4, NP, EXT)
    rows = (
        rows.reshape(4, NP, EXT)
        + jnp.where(node == NP - 1, pltpu.roll(east, NP - 1, 1), 0.0)
        + jnp.where(node == 0, pltpu.roll(west, 1, 1), 0.0)
    ).reshape(EDGE_ROWS, EXT)
    per_mass = 1.0 / edge_sum([mass], rims[3:], rows[3 * NP :])[0]

    def average(parts, rims=None, rows=None):
        return [part * per_mass for part in edge_sum(parts, rims, rows)]

    def tendency(s):
        return mass_tendency(table, *s, area_depth, root, mass_spin)

    def laplace(s):
        return [
            dot(table[3 * NODES :, : 3 * NODES], jnp.concatenate(high_low_high(part), 0))
            for part in s
        ]

    change = average(tendency(start), rims[:3], rows[: 3 * NP])
    one = [s + time_step * c for s, c in zip(start, change)]
    change = average(tendency(one))
    two = [0.75 * s + 0.25 * (o + time_step * c) for s, o, c in zip(start, one, change)]
    change = average(tendency(two))
    three = [s / 3.0 + 2.0 / 3.0 * (o + time_step * c) for s, o, c in zip(start, two, change)]
    three[0] = three[0] + tide
    biharmonic = average(laplace(average(laplace(three))))
    own = ext_ref[3:4, LANES : LANES + MID] != 0
    stepped = [
        jnp.where(
            own,
            (s - time_step * hyper_coeff * b)[:, LANES : LANES + MID],
            0.0,
        )
        for s, b in zip(three, biharmonic)
    ]
    stored = picked(jnp.concatenate(stepped, 0), hot_ref[...], dot_other)
    out_ref[...] = stored.reshape(out_ref.shape)


def on_device(fields, jacobian, water_depth, coriolis, tide_height, slot_of, seam_rows):
    block_cols = lax.axis_size("blk") // BY
    table, weight = operator_table()
    table, weight, lanes, ext, outer = map(jnp.asarray, (table, weight, *lane_tables()))
    vmem = pl.BlockSpec(memory_space=pltpu.VMEM)
    smem = pl.BlockSpec(memory_space=pltpu.SMEM)
    hbm = pl.BlockSpec(memory_space=pltpu.HBM)
    params = pltpu.CompilerParams(vmem_limit_bytes=48 * 2**20)
    held = (fields, jacobian, water_depth, coriolis, tide_height)

    def call(kernel, ins, outs, cost, scratch=(), name=None):
        return pl.pallas_call(
            kernel,
            out_shape=[jax.ShapeDtypeStruct(*out) for out in outs],
            in_specs=[spec for spec, value in ins],
            out_specs=[vmem] * len(outs),
            scratch_shapes=list(scratch),
            compiler_params=params,
            cost_estimate=pl.CostEstimate(
                flops=cost, bytes_accessed=2 * 2**20, transcendentals=0
            ),
            name=name,
        )(
            *[
                pltpu.with_memory_space_constraint(value, pltpu.HBM) if spec is hbm else value
                for spec, value in ins
            ]
        )

    strip = ((HALF_ROWS, LANES), f32)
    def room(values, spaces=None):
        spaces = spaces or [pltpu.VMEM] * len(values)
        buffers = [space(x.shape, x.dtype) for space, x in zip(spaces, values)]
        return buffers + [pltpu.SemaphoreType.DMA((len(values),))]

    needed = (seam_rows, slot_of, *held, table, weight)
    corner = ((CORNER_ROWS, LANES), f32)
    scratch = [pltpu.VMEM((1, 4 * NODES, LANES), f32)]
    strip1, far1, strip0, far0, to_next, to_pair, stored = call(
        functools.partial(strips_kernel, block_cols),
        [(hbm, x) for x in needed],
        [strip, corner, strip, corner, strip, strip, ((ROWS, ELEMENTS), f32)],
        10**8,
        scratch=room(needed, [pltpu.SMEM] + [pltpu.VMEM] * (len(needed) - 1)) + scratch,
        name="strips",
    )
    span = block_cols * BY
    both = ("face", "blk")
    places = [(f, x, y) for f in range(2) for x in range(block_cols) for y in range(BY)]

    def rank(face, block_x, block_y):
        return face * span + block_x * BY + block_y

    def same(y):
        return y

    def in_pair(y):
        return y ^ 1

    def next_pair(y):
        other = y + 1 if y % 2 else y - 1
        return other if 0 <= other < BY else y

    def swapped(value, partner):
        pairs = [
            (rank(f, x, y), rank(f if partner(y) != y else 1 - f, x, partner(y)))
            for f, x, y in places
        ]
        return lax.ppermute(value, both, pairs)

    def across(value0, value1, partner):
        last = block_cols - 1
        straight = {
            (f, x, y): (f, x + 1, partner(y)) if x < last else (1 - f, 0, partner(y))
            for f, x, y in places
        }
        turned = {
            (f, last, y): (1 - f, 0, BY - 1 - partner(y)) for f in range(2) for y in range(BY)
        }

        def eastward(value, pairs):
            return lax.ppermute(value, both, [(rank(*a), rank(*b)) for a, b in pairs.items()])

        def westward(value, pairs):
            return lax.ppermute(value, both, [(rank(*b), rank(*a)) for a, b in pairs.items()])

        if block_cols == 1:
            return eastward(value0, straight), eastward(value1, turned)
        flipped = (seam_rows[:, 1] - seam_rows[:, 0]) % seam_rows.shape[1] != 1
        face = lax.axis_index("face")
        block_x = lax.axis_index("blk") // BY
        return (
            jnp.where(
                (block_x == last) & flipped[face],
                westward(value1, turned),
                westward(value1, straight),
            ),
            jnp.where(
                (block_x == 0) & flipped[1 - face],
                eastward(value0, turned),
                eastward(value0, straight),
            ),
        )

    halo0, halo1 = across(strip0, strip1, same)
    far0, far1 = across(far0, far1, next_pair)
    from_next = swapped(to_next, next_pair)
    own, hot = call(
        own_kernel,
        [(vmem, x) for x in (stored, slot_of, lanes)],
        [((ROWS, MID), f32), ((ELEMENTS, MID), bf16)],
        10**8,
        name="own",
    )
    (to_pair,) = call(
        corners_kernel,
        [(vmem, x) for x in (halo1, halo0, to_pair, table, weight, hot, far1, far0, from_next)],
        [((HALF_ROWS + 2 * CORNER_ROWS, LANES), f32)],
        10**8,
        scratch=scratch,
        name="corners",
    )
    from_pair = swapped(to_pair, in_pair)
    tile = ((ALL_ROWS, LANES), f32)
    low, centre, high = call(
        functools.partial(middle_kernel, block_cols),
        [(smem, seam_rows)] + [(vmem, x) for x in (halo0, halo1, own, lanes)],
        [tile, tile, tile],
        10**8,
        name="middle",
    )
    (stepped,) = call(
        functools.partial(steps_kernel, block_cols),
        [(smem, seam_rows)]
        + [
            (vmem, x)
            for x in (
                from_pair, from_next, far0, far1, low, centre, high,
                hot, table, weight, ext, outer,
            )
        ],
        [(fields.shape, f32)],
        10**8,
        scratch=[pltpu.VMEM((EXT // LANES, 3 * NODES, LANES), f32)],
        name="steps",
    )
    return stepped


def solution(mesh):
    return jax.shard_map(
        on_device,
        mesh=mesh,
        in_specs=(
            P(None, None, None, ("face", "blk")),
            P(None, None, ("face", "blk")),
            P(None, None, ("face", "blk")),
            P(None, None, ("face", "blk")),
            P(None, None, ("face", "blk")),
            P(("face", "blk"), None),
            P(),
        ),
        out_specs=P(None, None, None, ("face", "blk")),
        check_vma=False,
    )
```

```python
import functools
import math

import jax
import jax.numpy as jnp
import ml_dtypes
import numpy as np
from jax import lax
from jax.experimental import pallas as pl
from jax.experimental.pallas import tpu as pltpu
from jax.sharding import PartitionSpec as P

BY = 16
GX = 16
GY = 16
NP = 8
NODES = NP * NP
ARRAYS = 7
ROWS = ARRAYS * NODES
MOVED = 6 * NODES
EDGE_ROWS = 4 * NP
ALL_ROWS = ROWS + EDGE_ROWS
HALF_ROWS = (MOVED + NODES // 2 + 2 * NP) // 2
RING = 4
RIM_ROWS = ROWS + 2 * EDGE_ROWS
CORNER_ROWS = (MOVED + NODES // 2 + 4 * NP) // 8
PITCH = GX + 2 * RING
MID = GY * PITCH
LANES = 128
EXT = MID + 2 * LANES
LEAD = LANES - RING * PITCH
ELEMENTS = GX * GY

time_step = 0.03
hyper_coeff = 0.0002

f32 = jnp.float32
bf16 = jnp.bfloat16
i32 = jnp.int32


def legendre_pair(location, degree):
    lower_value = 1.0
    upper_value = location
    for polynomial_order in range(2, degree + 1):
        lower_value, upper_value = (
            upper_value,
            (
                (2 * polynomial_order - 1) * location * upper_value
                - (polynomial_order - 1) * lower_value
            )
            / polynomial_order,
        )
    return (lower_value, upper_value)


def gll_tables(points):
    degree = points - 1
    locations = [-math.cos(math.pi * position / degree) for position in range(points)]
    for iteration in range(100):
        updated = []
        for location in locations:
            lower_value, upper_value = legendre_pair(location, degree)
            updated.append(
                location - (location * upper_value - lower_value) / ((degree + 1) * upper_value)
            )
        locations = updated
    locations[0] = -1.0
    locations[degree] = 1.0
    legendre_at = [legendre_pair(location, degree)[1] for location in locations]
    weights = [2.0 / (degree * (degree + 1) * value * value) for value in legendre_at]
    corner_value = degree * (degree + 1) / 4.0
    derivative = []
    for row_index in range(points):
        row_values = []
        for column_index in range(points):
            if row_index != column_index:
                row_values.append(
                    legendre_at[row_index]
                    / (legendre_at[column_index] * (locations[row_index] - locations[column_index]))
                )
            elif row_index == 0:
                row_values.append(-corner_value)
            elif row_index == degree:
                row_values.append(corner_value)
            else:
                row_values.append(0.0)
        derivative.append(row_values)
    return np.asarray(weights, np.float64), np.asarray(derivative, np.float64)


def in_three(matrix):
    high = matrix.astype(ml_dtypes.bfloat16)
    low = (matrix - high.astype(np.float64)).astype(ml_dtypes.bfloat16)
    return np.concatenate([high, high, low], 1)


def operator_table():
    weights, derivative = gll_tables(NP)
    eye = np.eye(NP)
    node_weight = np.outer(weights, weights).reshape(NODES, 1)
    along_x = node_weight * np.kron(derivative, eye)
    along_y = node_weight * np.kron(eye, derivative)
    second = derivative @ derivative
    both = node_weight * (np.kron(second, eye) + np.kron(eye, second))
    table = np.zeros((4 * NODES, 6 * NODES), ml_dtypes.bfloat16)
    table[:NODES, : 3 * NODES] = in_three(along_x)
    table[NODES : 2 * NODES, : 3 * NODES] = in_three(along_y)
    table[2 * NODES : 3 * NODES, : 3 * NODES] = in_three(along_x)
    table[2 * NODES : 3 * NODES, 3 * NODES :] = in_three(along_y)
    table[3 * NODES :, : 3 * NODES] = in_three(both)
    spread = np.broadcast_to(node_weight, (NODES, LANES)).astype(np.float32)
    return table.astype(np.float32), np.ascontiguousarray(spread)


def lane_tables():
    table = np.zeros((24, MID), np.int32)
    for lane in range(MID):
        row, col = divmod(lane, PITCH)
        x = col - RING
        own = 0 <= x < GX
        table[0:8, lane] = x * GY + row if own else -1
        if not own:
            table[8:16, lane] = row * RING + (col if x < 0 else x - GX)
        table[16:24, lane] = 0 if own else (1 if x < 0 else 2)
    ext = np.zeros((8, EXT), np.int32)
    outer = np.zeros((24, 2 * LANES), np.int32)
    for lane in range(EXT):
        row, col = divmod(lane - LEAD, PITCH)
        y = row - RING
        x = col - RING
        inside = 0 <= row < GY + 2 * RING
        ext[0, lane] = x in (-RING, GX + RING - 1)
        ext[1, lane] = y == GY - 1
        ext[2, lane] = y == 0
        ext[3, lane] = 0 <= y < GY and 0 <= x < GX
        ext[4, lane] = y == -RING
        ext[5, lane] = y == GY + RING - 1
        if inside and not 0 <= y < GY:
            place = lane if y < 0 else lane - LANES - MID + LANES
            step = y + RING if y < 0 else y - GY
            if 0 <= x < GX:
                outer[0:8, place] = step * GX + x
                outer[8:16, place] = 1
            else:
                outer[0:8, place] = LANES + step * RING + (x + RING if x < 0 else x - GX)
                outer[8:16, place] = 2 if x < 0 else 3
            outer[16:24, place] = y > 0
    return table, ext, outer


def dot(a, b):
    return jnp.dot(a, b, preferred_element_type=f32)


def picked(values, one_hot):
    high = values.astype(bf16)
    low = (values - high.astype(f32)).astype(bf16)
    return dot(high, one_hot) + dot(low, one_hot)


def as_one_hot(row_of_lane, depth):
    index = lax.broadcasted_iota(i32, (depth, row_of_lane.shape[1]), 0)
    return jnp.where(index == row_of_lane[0:1], 1.0, 0.0).astype(bf16)


def high_low_high(values):
    high = values.astype(bf16)
    low = (values - high.astype(f32)).astype(bf16)
    return [high, low, high]


def by_slot(slot_ref, cell_of_lane):
    slots = jnp.broadcast_to(slot_ref[...], (8, ELEMENTS)).astype(f32).astype(bf16)
    chosen = dot(slots, as_one_hot(cell_of_lane, ELEMENTS))
    chosen = jnp.where(cell_of_lane >= 0, chosen, -1.0)
    index = lax.broadcasted_iota(i32, (ELEMENTS, cell_of_lane.shape[1]), 0).astype(f32)
    return jnp.where(index == chosen[0:1], 1.0, 0.0).astype(bf16)


def brought(sources, buffers, sems):
    copies = [
        pltpu.make_async_copy(source, buffer, sems.at[k])
        for k, (source, buffer) in enumerate(zip(sources, buffers))
    ]
    for copy in copies:
        copy.start()
    for copy in copies:
        copy.wait()


def stored_rows(fields_ref, others):
    fields = fields_ref[...].reshape(3 * NODES, ELEMENTS)
    others = [ref[...].reshape(NODES, ELEMENTS) for ref in others]
    return jnp.concatenate([fields[:NODES] - others[-1], fields[NODES:]] + others, 0)


def mass_tendency(table, p, u, v, area_depth, weighted_area, spin):
    slopes = dot(table[: 2 * NODES, : 3 * NODES], jnp.concatenate(high_low_high(p), 0))
    flux = high_low_high(area_depth * u) + high_low_high(area_depth * v)
    spread = dot(table[2 * NODES : 3 * NODES], jnp.concatenate(flux, 0))
    return [
        -spread,
        spin * v - weighted_area * slopes[:NODES],
        -spin * u - weighted_area * slopes[NODES:],
    ]


def edge_values(table_ref, weight_ref, p, u, v, area, depth, spin):
    root = jnp.sqrt(area)
    mass = jnp.concatenate([weight_ref[...]] * (area.shape[1] // LANES), 1) * area
    table = table_ref[...].astype(bf16)
    return mass_tendency(table, p, u, v, root * depth, root, mass * spin) + [mass]


def row_edges(sums):
    return tuple(sums[0, pl.ds(j, EDGE_ROWS, stride=NP)] for j in (NP - 1, 0))


def beside(left, right):
    return jnp.concatenate([left, right], 1)


def one_of_four(parts, index):
    out = parts[0]
    for k in range(1, 4):
        out = jnp.where(index == k, parts[k], out)
    return out


def folded(tide, kept, late, step):
    half = NODES // 2
    back = pltpu.roll(tide[half:], LANES - step, 1)
    onward = pltpu.roll(tide[half:], step, 1)
    return jnp.where(kept, tide[:half], jnp.where(late, back, onward))


def unfolded(rows, late, step):
    back = pltpu.roll(rows, LANES - step, 1)
    onward = pltpu.roll(rows, step, 1)
    return jnp.concatenate([rows, jnp.where(late, onward, back)], 0)


def strip_rows(parts, late, shift, rims):
    lane = lax.broadcasted_iota(i32, (1, LANES), 1)
    index = (lane >> shift) & 3
    kept = jnp.where(late, index // 2, 1 - index // 2) != 0
    tide = folded(parts[6], kept, late, 2 << shift)
    rim = one_of_four(rims, index)
    return jnp.concatenate(parts[:6] + [tide, rim, jnp.zeros_like(rim)], 0)


def placed_rows(whole, late, shift):
    half = NODES // 2
    tide = unfolded(whole[MOVED : MOVED + half], late, 2 << shift)
    rim = whole[MOVED + half : MOVED + half + NP]
    return jnp.concatenate([whole[:MOVED], tide] + spread_out(rim, late, shift), 0)


def spread_out(rim, late, shift):
    parts = []
    for k in range(4):
        first = pltpu.roll(rim, (LANES - (k << shift)) % LANES, 1) if k else rim
        last = pltpu.roll(rim, (3 - k) << shift, 1) if k < 3 else rim
        parts.append(jnp.where(late, first, last))
    return parts


def with_row_rim(whole, sums, top):
    north, south = row_edges(sums)
    rim = jnp.where(top, pltpu.roll(north, RING, 1), pltpu.roll(south, LANES - RING, 1))
    parts = [rim[k * NP : (k + 1) * NP] for k in range(4)]
    lane = lax.broadcasted_iota(i32, (1, LANES), 1)
    spots = []
    for k, part in enumerate(parts):
        first = pltpu.roll(part, k * RING, 1) if k else part
        last = pltpu.roll(part, (LANES - (3 - k) * RING) % LANES, 1) if k < 3 else part
        spots.append(jnp.where(top, first, last))
    rim = one_of_four(spots, (lane >> 2) & 3)
    return jnp.concatenate([whole[: MOVED + NODES // 2 + NP], rim], 0)


def corner_of(whole, start, top):
    lane = lax.broadcasted_iota(i32, (1, LANES), 1)
    base = LANES - start - jnp.where(top != 0, 48, 0)
    whole = jnp.concatenate([whole, jnp.zeros((8 * CORNER_ROWS - whole.shape[0], LANES), f32)], 0)
    out = None
    for k in range(8):
        part = whole[k * CORNER_ROWS : (k + 1) * CORNER_ROWS]
        part = pltpu.roll(part, (base + 16 * k) & (LANES - 1), 1)
        out = part if k == 0 else jnp.where(lane >= 16 * k, part, out)
    return out


def packed(whole):
    second = lax.broadcasted_iota(i32, (1, LANES), 1) >= 64
    top, bottom = whole[:HALF_ROWS], whole[HALF_ROWS:]
    return (
        jnp.where(second, pltpu.roll(bottom, 64, 1), top),
        jnp.where(second, bottom, pltpu.roll(top, 64, 1)),
    )


def unpacked(in0, in1):
    second = lax.broadcasted_iota(i32, (1, LANES), 1) >= 64
    top = jnp.where(second, pltpu.roll(in1, 64, 1), in0)
    bottom = jnp.where(second, in1, pltpu.roll(in0, 64, 1))
    return jnp.concatenate([top, bottom], 0)


def seam_flags(seam_ref, block_cols):
    size_y = seam_ref.shape[1]
    face = lax.axis_index("face")
    blk = lax.axis_index("blk")
    block_x = blk // BY

    def flipped(k):
        return jnp.where(lax.rem(seam_ref[k, 1] - seam_ref[k, 0] + size_y, size_y) != 1, 1, 0)

    first, second = flipped(0), flipped(1)
    east_flip = jnp.where(face == 0, first, second)
    west_flip = jnp.where(face == 0, second, first)
    if block_cols == 1:
        return 1 - east_flip, 0, east_flip, 1
    at_east = jnp.where(block_x == block_cols - 1, east_flip, 0)
    at_west = jnp.where(block_x == 0, west_flip, 0)
    return 1, at_east, 0, at_west


def strips_kernel(block_cols, *refs):
    sources = refs[:9]
    out1_ref, far1_ref, out0_ref, far0_ref, next_ref, pair_ref, stored_ref = refs[9:16]
    buffers, sems, sums = refs[16:25], refs[25], refs[26]
    brought(sources, buffers, sems)
    seam_ref, slot_ref, fields_ref, area_ref, depth_ref, spin_ref, tide_ref = buffers[:7]
    table_ref, weight_ref = buffers[7:]
    east0, flip0, east1, flip1 = seam_flags(seam_ref, block_cols)
    lane = lax.broadcasted_iota(i32, (8, 2 * LANES), 1)
    second = (lane & 64) != 0
    place = lane & 63
    row = place >> 2
    row = jnp.where(jnp.where(second, flip1, flip0) != 0, GY - 1 - row, row)
    east = jnp.where(second, east1, east0) != 0
    col = jnp.where(east, GX - RING, 0) + (place & 3)
    col = jnp.where(lane >= LANES, jnp.where(east, GX - RING - 1, RING), col)
    cells = col * GY + row
    odd = lax.axis_index("blk") & 1

    def goes_up(lane):
        return jnp.where((lane & 64) != 0, odd, 1 - odd) != 0

    up = goes_up(lane)
    row = jnp.where(up, GY - RING, 0) + ((lane & 63) >> 4)
    row = jnp.where(lane >= LANES, jnp.where(up, GY - RING - 1, RING), row)
    one_hot = by_slot(slot_ref, beside(cells, (lane & 15) * GY + row))
    stored = stored_rows(fields_ref, (area_ref, depth_ref, spin_ref, tide_ref))
    stored_ref[...] = stored
    both = picked(stored, one_hot)

    lane = lax.broadcasted_iota(i32, (1, LANES), 1)
    second = lane >= 64
    flip = jnp.where(second, flip1, flip0) != 0
    sign = jnp.where(flip, -1.0, 1.0)
    node = lax.broadcasted_iota(i32, (1, NP, 1), 1)

    def in_frame(values):
        shaped = values.reshape(-1, NP, LANES)
        turned = pltpu.roll(shaped, 4, 1)
        turned = jnp.where((node & 2) == 0, pltpu.roll(turned, 6, 1), pltpu.roll(turned, 2, 1))
        turned = jnp.where((node & 1) == 0, pltpu.roll(turned, 7, 1), pltpu.roll(turned, 1, 1))
        values = jnp.where(flip[None], turned, shaped).reshape(values.shape)
        parts = [values[k * NODES : (k + 1) * NODES] for k in range(ARRAYS)]
        parts[2] = parts[2] * sign
        parts[5] = parts[5] * sign
        return parts

    strip, ring = in_frame(both[:, :LANES]), in_frame(both[:, LANES : 2 * LANES])
    rows, behind = (
        [part[k * NODES : (k + 1) * NODES] for k in range(ARRAYS)]
        for part in (both[:, 2 * LANES : 3 * LANES], both[:, 3 * LANES :])
    )
    edges = edge_values(
        table_ref,
        weight_ref,
        *(jnp.concatenate(parts, 1) for parts in zip(strip[:6], ring[:6], behind[:6])),
    )
    east = jnp.where(second, east1, east0) != 0
    ends = [part[:, LANES : 2 * LANES] for part in edges]
    ends = [jnp.where(east, part[NODES - NP :], part[:NP]) for part in ends]
    whole = strip_rows(strip, east, 0, ends)
    out0_ref[...], out1_ref[...] = packed(whole)
    sums[0] = jnp.concatenate([part[:, :LANES] for part in edges], 0)
    top0, top1 = odd ^ flip0, odd ^ flip1
    whole = with_row_rim(whole, sums, jnp.where(second, top1, top0) != 0)
    far0_ref[...] = corner_of(whole, 0, top0)
    far1_ref[...] = corner_of(whole, 64, top1)
    sums[0] = jnp.concatenate([part[:, 2 * LANES :] for part in edges], 0)
    up = goes_up(lane)
    rim = jnp.where(up, *row_edges(sums))
    rim = [rim[k * NP : (k + 1) * NP] for k in range(4)]
    pair_ref[...], next_ref[...] = packed(strip_rows(rows, up, 4, rim))


def corners_kernel(in1_ref, in0_ref, pair_ref, table_ref, weight_ref, *refs):
    out_ref, sums = refs[-2:]
    top = 1 - (lax.axis_index("blk") & 1)
    whole = unpacked(in0_ref[...], in1_ref[...])
    parts = [whole[k * NODES : (k + 1) * NODES] for k in range(6)]
    sums[0] = jnp.concatenate(edge_values(table_ref, weight_ref, *parts), 0)
    whole = with_row_rim(whole, sums, jnp.broadcast_to(top != 0, (1, LANES)))
    out_ref[:HALF_ROWS] = pair_ref[...]
    out_ref[HALF_ROWS : HALF_ROWS + CORNER_ROWS] = corner_of(whole, 0, top)
    out_ref[HALF_ROWS + CORNER_ROWS :] = corner_of(whole, 64, top)


def own_kernel(stored_ref, slot_ref, lanes_ref, own_ref, hot_ref):
    one_hot = by_slot(slot_ref, lanes_ref[0:8])
    own_ref[...] = picked(stored_ref[...], one_hot)
    hot_ref[...] = one_hot.astype(f32).T.astype(bf16)


def middle_kernel(
    block_cols, seam_ref, in0_ref, in1_ref, own_ref, lanes_ref, low_ref, centre_ref, high_ref
):
    east0, flip0, east1, flip1 = seam_flags(seam_ref, block_cols)
    second = lax.broadcasted_iota(i32, (1, LANES), 1) >= 64
    late = jnp.where(second, east1, east0) == 0
    whole = placed_rows(unpacked(in0_ref[...], in1_ref[...]), late, 0)
    side = lanes_ref[16:24]
    first_at = jnp.where(side == 2, 64 * (1 - east0), 64 * east0)
    place = jnp.where(side == 0, -1, lanes_ref[8:16] + first_at)
    placed = picked(whole, as_one_hot(place, LANES))
    for k, ref in enumerate((low_ref, centre_ref, high_ref)):
        part = slice(k * LANES, (k + 1) * LANES)
        ref[:ROWS] = placed[:ROWS, part] + own_ref[:, part]
        ref[ROWS:] = placed[ROWS:, part]


def steps_kernel(
    block_cols, seam_ref, pair_ref, next_ref, far0_ref, far1_ref, low_ref, centre_ref,
    high_ref, hot_ref, table_ref, weight_ref, ext_ref, outer_ref, out_ref, sums,
):
    east0, flip0, east1, flip1 = seam_flags(seam_ref, block_cols)
    odd = lax.axis_index("blk") & 1
    block_y = lax.rem(lax.axis_index("blk"), BY)

    lane = lax.broadcasted_iota(i32, (1, LANES), 1)
    pair = pair_ref[...]
    late = jnp.where(lane < 64, odd, 1 - odd) != 0
    strips = placed_rows(unpacked(pair[:HALF_ROWS], next_ref[...]), late, 4)
    strips = jnp.concatenate(
        [strips[:ROWS], jnp.zeros((EDGE_ROWS, LANES), f32), strips[ROWS:]], 0
    )
    near = pair[HALF_ROWS:]
    sources = (near[:CORNER_ROWS], near[CORNER_ROWS:], far0_ref[...], far1_ref[...])
    corners = []
    for k in range(8):
        rows = None
        for n, source in enumerate(sources):
            shift = 16 * (n - k) % LANES
            part = pltpu.roll(source, shift, 1) if shift else source
            rows = part if n == 0 else jnp.where(lane >= 16 * n, part, rows)
        corners.append(rows)
    corners = jnp.concatenate(corners, 0)
    rim = MOVED + NODES // 2 + NP
    late = jnp.where((lane & 16) != 0, east1, east0) == 0
    below = jnp.where((lane & 32) != 0, 1 - odd, odd) != 0
    corners = jnp.concatenate(
        [placed_rows(corners, late, 0)] + spread_out(corners[rim : rim + NP], below, 2), 0
    )
    around = jnp.concatenate([strips, corners], 1)
    kind = outer_ref[8:16]
    sender = jnp.where(outer_ref[16:24] != 0, odd, 1 - odd)
    strip_at = jnp.where(kind == 3, 16 * (1 - east0), 16 * east0)
    place = outer_ref[0:8] + jnp.where(kind == 1, 64 * sender, 32 * sender + strip_at)
    outer = picked(around, as_one_hot(jnp.where(kind == 0, -1, place), 2 * LANES))
    tiles = (outer[:, :LANES], low_ref, centre_ref, high_ref, outer[:, LANES:])
    count = len(tiles)
    table = table_ref[...].astype(bf16)
    weight = weight_ref[...]
    masks = [ext_ref[:, k * LANES : (k + 1) * LANES] for k in range(count)]
    at_rim = [mask[0:1] != 0 for mask in masks]
    closed_above = [jnp.where(block_y == BY - 1, mask[1:2], 0) != 0 for mask in masks]
    closed_below = [jnp.where(block_y == 0, mask[2:3], 0) != 0 for mask in masks]
    first_row = masks[0][4:5] != 0
    last_row = masks[-1][5:6] != 0

    def shifted(parts, by):
        turned = [pltpu.roll(part, -by % LANES, 1) for part in parts]
        if by > 0:
            return [
                jnp.where(lane >= LANES - by, turned[min(k + 1, count - 1)], turned[k])
                for k in range(count)
            ]
        return [jnp.where(lane < -by, turned[max(k - 1, 0)], turned[k]) for k in range(count)]

    def edge_sum(components, rims=None, rows=None):
        for c in range(components):
            west_at = slice(c * NODES, c * NODES + NP)
            east_at = slice((c + 1) * NODES - NP, (c + 1) * NODES)
            west = [sums[k, west_at] for k in range(count)]
            east = [sums[k, east_at] for k in range(count)]
            at_east, at_west = shifted(west, 1), shifted(east, -1)
            for k in range(count):
                if rims is not None:
                    at_east[k] = jnp.where(at_rim[k], rims[k][c], at_east[k])
                    at_west[k] = jnp.where(at_rim[k], rims[k][c], at_west[k])
                sums[k, west_at] = west[k] + at_west[k]
                sums[k, east_at] = east[k] + at_east[k]
        south_at = pl.ds(0, components * NP, stride=NP)
        north_at = pl.ds(NP - 1, components * NP, stride=NP)
        south = [sums[k, south_at] for k in range(count)]
        north = [sums[k, north_at] for k in range(count)]
        at_north, at_south = shifted(south, PITCH), shifted(north, -PITCH)
        for k in range(count):
            at_north[k] = jnp.where(closed_above[k], 0.0, at_north[k])
            at_south[k] = jnp.where(closed_below[k], 0.0, at_south[k])
        if rows is not None:
            at_south[0] = jnp.where(first_row, rows[0], at_south[0])
            at_north[-1] = jnp.where(last_row, rows[1], at_north[-1])
        for k in range(count):
            sums[k, south_at] = south[k] + at_south[k]
            sums[k, north_at] = north[k] + at_north[k]

    def part_of(k, n):
        return tiles[k][n * NODES : (n + 1) * NODES]

    node = lax.broadcasted_iota(i32, (1, NP, 1), 1)
    rows = []
    for tile in (tiles[0], tiles[-1]):
        rim = tile[ALL_ROWS:]
        east = pltpu.roll(rim, LANES - 1, 1).reshape(4, NP, LANES)
        west = pltpu.roll(rim, 1, 1).reshape(4, NP, LANES)
        rim = (
            rim.reshape(4, NP, LANES)
            + jnp.where(node == NP - 1, pltpu.roll(east, NP - 1, 1), 0.0)
            + jnp.where(node == 0, pltpu.roll(west, 1, 1), 0.0)
        )
        rows.append(rim.reshape(EDGE_ROWS, LANES))
    rims = [
        [tile[ROWS + c * NP : ROWS + (c + 1) * NP] for c in range(4)] for tile in tiles
    ]

    start, fixed = [], []
    for k in range(count):
        area = part_of(k, 3)
        root = jnp.sqrt(area)
        mass = weight * area
        start.append([part_of(k, c) for c in range(3)])
        fixed.append((root * part_of(k, 4), root, mass * part_of(k, 5)))
        sums[k, :NODES] = mass
    edge_sum(1, [rim[3:] for rim in rims], [rim[3 * NP :] for rim in rows])
    per_mass = [1.0 / sums[k, :NODES] for k in range(count)]

    def put(k, parts):
        for c, part in enumerate(parts):
            sums[k, c * NODES : (c + 1) * NODES] = part

    def average(k):
        return [sums[k, c * NODES : (c + 1) * NODES] * per_mass[k] for c in range(3)]

    def laplace(s):
        return [
            dot(table[3 * NODES :, : 3 * NODES], jnp.concatenate(high_low_high(part), 0))
            for part in s
        ]

    for k in range(count):
        put(k, mass_tendency(table, *start[k], *fixed[k]))
    edge_sum(3, rims, [rim[: 3 * NP] for rim in rows])
    one = []
    for k in range(count):
        one.append([s + time_step * c for s, c in zip(start[k], average(k))])
        put(k, mass_tendency(table, *one[k], *fixed[k]))
    edge_sum(3)
    two = []
    for k in range(count):
        two.append(
            [
                0.75 * s + 0.25 * (o + time_step * c)
                for s, o, c in zip(start[k], one[k], average(k))
            ]
        )
        put(k, mass_tendency(table, *two[k], *fixed[k]))
    edge_sum(3)
    three = []
    for k in range(count):
        now = [
            s / 3.0 + 2.0 / 3.0 * (o + time_step * c)
            for s, o, c in zip(start[k], two[k], average(k))
        ]
        now[0] = now[0] + part_of(k, 6)
        three.append(now)
        put(k, laplace(now))
    edge_sum(3)
    for k in range(count):
        put(k, laplace(average(k)))
    edge_sum(3)
    stepped = []
    for k in range(1, count - 1):
        now = [s - time_step * hyper_coeff * b for s, b in zip(three[k], average(k))]
        stepped.append(jnp.where(masks[k][3:4] != 0, jnp.concatenate(now, 0), 0.0))
    stored = picked(jnp.concatenate(stepped, 1), hot_ref[...])
    out_ref[...] = stored.reshape(out_ref.shape)


def on_device(fields, jacobian, water_depth, coriolis, tide_height, slot_of, seam_rows):
    block_cols = lax.axis_size("blk") // BY
    table, weight = operator_table()
    table, weight, lanes, ext, outer = map(jnp.asarray, (table, weight, *lane_tables()))
    vmem = pl.BlockSpec(memory_space=pltpu.VMEM)
    smem = pl.BlockSpec(memory_space=pltpu.SMEM)
    hbm = pl.BlockSpec(memory_space=pltpu.HBM)
    params = pltpu.CompilerParams(vmem_limit_bytes=48 * 2**20)
    held = (fields, jacobian, water_depth, coriolis, tide_height)

    def call(kernel, ins, outs, cost, scratch=(), name=None):
        return pl.pallas_call(
            kernel,
            out_shape=[jax.ShapeDtypeStruct(*out) for out in outs],
            in_specs=[spec for spec, value in ins],
            out_specs=[vmem] * len(outs),
            scratch_shapes=list(scratch),
            compiler_params=params,
            cost_estimate=pl.CostEstimate(
                flops=cost, bytes_accessed=2 * 2**20, transcendentals=0
            ),
            name=name,
        )(
            *[
                pltpu.with_memory_space_constraint(value, pltpu.HBM) if spec is hbm else value
                for spec, value in ins
            ]
        )

    strip = ((HALF_ROWS, LANES), f32)
    def room(values, spaces=None):
        spaces = spaces or [pltpu.VMEM] * len(values)
        buffers = [space(x.shape, x.dtype) for space, x in zip(spaces, values)]
        return buffers + [pltpu.SemaphoreType.DMA((len(values),))]

    needed = (seam_rows, slot_of, *held, table, weight)
    corner = ((CORNER_ROWS, LANES), f32)
    scratch = [pltpu.VMEM((1, 4 * NODES, LANES), f32)]
    strip1, far1, strip0, far0, to_next, to_pair, stored = call(
        functools.partial(strips_kernel, block_cols),
        [(hbm, x) for x in needed],
        [strip, corner, strip, corner, strip, strip, ((ROWS, ELEMENTS), f32)],
        10**8,
        scratch=room(needed, [pltpu.SMEM] + [pltpu.VMEM] * (len(needed) - 1)) + scratch,
        name="strips",
    )
    span = block_cols * BY
    both = ("face", "blk")
    places = [(f, x, y) for f in range(2) for x in range(block_cols) for y in range(BY)]

    def rank(face, block_x, block_y):
        return face * span + block_x * BY + block_y

    def same(y):
        return y

    def in_pair(y):
        return y ^ 1

    def next_pair(y):
        other = y + 1 if y % 2 else y - 1
        return other if 0 <= other < BY else y

    def swapped(value, partner):
        pairs = [
            (rank(f, x, y), rank(f if partner(y) != y else 1 - f, x, partner(y)))
            for f, x, y in places
        ]
        return lax.ppermute(value, both, pairs)

    def across(value0, value1, partner):
        last = block_cols - 1

        def aligned(y):
            return partner is same or partner(y) != y

        straight = {
            (f, x, y): (f, x + 1, partner(y)) if x < last else (1 - f, 0, partner(y))
            for f, x, y in places
        }
        turned = {
            (f, last, y): (1 - f, 0, BY - 1 - partner(y) if aligned(y) else y)
            for f in range(2)
            for y in range(BY)
        }

        def eastward(value, pairs):
            return lax.ppermute(value, both, [(rank(*a), rank(*b)) for a, b in pairs.items()])

        def westward(value, pairs):
            return lax.ppermute(value, both, [(rank(*b), rank(*a)) for a, b in pairs.items()])

        if block_cols == 1:
            return eastward(value0, straight), eastward(value1, turned)
        flipped = (seam_rows[:, 1] - seam_rows[:, 0]) % seam_rows.shape[1] != 1
        face = lax.axis_index("face")
        block_x = lax.axis_index("blk") // BY
        return (
            jnp.where(
                (block_x == last) & flipped[face],
                westward(value1, turned),
                westward(value1, straight),
            ),
            jnp.where(
                (block_x == 0) & flipped[1 - face],
                eastward(value0, turned),
                eastward(value0, straight),
            ),
        )

    halo0, halo1 = across(strip0, strip1, same)
    far0, far1 = across(far0, far1, next_pair)
    from_next = swapped(to_next, next_pair)
    own, hot = call(
        own_kernel,
        [(vmem, x) for x in (stored, slot_of, lanes)],
        [((ROWS, MID), f32), ((MID, ELEMENTS), bf16)],
        10**8,
        name="own",
    )
    (to_pair,) = call(
        corners_kernel,
        [(vmem, x) for x in (halo1, halo0, to_pair, table, weight, hot, far1, far0, from_next)],
        [((HALF_ROWS + 2 * CORNER_ROWS, LANES), f32)],
        10**8,
        scratch=scratch,
        name="corners",
    )
    from_pair = swapped(to_pair, in_pair)
    tile = ((ALL_ROWS, LANES), f32)
    low, centre, high = call(
        functools.partial(middle_kernel, block_cols),
        [(smem, seam_rows)] + [(vmem, x) for x in (halo0, halo1, own, lanes)],
        [tile, tile, tile],
        10**8,
        name="middle",
    )
    (stepped,) = call(
        functools.partial(steps_kernel, block_cols),
        [(smem, seam_rows)]
        + [
            (vmem, x)
            for x in (
                from_pair, from_next, far0, far1, low, centre, high,
                hot, table, weight, ext, outer,
            )
        ],
        [(fields.shape, f32)],
        10**8,
        scratch=[pltpu.VMEM((EXT // LANES, 3 * NODES, LANES), f32)],
        name="steps",
    )
    return stepped


def solution(mesh):
    return jax.shard_map(
        on_device,
        mesh=mesh,
        in_specs=(
            P(None, None, None, ("face", "blk")),
            P(None, None, ("face", "blk")),
            P(None, None, ("face", "blk")),
            P(None, None, ("face", "blk")),
            P(None, None, ("face", "blk")),
            P(("face", "blk"), None),
            P(),
        ),
        out_specs=P(None, None, None, ("face", "blk")),
        check_vma=False,
    )
```

```python
import functools
import math

import jax
import jax.numpy as jnp
import ml_dtypes
import numpy as np
from jax import lax
from jax.experimental import pallas as pl
from jax.experimental.pallas import tpu as pltpu
from jax.sharding import PartitionSpec as P

BY = 16
GX = 16
GY = 16
NP = 8
NODES = NP * NP
ARRAYS = 7
ROWS = ARRAYS * NODES
MOVED = 6 * NODES
EDGE_ROWS = 4 * NP
ALL_ROWS = ROWS + EDGE_ROWS
HALF_ROWS = (MOVED + NODES // 2 + 2 * NP) // 2
RING = 4
RIM_ROWS = ROWS + 2 * EDGE_ROWS
CORNER_ROWS = (MOVED + NODES // 2 + 4 * NP) // 8
PITCH = GX + 2 * RING
MID = GY * PITCH
LANES = 128
EXT = MID + 2 * LANES
LEAD = LANES - RING * PITCH
ELEMENTS = GX * GY

time_step = 0.03
hyper_coeff = 0.0002

f32 = jnp.float32
bf16 = jnp.bfloat16
i32 = jnp.int32


def legendre_pair(location, degree):
    lower_value = 1.0
    upper_value = location
    for polynomial_order in range(2, degree + 1):
        lower_value, upper_value = (
            upper_value,
            (
                (2 * polynomial_order - 1) * location * upper_value
                - (polynomial_order - 1) * lower_value
            )
            / polynomial_order,
        )
    return (lower_value, upper_value)


def gll_tables(points):
    degree = points - 1
    locations = [-math.cos(math.pi * position / degree) for position in range(points)]
    for iteration in range(100):
        updated = []
        for location in locations:
            lower_value, upper_value = legendre_pair(location, degree)
            updated.append(
                location - (location * upper_value - lower_value) / ((degree + 1) * upper_value)
            )
        locations = updated
    locations[0] = -1.0
    locations[degree] = 1.0
    legendre_at = [legendre_pair(location, degree)[1] for location in locations]
    weights = [2.0 / (degree * (degree + 1) * value * value) for value in legendre_at]
    corner_value = degree * (degree + 1) / 4.0
    derivative = []
    for row_index in range(points):
        row_values = []
        for column_index in range(points):
            if row_index != column_index:
                row_values.append(
                    legendre_at[row_index]
                    / (legendre_at[column_index] * (locations[row_index] - locations[column_index]))
                )
            elif row_index == 0:
                row_values.append(-corner_value)
            elif row_index == degree:
                row_values.append(corner_value)
            else:
                row_values.append(0.0)
        derivative.append(row_values)
    return np.asarray(weights, np.float64), np.asarray(derivative, np.float64)


def in_three(matrix):
    high = matrix.astype(ml_dtypes.bfloat16)
    low = (matrix - high.astype(np.float64)).astype(ml_dtypes.bfloat16)
    return np.concatenate([high, high, low], 1)


def operator_table():
    weights, derivative = gll_tables(NP)
    eye = np.eye(NP)
    node_weight = np.outer(weights, weights).reshape(NODES, 1)
    along_x = node_weight * np.kron(derivative, eye)
    along_y = node_weight * np.kron(eye, derivative)
    second = derivative @ derivative
    both = node_weight * (np.kron(second, eye) + np.kron(eye, second))
    table = np.zeros((5 * NODES, 4 * NODES), ml_dtypes.bfloat16)
    table[:NODES, : 3 * NODES] = in_three(along_x)
    table[NODES : 2 * NODES, : 3 * NODES] = in_three(along_y)
    flux = [in_three(along_x), in_three(along_y)]
    for k, part in enumerate(flux):
        at = 2 * k * NODES
        table[2 * NODES : 3 * NODES, at : at + 2 * NODES] = part[:, : 2 * NODES]
        table[3 * NODES : 4 * NODES, at : at + NODES] = part[:, 2 * NODES :]
    table[4 * NODES :, : 3 * NODES] = in_three(both)
    spread = np.broadcast_to(node_weight, (NODES, LANES)).astype(np.float32)
    return table.astype(np.float32), np.ascontiguousarray(spread)


def lane_tables():
    table = np.zeros((24, MID), np.int32)
    for lane in range(MID):
        row, col = divmod(lane, PITCH)
        x = col - RING
        own = 0 <= x < GX
        table[0:8, lane] = x * GY + row if own else -1
        if not own:
            table[8:16, lane] = row * RING + (col if x < 0 else x - GX)
        table[16:24, lane] = 0 if own else (1 if x < 0 else 2)
    ext = np.zeros((8, EXT), np.int32)
    outer = np.zeros((24, 2 * LANES), np.int32)
    for lane in range(EXT):
        row, col = divmod(lane - LEAD, PITCH)
        y = row - RING
        x = col - RING
        inside = 0 <= row < GY + 2 * RING
        ext[0, lane] = x in (-RING, GX + RING - 1)
        ext[1, lane] = y == GY - 1
        ext[2, lane] = y == 0
        ext[3, lane] = 0 <= y < GY and 0 <= x < GX
        ext[4, lane] = y == -RING
        ext[5, lane] = y == GY + RING - 1
        if inside and not 0 <= y < GY:
            place = lane if y < 0 else lane - LANES - MID + LANES
            step = y + RING if y < 0 else y - GY
            if 0 <= x < GX:
                outer[0:8, place] = step * GX + x
                outer[8:16, place] = 1
            else:
                outer[0:8, place] = LANES + step * RING + (x + RING if x < 0 else x - GX)
                outer[8:16, place] = 2 if x < 0 else 3
            outer[16:24, place] = y > 0
    return table, ext, outer


def dot(a, b):
    return jnp.dot(a, b, preferred_element_type=f32)


def picked(values, one_hot):
    high = values.astype(bf16)
    low = (values - high.astype(f32)).astype(bf16)
    return dot(high, one_hot) + dot(low, one_hot)


def as_one_hot(row_of_lane, depth):
    index = lax.broadcasted_iota(i32, (depth, row_of_lane.shape[1]), 0)
    return jnp.where(index == row_of_lane[0:1], 1.0, 0.0).astype(bf16)


def high_low_high(values):
    high = values.astype(bf16)
    low = (values - high.astype(f32)).astype(bf16)
    return [high, low, high]


def by_slot(slot_ref, cell_of_lane):
    slots = jnp.broadcast_to(slot_ref[...], (8, ELEMENTS)).astype(f32).astype(bf16)
    chosen = dot(slots, as_one_hot(cell_of_lane, ELEMENTS))
    chosen = jnp.where(cell_of_lane >= 0, chosen, -1.0)
    index = lax.broadcasted_iota(i32, (ELEMENTS, cell_of_lane.shape[1]), 0).astype(f32)
    return jnp.where(index == chosen[0:1], 1.0, 0.0).astype(bf16)


def brought(sources, buffers, sems):
    copies = [
        pltpu.make_async_copy(source, buffer, sems.at[k])
        for k, (source, buffer) in enumerate(zip(sources, buffers))
    ]
    for copy in copies:
        copy.start()
    for copy in copies:
        copy.wait()


def stored_rows(fields_ref, others):
    fields = fields_ref[...].reshape(3 * NODES, ELEMENTS)
    others = [ref[...].reshape(NODES, ELEMENTS) for ref in others]
    return jnp.concatenate([fields[:NODES] - others[-1], fields[NODES:]] + others, 0)


def mass_tendency(table, p, u, v, area_depth, weighted_area, spin):
    slopes = dot(table[: 2 * NODES, : 3 * NODES], jnp.concatenate(high_low_high(p), 0))
    flux = high_low_high(area_depth * u)[:2] + high_low_high(area_depth * v)[:2]
    spread = dot(table[2 * NODES : 4 * NODES], jnp.concatenate(flux, 0))
    return [
        -(spread[:NODES] + spread[NODES:]),
        spin * v - weighted_area * slopes[:NODES],
        -spin * u - weighted_area * slopes[NODES:],
    ]


def edge_values(table_ref, weight_ref, p, u, v, area, depth, spin):
    root = jnp.sqrt(area)
    mass = jnp.concatenate([weight_ref[...]] * (area.shape[1] // LANES), 1) * area
    table = table_ref[...].astype(bf16)
    return mass_tendency(table, p, u, v, root * depth, root, mass * spin) + [mass]


def row_edges(sums):
    return tuple(sums[0, pl.ds(j, EDGE_ROWS, stride=NP)] for j in (NP - 1, 0))


def beside(left, right):
    return jnp.concatenate([left, right], 1)


def one_of_four(parts, index):
    out = parts[0]
    for k in range(1, 4):
        out = jnp.where(index == k, parts[k], out)
    return out


def folded(tide, kept, late, step):
    half = NODES // 2
    back = pltpu.roll(tide[half:], LANES - step, 1)
    onward = pltpu.roll(tide[half:], step, 1)
    return jnp.where(kept, tide[:half], jnp.where(late, back, onward))


def unfolded(rows, late, step):
    back = pltpu.roll(rows, LANES - step, 1)
    onward = pltpu.roll(rows, step, 1)
    return jnp.concatenate([rows, jnp.where(late, onward, back)], 0)


def strip_rows(parts, late, shift, rims):
    lane = lax.broadcasted_iota(i32, (1, LANES), 1)
    index = (lane >> shift) & 3
    kept = jnp.where(late, index // 2, 1 - index // 2) != 0
    tide = folded(parts[6], kept, late, 2 << shift)
    rim = one_of_four(rims, index)
    return jnp.concatenate(parts[:6] + [tide, rim, jnp.zeros_like(rim)], 0)


def placed_rows(whole, late, shift):
    half = NODES // 2
    tide = unfolded(whole[MOVED : MOVED + half], late, 2 << shift)
    rim = whole[MOVED + half : MOVED + half + NP]
    return jnp.concatenate([whole[:MOVED], tide] + spread_out(rim, late, shift), 0)


def spread_out(rim, late, shift):
    parts = []
    for k in range(4):
        first = pltpu.roll(rim, (LANES - (k << shift)) % LANES, 1) if k else rim
        last = pltpu.roll(rim, (3 - k) << shift, 1) if k < 3 else rim
        parts.append(jnp.where(late, first, last))
    return parts


def with_row_rim(whole, sums, top):
    north, south = row_edges(sums)
    rim = jnp.where(top, pltpu.roll(north, RING, 1), pltpu.roll(south, LANES - RING, 1))
    parts = [rim[k * NP : (k + 1) * NP] for k in range(4)]
    lane = lax.broadcasted_iota(i32, (1, LANES), 1)
    spots = []
    for k, part in enumerate(parts):
        first = pltpu.roll(part, k * RING, 1) if k else part
        last = pltpu.roll(part, (LANES - (3 - k) * RING) % LANES, 1) if k < 3 else part
        spots.append(jnp.where(top, first, last))
    rim = one_of_four(spots, (lane >> 2) & 3)
    return jnp.concatenate([whole[: MOVED + NODES // 2 + NP], rim], 0)


def corner_of(whole, start, top):
    lane = lax.broadcasted_iota(i32, (1, LANES), 1)
    base = LANES - start - jnp.where(top != 0, 48, 0)
    whole = jnp.concatenate([whole, jnp.zeros((8 * CORNER_ROWS - whole.shape[0], LANES), f32)], 0)
    out = None
    for k in range(8):
        part = whole[k * CORNER_ROWS : (k + 1) * CORNER_ROWS]
        part = pltpu.roll(part, (base + 16 * k) & (LANES - 1), 1)
        out = part if k == 0 else jnp.where(lane >= 16 * k, part, out)
    return out


def packed(whole):
    second = lax.broadcasted_iota(i32, (1, LANES), 1) >= 64
    top, bottom = whole[:HALF_ROWS], whole[HALF_ROWS:]
    return (
        jnp.where(second, pltpu.roll(bottom, 64, 1), top),
        jnp.where(second, bottom, pltpu.roll(top, 64, 1)),
    )


def unpacked(in0, in1):
    second = lax.broadcasted_iota(i32, (1, LANES), 1) >= 64
    top = jnp.where(second, pltpu.roll(in1, 64, 1), in0)
    bottom = jnp.where(second, in1, pltpu.roll(in0, 64, 1))
    return jnp.concatenate([top, bottom], 0)


def seam_flags(seam_ref, block_cols):
    size_y = seam_ref.shape[1]
    face = lax.axis_index("face")
    blk = lax.axis_index("blk")
    block_x = blk // BY

    def flipped(k):
        return jnp.where(lax.rem(seam_ref[k, 1] - seam_ref[k, 0] + size_y, size_y) != 1, 1, 0)

    first, second = flipped(0), flipped(1)
    east_flip = jnp.where(face == 0, first, second)
    west_flip = jnp.where(face == 0, second, first)
    if block_cols == 1:
        return 1 - east_flip, 0, east_flip, 1
    at_east = jnp.where(block_x == block_cols - 1, east_flip, 0)
    at_west = jnp.where(block_x == 0, west_flip, 0)
    return 1, at_east, 0, at_west


def strips_kernel(block_cols, *refs):
    sources = refs[:9]
    out1_ref, far1_ref, out0_ref, far0_ref, next_ref, pair_ref, stored_ref = refs[9:16]
    buffers, sems, sums = refs[16:25], refs[25], refs[26]
    brought(sources, buffers, sems)
    seam_ref, slot_ref, fields_ref, area_ref, depth_ref, spin_ref, tide_ref = buffers[:7]
    table_ref, weight_ref = buffers[7:]
    east0, flip0, east1, flip1 = seam_flags(seam_ref, block_cols)
    lane = lax.broadcasted_iota(i32, (8, 2 * LANES), 1)
    second = (lane & 64) != 0
    place = lane & 63
    row = place >> 2
    row = jnp.where(jnp.where(second, flip1, flip0) != 0, GY - 1 - row, row)
    east = jnp.where(second, east1, east0) != 0
    col = jnp.where(east, GX - RING, 0) + (place & 3)
    col = jnp.where(lane >= LANES, jnp.where(east, GX - RING - 1, RING), col)
    cells = col * GY + row
    odd = lax.axis_index("blk") & 1

    def goes_up(lane):
        return jnp.where((lane & 64) != 0, odd, 1 - odd) != 0

    up = goes_up(lane)
    row = jnp.where(up, GY - RING, 0) + ((lane & 63) >> 4)
    row = jnp.where(lane >= LANES, jnp.where(up, GY - RING - 1, RING), row)
    one_hot = by_slot(slot_ref, beside(cells, (lane & 15) * GY + row))
    stored = stored_rows(fields_ref, (area_ref, depth_ref, spin_ref, tide_ref))
    stored_ref[...] = stored
    both = picked(stored, one_hot)

    lane = lax.broadcasted_iota(i32, (1, LANES), 1)
    second = lane >= 64
    flip = jnp.where(second, flip1, flip0) != 0
    sign = jnp.where(flip, -1.0, 1.0)
    node = lax.broadcasted_iota(i32, (1, NP, 1), 1)

    def in_frame(values):
        shaped = values.reshape(-1, NP, LANES)
        turned = pltpu.roll(shaped, 4, 1)
        turned = jnp.where((node & 2) == 0, pltpu.roll(turned, 6, 1), pltpu.roll(turned, 2, 1))
        turned = jnp.where((node & 1) == 0, pltpu.roll(turned, 7, 1), pltpu.roll(turned, 1, 1))
        values = jnp.where(flip[None], turned, shaped).reshape(values.shape)
        parts = [values[k * NODES : (k + 1) * NODES] for k in range(ARRAYS)]
        parts[2] = parts[2] * sign
        parts[5] = parts[5] * sign
        return parts

    strip, ring = in_frame(both[:, :LANES]), in_frame(both[:, LANES : 2 * LANES])
    rows, behind = (
        [part[k * NODES : (k + 1) * NODES] for k in range(ARRAYS)]
        for part in (both[:, 2 * LANES : 3 * LANES], both[:, 3 * LANES :])
    )
    edges = edge_values(
        table_ref,
        weight_ref,
        *(jnp.concatenate(parts, 1) for parts in zip(strip[:6], ring[:6], behind[:6])),
    )
    east = jnp.where(second, east1, east0) != 0
    ends = [part[:, LANES : 2 * LANES] for part in edges]
    ends = [jnp.where(east, part[NODES - NP :], part[:NP]) for part in ends]
    whole = strip_rows(strip, east, 0, ends)
    out0_ref[...], out1_ref[...] = packed(whole)
    sums[0] = jnp.concatenate([part[:, :LANES] for part in edges], 0)
    top0, top1 = odd ^ flip0, odd ^ flip1
    whole = with_row_rim(whole, sums, jnp.where(second, top1, top0) != 0)
    far0_ref[...] = corner_of(whole, 0, top0)
    far1_ref[...] = corner_of(whole, 64, top1)
    sums[0] = jnp.concatenate([part[:, 2 * LANES :] for part in edges], 0)
    up = goes_up(lane)
    rim = jnp.where(up, *row_edges(sums))
    rim = [rim[k * NP : (k + 1) * NP] for k in range(4)]
    pair_ref[...], next_ref[...] = packed(strip_rows(rows, up, 4, rim))


def corners_kernel(in1_ref, in0_ref, pair_ref, table_ref, weight_ref, *refs):
    out_ref, sums = refs[-2:]
    top = 1 - (lax.axis_index("blk") & 1)
    whole = unpacked(in0_ref[...], in1_ref[...])
    parts = [whole[k * NODES : (k + 1) * NODES] for k in range(6)]
    sums[0] = jnp.concatenate(edge_values(table_ref, weight_ref, *parts), 0)
    whole = with_row_rim(whole, sums, jnp.broadcast_to(top != 0, (1, LANES)))
    out_ref[:HALF_ROWS] = pair_ref[...]
    out_ref[HALF_ROWS : HALF_ROWS + CORNER_ROWS] = corner_of(whole, 0, top)
    out_ref[HALF_ROWS + CORNER_ROWS :] = corner_of(whole, 64, top)


def own_kernel(stored_ref, slot_ref, lanes_ref, own_ref, hot_ref):
    one_hot = by_slot(slot_ref, lanes_ref[0:8])
    own_ref[...] = picked(stored_ref[...], one_hot)
    hot_ref[...] = one_hot.astype(f32).T.astype(bf16)


def middle_kernel(block_cols, seam_ref, in0_ref, in1_ref, own_ref, lanes_ref, *refs):
    low_ref, centre_ref, high_ref = refs[-3:]
    east0, flip0, east1, flip1 = seam_flags(seam_ref, block_cols)
    second = lax.broadcasted_iota(i32, (1, LANES), 1) >= 64
    late = jnp.where(second, east1, east0) == 0
    whole = placed_rows(unpacked(in0_ref[...], in1_ref[...]), late, 0)
    side = lanes_ref[16:24]
    first_at = jnp.where(side == 2, 64 * (1 - east0), 64 * east0)
    place = jnp.where(side == 0, -1, lanes_ref[8:16] + first_at)
    placed = picked(whole, as_one_hot(place, LANES))
    for k, ref in enumerate((low_ref, centre_ref, high_ref)):
        part = slice(k * LANES, (k + 1) * LANES)
        ref[:ROWS] = placed[:ROWS, part] + own_ref[:, part]
        ref[ROWS:] = placed[ROWS:, part]


def steps_kernel(
    block_cols, seam_ref, pair_ref, next_ref, far0_ref, far1_ref, low_ref, centre_ref,
    high_ref, hot_ref, table_ref, weight_ref, ext_ref, outer_ref, out_ref, sums,
):
    east0, flip0, east1, flip1 = seam_flags(seam_ref, block_cols)
    odd = lax.axis_index("blk") & 1
    block_y = lax.rem(lax.axis_index("blk"), BY)

    lane = lax.broadcasted_iota(i32, (1, LANES), 1)
    pair = pair_ref[...]
    late = jnp.where(lane < 64, odd, 1 - odd) != 0
    strips = placed_rows(unpacked(pair[:HALF_ROWS], next_ref[...]), late, 4)
    strips = jnp.concatenate(
        [strips[:ROWS], jnp.zeros((EDGE_ROWS, LANES), f32), strips[ROWS:]], 0
    )
    near = pair[HALF_ROWS:]
    sources = (near[:CORNER_ROWS], near[CORNER_ROWS:], far0_ref[...], far1_ref[...])
    corners = []
    for k in range(8):
        rows = None
        for n, source in enumerate(sources):
            shift = 16 * (n - k) % LANES
            part = pltpu.roll(source, shift, 1) if shift else source
            rows = part if n == 0 else jnp.where(lane >= 16 * n, part, rows)
        corners.append(rows)
    corners = jnp.concatenate(corners, 0)
    rim = MOVED + NODES // 2 + NP
    late = jnp.where((lane & 16) != 0, east1, east0) == 0
    below = jnp.where((lane & 32) != 0, 1 - odd, odd) != 0
    corners = jnp.concatenate(
        [placed_rows(corners, late, 0)] + spread_out(corners[rim : rim + NP], below, 2), 0
    )
    around = jnp.concatenate([strips, corners], 1)
    kind = outer_ref[8:16]
    sender = jnp.where(outer_ref[16:24] != 0, odd, 1 - odd)
    strip_at = jnp.where(kind == 3, 16 * (1 - east0), 16 * east0)
    place = outer_ref[0:8] + jnp.where(kind == 1, 64 * sender, 32 * sender + strip_at)
    outer = picked(around, as_one_hot(jnp.where(kind == 0, -1, place), 2 * LANES))
    tiles = (outer[:, :LANES], low_ref, centre_ref, high_ref, outer[:, LANES:])
    count = len(tiles)
    table = table_ref[...].astype(bf16)
    weight = weight_ref[...]
    masks = [ext_ref[:, k * LANES : (k + 1) * LANES] for k in range(count)]
    at_rim = [mask[0:1] != 0 for mask in masks]
    closed_above = jnp.where(block_y == BY - 1, masks[-2][1:2], 0) != 0
    closed_below = jnp.where(block_y == 0, masks[1][2:3], 0) != 0
    first_row = masks[0][4:5] != 0
    last_row = masks[-1][5:6] != 0

    def shifted(parts, by, ring):
        turned = [pltpu.roll(part, -by % LANES, 1) for part in parts]
        size = len(parts)
        step = 1 if by > 0 else -1
        others = [(k + step) % size if ring else min(max(k + step, 0), size - 1) for k in range(size)]
        from_other = lane >= LANES - by if by > 0 else lane < -by
        return [jnp.where(from_other, turned[others[k]], turned[k]) for k in range(size)]

    def edge_sum(components, slots, rims=None, rows=None):
        ring = len(slots) < count
        for c in range(components):
            west_at = slice(c * NODES, c * NODES + NP)
            east_at = slice((c + 1) * NODES - NP, (c + 1) * NODES)
            west = [sums[k, west_at] for k in slots]
            east = [sums[k, east_at] for k in slots]
            at_east, at_west = shifted(west, 1, ring), shifted(east, -1, ring)
            for n, k in enumerate(slots):
                if rims is not None:
                    at_east[n] = jnp.where(at_rim[k], rims[k][c], at_east[n])
                    at_west[n] = jnp.where(at_rim[k], rims[k][c], at_west[n])
                sums[k, west_at] = west[n] + at_west[n]
                sums[k, east_at] = east[n] + at_east[n]
        south_at = pl.ds(0, components * NP, stride=NP)
        north_at = pl.ds(NP - 1, components * NP, stride=NP)
        south = [sums[k, south_at] for k in slots]
        north = [sums[k, north_at] for k in slots]
        at_north, at_south = shifted(south, PITCH, ring), shifted(north, -PITCH, ring)
        for n, k in enumerate(slots):
            if k == count - 2:
                at_north[n] = jnp.where(closed_above, 0.0, at_north[n])
            if k == 1:
                at_south[n] = jnp.where(closed_below, 0.0, at_south[n])
        if rows is not None:
            at_south[0] = jnp.where(first_row, rows[0], at_south[0])
            at_north[-1] = jnp.where(last_row, rows[1], at_north[-1])
        for n, k in enumerate(slots):
            sums[k, south_at] = south[n] + at_south[n]
            sums[k, north_at] = north[n] + at_north[n]

    node = lax.broadcasted_iota(i32, (1, NP, 1), 1)
    rows = []
    for tile in (tiles[0], tiles[-1]):
        rim = tile[ALL_ROWS:]
        east = pltpu.roll(rim, LANES - 1, 1).reshape(4, NP, LANES)
        west = pltpu.roll(rim, 1, 1).reshape(4, NP, LANES)
        rim = (
            rim.reshape(4, NP, LANES)
            + jnp.where(node == NP - 1, pltpu.roll(east, NP - 1, 1), 0.0)
            + jnp.where(node == 0, pltpu.roll(west, 1, 1), 0.0)
        )
        rows.append(rim.reshape(EDGE_ROWS, LANES))
    rims = [
        [tile[ROWS + c * NP : ROWS + (c + 1) * NP] for c in range(4)] for tile in tiles
    ]

    every = tuple(range(count))
    groups = (every[0:2], every[2:4], every[4:])

    def part_of(group, n):
        return jnp.concatenate([tiles[k][n * NODES : (n + 1) * NODES] for k in group], 1)

    def put(group, parts):
        for c, part in enumerate(parts):
            for n, k in enumerate(group):
                sums[k, c * NODES : (c + 1) * NODES] = part[:, n * LANES : (n + 1) * LANES]

    def summed(group, c):
        return jnp.concatenate([sums[k, c * NODES : (c + 1) * NODES] for k in group], 1)

    def average(group, per_mass):
        return [summed(group, c) * per_mass for c in range(3)]

    def laplace(s):
        return [
            dot(table[4 * NODES :, : 3 * NODES], jnp.concatenate(high_low_high(part), 0))
            for part in s
        ]

    start, fixed = [], []
    for group in groups:
        area = part_of(group, 3)
        root = jnp.sqrt(area)
        mass = jnp.concatenate([weight] * len(group), 1) * area
        start.append([part_of(group, c) for c in range(3)])
        fixed.append((root * part_of(group, 4), root, mass * part_of(group, 5)))
        put(group, [mass])
    edge_sum(1, every, [rim[3:] for rim in rims], [rim[3 * NP :] for rim in rows])
    per_mass = [1.0 / summed(group, 0) for group in groups]

    for n, group in enumerate(groups):
        put(group, mass_tendency(table, *start[n], *fixed[n]))
    edge_sum(3, every, rims, [rim[: 3 * NP] for rim in rows])
    one = []
    for n, group in enumerate(groups):
        change = average(group, per_mass[n])
        one.append([s + time_step * c for s, c in zip(start[n], change)])
        put(group, mass_tendency(table, *one[n], *fixed[n]))
    edge_sum(3, every)
    two = []
    for n, group in enumerate(groups):
        change = average(group, per_mass[n])
        two.append(
            [0.75 * s + 0.25 * (o + time_step * c) for s, o, c in zip(start[n], one[n], change)]
        )
        put(group, mass_tendency(table, *two[n], *fixed[n]))
    edge_sum(3, every)

    def regrouped(per_group):
        (outer_low, high_above) = per_group[0], per_group[1]
        below, low = outer_low[:, :LANES], outer_low[:, LANES:]
        centre, high = high_above[:, :LANES], high_above[:, LANES:]
        near = jnp.where(lane < LANES // 2, per_group[2], below)
        return [beside(low, centre), beside(high, near)]

    def of_groups(values):
        return [list(parts) for parts in zip(*(regrouped(part) for part in zip(*values)))]

    for c in range(3):
        rows_at = slice(c * NODES, (c + 1) * NODES)
        sums[count - 1, rows_at] = jnp.where(
            lane < LANES // 2, sums[count - 1, rows_at], sums[0, rows_at]
        )
    slots = every[1:]
    groups = (slots[0:2], slots[2:4])
    start, two = of_groups(start), of_groups(two)
    tide = regrouped([part_of(every[0:2], 6), part_of(every[2:4], 6), part_of(every[4:], 6)])
    per_mass = regrouped(per_mass)
    three = []
    for n, group in enumerate(groups):
        change = average(group, per_mass[n])
        now = [
            s / 3.0 + 2.0 / 3.0 * (o + time_step * c)
            for s, o, c in zip(start[n], two[n], change)
        ]
        now[0] = now[0] + tide[n]
        three.append(now)
        put(group, laplace(now))
    edge_sum(3, slots)
    for n, group in enumerate(groups):
        put(group, laplace(average(group, per_mass[n])))
    edge_sum(3, slots)
    stepped = []
    for n, group in enumerate(groups):
        change = average(group, per_mass[n])
        now = [s - time_step * hyper_coeff * b for s, b in zip(three[n], change)]
        stepped.append(jnp.concatenate(now, 0))
    stepped = jnp.concatenate(stepped, 1)[:, :MID]
    own = ext_ref[3:4, LANES : LANES + MID] != 0
    stored = picked(jnp.where(own, stepped, 0.0), hot_ref[...])
    out_ref[...] = stored.reshape(out_ref.shape)


def on_device(fields, jacobian, water_depth, coriolis, tide_height, slot_of, seam_rows):
    block_cols = lax.axis_size("blk") // BY
    table, weight = operator_table()
    table, weight, lanes, ext, outer = map(jnp.asarray, (table, weight, *lane_tables()))
    vmem = pl.BlockSpec(memory_space=pltpu.VMEM)
    smem = pl.BlockSpec(memory_space=pltpu.SMEM)
    hbm = pl.BlockSpec(memory_space=pltpu.HBM)
    params = pltpu.CompilerParams(vmem_limit_bytes=48 * 2**20)
    held = (fields, jacobian, water_depth, coriolis, tide_height)

    def call(kernel, ins, outs, cost, scratch=(), name=None):
        return pl.pallas_call(
            kernel,
            out_shape=[jax.ShapeDtypeStruct(*out) for out in outs],
            in_specs=[spec for spec, value in ins],
            out_specs=[vmem] * len(outs),
            scratch_shapes=list(scratch),
            compiler_params=params,
            cost_estimate=pl.CostEstimate(
                flops=cost, bytes_accessed=2 * 2**20, transcendentals=0
            ),
            name=name,
        )(
            *[
                pltpu.with_memory_space_constraint(value, pltpu.HBM) if spec is hbm else value
                for spec, value in ins
            ]
        )

    strip = ((HALF_ROWS, LANES), f32)
    def room(values, spaces=None):
        spaces = spaces or [pltpu.VMEM] * len(values)
        buffers = [space(x.shape, x.dtype) for space, x in zip(spaces, values)]
        return buffers + [pltpu.SemaphoreType.DMA((len(values),))]

    needed = (seam_rows, slot_of, *held, table, weight)
    corner = ((CORNER_ROWS, LANES), f32)
    scratch = [pltpu.VMEM((1, 4 * NODES, LANES), f32)]
    strip1, far1, strip0, far0, to_next, to_pair, stored = call(
        functools.partial(strips_kernel, block_cols),
        [(hbm, x) for x in needed],
        [strip, corner, strip, corner, strip, strip, ((ROWS, ELEMENTS), f32)],
        10**8,
        scratch=room(needed, [pltpu.SMEM] + [pltpu.VMEM] * (len(needed) - 1)) + scratch,
        name="strips",
    )
    span = block_cols * BY
    both = ("face", "blk")
    places = [(f, x, y) for f in range(2) for x in range(block_cols) for y in range(BY)]

    def rank(face, block_x, block_y):
        return face * span + block_x * BY + block_y

    def same(y):
        return y

    def in_pair(y):
        return y ^ 1

    def next_pair(y):
        other = y + 1 if y % 2 else y - 1
        return other if 0 <= other < BY else y

    def swapped(value, partner):
        pairs = [
            (rank(f, x, y), rank(f if partner(y) != y else 1 - f, x, partner(y)))
            for f, x, y in places
        ]
        return lax.ppermute(value, both, pairs)

    def across(value0, value1, partner):
        last = block_cols - 1

        def aligned(y):
            return partner is same or partner(y) != y

        straight = {
            (f, x, y): (f, x + 1, partner(y)) if x < last else (1 - f, 0, partner(y))
            for f, x, y in places
        }
        turned = {
            (f, last, y): (1 - f, 0, BY - 1 - partner(y) if aligned(y) else y)
            for f in range(2)
            for y in range(BY)
        }

        def eastward(value, pairs):
            return lax.ppermute(value, both, [(rank(*a), rank(*b)) for a, b in pairs.items()])

        def westward(value, pairs):
            return lax.ppermute(value, both, [(rank(*b), rank(*a)) for a, b in pairs.items()])

        if block_cols == 1:
            return eastward(value0, straight), eastward(value1, turned)
        flipped = (seam_rows[:, 1] - seam_rows[:, 0]) % seam_rows.shape[1] != 1
        face = lax.axis_index("face")
        block_x = lax.axis_index("blk") // BY
        return (
            jnp.where(
                (block_x == last) & flipped[face],
                westward(value1, turned),
                westward(value1, straight),
            ),
            jnp.where(
                (block_x == 0) & flipped[1 - face],
                eastward(value0, turned),
                eastward(value0, straight),
            ),
        )

    halo0, halo1 = across(strip0, strip1, same)
    far0, far1 = across(far0, far1, next_pair)
    from_next = swapped(to_next, next_pair)
    own, hot = call(
        own_kernel,
        [(vmem, x) for x in (stored, slot_of, lanes)],
        [((ROWS, MID), f32), ((MID, ELEMENTS), bf16)],
        10**8,
        name="own",
    )
    (to_pair,) = call(
        corners_kernel,
        [(vmem, x) for x in (halo1, halo0, to_pair, table, weight, hot)],
        [((HALF_ROWS + 2 * CORNER_ROWS, LANES), f32)],
        10**8,
        scratch=scratch,
        name="corners",
    )
    from_pair = swapped(to_pair, in_pair)
    tile = ((ALL_ROWS, LANES), f32)
    low, centre, high = call(
        functools.partial(middle_kernel, block_cols),
        [(smem, seam_rows)] + [(vmem, x) for x in (halo0, halo1, own, lanes, far1, far0, from_next)],
        [tile, tile, tile],
        10**11,
        name="middle",
    )
    (stepped,) = call(
        functools.partial(steps_kernel, block_cols),
        [(smem, seam_rows)]
        + [
            (vmem, x)
            for x in (
                from_pair, from_next, far0, far1, low, centre, high,
                hot, table, weight, ext, outer,
            )
        ],
        [(fields.shape, f32)],
        10**8,
        scratch=[pltpu.VMEM((EXT // LANES, 3 * NODES, LANES), f32)],
        name="steps",
    )
    return stepped


def solution(mesh):
    return jax.shard_map(
        on_device,
        mesh=mesh,
        in_specs=(
            P(None, None, None, ("face", "blk")),
            P(None, None, ("face", "blk")),
            P(None, None, ("face", "blk")),
            P(None, None, ("face", "blk")),
            P(None, None, ("face", "blk")),
            P(("face", "blk"), None),
            P(),
        ),
        out_specs=P(None, None, None, ("face", "blk")),
        check_vma=False,
    )
```

```python
import functools
import math

import jax
import jax.numpy as jnp
import ml_dtypes
import numpy as np
from jax import lax
from jax.experimental import pallas as pl
from jax.experimental.pallas import tpu as pltpu
from jax.sharding import PartitionSpec as P

BY = 16
GX = 16
GY = 16
NP = 8
NODES = NP * NP
ARRAYS = 7
ROWS = ARRAYS * NODES
MOVED = 6 * NODES
EDGE_ROWS = 4 * NP
ALL_ROWS = ROWS + EDGE_ROWS
HALF_ROWS = (MOVED + NODES // 2 + 2 * NP) // 2
RING = 4
RIM_ROWS = ROWS + 2 * EDGE_ROWS
CORNER_ROWS = (MOVED + NODES // 2 + 4 * NP) // 8
PITCH = GX + 2 * RING
MID = GY * PITCH
LANES = 128
EXT = MID + 2 * LANES
LEAD = LANES - RING * PITCH
ELEMENTS = GX * GY

time_step = 0.03
hyper_coeff = 0.0002

f32 = jnp.float32
bf16 = jnp.bfloat16
i32 = jnp.int32


def legendre_pair(location, degree):
    lower_value = 1.0
    upper_value = location
    for polynomial_order in range(2, degree + 1):
        lower_value, upper_value = (
            upper_value,
            (
                (2 * polynomial_order - 1) * location * upper_value
                - (polynomial_order - 1) * lower_value
            )
            / polynomial_order,
        )
    return (lower_value, upper_value)


def gll_tables(points):
    degree = points - 1
    locations = [-math.cos(math.pi * position / degree) for position in range(points)]
    for iteration in range(100):
        updated = []
        for location in locations:
            lower_value, upper_value = legendre_pair(location, degree)
            updated.append(
                location - (location * upper_value - lower_value) / ((degree + 1) * upper_value)
            )
        locations = updated
    locations[0] = -1.0
    locations[degree] = 1.0
    legendre_at = [legendre_pair(location, degree)[1] for location in locations]
    weights = [2.0 / (degree * (degree + 1) * value * value) for value in legendre_at]
    corner_value = degree * (degree + 1) / 4.0
    derivative = []
    for row_index in range(points):
        row_values = []
        for column_index in range(points):
            if row_index != column_index:
                row_values.append(
                    legendre_at[row_index]
                    / (legendre_at[column_index] * (locations[row_index] - locations[column_index]))
                )
            elif row_index == 0:
                row_values.append(-corner_value)
            elif row_index == degree:
                row_values.append(corner_value)
            else:
                row_values.append(0.0)
        derivative.append(row_values)
    return np.asarray(weights, np.float64), np.asarray(derivative, np.float64)


def in_three(matrix):
    high = matrix.astype(ml_dtypes.bfloat16)
    low = (matrix - high.astype(np.float64)).astype(ml_dtypes.bfloat16)
    return np.concatenate([high, high, low], 1)


def operator_table():
    weights, derivative = gll_tables(NP)
    eye = np.eye(NP)
    node_weight = np.outer(weights, weights).reshape(NODES, 1)
    along_x = node_weight * np.kron(derivative, eye)
    along_y = node_weight * np.kron(eye, derivative)
    second = derivative @ derivative
    both = node_weight * (np.kron(second, eye) + np.kron(eye, second))
    table = np.zeros((5 * NODES, 4 * NODES), ml_dtypes.bfloat16)
    table[:NODES, : 3 * NODES] = in_three(along_x)
    table[NODES : 2 * NODES, : 3 * NODES] = in_three(along_y)
    flux = [in_three(along_x), in_three(along_y)]
    for k, part in enumerate(flux):
        at = 2 * k * NODES
        table[2 * NODES : 3 * NODES, at : at + 2 * NODES] = part[:, : 2 * NODES]
        table[3 * NODES : 4 * NODES, at : at + NODES] = part[:, 2 * NODES :]
    table[4 * NODES :, : 3 * NODES] = in_three(both)
    spread = np.broadcast_to(node_weight, (NODES, LANES)).astype(np.float32)
    return table.astype(np.float32), np.ascontiguousarray(spread)


def lane_tables():
    table = np.zeros((24, MID), np.int32)
    for lane in range(MID):
        row, col = divmod(lane, PITCH)
        x = col - RING
        own = 0 <= x < GX
        table[0:8, lane] = x * GY + row if own else -1
        if not own:
            table[8:16, lane] = row * RING + (col if x < 0 else x - GX)
        table[16:24, lane] = 0 if own else (1 if x < 0 else 2)
    ext = np.zeros((8, EXT), np.int32)
    outer = np.zeros((24, 2 * LANES), np.int32)
    for lane in range(EXT):
        row, col = divmod(lane - LEAD, PITCH)
        y = row - RING
        x = col - RING
        inside = 0 <= row < GY + 2 * RING
        ext[0, lane] = x in (-RING, GX + RING - 1)
        ext[1, lane] = y == GY - 1
        ext[2, lane] = y == 0
        ext[3, lane] = 0 <= y < GY and 0 <= x < GX
        ext[4, lane] = y == -RING
        ext[5, lane] = y == GY + RING - 1
        if inside and not 0 <= y < GY:
            place = lane if y < 0 else lane - LANES - MID + LANES
            step = y + RING if y < 0 else y - GY
            if 0 <= x < GX:
                outer[0:8, place] = step * GX + x
                outer[8:16, place] = 1
            else:
                outer[0:8, place] = LANES + step * RING + (x + RING if x < 0 else x - GX)
                outer[8:16, place] = 2 if x < 0 else 3
            outer[16:24, place] = y > 0
    return table, ext, outer


def dot(a, b):
    return jnp.dot(a, b, preferred_element_type=f32)


def picked(values, one_hot):
    high = values.astype(bf16)
    low = (values - high.astype(f32)).astype(bf16)
    return dot(high, one_hot) + dot(low, one_hot)


def as_one_hot(row_of_lane, depth):
    index = lax.broadcasted_iota(i32, (depth, row_of_lane.shape[1]), 0)
    return jnp.where(index == row_of_lane[0:1], 1.0, 0.0).astype(bf16)


def high_low_high(values):
    high = values.astype(bf16)
    low = (values - high.astype(f32)).astype(bf16)
    return [high, low, high]


def by_slot(slot_ref, cell_of_lane):
    slots = jnp.broadcast_to(slot_ref[...], (8, ELEMENTS)).astype(f32).astype(bf16)
    chosen = dot(slots, as_one_hot(cell_of_lane, ELEMENTS))
    chosen = jnp.where(cell_of_lane >= 0, chosen, -1.0)
    index = lax.broadcasted_iota(i32, (ELEMENTS, cell_of_lane.shape[1]), 0).astype(f32)
    return jnp.where(index == chosen[0:1], 1.0, 0.0).astype(bf16)


def stored_rows(fields_ref, others):
    fields = fields_ref[...].reshape(3 * NODES, ELEMENTS)
    others = [ref[...].reshape(NODES, ELEMENTS) for ref in others]
    return jnp.concatenate([fields[:NODES] - others[-1], fields[NODES:]] + others, 0)


def mass_tendency(table, p, u, v, area_depth, weighted_area, spin):
    slopes = dot(table[: 2 * NODES, : 3 * NODES], jnp.concatenate(high_low_high(p), 0))
    flux = high_low_high(area_depth * u)[:2] + high_low_high(area_depth * v)[:2]
    spread = dot(table[2 * NODES : 4 * NODES], jnp.concatenate(flux, 0))
    return [
        -(spread[:NODES] + spread[NODES:]),
        spin * v - weighted_area * slopes[:NODES],
        -spin * u - weighted_area * slopes[NODES:],
    ]


def edge_values(table_ref, weight_ref, p, u, v, area, depth, spin):
    root = jnp.sqrt(area)
    mass = jnp.concatenate([weight_ref[...]] * (area.shape[1] // LANES), 1) * area
    table = table_ref[...].astype(bf16)
    return mass_tendency(table, p, u, v, root * depth, root, mass * spin) + [mass]


def row_edges(sums):
    return tuple(sums[0, pl.ds(j, EDGE_ROWS, stride=NP)] for j in (NP - 1, 0))


def beside(left, right):
    return jnp.concatenate([left, right], 1)


def one_of_four(parts, index):
    out = parts[0]
    for k in range(1, 4):
        out = jnp.where(index == k, parts[k], out)
    return out


def folded(tide, kept, late, step):
    half = NODES // 2
    back = pltpu.roll(tide[half:], LANES - step, 1)
    onward = pltpu.roll(tide[half:], step, 1)
    return jnp.where(kept, tide[:half], jnp.where(late, back, onward))


def unfolded(rows, late, step):
    back = pltpu.roll(rows, LANES - step, 1)
    onward = pltpu.roll(rows, step, 1)
    return jnp.concatenate([rows, jnp.where(late, onward, back)], 0)


def strip_rows(parts, late, shift, rims):
    lane = lax.broadcasted_iota(i32, (1, LANES), 1)
    index = (lane >> shift) & 3
    kept = jnp.where(late, index // 2, 1 - index // 2) != 0
    tide = folded(parts[6], kept, late, 2 << shift)
    rim = one_of_four(rims, index)
    return jnp.concatenate(parts[:6] + [tide, rim, jnp.zeros_like(rim)], 0)


def placed_rows(whole, late, shift):
    half = NODES // 2
    tide = unfolded(whole[MOVED : MOVED + half], late, 2 << shift)
    rim = whole[MOVED + half : MOVED + half + NP]
    return jnp.concatenate([whole[:MOVED], tide] + spread_out(rim, late, shift), 0)


def spread_out(rim, late, shift):
    parts = []
    for k in range(4):
        first = pltpu.roll(rim, (LANES - (k << shift)) % LANES, 1) if k else rim
        last = pltpu.roll(rim, (3 - k) << shift, 1) if k < 3 else rim
        parts.append(jnp.where(late, first, last))
    return parts


def with_row_rim(whole, sums, top):
    north, south = row_edges(sums)
    rim = jnp.where(top, pltpu.roll(north, RING, 1), pltpu.roll(south, LANES - RING, 1))
    parts = [rim[k * NP : (k + 1) * NP] for k in range(4)]
    lane = lax.broadcasted_iota(i32, (1, LANES), 1)
    spots = []
    for k, part in enumerate(parts):
        first = pltpu.roll(part, k * RING, 1) if k else part
        last = pltpu.roll(part, (LANES - (3 - k) * RING) % LANES, 1) if k < 3 else part
        spots.append(jnp.where(top, first, last))
    rim = one_of_four(spots, (lane >> 2) & 3)
    return jnp.concatenate([whole[: MOVED + NODES // 2 + NP], rim], 0)


def corner_of(whole, start, top):
    lane = lax.broadcasted_iota(i32, (1, LANES), 1)
    base = LANES - start - jnp.where(top != 0, 48, 0)
    whole = jnp.concatenate([whole, jnp.zeros((8 * CORNER_ROWS - whole.shape[0], LANES), f32)], 0)
    out = None
    for k in range(8):
        part = whole[k * CORNER_ROWS : (k + 1) * CORNER_ROWS]
        part = pltpu.roll(part, (base + 16 * k) & (LANES - 1), 1)
        out = part if k == 0 else jnp.where(lane >= 16 * k, part, out)
    return out


def packed(whole):
    second = lax.broadcasted_iota(i32, (1, LANES), 1) >= 64
    top, bottom = whole[:HALF_ROWS], whole[HALF_ROWS:]
    return (
        jnp.where(second, pltpu.roll(bottom, 64, 1), top),
        jnp.where(second, bottom, pltpu.roll(top, 64, 1)),
    )


def unpacked(in0, in1):
    second = lax.broadcasted_iota(i32, (1, LANES), 1) >= 64
    top = jnp.where(second, pltpu.roll(in1, 64, 1), in0)
    bottom = jnp.where(second, in1, pltpu.roll(in0, 64, 1))
    return jnp.concatenate([top, bottom], 0)


def seam_flags(seam_ref, block_cols):
    size_y = seam_ref.shape[1]
    face = lax.axis_index("face")
    blk = lax.axis_index("blk")
    block_x = blk // BY

    def flipped(k):
        return jnp.where(lax.rem(seam_ref[k, 1] - seam_ref[k, 0] + size_y, size_y) != 1, 1, 0)

    first, second = flipped(0), flipped(1)
    east_flip = jnp.where(face == 0, first, second)
    west_flip = jnp.where(face == 0, second, first)
    if block_cols == 1:
        return 1 - east_flip, 0, east_flip, 1
    at_east = jnp.where(block_x == block_cols - 1, east_flip, 0)
    at_west = jnp.where(block_x == 0, west_flip, 0)
    return 1, at_east, 0, at_west


def strips_kernel(block_cols, *refs):
    sources, (out1_ref, out0_ref, stored_ref) = refs[:9], refs[9:12]
    buffers, sems = refs[12:21], refs[21]
    copies = [
        pltpu.make_async_copy(source, buffer, sems.at[k])
        for k, (source, buffer) in enumerate(zip(sources, buffers))
    ]
    for copy in copies:
        copy.start()
    seam_ref, slot_ref, fields_ref, area_ref, depth_ref, spin_ref, tide_ref = buffers[:7]
    table_ref, weight_ref = buffers[7:]
    for copy in copies[:2]:
        copy.wait()
    east0, flip0, east1, flip1 = seam_flags(seam_ref, block_cols)
    lane = lax.broadcasted_iota(i32, (8, 2 * LANES), 1)
    second = (lane & 64) != 0
    place = lane & 63
    row = place >> 2
    row = jnp.where(jnp.where(second, flip1, flip0) != 0, GY - 1 - row, row)
    east = jnp.where(second, east1, east0) != 0
    col = jnp.where(east, GX - RING, 0) + (place & 3)
    col = jnp.where(lane >= LANES, jnp.where(east, GX - RING - 1, RING), col)
    one_hot = by_slot(slot_ref, col * GY + row)
    for copy in copies[2:7]:
        copy.wait()
    stored = stored_rows(fields_ref, (area_ref, depth_ref, spin_ref, tide_ref))
    both = picked(stored, one_hot)

    lane = lax.broadcasted_iota(i32, (1, LANES), 1)
    second = lane >= 64
    flip = jnp.where(second, flip1, flip0) != 0
    sign = jnp.where(flip, -1.0, 1.0)
    node = lax.broadcasted_iota(i32, (1, NP, 1), 1)

    def in_frame(values):
        shaped = values.reshape(-1, NP, LANES)
        turned = pltpu.roll(shaped, 4, 1)
        turned = jnp.where((node & 2) == 0, pltpu.roll(turned, 6, 1), pltpu.roll(turned, 2, 1))
        turned = jnp.where((node & 1) == 0, pltpu.roll(turned, 7, 1), pltpu.roll(turned, 1, 1))
        values = jnp.where(flip[None], turned, shaped).reshape(values.shape)
        parts = [values[k * NODES : (k + 1) * NODES] for k in range(ARRAYS)]
        parts[2] = parts[2] * sign
        parts[5] = parts[5] * sign
        return parts

    strip, ring = in_frame(both[:, :LANES]), in_frame(both[:, LANES:])
    for copy in copies[7:]:
        copy.wait()
    edges = edge_values(table_ref, weight_ref, *ring[:6])
    east = jnp.where(second, east1, east0) != 0
    ends = [jnp.where(east, part[NODES - NP :], part[:NP]) for part in edges]
    out0_ref[...], out1_ref[...] = packed(strip_rows(strip, east, 0, ends))
    stored_ref[...] = stored


def rows_kernel(
    block_cols, seam_ref, stored_ref, strip1_ref, strip0_ref, slot_ref, table_ref, weight_ref,
    next_ref, far0_ref, far1_ref, pair_ref, sums,
):
    east0, flip0, east1, flip1 = seam_flags(seam_ref, block_cols)
    odd = lax.axis_index("blk") & 1

    def goes_up(lane):
        return jnp.where((lane & 64) != 0, odd, 1 - odd) != 0

    lane = lax.broadcasted_iota(i32, (8, 2 * LANES), 1)
    up = goes_up(lane)
    row = jnp.where(up, GY - RING, 0) + ((lane & 63) >> 4)
    row = jnp.where(lane >= LANES, jnp.where(up, GY - RING - 1, RING), row)
    both = picked(stored_ref[...], by_slot(slot_ref, (lane & 15) * GY + row))
    rows, behind = (
        [part[k * NODES : (k + 1) * NODES] for k in range(ARRAYS)]
        for part in (both[:, :LANES], both[:, LANES:])
    )
    whole = unpacked(strip0_ref[...], strip1_ref[...])
    strip = [whole[k * NODES : (k + 1) * NODES] for k in range(6)]
    edges = edge_values(table_ref, weight_ref, *map(beside, strip, behind[:6]))
    sums[0] = jnp.concatenate([part[:, :LANES] for part in edges], 0)
    lane = lax.broadcasted_iota(i32, (1, LANES), 1)
    top0, top1 = odd ^ flip0, odd ^ flip1
    whole = with_row_rim(whole, sums, jnp.where(lane >= 64, top1, top0) != 0)
    far0_ref[...] = corner_of(whole, 0, top0)
    far1_ref[...] = corner_of(whole, 64, top1)
    sums[0] = jnp.concatenate([part[:, LANES:] for part in edges], 0)
    up = goes_up(lane)
    rim = jnp.where(up, *row_edges(sums))
    rim = [rim[k * NP : (k + 1) * NP] for k in range(4)]
    pair_ref[...], next_ref[...] = packed(strip_rows(rows, up, 4, rim))


def corners_kernel(in1_ref, in0_ref, pair_ref, table_ref, weight_ref, *refs):
    out_ref, sums = refs[-2:]
    top = 1 - (lax.axis_index("blk") & 1)
    whole = unpacked(in0_ref[...], in1_ref[...])
    parts = [whole[k * NODES : (k + 1) * NODES] for k in range(6)]
    sums[0] = jnp.concatenate(edge_values(table_ref, weight_ref, *parts), 0)
    whole = with_row_rim(whole, sums, jnp.broadcast_to(top != 0, (1, LANES)))
    out_ref[:HALF_ROWS] = pair_ref[...]
    out_ref[HALF_ROWS : HALF_ROWS + CORNER_ROWS] = corner_of(whole, 0, top)
    out_ref[HALF_ROWS + CORNER_ROWS :] = corner_of(whole, 64, top)


def own_kernel(stored_ref, slot_ref, lanes_ref, own_ref, hot_ref):
    one_hot = by_slot(slot_ref, lanes_ref[0:8])
    own_ref[...] = picked(stored_ref[...], one_hot)
    hot_ref[...] = one_hot.astype(f32).T.astype(bf16)


def middle_kernel(
    block_cols, seam_ref, in0_ref, in1_ref, own_ref, lanes_ref, low_ref, centre_ref, high_ref
):
    east0, flip0, east1, flip1 = seam_flags(seam_ref, block_cols)
    second = lax.broadcasted_iota(i32, (1, LANES), 1) >= 64
    late = jnp.where(second, east1, east0) == 0
    whole = placed_rows(unpacked(in0_ref[...], in1_ref[...]), late, 0)
    side = lanes_ref[16:24]
    first_at = jnp.where(side == 2, 64 * (1 - east0), 64 * east0)
    place = jnp.where(side == 0, -1, lanes_ref[8:16] + first_at)
    placed = picked(whole, as_one_hot(place, LANES))
    for k, ref in enumerate((low_ref, centre_ref, high_ref)):
        part = slice(k * LANES, (k + 1) * LANES)
        ref[:ROWS] = placed[:ROWS, part] + own_ref[:, part]
        ref[ROWS:] = placed[ROWS:, part]


def far_kernel(far1_ref, far0_ref, *refs):
    out_ref = refs[-1]
    out_ref[:CORNER_ROWS] = far0_ref[...]
    out_ref[CORNER_ROWS:] = far1_ref[...]


def steps_kernel(
    block_cols, seam_ref, pair_ref, next_ref, far_ref, low_ref, centre_ref,
    high_ref, hot_ref, table_ref, weight_ref, ext_ref, outer_ref, out_ref, sums,
):
    east0, flip0, east1, flip1 = seam_flags(seam_ref, block_cols)
    odd = lax.axis_index("blk") & 1
    block_y = lax.rem(lax.axis_index("blk"), BY)

    lane = lax.broadcasted_iota(i32, (1, LANES), 1)
    pair = pair_ref[...]
    late = jnp.where(lane < 64, odd, 1 - odd) != 0
    strips = placed_rows(unpacked(pair[:HALF_ROWS], next_ref[...]), late, 4)
    strips = jnp.concatenate(
        [strips[:ROWS], jnp.zeros((EDGE_ROWS, LANES), f32), strips[ROWS:]], 0
    )
    near = pair[HALF_ROWS:]
    far = far_ref[...]
    sources = (near[:CORNER_ROWS], near[CORNER_ROWS:], far[:CORNER_ROWS], far[CORNER_ROWS:])
    corners = []
    for k in range(8):
        rows = None
        for n, source in enumerate(sources):
            shift = 16 * (n - k) % LANES
            part = pltpu.roll(source, shift, 1) if shift else source
            rows = part if n == 0 else jnp.where(lane >= 16 * n, part, rows)
        corners.append(rows)
    corners = jnp.concatenate(corners, 0)
    rim = MOVED + NODES // 2 + NP
    late = jnp.where((lane & 16) != 0, east1, east0) == 0
    below = jnp.where((lane & 32) != 0, 1 - odd, odd) != 0
    corners = jnp.concatenate(
        [placed_rows(corners, late, 0)] + spread_out(corners[rim : rim + NP], below, 2), 0
    )
    around = jnp.concatenate([strips, corners], 1)
    kind = outer_ref[8:16]
    sender = jnp.where(outer_ref[16:24] != 0, odd, 1 - odd)
    strip_at = jnp.where(kind == 3, 16 * (1 - east0), 16 * east0)
    place = outer_ref[0:8] + jnp.where(kind == 1, 64 * sender, 32 * sender + strip_at)
    outer = picked(around, as_one_hot(jnp.where(kind == 0, -1, place), 2 * LANES))
    tiles = (outer[:, :LANES], low_ref, centre_ref, high_ref, outer[:, LANES:])
    count = len(tiles)
    table = table_ref[...].astype(bf16)
    weight = weight_ref[...]
    masks = [ext_ref[:, k * LANES : (k + 1) * LANES] for k in range(count)]
    at_rim = [mask[0:1] != 0 for mask in masks]
    closed_above = jnp.where(block_y == BY - 1, masks[-2][1:2], 0) != 0
    closed_below = jnp.where(block_y == 0, masks[1][2:3], 0) != 0
    first_row = masks[0][4:5] != 0
    last_row = masks[-1][5:6] != 0

    def shifted(parts, by, ring):
        turned = [pltpu.roll(part, -by % LANES, 1) for part in parts]
        size = len(parts)
        step = 1 if by > 0 else -1
        others = [(k + step) % size if ring else min(max(k + step, 0), size - 1) for k in range(size)]
        from_other = lane >= LANES - by if by > 0 else lane < -by
        return [jnp.where(from_other, turned[others[k]], turned[k]) for k in range(size)]

    def edge_sum(components, slots, rims=None, rows=None):
        ring = len(slots) < count
        for c in range(components):
            west_at = slice(c * NODES, c * NODES + NP)
            east_at = slice((c + 1) * NODES - NP, (c + 1) * NODES)
            west = [sums[k, west_at] for k in slots]
            east = [sums[k, east_at] for k in slots]
            at_east, at_west = shifted(west, 1, ring), shifted(east, -1, ring)
            for n, k in enumerate(slots):
                if rims is not None:
                    at_east[n] = jnp.where(at_rim[k], rims[k][c], at_east[n])
                    at_west[n] = jnp.where(at_rim[k], rims[k][c], at_west[n])
                sums[k, west_at] = west[n] + at_west[n]
                sums[k, east_at] = east[n] + at_east[n]
        south_at = pl.ds(0, components * NP, stride=NP)
        north_at = pl.ds(NP - 1, components * NP, stride=NP)
        south = [sums[k, south_at] for k in slots]
        north = [sums[k, north_at] for k in slots]
        at_north, at_south = shifted(south, PITCH, ring), shifted(north, -PITCH, ring)
        for n, k in enumerate(slots):
            if k == count - 2:
                at_north[n] = jnp.where(closed_above, 0.0, at_north[n])
            if k == 1:
                at_south[n] = jnp.where(closed_below, 0.0, at_south[n])
        if rows is not None:
            at_south[0] = jnp.where(first_row, rows[0], at_south[0])
            at_north[-1] = jnp.where(last_row, rows[1], at_north[-1])
        for n, k in enumerate(slots):
            sums[k, south_at] = south[n] + at_south[n]
            sums[k, north_at] = north[n] + at_north[n]

    node = lax.broadcasted_iota(i32, (1, NP, 1), 1)
    rows = []
    for tile in (tiles[0], tiles[-1]):
        rim = tile[ALL_ROWS:]
        east = pltpu.roll(rim, LANES - 1, 1).reshape(4, NP, LANES)
        west = pltpu.roll(rim, 1, 1).reshape(4, NP, LANES)
        rim = (
            rim.reshape(4, NP, LANES)
            + jnp.where(node == NP - 1, pltpu.roll(east, NP - 1, 1), 0.0)
            + jnp.where(node == 0, pltpu.roll(west, 1, 1), 0.0)
        )
        rows.append(rim.reshape(EDGE_ROWS, LANES))
    rims = [
        [tile[ROWS + c * NP : ROWS + (c + 1) * NP] for c in range(4)] for tile in tiles
    ]

    every = tuple(range(count))
    groups = (every[0:2], every[2:4], every[4:])

    def part_of(group, n):
        return jnp.concatenate([tiles[k][n * NODES : (n + 1) * NODES] for k in group], 1)

    def put(group, parts):
        for c, part in enumerate(parts):
            for n, k in enumerate(group):
                sums[k, c * NODES : (c + 1) * NODES] = part[:, n * LANES : (n + 1) * LANES]

    def summed(group, c):
        return jnp.concatenate([sums[k, c * NODES : (c + 1) * NODES] for k in group], 1)

    def average(group, per_mass):
        return [summed(group, c) * per_mass for c in range(3)]

    def laplace(s):
        return [
            dot(table[4 * NODES :, : 3 * NODES], jnp.concatenate(high_low_high(part), 0))
            for part in s
        ]

    start, fixed = [], []
    for group in groups:
        area = part_of(group, 3)
        root = jnp.sqrt(area)
        mass = jnp.concatenate([weight] * len(group), 1) * area
        start.append([part_of(group, c) for c in range(3)])
        fixed.append((root * part_of(group, 4), root, mass * part_of(group, 5)))
        put(group, [mass])
    edge_sum(1, every, [rim[3:] for rim in rims], [rim[3 * NP :] for rim in rows])
    per_mass = [1.0 / summed(group, 0) for group in groups]

    for n, group in enumerate(groups):
        put(group, mass_tendency(table, *start[n], *fixed[n]))
    edge_sum(3, every, rims, [rim[: 3 * NP] for rim in rows])
    one = []
    for n, group in enumerate(groups):
        change = average(group, per_mass[n])
        one.append([s + time_step * c for s, c in zip(start[n], change)])
        put(group, mass_tendency(table, *one[n], *fixed[n]))
    edge_sum(3, every)
    two = []
    for n, group in enumerate(groups):
        change = average(group, per_mass[n])
        two.append(
            [0.75 * s + 0.25 * (o + time_step * c) for s, o, c in zip(start[n], one[n], change)]
        )
        put(group, mass_tendency(table, *two[n], *fixed[n]))
    edge_sum(3, every)

    def regrouped(per_group):
        (outer_low, high_above) = per_group[0], per_group[1]
        below, low = outer_low[:, :LANES], outer_low[:, LANES:]
        centre, high = high_above[:, :LANES], high_above[:, LANES:]
        near = jnp.where(lane < LANES // 2, per_group[2], below)
        return [beside(low, centre), beside(high, near)]

    def of_groups(values):
        return [list(parts) for parts in zip(*(regrouped(part) for part in zip(*values)))]

    for c in range(3):
        rows_at = slice(c * NODES, (c + 1) * NODES)
        sums[count - 1, rows_at] = jnp.where(
            lane < LANES // 2, sums[count - 1, rows_at], sums[0, rows_at]
        )
    slots = every[1:]
    groups = (slots[0:2], slots[2:4])
    start, two = of_groups(start), of_groups(two)
    tide = regrouped([part_of(every[0:2], 6), part_of(every[2:4], 6), part_of(every[4:], 6)])
    per_mass = regrouped(per_mass)
    three = []
    for n, group in enumerate(groups):
        change = average(group, per_mass[n])
        now = [
            s / 3.0 + 2.0 / 3.0 * (o + time_step * c)
            for s, o, c in zip(start[n], two[n], change)
        ]
        now[0] = now[0] + tide[n]
        three.append(now)
        put(group, laplace(now))
    edge_sum(3, slots)
    for n, group in enumerate(groups):
        put(group, laplace(average(group, per_mass[n])))
    edge_sum(3, slots)
    stepped = []
    for n, group in enumerate(groups):
        change = average(group, per_mass[n])
        now = [s - time_step * hyper_coeff * b for s, b in zip(three[n], change)]
        stepped.append(jnp.concatenate(now, 0))
    stepped = jnp.concatenate(stepped, 1)[:, :MID]
    own = ext_ref[3:4, LANES : LANES + MID] != 0
    stored = picked(jnp.where(own, stepped, 0.0), hot_ref[...])
    out_ref[...] = stored.reshape(out_ref.shape)


def on_device(fields, jacobian, water_depth, coriolis, tide_height, slot_of, seam_rows):
    block_cols = lax.axis_size("blk") // BY
    table, weight = operator_table()
    table, weight, lanes, ext, outer = map(jnp.asarray, (table, weight, *lane_tables()))
    vmem = pl.BlockSpec(memory_space=pltpu.VMEM)
    smem = pl.BlockSpec(memory_space=pltpu.SMEM)
    hbm = pl.BlockSpec(memory_space=pltpu.HBM)
    params = pltpu.CompilerParams(vmem_limit_bytes=48 * 2**20)
    held = (fields, jacobian, water_depth, coriolis, tide_height)

    def call(kernel, ins, outs, cost, scratch=(), name=None):
        return pl.pallas_call(
            kernel,
            out_shape=[jax.ShapeDtypeStruct(*out) for out in outs],
            in_specs=[spec for spec, value in ins],
            out_specs=[vmem] * len(outs),
            scratch_shapes=list(scratch),
            compiler_params=params,
            cost_estimate=pl.CostEstimate(
                flops=cost, bytes_accessed=2 * 2**20, transcendentals=0
            ),
            name=name,
        )(
            *[
                pltpu.with_memory_space_constraint(value, pltpu.HBM) if spec is hbm else value
                for spec, value in ins
            ]
        )

    strip = ((HALF_ROWS, LANES), f32)
    def room(values, spaces=None):
        spaces = spaces or [pltpu.VMEM] * len(values)
        buffers = [space(x.shape, x.dtype) for space, x in zip(spaces, values)]
        return buffers + [pltpu.SemaphoreType.DMA((len(values),))]

    needed = (seam_rows, slot_of, *held, table, weight)
    corner = ((CORNER_ROWS, LANES), f32)
    scratch = [pltpu.VMEM((1, 4 * NODES, LANES), f32)]
    strip1, strip0, stored = call(
        functools.partial(strips_kernel, block_cols),
        [(hbm, x) for x in needed],
        [strip, strip, ((ROWS, ELEMENTS), f32)],
        10**8,
        scratch=room(needed, [pltpu.SMEM] + [pltpu.VMEM] * (len(needed) - 1)),
        name="strips",
    )
    to_next, far0, far1, to_pair = call(
        functools.partial(rows_kernel, block_cols),
        [(smem, seam_rows)]
        + [(vmem, x) for x in (stored, strip1, strip0, slot_of, table, weight)],
        [strip, corner, corner, strip],
        10**8,
        scratch=scratch,
        name="rows",
    )
    span = block_cols * BY
    both = ("face", "blk")
    places = [(f, x, y) for f in range(2) for x in range(block_cols) for y in range(BY)]

    def rank(face, block_x, block_y):
        return face * span + block_x * BY + block_y

    def same(y):
        return y

    def in_pair(y):
        return y ^ 1

    def next_pair(y):
        other = y + 1 if y % 2 else y - 1
        return other if 0 <= other < BY else y

    def swapped(value, partner):
        pairs = [
            (rank(f, x, y), rank(f if partner(y) != y else 1 - f, x, partner(y)))
            for f, x, y in places
        ]
        return lax.ppermute(value, both, pairs)

    def across(value0, value1, partner):
        last = block_cols - 1

        def aligned(y):
            return partner is same or partner(y) != y

        straight = {
            (f, x, y): (f, x + 1, partner(y)) if x < last else (1 - f, 0, partner(y))
            for f, x, y in places
        }
        turned = {
            (f, last, y): (1 - f, 0, BY - 1 - partner(y) if aligned(y) else y)
            for f in range(2)
            for y in range(BY)
        }

        def eastward(value, pairs):
            return lax.ppermute(value, both, [(rank(*a), rank(*b)) for a, b in pairs.items()])

        def westward(value, pairs):
            return lax.ppermute(value, both, [(rank(*b), rank(*a)) for a, b in pairs.items()])

        if block_cols == 1:
            return eastward(value0, straight), eastward(value1, turned)
        flipped = (seam_rows[:, 1] - seam_rows[:, 0]) % seam_rows.shape[1] != 1
        face = lax.axis_index("face")
        block_x = lax.axis_index("blk") // BY
        return (
            jnp.where(
                (block_x == last) & flipped[face],
                westward(value1, turned),
                westward(value1, straight),
            ),
            jnp.where(
                (block_x == 0) & flipped[1 - face],
                eastward(value0, turned),
                eastward(value0, straight),
            ),
        )

    halo0, halo1 = across(strip0, strip1, same)
    far0, far1 = across(far0, far1, next_pair)
    from_next = swapped(to_next, next_pair)
    own, hot = call(
        own_kernel,
        [(vmem, x) for x in (stored, slot_of, lanes)],
        [((ROWS, MID), f32), ((MID, ELEMENTS), bf16)],
        10**8,
        name="own",
    )
    (to_pair,) = call(
        corners_kernel,
        [(vmem, x) for x in (halo1, halo0, to_pair, table, weight, hot)],
        [((HALF_ROWS + 2 * CORNER_ROWS, LANES), f32)],
        10**8,
        scratch=scratch,
        name="corners",
    )
    from_pair = swapped(to_pair, in_pair)
    tile = ((ALL_ROWS, LANES), f32)
    low, centre, high = call(
        functools.partial(middle_kernel, block_cols),
        [(smem, seam_rows)] + [(vmem, x) for x in (halo0, halo1, own, lanes)],
        [tile, tile, tile],
        10**8,
        name="middle",
    )
    (far,) = call(
        far_kernel,
        [(vmem, x) for x in (far1, far0, from_next, low)],
        [((2 * CORNER_ROWS, LANES), f32)],
        10**11,
        name="far",
    )
    (stepped,) = call(
        functools.partial(steps_kernel, block_cols),
        [(smem, seam_rows)]
        + [
            (vmem, x)
            for x in (
                from_pair, from_next, far, low, centre, high,
                hot, table, weight, ext, outer,
            )
        ],
        [(fields.shape, f32)],
        10**8,
        scratch=[pltpu.VMEM((EXT // LANES, 3 * NODES, LANES), f32)],
        name="steps",
    )
    return stepped


def solution(mesh):
    return jax.shard_map(
        on_device,
        mesh=mesh,
        in_specs=(
            P(None, None, None, ("face", "blk")),
            P(None, None, ("face", "blk")),
            P(None, None, ("face", "blk")),
            P(None, None, ("face", "blk")),
            P(None, None, ("face", "blk")),
            P(("face", "blk"), None),
            P(),
        ),
        out_specs=P(None, None, None, ("face", "blk")),
        check_vma=False,
    )
```

```python
import functools
import math

import jax
import jax.numpy as jnp
import ml_dtypes
import numpy as np
from jax import lax
from jax.experimental import pallas as pl
from jax.experimental.pallas import tpu as pltpu
from jax.sharding import PartitionSpec as P

BY = 16
GX = 16
GY = 16
NP = 8
NODES = NP * NP
ARRAYS = 7
ROWS = ARRAYS * NODES
MOVED = 6 * NODES
EDGE_ROWS = 4 * NP
ALL_ROWS = ROWS + EDGE_ROWS
HALF_ROWS = (MOVED + NODES // 2 + 2 * NP) // 2
RING = 4
RIM_ROWS = ROWS + 2 * EDGE_ROWS
CORNER_ROWS = (MOVED + NODES // 2 + 4 * NP) // 8
PITCH = GX + 2 * RING
MID = GY * PITCH
LANES = 128
EXT = MID + 2 * LANES
LEAD = LANES - RING * PITCH
ELEMENTS = GX * GY

time_step = 0.03
hyper_coeff = 0.0002

f32 = jnp.float32
bf16 = jnp.bfloat16
i32 = jnp.int32


def legendre_pair(location, degree):
    lower_value = 1.0
    upper_value = location
    for polynomial_order in range(2, degree + 1):
        lower_value, upper_value = (
            upper_value,
            (
                (2 * polynomial_order - 1) * location * upper_value
                - (polynomial_order - 1) * lower_value
            )
            / polynomial_order,
        )
    return (lower_value, upper_value)


def gll_tables(points):
    degree = points - 1
    locations = [-math.cos(math.pi * position / degree) for position in range(points)]
    for iteration in range(100):
        updated = []
        for location in locations:
            lower_value, upper_value = legendre_pair(location, degree)
            updated.append(
                location - (location * upper_value - lower_value) / ((degree + 1) * upper_value)
            )
        locations = updated
    locations[0] = -1.0
    locations[degree] = 1.0
    legendre_at = [legendre_pair(location, degree)[1] for location in locations]
    weights = [2.0 / (degree * (degree + 1) * value * value) for value in legendre_at]
    corner_value = degree * (degree + 1) / 4.0
    derivative = []
    for row_index in range(points):
        row_values = []
        for column_index in range(points):
            if row_index != column_index:
                row_values.append(
                    legendre_at[row_index]
                    / (legendre_at[column_index] * (locations[row_index] - locations[column_index]))
                )
            elif row_index == 0:
                row_values.append(-corner_value)
            elif row_index == degree:
                row_values.append(corner_value)
            else:
                row_values.append(0.0)
        derivative.append(row_values)
    return np.asarray(weights, np.float64), np.asarray(derivative, np.float64)


def in_three(matrix):
    high = matrix.astype(ml_dtypes.bfloat16)
    low = (matrix - high.astype(np.float64)).astype(ml_dtypes.bfloat16)
    return np.concatenate([high, high, low], 1)


def operator_table():
    weights, derivative = gll_tables(NP)
    eye = np.eye(NP)
    node_weight = np.outer(weights, weights).reshape(NODES, 1)
    along_x = node_weight * np.kron(derivative, eye)
    along_y = node_weight * np.kron(eye, derivative)
    second = derivative @ derivative
    both = node_weight * (np.kron(second, eye) + np.kron(eye, second))
    table = np.zeros((5 * NODES, 4 * NODES), ml_dtypes.bfloat16)
    table[:NODES, : 3 * NODES] = in_three(along_x)
    table[NODES : 2 * NODES, : 3 * NODES] = in_three(along_y)
    flux = [in_three(along_x), in_three(along_y)]
    for k, part in enumerate(flux):
        at = 2 * k * NODES
        table[2 * NODES : 3 * NODES, at : at + 2 * NODES] = part[:, : 2 * NODES]
        table[3 * NODES : 4 * NODES, at : at + NODES] = part[:, 2 * NODES :]
    table[4 * NODES :, : 3 * NODES] = in_three(both)
    spread = np.broadcast_to(node_weight, (NODES, LANES)).astype(np.float32)
    return table.astype(np.float32), np.ascontiguousarray(spread)


def lane_tables():
    table = np.zeros((24, MID), np.int32)
    for lane in range(MID):
        row, col = divmod(lane, PITCH)
        x = col - RING
        own = 0 <= x < GX
        table[0:8, lane] = x * GY + row if own else -1
        if not own:
            table[8:16, lane] = row * RING + (col if x < 0 else x - GX)
        table[16:24, lane] = 0 if own else (1 if x < 0 else 2)
    ext = np.zeros((8, EXT), np.int32)
    outer = np.zeros((24, 2 * LANES), np.int32)
    for lane in range(EXT):
        row, col = divmod(lane - LEAD, PITCH)
        y = row - RING
        x = col - RING
        inside = 0 <= row < GY + 2 * RING
        ext[0, lane] = x in (-RING, GX + RING - 1)
        ext[1, lane] = y == GY - 1
        ext[2, lane] = y == 0
        ext[3, lane] = 0 <= y < GY and 0 <= x < GX
        ext[4, lane] = y == -RING
        ext[5, lane] = y == GY + RING - 1
        if inside and not 0 <= y < GY:
            place = lane if y < 0 else lane - LANES - MID + LANES
            step = y + RING if y < 0 else y - GY
            if 0 <= x < GX:
                outer[0:8, place] = step * GX + x
                outer[8:16, place] = 1
            else:
                outer[0:8, place] = LANES + step * RING + (x + RING if x < 0 else x - GX)
                outer[8:16, place] = 2 if x < 0 else 3
            outer[16:24, place] = y > 0
    whole = np.zeros((56, EXT), np.int32)
    whole[0:24, :MID] = table
    whole[24:32] = ext
    whole[32:56, : 2 * LANES] = outer
    return whole


def dot(a, b):
    return jnp.dot(a, b, preferred_element_type=f32)


def picked(values, one_hot):
    high = values.astype(bf16)
    low = (values - high.astype(f32)).astype(bf16)
    return dot(high, one_hot) + dot(low, one_hot)


def as_one_hot(row_of_lane, depth):
    index = lax.broadcasted_iota(i32, (depth, row_of_lane.shape[1]), 0)
    return jnp.where(index == row_of_lane[0:1], 1.0, 0.0).astype(bf16)


def high_low_high(values):
    high = values.astype(bf16)
    low = (values - high.astype(f32)).astype(bf16)
    return [high, low, high]


def by_slot(slot_ref, cell_of_lane):
    slots = jnp.broadcast_to(slot_ref[...], (8, ELEMENTS)).astype(f32).astype(bf16)
    chosen = dot(slots, as_one_hot(cell_of_lane, ELEMENTS))
    chosen = jnp.where(cell_of_lane >= 0, chosen, -1.0)
    index = lax.broadcasted_iota(i32, (ELEMENTS, cell_of_lane.shape[1]), 0).astype(f32)
    return jnp.where(index == chosen[0:1], 1.0, 0.0).astype(bf16)


def stored_rows(fields_ref, others):
    fields = fields_ref[...].reshape(3 * NODES, ELEMENTS)
    others = [ref[...].reshape(NODES, ELEMENTS) for ref in others]
    return jnp.concatenate([fields[:NODES] - others[-1], fields[NODES:]] + others, 0)


def mass_tendency(table, p, u, v, area_depth, weighted_area, spin):
    slopes = dot(table[: 2 * NODES, : 3 * NODES], jnp.concatenate(high_low_high(p), 0))
    flux = high_low_high(area_depth * u)[:2] + high_low_high(area_depth * v)[:2]
    spread = dot(table[2 * NODES : 4 * NODES], jnp.concatenate(flux, 0))
    return [
        -(spread[:NODES] + spread[NODES:]),
        spin * v - weighted_area * slopes[:NODES],
        -spin * u - weighted_area * slopes[NODES:],
    ]


def edge_values(table_ref, weight_ref, p, u, v, area, depth, spin):
    root = jnp.sqrt(area)
    mass = jnp.concatenate([weight_ref[...]] * (area.shape[1] // LANES), 1) * area
    table = table_ref[...].astype(bf16)
    return mass_tendency(table, p, u, v, root * depth, root, mass * spin) + [mass]


def row_edges(sums):
    return tuple(sums[0, pl.ds(j, EDGE_ROWS, stride=NP)] for j in (NP - 1, 0))


def beside(left, right):
    return jnp.concatenate([left, right], 1)


def one_of_four(parts, index):
    out = parts[0]
    for k in range(1, 4):
        out = jnp.where(index == k, parts[k], out)
    return out


def folded(tide, kept, late, step):
    half = NODES // 2
    back = pltpu.roll(tide[half:], LANES - step, 1)
    onward = pltpu.roll(tide[half:], step, 1)
    return jnp.where(kept, tide[:half], jnp.where(late, back, onward))


def unfolded(rows, late, step):
    back = pltpu.roll(rows, LANES - step, 1)
    onward = pltpu.roll(rows, step, 1)
    return jnp.concatenate([rows, jnp.where(late, onward, back)], 0)


def strip_rows(parts, late, shift, rims):
    lane = lax.broadcasted_iota(i32, (1, LANES), 1)
    index = (lane >> shift) & 3
    kept = jnp.where(late, index // 2, 1 - index // 2) != 0
    tide = folded(parts[6], kept, late, 2 << shift)
    rim = one_of_four(rims, index)
    return jnp.concatenate(parts[:6] + [tide, rim, jnp.zeros_like(rim)], 0)


def placed_rows(whole, late, shift):
    half = NODES // 2
    tide = unfolded(whole[MOVED : MOVED + half], late, 2 << shift)
    rim = whole[MOVED + half : MOVED + half + NP]
    return jnp.concatenate([whole[:MOVED], tide] + spread_out(rim, late, shift), 0)


def spread_out(rim, late, shift):
    parts = []
    for k in range(4):
        first = pltpu.roll(rim, (LANES - (k << shift)) % LANES, 1) if k else rim
        last = pltpu.roll(rim, (3 - k) << shift, 1) if k < 3 else rim
        parts.append(jnp.where(late, first, last))
    return parts


def with_row_rim(whole, sums, top):
    north, south = row_edges(sums)
    rim = jnp.where(top, pltpu.roll(north, RING, 1), pltpu.roll(south, LANES - RING, 1))
    parts = [rim[k * NP : (k + 1) * NP] for k in range(4)]
    lane = lax.broadcasted_iota(i32, (1, LANES), 1)
    spots = []
    for k, part in enumerate(parts):
        first = pltpu.roll(part, k * RING, 1) if k else part
        last = pltpu.roll(part, (LANES - (3 - k) * RING) % LANES, 1) if k < 3 else part
        spots.append(jnp.where(top, first, last))
    rim = one_of_four(spots, (lane >> 2) & 3)
    return jnp.concatenate([whole[: MOVED + NODES // 2 + NP], rim], 0)


def corner_of(whole, start, top):
    lane = lax.broadcasted_iota(i32, (1, LANES), 1)
    base = LANES - start - jnp.where(top != 0, 48, 0)
    whole = jnp.concatenate([whole, jnp.zeros((8 * CORNER_ROWS - whole.shape[0], LANES), f32)], 0)
    out = None
    for k in range(8):
        part = whole[k * CORNER_ROWS : (k + 1) * CORNER_ROWS]
        part = pltpu.roll(part, (base + 16 * k) & (LANES - 1), 1)
        out = part if k == 0 else jnp.where(lane >= 16 * k, part, out)
    return out


def packed(whole):
    second = lax.broadcasted_iota(i32, (1, LANES), 1) >= 64
    top, bottom = whole[:HALF_ROWS], whole[HALF_ROWS:]
    return (
        jnp.where(second, pltpu.roll(bottom, 64, 1), top),
        jnp.where(second, bottom, pltpu.roll(top, 64, 1)),
    )


def unpacked(in0, in1):
    second = lax.broadcasted_iota(i32, (1, LANES), 1) >= 64
    top = jnp.where(second, pltpu.roll(in1, 64, 1), in0)
    bottom = jnp.where(second, in1, pltpu.roll(in0, 64, 1))
    return jnp.concatenate([top, bottom], 0)


def seam_flags(seam_ref, block_cols):
    size_y = seam_ref.shape[1]
    face = lax.axis_index("face")
    blk = lax.axis_index("blk")
    block_x = blk // BY

    def flipped(k):
        return jnp.where(lax.rem(seam_ref[k, 1] - seam_ref[k, 0] + size_y, size_y) != 1, 1, 0)

    first, second = flipped(0), flipped(1)
    east_flip = jnp.where(face == 0, first, second)
    west_flip = jnp.where(face == 0, second, first)
    if block_cols == 1:
        return 1 - east_flip, 0, east_flip, 1
    at_east = jnp.where(block_x == block_cols - 1, east_flip, 0)
    at_west = jnp.where(block_x == 0, west_flip, 0)
    return 1, at_east, 0, at_west


def strips_kernel(block_cols, *refs):
    sources, (out1_ref, out0_ref, stored_ref) = refs[:9], refs[9:12]
    buffers, sems = refs[12:21], refs[21]
    copies = [
        pltpu.make_async_copy(source, buffer, sems.at[k])
        for k, (source, buffer) in enumerate(zip(sources, buffers))
    ]
    for copy in copies:
        copy.start()
    seam_ref, slot_ref, fields_ref, area_ref, depth_ref, spin_ref, tide_ref = buffers[:7]
    table_ref, weight_ref = buffers[7:]
    for copy in copies[:2]:
        copy.wait()
    east0, flip0, east1, flip1 = seam_flags(seam_ref, block_cols)
    lane = lax.broadcasted_iota(i32, (8, 2 * LANES), 1)
    second = (lane & 64) != 0
    place = lane & 63
    row = place >> 2
    row = jnp.where(jnp.where(second, flip1, flip0) != 0, GY - 1 - row, row)
    east = jnp.where(second, east1, east0) != 0
    col = jnp.where(east, GX - RING, 0) + (place & 3)
    col = jnp.where(lane >= LANES, jnp.where(east, GX - RING - 1, RING), col)
    one_hot = by_slot(slot_ref, col * GY + row)
    for copy in copies[2:7]:
        copy.wait()
    stored = stored_rows(fields_ref, (area_ref, depth_ref, spin_ref, tide_ref))
    both = picked(stored, one_hot)

    lane = lax.broadcasted_iota(i32, (1, LANES), 1)
    second = lane >= 64
    flip = jnp.where(second, flip1, flip0) != 0
    sign = jnp.where(flip, -1.0, 1.0)
    node = lax.broadcasted_iota(i32, (1, NP, 1), 1)

    def in_frame(values):
        shaped = values.reshape(-1, NP, LANES)
        turned = pltpu.roll(shaped, 4, 1)
        turned = jnp.where((node & 2) == 0, pltpu.roll(turned, 6, 1), pltpu.roll(turned, 2, 1))
        turned = jnp.where((node & 1) == 0, pltpu.roll(turned, 7, 1), pltpu.roll(turned, 1, 1))
        values = jnp.where(flip[None], turned, shaped).reshape(values.shape)
        parts = [values[k * NODES : (k + 1) * NODES] for k in range(ARRAYS)]
        parts[2] = parts[2] * sign
        parts[5] = parts[5] * sign
        return parts

    strip, ring = in_frame(both[:, :LANES]), in_frame(both[:, LANES:])
    for copy in copies[7:]:
        copy.wait()
    edges = edge_values(table_ref, weight_ref, *ring[:6])
    east = jnp.where(second, east1, east0) != 0
    ends = [jnp.where(east, part[NODES - NP :], part[:NP]) for part in edges]
    out0_ref[...], out1_ref[...] = packed(strip_rows(strip, east, 0, ends))
    stored_ref[...] = stored


def rows_kernel(
    block_cols, seam_ref, stored_ref, strip1_ref, strip0_ref, slot_ref, table_ref, weight_ref,
    next_ref, far0_ref, far1_ref, pair_ref, sums,
):
    east0, flip0, east1, flip1 = seam_flags(seam_ref, block_cols)
    odd = lax.axis_index("blk") & 1

    def goes_up(lane):
        return jnp.where((lane & 64) != 0, odd, 1 - odd) != 0

    lane = lax.broadcasted_iota(i32, (8, 2 * LANES), 1)
    up = goes_up(lane)
    row = jnp.where(up, GY - RING, 0) + ((lane & 63) >> 4)
    row = jnp.where(lane >= LANES, jnp.where(up, GY - RING - 1, RING), row)
    both = picked(stored_ref[...], by_slot(slot_ref, (lane & 15) * GY + row))
    rows, behind = (
        [part[k * NODES : (k + 1) * NODES] for k in range(ARRAYS)]
        for part in (both[:, :LANES], both[:, LANES:])
    )
    whole = unpacked(strip0_ref[...], strip1_ref[...])
    strip = [whole[k * NODES : (k + 1) * NODES] for k in range(6)]
    edges = edge_values(table_ref, weight_ref, *map(beside, strip, behind[:6]))
    sums[0] = jnp.concatenate([part[:, :LANES] for part in edges], 0)
    lane = lax.broadcasted_iota(i32, (1, LANES), 1)
    top0, top1 = odd ^ flip0, odd ^ flip1
    whole = with_row_rim(whole, sums, jnp.where(lane >= 64, top1, top0) != 0)
    far0_ref[...] = corner_of(whole, 0, top0)
    far1_ref[...] = corner_of(whole, 64, top1)
    sums[0] = jnp.concatenate([part[:, LANES:] for part in edges], 0)
    up = goes_up(lane)
    rim = jnp.where(up, *row_edges(sums))
    rim = [rim[k * NP : (k + 1) * NP] for k in range(4)]
    pair_ref[...], next_ref[...] = packed(strip_rows(rows, up, 4, rim))


def corners_kernel(in1_ref, in0_ref, pair_ref, table_ref, weight_ref, *refs):
    out_ref, sums = refs[-2:]
    top = 1 - (lax.axis_index("blk") & 1)
    whole = unpacked(in0_ref[...], in1_ref[...])
    parts = [whole[k * NODES : (k + 1) * NODES] for k in range(6)]
    sums[0] = jnp.concatenate(edge_values(table_ref, weight_ref, *parts), 0)
    whole = with_row_rim(whole, sums, jnp.broadcast_to(top != 0, (1, LANES)))
    out_ref[:HALF_ROWS] = pair_ref[...]
    out_ref[HALF_ROWS : HALF_ROWS + CORNER_ROWS] = corner_of(whole, 0, top)
    out_ref[HALF_ROWS + CORNER_ROWS :] = corner_of(whole, 64, top)


def own_kernel(stored_ref, slot_ref, lanes_ref, own_ref, hot_ref):
    one_hot = by_slot(slot_ref, lanes_ref[0:8, :MID])
    own_ref[...] = picked(stored_ref[...], one_hot)
    hot_ref[...] = one_hot.astype(f32).T.astype(bf16)


def first_sums(table, weight, parts, rims, at_rim):
    p, u, v, area, depth, spin, tide = parts
    size = area.shape[1]
    root = jnp.sqrt(area)
    mass = jnp.concatenate([weight] * (size // LANES), 1) * area
    used = [p, u, v, root * depth, root, mass * spin, tide]
    for part, rim in zip(mass_tendency(table, p, u, v, *used[3:6]) + [mass], rims):
        west, east = part[:NP], part[NODES - NP :]
        at_east = jnp.where(at_rim, rim, pltpu.roll(west, size - 1, 1))
        at_west = jnp.where(at_rim, rim, pltpu.roll(east, 1, 1))
        used.append(
            jnp.concatenate([west + at_west, part[NP : NODES - NP], east + at_east], 0)
        )
    return used


def middle_kernel(
    block_cols, seam_ref, in0_ref, in1_ref, own_ref, lanes_ref, table_ref, weight_ref,
    low_ref, centre_ref, high_ref,
):
    east0, flip0, east1, flip1 = seam_flags(seam_ref, block_cols)
    second = lax.broadcasted_iota(i32, (1, LANES), 1) >= 64
    late = jnp.where(second, east1, east0) == 0
    whole = placed_rows(unpacked(in0_ref[...], in1_ref[...]), late, 0)
    side = lanes_ref[16:24, :MID]
    first_at = jnp.where(side == 2, 64 * (1 - east0), 64 * east0)
    place = jnp.where(side == 0, -1, lanes_ref[8:16, :MID] + first_at)
    placed = picked(whole, as_one_hot(place, LANES))
    parts = [
        placed[k * NODES : (k + 1) * NODES] + own_ref[k * NODES : (k + 1) * NODES]
        for k in range(ARRAYS)
    ]
    rims = [placed[ROWS + c * NP : ROWS + (c + 1) * NP] for c in range(4)]
    at_rim = lanes_ref[24:25, LANES : LANES + MID] != 0
    used = first_sums(table_ref[...].astype(bf16), weight_ref[...], parts, rims, at_rim)
    for k, ref in enumerate((low_ref, centre_ref, high_ref)):
        for n, part in enumerate(used):
            ref[n * NODES : (n + 1) * NODES] = part[:, k * LANES : (k + 1) * LANES]


def far_kernel(far1_ref, far0_ref, *refs):
    out_ref = refs[-1]
    out_ref[:CORNER_ROWS] = far0_ref[...]
    out_ref[CORNER_ROWS:] = far1_ref[...]


def steps_kernel(
    block_cols, seam_ref, pair_ref, next_ref, far_ref, low_ref, centre_ref,
    high_ref, hot_ref, table_ref, weight_ref, lanes_ref, out_ref, sums, leaving, sems,
):
    east0, flip0, east1, flip1 = seam_flags(seam_ref, block_cols)
    odd = lax.axis_index("blk") & 1
    block_y = lax.rem(lax.axis_index("blk"), BY)

    lane = lax.broadcasted_iota(i32, (1, LANES), 1)
    pair = pair_ref[...]
    late = jnp.where(lane < 64, odd, 1 - odd) != 0
    strips = placed_rows(unpacked(pair[:HALF_ROWS], next_ref[...]), late, 4)
    strips = jnp.concatenate(
        [strips[:ROWS], jnp.zeros((EDGE_ROWS, LANES), f32), strips[ROWS:]], 0
    )
    near = pair[HALF_ROWS:]
    far = far_ref[...]
    sources = (near[:CORNER_ROWS], near[CORNER_ROWS:], far[:CORNER_ROWS], far[CORNER_ROWS:])
    corners = []
    for k in range(8):
        rows = None
        for n, source in enumerate(sources):
            shift = 16 * (n - k) % LANES
            part = pltpu.roll(source, shift, 1) if shift else source
            rows = part if n == 0 else jnp.where(lane >= 16 * n, part, rows)
        corners.append(rows)
    corners = jnp.concatenate(corners, 0)
    rim = MOVED + NODES // 2 + NP
    late = jnp.where((lane & 16) != 0, east1, east0) == 0
    below = jnp.where((lane & 32) != 0, 1 - odd, odd) != 0
    corners = jnp.concatenate(
        [placed_rows(corners, late, 0)] + spread_out(corners[rim : rim + NP], below, 2), 0
    )
    around = jnp.concatenate([strips, corners], 1)
    kind = lanes_ref[40:48, : 2 * LANES]
    sender = jnp.where(lanes_ref[48:56, : 2 * LANES] != 0, odd, 1 - odd)
    strip_at = jnp.where(kind == 3, 16 * (1 - east0), 16 * east0)
    place = lanes_ref[32:40, : 2 * LANES]
    place = place + jnp.where(kind == 1, 64 * sender, 32 * sender + strip_at)
    outer = picked(around, as_one_hot(jnp.where(kind == 0, -1, place), 2 * LANES))
    table = table_ref[...].astype(bf16)
    tiles = (None, low_ref, centre_ref, high_ref, None)
    count = len(tiles)
    masks = [lanes_ref[24:32, k * LANES : (k + 1) * LANES] for k in range(count)]
    closed_above = jnp.where(block_y == BY - 1, masks[-2][1:2], 0) != 0
    closed_below = jnp.where(block_y == 0, masks[1][2:3], 0) != 0
    first_row = masks[0][4:5] != 0
    last_row = masks[-1][5:6] != 0
    outer_used = first_sums(
        table,
        weight_ref[...],
        [outer[k * NODES : (k + 1) * NODES] for k in range(ARRAYS)],
        [outer[ROWS + c * NP : ROWS + (c + 1) * NP] for c in range(4)],
        beside(masks[0][0:1], masks[-1][0:1]) != 0,
    )

    def shifted(parts, by, ring):
        turned = [pltpu.roll(part, -by % LANES, 1) for part in parts]
        size = len(parts)
        step = 1 if by > 0 else -1
        others = [(k + step) % size if ring else min(max(k + step, 0), size - 1) for k in range(size)]
        from_other = lane >= LANES - by if by > 0 else lane < -by
        return [jnp.where(from_other, turned[others[k]], turned[k]) for k in range(size)]

    def edge_x(components, slots):
        ring = len(slots) < count
        for c in range(components):
            west_at = slice(c * NODES, c * NODES + NP)
            east_at = slice((c + 1) * NODES - NP, (c + 1) * NODES)
            west = [sums[k, west_at] for k in slots]
            east = [sums[k, east_at] for k in slots]
            at_east, at_west = shifted(west, 1, ring), shifted(east, -1, ring)
            for n, k in enumerate(slots):
                sums[k, west_at] = west[n] + at_west[n]
                sums[k, east_at] = east[n] + at_east[n]

    def edge_y(components, slots, rows=None):
        ring = len(slots) < count
        south_at = pl.ds(0, components * NP, stride=NP)
        north_at = pl.ds(NP - 1, components * NP, stride=NP)
        south = [sums[k, south_at] for k in slots]
        north = [sums[k, north_at] for k in slots]
        at_north, at_south = shifted(south, PITCH, ring), shifted(north, -PITCH, ring)
        for n, k in enumerate(slots):
            if k == count - 2:
                at_north[n] = jnp.where(closed_above, 0.0, at_north[n])
            if k == 1:
                at_south[n] = jnp.where(closed_below, 0.0, at_south[n])
        if rows is not None:
            at_south[0] = jnp.where(first_row, rows[0], at_south[0])
            at_north[-1] = jnp.where(last_row, rows[1], at_north[-1])
        for n, k in enumerate(slots):
            sums[k, south_at] = south[n] + at_south[n]
            sums[k, north_at] = north[n] + at_north[n]

    def edge_sum(slots):
        edge_x(3, slots)
        edge_y(3, slots)

    node = lax.broadcasted_iota(i32, (1, NP, 1), 1)
    rows = []
    for rim in (outer[ALL_ROWS:, :LANES], outer[ALL_ROWS:, LANES:]):
        east = pltpu.roll(rim, LANES - 1, 1).reshape(4, NP, LANES)
        west = pltpu.roll(rim, 1, 1).reshape(4, NP, LANES)
        rim = (
            rim.reshape(4, NP, LANES)
            + jnp.where(node == NP - 1, pltpu.roll(east, NP - 1, 1), 0.0)
            + jnp.where(node == 0, pltpu.roll(west, 1, 1), 0.0)
        )
        rows.append(rim.reshape(EDGE_ROWS, LANES))

    every = tuple(range(count))
    groups = (every[0:2], every[2:4], every[4:])

    def tile_part(k, n):
        if tiles[k] is None:
            return outer_used[n][:, :LANES] if k == 0 else outer_used[n][:, LANES:]
        return tiles[k][n * NODES : (n + 1) * NODES]

    def part_of(group, n):
        return jnp.concatenate([tile_part(k, n) for k in group], 1)

    def put(group, parts):
        for c, part in enumerate(parts):
            for n, k in enumerate(group):
                sums[k, c * NODES : (c + 1) * NODES] = part[:, n * LANES : (n + 1) * LANES]

    def summed(group, c):
        return jnp.concatenate([sums[k, c * NODES : (c + 1) * NODES] for k in group], 1)

    def average(group, per_mass):
        return [summed(group, c) * per_mass for c in range(3)]

    def laplace(s):
        return [
            dot(table[4 * NODES :, : 3 * NODES], jnp.concatenate(high_low_high(part), 0))
            for part in s
        ]

    start = [[part_of(group, n) for n in range(3)] for group in groups]
    fixed = [[part_of(group, n) for n in range(3, 6)] for group in groups]
    for k in every:
        put((k,), [tile_part(k, n) for n in range(7, 11)])
    edge_y(4, every, rows)
    per_mass = [1.0 / summed(group, 3) for group in groups]
    one = []
    for n, group in enumerate(groups):
        change = average(group, per_mass[n])
        one.append([s + time_step * c for s, c in zip(start[n], change)])
        put(group, mass_tendency(table, *one[n], *fixed[n]))
    edge_sum(every)
    two = []
    for n, group in enumerate(groups):
        change = average(group, per_mass[n])
        two.append(
            [0.75 * s + 0.25 * (o + time_step * c) for s, o, c in zip(start[n], one[n], change)]
        )
        put(group, mass_tendency(table, *two[n], *fixed[n]))
    edge_sum(every)

    def regrouped(per_group):
        (outer_low, high_above) = per_group[0], per_group[1]
        below, low = outer_low[:, :LANES], outer_low[:, LANES:]
        centre, high = high_above[:, :LANES], high_above[:, LANES:]
        near = jnp.where(lane < LANES // 2, per_group[2], below)
        return [beside(low, centre), beside(high, near)]

    def of_groups(values):
        return [list(parts) for parts in zip(*(regrouped(part) for part in zip(*values)))]

    for c in range(3):
        rows_at = slice(c * NODES, (c + 1) * NODES)
        sums[count - 1, rows_at] = jnp.where(
            lane < LANES // 2, sums[count - 1, rows_at], sums[0, rows_at]
        )
    slots = every[1:]
    groups = (slots[0:2], slots[2:4])
    start, two = of_groups(start), of_groups(two)
    tide = regrouped([part_of(every[0:2], 6), part_of(every[2:4], 6), part_of(every[4:], 6)])
    per_mass = regrouped(per_mass)
    three = []
    for n, group in enumerate(groups):
        change = average(group, per_mass[n])
        now = [
            s / 3.0 + 2.0 / 3.0 * (o + time_step * c)
            for s, o, c in zip(start[n], two[n], change)
        ]
        now[0] = now[0] + tide[n]
        three.append(now)
        put(group, laplace(now))
    edge_sum(slots)
    for n, group in enumerate(groups):
        put(group, laplace(average(group, per_mass[n])))
    edge_sum(slots)
    own = lanes_ref[27:28, LANES : LANES + MID] != 0
    hot = hot_ref[...]
    change = [average(group, per_mass[n]) for n, group in enumerate(groups)]
    copies = []
    for c in range(3):
        now = [s[c] - time_step * hyper_coeff * b[c] for s, b in zip(three, change)]
        stepped = jnp.concatenate(now, 1)[:, :MID]
        stored = picked(jnp.where(own, stepped, 0.0), hot)
        leaving[c] = stored.reshape(leaving.shape[1:])
        copies.append(pltpu.make_async_copy(leaving.at[c], out_ref.at[c], sems.at[c]))
        copies[c].start()
    for copy in copies:
        copy.wait()


def on_device(fields, jacobian, water_depth, coriolis, tide_height, slot_of, seam_rows):
    block_cols = lax.axis_size("blk") // BY
    table, weight = operator_table()
    table, weight, lanes = map(jnp.asarray, (table, weight, lane_tables()))
    vmem = pl.BlockSpec(memory_space=pltpu.VMEM)
    smem = pl.BlockSpec(memory_space=pltpu.SMEM)
    hbm = pl.BlockSpec(memory_space=pltpu.HBM)
    params = pltpu.CompilerParams(vmem_limit_bytes=48 * 2**20)
    held = (fields, jacobian, water_depth, coriolis, tide_height)

    def call(kernel, ins, outs, cost, scratch=(), name=None, out_specs=None):
        return pl.pallas_call(
            kernel,
            out_shape=[jax.ShapeDtypeStruct(*out) for out in outs],
            in_specs=[spec for spec, value in ins],
            out_specs=out_specs or [vmem] * len(outs),
            scratch_shapes=list(scratch),
            compiler_params=params,
            cost_estimate=pl.CostEstimate(
                flops=cost, bytes_accessed=2 * 2**20, transcendentals=0
            ),
            name=name,
        )(
            *[
                pltpu.with_memory_space_constraint(value, pltpu.HBM) if spec is hbm else value
                for spec, value in ins
            ]
        )

    strip = ((HALF_ROWS, LANES), f32)
    def room(values, spaces=None):
        spaces = spaces or [pltpu.VMEM] * len(values)
        buffers = [space(x.shape, x.dtype) for space, x in zip(spaces, values)]
        return buffers + [pltpu.SemaphoreType.DMA((len(values),))]

    needed = (seam_rows, slot_of, *held, table, weight)
    corner = ((CORNER_ROWS, LANES), f32)
    scratch = [pltpu.VMEM((1, 4 * NODES, LANES), f32)]
    strip1, strip0, stored = call(
        functools.partial(strips_kernel, block_cols),
        [(hbm, x) for x in needed],
        [strip, strip, ((ROWS, ELEMENTS), f32)],
        10**8,
        scratch=room(needed, [pltpu.SMEM] + [pltpu.VMEM] * (len(needed) - 1)),
        name="strips",
    )
    to_next, far0, far1, to_pair = call(
        functools.partial(rows_kernel, block_cols),
        [(smem, seam_rows)]
        + [(vmem, x) for x in (stored, strip1, strip0, slot_of, table, weight)],
        [strip, corner, corner, strip],
        10**8,
        scratch=scratch,
        name="rows",
    )
    span = block_cols * BY
    both = ("face", "blk")
    places = [(f, x, y) for f in range(2) for x in range(block_cols) for y in range(BY)]

    def rank(face, block_x, block_y):
        return face * span + block_x * BY + block_y

    def same(y):
        return y

    def in_pair(y):
        return y ^ 1

    def next_pair(y):
        other = y + 1 if y % 2 else y - 1
        return other if 0 <= other < BY else y

    def swapped(value, partner):
        pairs = [
            (rank(f, x, y), rank(f if partner(y) != y else 1 - f, x, partner(y)))
            for f, x, y in places
        ]
        return lax.ppermute(value, both, pairs)

    def across(value0, value1, partner):
        last = block_cols - 1

        def aligned(y):
            return partner is same or partner(y) != y

        straight = {
            (f, x, y): (f, x + 1, partner(y)) if x < last else (1 - f, 0, partner(y))
            for f, x, y in places
        }
        turned = {
            (f, last, y): (1 - f, 0, BY - 1 - partner(y) if aligned(y) else y)
            for f in range(2)
            for y in range(BY)
        }

        def eastward(value, pairs):
            return lax.ppermute(value, both, [(rank(*a), rank(*b)) for a, b in pairs.items()])

        def westward(value, pairs):
            return lax.ppermute(value, both, [(rank(*b), rank(*a)) for a, b in pairs.items()])

        if block_cols == 1:
            return eastward(value0, straight), eastward(value1, turned)
        flipped = (seam_rows[:, 1] - seam_rows[:, 0]) % seam_rows.shape[1] != 1
        face = lax.axis_index("face")
        block_x = lax.axis_index("blk") // BY
        return (
            jnp.where(
                (block_x == last) & flipped[face],
                westward(value1, turned),
                westward(value1, straight),
            ),
            jnp.where(
                (block_x == 0) & flipped[1 - face],
                eastward(value0, turned),
                eastward(value0, straight),
            ),
        )

    halo0, halo1 = across(strip0, strip1, same)
    far0, far1 = across(far0, far1, next_pair)
    from_next = swapped(to_next, next_pair)
    own, hot = call(
        own_kernel,
        [(vmem, x) for x in (stored, slot_of, lanes)],
        [((ROWS, MID), f32), ((MID, ELEMENTS), bf16)],
        10**8,
        name="own",
    )
    (to_pair,) = call(
        corners_kernel,
        [(vmem, x) for x in (halo1, halo0, to_pair, table, weight, hot)],
        [((HALF_ROWS + 2 * CORNER_ROWS, LANES), f32)],
        10**8,
        scratch=scratch,
        name="corners",
    )
    from_pair = swapped(to_pair, in_pair)
    tile = ((11 * NODES, LANES), f32)
    low, centre, high = call(
        functools.partial(middle_kernel, block_cols),
        [(smem, seam_rows)] + [(vmem, x) for x in (halo0, halo1, own, lanes, table, weight)],
        [tile, tile, tile],
        10**8,
        name="middle",
    )
    (far,) = call(
        far_kernel,
        [(vmem, x) for x in (far1, far0, from_next, low)],
        [((2 * CORNER_ROWS, LANES), f32)],
        10**11,
        name="far",
    )
    (stepped,) = call(
        functools.partial(steps_kernel, block_cols),
        [(smem, seam_rows)]
        + [
            (vmem, x)
            for x in (
                from_pair, from_next, far, low, centre, high,
                hot, table, weight, lanes,
            )
        ],
        [(fields.shape, f32)],
        10**8,
        scratch=[
            pltpu.VMEM((EXT // LANES, 4 * NODES, LANES), f32),
            pltpu.VMEM(fields.shape, f32),
            pltpu.SemaphoreType.DMA((3,)),
        ],
        out_specs=[hbm],
        name="steps",
    )
    return stepped


def solution(mesh):
    return jax.shard_map(
        on_device,
        mesh=mesh,
        in_specs=(
            P(None, None, None, ("face", "blk")),
            P(None, None, ("face", "blk")),
            P(None, None, ("face", "blk")),
            P(None, None, ("face", "blk")),
            P(None, None, ("face", "blk")),
            P(("face", "blk"), None),
            P(),
        ),
        out_specs=P(None, None, None, ("face", "blk")),
        check_vma=False,
    )
```

```python
import functools
import math

import jax
import jax.numpy as jnp
import ml_dtypes
import numpy as np
from jax import lax
from jax.experimental import pallas as pl
from jax.experimental.pallas import tpu as pltpu
from jax.sharding import PartitionSpec as P

BY = 16
GX = 16
GY = 16
NP = 8
NODES = NP * NP
ARRAYS = 7
ROWS = ARRAYS * NODES
MOVED = 6 * NODES
EDGE_ROWS = 4 * NP
ALL_ROWS = ROWS + EDGE_ROWS
HALF_ROWS = (MOVED + NODES // 2 + 2 * NP) // 2
RING = 4
RIM_ROWS = ROWS + 2 * EDGE_ROWS
CORNER_ROWS = (MOVED + NODES // 2 + 4 * NP) // 8
PITCH = GX + 2 * RING
MID = GY * PITCH
LANES = 128
EXT = MID + 2 * LANES
LEAD = LANES - RING * PITCH
ELEMENTS = GX * GY

time_step = 0.03
hyper_coeff = 0.0002

f32 = jnp.float32
bf16 = jnp.bfloat16
i32 = jnp.int32


def legendre_pair(location, degree):
    lower_value = 1.0
    upper_value = location
    for polynomial_order in range(2, degree + 1):
        lower_value, upper_value = (
            upper_value,
            (
                (2 * polynomial_order - 1) * location * upper_value
                - (polynomial_order - 1) * lower_value
            )
            / polynomial_order,
        )
    return (lower_value, upper_value)


def gll_tables(points):
    degree = points - 1
    locations = [-math.cos(math.pi * position / degree) for position in range(points)]
    for iteration in range(100):
        updated = []
        for location in locations:
            lower_value, upper_value = legendre_pair(location, degree)
            updated.append(
                location - (location * upper_value - lower_value) / ((degree + 1) * upper_value)
            )
        locations = updated
    locations[0] = -1.0
    locations[degree] = 1.0
    legendre_at = [legendre_pair(location, degree)[1] for location in locations]
    weights = [2.0 / (degree * (degree + 1) * value * value) for value in legendre_at]
    corner_value = degree * (degree + 1) / 4.0
    derivative = []
    for row_index in range(points):
        row_values = []
        for column_index in range(points):
            if row_index != column_index:
                row_values.append(
                    legendre_at[row_index]
                    / (legendre_at[column_index] * (locations[row_index] - locations[column_index]))
                )
            elif row_index == 0:
                row_values.append(-corner_value)
            elif row_index == degree:
                row_values.append(corner_value)
            else:
                row_values.append(0.0)
        derivative.append(row_values)
    return np.asarray(weights, np.float64), np.asarray(derivative, np.float64)


def in_three(matrix):
    high = matrix.astype(ml_dtypes.bfloat16)
    low = (matrix - high.astype(np.float64)).astype(ml_dtypes.bfloat16)
    return np.concatenate([high, high, low], 1)


def operator_table():
    weights, derivative = gll_tables(NP)
    eye = np.eye(NP)
    node_weight = np.outer(weights, weights).reshape(NODES, 1)
    along_x = node_weight * np.kron(derivative, eye)
    along_y = node_weight * np.kron(eye, derivative)
    second = derivative @ derivative
    both = node_weight * (np.kron(second, eye) + np.kron(eye, second))
    table = np.zeros((5 * NODES, 4 * NODES), ml_dtypes.bfloat16)
    table[:NODES, : 3 * NODES] = in_three(along_x)
    table[NODES : 2 * NODES, : 3 * NODES] = in_three(along_y)
    flux = [in_three(along_x), in_three(along_y)]
    for k, part in enumerate(flux):
        at = 2 * k * NODES
        table[2 * NODES : 3 * NODES, at : at + 2 * NODES] = part[:, : 2 * NODES]
        table[3 * NODES : 4 * NODES, at : at + NODES] = part[:, 2 * NODES :]
    table[4 * NODES :, : 3 * NODES] = in_three(both)
    spread = np.broadcast_to(node_weight, (NODES, LANES)).astype(np.float32)
    return table.astype(np.float32), np.ascontiguousarray(spread)


def lane_tables():
    table = np.zeros((24, MID), np.int32)
    for lane in range(MID):
        row, col = divmod(lane, PITCH)
        x = col - RING
        own = 0 <= x < GX
        table[0:8, lane] = x * GY + row if own else -1
        if not own:
            table[8:16, lane] = row * RING + (col if x < 0 else x - GX)
        table[16:24, lane] = 0 if own else (1 if x < 0 else 2)
    ext = np.zeros((8, EXT), np.int32)
    outer = np.zeros((24, 2 * LANES), np.int32)
    for lane in range(EXT):
        row, col = divmod(lane - LEAD, PITCH)
        y = row - RING
        x = col - RING
        inside = 0 <= row < GY + 2 * RING
        ext[0, lane] = x in (-RING, GX + RING - 1)
        ext[1, lane] = y == GY - 1
        ext[2, lane] = y == 0
        ext[3, lane] = 0 <= y < GY and 0 <= x < GX
        ext[4, lane] = y == -RING
        ext[5, lane] = y == GY + RING - 1
        if inside and not 0 <= y < GY:
            place = lane if y < 0 else lane - LANES - MID + LANES
            step = y + RING if y < 0 else y - GY
            if 0 <= x < GX:
                outer[0:8, place] = step * GX + x
                outer[8:16, place] = 1
            else:
                outer[0:8, place] = LANES + step * RING + (x + RING if x < 0 else x - GX)
                outer[8:16, place] = 2 if x < 0 else 3
            outer[16:24, place] = y > 0
    whole = np.zeros((56, EXT), np.int32)
    whole[0:24, :MID] = table
    whole[24:32] = ext
    whole[32:56, : 2 * LANES] = outer
    return whole


def dot(a, b):
    return jnp.dot(a, b, preferred_element_type=f32)


def picked(values, one_hot):
    high = values.astype(bf16)
    low = (values - high.astype(f32)).astype(bf16)
    both = dot(jnp.concatenate([high, low], 0), one_hot)
    return both[: values.shape[0]] + both[values.shape[0] :]


def as_one_hot(row_of_lane, depth):
    index = lax.broadcasted_iota(i32, (depth, row_of_lane.shape[1]), 0)
    return jnp.where(index == row_of_lane[0:1], 1.0, 0.0).astype(bf16)


def high_low_high(values):
    high = values.astype(bf16)
    low = (values - high.astype(f32)).astype(bf16)
    return [high, low, high]


def by_slot(slot_ref, cell_of_lane):
    slots = jnp.broadcast_to(slot_ref[...], (8, ELEMENTS)).astype(f32).astype(bf16)
    chosen = dot(slots, as_one_hot(cell_of_lane, ELEMENTS))
    chosen = jnp.where(cell_of_lane >= 0, chosen, -1.0)
    index = lax.broadcasted_iota(i32, (ELEMENTS, cell_of_lane.shape[1]), 0).astype(f32)
    return jnp.where(index == chosen[0:1], 1.0, 0.0).astype(bf16)


def stored_rows(fields_ref, others):
    fields = fields_ref[...].reshape(3 * NODES, ELEMENTS)
    others = [ref[...].reshape(NODES, ELEMENTS) for ref in others]
    return jnp.concatenate([fields[:NODES] - others[-1], fields[NODES:]] + others, 0)


def mass_tendency(table, p, u, v, area_depth, weighted_area, spin):
    slopes = dot(table[: 2 * NODES, : 3 * NODES], jnp.concatenate(high_low_high(p), 0))
    flux = high_low_high(area_depth * u)[:2] + high_low_high(area_depth * v)[:2]
    spread = dot(table[2 * NODES : 4 * NODES], jnp.concatenate(flux, 0))
    return [
        -(spread[:NODES] + spread[NODES:]),
        spin * v - weighted_area * slopes[:NODES],
        -spin * u - weighted_area * slopes[NODES:],
    ]


def edge_values(table_ref, weight_ref, p, u, v, area, depth, spin):
    root = jnp.sqrt(area)
    mass = jnp.concatenate([weight_ref[...]] * (area.shape[1] // LANES), 1) * area
    table = table_ref[...].astype(bf16)
    return mass_tendency(table, p, u, v, root * depth, root, mass * spin) + [mass]


def row_edges(sums):
    return tuple(sums[0, pl.ds(j, EDGE_ROWS, stride=NP)] for j in (NP - 1, 0))


def beside(left, right):
    return jnp.concatenate([left, right], 1)


def one_of_four(parts, index):
    out = parts[0]
    for k in range(1, 4):
        out = jnp.where(index == k, parts[k], out)
    return out


def folded(tide, kept, late, step):
    half = NODES // 2
    back = pltpu.roll(tide[half:], LANES - step, 1)
    onward = pltpu.roll(tide[half:], step, 1)
    return jnp.where(kept, tide[:half], jnp.where(late, back, onward))


def unfolded(rows, late, step):
    back = pltpu.roll(rows, LANES - step, 1)
    onward = pltpu.roll(rows, step, 1)
    return jnp.concatenate([rows, jnp.where(late, onward, back)], 0)


def strip_rows(parts, late, shift, rims):
    lane = lax.broadcasted_iota(i32, (1, LANES), 1)
    index = (lane >> shift) & 3
    kept = jnp.where(late, index // 2, 1 - index // 2) != 0
    tide = folded(parts[6], kept, late, 2 << shift)
    rim = one_of_four(rims, index)
    return jnp.concatenate(parts[:6] + [tide, rim, jnp.zeros_like(rim)], 0)


def placed_rows(whole, late, shift):
    half = NODES // 2
    tide = unfolded(whole[MOVED : MOVED + half], late, 2 << shift)
    rim = whole[MOVED + half : MOVED + half + NP]
    return jnp.concatenate([whole[:MOVED], tide] + spread_out(rim, late, shift), 0)


def spread_out(rim, late, shift):
    parts = []
    for k in range(4):
        first = pltpu.roll(rim, (LANES - (k << shift)) % LANES, 1) if k else rim
        last = pltpu.roll(rim, (3 - k) << shift, 1) if k < 3 else rim
        parts.append(jnp.where(late, first, last))
    return parts


def with_row_rim(whole, sums, top):
    north, south = row_edges(sums)
    rim = jnp.where(top, pltpu.roll(north, RING, 1), pltpu.roll(south, LANES - RING, 1))
    parts = [rim[k * NP : (k + 1) * NP] for k in range(4)]
    lane = lax.broadcasted_iota(i32, (1, LANES), 1)
    spots = []
    for k, part in enumerate(parts):
        first = pltpu.roll(part, k * RING, 1) if k else part
        last = pltpu.roll(part, (LANES - (3 - k) * RING) % LANES, 1) if k < 3 else part
        spots.append(jnp.where(top, first, last))
    rim = one_of_four(spots, (lane >> 2) & 3)
    return jnp.concatenate([whole[: MOVED + NODES // 2 + NP], rim], 0)


def corner_of(whole, start, top):
    lane = lax.broadcasted_iota(i32, (1, LANES), 1)
    base = LANES - start - jnp.where(top != 0, 48, 0)
    whole = jnp.concatenate([whole, jnp.zeros((8 * CORNER_ROWS - whole.shape[0], LANES), f32)], 0)
    out = None
    for k in range(8):
        part = whole[k * CORNER_ROWS : (k + 1) * CORNER_ROWS]
        part = pltpu.roll(part, (base + 16 * k) & (LANES - 1), 1)
        out = part if k == 0 else jnp.where(lane >= 16 * k, part, out)
    return out


def packed(whole):
    second = lax.broadcasted_iota(i32, (1, LANES), 1) >= 64
    top, bottom = whole[:HALF_ROWS], whole[HALF_ROWS:]
    return (
        jnp.where(second, pltpu.roll(bottom, 64, 1), top),
        jnp.where(second, bottom, pltpu.roll(top, 64, 1)),
    )


def unpacked(in0, in1):
    second = lax.broadcasted_iota(i32, (1, LANES), 1) >= 64
    top = jnp.where(second, pltpu.roll(in1, 64, 1), in0)
    bottom = jnp.where(second, in1, pltpu.roll(in0, 64, 1))
    return jnp.concatenate([top, bottom], 0)


def seam_flags(seam_ref, block_cols):
    size_y = seam_ref.shape[1]
    face = lax.axis_index("face")
    blk = lax.axis_index("blk")
    block_x = blk // BY

    def flipped(k):
        return jnp.where(lax.rem(seam_ref[k, 1] - seam_ref[k, 0] + size_y, size_y) != 1, 1, 0)

    first, second = flipped(0), flipped(1)
    east_flip = jnp.where(face == 0, first, second)
    west_flip = jnp.where(face == 0, second, first)
    if block_cols == 1:
        return 1 - east_flip, 0, east_flip, 1
    at_east = jnp.where(block_x == block_cols - 1, east_flip, 0)
    at_west = jnp.where(block_x == 0, west_flip, 0)
    return 1, at_east, 0, at_west


def strips_kernel(block_cols, *refs):
    sources, (out1_ref, out0_ref, stored_ref) = refs[:9], refs[9:12]
    buffers, sems = refs[12:21], refs[21]
    copies = [
        pltpu.make_async_copy(source, buffer, sems.at[k])
        for k, (source, buffer) in enumerate(zip(sources, buffers))
    ]
    for copy in copies:
        copy.start()
    seam_ref, slot_ref, fields_ref, area_ref, depth_ref, spin_ref, tide_ref = buffers[:7]
    table_ref, weight_ref = buffers[7:]
    for copy in copies[:2]:
        copy.wait()
    east0, flip0, east1, flip1 = seam_flags(seam_ref, block_cols)
    lane = lax.broadcasted_iota(i32, (8, 2 * LANES), 1)
    second = (lane & 64) != 0
    place = lane & 63
    row = place >> 2
    row = jnp.where(jnp.where(second, flip1, flip0) != 0, GY - 1 - row, row)
    east = jnp.where(second, east1, east0) != 0
    col = jnp.where(east, GX - RING, 0) + (place & 3)
    col = jnp.where(lane >= LANES, jnp.where(east, GX - RING - 1, RING), col)
    one_hot = by_slot(slot_ref, col * GY + row)
    for copy in copies[2:7]:
        copy.wait()
    stored = stored_rows(fields_ref, (area_ref, depth_ref, spin_ref, tide_ref))
    both = picked(stored, one_hot)

    lane = lax.broadcasted_iota(i32, (1, LANES), 1)
    second = lane >= 64
    flip = jnp.where(second, flip1, flip0) != 0
    sign = jnp.where(flip, -1.0, 1.0)
    node = lax.broadcasted_iota(i32, (1, NP, 1), 1)

    def in_frame(values):
        shaped = values.reshape(-1, NP, LANES)
        turned = pltpu.roll(shaped, 4, 1)
        turned = jnp.where((node & 2) == 0, pltpu.roll(turned, 6, 1), pltpu.roll(turned, 2, 1))
        turned = jnp.where((node & 1) == 0, pltpu.roll(turned, 7, 1), pltpu.roll(turned, 1, 1))
        values = jnp.where(flip[None], turned, shaped).reshape(values.shape)
        parts = [values[k * NODES : (k + 1) * NODES] for k in range(ARRAYS)]
        parts[2] = parts[2] * sign
        parts[5] = parts[5] * sign
        return parts

    strip, ring = in_frame(both[:, :LANES]), in_frame(both[:, LANES:])
    for copy in copies[7:]:
        copy.wait()
    edges = edge_values(table_ref, weight_ref, *ring[:6])
    east = jnp.where(second, east1, east0) != 0
    ends = [jnp.where(east, part[NODES - NP :], part[:NP]) for part in edges]
    out0_ref[...], out1_ref[...] = packed(strip_rows(strip, east, 0, ends))
    stored_ref[...] = stored


def rows_kernel(
    block_cols, seam_ref, stored_ref, strip1_ref, strip0_ref, slot_ref, table_ref, weight_ref,
    next_ref, far0_ref, far1_ref, pair_ref, sums,
):
    east0, flip0, east1, flip1 = seam_flags(seam_ref, block_cols)
    odd = lax.axis_index("blk") & 1

    def goes_up(lane):
        return jnp.where((lane & 64) != 0, odd, 1 - odd) != 0

    lane = lax.broadcasted_iota(i32, (8, 2 * LANES), 1)
    up = goes_up(lane)
    row = jnp.where(up, GY - RING, 0) + ((lane & 63) >> 4)
    row = jnp.where(lane >= LANES, jnp.where(up, GY - RING - 1, RING), row)
    both = picked(stored_ref[...], by_slot(slot_ref, (lane & 15) * GY + row))
    rows, behind = (
        [part[k * NODES : (k + 1) * NODES] for k in range(ARRAYS)]
        for part in (both[:, :LANES], both[:, LANES:])
    )
    whole = unpacked(strip0_ref[...], strip1_ref[...])
    strip = [whole[k * NODES : (k + 1) * NODES] for k in range(6)]
    edges = edge_values(table_ref, weight_ref, *map(beside, strip, behind[:6]))
    sums[0] = jnp.concatenate([part[:, :LANES] for part in edges], 0)
    lane = lax.broadcasted_iota(i32, (1, LANES), 1)
    top0, top1 = odd ^ flip0, odd ^ flip1
    whole = with_row_rim(whole, sums, jnp.where(lane >= 64, top1, top0) != 0)
    far0_ref[...] = corner_of(whole, 0, top0)
    far1_ref[...] = corner_of(whole, 64, top1)
    sums[0] = jnp.concatenate([part[:, LANES:] for part in edges], 0)
    up = goes_up(lane)
    rim = jnp.where(up, *row_edges(sums))
    rim = [rim[k * NP : (k + 1) * NP] for k in range(4)]
    pair_ref[...], next_ref[...] = packed(strip_rows(rows, up, 4, rim))


def corners_kernel(in1_ref, in0_ref, pair_ref, table_ref, weight_ref, *refs):
    out_ref, sums = refs[-2:]
    top = 1 - (lax.axis_index("blk") & 1)
    whole = unpacked(in0_ref[...], in1_ref[...])
    parts = [whole[k * NODES : (k + 1) * NODES] for k in range(6)]
    sums[0] = jnp.concatenate(edge_values(table_ref, weight_ref, *parts), 0)
    whole = with_row_rim(whole, sums, jnp.broadcast_to(top != 0, (1, LANES)))
    out_ref[:HALF_ROWS] = pair_ref[...]
    out_ref[HALF_ROWS : HALF_ROWS + CORNER_ROWS] = corner_of(whole, 0, top)
    out_ref[HALF_ROWS + CORNER_ROWS :] = corner_of(whole, 64, top)


def own_kernel(stored_ref, slot_ref, lanes_ref, own_ref, hot_ref):
    one_hot = by_slot(slot_ref, lanes_ref[0:8, :MID])
    own_ref[...] = picked(stored_ref[...], one_hot)
    hot_ref[...] = one_hot.astype(f32).T.astype(bf16)


def first_sums(table, weight, parts, rims, at_rim):
    p, u, v, area, depth, spin, tide = parts
    size = area.shape[1]
    root = jnp.sqrt(area)
    mass = jnp.concatenate([weight] * (size // LANES), 1) * area
    used = [p, u, v, root * depth, root, mass * spin, tide]
    for part, rim in zip(mass_tendency(table, p, u, v, *used[3:6]) + [mass], rims):
        west, east = part[:NP], part[NODES - NP :]
        at_east = jnp.where(at_rim, rim, pltpu.roll(west, size - 1, 1))
        at_west = jnp.where(at_rim, rim, pltpu.roll(east, 1, 1))
        used.append(
            jnp.concatenate([west + at_west, part[NP : NODES - NP], east + at_east], 0)
        )
    return used


def middle_kernel(
    block_cols, seam_ref, in0_ref, in1_ref, own_ref, lanes_ref, table_ref, weight_ref,
    low_ref, centre_ref, high_ref,
):
    east0, flip0, east1, flip1 = seam_flags(seam_ref, block_cols)
    second = lax.broadcasted_iota(i32, (1, LANES), 1) >= 64
    late = jnp.where(second, east1, east0) == 0
    whole = placed_rows(unpacked(in0_ref[...], in1_ref[...]), late, 0)
    side = lanes_ref[16:24, :MID]
    first_at = jnp.where(side == 2, 64 * (1 - east0), 64 * east0)
    place = jnp.where(side == 0, -1, lanes_ref[8:16, :MID] + first_at)
    placed = picked(whole, as_one_hot(place, LANES))
    parts = [
        placed[k * NODES : (k + 1) * NODES] + own_ref[k * NODES : (k + 1) * NODES]
        for k in range(ARRAYS)
    ]
    rims = [placed[ROWS + c * NP : ROWS + (c + 1) * NP] for c in range(4)]
    at_rim = lanes_ref[24:25, LANES : LANES + MID] != 0
    used = first_sums(table_ref[...].astype(bf16), weight_ref[...], parts, rims, at_rim)
    for k, ref in enumerate((low_ref, centre_ref, high_ref)):
        for n, part in enumerate(used):
            ref[n * NODES : (n + 1) * NODES] = part[:, k * LANES : (k + 1) * LANES]


def far_kernel(far1_ref, far0_ref, *refs):
    out_ref = refs[-1]
    out_ref[:CORNER_ROWS] = far0_ref[...]
    out_ref[CORNER_ROWS:] = far1_ref[...]


def steps_kernel(
    block_cols, seam_ref, pair_ref, next_ref, far_ref, low_ref, centre_ref,
    high_ref, hot_ref, table_ref, weight_ref, lanes_ref, out_ref, sums,
):
    east0, flip0, east1, flip1 = seam_flags(seam_ref, block_cols)
    odd = lax.axis_index("blk") & 1
    block_y = lax.rem(lax.axis_index("blk"), BY)

    lane = lax.broadcasted_iota(i32, (1, LANES), 1)
    pair = pair_ref[...]
    late = jnp.where(lane < 64, odd, 1 - odd) != 0
    strips = placed_rows(unpacked(pair[:HALF_ROWS], next_ref[...]), late, 4)
    strips = jnp.concatenate(
        [strips[:ROWS], jnp.zeros((EDGE_ROWS, LANES), f32), strips[ROWS:]], 0
    )
    near = pair[HALF_ROWS:]
    far = far_ref[...]
    sources = (near[:CORNER_ROWS], near[CORNER_ROWS:], far[:CORNER_ROWS], far[CORNER_ROWS:])
    corners = []
    for k in range(8):
        rows = None
        for n, source in enumerate(sources):
            shift = 16 * (n - k) % LANES
            part = pltpu.roll(source, shift, 1) if shift else source
            rows = part if n == 0 else jnp.where(lane >= 16 * n, part, rows)
        corners.append(rows)
    corners = jnp.concatenate(corners, 0)
    rim = MOVED + NODES // 2 + NP
    late = jnp.where((lane & 16) != 0, east1, east0) == 0
    below = jnp.where((lane & 32) != 0, 1 - odd, odd) != 0
    corners = jnp.concatenate(
        [placed_rows(corners, late, 0)] + spread_out(corners[rim : rim + NP], below, 2), 0
    )
    around = jnp.concatenate([strips, corners], 1)
    kind = lanes_ref[40:48, : 2 * LANES]
    sender = jnp.where(lanes_ref[48:56, : 2 * LANES] != 0, odd, 1 - odd)
    strip_at = jnp.where(kind == 3, 16 * (1 - east0), 16 * east0)
    place = lanes_ref[32:40, : 2 * LANES]
    place = place + jnp.where(kind == 1, 64 * sender, 32 * sender + strip_at)
    outer = picked(around, as_one_hot(jnp.where(kind == 0, -1, place), 2 * LANES))
    table = table_ref[...].astype(bf16)
    tiles = (None, low_ref, centre_ref, high_ref, None)
    count = len(tiles)
    masks = [lanes_ref[24:32, k * LANES : (k + 1) * LANES] for k in range(count)]
    closed_above = jnp.where(block_y == BY - 1, masks[-2][1:2], 0) != 0
    closed_below = jnp.where(block_y == 0, masks[1][2:3], 0) != 0
    first_row = masks[0][4:5] != 0
    last_row = masks[-1][5:6] != 0
    outer_used = first_sums(
        table,
        weight_ref[...],
        [outer[k * NODES : (k + 1) * NODES] for k in range(ARRAYS)],
        [outer[ROWS + c * NP : ROWS + (c + 1) * NP] for c in range(4)],
        beside(masks[0][0:1], masks[-1][0:1]) != 0,
    )

    def shifted(parts, by, ring):
        turned = [pltpu.roll(part, -by % LANES, 1) for part in parts]
        size = len(parts)
        step = 1 if by > 0 else -1
        others = [(k + step) % size if ring else min(max(k + step, 0), size - 1) for k in range(size)]
        from_other = lane >= LANES - by if by > 0 else lane < -by
        return [jnp.where(from_other, turned[others[k]], turned[k]) for k in range(size)]

    def put_x_sums(groups, components):
        slots = [k for group in groups for k in group]
        ring = len(slots) < count
        per_tile = [
            [part[:, n * LANES : (n + 1) * LANES] for part in parts]
            for group, parts in zip(groups, components)
            for n in range(len(group))
        ]
        for c in range(3):
            parts = [tile[c] for tile in per_tile]
            west = [part[:NP] for part in parts]
            east = [part[NODES - NP :] for part in parts]
            at_east, at_west = shifted(west, 1, ring), shifted(east, -1, ring)
            for n, k in enumerate(slots):
                sums[k, c * NODES : c * NODES + NP] = west[n] + at_west[n]
                sums[k, c * NODES + NP : (c + 1) * NODES - NP] = parts[n][NP : NODES - NP]
                sums[k, (c + 1) * NODES - NP : (c + 1) * NODES] = east[n] + at_east[n]

    def edge_y(components, slots, rows=None):
        ring = len(slots) < count
        south_at = pl.ds(0, components * NP, stride=NP)
        north_at = pl.ds(NP - 1, components * NP, stride=NP)
        south = [sums[k, south_at] for k in slots]
        north = [sums[k, north_at] for k in slots]
        at_north, at_south = shifted(south, PITCH, ring), shifted(north, -PITCH, ring)
        for n, k in enumerate(slots):
            if k == count - 2:
                at_north[n] = jnp.where(closed_above, 0.0, at_north[n])
            if k == 1:
                at_south[n] = jnp.where(closed_below, 0.0, at_south[n])
        if rows is not None:
            at_south[0] = jnp.where(first_row, rows[0], at_south[0])
            at_north[-1] = jnp.where(last_row, rows[1], at_north[-1])
        for n, k in enumerate(slots):
            sums[k, south_at] = south[n] + at_south[n]
            sums[k, north_at] = north[n] + at_north[n]

    node = lax.broadcasted_iota(i32, (1, NP, 1), 1)
    rows = []
    for rim in (outer[ALL_ROWS:, :LANES], outer[ALL_ROWS:, LANES:]):
        east = pltpu.roll(rim, LANES - 1, 1).reshape(4, NP, LANES)
        west = pltpu.roll(rim, 1, 1).reshape(4, NP, LANES)
        rim = (
            rim.reshape(4, NP, LANES)
            + jnp.where(node == NP - 1, pltpu.roll(east, NP - 1, 1), 0.0)
            + jnp.where(node == 0, pltpu.roll(west, 1, 1), 0.0)
        )
        rows.append(rim.reshape(EDGE_ROWS, LANES))

    every = tuple(range(count))
    groups = (every[0:2], every[2:4], every[4:])

    def tile_part(k, n):
        if tiles[k] is None:
            return outer_used[n][:, :LANES] if k == 0 else outer_used[n][:, LANES:]
        return tiles[k][n * NODES : (n + 1) * NODES]

    def part_of(group, n):
        return jnp.concatenate([tile_part(k, n) for k in group], 1)

    def summed(group, c):
        return jnp.concatenate([sums[k, c * NODES : (c + 1) * NODES] for k in group], 1)

    def average(group, per_mass):
        return [summed(group, c) * per_mass for c in range(3)]

    def laplace(s):
        return [
            dot(table[4 * NODES :, : 3 * NODES], jnp.concatenate(high_low_high(part), 0))
            for part in s
        ]

    start = [[part_of(group, n) for n in range(3)] for group in groups]
    fixed = [[part_of(group, n) for n in range(3, 6)] for group in groups]
    for k in every:
        for c in range(4):
            sums[k, c * NODES : (c + 1) * NODES] = tile_part(k, 7 + c)
    edge_y(4, every, rows)
    per_mass = [1.0 / summed(group, 3) for group in groups]
    one = []
    for n, group in enumerate(groups):
        change = average(group, per_mass[n])
        one.append([s + time_step * c for s, c in zip(start[n], change)])
    put_x_sums(groups, [mass_tendency(table, *s, *f) for s, f in zip(one, fixed)])
    edge_y(3, every)
    two = []
    for n, group in enumerate(groups):
        change = average(group, per_mass[n])
        two.append(
            [0.75 * s + 0.25 * (o + time_step * c) for s, o, c in zip(start[n], one[n], change)]
        )
    put_x_sums(groups, [mass_tendency(table, *s, *f) for s, f in zip(two, fixed)])
    edge_y(3, every)

    def regrouped(per_group):
        (outer_low, high_above) = per_group[0], per_group[1]
        below, low = outer_low[:, :LANES], outer_low[:, LANES:]
        centre, high = high_above[:, :LANES], high_above[:, LANES:]
        near = jnp.where(lane < LANES // 2, per_group[2], below)
        return [beside(low, centre), beside(high, near)]

    def of_groups(values):
        return [list(parts) for parts in zip(*(regrouped(part) for part in zip(*values)))]

    for c in range(3):
        rows_at = slice(c * NODES, (c + 1) * NODES)
        sums[count - 1, rows_at] = jnp.where(
            lane < LANES // 2, sums[count - 1, rows_at], sums[0, rows_at]
        )
    slots = every[1:]
    groups = (slots[0:2], slots[2:4])
    start, two = of_groups(start), of_groups(two)
    tide = regrouped([part_of(every[0:2], 6), part_of(every[2:4], 6), part_of(every[4:], 6)])
    per_mass = regrouped(per_mass)
    three = []
    for n, group in enumerate(groups):
        change = average(group, per_mass[n])
        now = [
            s / 3.0 + 2.0 / 3.0 * (o + time_step * c)
            for s, o, c in zip(start[n], two[n], change)
        ]
        now[0] = now[0] + tide[n]
        three.append(now)
    put_x_sums(groups, [laplace(s) for s in three])
    edge_y(3, slots)
    change = [average(group, per_mass[n]) for n, group in enumerate(groups)]
    put_x_sums(groups, [laplace(s) for s in change])
    edge_y(3, slots)
    stepped = []
    for n, group in enumerate(groups):
        change = average(group, per_mass[n])
        now = [s - time_step * hyper_coeff * b for s, b in zip(three[n], change)]
        stepped.append(jnp.concatenate(now, 0))
    stepped = jnp.concatenate(stepped, 1)[:, :MID]
    own = lanes_ref[27:28, LANES : LANES + MID] != 0
    stored = picked(jnp.where(own, stepped, 0.0), hot_ref[...])
    out_ref[...] = stored.reshape(out_ref.shape)


def on_device(fields, jacobian, water_depth, coriolis, tide_height, slot_of, seam_rows):
    block_cols = lax.axis_size("blk") // BY
    table, weight = operator_table()
    table, weight, lanes = map(jnp.asarray, (table, weight, lane_tables()))
    vmem = pl.BlockSpec(memory_space=pltpu.VMEM)
    smem = pl.BlockSpec(memory_space=pltpu.SMEM)
    hbm = pl.BlockSpec(memory_space=pltpu.HBM)
    params = pltpu.CompilerParams(vmem_limit_bytes=48 * 2**20)
    held = (fields, jacobian, water_depth, coriolis, tide_height)

    def call(kernel, ins, outs, cost, scratch=(), name=None):
        return pl.pallas_call(
            kernel,
            out_shape=[jax.ShapeDtypeStruct(*out) for out in outs],
            in_specs=[spec for spec, value in ins],
            out_specs=[vmem] * len(outs),
            scratch_shapes=list(scratch),
            compiler_params=params,
            cost_estimate=pl.CostEstimate(
                flops=cost, bytes_accessed=2 * 2**20, transcendentals=0
            ),
            name=name,
        )(
            *[
                pltpu.with_memory_space_constraint(value, pltpu.HBM) if spec is hbm else value
                for spec, value in ins
            ]
        )

    strip = ((HALF_ROWS, LANES), f32)
    def room(values, spaces=None):
        spaces = spaces or [pltpu.VMEM] * len(values)
        buffers = [space(x.shape, x.dtype) for space, x in zip(spaces, values)]
        return buffers + [pltpu.SemaphoreType.DMA((len(values),))]

    needed = (seam_rows, slot_of, *held, table, weight)
    corner = ((CORNER_ROWS, LANES), f32)
    scratch = [pltpu.VMEM((1, 4 * NODES, LANES), f32)]
    strip1, strip0, stored = call(
        functools.partial(strips_kernel, block_cols),
        [(hbm, x) for x in needed],
        [strip, strip, ((ROWS, ELEMENTS), f32)],
        10**8,
        scratch=room(needed, [pltpu.SMEM] + [pltpu.VMEM] * (len(needed) - 1)),
        name="strips",
    )
    to_next, far0, far1, to_pair = call(
        functools.partial(rows_kernel, block_cols),
        [(smem, seam_rows)]
        + [(vmem, x) for x in (stored, strip1, strip0, slot_of, table, weight)],
        [strip, corner, corner, strip],
        10**8,
        scratch=scratch,
        name="rows",
    )
    span = block_cols * BY
    both = ("face", "blk")
    places = [(f, x, y) for f in range(2) for x in range(block_cols) for y in range(BY)]

    def rank(face, block_x, block_y):
        return face * span + block_x * BY + block_y

    def same(y):
        return y

    def in_pair(y):
        return y ^ 1

    def next_pair(y):
        other = y + 1 if y % 2 else y - 1
        return other if 0 <= other < BY else y

    def swapped(value, partner):
        pairs = [
            (rank(f, x, y), rank(f if partner(y) != y else 1 - f, x, partner(y)))
            for f, x, y in places
        ]
        return lax.ppermute(value, both, pairs)

    def across(value0, value1, partner):
        last = block_cols - 1

        def aligned(y):
            return partner is same or partner(y) != y

        straight = {
            (f, x, y): (f, x + 1, partner(y)) if x < last else (1 - f, 0, partner(y))
            for f, x, y in places
        }
        turned = {
            (f, last, y): (1 - f, 0, BY - 1 - partner(y) if aligned(y) else y)
            for f in range(2)
            for y in range(BY)
        }

        def eastward(value, pairs):
            return lax.ppermute(value, both, [(rank(*a), rank(*b)) for a, b in pairs.items()])

        def westward(value, pairs):
            return lax.ppermute(value, both, [(rank(*b), rank(*a)) for a, b in pairs.items()])

        if block_cols == 1:
            return eastward(value0, straight), eastward(value1, turned)
        flipped = (seam_rows[:, 1] - seam_rows[:, 0]) % seam_rows.shape[1] != 1
        face = lax.axis_index("face")
        block_x = lax.axis_index("blk") // BY
        return (
            jnp.where(
                (block_x == last) & flipped[face],
                westward(value1, turned),
                westward(value1, straight),
            ),
            jnp.where(
                (block_x == 0) & flipped[1 - face],
                eastward(value0, turned),
                eastward(value0, straight),
            ),
        )

    halo0, halo1 = across(strip0, strip1, same)
    far0, far1 = across(far0, far1, next_pair)
    from_next = swapped(to_next, next_pair)
    own, hot = call(
        own_kernel,
        [(vmem, x) for x in (stored, slot_of, lanes)],
        [((ROWS, MID), f32), ((MID, ELEMENTS), bf16)],
        10**8,
        name="own",
    )
    (to_pair,) = call(
        corners_kernel,
        [(vmem, x) for x in (halo1, halo0, to_pair, table, weight, hot)],
        [((HALF_ROWS + 2 * CORNER_ROWS, LANES), f32)],
        10**8,
        scratch=scratch,
        name="corners",
    )
    from_pair = swapped(to_pair, in_pair)
    tile = ((11 * NODES, LANES), f32)
    low, centre, high = call(
        functools.partial(middle_kernel, block_cols),
        [(smem, seam_rows)] + [(vmem, x) for x in (halo0, halo1, own, lanes, table, weight)],
        [tile, tile, tile],
        10**8,
        name="middle",
    )
    (far,) = call(
        far_kernel,
        [(vmem, x) for x in (far1, far0, from_next, low)],
        [((2 * CORNER_ROWS, LANES), f32)],
        10**11,
        name="far",
    )
    (stepped,) = call(
        functools.partial(steps_kernel, block_cols),
        [(smem, seam_rows)]
        + [
            (vmem, x)
            for x in (
                from_pair, from_next, far, low, centre, high,
                hot, table, weight, lanes,
            )
        ],
        [(fields.shape, f32)],
        10**8,
        scratch=[pltpu.VMEM((EXT // LANES, 4 * NODES, LANES), f32)],
        name="steps",
    )
    return stepped


def solution(mesh):
    return jax.shard_map(
        on_device,
        mesh=mesh,
        in_specs=(
            P(None, None, None, ("face", "blk")),
            P(None, None, ("face", "blk")),
            P(None, None, ("face", "blk")),
            P(None, None, ("face", "blk")),
            P(None, None, ("face", "blk")),
            P(("face", "blk"), None),
            P(),
        ),
        out_specs=P(None, None, None, ("face", "blk")),
        check_vma=False,
    )
```

```python
import functools
import math

import jax
import jax.numpy as jnp
import ml_dtypes
import numpy as np
from jax import lax
from jax.experimental import pallas as pl
from jax.experimental.pallas import tpu as pltpu
from jax.sharding import PartitionSpec as P

BY = 16
GX = 16
GY = 16
NP = 8
NODES = NP * NP
ARRAYS = 7
ROWS = ARRAYS * NODES
MOVED = 6 * NODES
EDGE_ROWS = 4 * NP
ALL_ROWS = ROWS + EDGE_ROWS
HALF_ROWS = (MOVED + NODES // 2 + 2 * NP) // 2
RING = 4
RIM_ROWS = ROWS + 2 * EDGE_ROWS
CORNER_ROWS = (MOVED + NODES // 2 + 4 * NP) // 8
PITCH = GX + 2 * RING
MID = GY * PITCH
LANES = 128
EXT = MID + 2 * LANES
LEAD = LANES - RING * PITCH
ELEMENTS = GX * GY

time_step = 0.03
hyper_coeff = 0.0002

f32 = jnp.float32
bf16 = jnp.bfloat16
i32 = jnp.int32


def legendre_pair(location, degree):
    lower_value = 1.0
    upper_value = location
    for polynomial_order in range(2, degree + 1):
        lower_value, upper_value = (
            upper_value,
            (
                (2 * polynomial_order - 1) * location * upper_value
                - (polynomial_order - 1) * lower_value
            )
            / polynomial_order,
        )
    return (lower_value, upper_value)


def gll_tables(points):
    degree = points - 1
    locations = [-math.cos(math.pi * position / degree) for position in range(points)]
    for iteration in range(100):
        updated = []
        for location in locations:
            lower_value, upper_value = legendre_pair(location, degree)
            updated.append(
                location - (location * upper_value - lower_value) / ((degree + 1) * upper_value)
            )
        locations = updated
    locations[0] = -1.0
    locations[degree] = 1.0
    legendre_at = [legendre_pair(location, degree)[1] for location in locations]
    weights = [2.0 / (degree * (degree + 1) * value * value) for value in legendre_at]
    corner_value = degree * (degree + 1) / 4.0
    derivative = []
    for row_index in range(points):
        row_values = []
        for column_index in range(points):
            if row_index != column_index:
                row_values.append(
                    legendre_at[row_index]
                    / (legendre_at[column_index] * (locations[row_index] - locations[column_index]))
                )
            elif row_index == 0:
                row_values.append(-corner_value)
            elif row_index == degree:
                row_values.append(corner_value)
            else:
                row_values.append(0.0)
        derivative.append(row_values)
    return np.asarray(weights, np.float64), np.asarray(derivative, np.float64)


def in_three(matrix):
    high = matrix.astype(ml_dtypes.bfloat16)
    low = (matrix - high.astype(np.float64)).astype(ml_dtypes.bfloat16)
    return np.concatenate([high, high, low], 1)


def operator_table():
    weights, derivative = gll_tables(NP)
    eye = np.eye(NP)
    node_weight = np.outer(weights, weights).reshape(NODES, 1)
    along_x = node_weight * np.kron(derivative, eye)
    along_y = node_weight * np.kron(eye, derivative)
    second = derivative @ derivative
    both = node_weight * (np.kron(second, eye) + np.kron(eye, second))
    table = np.zeros((5 * NODES, 4 * NODES), ml_dtypes.bfloat16)
    table[:NODES, : 3 * NODES] = in_three(along_x)
    table[NODES : 2 * NODES, : 3 * NODES] = in_three(along_y)
    flux = [in_three(along_x), in_three(along_y)]
    for k, part in enumerate(flux):
        at = 2 * k * NODES
        table[2 * NODES : 3 * NODES, at : at + 2 * NODES] = part[:, : 2 * NODES]
        table[3 * NODES : 4 * NODES, at : at + NODES] = part[:, 2 * NODES :]
    table[4 * NODES :, : 3 * NODES] = in_three(both)
    spread = np.broadcast_to(node_weight, (NODES, LANES)).astype(np.float32)
    return table.astype(np.float32), np.ascontiguousarray(spread)


def lane_tables():
    table = np.zeros((24, MID), np.int32)
    for lane in range(MID):
        row, col = divmod(lane, PITCH)
        x = col - RING
        own = 0 <= x < GX
        table[0:8, lane] = x * GY + row if own else -1
        if not own:
            table[8:16, lane] = row * RING + (col if x < 0 else x - GX)
        table[16:24, lane] = 0 if own else (1 if x < 0 else 2)
    ext = np.zeros((8, EXT), np.int32)
    outer = np.zeros((24, 2 * LANES), np.int32)
    for lane in range(EXT):
        row, col = divmod(lane - LEAD, PITCH)
        y = row - RING
        x = col - RING
        inside = 0 <= row < GY + 2 * RING
        ext[0, lane] = x in (-RING, GX + RING - 1)
        ext[1, lane] = y == GY - 1
        ext[2, lane] = y == 0
        ext[3, lane] = 0 <= y < GY and 0 <= x < GX
        ext[4, lane] = y == -RING
        ext[5, lane] = y == GY + RING - 1
        if inside and not 0 <= y < GY:
            place = lane if y < 0 else lane - LANES - MID + LANES
            step = y + RING if y < 0 else y - GY
            if 0 <= x < GX:
                outer[0:8, place] = step * GX + x
                outer[8:16, place] = 1
            else:
                outer[0:8, place] = LANES + step * RING + (x + RING if x < 0 else x - GX)
                outer[8:16, place] = 2 if x < 0 else 3
            outer[16:24, place] = y > 0
    whole = np.zeros((56, EXT), np.int32)
    whole[0:24, :MID] = table
    whole[24:32] = ext
    whole[32:56, : 2 * LANES] = outer
    return whole


def dot(a, b):
    return jnp.dot(a, b, preferred_element_type=f32)


def picked(values, one_hot):
    high = values.astype(bf16)
    low = (values - high.astype(f32)).astype(bf16)
    both = dot(jnp.concatenate([high, low], 0), one_hot)
    return both[: values.shape[0]] + both[values.shape[0] :]


def as_one_hot(row_of_lane, depth):
    index = lax.broadcasted_iota(i32, (depth, row_of_lane.shape[1]), 0)
    return jnp.where(index == row_of_lane[0:1], 1.0, 0.0).astype(bf16)


def high_low_high(values):
    high = values.astype(bf16)
    low = (values - high.astype(f32)).astype(bf16)
    return [high, low, high]


def by_slot(slot_ref, cell_of_lane):
    slots = jnp.broadcast_to(slot_ref[...], (8, ELEMENTS)).astype(f32).astype(bf16)
    chosen = dot(slots, as_one_hot(cell_of_lane, ELEMENTS))
    chosen = jnp.where(cell_of_lane >= 0, chosen, -1.0)
    index = lax.broadcasted_iota(i32, (ELEMENTS, cell_of_lane.shape[1]), 0).astype(f32)
    return jnp.where(index == chosen[0:1], 1.0, 0.0).astype(bf16)


def stored_rows(fields_ref, others):
    fields = fields_ref[...].reshape(3 * NODES, ELEMENTS)
    others = [ref[...].reshape(NODES, ELEMENTS) for ref in others]
    return jnp.concatenate([fields[:NODES] - others[-1], fields[NODES:]] + others, 0)


def mass_tendency(table, p, u, v, area_depth, weighted_area, spin):
    slopes = dot(table[: 2 * NODES, : 3 * NODES], jnp.concatenate(high_low_high(p), 0))
    flux = high_low_high(area_depth * u)[:2] + high_low_high(area_depth * v)[:2]
    spread = dot(table[2 * NODES : 4 * NODES], jnp.concatenate(flux, 0))
    return [
        -(spread[:NODES] + spread[NODES:]),
        spin * v - weighted_area * slopes[:NODES],
        -spin * u - weighted_area * slopes[NODES:],
    ]


def edge_values(table_ref, weight_ref, p, u, v, area, depth, spin):
    root = jnp.sqrt(area)
    mass = jnp.concatenate([weight_ref[...]] * (area.shape[1] // LANES), 1) * area
    table = table_ref[...].astype(bf16)
    return mass_tendency(table, p, u, v, root * depth, root, mass * spin) + [mass]


def row_edges(sums):
    return tuple(sums[0, pl.ds(j, EDGE_ROWS, stride=NP)] for j in (NP - 1, 0))


def beside(left, right):
    return jnp.concatenate([left, right], 1)


def one_of_four(parts, index):
    out = parts[0]
    for k in range(1, 4):
        out = jnp.where(index == k, parts[k], out)
    return out


def folded(tide, kept, late, step):
    half = NODES // 2
    back = pltpu.roll(tide[half:], LANES - step, 1)
    onward = pltpu.roll(tide[half:], step, 1)
    return jnp.where(kept, tide[:half], jnp.where(late, back, onward))


def unfolded(rows, late, step):
    back = pltpu.roll(rows, LANES - step, 1)
    onward = pltpu.roll(rows, step, 1)
    return jnp.concatenate([rows, jnp.where(late, onward, back)], 0)


def strip_rows(parts, late, shift, rims):
    lane = lax.broadcasted_iota(i32, (1, LANES), 1)
    index = (lane >> shift) & 3
    kept = jnp.where(late, index // 2, 1 - index // 2) != 0
    tide = folded(parts[6], kept, late, 2 << shift)
    rim = one_of_four(rims, index)
    return jnp.concatenate(parts[:6] + [tide, rim, jnp.zeros_like(rim)], 0)


def placed_rows(whole, late, shift):
    half = NODES // 2
    tide = unfolded(whole[MOVED : MOVED + half], late, 2 << shift)
    rim = whole[MOVED + half : MOVED + half + NP]
    return jnp.concatenate([whole[:MOVED], tide] + spread_out(rim, late, shift), 0)


def spread_out(rim, late, shift):
    parts = []
    for k in range(4):
        first = pltpu.roll(rim, (LANES - (k << shift)) % LANES, 1) if k else rim
        last = pltpu.roll(rim, (3 - k) << shift, 1) if k < 3 else rim
        parts.append(jnp.where(late, first, last))
    return parts


def with_row_rim(whole, sums, top):
    north, south = row_edges(sums)
    rim = jnp.where(top, pltpu.roll(north, RING, 1), pltpu.roll(south, LANES - RING, 1))
    parts = [rim[k * NP : (k + 1) * NP] for k in range(4)]
    lane = lax.broadcasted_iota(i32, (1, LANES), 1)
    spots = []
    for k, part in enumerate(parts):
        first = pltpu.roll(part, k * RING, 1) if k else part
        last = pltpu.roll(part, (LANES - (3 - k) * RING) % LANES, 1) if k < 3 else part
        spots.append(jnp.where(top, first, last))
    rim = one_of_four(spots, (lane >> 2) & 3)
    return jnp.concatenate([whole[: MOVED + NODES // 2 + NP], rim], 0)


def corner_of(whole, start, top):
    lane = lax.broadcasted_iota(i32, (1, LANES), 1)
    base = LANES - start - jnp.where(top != 0, 48, 0)
    whole = jnp.concatenate([whole, jnp.zeros((8 * CORNER_ROWS - whole.shape[0], LANES), f32)], 0)
    out = None
    for k in range(8):
        part = whole[k * CORNER_ROWS : (k + 1) * CORNER_ROWS]
        part = pltpu.roll(part, (base + 16 * k) & (LANES - 1), 1)
        out = part if k == 0 else jnp.where(lane >= 16 * k, part, out)
    return out


def packed(whole):
    second = lax.broadcasted_iota(i32, (1, LANES), 1) >= 64
    top, bottom = whole[:HALF_ROWS], whole[HALF_ROWS:]
    return (
        jnp.where(second, pltpu.roll(bottom, 64, 1), top),
        jnp.where(second, bottom, pltpu.roll(top, 64, 1)),
    )


def unpacked(in0, in1):
    second = lax.broadcasted_iota(i32, (1, LANES), 1) >= 64
    top = jnp.where(second, pltpu.roll(in1, 64, 1), in0)
    bottom = jnp.where(second, in1, pltpu.roll(in0, 64, 1))
    return jnp.concatenate([top, bottom], 0)


def seam_flags(seam_ref, block_cols):
    size_y = seam_ref.shape[1]
    face = lax.axis_index("face")
    blk = lax.axis_index("blk")
    block_x = blk // BY

    def flipped(k):
        return jnp.where(lax.rem(seam_ref[k, 1] - seam_ref[k, 0] + size_y, size_y) != 1, 1, 0)

    first, second = flipped(0), flipped(1)
    east_flip = jnp.where(face == 0, first, second)
    west_flip = jnp.where(face == 0, second, first)
    if block_cols == 1:
        return 1 - east_flip, 0, east_flip, 1
    at_east = jnp.where(block_x == block_cols - 1, east_flip, 0)
    at_west = jnp.where(block_x == 0, west_flip, 0)
    return 1, at_east, 0, at_west


def strips_kernel(block_cols, *refs):
    sources, (out1_ref, out0_ref, stored_ref) = refs[:9], refs[9:12]
    buffers, sems = refs[12:21], refs[21]
    copies = [
        pltpu.make_async_copy(source, buffer, sems.at[k])
        for k, (source, buffer) in enumerate(zip(sources, buffers))
    ]
    for copy in copies:
        copy.start()
    seam_ref, slot_ref, fields_ref, area_ref, depth_ref, spin_ref, tide_ref = buffers[:7]
    table_ref, weight_ref = buffers[7:]
    for copy in copies[:2]:
        copy.wait()
    east0, flip0, east1, flip1 = seam_flags(seam_ref, block_cols)
    lane = lax.broadcasted_iota(i32, (8, 2 * LANES), 1)
    second = (lane & 64) != 0
    place = lane & 63
    row = place >> 2
    row = jnp.where(jnp.where(second, flip1, flip0) != 0, GY - 1 - row, row)
    east = jnp.where(second, east1, east0) != 0
    col = jnp.where(east, GX - RING, 0) + (place & 3)
    col = jnp.where(lane >= LANES, jnp.where(east, GX - RING - 1, RING), col)
    one_hot = by_slot(slot_ref, col * GY + row)
    for copy in copies[2:7]:
        copy.wait()
    stored = stored_rows(fields_ref, (area_ref, depth_ref, spin_ref, tide_ref))
    both = picked(stored, one_hot)

    lane = lax.broadcasted_iota(i32, (1, LANES), 1)
    second = lane >= 64
    flip = jnp.where(second, flip1, flip0) != 0
    sign = jnp.where(flip, -1.0, 1.0)
    node = lax.broadcasted_iota(i32, (1, NP, 1), 1)

    def in_frame(values):
        shaped = values.reshape(-1, NP, LANES)
        turned = pltpu.roll(shaped, 4, 1)
        turned = jnp.where((node & 2) == 0, pltpu.roll(turned, 6, 1), pltpu.roll(turned, 2, 1))
        turned = jnp.where((node & 1) == 0, pltpu.roll(turned, 7, 1), pltpu.roll(turned, 1, 1))
        values = jnp.where(flip[None], turned, shaped).reshape(values.shape)
        parts = [values[k * NODES : (k + 1) * NODES] for k in range(ARRAYS)]
        parts[2] = parts[2] * sign
        parts[5] = parts[5] * sign
        return parts

    strip, ring = in_frame(both[:, :LANES]), in_frame(both[:, LANES:])
    for copy in copies[7:]:
        copy.wait()
    edges = edge_values(table_ref, weight_ref, *ring[:6])
    east = jnp.where(second, east1, east0) != 0
    ends = [jnp.where(east, part[NODES - NP :], part[:NP]) for part in edges]
    out0_ref[...], out1_ref[...] = packed(strip_rows(strip, east, 0, ends))
    stored_ref[...] = stored


def rows_kernel(
    block_cols, seam_ref, stored_ref, strip1_ref, strip0_ref, slot_ref, table_ref, weight_ref,
    next_ref, far0_ref, far1_ref, pair_ref, sums,
):
    east0, flip0, east1, flip1 = seam_flags(seam_ref, block_cols)
    odd = lax.axis_index("blk") & 1

    def goes_up(lane):
        return jnp.where((lane & 64) != 0, odd, 1 - odd) != 0

    lane = lax.broadcasted_iota(i32, (8, 2 * LANES), 1)
    up = goes_up(lane)
    row = jnp.where(up, GY - RING, 0) + ((lane & 63) >> 4)
    row = jnp.where(lane >= LANES, jnp.where(up, GY - RING - 1, RING), row)
    both = picked(stored_ref[...], by_slot(slot_ref, (lane & 15) * GY + row))
    rows, behind = (
        [part[k * NODES : (k + 1) * NODES] for k in range(ARRAYS)]
        for part in (both[:, :LANES], both[:, LANES:])
    )
    whole = unpacked(strip0_ref[...], strip1_ref[...])
    strip = [whole[k * NODES : (k + 1) * NODES] for k in range(6)]
    edges = edge_values(table_ref, weight_ref, *map(beside, strip, behind[:6]))
    sums[0] = jnp.concatenate([part[:, :LANES] for part in edges], 0)
    lane = lax.broadcasted_iota(i32, (1, LANES), 1)
    top0, top1 = odd ^ flip0, odd ^ flip1
    whole = with_row_rim(whole, sums, jnp.where(lane >= 64, top1, top0) != 0)
    far0_ref[...] = corner_of(whole, 0, top0)
    far1_ref[...] = corner_of(whole, 64, top1)
    sums[0] = jnp.concatenate([part[:, LANES:] for part in edges], 0)
    up = goes_up(lane)
    rim = jnp.where(up, *row_edges(sums))
    rim = [rim[k * NP : (k + 1) * NP] for k in range(4)]
    pair_ref[...], next_ref[...] = packed(strip_rows(rows, up, 4, rim))


def corners_kernel(in1_ref, in0_ref, pair_ref, table_ref, weight_ref, *refs):
    out_ref, sums = refs[-2:]
    top = 1 - (lax.axis_index("blk") & 1)
    whole = unpacked(in0_ref[...], in1_ref[...])
    parts = [whole[k * NODES : (k + 1) * NODES] for k in range(6)]
    sums[0] = jnp.concatenate(edge_values(table_ref, weight_ref, *parts), 0)
    whole = with_row_rim(whole, sums, jnp.broadcast_to(top != 0, (1, LANES)))
    out_ref[:HALF_ROWS] = pair_ref[...]
    out_ref[HALF_ROWS : HALF_ROWS + CORNER_ROWS] = corner_of(whole, 0, top)
    out_ref[HALF_ROWS + CORNER_ROWS :] = corner_of(whole, 64, top)


def own_kernel(stored_ref, slot_ref, lanes_ref, own_ref, hot_ref):
    one_hot = by_slot(slot_ref, lanes_ref[0:8, :MID])
    own_ref[...] = picked(stored_ref[...], one_hot)
    hot_ref[...] = one_hot.astype(f32).T.astype(bf16)


def first_sums(table, weight, parts, rims, at_rim):
    p, u, v, area, depth, spin, tide = parts
    size = area.shape[1]
    root = jnp.sqrt(area)
    mass = jnp.concatenate([weight] * (size // LANES), 1) * area
    used = [p, u, v, root * depth, root, mass * spin, tide]
    for part, rim in zip(mass_tendency(table, p, u, v, *used[3:6]) + [mass], rims):
        west, east = part[:NP], part[NODES - NP :]
        at_east = jnp.where(at_rim, rim, pltpu.roll(west, size - 1, 1))
        at_west = jnp.where(at_rim, rim, pltpu.roll(east, 1, 1))
        used.append(
            jnp.concatenate([west + at_west, part[NP : NODES - NP], east + at_east], 0)
        )
    return used


def middle_kernel(
    block_cols, seam_ref, in0_ref, in1_ref, own_ref, lanes_ref, table_ref, weight_ref,
    low_ref, centre_ref, high_ref,
):
    east0, flip0, east1, flip1 = seam_flags(seam_ref, block_cols)
    second = lax.broadcasted_iota(i32, (1, LANES), 1) >= 64
    late = jnp.where(second, east1, east0) == 0
    whole = placed_rows(unpacked(in0_ref[...], in1_ref[...]), late, 0)
    side = lanes_ref[16:24, :MID]
    first_at = jnp.where(side == 2, 64 * (1 - east0), 64 * east0)
    place = jnp.where(side == 0, -1, lanes_ref[8:16, :MID] + first_at)
    placed = picked(whole, as_one_hot(place, LANES))
    parts = [
        placed[k * NODES : (k + 1) * NODES] + own_ref[k * NODES : (k + 1) * NODES]
        for k in range(ARRAYS)
    ]
    rims = [placed[ROWS + c * NP : ROWS + (c + 1) * NP] for c in range(4)]
    at_rim = lanes_ref[24:25, LANES : LANES + MID] != 0
    used = first_sums(table_ref[...].astype(bf16), weight_ref[...], parts, rims, at_rim)
    for k, ref in enumerate((low_ref, centre_ref, high_ref)):
        for n, part in enumerate(used):
            ref[n * NODES : (n + 1) * NODES] = part[:, k * LANES : (k + 1) * LANES]


def next_kernel(next_ref, _, out_ref):
    out_ref[...] = next_ref[...]


def far_kernel(far1_ref, far0_ref, *refs):
    out_ref = refs[-1]
    out_ref[:CORNER_ROWS] = far0_ref[...]
    out_ref[CORNER_ROWS:] = far1_ref[...]


def steps_kernel(
    block_cols, seam_ref, pair_ref, next_ref, far_ref, low_ref, centre_ref,
    high_ref, hot_ref, table_ref, weight_ref, lanes_ref, out_ref, sums,
):
    east0, flip0, east1, flip1 = seam_flags(seam_ref, block_cols)
    odd = lax.axis_index("blk") & 1
    block_y = lax.rem(lax.axis_index("blk"), BY)

    lane = lax.broadcasted_iota(i32, (1, LANES), 1)
    pair = pair_ref[...]
    late = jnp.where(lane < 64, odd, 1 - odd) != 0
    strips = placed_rows(unpacked(pair[:HALF_ROWS], next_ref[...]), late, 4)
    strips = jnp.concatenate(
        [strips[:ROWS], jnp.zeros((EDGE_ROWS, LANES), f32), strips[ROWS:]], 0
    )
    near = pair[HALF_ROWS:]
    far = far_ref[...]
    sources = (near[:CORNER_ROWS], near[CORNER_ROWS:], far[:CORNER_ROWS], far[CORNER_ROWS:])
    corners = []
    for k in range(8):
        rows = None
        for n, source in enumerate(sources):
            shift = 16 * (n - k) % LANES
            part = pltpu.roll(source, shift, 1) if shift else source
            rows = part if n == 0 else jnp.where(lane >= 16 * n, part, rows)
        corners.append(rows)
    corners = jnp.concatenate(corners, 0)
    rim = MOVED + NODES // 2 + NP
    late = jnp.where((lane & 16) != 0, east1, east0) == 0
    below = jnp.where((lane & 32) != 0, 1 - odd, odd) != 0
    corners = jnp.concatenate(
        [placed_rows(corners, late, 0)] + spread_out(corners[rim : rim + NP], below, 2), 0
    )
    around = jnp.concatenate([strips, corners], 1)
    kind = lanes_ref[40:48, : 2 * LANES]
    sender = jnp.where(lanes_ref[48:56, : 2 * LANES] != 0, odd, 1 - odd)
    strip_at = jnp.where(kind == 3, 16 * (1 - east0), 16 * east0)
    place = lanes_ref[32:40, : 2 * LANES]
    place = place + jnp.where(kind == 1, 64 * sender, 32 * sender + strip_at)
    outer = picked(around, as_one_hot(jnp.where(kind == 0, -1, place), 2 * LANES))
    table = table_ref[...].astype(bf16)
    tiles = (None, low_ref, centre_ref, high_ref, None)
    count = len(tiles)
    masks = [lanes_ref[24:32, k * LANES : (k + 1) * LANES] for k in range(count)]
    closed_above = jnp.where(block_y == BY - 1, masks[-2][1:2], 0) != 0
    closed_below = jnp.where(block_y == 0, masks[1][2:3], 0) != 0
    first_row = masks[0][4:5] != 0
    last_row = masks[-1][5:6] != 0
    outer_used = first_sums(
        table,
        weight_ref[...],
        [outer[k * NODES : (k + 1) * NODES] for k in range(ARRAYS)],
        [outer[ROWS + c * NP : ROWS + (c + 1) * NP] for c in range(4)],
        beside(masks[0][0:1], masks[-1][0:1]) != 0,
    )

    def shifted(parts, by, ring):
        turned = [pltpu.roll(part, -by % LANES, 1) for part in parts]
        size = len(parts)
        step = 1 if by > 0 else -1
        others = [(k + step) % size if ring else min(max(k + step, 0), size - 1) for k in range(size)]
        from_other = lane >= LANES - by if by > 0 else lane < -by
        return [jnp.where(from_other, turned[others[k]], turned[k]) for k in range(size)]

    def put_x_sums(groups, components):
        slots = [k for group in groups for k in group]
        ring = len(slots) < count
        per_tile = [
            [part[:, n * LANES : (n + 1) * LANES] for part in parts]
            for group, parts in zip(groups, components)
            for n in range(len(group))
        ]
        for c in range(3):
            parts = [tile[c] for tile in per_tile]
            west = [part[:NP] for part in parts]
            east = [part[NODES - NP :] for part in parts]
            at_east, at_west = shifted(west, 1, ring), shifted(east, -1, ring)
            for n, k in enumerate(slots):
                sums[k, c * NODES : c * NODES + NP] = west[n] + at_west[n]
                sums[k, c * NODES + NP : (c + 1) * NODES - NP] = parts[n][NP : NODES - NP]
                sums[k, (c + 1) * NODES - NP : (c + 1) * NODES] = east[n] + at_east[n]

    def edge_y(components, slots, rows=None):
        ring = len(slots) < count
        south_at = pl.ds(0, components * NP, stride=NP)
        north_at = pl.ds(NP - 1, components * NP, stride=NP)
        south = [sums[k, south_at] for k in slots]
        north = [sums[k, north_at] for k in slots]
        at_north, at_south = shifted(south, PITCH, ring), shifted(north, -PITCH, ring)
        for n, k in enumerate(slots):
            if k == count - 2:
                at_north[n] = jnp.where(closed_above, 0.0, at_north[n])
            if k == 1:
                at_south[n] = jnp.where(closed_below, 0.0, at_south[n])
        if rows is not None:
            at_south[0] = jnp.where(first_row, rows[0], at_south[0])
            at_north[-1] = jnp.where(last_row, rows[1], at_north[-1])
        for n, k in enumerate(slots):
            sums[k, south_at] = south[n] + at_south[n]
            sums[k, north_at] = north[n] + at_north[n]

    node = lax.broadcasted_iota(i32, (1, NP, 1), 1)
    rows = []
    for rim in (outer[ALL_ROWS:, :LANES], outer[ALL_ROWS:, LANES:]):
        east = pltpu.roll(rim, LANES - 1, 1).reshape(4, NP, LANES)
        west = pltpu.roll(rim, 1, 1).reshape(4, NP, LANES)
        rim = (
            rim.reshape(4, NP, LANES)
            + jnp.where(node == NP - 1, pltpu.roll(east, NP - 1, 1), 0.0)
            + jnp.where(node == 0, pltpu.roll(west, 1, 1), 0.0)
        )
        rows.append(rim.reshape(EDGE_ROWS, LANES))

    every = tuple(range(count))
    groups = (every[0:2], every[2:4], every[4:])

    def tile_part(k, n):
        if tiles[k] is None:
            return outer_used[n][:, :LANES] if k == 0 else outer_used[n][:, LANES:]
        return tiles[k][n * NODES : (n + 1) * NODES]

    def part_of(group, n):
        return jnp.concatenate([tile_part(k, n) for k in group], 1)

    def summed(group, c):
        return jnp.concatenate([sums[k, c * NODES : (c + 1) * NODES] for k in group], 1)

    def average(group, per_mass):
        return [summed(group, c) * per_mass for c in range(3)]

    def laplace(s):
        return [
            dot(table[4 * NODES :, : 3 * NODES], jnp.concatenate(high_low_high(part), 0))
            for part in s
        ]

    start = [[part_of(group, n) for n in range(3)] for group in groups]
    fixed = [[part_of(group, n) for n in range(3, 6)] for group in groups]
    for k in every:
        for c in range(4):
            sums[k, c * NODES : (c + 1) * NODES] = tile_part(k, 7 + c)
    edge_y(4, every, rows)
    per_mass = [1.0 / summed(group, 3) for group in groups]
    one = []
    for n, group in enumerate(groups):
        change = average(group, per_mass[n])
        one.append([s + time_step * c for s, c in zip(start[n], change)])
    put_x_sums(groups, [mass_tendency(table, *s, *f) for s, f in zip(one, fixed)])
    edge_y(3, every)
    two = []
    for n, group in enumerate(groups):
        change = average(group, per_mass[n])
        two.append(
            [0.75 * s + 0.25 * (o + time_step * c) for s, o, c in zip(start[n], one[n], change)]
        )
    put_x_sums(groups, [mass_tendency(table, *s, *f) for s, f in zip(two, fixed)])
    edge_y(3, every)

    def regrouped(per_group):
        (outer_low, high_above) = per_group[0], per_group[1]
        below, low = outer_low[:, :LANES], outer_low[:, LANES:]
        centre, high = high_above[:, :LANES], high_above[:, LANES:]
        near = jnp.where(lane < LANES // 2, per_group[2], below)
        return [beside(low, centre), beside(high, near)]

    def of_groups(values):
        return [list(parts) for parts in zip(*(regrouped(part) for part in zip(*values)))]

    for c in range(3):
        rows_at = slice(c * NODES, (c + 1) * NODES)
        sums[count - 1, rows_at] = jnp.where(
            lane < LANES // 2, sums[count - 1, rows_at], sums[0, rows_at]
        )
    slots = every[1:]
    groups = (slots[0:2], slots[2:4])
    start, two = of_groups(start), of_groups(two)
    tide = regrouped([part_of(every[0:2], 6), part_of(every[2:4], 6), part_of(every[4:], 6)])
    per_mass = regrouped(per_mass)
    three = []
    for n, group in enumerate(groups):
        change = average(group, per_mass[n])
        now = [
            s / 3.0 + 2.0 / 3.0 * (o + time_step * c)
            for s, o, c in zip(start[n], two[n], change)
        ]
        now[0] = now[0] + tide[n]
        three.append(now)
    put_x_sums(groups, [laplace(s) for s in three])
    edge_y(3, slots)
    change = [average(group, per_mass[n]) for n, group in enumerate(groups)]
    put_x_sums(groups, [laplace(s) for s in change])
    edge_y(3, slots)
    stepped = []
    for n, group in enumerate(groups):
        change = average(group, per_mass[n])
        now = [s - time_step * hyper_coeff * b for s, b in zip(three[n], change)]
        stepped.append(jnp.concatenate(now, 0))
    stepped = jnp.concatenate(stepped, 1)[:, :MID]
    own = lanes_ref[27:28, LANES : LANES + MID] != 0
    stored = picked(jnp.where(own, stepped, 0.0), hot_ref[...])
    out_ref[...] = stored.reshape(out_ref.shape)


def on_device(fields, jacobian, water_depth, coriolis, tide_height, slot_of, seam_rows):
    block_cols = lax.axis_size("blk") // BY
    table, weight = operator_table()
    table, weight, lanes = map(jnp.asarray, (table, weight, lane_tables()))
    vmem = pl.BlockSpec(memory_space=pltpu.VMEM)
    smem = pl.BlockSpec(memory_space=pltpu.SMEM)
    hbm = pl.BlockSpec(memory_space=pltpu.HBM)
    params = pltpu.CompilerParams(vmem_limit_bytes=48 * 2**20)
    held = (fields, jacobian, water_depth, coriolis, tide_height)

    def call(kernel, ins, outs, cost, scratch=(), name=None):
        return pl.pallas_call(
            kernel,
            out_shape=[jax.ShapeDtypeStruct(*out) for out in outs],
            in_specs=[spec for spec, value in ins],
            out_specs=[vmem] * len(outs),
            scratch_shapes=list(scratch),
            compiler_params=params,
            cost_estimate=pl.CostEstimate(
                flops=cost, bytes_accessed=2 * 2**20, transcendentals=0
            ),
            name=name,
        )(
            *[
                pltpu.with_memory_space_constraint(value, pltpu.HBM) if spec is hbm else value
                for spec, value in ins
            ]
        )

    strip = ((HALF_ROWS, LANES), f32)
    def room(values, spaces=None):
        spaces = spaces or [pltpu.VMEM] * len(values)
        buffers = [space(x.shape, x.dtype) for space, x in zip(spaces, values)]
        return buffers + [pltpu.SemaphoreType.DMA((len(values),))]

    needed = (seam_rows, slot_of, *held, table, weight)
    corner = ((CORNER_ROWS, LANES), f32)
    scratch = [pltpu.VMEM((1, 4 * NODES, LANES), f32)]
    strip1, strip0, stored = call(
        functools.partial(strips_kernel, block_cols),
        [(hbm, x) for x in needed],
        [strip, strip, ((ROWS, ELEMENTS), f32)],
        10**8,
        scratch=room(needed, [pltpu.SMEM] + [pltpu.VMEM] * (len(needed) - 1)),
        name="strips",
    )
    to_next, far0, far1, to_pair = call(
        functools.partial(rows_kernel, block_cols),
        [(smem, seam_rows)]
        + [(vmem, x) for x in (stored, strip1, strip0, slot_of, table, weight)],
        [strip, corner, corner, strip],
        10**8,
        scratch=scratch,
        name="rows",
    )
    span = block_cols * BY
    both = ("face", "blk")
    places = [(f, x, y) for f in range(2) for x in range(block_cols) for y in range(BY)]

    def rank(face, block_x, block_y):
        return face * span + block_x * BY + block_y

    def same(y):
        return y

    def in_pair(y):
        return y ^ 1

    def next_pair(y):
        other = y + 1 if y % 2 else y - 1
        return other if 0 <= other < BY else y

    def swapped(value, partner):
        pairs = [
            (rank(f, x, y), rank(f if partner(y) != y else 1 - f, x, partner(y)))
            for f, x, y in places
        ]
        return lax.ppermute(value, both, pairs)

    def across(value0, value1, partner):
        last = block_cols - 1

        def aligned(y):
            return partner is same or partner(y) != y

        straight = {
            (f, x, y): (f, x + 1, partner(y)) if x < last else (1 - f, 0, partner(y))
            for f, x, y in places
        }
        turned = {
            (f, last, y): (1 - f, 0, BY - 1 - partner(y) if aligned(y) else y)
            for f in range(2)
            for y in range(BY)
        }

        def eastward(value, pairs):
            return lax.ppermute(value, both, [(rank(*a), rank(*b)) for a, b in pairs.items()])

        def westward(value, pairs):
            return lax.ppermute(value, both, [(rank(*b), rank(*a)) for a, b in pairs.items()])

        if block_cols == 1:
            return eastward(value0, straight), eastward(value1, turned)
        flipped = (seam_rows[:, 1] - seam_rows[:, 0]) % seam_rows.shape[1] != 1
        face = lax.axis_index("face")
        block_x = lax.axis_index("blk") // BY
        return (
            jnp.where(
                (block_x == last) & flipped[face],
                westward(value1, turned),
                westward(value1, straight),
            ),
            jnp.where(
                (block_x == 0) & flipped[1 - face],
                eastward(value0, turned),
                eastward(value0, straight),
            ),
        )

    halo0, halo1 = across(strip0, strip1, same)
    far0, far1 = across(far0, far1, next_pair)
    from_next = swapped(to_next, next_pair)
    own, hot = call(
        own_kernel,
        [(vmem, x) for x in (stored, slot_of, lanes)],
        [((ROWS, MID), f32), ((MID, ELEMENTS), bf16)],
        10**8,
        name="own",
    )
    (to_pair,) = call(
        corners_kernel,
        [(vmem, x) for x in (halo1, halo0, to_pair, table, weight, hot)],
        [((HALF_ROWS + 2 * CORNER_ROWS, LANES), f32)],
        10**8,
        scratch=scratch,
        name="corners",
    )
    from_pair = swapped(to_pair, in_pair)
    tile = ((11 * NODES, LANES), f32)
    low, centre, high = call(
        functools.partial(middle_kernel, block_cols),
        [(smem, seam_rows)] + [(vmem, x) for x in (halo0, halo1, own, lanes, table, weight)],
        [tile, tile, tile],
        10**8,
        name="middle",
    )
    (far,) = call(
        far_kernel,
        [(vmem, x) for x in (far1, far0, low)],
        [((2 * CORNER_ROWS, LANES), f32)],
        10**11,
        name="far",
    )
    (from_next,) = call(
        next_kernel,
        [(vmem, x) for x in (from_next, far)],
        [strip],
        10**10,
        name="next",
    )
    (stepped,) = call(
        functools.partial(steps_kernel, block_cols),
        [(smem, seam_rows)]
        + [
            (vmem, x)
            for x in (
                from_pair, from_next, far, low, centre, high,
                hot, table, weight, lanes,
            )
        ],
        [(fields.shape, f32)],
        10**8,
        scratch=[pltpu.VMEM((EXT // LANES, 4 * NODES, LANES), f32)],
        name="steps",
    )
    return stepped


def solution(mesh):
    return jax.shard_map(
        on_device,
        mesh=mesh,
        in_specs=(
            P(None, None, None, ("face", "blk")),
            P(None, None, ("face", "blk")),
            P(None, None, ("face", "blk")),
            P(None, None, ("face", "blk")),
            P(None, None, ("face", "blk")),
            P(("face", "blk"), None),
            P(),
        ),
        out_specs=P(None, None, None, ("face", "blk")),
        check_vma=False,
    )
```

```python
import functools
import math

import jax
import jax.numpy as jnp
import ml_dtypes
import numpy as np
from jax import lax
from jax.experimental import pallas as pl
from jax.experimental.pallas import tpu as pltpu
from jax.sharding import PartitionSpec as P

BY = 16
GX = 16
GY = 16
NP = 8
NODES = NP * NP
ARRAYS = 7
ROWS = ARRAYS * NODES
MOVED = 6 * NODES
EDGE_ROWS = 4 * NP
ALL_ROWS = ROWS + EDGE_ROWS
HALF_ROWS = (MOVED + NODES // 2 + 2 * NP) // 2
RING = 4
RIM_ROWS = ROWS + 2 * EDGE_ROWS
CORNER_ROWS = (MOVED + NODES // 2 + 4 * NP) // 8
PITCH = GX + 2 * RING
MID = GY * PITCH
LANES = 128
EXT = MID + 2 * LANES
LEAD = LANES - RING * PITCH
ELEMENTS = GX * GY

time_step = 0.03
hyper_coeff = 0.0002

f32 = jnp.float32
bf16 = jnp.bfloat16
i32 = jnp.int32


def legendre_pair(location, degree):
    lower_value = 1.0
    upper_value = location
    for polynomial_order in range(2, degree + 1):
        lower_value, upper_value = (
            upper_value,
            (
                (2 * polynomial_order - 1) * location * upper_value
                - (polynomial_order - 1) * lower_value
            )
            / polynomial_order,
        )
    return (lower_value, upper_value)


def gll_tables(points):
    degree = points - 1
    locations = [-math.cos(math.pi * position / degree) for position in range(points)]
    for iteration in range(100):
        updated = []
        for location in locations:
            lower_value, upper_value = legendre_pair(location, degree)
            updated.append(
                location - (location * upper_value - lower_value) / ((degree + 1) * upper_value)
            )
        locations = updated
    locations[0] = -1.0
    locations[degree] = 1.0
    legendre_at = [legendre_pair(location, degree)[1] for location in locations]
    weights = [2.0 / (degree * (degree + 1) * value * value) for value in legendre_at]
    corner_value = degree * (degree + 1) / 4.0
    derivative = []
    for row_index in range(points):
        row_values = []
        for column_index in range(points):
            if row_index != column_index:
                row_values.append(
                    legendre_at[row_index]
                    / (legendre_at[column_index] * (locations[row_index] - locations[column_index]))
                )
            elif row_index == 0:
                row_values.append(-corner_value)
            elif row_index == degree:
                row_values.append(corner_value)
            else:
                row_values.append(0.0)
        derivative.append(row_values)
    return np.asarray(weights, np.float64), np.asarray(derivative, np.float64)


def in_three(matrix):
    high = matrix.astype(ml_dtypes.bfloat16)
    low = (matrix - high.astype(np.float64)).astype(ml_dtypes.bfloat16)
    return np.concatenate([high, high, low], 1)


def operator_table():
    weights, derivative = gll_tables(NP)
    eye = np.eye(NP)
    node_weight = np.outer(weights, weights).reshape(NODES, 1)
    along_x = node_weight * np.kron(derivative, eye)
    along_y = node_weight * np.kron(eye, derivative)
    second = derivative @ derivative
    both = node_weight * (np.kron(second, eye) + np.kron(eye, second))
    table = np.zeros((5 * NODES, 4 * NODES), ml_dtypes.bfloat16)
    table[:NODES, : 3 * NODES] = in_three(along_x)
    table[NODES : 2 * NODES, : 3 * NODES] = in_three(along_y)
    flux = [in_three(along_x), in_three(along_y)]
    for k, part in enumerate(flux):
        at = 2 * k * NODES
        table[2 * NODES : 3 * NODES, at : at + 2 * NODES] = part[:, : 2 * NODES]
        table[3 * NODES : 4 * NODES, at : at + NODES] = part[:, 2 * NODES :]
    table[4 * NODES :, : 3 * NODES] = in_three(both)
    spread = np.broadcast_to(node_weight, (NODES, LANES)).astype(np.float32)
    return table.astype(np.float32), np.ascontiguousarray(spread)


def lane_tables():
    table = np.zeros((24, MID), np.int32)
    for lane in range(MID):
        row, col = divmod(lane, PITCH)
        x = col - RING
        own = 0 <= x < GX
        table[0:8, lane] = x * GY + row if own else -1
        if not own:
            table[8:16, lane] = row * RING + (col if x < 0 else x - GX)
        table[16:24, lane] = 0 if own else (1 if x < 0 else 2)
    ext = np.zeros((8, EXT), np.int32)
    outer = np.zeros((24, 2 * LANES), np.int32)
    for lane in range(EXT):
        row, col = divmod(lane - LEAD, PITCH)
        y = row - RING
        x = col - RING
        inside = 0 <= row < GY + 2 * RING
        ext[0, lane] = x in (-RING, GX + RING - 1)
        ext[1, lane] = y == GY - 1
        ext[2, lane] = y == 0
        ext[3, lane] = 0 <= y < GY and 0 <= x < GX
        ext[4, lane] = y == -RING
        ext[5, lane] = y == GY + RING - 1
        if inside and not 0 <= y < GY:
            place = lane if y < 0 else lane - LANES - MID + LANES
            step = y + RING if y < 0 else y - GY
            if 0 <= x < GX:
                outer[0:8, place] = step * GX + x
                outer[8:16, place] = 1
            else:
                outer[0:8, place] = LANES + step * RING + (x + RING if x < 0 else x - GX)
                outer[8:16, place] = 2 if x < 0 else 3
            outer[16:24, place] = y > 0
    whole = np.zeros((56, EXT), np.int32)
    whole[0:24, :MID] = table
    whole[24:32] = ext
    whole[32:56, : 2 * LANES] = outer
    return whole


def dot(a, b):
    return jnp.dot(a, b, preferred_element_type=f32)


def picked(values, one_hot):
    high = values.astype(bf16)
    low = (values - high.astype(f32)).astype(bf16)
    both = dot(jnp.concatenate([high, low], 0), one_hot)
    return both[: values.shape[0]] + both[values.shape[0] :]


def as_one_hot(row_of_lane, depth):
    index = lax.broadcasted_iota(i32, (depth, row_of_lane.shape[1]), 0)
    return jnp.where(index == row_of_lane[0:1], 1.0, 0.0).astype(bf16)


def high_low_high(values):
    high = values.astype(bf16)
    low = (values - high.astype(f32)).astype(bf16)
    return [high, low, high]


def by_slot(slot_ref, cell_of_lane):
    size = cell_of_lane.shape[1]
    halves = [
        jnp.broadcast_to(slot_ref[:, k * LANES : (k + 1) * LANES], (8, LANES)) for k in range(2)
    ]
    chosen = []
    for k in range(size // LANES):
        cell = cell_of_lane[:, k * LANES : (k + 1) * LANES]
        low, high = (jnp.take_along_axis(half, cell & (LANES - 1), axis=1) for half in halves)
        chosen.append(jnp.where(cell < 0, -1, jnp.where(cell < LANES, low, high)))
    return as_one_hot(jnp.concatenate(chosen, 1), ELEMENTS)


def stored_rows(fields_ref, others):
    fields = fields_ref[...].reshape(3 * NODES, ELEMENTS)
    others = [ref[...].reshape(NODES, ELEMENTS) for ref in others]
    return jnp.concatenate([fields[:NODES] - others[-1], fields[NODES:]] + others, 0)


def mass_tendency(table, p, u, v, area_depth, weighted_area, spin):
    slopes = dot(table[: 2 * NODES, : 3 * NODES], jnp.concatenate(high_low_high(p), 0))
    flux = high_low_high(area_depth * u)[:2] + high_low_high(area_depth * v)[:2]
    spread = dot(table[2 * NODES : 4 * NODES], jnp.concatenate(flux, 0))
    return [
        -(spread[:NODES] + spread[NODES:]),
        spin * v - weighted_area * slopes[:NODES],
        -spin * u - weighted_area * slopes[NODES:],
    ]


def edge_values(table_ref, weight_ref, p, u, v, area, depth, spin):
    root = jnp.sqrt(area)
    mass = jnp.concatenate([weight_ref[...]] * (area.shape[1] // LANES), 1) * area
    table = table_ref[...].astype(bf16)
    return mass_tendency(table, p, u, v, root * depth, root, mass * spin) + [mass]


def row_edges(sums):
    return tuple(sums[0, pl.ds(j, EDGE_ROWS, stride=NP)] for j in (NP - 1, 0))


def beside(left, right):
    return jnp.concatenate([left, right], 1)


def one_of_four(parts, index):
    out = parts[0]
    for k in range(1, 4):
        out = jnp.where(index == k, parts[k], out)
    return out


def folded(tide, kept, late, step):
    half = NODES // 2
    back = pltpu.roll(tide[half:], LANES - step, 1)
    onward = pltpu.roll(tide[half:], step, 1)
    return jnp.where(kept, tide[:half], jnp.where(late, back, onward))


def unfolded(rows, late, step):
    back = pltpu.roll(rows, LANES - step, 1)
    onward = pltpu.roll(rows, step, 1)
    return jnp.concatenate([rows, jnp.where(late, onward, back)], 0)


def strip_rows(parts, late, shift, rims):
    lane = lax.broadcasted_iota(i32, (1, LANES), 1)
    index = (lane >> shift) & 3
    kept = jnp.where(late, index // 2, 1 - index // 2) != 0
    tide = folded(parts[6], kept, late, 2 << shift)
    rim = one_of_four(rims, index)
    return jnp.concatenate(parts[:6] + [tide, rim, jnp.zeros_like(rim)], 0)


def placed_rows(whole, late, shift):
    half = NODES // 2
    tide = unfolded(whole[MOVED : MOVED + half], late, 2 << shift)
    rim = whole[MOVED + half : MOVED + half + NP]
    return jnp.concatenate([whole[:MOVED], tide] + spread_out(rim, late, shift), 0)


def spread_out(rim, late, shift):
    parts = []
    for k in range(4):
        first = pltpu.roll(rim, (LANES - (k << shift)) % LANES, 1) if k else rim
        last = pltpu.roll(rim, (3 - k) << shift, 1) if k < 3 else rim
        parts.append(jnp.where(late, first, last))
    return parts


def with_row_rim(whole, sums, top):
    north, south = row_edges(sums)
    rim = jnp.where(top, pltpu.roll(north, RING, 1), pltpu.roll(south, LANES - RING, 1))
    parts = [rim[k * NP : (k + 1) * NP] for k in range(4)]
    lane = lax.broadcasted_iota(i32, (1, LANES), 1)
    spots = []
    for k, part in enumerate(parts):
        first = pltpu.roll(part, k * RING, 1) if k else part
        last = pltpu.roll(part, (LANES - (3 - k) * RING) % LANES, 1) if k < 3 else part
        spots.append(jnp.where(top, first, last))
    rim = one_of_four(spots, (lane >> 2) & 3)
    return jnp.concatenate([whole[: MOVED + NODES // 2 + NP], rim], 0)


def corner_of(whole, start, top):
    lane = lax.broadcasted_iota(i32, (1, LANES), 1)
    base = LANES - start - jnp.where(top != 0, 48, 0)
    whole = jnp.concatenate([whole, jnp.zeros((8 * CORNER_ROWS - whole.shape[0], LANES), f32)], 0)
    out = None
    for k in range(8):
        part = whole[k * CORNER_ROWS : (k + 1) * CORNER_ROWS]
        part = pltpu.roll(part, (base + 16 * k) & (LANES - 1), 1)
        out = part if k == 0 else jnp.where(lane >= 16 * k, part, out)
    return out


def packed(whole):
    second = lax.broadcasted_iota(i32, (1, LANES), 1) >= 64
    top, bottom = whole[:HALF_ROWS], whole[HALF_ROWS:]
    return (
        jnp.where(second, pltpu.roll(bottom, 64, 1), top),
        jnp.where(second, bottom, pltpu.roll(top, 64, 1)),
    )


def unpacked(in0, in1):
    second = lax.broadcasted_iota(i32, (1, LANES), 1) >= 64
    top = jnp.where(second, pltpu.roll(in1, 64, 1), in0)
    bottom = jnp.where(second, in1, pltpu.roll(in0, 64, 1))
    return jnp.concatenate([top, bottom], 0)


def seam_flags(seam_ref, block_cols):
    size_y = seam_ref.shape[1]
    face = lax.axis_index("face")
    blk = lax.axis_index("blk")
    block_x = blk // BY

    def flipped(k):
        return jnp.where(lax.rem(seam_ref[k, 1] - seam_ref[k, 0] + size_y, size_y) != 1, 1, 0)

    first, second = flipped(0), flipped(1)
    east_flip = jnp.where(face == 0, first, second)
    west_flip = jnp.where(face == 0, second, first)
    if block_cols == 1:
        return 1 - east_flip, 0, east_flip, 1
    at_east = jnp.where(block_x == block_cols - 1, east_flip, 0)
    at_west = jnp.where(block_x == 0, west_flip, 0)
    return 1, at_east, 0, at_west


def strips_kernel(block_cols, *refs):
    sources, (out1_ref, out0_ref, stored_ref) = refs[:9], refs[9:12]
    buffers, sems = refs[12:21], refs[21]
    copies = [
        pltpu.make_async_copy(source, buffer, sems.at[k])
        for k, (source, buffer) in enumerate(zip(sources, buffers))
    ]
    for copy in copies:
        copy.start()
    seam_ref, slot_ref, fields_ref, area_ref, depth_ref, spin_ref, tide_ref = buffers[:7]
    table_ref, weight_ref = buffers[7:]
    for copy in copies[:2]:
        copy.wait()
    east0, flip0, east1, flip1 = seam_flags(seam_ref, block_cols)
    lane = lax.broadcasted_iota(i32, (8, 2 * LANES), 1)
    second = (lane & 64) != 0
    place = lane & 63
    row = place >> 2
    row = jnp.where(jnp.where(second, flip1, flip0) != 0, GY - 1 - row, row)
    east = jnp.where(second, east1, east0) != 0
    col = jnp.where(east, GX - RING, 0) + (place & 3)
    col = jnp.where(lane >= LANES, jnp.where(east, GX - RING - 1, RING), col)
    one_hot = by_slot(slot_ref, col * GY + row)
    for copy in copies[2:7]:
        copy.wait()
    stored = stored_rows(fields_ref, (area_ref, depth_ref, spin_ref, tide_ref))
    both = picked(stored, one_hot)

    lane = lax.broadcasted_iota(i32, (1, LANES), 1)
    second = lane >= 64
    flip = jnp.where(second, flip1, flip0) != 0
    sign = jnp.where(flip, -1.0, 1.0)
    node = lax.broadcasted_iota(i32, (1, NP, 1), 1)

    def turned(values):
        shaped = values.reshape(-1, NP, LANES)
        shaped = pltpu.roll(shaped, 4, 1)
        shaped = jnp.where((node & 2) == 0, pltpu.roll(shaped, 6, 1), pltpu.roll(shaped, 2, 1))
        shaped = jnp.where((node & 1) == 0, pltpu.roll(shaped, 7, 1), pltpu.roll(shaped, 1, 1))
        return shaped.reshape(values.shape)

    strip, ring = (
        [part[k * NODES : (k + 1) * NODES] for k in range(ARRAYS)]
        for part in (both[:, :LANES], both[:, LANES:])
    )
    for copy in copies[7:]:
        copy.wait()
    edges = edge_values(table_ref, weight_ref, *ring[:6])
    east = jnp.where(second, east1, east0) != 0
    ends = [jnp.where(east, part[NODES - NP :], part[:NP]) for part in edges]
    ends[2] = ends[2] * sign
    strip[2] = strip[2] * sign
    strip[5] = strip[5] * sign
    for ref, part, flip in zip(
        (out0_ref, out1_ref), packed(strip_rows(strip, east, 0, ends)), (flip0, flip1)
    ):
        if isinstance(flip, int):
            ref[...] = turned(part) if flip else part
        else:
            ref[...] = jnp.where(flip != 0, turned(part), part)
    stored_ref[...] = stored


def rows_kernel(
    block_cols, seam_ref, stored_ref, strip1_ref, strip0_ref, slot_ref, table_ref, weight_ref,
    next_ref, far0_ref, far1_ref, pair_ref, sums,
):
    east0, flip0, east1, flip1 = seam_flags(seam_ref, block_cols)
    odd = lax.axis_index("blk") & 1

    def goes_up(lane):
        return jnp.where((lane & 64) != 0, odd, 1 - odd) != 0

    lane = lax.broadcasted_iota(i32, (8, 2 * LANES), 1)
    up = goes_up(lane)
    row = jnp.where(up, GY - RING, 0) + ((lane & 63) >> 4)
    row = jnp.where(lane >= LANES, jnp.where(up, GY - RING - 1, RING), row)
    both = picked(stored_ref[...], by_slot(slot_ref, (lane & 15) * GY + row))
    rows, behind = (
        [part[k * NODES : (k + 1) * NODES] for k in range(ARRAYS)]
        for part in (both[:, :LANES], both[:, LANES:])
    )
    whole = unpacked(strip0_ref[...], strip1_ref[...])
    strip = [whole[k * NODES : (k + 1) * NODES] for k in range(6)]
    edges = edge_values(table_ref, weight_ref, *map(beside, strip, behind[:6]))
    sums[0] = jnp.concatenate([part[:, :LANES] for part in edges], 0)
    lane = lax.broadcasted_iota(i32, (1, LANES), 1)
    top0, top1 = odd ^ flip0, odd ^ flip1
    whole = with_row_rim(whole, sums, jnp.where(lane >= 64, top1, top0) != 0)
    far0_ref[...] = corner_of(whole, 0, top0)
    far1_ref[...] = corner_of(whole, 64, top1)
    sums[0] = jnp.concatenate([part[:, LANES:] for part in edges], 0)
    up = goes_up(lane)
    rim = jnp.where(up, *row_edges(sums))
    rim = [rim[k * NP : (k + 1) * NP] for k in range(4)]
    pair_ref[...], next_ref[...] = packed(strip_rows(rows, up, 4, rim))


def corners_kernel(in1_ref, in0_ref, pair_ref, table_ref, weight_ref, *refs):
    out_ref, sums = refs[-2:]
    top = 1 - (lax.axis_index("blk") & 1)
    whole = unpacked(in0_ref[...], in1_ref[...])
    parts = [whole[k * NODES : (k + 1) * NODES] for k in range(6)]
    sums[0] = jnp.concatenate(edge_values(table_ref, weight_ref, *parts), 0)
    whole = with_row_rim(whole, sums, jnp.broadcast_to(top != 0, (1, LANES)))
    out_ref[:HALF_ROWS] = pair_ref[...]
    out_ref[HALF_ROWS : HALF_ROWS + CORNER_ROWS] = corner_of(whole, 0, top)
    out_ref[HALF_ROWS + CORNER_ROWS :] = corner_of(whole, 64, top)


def own_kernel(stored_ref, slot_ref, lanes_ref, own_ref, hot_ref):
    one_hot = by_slot(slot_ref, lanes_ref[0:8, :MID])
    own_ref[...] = picked(stored_ref[...], one_hot)
    hot_ref[...] = one_hot.astype(f32).T.astype(bf16)


def first_sums(table, weight, parts, rims, at_rim):
    p, u, v, area, depth, spin, tide = parts
    size = area.shape[1]
    root = jnp.sqrt(area)
    mass = jnp.concatenate([weight] * (size // LANES), 1) * area
    used = [p, u, v, root * depth, root, mass * spin, tide]
    for part, rim in zip(mass_tendency(table, p, u, v, *used[3:6]) + [mass], rims):
        west, east = part[:NP], part[NODES - NP :]
        at_east = jnp.where(at_rim, rim, pltpu.roll(west, size - 1, 1))
        at_west = jnp.where(at_rim, rim, pltpu.roll(east, 1, 1))
        used.append(
            jnp.concatenate([west + at_west, part[NP : NODES - NP], east + at_east], 0)
        )
    return used


def middle_kernel(
    block_cols, seam_ref, in0_ref, in1_ref, own_ref, lanes_ref, table_ref, weight_ref,
    low_ref, centre_ref, high_ref,
):
    east0, flip0, east1, flip1 = seam_flags(seam_ref, block_cols)
    second = lax.broadcasted_iota(i32, (1, LANES), 1) >= 64
    late = jnp.where(second, east1, east0) == 0
    whole = placed_rows(unpacked(in0_ref[...], in1_ref[...]), late, 0)
    side = lanes_ref[16:24, :MID]
    first_at = jnp.where(side == 2, 64 * (1 - east0), 64 * east0)
    place = jnp.where(side == 0, -1, lanes_ref[8:16, :MID] + first_at)
    placed = picked(whole, as_one_hot(place, LANES))
    parts = [
        placed[k * NODES : (k + 1) * NODES] + own_ref[k * NODES : (k + 1) * NODES]
        for k in range(ARRAYS)
    ]
    rims = [placed[ROWS + c * NP : ROWS + (c + 1) * NP] for c in range(4)]
    at_rim = lanes_ref[24:25, LANES : LANES + MID] != 0
    used = first_sums(table_ref[...].astype(bf16), weight_ref[...], parts, rims, at_rim)
    for k, ref in enumerate((low_ref, centre_ref, high_ref)):
        for n, part in enumerate(used):
            ref[n * NODES : (n + 1) * NODES] = part[:, k * LANES : (k + 1) * LANES]


def far_kernel(far1_ref, far0_ref, *refs):
    out_ref = refs[-1]
    out_ref[:CORNER_ROWS] = far0_ref[...]
    out_ref[CORNER_ROWS:] = far1_ref[...]


def steps_kernel(
    block_cols, seam_ref, pair_ref, next_ref, far_ref, low_ref, centre_ref,
    high_ref, hot_ref, table_ref, weight_ref, lanes_ref, out_ref, sums,
):
    east0, flip0, east1, flip1 = seam_flags(seam_ref, block_cols)
    odd = lax.axis_index("blk") & 1
    block_y = lax.rem(lax.axis_index("blk"), BY)

    lane = lax.broadcasted_iota(i32, (1, LANES), 1)
    pair = pair_ref[...]
    late = jnp.where(lane < 64, odd, 1 - odd) != 0
    strips = placed_rows(unpacked(pair[:HALF_ROWS], next_ref[...]), late, 4)
    strips = jnp.concatenate(
        [strips[:ROWS], jnp.zeros((EDGE_ROWS, LANES), f32), strips[ROWS:]], 0
    )
    near = pair[HALF_ROWS:]
    far = far_ref[...]
    sources = (near[:CORNER_ROWS], near[CORNER_ROWS:], far[:CORNER_ROWS], far[CORNER_ROWS:])
    corners = []
    for k in range(8):
        rows = None
        for n, source in enumerate(sources):
            shift = 16 * (n - k) % LANES
            part = pltpu.roll(source, shift, 1) if shift else source
            rows = part if n == 0 else jnp.where(lane >= 16 * n, part, rows)
        corners.append(rows)
    corners = jnp.concatenate(corners, 0)
    rim = MOVED + NODES // 2 + NP
    late = jnp.where((lane & 16) != 0, east1, east0) == 0
    below = jnp.where((lane & 32) != 0, 1 - odd, odd) != 0
    corners = jnp.concatenate(
        [placed_rows(corners, late, 0)] + spread_out(corners[rim : rim + NP], below, 2), 0
    )
    around = jnp.concatenate([strips, corners], 1)
    kind = lanes_ref[40:48, : 2 * LANES]
    sender = jnp.where(lanes_ref[48:56, : 2 * LANES] != 0, odd, 1 - odd)
    strip_at = jnp.where(kind == 3, 16 * (1 - east0), 16 * east0)
    place = lanes_ref[32:40, : 2 * LANES]
    place = place + jnp.where(kind == 1, 64 * sender, 32 * sender + strip_at)
    outer = picked(around, as_one_hot(jnp.where(kind == 0, -1, place), 2 * LANES))
    table = table_ref[...].astype(bf16)
    tiles = (None, low_ref, centre_ref, high_ref, None)
    count = len(tiles)
    masks = [lanes_ref[24:32, k * LANES : (k + 1) * LANES] for k in range(count)]
    closed_above = jnp.where(block_y == BY - 1, masks[-2][1:2], 0) != 0
    closed_below = jnp.where(block_y == 0, masks[1][2:3], 0) != 0
    first_row = masks[0][4:5] != 0
    last_row = masks[-1][5:6] != 0
    outer_used = first_sums(
        table,
        weight_ref[...],
        [outer[k * NODES : (k + 1) * NODES] for k in range(ARRAYS)],
        [outer[ROWS + c * NP : ROWS + (c + 1) * NP] for c in range(4)],
        beside(masks[0][0:1], masks[-1][0:1]) != 0,
    )

    def shifted(parts, by, ring):
        turned = [pltpu.roll(part, -by % LANES, 1) for part in parts]
        size = len(parts)
        step = 1 if by > 0 else -1
        others = [(k + step) % size if ring else min(max(k + step, 0), size - 1) for k in range(size)]
        from_other = lane >= LANES - by if by > 0 else lane < -by
        return [jnp.where(from_other, turned[others[k]], turned[k]) for k in range(size)]

    def put_x_sums(groups, components):
        slots = [k for group in groups for k in group]
        ring = len(slots) < count
        per_tile = [
            [part[:, n * LANES : (n + 1) * LANES] for part in parts]
            for group, parts in zip(groups, components)
            for n in range(len(group))
        ]
        for c in range(3):
            parts = [tile[c] for tile in per_tile]
            west = [part[:NP] for part in parts]
            east = [part[NODES - NP :] for part in parts]
            at_east, at_west = shifted(west, 1, ring), shifted(east, -1, ring)
            for n, k in enumerate(slots):
                sums[k, c * NODES : c * NODES + NP] = west[n] + at_west[n]
                sums[k, c * NODES + NP : (c + 1) * NODES - NP] = parts[n][NP : NODES - NP]
                sums[k, (c + 1) * NODES - NP : (c + 1) * NODES] = east[n] + at_east[n]

    def edge_y(components, slots, rows=None):
        ring = len(slots) < count
        south_at = pl.ds(0, components * NP, stride=NP)
        north_at = pl.ds(NP - 1, components * NP, stride=NP)
        south = [sums[k, south_at] for k in slots]
        north = [sums[k, north_at] for k in slots]
        at_north, at_south = shifted(south, PITCH, ring), shifted(north, -PITCH, ring)
        for n, k in enumerate(slots):
            if k == count - 2:
                at_north[n] = jnp.where(closed_above, 0.0, at_north[n])
            if k == 1:
                at_south[n] = jnp.where(closed_below, 0.0, at_south[n])
        if rows is not None:
            at_south[0] = jnp.where(first_row, rows[0], at_south[0])
            at_north[-1] = jnp.where(last_row, rows[1], at_north[-1])
        for n, k in enumerate(slots):
            sums[k, south_at] = south[n] + at_south[n]
            sums[k, north_at] = north[n] + at_north[n]

    node = lax.broadcasted_iota(i32, (1, NP, 1), 1)
    rows = []
    for rim in (outer[ALL_ROWS:, :LANES], outer[ALL_ROWS:, LANES:]):
        east = pltpu.roll(rim, LANES - 1, 1).reshape(4, NP, LANES)
        west = pltpu.roll(rim, 1, 1).reshape(4, NP, LANES)
        rim = (
            rim.reshape(4, NP, LANES)
            + jnp.where(node == NP - 1, pltpu.roll(east, NP - 1, 1), 0.0)
            + jnp.where(node == 0, pltpu.roll(west, 1, 1), 0.0)
        )
        rows.append(rim.reshape(EDGE_ROWS, LANES))

    every = tuple(range(count))
    groups = (every[0:2], every[2:4], every[4:])

    def tile_part(k, n):
        if tiles[k] is None:
            return outer_used[n][:, :LANES] if k == 0 else outer_used[n][:, LANES:]
        return tiles[k][n * NODES : (n + 1) * NODES]

    def part_of(group, n):
        return jnp.concatenate([tile_part(k, n) for k in group], 1)

    def summed(group, c):
        return jnp.concatenate([sums[k, c * NODES : (c + 1) * NODES] for k in group], 1)

    def average(group, per_mass):
        return [summed(group, c) * per_mass for c in range(3)]

    def laplace(s):
        return [
            dot(table[4 * NODES :, : 3 * NODES], jnp.concatenate(high_low_high(part), 0))
            for part in s
        ]

    start = [[part_of(group, n) for n in range(3)] for group in groups]
    fixed = [[part_of(group, n) for n in range(3, 6)] for group in groups]
    for k in every:
        for c in range(4):
            sums[k, c * NODES : (c + 1) * NODES] = tile_part(k, 7 + c)
    edge_y(4, every, rows)
    per_mass = [1.0 / summed(group, 3) for group in groups]
    one = []
    for n, group in enumerate(groups):
        change = average(group, per_mass[n])
        one.append([s + time_step * c for s, c in zip(start[n], change)])
    put_x_sums(groups, [mass_tendency(table, *s, *f) for s, f in zip(one, fixed)])
    edge_y(3, every)
    two = []
    for n, group in enumerate(groups):
        change = average(group, per_mass[n])
        two.append(
            [0.75 * s + 0.25 * (o + time_step * c) for s, o, c in zip(start[n], one[n], change)]
        )
    put_x_sums(groups, [mass_tendency(table, *s, *f) for s, f in zip(two, fixed)])
    edge_y(3, every)

    def regrouped(per_group):
        (outer_low, high_above) = per_group[0], per_group[1]
        below, low = outer_low[:, :LANES], outer_low[:, LANES:]
        centre, high = high_above[:, :LANES], high_above[:, LANES:]
        near = jnp.where(lane < LANES // 2, per_group[2], below)
        return [beside(low, centre), beside(high, near)]

    def of_groups(values):
        return [list(parts) for parts in zip(*(regrouped(part) for part in zip(*values)))]

    for c in range(3):
        rows_at = slice(c * NODES, (c + 1) * NODES)
        sums[count - 1, rows_at] = jnp.where(
            lane < LANES // 2, sums[count - 1, rows_at], sums[0, rows_at]
        )
    slots = every[1:]
    groups = (slots[0:2], slots[2:4])
    start, two = of_groups(start), of_groups(two)
    tide = regrouped([part_of(every[0:2], 6), part_of(every[2:4], 6), part_of(every[4:], 6)])
    per_mass = regrouped(per_mass)
    three = []
    for n, group in enumerate(groups):
        change = average(group, per_mass[n])
        now = [
            s / 3.0 + 2.0 / 3.0 * (o + time_step * c)
            for s, o, c in zip(start[n], two[n], change)
        ]
        now[0] = now[0] + tide[n]
        three.append(now)
    put_x_sums(groups, [laplace(s) for s in three])
    edge_y(3, slots)
    change = [average(group, per_mass[n]) for n, group in enumerate(groups)]
    put_x_sums(groups, [laplace(s) for s in change])
    edge_y(3, slots)
    stepped = []
    for n, group in enumerate(groups):
        change = average(group, per_mass[n])
        now = [s - time_step * hyper_coeff * b for s, b in zip(three[n], change)]
        stepped.append(jnp.concatenate(now, 0))
    stepped = jnp.concatenate(stepped, 1)[:, :MID]
    own = lanes_ref[27:28, LANES : LANES + MID] != 0
    stored = picked(jnp.where(own, stepped, 0.0), hot_ref[...])
    out_ref[...] = stored.reshape(out_ref.shape)


def on_device(fields, jacobian, water_depth, coriolis, tide_height, slot_of, seam_rows):
    block_cols = lax.axis_size("blk") // BY
    table, weight = operator_table()
    table, weight, lanes = map(jnp.asarray, (table, weight, lane_tables()))
    vmem = pl.BlockSpec(memory_space=pltpu.VMEM)
    smem = pl.BlockSpec(memory_space=pltpu.SMEM)
    hbm = pl.BlockSpec(memory_space=pltpu.HBM)
    params = pltpu.CompilerParams(vmem_limit_bytes=48 * 2**20)
    held = (fields, jacobian, water_depth, coriolis, tide_height)

    def call(kernel, ins, outs, cost, scratch=(), name=None):
        return pl.pallas_call(
            kernel,
            out_shape=[jax.ShapeDtypeStruct(*out) for out in outs],
            in_specs=[spec for spec, value in ins],
            out_specs=[vmem] * len(outs),
            scratch_shapes=list(scratch),
            compiler_params=params,
            cost_estimate=pl.CostEstimate(
                flops=cost, bytes_accessed=2 * 2**20, transcendentals=0
            ),
            name=name,
        )(
            *[
                pltpu.with_memory_space_constraint(value, pltpu.HBM) if spec is hbm else value
                for spec, value in ins
            ]
        )

    strip = ((HALF_ROWS, LANES), f32)
    def room(values, spaces=None):
        spaces = spaces or [pltpu.VMEM] * len(values)
        buffers = [space(x.shape, x.dtype) for space, x in zip(spaces, values)]
        return buffers + [pltpu.SemaphoreType.DMA((len(values),))]

    needed = (seam_rows, slot_of, *held, table, weight)
    corner = ((CORNER_ROWS, LANES), f32)
    scratch = [pltpu.VMEM((1, 4 * NODES, LANES), f32)]
    strip1, strip0, stored = call(
        functools.partial(strips_kernel, block_cols),
        [(hbm, x) for x in needed],
        [strip, strip, ((ROWS, ELEMENTS), f32)],
        10**8,
        scratch=room(needed, [pltpu.SMEM] + [pltpu.VMEM] * (len(needed) - 1)),
        name="strips",
    )
    to_next, far0, far1, to_pair = call(
        functools.partial(rows_kernel, block_cols),
        [(smem, seam_rows)]
        + [(vmem, x) for x in (stored, strip1, strip0, slot_of, table, weight)],
        [strip, corner, corner, strip],
        10**8,
        scratch=scratch,
        name="rows",
    )
    span = block_cols * BY
    both = ("face", "blk")
    places = [(f, x, y) for f in range(2) for x in range(block_cols) for y in range(BY)]

    def rank(face, block_x, block_y):
        return face * span + block_x * BY + block_y

    def same(y):
        return y

    def in_pair(y):
        return y ^ 1

    def next_pair(y):
        other = y + 1 if y % 2 else y - 1
        return other if 0 <= other < BY else y

    def swapped(value, partner):
        pairs = [
            (rank(f, x, y), rank(f if partner(y) != y else 1 - f, x, partner(y)))
            for f, x, y in places
        ]
        return lax.ppermute(value, both, pairs)

    def across(value0, value1, partner):
        last = block_cols - 1

        def aligned(y):
            return partner is same or partner(y) != y

        straight = {
            (f, x, y): (f, x + 1, partner(y)) if x < last else (1 - f, 0, partner(y))
            for f, x, y in places
        }
        turned = {
            (f, last, y): (1 - f, 0, BY - 1 - partner(y) if aligned(y) else y)
            for f in range(2)
            for y in range(BY)
        }

        def eastward(value, pairs):
            return lax.ppermute(value, both, [(rank(*a), rank(*b)) for a, b in pairs.items()])

        def westward(value, pairs):
            return lax.ppermute(value, both, [(rank(*b), rank(*a)) for a, b in pairs.items()])

        if block_cols == 1:
            return eastward(value0, straight), eastward(value1, turned)
        flipped = (seam_rows[:, 1] - seam_rows[:, 0]) % seam_rows.shape[1] != 1
        face = lax.axis_index("face")
        block_x = lax.axis_index("blk") // BY
        return (
            jnp.where(
                (block_x == last) & flipped[face],
                westward(value1, turned),
                westward(value1, straight),
            ),
            jnp.where(
                (block_x == 0) & flipped[1 - face],
                eastward(value0, turned),
                eastward(value0, straight),
            ),
        )

    halo0, halo1 = across(strip0, strip1, same)
    far0, far1 = across(far0, far1, next_pair)
    from_next = swapped(to_next, next_pair)
    own, hot = call(
        own_kernel,
        [(vmem, x) for x in (stored, slot_of, lanes)],
        [((ROWS, MID), f32), ((MID, ELEMENTS), bf16)],
        10**8,
        name="own",
    )
    (to_pair,) = call(
        corners_kernel,
        [(vmem, x) for x in (halo1, halo0, to_pair, table, weight, hot)],
        [((HALF_ROWS + 2 * CORNER_ROWS, LANES), f32)],
        10**8,
        scratch=scratch,
        name="corners",
    )
    from_pair = swapped(to_pair, in_pair)
    tile = ((11 * NODES, LANES), f32)
    low, centre, high = call(
        functools.partial(middle_kernel, block_cols),
        [(smem, seam_rows)] + [(vmem, x) for x in (halo0, halo1, own, lanes, table, weight)],
        [tile, tile, tile],
        10**8,
        name="middle",
    )
    (far,) = call(
        far_kernel,
        [(vmem, x) for x in (far1, far0, from_next, low)],
        [((2 * CORNER_ROWS, LANES), f32)],
        10**11,
        name="far",
    )
    (stepped,) = call(
        functools.partial(steps_kernel, block_cols),
        [(smem, seam_rows)]
        + [
            (vmem, x)
            for x in (
                from_pair, from_next, far, low, centre, high,
                hot, table, weight, lanes,
            )
        ],
        [(fields.shape, f32)],
        10**8,
        scratch=[pltpu.VMEM((EXT // LANES, 4 * NODES, LANES), f32)],
        name="steps",
    )
    return stepped


def solution(mesh):
    return jax.shard_map(
        on_device,
        mesh=mesh,
        in_specs=(
            P(None, None, None, ("face", "blk")),
            P(None, None, ("face", "blk")),
            P(None, None, ("face", "blk")),
            P(None, None, ("face", "blk")),
            P(None, None, ("face", "blk")),
            P(("face", "blk"), None),
            P(),
        ),
        out_specs=P(None, None, None, ("face", "blk")),
        check_vma=False,
    )
```

```python
import functools
import math

import jax
import jax.numpy as jnp
import ml_dtypes
import numpy as np
from jax import lax
from jax.experimental import pallas as pl
from jax.experimental.pallas import tpu as pltpu
from jax.sharding import PartitionSpec as P

BY = 16
GX = 16
GY = 16
NP = 8
NODES = NP * NP
ARRAYS = 7
ROWS = ARRAYS * NODES
MOVED = 6 * NODES
EDGE_ROWS = 4 * NP
ALL_ROWS = ROWS + EDGE_ROWS
HALF_ROWS = (MOVED + NODES // 2 + 2 * NP) // 2
RING = 4
RIM_ROWS = ROWS + 2 * EDGE_ROWS
CORNER_ROWS = (MOVED + NODES // 2 + 4 * NP) // 8
PITCH = GX + 2 * RING
MID = GY * PITCH
LANES = 128
EXT = MID + 2 * LANES
LEAD = LANES - RING * PITCH
ELEMENTS = GX * GY

time_step = 0.03
hyper_coeff = 0.0002

f32 = jnp.float32
bf16 = jnp.bfloat16
i32 = jnp.int32


def legendre_pair(location, degree):
    lower_value = 1.0
    upper_value = location
    for polynomial_order in range(2, degree + 1):
        lower_value, upper_value = (
            upper_value,
            (
                (2 * polynomial_order - 1) * location * upper_value
                - (polynomial_order - 1) * lower_value
            )
            / polynomial_order,
        )
    return (lower_value, upper_value)


def gll_tables(points):
    degree = points - 1
    locations = [-math.cos(math.pi * position / degree) for position in range(points)]
    for iteration in range(100):
        updated = []
        for location in locations:
            lower_value, upper_value = legendre_pair(location, degree)
            updated.append(
                location - (location * upper_value - lower_value) / ((degree + 1) * upper_value)
            )
        locations = updated
    locations[0] = -1.0
    locations[degree] = 1.0
    legendre_at = [legendre_pair(location, degree)[1] for location in locations]
    weights = [2.0 / (degree * (degree + 1) * value * value) for value in legendre_at]
    corner_value = degree * (degree + 1) / 4.0
    derivative = []
    for row_index in range(points):
        row_values = []
        for column_index in range(points):
            if row_index != column_index:
                row_values.append(
                    legendre_at[row_index]
                    / (legendre_at[column_index] * (locations[row_index] - locations[column_index]))
                )
            elif row_index == 0:
                row_values.append(-corner_value)
            elif row_index == degree:
                row_values.append(corner_value)
            else:
                row_values.append(0.0)
        derivative.append(row_values)
    return np.asarray(weights, np.float64), np.asarray(derivative, np.float64)


def in_three(matrix):
    high = matrix.astype(ml_dtypes.bfloat16)
    low = (matrix - high.astype(np.float64)).astype(ml_dtypes.bfloat16)
    return np.concatenate([high, high, low], 1)


def operator_table():
    weights, derivative = gll_tables(NP)
    eye = np.eye(NP)
    node_weight = np.outer(weights, weights).reshape(NODES, 1)
    along_x = node_weight * np.kron(derivative, eye)
    along_y = node_weight * np.kron(eye, derivative)
    second = derivative @ derivative
    both = node_weight * (np.kron(second, eye) + np.kron(eye, second))
    table = np.zeros((5 * NODES, 4 * NODES), ml_dtypes.bfloat16)
    table[:NODES, : 3 * NODES] = in_three(along_x)
    table[NODES : 2 * NODES, : 3 * NODES] = in_three(along_y)
    flux = [in_three(along_x), in_three(along_y)]
    for k, part in enumerate(flux):
        at = 2 * k * NODES
        table[2 * NODES : 3 * NODES, at : at + 2 * NODES] = part[:, : 2 * NODES]
        table[3 * NODES : 4 * NODES, at : at + NODES] = part[:, 2 * NODES :]
    table[4 * NODES :, : 3 * NODES] = in_three(both)
    spread = np.broadcast_to(node_weight, (NODES, LANES)).astype(np.float32)
    return table.astype(np.float32), np.ascontiguousarray(spread)


def lane_tables():
    table = np.zeros((24, MID), np.int32)
    for lane in range(MID):
        row, col = divmod(lane, PITCH)
        x = col - RING
        own = 0 <= x < GX
        table[0:8, lane] = x * GY + row if own else -1
        if not own:
            table[8:16, lane] = row * RING + (col if x < 0 else x - GX)
        table[16:24, lane] = 0 if own else (1 if x < 0 else 2)
    ext = np.zeros((8, EXT), np.int32)
    outer = np.zeros((24, 2 * LANES), np.int32)
    for lane in range(EXT):
        row, col = divmod(lane - LEAD, PITCH)
        y = row - RING
        x = col - RING
        inside = 0 <= row < GY + 2 * RING
        ext[0, lane] = x in (-RING, GX + RING - 1)
        ext[1, lane] = y == GY - 1
        ext[2, lane] = y == 0
        ext[3, lane] = 0 <= y < GY and 0 <= x < GX
        ext[4, lane] = y == -RING
        ext[5, lane] = y == GY + RING - 1
        if inside and not 0 <= y < GY:
            place = lane if y < 0 else lane - LANES - MID + LANES
            step = y + RING if y < 0 else y - GY
            if 0 <= x < GX:
                outer[0:8, place] = step * GX + x
                outer[8:16, place] = 1
            else:
                outer[0:8, place] = LANES + step * RING + (x + RING if x < 0 else x - GX)
                outer[8:16, place] = 2 if x < 0 else 3
            outer[16:24, place] = y > 0
    whole = np.zeros((56, EXT), np.int32)
    whole[0:24, :MID] = table
    whole[24:32] = ext
    whole[32:56, : 2 * LANES] = outer
    return whole


def dot(a, b):
    return jnp.dot(a, b, preferred_element_type=f32)


def picked(values, one_hot):
    high = values.astype(bf16)
    low = (values - high.astype(f32)).astype(bf16)
    both = dot(jnp.concatenate([high, low], 0), one_hot)
    return both[: values.shape[0]] + both[values.shape[0] :]


def as_one_hot(row_of_lane, depth):
    index = lax.broadcasted_iota(i32, (depth, row_of_lane.shape[1]), 0)
    return jnp.where(index == row_of_lane[0:1], 1.0, 0.0).astype(bf16)


def high_low_high(values):
    high = values.astype(bf16)
    low = (values - high.astype(f32)).astype(bf16)
    return [high, low, high]


def by_slot(slot_ref, cell_of_lane):
    size = cell_of_lane.shape[1]
    halves = [
        jnp.broadcast_to(slot_ref[:, k * LANES : (k + 1) * LANES], (8, LANES)) for k in range(2)
    ]
    chosen = []
    for k in range(size // LANES):
        cell = cell_of_lane[:, k * LANES : (k + 1) * LANES]
        low, high = (jnp.take_along_axis(half, cell & (LANES - 1), axis=1) for half in halves)
        chosen.append(jnp.where(cell < 0, -1, jnp.where(cell < LANES, low, high)))
    return as_one_hot(jnp.concatenate(chosen, 1), ELEMENTS)


def stored_rows(fields_ref, others):
    fields = fields_ref[...].reshape(3 * NODES, ELEMENTS)
    others = [ref[...].reshape(NODES, ELEMENTS) for ref in others]
    return jnp.concatenate([fields[:NODES] - others[-1], fields[NODES:]] + others, 0)


def mass_tendency(table, p, u, v, area_depth, weighted_area, spin):
    slopes = dot(table[: 2 * NODES, : 3 * NODES], jnp.concatenate(high_low_high(p), 0))
    flux = high_low_high(area_depth * u)[:2] + high_low_high(area_depth * v)[:2]
    spread = dot(table[2 * NODES : 4 * NODES], jnp.concatenate(flux, 0))
    return [
        -(spread[:NODES] + spread[NODES:]),
        spin * v - weighted_area * slopes[:NODES],
        -spin * u - weighted_area * slopes[NODES:],
    ]


def edge_values(table_ref, weight_ref, p, u, v, area, depth, spin):
    root = jnp.sqrt(area)
    mass = jnp.concatenate([weight_ref[...]] * (area.shape[1] // LANES), 1) * area
    table = table_ref[...].astype(bf16)
    return mass_tendency(table, p, u, v, root * depth, root, mass * spin) + [mass]


def row_edges(sums):
    return tuple(sums[0, pl.ds(j, EDGE_ROWS, stride=NP)] for j in (NP - 1, 0))


def beside(left, right):
    return jnp.concatenate([left, right], 1)


def one_of_four(parts, index):
    out = parts[0]
    for k in range(1, 4):
        out = jnp.where(index == k, parts[k], out)
    return out


def folded(tide, kept, late, step):
    half = NODES // 2
    back = pltpu.roll(tide[half:], LANES - step, 1)
    onward = pltpu.roll(tide[half:], step, 1)
    return jnp.where(kept, tide[:half], jnp.where(late, back, onward))


def unfolded(rows, late, step):
    back = pltpu.roll(rows, LANES - step, 1)
    onward = pltpu.roll(rows, step, 1)
    return jnp.concatenate([rows, jnp.where(late, onward, back)], 0)


def strip_rows(parts, late, shift, rims):
    lane = lax.broadcasted_iota(i32, (1, LANES), 1)
    index = (lane >> shift) & 3
    kept = jnp.where(late, index // 2, 1 - index // 2) != 0
    tide = folded(parts[6], kept, late, 2 << shift)
    rim = one_of_four(rims, index)
    return jnp.concatenate(parts[:6] + [tide, rim, jnp.zeros_like(rim)], 0)


def placed_rows(whole, late, shift):
    half = NODES // 2
    tide = unfolded(whole[MOVED : MOVED + half], late, 2 << shift)
    rim = whole[MOVED + half : MOVED + half + NP]
    return jnp.concatenate([whole[:MOVED], tide] + spread_out(rim, late, shift), 0)


def spread_out(rim, late, shift):
    parts = []
    for k in range(4):
        first = pltpu.roll(rim, (LANES - (k << shift)) % LANES, 1) if k else rim
        last = pltpu.roll(rim, (3 - k) << shift, 1) if k < 3 else rim
        parts.append(jnp.where(late, first, last))
    return parts


def with_row_rim(whole, sums, top):
    north, south = row_edges(sums)
    rim = jnp.where(top, pltpu.roll(north, RING, 1), pltpu.roll(south, LANES - RING, 1))
    parts = [rim[k * NP : (k + 1) * NP] for k in range(4)]
    lane = lax.broadcasted_iota(i32, (1, LANES), 1)
    spots = []
    for k, part in enumerate(parts):
        first = pltpu.roll(part, k * RING, 1) if k else part
        last = pltpu.roll(part, (LANES - (3 - k) * RING) % LANES, 1) if k < 3 else part
        spots.append(jnp.where(top, first, last))
    rim = one_of_four(spots, (lane >> 2) & 3)
    return jnp.concatenate([whole[: MOVED + NODES // 2 + NP], rim], 0)


def corner_of(whole, start, top):
    lane = lax.broadcasted_iota(i32, (1, LANES), 1)
    base = LANES - start - jnp.where(top != 0, 48, 0)
    whole = jnp.concatenate([whole, jnp.zeros((8 * CORNER_ROWS - whole.shape[0], LANES), f32)], 0)
    out = None
    for k in range(8):
        part = whole[k * CORNER_ROWS : (k + 1) * CORNER_ROWS]
        part = pltpu.roll(part, (base + 16 * k) & (LANES - 1), 1)
        out = part if k == 0 else jnp.where(lane >= 16 * k, part, out)
    return out


def packed(whole):
    second = lax.broadcasted_iota(i32, (1, LANES), 1) >= 64
    top, bottom = whole[:HALF_ROWS], whole[HALF_ROWS:]
    return (
        jnp.where(second, pltpu.roll(bottom, 64, 1), top),
        jnp.where(second, bottom, pltpu.roll(top, 64, 1)),
    )


def unpacked(in0, in1):
    second = lax.broadcasted_iota(i32, (1, LANES), 1) >= 64
    top = jnp.where(second, pltpu.roll(in1, 64, 1), in0)
    bottom = jnp.where(second, in1, pltpu.roll(in0, 64, 1))
    return jnp.concatenate([top, bottom], 0)


def seam_flags(seam_ref, block_cols):
    size_y = seam_ref.shape[1]
    face = lax.axis_index("face")
    blk = lax.axis_index("blk")
    block_x = blk // BY

    def flipped(k):
        return jnp.where(lax.rem(seam_ref[k, 1] - seam_ref[k, 0] + size_y, size_y) != 1, 1, 0)

    first, second = flipped(0), flipped(1)
    east_flip = jnp.where(face == 0, first, second)
    west_flip = jnp.where(face == 0, second, first)
    if block_cols == 1:
        return 1 - east_flip, 0, east_flip, 1
    at_east = jnp.where(block_x == block_cols - 1, east_flip, 0)
    at_west = jnp.where(block_x == 0, west_flip, 0)
    return 1, at_east, 0, at_west


def strips_kernel(block_cols, *refs):
    sources, (out1_ref, out0_ref, stored_ref) = refs[:9], refs[9:12]
    buffers, sems = refs[12:21], refs[21]
    copies = [
        pltpu.make_async_copy(source, buffer, sems.at[k])
        for k, (source, buffer) in enumerate(zip(sources, buffers))
    ]
    for copy in copies:
        copy.start()
    seam_ref, slot_ref, fields_ref, area_ref, depth_ref, spin_ref, tide_ref = buffers[:7]
    table_ref, weight_ref = buffers[7:]
    for copy in copies[:2]:
        copy.wait()
    east0, flip0, east1, flip1 = seam_flags(seam_ref, block_cols)
    lane = lax.broadcasted_iota(i32, (8, 2 * LANES), 1)
    second = (lane & 64) != 0
    place = lane & 63
    row = place >> 2
    row = jnp.where(jnp.where(second, flip1, flip0) != 0, GY - 1 - row, row)
    east = jnp.where(second, east1, east0) != 0
    col = jnp.where(east, GX - RING, 0) + (place & 3)
    col = jnp.where(lane >= LANES, jnp.where(east, GX - RING - 1, RING), col)
    one_hot = by_slot(slot_ref, col * GY + row)
    for copy in copies[2:7]:
        copy.wait()
    stored = stored_rows(fields_ref, (area_ref, depth_ref, spin_ref, tide_ref))
    both = picked(stored, one_hot)

    lane = lax.broadcasted_iota(i32, (1, LANES), 1)
    second = lane >= 64
    flip = jnp.where(second, flip1, flip0) != 0
    sign = jnp.where(flip, -1.0, 1.0)
    node = lax.broadcasted_iota(i32, (1, NP, 1), 1)

    def turned(values):
        shaped = values.reshape(-1, NP, LANES)
        shaped = pltpu.roll(shaped, 4, 1)
        shaped = jnp.where((node & 2) == 0, pltpu.roll(shaped, 6, 1), pltpu.roll(shaped, 2, 1))
        shaped = jnp.where((node & 1) == 0, pltpu.roll(shaped, 7, 1), pltpu.roll(shaped, 1, 1))
        return shaped.reshape(values.shape)

    strip, ring = (
        [part[k * NODES : (k + 1) * NODES] for k in range(ARRAYS)]
        for part in (both[:, :LANES], both[:, LANES:])
    )
    for copy in copies[7:]:
        copy.wait()
    edges = edge_values(table_ref, weight_ref, *ring[:6])
    east = jnp.where(second, east1, east0) != 0
    ends = [jnp.where(east, part[NODES - NP :], part[:NP]) for part in edges]
    ends[2] = ends[2] * sign
    strip[2] = strip[2] * sign
    strip[5] = strip[5] * sign
    for ref, part, flip in zip(
        (out0_ref, out1_ref), packed(strip_rows(strip, east, 0, ends)), (flip0, flip1)
    ):
        if isinstance(flip, int):
            ref[...] = turned(part) if flip else part
        else:
            ref[...] = jnp.where(flip != 0, turned(part), part)
    stored_ref[...] = stored


def rows_kernel(
    block_cols, seam_ref, stored_ref, strip1_ref, strip0_ref, slot_ref, table_ref, weight_ref,
    next_ref, far0_ref, far1_ref, pair_ref, sums,
):
    east0, flip0, east1, flip1 = seam_flags(seam_ref, block_cols)
    odd = lax.axis_index("blk") & 1

    def goes_up(lane):
        return jnp.where((lane & 64) != 0, odd, 1 - odd) != 0

    lane = lax.broadcasted_iota(i32, (8, 2 * LANES), 1)
    up = goes_up(lane)
    row = jnp.where(up, GY - RING, 0) + ((lane & 63) >> 4)
    row = jnp.where(lane >= LANES, jnp.where(up, GY - RING - 1, RING), row)
    both = picked(stored_ref[...], by_slot(slot_ref, (lane & 15) * GY + row))
    rows, behind = (
        [part[k * NODES : (k + 1) * NODES] for k in range(ARRAYS)]
        for part in (both[:, :LANES], both[:, LANES:])
    )
    whole = unpacked(strip0_ref[...], strip1_ref[...])
    strip = [whole[k * NODES : (k + 1) * NODES] for k in range(6)]
    edges = edge_values(table_ref, weight_ref, *map(beside, strip, behind[:6]))
    sums[0] = jnp.concatenate([part[:, :LANES] for part in edges], 0)
    lane = lax.broadcasted_iota(i32, (1, LANES), 1)
    top0, top1 = odd ^ flip0, odd ^ flip1
    whole = with_row_rim(whole, sums, jnp.where(lane >= 64, top1, top0) != 0)
    far0_ref[...] = corner_of(whole, 0, top0)
    far1_ref[...] = corner_of(whole, 64, top1)
    sums[0] = jnp.concatenate([part[:, LANES:] for part in edges], 0)
    up = goes_up(lane)
    rim = jnp.where(up, *row_edges(sums))
    rim = [rim[k * NP : (k + 1) * NP] for k in range(4)]
    pair_ref[...], next_ref[...] = packed(strip_rows(rows, up, 4, rim))


def corners_kernel(in0_ref, in1_ref, pair_ref, table_ref, weight_ref, *refs):
    out_ref, sums = refs[-2:]
    top = 1 - (lax.axis_index("blk") & 1)
    whole = unpacked(in0_ref[...], in1_ref[...])
    parts = [whole[k * NODES : (k + 1) * NODES] for k in range(6)]
    sums[0] = jnp.concatenate(edge_values(table_ref, weight_ref, *parts), 0)
    whole = with_row_rim(whole, sums, jnp.broadcast_to(top != 0, (1, LANES)))
    out_ref[:HALF_ROWS] = pair_ref[...]
    out_ref[HALF_ROWS : HALF_ROWS + CORNER_ROWS] = corner_of(whole, 0, top)
    out_ref[HALF_ROWS + CORNER_ROWS :] = corner_of(whole, 64, top)


def own_kernel(stored_ref, slot_ref, lanes_ref, own_ref, hot_ref):
    one_hot = by_slot(slot_ref, lanes_ref[0:8, :MID])
    own_ref[...] = picked(stored_ref[...], one_hot)
    hot_ref[...] = one_hot.astype(f32).T.astype(bf16)


def first_sums(table, weight, parts, rims, at_rim):
    p, u, v, area, depth, spin, tide = parts
    size = area.shape[1]
    root = jnp.sqrt(area)
    mass = jnp.concatenate([weight] * (size // LANES), 1) * area
    used = [p, u, v, root * depth, root, mass * spin, tide]
    for part, rim in zip(mass_tendency(table, p, u, v, *used[3:6]) + [mass], rims):
        west, east = part[:NP], part[NODES - NP :]
        at_east = jnp.where(at_rim, rim, pltpu.roll(west, size - 1, 1))
        at_west = jnp.where(at_rim, rim, pltpu.roll(east, 1, 1))
        used.append(
            jnp.concatenate([west + at_west, part[NP : NODES - NP], east + at_east], 0)
        )
    return used


def middle_kernel(
    block_cols, seam_ref, in0_ref, in1_ref, own_ref, lanes_ref, table_ref, weight_ref,
    low_ref, centre_ref, high_ref,
):
    east0, flip0, east1, flip1 = seam_flags(seam_ref, block_cols)
    second = lax.broadcasted_iota(i32, (1, LANES), 1) >= 64
    late = jnp.where(second, east1, east0) == 0
    whole = placed_rows(unpacked(in0_ref[...], in1_ref[...]), late, 0)
    side = lanes_ref[16:24, :MID]
    first_at = jnp.where(side == 2, 64 * (1 - east0), 64 * east0)
    place = jnp.where(side == 0, -1, lanes_ref[8:16, :MID] + first_at)
    placed = picked(whole, as_one_hot(place, LANES))
    parts = [
        placed[k * NODES : (k + 1) * NODES] + own_ref[k * NODES : (k + 1) * NODES]
        for k in range(ARRAYS)
    ]
    rims = [placed[ROWS + c * NP : ROWS + (c + 1) * NP] for c in range(4)]
    at_rim = lanes_ref[24:25, LANES : LANES + MID] != 0
    used = first_sums(table_ref[...].astype(bf16), weight_ref[...], parts, rims, at_rim)
    for k, ref in enumerate((low_ref, centre_ref, high_ref)):
        for n, part in enumerate(used):
            ref[n * NODES : (n + 1) * NODES] = part[:, k * LANES : (k + 1) * LANES]


def far_kernel(far1_ref, far0_ref, *refs):
    out_ref = refs[-1]
    out_ref[:CORNER_ROWS] = far0_ref[...]
    out_ref[CORNER_ROWS:] = far1_ref[...]


def steps_kernel(
    block_cols, seam_ref, pair_ref, next_ref, far_ref, low_ref, centre_ref,
    high_ref, hot_ref, table_ref, weight_ref, lanes_ref, out_ref, sums,
):
    east0, flip0, east1, flip1 = seam_flags(seam_ref, block_cols)
    odd = lax.axis_index("blk") & 1
    block_y = lax.rem(lax.axis_index("blk"), BY)

    lane = lax.broadcasted_iota(i32, (1, LANES), 1)
    pair = pair_ref[...]
    late = jnp.where(lane < 64, odd, 1 - odd) != 0
    strips = placed_rows(unpacked(pair[:HALF_ROWS], next_ref[...]), late, 4)
    strips = jnp.concatenate(
        [strips[:ROWS], jnp.zeros((EDGE_ROWS, LANES), f32), strips[ROWS:]], 0
    )
    near = pair[HALF_ROWS:]
    far = far_ref[...]
    sources = (near[:CORNER_ROWS], near[CORNER_ROWS:], far[:CORNER_ROWS], far[CORNER_ROWS:])
    corners = []
    for k in range(8):
        rows = None
        for n, source in enumerate(sources):
            shift = 16 * (n - k) % LANES
            part = pltpu.roll(source, shift, 1) if shift else source
            rows = part if n == 0 else jnp.where(lane >= 16 * n, part, rows)
        corners.append(rows)
    corners = jnp.concatenate(corners, 0)
    rim = MOVED + NODES // 2 + NP
    late = jnp.where((lane & 16) != 0, east1, east0) == 0
    below = jnp.where((lane & 32) != 0, 1 - odd, odd) != 0
    corners = jnp.concatenate(
        [placed_rows(corners, late, 0)] + spread_out(corners[rim : rim + NP], below, 2), 0
    )
    around = jnp.concatenate([strips, corners], 1)
    kind = lanes_ref[40:48, : 2 * LANES]
    sender = jnp.where(lanes_ref[48:56, : 2 * LANES] != 0, odd, 1 - odd)
    strip_at = jnp.where(kind == 3, 16 * (1 - east0), 16 * east0)
    place = lanes_ref[32:40, : 2 * LANES]
    place = place + jnp.where(kind == 1, 64 * sender, 32 * sender + strip_at)
    outer = picked(around, as_one_hot(jnp.where(kind == 0, -1, place), 2 * LANES))
    table = table_ref[...].astype(bf16)
    tiles = (None, low_ref, centre_ref, high_ref, None)
    count = len(tiles)
    masks = [lanes_ref[24:32, k * LANES : (k + 1) * LANES] for k in range(count)]
    closed_above = jnp.where(block_y == BY - 1, masks[-2][1:2], 0) != 0
    closed_below = jnp.where(block_y == 0, masks[1][2:3], 0) != 0
    first_row = masks[0][4:5] != 0
    last_row = masks[-1][5:6] != 0
    outer_used = first_sums(
        table,
        weight_ref[...],
        [outer[k * NODES : (k + 1) * NODES] for k in range(ARRAYS)],
        [outer[ROWS + c * NP : ROWS + (c + 1) * NP] for c in range(4)],
        beside(masks[0][0:1], masks[-1][0:1]) != 0,
    )

    def shifted(parts, by, ring):
        turned = [pltpu.roll(part, -by % LANES, 1) for part in parts]
        size = len(parts)
        step = 1 if by > 0 else -1
        others = [(k + step) % size if ring else min(max(k + step, 0), size - 1) for k in range(size)]
        from_other = lane >= LANES - by if by > 0 else lane < -by
        return [jnp.where(from_other, turned[others[k]], turned[k]) for k in range(size)]

    def put_x_sums(groups, components):
        slots = [k for group in groups for k in group]
        ring = len(slots) < count
        per_tile = [
            [part[:, n * LANES : (n + 1) * LANES] for part in parts]
            for group, parts in zip(groups, components)
            for n in range(len(group))
        ]
        for c in range(3):
            parts = [tile[c] for tile in per_tile]
            west = [part[:NP] for part in parts]
            east = [part[NODES - NP :] for part in parts]
            at_east, at_west = shifted(west, 1, ring), shifted(east, -1, ring)
            for n, k in enumerate(slots):
                sums[k, c * NODES : c * NODES + NP] = west[n] + at_west[n]
                sums[k, c * NODES + NP : (c + 1) * NODES - NP] = parts[n][NP : NODES - NP]
                sums[k, (c + 1) * NODES - NP : (c + 1) * NODES] = east[n] + at_east[n]

    def edge_y(components, slots, rows=None):
        ring = len(slots) < count
        south_at = pl.ds(0, components * NP, stride=NP)
        north_at = pl.ds(NP - 1, components * NP, stride=NP)
        south = [sums[k, south_at] for k in slots]
        north = [sums[k, north_at] for k in slots]
        at_north, at_south = shifted(south, PITCH, ring), shifted(north, -PITCH, ring)
        for n, k in enumerate(slots):
            if k == count - 2:
                at_north[n] = jnp.where(closed_above, 0.0, at_north[n])
            if k == 1:
                at_south[n] = jnp.where(closed_below, 0.0, at_south[n])
        if rows is not None:
            at_south[0] = jnp.where(first_row, rows[0], at_south[0])
            at_north[-1] = jnp.where(last_row, rows[1], at_north[-1])
        for n, k in enumerate(slots):
            sums[k, south_at] = south[n] + at_south[n]
            sums[k, north_at] = north[n] + at_north[n]

    node = lax.broadcasted_iota(i32, (1, NP, 1), 1)
    rows = []
    for rim in (outer[ALL_ROWS:, :LANES], outer[ALL_ROWS:, LANES:]):
        east = pltpu.roll(rim, LANES - 1, 1).reshape(4, NP, LANES)
        west = pltpu.roll(rim, 1, 1).reshape(4, NP, LANES)
        rim = (
            rim.reshape(4, NP, LANES)
            + jnp.where(node == NP - 1, pltpu.roll(east, NP - 1, 1), 0.0)
            + jnp.where(node == 0, pltpu.roll(west, 1, 1), 0.0)
        )
        rows.append(rim.reshape(EDGE_ROWS, LANES))

    every = tuple(range(count))
    groups = (every[0:2], every[2:4], every[4:])

    def tile_part(k, n):
        if tiles[k] is None:
            return outer_used[n][:, :LANES] if k == 0 else outer_used[n][:, LANES:]
        return tiles[k][n * NODES : (n + 1) * NODES]

    def part_of(group, n):
        return jnp.concatenate([tile_part(k, n) for k in group], 1)

    def summed(group, c):
        return jnp.concatenate([sums[k, c * NODES : (c + 1) * NODES] for k in group], 1)

    def average(group, per_mass):
        return [summed(group, c) * per_mass for c in range(3)]

    def laplace(s):
        return [
            dot(table[4 * NODES :, : 3 * NODES], jnp.concatenate(high_low_high(part), 0))
            for part in s
        ]

    start = [[part_of(group, n) for n in range(3)] for group in groups]
    fixed = [[part_of(group, n) for n in range(3, 6)] for group in groups]
    for k in every:
        for c in range(4):
            sums[k, c * NODES : (c + 1) * NODES] = tile_part(k, 7 + c)
    edge_y(4, every, rows)
    per_mass = [1.0 / summed(group, 3) for group in groups]
    one = []
    for n, group in enumerate(groups):
        change = average(group, per_mass[n])
        one.append([s + time_step * c for s, c in zip(start[n], change)])
    put_x_sums(groups, [mass_tendency(table, *s, *f) for s, f in zip(one, fixed)])
    edge_y(3, every)
    two = []
    for n, group in enumerate(groups):
        change = average(group, per_mass[n])
        two.append(
            [0.75 * s + 0.25 * (o + time_step * c) for s, o, c in zip(start[n], one[n], change)]
        )
    put_x_sums(groups, [mass_tendency(table, *s, *f) for s, f in zip(two, fixed)])
    edge_y(3, every)

    def regrouped(per_group):
        (outer_low, high_above) = per_group[0], per_group[1]
        below, low = outer_low[:, :LANES], outer_low[:, LANES:]
        centre, high = high_above[:, :LANES], high_above[:, LANES:]
        near = jnp.where(lane < LANES // 2, per_group[2], below)
        return [beside(low, centre), beside(high, near)]

    def of_groups(values):
        return [list(parts) for parts in zip(*(regrouped(part) for part in zip(*values)))]

    for c in range(3):
        rows_at = slice(c * NODES, (c + 1) * NODES)
        sums[count - 1, rows_at] = jnp.where(
            lane < LANES // 2, sums[count - 1, rows_at], sums[0, rows_at]
        )
    slots = every[1:]
    groups = (slots[0:2], slots[2:4])
    start, two = of_groups(start), of_groups(two)
    tide = regrouped([part_of(every[0:2], 6), part_of(every[2:4], 6), part_of(every[4:], 6)])
    per_mass = regrouped(per_mass)
    three = []
    for n, group in enumerate(groups):
        change = average(group, per_mass[n])
        now = [
            s / 3.0 + 2.0 / 3.0 * (o + time_step * c)
            for s, o, c in zip(start[n], two[n], change)
        ]
        now[0] = now[0] + tide[n]
        three.append(now)
    put_x_sums(groups, [laplace(s) for s in three])
    edge_y(3, slots)
    change = [average(group, per_mass[n]) for n, group in enumerate(groups)]
    put_x_sums(groups, [laplace(s) for s in change])
    edge_y(3, slots)
    stepped = []
    for n, group in enumerate(groups):
        change = average(group, per_mass[n])
        now = [s - time_step * hyper_coeff * b for s, b in zip(three[n], change)]
        stepped.append(jnp.concatenate(now, 0))
    stepped = jnp.concatenate(stepped, 1)[:, :MID]
    own = lanes_ref[27:28, LANES : LANES + MID] != 0
    stored = picked(jnp.where(own, stepped, 0.0), hot_ref[...])
    out_ref[...] = stored.reshape(out_ref.shape)


def on_device(fields, jacobian, water_depth, coriolis, tide_height, slot_of, seam_rows):
    block_cols = lax.axis_size("blk") // BY
    table, weight = operator_table()
    table, weight, lanes = map(jnp.asarray, (table, weight, lane_tables()))
    vmem = pl.BlockSpec(memory_space=pltpu.VMEM)
    smem = pl.BlockSpec(memory_space=pltpu.SMEM)
    hbm = pl.BlockSpec(memory_space=pltpu.HBM)
    params = pltpu.CompilerParams(vmem_limit_bytes=48 * 2**20)
    held = (fields, jacobian, water_depth, coriolis, tide_height)

    def call(kernel, ins, outs, cost, scratch=(), name=None):
        return pl.pallas_call(
            kernel,
            out_shape=[jax.ShapeDtypeStruct(*out) for out in outs],
            in_specs=[spec for spec, value in ins],
            out_specs=[vmem] * len(outs),
            scratch_shapes=list(scratch),
            compiler_params=params,
            cost_estimate=pl.CostEstimate(
                flops=cost, bytes_accessed=2 * 2**20, transcendentals=0
            ),
            name=name,
        )(
            *[
                pltpu.with_memory_space_constraint(value, pltpu.HBM) if spec is hbm else value
                for spec, value in ins
            ]
        )

    strip = ((HALF_ROWS, LANES), f32)
    def room(values, spaces=None):
        spaces = spaces or [pltpu.VMEM] * len(values)
        buffers = [space(x.shape, x.dtype) for space, x in zip(spaces, values)]
        return buffers + [pltpu.SemaphoreType.DMA((len(values),))]

    needed = (seam_rows, slot_of, *held, table, weight)
    corner = ((CORNER_ROWS, LANES), f32)
    scratch = [pltpu.VMEM((1, 4 * NODES, LANES), f32)]
    strip1, strip0, stored = call(
        functools.partial(strips_kernel, block_cols),
        [(hbm, x) for x in needed],
        [strip, strip, ((ROWS, ELEMENTS), f32)],
        10**8,
        scratch=room(needed, [pltpu.SMEM] + [pltpu.VMEM] * (len(needed) - 1)),
        name="strips",
    )
    to_next, far0, far1, to_pair = call(
        functools.partial(rows_kernel, block_cols),
        [(smem, seam_rows)]
        + [(vmem, x) for x in (stored, strip1, strip0, slot_of, table, weight)],
        [strip, corner, corner, strip],
        10**8,
        scratch=scratch,
        name="rows",
    )
    span = block_cols * BY
    both = ("face", "blk")
    places = [(f, x, y) for f in range(2) for x in range(block_cols) for y in range(BY)]

    def rank(face, block_x, block_y):
        return face * span + block_x * BY + block_y

    def same(y):
        return y

    def in_pair(y):
        return y ^ 1

    def next_pair(y):
        other = y + 1 if y % 2 else y - 1
        return other if 0 <= other < BY else y

    def swapped(value, partner):
        pairs = [
            (rank(f, x, y), rank(f if partner(y) != y else 1 - f, x, partner(y)))
            for f, x, y in places
        ]
        return lax.ppermute(value, both, pairs)

    def across(value0, value1, partner):
        last = block_cols - 1

        def aligned(y):
            return partner is same or partner(y) != y

        straight = {
            (f, x, y): (f, x + 1, partner(y)) if x < last else (1 - f, 0, partner(y))
            for f, x, y in places
        }
        turned = {
            (f, last, y): (1 - f, 0, BY - 1 - partner(y) if aligned(y) else y)
            for f in range(2)
            for y in range(BY)
        }

        def eastward(value, pairs):
            return lax.ppermute(value, both, [(rank(*a), rank(*b)) for a, b in pairs.items()])

        def westward(value, pairs):
            return lax.ppermute(value, both, [(rank(*b), rank(*a)) for a, b in pairs.items()])

        if block_cols == 1:
            return eastward(value0, straight), eastward(value1, turned)
        flipped = (seam_rows[:, 1] - seam_rows[:, 0]) % seam_rows.shape[1] != 1
        face = lax.axis_index("face")
        block_x = lax.axis_index("blk") // BY
        return (
            jnp.where(
                (block_x == last) & flipped[face],
                westward(value1, turned),
                westward(value1, straight),
            ),
            jnp.where(
                (block_x == 0) & flipped[1 - face],
                eastward(value0, turned),
                eastward(value0, straight),
            ),
        )

    halo0, halo1 = across(strip0, strip1, same)
    far0, far1 = across(far0, far1, next_pair)
    from_next = swapped(to_next, next_pair)
    own, hot = call(
        own_kernel,
        [(vmem, x) for x in (stored, slot_of, lanes)],
        [((ROWS, MID), f32), ((MID, ELEMENTS), bf16)],
        10**8,
        name="own",
    )
    (to_pair,) = call(
        corners_kernel,
        [(vmem, x) for x in (halo0, halo1, to_pair, table, weight, hot)],
        [((HALF_ROWS + 2 * CORNER_ROWS, LANES), f32)],
        10**8,
        scratch=scratch,
        name="corners",
    )
    from_pair = swapped(to_pair, in_pair)
    tile = ((11 * NODES, LANES), f32)
    low, centre, high = call(
        functools.partial(middle_kernel, block_cols),
        [(smem, seam_rows)] + [(vmem, x) for x in (halo0, halo1, own, lanes, table, weight)],
        [tile, tile, tile],
        10**8,
        name="middle",
    )
    (far,) = call(
        far_kernel,
        [(vmem, x) for x in (far1, far0, from_next, low)],
        [((2 * CORNER_ROWS, LANES), f32)],
        10**11,
        name="far",
    )
    (stepped,) = call(
        functools.partial(steps_kernel, block_cols),
        [(smem, seam_rows)]
        + [
            (vmem, x)
            for x in (
                from_pair, from_next, far, low, centre, high,
                hot, table, weight, lanes,
            )
        ],
        [(fields.shape, f32)],
        10**8,
        scratch=[pltpu.VMEM((EXT // LANES, 4 * NODES, LANES), f32)],
        name="steps",
    )
    return stepped


def solution(mesh):
    return jax.shard_map(
        on_device,
        mesh=mesh,
        in_specs=(
            P(None, None, None, ("face", "blk")),
            P(None, None, ("face", "blk")),
            P(None, None, ("face", "blk")),
            P(None, None, ("face", "blk")),
            P(None, None, ("face", "blk")),
            P(("face", "blk"), None),
            P(),
        ),
        out_specs=P(None, None, None, ("face", "blk")),
        check_vma=False,
    )
```

```python
import functools
import math

import jax
import jax.numpy as jnp
import ml_dtypes
import numpy as np
from jax import lax
from jax.experimental import pallas as pl
from jax.experimental.pallas import tpu as pltpu
from jax.sharding import PartitionSpec as P

BY = 16
GX = 16
GY = 16
NP = 8
NODES = NP * NP
ARRAYS = 7
ROWS = ARRAYS * NODES
MOVED = 6 * NODES
EDGE_ROWS = 4 * NP
ALL_ROWS = ROWS + EDGE_ROWS
HALF_ROWS = (MOVED + NODES // 2 + 2 * NP) // 2
RING = 4
RIM_ROWS = ROWS + 2 * EDGE_ROWS
CORNER_ROWS = (MOVED + NODES // 2 + 4 * NP) // 8
PITCH = GX + 2 * RING
MID = GY * PITCH
LANES = 128
EXT = MID + 2 * LANES
LEAD = LANES - RING * PITCH
ELEMENTS = GX * GY

time_step = 0.03
hyper_coeff = 0.0002

f32 = jnp.float32
bf16 = jnp.bfloat16
i32 = jnp.int32


def legendre_pair(location, degree):
    lower_value = 1.0
    upper_value = location
    for polynomial_order in range(2, degree + 1):
        lower_value, upper_value = (
            upper_value,
            (
                (2 * polynomial_order - 1) * location * upper_value
                - (polynomial_order - 1) * lower_value
            )
            / polynomial_order,
        )
    return (lower_value, upper_value)


def gll_tables(points):
    degree = points - 1
    locations = [-math.cos(math.pi * position / degree) for position in range(points)]
    for iteration in range(100):
        updated = []
        for location in locations:
            lower_value, upper_value = legendre_pair(location, degree)
            updated.append(
                location - (location * upper_value - lower_value) / ((degree + 1) * upper_value)
            )
        locations = updated
    locations[0] = -1.0
    locations[degree] = 1.0
    legendre_at = [legendre_pair(location, degree)[1] for location in locations]
    weights = [2.0 / (degree * (degree + 1) * value * value) for value in legendre_at]
    corner_value = degree * (degree + 1) / 4.0
    derivative = []
    for row_index in range(points):
        row_values = []
        for column_index in range(points):
            if row_index != column_index:
                row_values.append(
                    legendre_at[row_index]
                    / (legendre_at[column_index] * (locations[row_index] - locations[column_index]))
                )
            elif row_index == 0:
                row_values.append(-corner_value)
            elif row_index == degree:
                row_values.append(corner_value)
            else:
                row_values.append(0.0)
        derivative.append(row_values)
    return np.asarray(weights, np.float64), np.asarray(derivative, np.float64)


def in_three(matrix):
    high = matrix.astype(ml_dtypes.bfloat16)
    low = (matrix - high.astype(np.float64)).astype(ml_dtypes.bfloat16)
    return np.concatenate([high, high, low], 1)


def operator_table():
    weights, derivative = gll_tables(NP)
    eye = np.eye(NP)
    node_weight = np.outer(weights, weights).reshape(NODES, 1)
    along_x = node_weight * np.kron(derivative, eye)
    along_y = node_weight * np.kron(eye, derivative)
    second = derivative @ derivative
    both = node_weight * (np.kron(second, eye) + np.kron(eye, second))
    table = np.zeros((5 * NODES, 4 * NODES), ml_dtypes.bfloat16)
    table[:NODES, : 3 * NODES] = in_three(along_x)
    table[NODES : 2 * NODES, : 3 * NODES] = in_three(along_y)
    flux = [in_three(along_x), in_three(along_y)]
    for k, part in enumerate(flux):
        at = 2 * k * NODES
        table[2 * NODES : 3 * NODES, at : at + 2 * NODES] = part[:, : 2 * NODES]
        table[3 * NODES : 4 * NODES, at : at + NODES] = part[:, 2 * NODES :]
    table[4 * NODES :, : 3 * NODES] = in_three(both)
    spread = np.broadcast_to(node_weight, (NODES, LANES)).astype(np.float32)
    return table.astype(np.float32), np.ascontiguousarray(spread)


def lane_tables():
    table = np.zeros((24, MID), np.int32)
    for lane in range(MID):
        row, col = divmod(lane, PITCH)
        x = col - RING
        own = 0 <= x < GX
        table[0:8, lane] = x * GY + row if own else -1
        if not own:
            table[8:16, lane] = row * RING + (col if x < 0 else x - GX)
        table[16:24, lane] = 0 if own else (1 if x < 0 else 2)
    ext = np.zeros((8, EXT), np.int32)
    outer = np.zeros((32, 2 * LANES), np.int32)
    for lane in range(EXT):
        row, col = divmod(lane - LEAD, PITCH)
        y = row - RING
        x = col - RING
        ext[0, lane] = x in (-RING, GX + RING - 1)
        ext[1, lane] = y == GY - 1
        ext[2, lane] = y == 0
        ext[3, lane] = 0 <= y < GY and 0 <= x < GX
        ext[4, lane] = y == -RING
        ext[5, lane] = y == GY + RING - 1
        if -RING - 1 <= y < 0 or GY <= y <= GY + RING:
            place = lane if y < 0 else lane - MID
            step = y + RING if y < 0 else y - GY
            near = step + 1 if y < 0 else step
            far = 0 <= step < RING
            if 0 <= x < GX:
                outer[0:8, place] = near * GX + x
                outer[8:16, place] = 1
                outer[24:32, place] = LANES + step * GX + x if far else -1
            else:
                across = x + RING if x < 0 else x - GX
                outer[0:8, place] = (RING + 1) * GX + near * RING + across
                outer[8:16, place] = 2 if x < 0 else 3
                outer[24:32, place] = LANES + RING * GX + step * RING + across if far else -1
            outer[16:24, place] = y > 0
    whole = np.zeros((64, EXT), np.int32)
    whole[0:24, :MID] = table
    whole[24:32] = ext
    whole[32:64, : 2 * LANES] = outer
    return whole


def dot(a, b):
    return jnp.dot(a, b, preferred_element_type=f32)


def picked(values, one_hot):
    high = values.astype(bf16)
    low = (values - high.astype(f32)).astype(bf16)
    both = dot(jnp.concatenate([high, low], 0), one_hot)
    return both[: values.shape[0]] + both[values.shape[0] :]


def as_one_hot(row_of_lane, depth):
    index = lax.broadcasted_iota(i32, (depth, row_of_lane.shape[1]), 0)
    return jnp.where(index == row_of_lane[0:1], 1.0, 0.0).astype(bf16)


def high_low_high(values):
    high = values.astype(bf16)
    low = (values - high.astype(f32)).astype(bf16)
    return [high, low, high]


def by_slot(slot_ref, cell_of_lane):
    size = cell_of_lane.shape[1]
    halves = [
        jnp.broadcast_to(slot_ref[:, k * LANES : (k + 1) * LANES], (8, LANES)) for k in range(2)
    ]
    chosen = []
    for k in range(size // LANES):
        cell = cell_of_lane[:, k * LANES : (k + 1) * LANES]
        low, high = (jnp.take_along_axis(half, cell & (LANES - 1), axis=1) for half in halves)
        chosen.append(jnp.where(cell < 0, -1, jnp.where(cell < LANES, low, high)))
    return as_one_hot(jnp.concatenate(chosen, 1), ELEMENTS)


def stored_rows(fields_ref, others):
    fields = fields_ref[...].reshape(3 * NODES, ELEMENTS)
    others = [ref[...].reshape(NODES, ELEMENTS) for ref in others]
    return jnp.concatenate([fields[:NODES] - others[-1], fields[NODES:]] + others, 0)


def mass_tendency(table, p, u, v, area_depth, weighted_area, spin):
    slopes = dot(table[: 2 * NODES, : 3 * NODES], jnp.concatenate(high_low_high(p), 0))
    flux = high_low_high(area_depth * u)[:2] + high_low_high(area_depth * v)[:2]
    spread = dot(table[2 * NODES : 4 * NODES], jnp.concatenate(flux, 0))
    return [
        -(spread[:NODES] + spread[NODES:]),
        spin * v - weighted_area * slopes[:NODES],
        -spin * u - weighted_area * slopes[NODES:],
    ]


def edge_values(table_ref, weight_ref, p, u, v, area, depth, spin):
    root = jnp.sqrt(area)
    mass = jnp.concatenate([weight_ref[...]] * (area.shape[1] // LANES), 1) * area
    table = table_ref[...].astype(bf16)
    return mass_tendency(table, p, u, v, root * depth, root, mass * spin) + [mass]


def row_edges(sums):
    return tuple(sums[0, pl.ds(j, EDGE_ROWS, stride=NP)] for j in (NP - 1, 0))


def beside(left, right):
    return jnp.concatenate([left, right], 1)


def one_of_four(parts, index):
    out = parts[0]
    for k in range(1, 4):
        out = jnp.where(index == k, parts[k], out)
    return out


def folded(tide, kept, late, step):
    half = NODES // 2
    back = pltpu.roll(tide[half:], LANES - step, 1)
    onward = pltpu.roll(tide[half:], step, 1)
    return jnp.where(kept, tide[:half], jnp.where(late, back, onward))


def unfolded(rows, late, step):
    back = pltpu.roll(rows, LANES - step, 1)
    onward = pltpu.roll(rows, step, 1)
    return jnp.concatenate([rows, jnp.where(late, onward, back)], 0)


def strip_rows(parts, late, shift, rims):
    lane = lax.broadcasted_iota(i32, (1, LANES), 1)
    index = (lane >> shift) & 3
    kept = jnp.where(late, index // 2, 1 - index // 2) != 0
    tide = folded(parts[6], kept, late, 2 << shift)
    rim = one_of_four(rims, index)
    return jnp.concatenate(parts[:6] + [tide, rim, jnp.zeros_like(rim)], 0)


def placed_rows(whole, late, shift):
    half = NODES // 2
    tide = unfolded(whole[MOVED : MOVED + half], late, 2 << shift)
    rim = whole[MOVED + half : MOVED + half + NP]
    return jnp.concatenate([whole[:MOVED], tide] + spread_out(rim, late, shift), 0)


def spread_out(rim, late, shift):
    parts = []
    for k in range(4):
        first = pltpu.roll(rim, (LANES - (k << shift)) % LANES, 1) if k else rim
        last = pltpu.roll(rim, (3 - k) << shift, 1) if k < 3 else rim
        parts.append(jnp.where(late, first, last))
    return parts


def with_row_rim(whole, sums, top):
    north, south = row_edges(sums)
    rim = jnp.where(top, pltpu.roll(north, RING, 1), pltpu.roll(south, LANES - RING, 1))
    parts = [rim[k * NP : (k + 1) * NP] for k in range(4)]
    lane = lax.broadcasted_iota(i32, (1, LANES), 1)
    spots = []
    for k, part in enumerate(parts):
        first = pltpu.roll(part, k * RING, 1) if k else part
        last = pltpu.roll(part, (LANES - (3 - k) * RING) % LANES, 1) if k < 3 else part
        spots.append(jnp.where(top, first, last))
    rim = one_of_four(spots, (lane >> 2) & 3)
    return jnp.concatenate([whole[: MOVED + NODES // 2 + NP], rim], 0)


def corner_of(whole, start, top):
    lane = lax.broadcasted_iota(i32, (1, LANES), 1)
    base = LANES - start - jnp.where(top != 0, 48, 0)
    whole = jnp.concatenate([whole, jnp.zeros((8 * CORNER_ROWS - whole.shape[0], LANES), f32)], 0)
    out = None
    for k in range(8):
        part = whole[k * CORNER_ROWS : (k + 1) * CORNER_ROWS]
        part = pltpu.roll(part, (base + 16 * k) & (LANES - 1), 1)
        out = part if k == 0 else jnp.where(lane >= 16 * k, part, out)
    return out


def packed(whole):
    second = lax.broadcasted_iota(i32, (1, LANES), 1) >= 64
    top, bottom = whole[:HALF_ROWS], whole[HALF_ROWS:]
    return (
        jnp.where(second, pltpu.roll(bottom, 64, 1), top),
        jnp.where(second, bottom, pltpu.roll(top, 64, 1)),
    )


def unpacked(in0, in1):
    second = lax.broadcasted_iota(i32, (1, LANES), 1) >= 64
    top = jnp.where(second, pltpu.roll(in1, 64, 1), in0)
    bottom = jnp.where(second, in1, pltpu.roll(in0, 64, 1))
    return jnp.concatenate([top, bottom], 0)


def seam_flags(seam_ref, block_cols):
    size_y = seam_ref.shape[1]
    face = lax.axis_index("face")
    blk = lax.axis_index("blk")
    block_x = blk // BY

    def flipped(k):
        return jnp.where(lax.rem(seam_ref[k, 1] - seam_ref[k, 0] + size_y, size_y) != 1, 1, 0)

    first, second = flipped(0), flipped(1)
    east_flip = jnp.where(face == 0, first, second)
    west_flip = jnp.where(face == 0, second, first)
    if block_cols == 1:
        return 1 - east_flip, 0, east_flip, 1
    at_east = jnp.where(block_x == block_cols - 1, east_flip, 0)
    at_west = jnp.where(block_x == 0, west_flip, 0)
    return 1, at_east, 0, at_west


def strips_kernel(block_cols, *refs):
    sources, (out1_ref, out0_ref, stored_ref) = refs[:9], refs[9:12]
    buffers, sems = refs[12:21], refs[21]
    copies = [
        pltpu.make_async_copy(source, buffer, sems.at[k])
        for k, (source, buffer) in enumerate(zip(sources, buffers))
    ]
    for copy in copies:
        copy.start()
    seam_ref, slot_ref, fields_ref, area_ref, depth_ref, spin_ref, tide_ref = buffers[:7]
    table_ref, weight_ref = buffers[7:]
    for copy in copies[:2]:
        copy.wait()
    east0, flip0, east1, flip1 = seam_flags(seam_ref, block_cols)
    lane = lax.broadcasted_iota(i32, (8, 2 * LANES), 1)
    second = (lane & 64) != 0
    place = lane & 63
    row = place >> 2
    row = jnp.where(jnp.where(second, flip1, flip0) != 0, GY - 1 - row, row)
    east = jnp.where(second, east1, east0) != 0
    col = jnp.where(east, GX - RING, 0) + (place & 3)
    col = jnp.where(lane >= LANES, jnp.where(east, GX - RING - 1, RING), col)
    one_hot = by_slot(slot_ref, col * GY + row)
    for copy in copies[2:7]:
        copy.wait()
    stored = stored_rows(fields_ref, (area_ref, depth_ref, spin_ref, tide_ref))
    both = picked(stored, one_hot)

    lane = lax.broadcasted_iota(i32, (1, LANES), 1)
    second = lane >= 64
    flip = jnp.where(second, flip1, flip0) != 0
    sign = jnp.where(flip, -1.0, 1.0)
    node = lax.broadcasted_iota(i32, (1, NP, 1), 1)

    def turned(values):
        shaped = values.reshape(-1, NP, LANES)
        shaped = pltpu.roll(shaped, 4, 1)
        shaped = jnp.where((node & 2) == 0, pltpu.roll(shaped, 6, 1), pltpu.roll(shaped, 2, 1))
        shaped = jnp.where((node & 1) == 0, pltpu.roll(shaped, 7, 1), pltpu.roll(shaped, 1, 1))
        return shaped.reshape(values.shape)

    strip, ring = (
        [part[k * NODES : (k + 1) * NODES] for k in range(ARRAYS)]
        for part in (both[:, :LANES], both[:, LANES:])
    )
    for copy in copies[7:]:
        copy.wait()
    edges = edge_values(table_ref, weight_ref, *ring[:6])
    east = jnp.where(second, east1, east0) != 0
    ends = [jnp.where(east, part[NODES - NP :], part[:NP]) for part in edges]
    ends[2] = ends[2] * sign
    strip[2] = strip[2] * sign
    strip[5] = strip[5] * sign
    for ref, part, flip in zip(
        (out0_ref, out1_ref), packed(strip_rows(strip, east, 0, ends)), (flip0, flip1)
    ):
        if isinstance(flip, int):
            ref[...] = turned(part) if flip else part
        else:
            ref[...] = jnp.where(flip != 0, turned(part), part)
    stored_ref[...] = stored


def rows_kernel(
    block_cols, seam_ref, stored_ref, strip1_ref, strip0_ref, slot_ref, table_ref, weight_ref,
    next_ref, far0_ref, far1_ref, pair_ref, sums,
):
    east0, flip0, east1, flip1 = seam_flags(seam_ref, block_cols)
    odd = lax.axis_index("blk") & 1
    lane = lax.broadcasted_iota(i32, (8, 2 * LANES), 1)
    row = jnp.where(odd != 0, GY - RING, 0) + ((lane & 63) >> 4)
    row = jnp.where((lane & 64) != 0, jnp.where(odd != 0, GY - RING - 1, RING), row)
    five = jnp.where(odd != 0, 0, GY - RING - 1) + jnp.minimum((lane & (LANES - 1)) >> 4, RING)
    row = jnp.where(lane >= LANES, five, row)
    both = picked(stored_ref[...], by_slot(slot_ref, (lane & 15) * GY + row))
    pair_ref[...] = both[:, LANES:]
    rows = [both[k * NODES : (k + 1) * NODES, :LANES] for k in range(ARRAYS)]
    whole = unpacked(strip0_ref[...], strip1_ref[...])
    strip = [whole[k * NODES : (k + 1) * NODES] for k in range(6)]
    edges = edge_values(table_ref, weight_ref, *map(beside, strip, rows[:6]))
    sums[0] = jnp.concatenate([part[:, :LANES] for part in edges], 0)
    lane = lax.broadcasted_iota(i32, (1, LANES), 1)
    top0, top1 = odd ^ flip0, odd ^ flip1
    whole = with_row_rim(whole, sums, jnp.where(lane >= 64, top1, top0) != 0)
    far0_ref[...] = corner_of(whole, 0, top0)
    far1_ref[...] = corner_of(whole, 64, top1)
    sums[0] = jnp.concatenate([part[:, LANES:] for part in edges], 0)
    up = jnp.broadcast_to(odd != 0, (1, LANES))
    rim = pltpu.roll(jnp.where(up, *row_edges(sums)), 64, 1)
    rim = [rim[k * NP : (k + 1) * NP] for k in range(4)]
    whole = strip_rows(rows, up, 4, rim)
    top, bottom = whole[:HALF_ROWS], whole[HALF_ROWS:]
    next_ref[...] = jnp.where(lane >= 64, pltpu.roll(bottom, 64, 1), top)


def corners_kernel(block_cols, seam_ref, in0_ref, in1_ref, pair_ref, _, out_ref):
    east0, flip0, east1, flip1 = seam_flags(seam_ref, block_cols)
    top = 1 - (lax.axis_index("blk") & 1)
    lane = lax.broadcasted_iota(i32, (1, LANES), 1)
    late = jnp.where(lane >= 64, east1, east0) == 0
    whole = placed_rows(unpacked(in0_ref[...], in1_ref[...]), late, 0)
    pair = jnp.concatenate([pair_ref[...], jnp.zeros((EDGE_ROWS, LANES), f32)], 0)
    first = pltpu.roll(whole, jnp.where(top != 0, 36, 80), 1)
    other = pltpu.roll(whole, jnp.where(top != 0, LANES - 8, 36), 1)
    out_ref[...] = jnp.where(lane < 80, pair, jnp.where(lane < 100, first, other))


def own_kernel(stored_ref, slot_ref, lanes_ref, own_ref, hot_ref):
    one_hot = by_slot(slot_ref, lanes_ref[0:8, :MID])
    own_ref[...] = picked(stored_ref[...], one_hot)
    hot_ref[...] = one_hot.astype(f32).T.astype(bf16)


def first_sums(table, weight, parts, rims, at_rim):
    p, u, v, area, depth, spin, tide = parts
    size = area.shape[1]
    root = jnp.sqrt(area)
    mass = jnp.concatenate([weight] * (size // LANES), 1) * area
    used = [p, u, v, root * depth, root, mass * spin, tide]
    for part, rim in zip(mass_tendency(table, p, u, v, *used[3:6]) + [mass], rims):
        west, east = part[:NP], part[NODES - NP :]
        at_east = jnp.where(at_rim, rim, pltpu.roll(west, size - 1, 1))
        at_west = jnp.where(at_rim, rim, pltpu.roll(east, 1, 1))
        used.append(
            jnp.concatenate([west + at_west, part[NP : NODES - NP], east + at_east], 0)
        )
    return used


def middle_kernel(
    block_cols, seam_ref, in0_ref, in1_ref, own_ref, lanes_ref, table_ref, weight_ref,
    low_ref, centre_ref, high_ref,
):
    east0, flip0, east1, flip1 = seam_flags(seam_ref, block_cols)
    second = lax.broadcasted_iota(i32, (1, LANES), 1) >= 64
    late = jnp.where(second, east1, east0) == 0
    whole = placed_rows(unpacked(in0_ref[...], in1_ref[...]), late, 0)
    side = lanes_ref[16:24, :MID]
    first_at = jnp.where(side == 2, 64 * (1 - east0), 64 * east0)
    place = jnp.where(side == 0, -1, lanes_ref[8:16, :MID] + first_at)
    placed = picked(whole, as_one_hot(place, LANES))
    parts = [
        placed[k * NODES : (k + 1) * NODES] + own_ref[k * NODES : (k + 1) * NODES]
        for k in range(ARRAYS)
    ]
    rims = [placed[ROWS + c * NP : ROWS + (c + 1) * NP] for c in range(4)]
    at_rim = lanes_ref[24:25, LANES : LANES + MID] != 0
    used = first_sums(table_ref[...].astype(bf16), weight_ref[...], parts, rims, at_rim)
    for k, ref in enumerate((low_ref, centre_ref, high_ref)):
        for n, part in enumerate(used):
            ref[n * NODES : (n + 1) * NODES] = part[:, k * LANES : (k + 1) * LANES]


def far_kernel(far1_ref, far0_ref, *refs):
    out_ref = refs[-1]
    out_ref[:CORNER_ROWS] = far0_ref[...]
    out_ref[CORNER_ROWS:] = far1_ref[...]


def steps_kernel(
    block_cols, seam_ref, pair_ref, next_ref, far_ref, low_ref, centre_ref,
    high_ref, hot_ref, table_ref, weight_ref, lanes_ref, out_ref, sums,
):
    east0, flip0, east1, flip1 = seam_flags(seam_ref, block_cols)
    odd = lax.axis_index("blk") & 1
    block_y = lax.rem(lax.axis_index("blk"), BY)

    lane = lax.broadcasted_iota(i32, (1, LANES), 1)
    strip = jnp.concatenate([next_ref[...], pltpu.roll(next_ref[...], 64, 1)], 0)
    strip = placed_rows(strip, jnp.broadcast_to(odd == 0, (1, LANES)), 4)
    strip = jnp.concatenate(
        [strip[:ROWS], jnp.zeros((EDGE_ROWS, LANES), f32), strip[ROWS:]], 0
    )
    far = far_ref[...]
    corners = []
    for k in range(8):
        first = pltpu.roll(far[:CORNER_ROWS], (64 - 16 * k) % LANES, 1)
        other = pltpu.roll(far[CORNER_ROWS:], (80 - 16 * k) % LANES, 1)
        corners.append(jnp.where((lane & 16) == 0, first, other))
    corners = jnp.concatenate(corners, 0)
    rim = MOVED + NODES // 2 + NP
    late = jnp.where((lane & 16) != 0, east1, east0) == 0
    below = jnp.broadcast_to(odd == 0, (1, LANES))
    corners = jnp.concatenate(
        [placed_rows(corners, late, 0)] + spread_out(corners[rim : rim + NP], below, 2), 0
    )
    pair = jnp.concatenate([pair_ref[...], jnp.zeros((EDGE_ROWS, LANES), f32)], 0)
    around = beside(pair, jnp.where(lane < 64, strip, corners))
    outer_at = [lanes_ref[32 + 8 * k : 40 + 8 * k, : 2 * LANES] for k in range(4)]
    kind = outer_at[1]
    from_pair = jnp.where(outer_at[2] != 0, 1 - odd, odd) != 0
    strip_at = jnp.where(kind == 3, 1 - east0, jnp.where(kind == 2, east0, 0))
    place = jnp.where(
        from_pair,
        outer_at[0] + (RING + 1) * RING * strip_at,
        jnp.where(outer_at[3] < 0, -1, outer_at[3] + RING * RING * strip_at),
    )
    outer = picked(around, as_one_hot(jnp.where(kind == 0, -1, place), 2 * LANES))
    table = table_ref[...].astype(bf16)
    tiles = (None, low_ref, centre_ref, high_ref, None)
    count = len(tiles)
    masks = [lanes_ref[24:32, k * LANES : (k + 1) * LANES] for k in range(count)]
    closed_above = jnp.where(block_y == BY - 1, masks[-2][1:2], 0) != 0
    closed_below = jnp.where(block_y == 0, masks[1][2:3], 0) != 0
    first_row = jnp.where(odd == 0, masks[0][4:5], 0) != 0
    last_row = jnp.where(odd != 0, masks[-1][5:6], 0) != 0
    outer_used = first_sums(
        table,
        weight_ref[...],
        [outer[k * NODES : (k + 1) * NODES] for k in range(ARRAYS)],
        [outer[ROWS + c * NP : ROWS + (c + 1) * NP] for c in range(4)],
        beside(masks[0][0:1], masks[-1][0:1]) != 0,
    )

    def shifted(parts, by, ring):
        turned = [pltpu.roll(part, -by % LANES, 1) for part in parts]
        size = len(parts)
        step = 1 if by > 0 else -1
        others = [(k + step) % size if ring else min(max(k + step, 0), size - 1) for k in range(size)]
        from_other = lane >= LANES - by if by > 0 else lane < -by
        return [jnp.where(from_other, turned[others[k]], turned[k]) for k in range(size)]

    def put_x_sums(groups, components):
        slots = [k for group in groups for k in group]
        ring = len(slots) < count
        per_tile = [
            [part[:, n * LANES : (n + 1) * LANES] for part in parts]
            for group, parts in zip(groups, components)
            for n in range(len(group))
        ]
        for c in range(3):
            parts = [tile[c] for tile in per_tile]
            west = [part[:NP] for part in parts]
            east = [part[NODES - NP :] for part in parts]
            at_east, at_west = shifted(west, 1, ring), shifted(east, -1, ring)
            for n, k in enumerate(slots):
                sums[k, c * NODES : c * NODES + NP] = west[n] + at_west[n]
                sums[k, c * NODES + NP : (c + 1) * NODES - NP] = parts[n][NP : NODES - NP]
                sums[k, (c + 1) * NODES - NP : (c + 1) * NODES] = east[n] + at_east[n]

    def edge_y(components, slots, rows=None):
        ring = len(slots) < count
        south_at = pl.ds(0, components * NP, stride=NP)
        north_at = pl.ds(NP - 1, components * NP, stride=NP)
        south = [sums[k, south_at] for k in slots]
        north = [sums[k, north_at] for k in slots]
        at_north, at_south = shifted(south, PITCH, ring), shifted(north, -PITCH, ring)
        for n, k in enumerate(slots):
            if k == count - 2:
                at_north[n] = jnp.where(closed_above, 0.0, at_north[n])
            if k == 1:
                at_south[n] = jnp.where(closed_below, 0.0, at_south[n])
        if rows is not None:
            at_south[0] = jnp.where(first_row, rows[0], at_south[0])
            at_north[-1] = jnp.where(last_row, rows[1], at_north[-1])
        for n, k in enumerate(slots):
            sums[k, south_at] = south[n] + at_south[n]
            sums[k, north_at] = north[n] + at_north[n]

    node = lax.broadcasted_iota(i32, (1, NP, 1), 1)
    rows = []
    for rim in (outer[ALL_ROWS:, :LANES], outer[ALL_ROWS:, LANES:]):
        east = pltpu.roll(rim, LANES - 1, 1).reshape(4, NP, LANES)
        west = pltpu.roll(rim, 1, 1).reshape(4, NP, LANES)
        rim = (
            rim.reshape(4, NP, LANES)
            + jnp.where(node == NP - 1, pltpu.roll(east, NP - 1, 1), 0.0)
            + jnp.where(node == 0, pltpu.roll(west, 1, 1), 0.0)
        )
        rows.append(rim.reshape(EDGE_ROWS, LANES))

    every = tuple(range(count))
    groups = (every[0:2], every[2:4], every[4:])

    def tile_part(k, n):
        if tiles[k] is None:
            return outer_used[n][:, :LANES] if k == 0 else outer_used[n][:, LANES:]
        return tiles[k][n * NODES : (n + 1) * NODES]

    def part_of(group, n):
        return jnp.concatenate([tile_part(k, n) for k in group], 1)

    def summed(group, c):
        return jnp.concatenate([sums[k, c * NODES : (c + 1) * NODES] for k in group], 1)

    def average(group, per_mass):
        return [summed(group, c) * per_mass for c in range(3)]

    def laplace(s):
        return [
            dot(table[4 * NODES :, : 3 * NODES], jnp.concatenate(high_low_high(part), 0))
            for part in s
        ]

    start = [[part_of(group, n) for n in range(3)] for group in groups]
    fixed = [[part_of(group, n) for n in range(3, 6)] for group in groups]
    for k in every:
        for c in range(4):
            sums[k, c * NODES : (c + 1) * NODES] = tile_part(k, 7 + c)
    edge_y(4, every, rows)
    per_mass = [1.0 / summed(group, 3) for group in groups]
    one = []
    for n, group in enumerate(groups):
        change = average(group, per_mass[n])
        one.append([s + time_step * c for s, c in zip(start[n], change)])
    put_x_sums(groups, [mass_tendency(table, *s, *f) for s, f in zip(one, fixed)])
    edge_y(3, every)
    two = []
    for n, group in enumerate(groups):
        change = average(group, per_mass[n])
        two.append(
            [0.75 * s + 0.25 * (o + time_step * c) for s, o, c in zip(start[n], one[n], change)]
        )
    put_x_sums(groups, [mass_tendency(table, *s, *f) for s, f in zip(two, fixed)])
    edge_y(3, every)

    def regrouped(per_group):
        (outer_low, high_above) = per_group[0], per_group[1]
        below, low = outer_low[:, :LANES], outer_low[:, LANES:]
        centre, high = high_above[:, :LANES], high_above[:, LANES:]
        near = jnp.where(lane < LANES // 2, per_group[2], below)
        return [beside(low, centre), beside(high, near)]

    def of_groups(values):
        return [list(parts) for parts in zip(*(regrouped(part) for part in zip(*values)))]

    for c in range(3):
        rows_at = slice(c * NODES, (c + 1) * NODES)
        sums[count - 1, rows_at] = jnp.where(
            lane < LANES // 2, sums[count - 1, rows_at], sums[0, rows_at]
        )
    slots = every[1:]
    groups = (slots[0:2], slots[2:4])
    start, two = of_groups(start), of_groups(two)
    tide = regrouped([part_of(every[0:2], 6), part_of(every[2:4], 6), part_of(every[4:], 6)])
    per_mass = regrouped(per_mass)
    three = []
    for n, group in enumerate(groups):
        change = average(group, per_mass[n])
        now = [
            s / 3.0 + 2.0 / 3.0 * (o + time_step * c)
            for s, o, c in zip(start[n], two[n], change)
        ]
        now[0] = now[0] + tide[n]
        three.append(now)
    put_x_sums(groups, [laplace(s) for s in three])
    edge_y(3, slots)
    change = [average(group, per_mass[n]) for n, group in enumerate(groups)]
    put_x_sums(groups, [laplace(s) for s in change])
    edge_y(3, slots)
    stepped = []
    for n, group in enumerate(groups):
        change = average(group, per_mass[n])
        now = [s - time_step * hyper_coeff * b for s, b in zip(three[n], change)]
        stepped.append(jnp.concatenate(now, 0))
    stepped = jnp.concatenate(stepped, 1)[:, :MID]
    own = lanes_ref[27:28, LANES : LANES + MID] != 0
    stored = picked(jnp.where(own, stepped, 0.0), hot_ref[...])
    out_ref[...] = stored.reshape(out_ref.shape)


def on_device(fields, jacobian, water_depth, coriolis, tide_height, slot_of, seam_rows):
    block_cols = lax.axis_size("blk") // BY
    table, weight = operator_table()
    table, weight, lanes = map(jnp.asarray, (table, weight, lane_tables()))
    vmem = pl.BlockSpec(memory_space=pltpu.VMEM)
    smem = pl.BlockSpec(memory_space=pltpu.SMEM)
    hbm = pl.BlockSpec(memory_space=pltpu.HBM)
    params = pltpu.CompilerParams(vmem_limit_bytes=48 * 2**20)
    held = (fields, jacobian, water_depth, coriolis, tide_height)

    def call(kernel, ins, outs, cost, scratch=(), name=None):
        return pl.pallas_call(
            kernel,
            out_shape=[jax.ShapeDtypeStruct(*out) for out in outs],
            in_specs=[spec for spec, value in ins],
            out_specs=[vmem] * len(outs),
            scratch_shapes=list(scratch),
            compiler_params=params,
            cost_estimate=pl.CostEstimate(
                flops=cost, bytes_accessed=2 * 2**20, transcendentals=0
            ),
            name=name,
        )(
            *[
                pltpu.with_memory_space_constraint(value, pltpu.HBM) if spec is hbm else value
                for spec, value in ins
            ]
        )

    strip = ((HALF_ROWS, LANES), f32)
    def room(values, spaces=None):
        spaces = spaces or [pltpu.VMEM] * len(values)
        buffers = [space(x.shape, x.dtype) for space, x in zip(spaces, values)]
        return buffers + [pltpu.SemaphoreType.DMA((len(values),))]

    needed = (seam_rows, slot_of, *held, table, weight)
    corner = ((CORNER_ROWS, LANES), f32)
    scratch = [pltpu.VMEM((1, 4 * NODES, LANES), f32)]
    strip1, strip0, stored = call(
        functools.partial(strips_kernel, block_cols),
        [(hbm, x) for x in needed],
        [strip, strip, ((ROWS, ELEMENTS), f32)],
        10**8,
        scratch=room(needed, [pltpu.SMEM] + [pltpu.VMEM] * (len(needed) - 1)),
        name="strips",
    )
    to_next, far0, far1, to_pair = call(
        functools.partial(rows_kernel, block_cols),
        [(smem, seam_rows)]
        + [(vmem, x) for x in (stored, strip1, strip0, slot_of, table, weight)],
        [strip, corner, corner, ((ROWS, LANES), f32)],
        10**8,
        scratch=scratch,
        name="rows",
    )
    span = block_cols * BY
    both = ("face", "blk")
    places = [(f, x, y) for f in range(2) for x in range(block_cols) for y in range(BY)]

    def rank(face, block_x, block_y):
        return face * span + block_x * BY + block_y

    def same(y):
        return y

    def in_pair(y):
        return y ^ 1

    def next_pair(y):
        other = y + 1 if y % 2 else y - 1
        return other if 0 <= other < BY else y

    def swapped(value, partner):
        pairs = [
            (rank(f, x, y), rank(f if partner(y) != y else 1 - f, x, partner(y)))
            for f, x, y in places
        ]
        return lax.ppermute(value, both, pairs)

    def across(value0, value1, partner):
        last = block_cols - 1

        def aligned(y):
            return partner is same or partner(y) != y

        straight = {
            (f, x, y): (f, x + 1, partner(y)) if x < last else (1 - f, 0, partner(y))
            for f, x, y in places
        }
        turned = {
            (f, last, y): (1 - f, 0, BY - 1 - partner(y) if aligned(y) else y)
            for f in range(2)
            for y in range(BY)
        }

        def eastward(value, pairs):
            return lax.ppermute(value, both, [(rank(*a), rank(*b)) for a, b in pairs.items()])

        def westward(value, pairs):
            return lax.ppermute(value, both, [(rank(*b), rank(*a)) for a, b in pairs.items()])

        if block_cols == 1:
            return eastward(value0, straight), eastward(value1, turned)
        flipped = (seam_rows[:, 1] - seam_rows[:, 0]) % seam_rows.shape[1] != 1
        face = lax.axis_index("face")
        block_x = lax.axis_index("blk") // BY
        return (
            jnp.where(
                (block_x == last) & flipped[face],
                westward(value1, turned),
                westward(value1, straight),
            ),
            jnp.where(
                (block_x == 0) & flipped[1 - face],
                eastward(value0, turned),
                eastward(value0, straight),
            ),
        )

    halo0, halo1 = across(strip0, strip1, same)
    far0, far1 = across(far0, far1, next_pair)
    from_next = swapped(to_next, next_pair)
    own, hot = call(
        own_kernel,
        [(vmem, x) for x in (stored, slot_of, lanes)],
        [((ROWS, MID), f32), ((MID, ELEMENTS), bf16)],
        10**8,
        name="own",
    )
    (to_pair,) = call(
        functools.partial(corners_kernel, block_cols),
        [(smem, seam_rows)] + [(vmem, x) for x in (halo0, halo1, to_pair, hot)],
        [((ALL_ROWS, LANES), f32)],
        10**8,
        name="corners",
    )
    from_pair = swapped(to_pair, in_pair)
    tile = ((11 * NODES, LANES), f32)
    low, centre, high = call(
        functools.partial(middle_kernel, block_cols),
        [(smem, seam_rows)] + [(vmem, x) for x in (halo0, halo1, own, lanes, table, weight)],
        [tile, tile, tile],
        10**8,
        name="middle",
    )
    (far,) = call(
        far_kernel,
        [(vmem, x) for x in (far1, far0, from_next, low)],
        [((2 * CORNER_ROWS, LANES), f32)],
        10**11,
        name="far",
    )
    (stepped,) = call(
        functools.partial(steps_kernel, block_cols),
        [(smem, seam_rows)]
        + [
            (vmem, x)
            for x in (
                from_pair, from_next, far, low, centre, high,
                hot, table, weight, lanes,
            )
        ],
        [(fields.shape, f32)],
        10**8,
        scratch=[pltpu.VMEM((EXT // LANES, 4 * NODES, LANES), f32)],
        name="steps",
    )
    return stepped


def solution(mesh):
    return jax.shard_map(
        on_device,
        mesh=mesh,
        in_specs=(
            P(None, None, None, ("face", "blk")),
            P(None, None, ("face", "blk")),
            P(None, None, ("face", "blk")),
            P(None, None, ("face", "blk")),
            P(None, None, ("face", "blk")),
            P(("face", "blk"), None),
            P(),
        ),
        out_specs=P(None, None, None, ("face", "blk")),
        check_vma=False,
    )
```

```python
import functools
import math

import jax
import jax.numpy as jnp
import ml_dtypes
import numpy as np
from jax import lax
from jax.experimental import pallas as pl
from jax.experimental.pallas import tpu as pltpu
from jax.sharding import PartitionSpec as P

BY = 16
GX = 16
GY = 16
NP = 8
NODES = NP * NP
ARRAYS = 7
ROWS = ARRAYS * NODES
MOVED = 6 * NODES
EDGE_ROWS = 4 * NP
ALL_ROWS = ROWS + EDGE_ROWS
HALF_ROWS = (MOVED + NODES // 2 + 2 * NP) // 2
RING = 4
RIM_ROWS = ROWS + 2 * EDGE_ROWS
CORNER_ROWS = (MOVED + NODES // 2 + 4 * NP) // 8
PITCH = GX + 2 * RING
MID = GY * PITCH
LANES = 128
EXT = MID + 2 * LANES
LEAD = LANES - RING * PITCH
ELEMENTS = GX * GY

time_step = 0.03
hyper_coeff = 0.0002

f32 = jnp.float32
bf16 = jnp.bfloat16
i32 = jnp.int32


def legendre_pair(location, degree):
    lower_value = 1.0
    upper_value = location
    for polynomial_order in range(2, degree + 1):
        lower_value, upper_value = (
            upper_value,
            (
                (2 * polynomial_order - 1) * location * upper_value
                - (polynomial_order - 1) * lower_value
            )
            / polynomial_order,
        )
    return (lower_value, upper_value)


def gll_tables(points):
    degree = points - 1
    locations = [-math.cos(math.pi * position / degree) for position in range(points)]
    for iteration in range(100):
        updated = []
        for location in locations:
            lower_value, upper_value = legendre_pair(location, degree)
            updated.append(
                location - (location * upper_value - lower_value) / ((degree + 1) * upper_value)
            )
        locations = updated
    locations[0] = -1.0
    locations[degree] = 1.0
    legendre_at = [legendre_pair(location, degree)[1] for location in locations]
    weights = [2.0 / (degree * (degree + 1) * value * value) for value in legendre_at]
    corner_value = degree * (degree + 1) / 4.0
    derivative = []
    for row_index in range(points):
        row_values = []
        for column_index in range(points):
            if row_index != column_index:
                row_values.append(
                    legendre_at[row_index]
                    / (legendre_at[column_index] * (locations[row_index] - locations[column_index]))
                )
            elif row_index == 0:
                row_values.append(-corner_value)
            elif row_index == degree:
                row_values.append(corner_value)
            else:
                row_values.append(0.0)
        derivative.append(row_values)
    return np.asarray(weights, np.float64), np.asarray(derivative, np.float64)


def in_three(matrix):
    high = matrix.astype(ml_dtypes.bfloat16)
    low = (matrix - high.astype(np.float64)).astype(ml_dtypes.bfloat16)
    return np.concatenate([high, high, low], 1)


def operator_table():
    weights, derivative = gll_tables(NP)
    eye = np.eye(NP)
    node_weight = np.outer(weights, weights).reshape(NODES, 1)
    along_x = node_weight * np.kron(derivative, eye)
    along_y = node_weight * np.kron(eye, derivative)
    second = derivative @ derivative
    both = node_weight * (np.kron(second, eye) + np.kron(eye, second))
    table = np.zeros((5 * NODES, 4 * NODES), ml_dtypes.bfloat16)
    table[:NODES, : 3 * NODES] = in_three(along_x)
    table[NODES : 2 * NODES, : 3 * NODES] = in_three(along_y)
    flux = [in_three(along_x), in_three(along_y)]
    for k, part in enumerate(flux):
        at = 2 * k * NODES
        table[2 * NODES : 3 * NODES, at : at + 2 * NODES] = part[:, : 2 * NODES]
        table[3 * NODES : 4 * NODES, at : at + NODES] = part[:, 2 * NODES :]
    table[4 * NODES :, : 3 * NODES] = in_three(both)
    spread = np.broadcast_to(node_weight, (NODES, LANES)).astype(np.float32)
    return table.astype(np.float32), np.ascontiguousarray(spread)


def lane_tables():
    table = np.zeros((24, MID), np.int32)
    for lane in range(MID):
        row, col = divmod(lane, PITCH)
        x = col - RING
        own = 0 <= x < GX
        table[0:8, lane] = x * GY + row if own else -1
        if not own:
            table[8:16, lane] = row * RING + (col if x < 0 else x - GX)
        table[16:24, lane] = 0 if own else (1 if x < 0 else 2)
    ext = np.zeros((8, EXT), np.int32)
    outer = np.zeros((32, 2 * LANES), np.int32)
    for lane in range(EXT):
        row, col = divmod(lane - LEAD, PITCH)
        y = row - RING
        x = col - RING
        ext[0, lane] = x in (-RING, GX + RING - 1)
        ext[1, lane] = y == GY - 1
        ext[2, lane] = y == 0
        ext[3, lane] = 0 <= y < GY and 0 <= x < GX
        ext[4, lane] = y == -RING
        ext[5, lane] = y == GY + RING - 1
        if -RING - 1 <= y < 0 or GY <= y <= GY + RING:
            place = lane if y < 0 else lane - MID
            step = y + RING if y < 0 else y - GY
            near = step + 1 if y < 0 else step
            far = 0 <= step < RING
            if 0 <= x < GX:
                outer[0:8, place] = near * GX + x
                outer[8:16, place] = 1
                outer[24:32, place] = LANES + step * GX + x if far else -1
            else:
                across = x + RING if x < 0 else x - GX
                outer[0:8, place] = (RING + 1) * GX + near * RING + across
                outer[8:16, place] = 2 if x < 0 else 3
                outer[24:32, place] = LANES + RING * GX + step * RING + across if far else -1
            outer[16:24, place] = y > 0
    whole = np.zeros((64, EXT), np.int32)
    whole[0:24, :MID] = table
    whole[24:32] = ext
    whole[32:64, : 2 * LANES] = outer
    return whole


def dot(a, b):
    return jnp.dot(a, b, preferred_element_type=f32)


def picked(values, one_hot):
    high = values.astype(bf16)
    low = (values - high.astype(f32)).astype(bf16)
    both = dot(jnp.concatenate([high, low], 0), one_hot)
    return both[: values.shape[0]] + both[values.shape[0] :]


def as_one_hot(row_of_lane, depth):
    index = lax.broadcasted_iota(i32, (depth, row_of_lane.shape[1]), 0)
    return jnp.where(index == row_of_lane[0:1], 1.0, 0.0).astype(bf16)


def high_low_high(values):
    high = values.astype(bf16)
    low = (values - high.astype(f32)).astype(bf16)
    return [high, low, high]


def by_slot(slot_ref, cell_of_lane):
    size = cell_of_lane.shape[1]
    halves = [
        jnp.broadcast_to(slot_ref[:, k * LANES : (k + 1) * LANES], (8, LANES)) for k in range(2)
    ]
    chosen = []
    for k in range(size // LANES):
        cell = cell_of_lane[:, k * LANES : (k + 1) * LANES]
        low, high = (jnp.take_along_axis(half, cell & (LANES - 1), axis=1) for half in halves)
        chosen.append(jnp.where(cell < 0, -1, jnp.where(cell < LANES, low, high)))
    return as_one_hot(jnp.concatenate(chosen, 1), ELEMENTS)


def stored_rows(fields_ref, others):
    fields = fields_ref[...].reshape(3 * NODES, ELEMENTS)
    others = [ref[...].reshape(NODES, ELEMENTS) for ref in others]
    return jnp.concatenate([fields[:NODES] - others[-1], fields[NODES:]] + others, 0)


def mass_tendency(table, p, u, v, area_depth, weighted_area, spin):
    slopes = dot(table[: 2 * NODES, : 3 * NODES], jnp.concatenate(high_low_high(p), 0))
    flux = high_low_high(area_depth * u)[:2] + high_low_high(area_depth * v)[:2]
    spread = dot(table[2 * NODES : 4 * NODES], jnp.concatenate(flux, 0))
    return [
        -(spread[:NODES] + spread[NODES:]),
        spin * v - weighted_area * slopes[:NODES],
        -spin * u - weighted_area * slopes[NODES:],
    ]


def edge_values(table_ref, weight_ref, p, u, v, area, depth, spin):
    root = jnp.sqrt(area)
    mass = jnp.concatenate([weight_ref[...]] * (area.shape[1] // LANES), 1) * area
    table = table_ref[...].astype(bf16)
    return mass_tendency(table, p, u, v, root * depth, root, mass * spin) + [mass]


def row_edges(sums):
    return tuple(sums[0, pl.ds(j, EDGE_ROWS, stride=NP)] for j in (NP - 1, 0))


def beside(left, right):
    return jnp.concatenate([left, right], 1)


def one_of_four(parts, index):
    out = parts[0]
    for k in range(1, 4):
        out = jnp.where(index == k, parts[k], out)
    return out


def folded(tide, kept, late, step):
    half = NODES // 2
    back = pltpu.roll(tide[half:], LANES - step, 1)
    onward = pltpu.roll(tide[half:], step, 1)
    return jnp.where(kept, tide[:half], jnp.where(late, back, onward))


def unfolded(rows, late, step):
    back = pltpu.roll(rows, LANES - step, 1)
    onward = pltpu.roll(rows, step, 1)
    return jnp.concatenate([rows, jnp.where(late, onward, back)], 0)


def strip_rows(parts, late, shift, rims):
    lane = lax.broadcasted_iota(i32, (1, LANES), 1)
    index = (lane >> shift) & 3
    kept = jnp.where(late, index // 2, 1 - index // 2) != 0
    tide = folded(parts[6], kept, late, 2 << shift)
    rim = one_of_four(rims, index)
    return jnp.concatenate(parts[:6] + [tide, rim, jnp.zeros_like(rim)], 0)


def placed_rows(whole, late, shift):
    half = NODES // 2
    tide = unfolded(whole[MOVED : MOVED + half], late, 2 << shift)
    rim = whole[MOVED + half : MOVED + half + NP]
    return jnp.concatenate([whole[:MOVED], tide] + spread_out(rim, late, shift), 0)


def spread_out(rim, late, shift):
    parts = []
    for k in range(4):
        first = pltpu.roll(rim, (LANES - (k << shift)) % LANES, 1) if k else rim
        last = pltpu.roll(rim, (3 - k) << shift, 1) if k < 3 else rim
        parts.append(jnp.where(late, first, last))
    return parts


def with_row_rim(whole, sums, top):
    north, south = row_edges(sums)
    rim = jnp.where(top, pltpu.roll(north, RING, 1), pltpu.roll(south, LANES - RING, 1))
    parts = [rim[k * NP : (k + 1) * NP] for k in range(4)]
    lane = lax.broadcasted_iota(i32, (1, LANES), 1)
    spots = []
    for k, part in enumerate(parts):
        first = pltpu.roll(part, k * RING, 1) if k else part
        last = pltpu.roll(part, (LANES - (3 - k) * RING) % LANES, 1) if k < 3 else part
        spots.append(jnp.where(top, first, last))
    rim = one_of_four(spots, (lane >> 2) & 3)
    return jnp.concatenate([whole[: MOVED + NODES // 2 + NP], rim], 0)


def in_eight(whole):
    whole = jnp.concatenate([whole, jnp.zeros((8 * CORNER_ROWS - whole.shape[0], LANES), f32)], 0)
    return [whole[k * CORNER_ROWS : (k + 1) * CORNER_ROWS] for k in range(8)]


def corner_of(whole, start, top):
    lane = lax.broadcasted_iota(i32, (1, LANES), 1)
    out = None
    for k, part in enumerate(in_eight(whole)):
        last = pltpu.roll(part, (LANES - start - 48 + 16 * k) % LANES, 1)
        first = pltpu.roll(part, (LANES - start + 16 * k) % LANES, 1)
        part = jnp.where(top != 0, last, first)
        out = part if k == 0 else jnp.where(lane >= 16 * k, part, out)
    return out


def both_corners(whole, odd):
    group = lax.broadcasted_iota(i32, (1, LANES), 1) >> 4
    other_group = (group + jnp.where(odd != 0, 7, 1)) & 7
    first, other = None, None
    for k, part in enumerate(in_eight(whole)):
        part = pltpu.roll(part, (LANES + 16 * k - 48 * odd) & (LANES - 1), 1)
        first = part if k == 0 else jnp.where(group == k, part, first)
        other = part if k == 0 else jnp.where(other_group == k, part, other)
    return first, other


def arrived_corners(far, block_cols, odd):
    lane = lax.broadcasted_iota(i32, (1, LANES), 1)
    far0, far1 = far[:CORNER_ROWS], far[CORNER_ROWS:]
    corners = []
    for k in range(8):
        if block_cols == 1:
            part = jnp.where((lane >> 4) == k, far0, far1)
            part = pltpu.roll(part, (LANES + 64 + 16 * (1 - odd) - 16 * k) & (LANES - 1), 1)
        else:
            first = pltpu.roll(far0, (64 - 16 * k) % LANES, 1)
            other = pltpu.roll(far1, (80 - 16 * k) % LANES, 1)
            part = jnp.where((lane & 16) == 0, first, other)
        corners.append(part)
    return jnp.concatenate(corners, 0), ((lane >> 4) & 1) ^ (1 - odd if block_cols == 1 else 0)


def packed(whole):
    second = lax.broadcasted_iota(i32, (1, LANES), 1) >= 64
    top, bottom = whole[:HALF_ROWS], whole[HALF_ROWS:]
    return (
        jnp.where(second, pltpu.roll(bottom, 64, 1), top),
        jnp.where(second, bottom, pltpu.roll(top, 64, 1)),
    )


def unpacked(in0, in1):
    second = lax.broadcasted_iota(i32, (1, LANES), 1) >= 64
    top = jnp.where(second, pltpu.roll(in1, 64, 1), in0)
    bottom = jnp.where(second, in1, pltpu.roll(in0, 64, 1))
    return jnp.concatenate([top, bottom], 0)


def seam_flags(seam_ref, block_cols):
    size_y = seam_ref.shape[1]
    face = lax.axis_index("face")
    blk = lax.axis_index("blk")
    block_x = blk // BY

    def flipped(k):
        return jnp.where(lax.rem(seam_ref[k, 1] - seam_ref[k, 0] + size_y, size_y) != 1, 1, 0)

    first, second = flipped(0), flipped(1)
    east_flip = jnp.where(face == 0, first, second)
    west_flip = jnp.where(face == 0, second, first)
    if block_cols == 1:
        return 1 - east_flip, 0, east_flip, 1
    at_east = jnp.where(block_x == block_cols - 1, east_flip, 0)
    at_west = jnp.where(block_x == 0, west_flip, 0)
    return 1, at_east, 0, at_west


def flags_in(flags_ref, tiles=1):
    return [jnp.concatenate([flags_ref[k : k + 1]] * tiles, 1) for k in range(4)]


def strips_kernel(block_cols, *refs):
    sources, (out1_ref, out0_ref, stored_ref, flags_ref) = refs[:9], refs[9:13]
    buffers, sems = refs[13:22], refs[22]
    copies = [
        pltpu.make_async_copy(source, buffer, sems.at[k])
        for k, (source, buffer) in enumerate(zip(sources, buffers))
    ]
    for copy in copies:
        copy.start()
    seam_ref, slot_ref, fields_ref, area_ref, depth_ref, spin_ref, tide_ref = buffers[:7]
    table_ref, weight_ref = buffers[7:]
    for copy in copies[:2]:
        copy.wait()
    east0, flip0, east1, flip1 = flags = seam_flags(seam_ref, block_cols)
    index = lax.broadcasted_iota(i32, (8, LANES), 0)
    flags_ref[...] = sum(jnp.where(index == k, flag, 0) for k, flag in enumerate(flags))
    lane = lax.broadcasted_iota(i32, (8, 2 * LANES), 1)
    second = (lane & 64) != 0
    place = lane & 63
    row = place >> 2
    row = jnp.where(jnp.where(second, flip1, flip0) != 0, GY - 1 - row, row)
    east = jnp.where(second, east1, east0) != 0
    col = jnp.where(east, GX - RING, 0) + (place & 3)
    col = jnp.where(lane >= LANES, jnp.where(east, GX - RING - 1, RING), col)
    one_hot = by_slot(slot_ref, col * GY + row)
    for copy in copies[2:7]:
        copy.wait()
    stored = stored_rows(fields_ref, (area_ref, depth_ref, spin_ref, tide_ref))
    both = picked(stored, one_hot)

    lane = lax.broadcasted_iota(i32, (1, LANES), 1)
    second = lane >= 64
    flip = jnp.where(second, flip1, flip0) != 0
    sign = jnp.where(flip, -1.0, 1.0)
    node = lax.broadcasted_iota(i32, (1, NP, 1), 1)

    def turned(values):
        shaped = values.reshape(-1, NP, LANES)
        shaped = pltpu.roll(shaped, 4, 1)
        shaped = jnp.where((node & 2) == 0, pltpu.roll(shaped, 6, 1), pltpu.roll(shaped, 2, 1))
        shaped = jnp.where((node & 1) == 0, pltpu.roll(shaped, 7, 1), pltpu.roll(shaped, 1, 1))
        return shaped.reshape(values.shape)

    strip, ring = (
        [part[k * NODES : (k + 1) * NODES] for k in range(ARRAYS)]
        for part in (both[:, :LANES], both[:, LANES:])
    )
    for copy in copies[7:]:
        copy.wait()
    edges = edge_values(table_ref, weight_ref, *ring[:6])
    east = jnp.where(second, east1, east0) != 0
    ends = [jnp.where(east, part[NODES - NP :], part[:NP]) for part in edges]
    ends[2] = ends[2] * sign
    strip[2] = strip[2] * sign
    strip[5] = strip[5] * sign
    for ref, part, flip in zip(
        (out0_ref, out1_ref), packed(strip_rows(strip, east, 0, ends)), (flip0, flip1)
    ):
        if isinstance(flip, int):
            ref[...] = turned(part) if flip else part
        else:
            ref[...] = jnp.where(flip != 0, turned(part), part)
    stored_ref[...] = stored


def rows_kernel(
    block_cols, flags_ref, stored_ref, strip1_ref, strip0_ref, slot_ref, table_ref, weight_ref,
    next_ref, far0_ref, far1_ref, pair_ref, sums,
):
    east0, flip0, east1, flip1 = flags_in(flags_ref)
    odd = lax.axis_index("blk") & 1
    lane = lax.broadcasted_iota(i32, (8, 2 * LANES), 1)
    row = jnp.where(odd != 0, GY - RING, 0) + ((lane & 63) >> 4)
    row = jnp.where((lane & 64) != 0, jnp.where(odd != 0, GY - RING - 1, RING), row)
    five = jnp.where(odd != 0, 0, GY - RING - 1) + jnp.minimum((lane & (LANES - 1)) >> 4, RING)
    row = jnp.where(lane >= LANES, five, row)
    both = picked(stored_ref[...], by_slot(slot_ref, (lane & 15) * GY + row))
    pair_ref[...] = both[:, LANES:]
    rows = [both[k * NODES : (k + 1) * NODES, :LANES] for k in range(ARRAYS)]
    whole = unpacked(strip0_ref[...], strip1_ref[...])
    strip = [whole[k * NODES : (k + 1) * NODES] for k in range(6)]
    edges = edge_values(table_ref, weight_ref, *map(beside, strip, rows[:6]))
    sums[0] = jnp.concatenate([part[:, :LANES] for part in edges], 0)
    lane = lax.broadcasted_iota(i32, (1, LANES), 1)
    top0, top1 = odd ^ flip0, odd ^ flip1
    whole = with_row_rim(whole, sums, jnp.where(lane >= 64, top1, top0) != 0)
    if block_cols == 1:
        far0_ref[...], far1_ref[...] = both_corners(whole, odd)
    else:
        far0_ref[...] = corner_of(whole, 0, top0)
        far1_ref[...] = corner_of(whole, 64, top1)
    sums[0] = jnp.concatenate([part[:, LANES:] for part in edges], 0)
    up = jnp.broadcast_to(odd != 0, (1, LANES))
    rim = pltpu.roll(jnp.where(up, *row_edges(sums)), 64, 1)
    rim = [rim[k * NP : (k + 1) * NP] for k in range(4)]
    whole = strip_rows(rows, up, 4, rim)
    top, bottom = whole[:HALF_ROWS], whole[HALF_ROWS:]
    next_ref[...] = jnp.where(lane >= 64, pltpu.roll(bottom, 64, 1), top)


def corners_kernel(flags_ref, in0_ref, in1_ref, pair_ref, _, out_ref):
    east0, flip0, east1, flip1 = flags_in(flags_ref)
    top = 1 - (lax.axis_index("blk") & 1)
    lane = lax.broadcasted_iota(i32, (1, LANES), 1)
    halves = []
    for start in (0, 64):
        at0 = jnp.where(top != 0, 36, 80)
        at1 = jnp.where(top != 0, 56, 100)
        first = pltpu.roll(in0_ref[...], (at0 - start) & (LANES - 1), 1)
        other = pltpu.roll(in1_ref[...], (at1 - start) & (LANES - 1), 1)
        halves.append(jnp.where(lane < 100, first, other))
    late = jnp.where(lane < 100, east0, east1) == 0
    whole = placed_rows(jnp.concatenate(halves, 0), late, 0)
    out_ref[:ROWS] = jnp.where(lane < 80, pair_ref[...], whole[:ROWS])
    out_ref[ROWS:] = whole[ROWS:]


def own_kernel(stored_ref, slot_ref, lanes_ref, own_ref, hot_ref):
    one_hot = by_slot(slot_ref, lanes_ref[0:8, :MID])
    own_ref[...] = picked(stored_ref[...], one_hot)
    hot_ref[...] = one_hot.astype(f32).T.astype(bf16)


def first_sums(table, weight, parts, rims, at_rim):
    p, u, v, area, depth, spin, tide = parts
    size = area.shape[1]
    root = jnp.sqrt(area)
    mass = jnp.concatenate([weight] * (size // LANES), 1) * area
    used = [p, u, v, root * depth, root, mass * spin, tide]
    for part, rim in zip(mass_tendency(table, p, u, v, *used[3:6]) + [mass], rims):
        west, east = part[:NP], part[NODES - NP :]
        at_east = jnp.where(at_rim, rim, pltpu.roll(west, size - 1, 1))
        at_west = jnp.where(at_rim, rim, pltpu.roll(east, 1, 1))
        used.append(
            jnp.concatenate([west + at_west, part[NP : NODES - NP], east + at_east], 0)
        )
    return used


def middle_kernel(
    flags_ref, in0_ref, in1_ref, own_ref, lanes_ref, table_ref, weight_ref,
    low_ref, centre_ref, high_ref,
):
    east0, flip0, east1, flip1 = flags_in(flags_ref)
    second = lax.broadcasted_iota(i32, (1, LANES), 1) >= 64
    late = jnp.where(second, east1, east0) == 0
    whole = placed_rows(unpacked(in0_ref[...], in1_ref[...]), late, 0)
    side = lanes_ref[16:24, :MID]
    east = flags_in(flags_ref, MID // LANES)[0]
    first_at = jnp.where(side == 2, 64 * (1 - east), 64 * east)
    place = jnp.where(side == 0, -1, lanes_ref[8:16, :MID] + first_at)
    placed = picked(whole, as_one_hot(place, LANES))
    parts = [
        placed[k * NODES : (k + 1) * NODES] + own_ref[k * NODES : (k + 1) * NODES]
        for k in range(ARRAYS)
    ]
    rims = [placed[ROWS + c * NP : ROWS + (c + 1) * NP] for c in range(4)]
    at_rim = lanes_ref[24:25, LANES : LANES + MID] != 0
    used = first_sums(table_ref[...].astype(bf16), weight_ref[...], parts, rims, at_rim)
    for k, ref in enumerate((low_ref, centre_ref, high_ref)):
        for n, part in enumerate(used):
            ref[n * NODES : (n + 1) * NODES] = part[:, k * LANES : (k + 1) * LANES]


def far_kernel(far1_ref, far0_ref, *refs):
    out_ref = refs[-1]
    out_ref[:CORNER_ROWS] = far0_ref[...]
    out_ref[CORNER_ROWS:] = far1_ref[...]


def steps_kernel(
    block_cols, flags_ref, pair_ref, next_ref, far_ref, low_ref, centre_ref,
    high_ref, hot_ref, table_ref, weight_ref, lanes_ref, out_ref, sums,
):
    east0, flip0, east1, flip1 = flags_in(flags_ref)
    odd = lax.axis_index("blk") & 1
    block_y = lax.rem(lax.axis_index("blk"), BY)

    lane = lax.broadcasted_iota(i32, (1, LANES), 1)
    strip = jnp.concatenate([next_ref[...], pltpu.roll(next_ref[...], 64, 1)], 0)
    strip = placed_rows(strip, jnp.broadcast_to(odd == 0, (1, LANES)), 4)
    strip = jnp.concatenate(
        [strip[:ROWS], jnp.zeros((EDGE_ROWS, LANES), f32), strip[ROWS:]], 0
    )
    corners, strip_of = arrived_corners(far_ref[...], block_cols, odd)
    rim = MOVED + NODES // 2 + NP
    late = jnp.where(strip_of != 0, east1, east0) == 0
    below = jnp.broadcast_to(odd == 0, (1, LANES))
    corners = jnp.concatenate(
        [placed_rows(corners, late, 0)] + spread_out(corners[rim : rim + NP], below, 2), 0
    )
    pair = jnp.concatenate([pair_ref[...], jnp.zeros((EDGE_ROWS, LANES), f32)], 0)
    around = beside(pair, jnp.where(lane < 64, strip, corners))
    outer_at = [lanes_ref[32 + 8 * k : 40 + 8 * k, : 2 * LANES] for k in range(4)]
    kind = outer_at[1]
    from_pair = jnp.where(outer_at[2] != 0, 1 - odd, odd) != 0
    east = flags_in(flags_ref, 2)[0]
    strip_at = jnp.where(kind == 3, 1 - east, east)
    far_at = strip_at ^ (1 - odd) if block_cols == 1 else strip_at
    strip_at, far_at = (jnp.where(kind > 1, at, 0) for at in (strip_at, far_at))
    place = jnp.where(
        from_pair,
        outer_at[0] + (RING + 1) * RING * strip_at,
        jnp.where(outer_at[3] < 0, -1, outer_at[3] + RING * RING * far_at),
    )
    outer = picked(around, as_one_hot(jnp.where(kind == 0, -1, place), 2 * LANES))
    table = table_ref[...].astype(bf16)
    tiles = (None, low_ref, centre_ref, high_ref, None)
    count = len(tiles)
    masks = [lanes_ref[24:32, k * LANES : (k + 1) * LANES] for k in range(count)]
    closed_above = jnp.where(block_y == BY - 1, masks[-2][1:2], 0) != 0
    closed_below = jnp.where(block_y == 0, masks[1][2:3], 0) != 0
    first_row = jnp.where(odd == 0, masks[0][4:5], 0) != 0
    last_row = jnp.where(odd != 0, masks[-1][5:6], 0) != 0
    outer_used = first_sums(
        table,
        weight_ref[...],
        [outer[k * NODES : (k + 1) * NODES] for k in range(ARRAYS)],
        [outer[ROWS + c * NP : ROWS + (c + 1) * NP] for c in range(4)],
        beside(masks[0][0:1], masks[-1][0:1]) != 0,
    )

    def shifted(parts, by, ring):
        turned = [pltpu.roll(part, -by % LANES, 1) for part in parts]
        size = len(parts)
        step = 1 if by > 0 else -1
        others = [(k + step) % size if ring else min(max(k + step, 0), size - 1) for k in range(size)]
        from_other = lane >= LANES - by if by > 0 else lane < -by
        return [jnp.where(from_other, turned[others[k]], turned[k]) for k in range(size)]

    def put_x_sums(groups, components):
        slots = [k for group in groups for k in group]
        ring = len(slots) < count
        per_tile = [
            [part[:, n * LANES : (n + 1) * LANES] for part in parts]
            for group, parts in zip(groups, components)
            for n in range(len(group))
        ]
        for c in range(3):
            parts = [tile[c] for tile in per_tile]
            west = [part[:NP] for part in parts]
            east = [part[NODES - NP :] for part in parts]
            at_east, at_west = shifted(west, 1, ring), shifted(east, -1, ring)
            for n, k in enumerate(slots):
                sums[k, c * NODES : c * NODES + NP] = west[n] + at_west[n]
                sums[k, c * NODES + NP : (c + 1) * NODES - NP] = parts[n][NP : NODES - NP]
                sums[k, (c + 1) * NODES - NP : (c + 1) * NODES] = east[n] + at_east[n]

    def edge_y(components, slots, rows=None):
        ring = len(slots) < count
        south_at = pl.ds(0, components * NP, stride=NP)
        north_at = pl.ds(NP - 1, components * NP, stride=NP)
        south = [sums[k, south_at] for k in slots]
        north = [sums[k, north_at] for k in slots]
        at_north, at_south = shifted(south, PITCH, ring), shifted(north, -PITCH, ring)
        for n, k in enumerate(slots):
            if k == count - 2:
                at_north[n] = jnp.where(closed_above, 0.0, at_north[n])
            if k == 1:
                at_south[n] = jnp.where(closed_below, 0.0, at_south[n])
        if rows is not None:
            at_south[0] = jnp.where(first_row, rows[0], at_south[0])
            at_north[-1] = jnp.where(last_row, rows[1], at_north[-1])
        for n, k in enumerate(slots):
            sums[k, south_at] = south[n] + at_south[n]
            sums[k, north_at] = north[n] + at_north[n]

    node = lax.broadcasted_iota(i32, (1, NP, 1), 1)
    rows = []
    for rim in (outer[ALL_ROWS:, :LANES], outer[ALL_ROWS:, LANES:]):
        east = pltpu.roll(rim, LANES - 1, 1).reshape(4, NP, LANES)
        west = pltpu.roll(rim, 1, 1).reshape(4, NP, LANES)
        rim = (
            rim.reshape(4, NP, LANES)
            + jnp.where(node == NP - 1, pltpu.roll(east, NP - 1, 1), 0.0)
            + jnp.where(node == 0, pltpu.roll(west, 1, 1), 0.0)
        )
        rows.append(rim.reshape(EDGE_ROWS, LANES))

    every = tuple(range(count))
    groups = (every[0:2], every[2:4], every[4:])

    def tile_part(k, n):
        if tiles[k] is None:
            return outer_used[n][:, :LANES] if k == 0 else outer_used[n][:, LANES:]
        return tiles[k][n * NODES : (n + 1) * NODES]

    def part_of(group, n):
        return jnp.concatenate([tile_part(k, n) for k in group], 1)

    def summed(group, c):
        return jnp.concatenate([sums[k, c * NODES : (c + 1) * NODES] for k in group], 1)

    def average(group, per_mass):
        return [summed(group, c) * per_mass for c in range(3)]

    def laplace(s):
        return [
            dot(table[4 * NODES :, : 3 * NODES], jnp.concatenate(high_low_high(part), 0))
            for part in s
        ]

    start = [[part_of(group, n) for n in range(3)] for group in groups]
    fixed = [[part_of(group, n) for n in range(3, 6)] for group in groups]
    for k in every:
        for c in range(4):
            sums[k, c * NODES : (c + 1) * NODES] = tile_part(k, 7 + c)
    edge_y(4, every, rows)
    per_mass = [1.0 / summed(group, 3) for group in groups]
    one = []
    for n, group in enumerate(groups):
        change = average(group, per_mass[n])
        one.append([s + time_step * c for s, c in zip(start[n], change)])
    put_x_sums(groups, [mass_tendency(table, *s, *f) for s, f in zip(one, fixed)])
    edge_y(3, every)
    two = []
    for n, group in enumerate(groups):
        change = average(group, per_mass[n])
        two.append(
            [0.75 * s + 0.25 * (o + time_step * c) for s, o, c in zip(start[n], one[n], change)]
        )
    put_x_sums(groups, [mass_tendency(table, *s, *f) for s, f in zip(two, fixed)])
    edge_y(3, every)

    def regrouped(per_group):
        (outer_low, high_above) = per_group[0], per_group[1]
        below, low = outer_low[:, :LANES], outer_low[:, LANES:]
        centre, high = high_above[:, :LANES], high_above[:, LANES:]
        near = jnp.where(lane < LANES // 2, per_group[2], below)
        return [beside(low, centre), beside(high, near)]

    def of_groups(values):
        return [list(parts) for parts in zip(*(regrouped(part) for part in zip(*values)))]

    for c in range(3):
        rows_at = slice(c * NODES, (c + 1) * NODES)
        sums[count - 1, rows_at] = jnp.where(
            lane < LANES // 2, sums[count - 1, rows_at], sums[0, rows_at]
        )
    slots = every[1:]
    groups = (slots[0:2], slots[2:4])
    start, two = of_groups(start), of_groups(two)
    tide = regrouped([part_of(every[0:2], 6), part_of(every[2:4], 6), part_of(every[4:], 6)])
    per_mass = regrouped(per_mass)
    three = []
    for n, group in enumerate(groups):
        change = average(group, per_mass[n])
        now = [
            s / 3.0 + 2.0 / 3.0 * (o + time_step * c)
            for s, o, c in zip(start[n], two[n], change)
        ]
        now[0] = now[0] + tide[n]
        three.append(now)
    put_x_sums(groups, [laplace(s) for s in three])
    edge_y(3, slots)
    change = [average(group, per_mass[n]) for n, group in enumerate(groups)]
    put_x_sums(groups, [laplace(s) for s in change])
    edge_y(3, slots)
    stepped = []
    for n, group in enumerate(groups):
        change = average(group, per_mass[n])
        now = [s - time_step * hyper_coeff * b for s, b in zip(three[n], change)]
        stepped.append(jnp.concatenate(now, 0))
    stepped = jnp.concatenate(stepped, 1)[:, :MID]
    own = lanes_ref[27:28, LANES : LANES + MID] != 0
    stored = picked(jnp.where(own, stepped, 0.0), hot_ref[...])
    out_ref[...] = stored.reshape(out_ref.shape)


def on_device(fields, jacobian, water_depth, coriolis, tide_height, slot_of, seam_rows):
    block_cols = lax.axis_size("blk") // BY
    table, weight = operator_table()
    table, weight, lanes = map(jnp.asarray, (table, weight, lane_tables()))
    vmem = pl.BlockSpec(memory_space=pltpu.VMEM)
    hbm = pl.BlockSpec(memory_space=pltpu.HBM)
    params = pltpu.CompilerParams(vmem_limit_bytes=48 * 2**20)
    held = (fields, jacobian, water_depth, coriolis, tide_height)

    def call(kernel, ins, outs, cost, scratch=(), name=None):
        return pl.pallas_call(
            kernel,
            out_shape=[jax.ShapeDtypeStruct(*out) for out in outs],
            in_specs=[spec for spec, value in ins],
            out_specs=[vmem] * len(outs),
            scratch_shapes=list(scratch),
            compiler_params=params,
            cost_estimate=pl.CostEstimate(
                flops=cost, bytes_accessed=2 * 2**20, transcendentals=0
            ),
            name=name,
        )(
            *[
                pltpu.with_memory_space_constraint(value, pltpu.HBM) if spec is hbm else value
                for spec, value in ins
            ]
        )

    strip = ((HALF_ROWS, LANES), f32)
    def room(values, spaces=None):
        spaces = spaces or [pltpu.VMEM] * len(values)
        buffers = [space(x.shape, x.dtype) for space, x in zip(spaces, values)]
        return buffers + [pltpu.SemaphoreType.DMA((len(values),))]

    needed = (seam_rows, slot_of, *held, table, weight)
    corner = ((CORNER_ROWS, LANES), f32)
    scratch = [pltpu.VMEM((1, 4 * NODES, LANES), f32)]
    strip1, strip0, stored, flags = call(
        functools.partial(strips_kernel, block_cols),
        [(hbm, x) for x in needed],
        [strip, strip, ((ROWS, ELEMENTS), f32), ((8, LANES), i32)],
        10**8,
        scratch=room(needed, [pltpu.SMEM] + [pltpu.VMEM] * (len(needed) - 1)),
        name="strips",
    )
    to_next, far0, far1, to_pair = call(
        functools.partial(rows_kernel, block_cols),
        [(vmem, x) for x in (flags, stored, strip1, strip0, slot_of, table, weight)],
        [strip, corner, corner, ((ROWS, LANES), f32)],
        10**8,
        scratch=scratch,
        name="rows",
    )
    span = block_cols * BY
    both = ("face", "blk")
    places = [(f, x, y) for f in range(2) for x in range(block_cols) for y in range(BY)]

    def rank(face, block_x, block_y):
        return face * span + block_x * BY + block_y

    def same(y):
        return y

    def in_pair(y):
        return y ^ 1

    def next_pair(y):
        other = y + 1 if y % 2 else y - 1
        return other if 0 <= other < BY else y

    def swapped(value, partner):
        pairs = [
            (rank(f, x, y), rank(f if partner(y) != y else 1 - f, x, partner(y)))
            for f, x, y in places
        ]
        return lax.ppermute(value, both, pairs)

    def across(value0, value1, partner):
        last = block_cols - 1

        def aligned(y):
            return partner is same or partner(y) != y

        straight = {
            (f, x, y): (f, x + 1, partner(y)) if x < last else (1 - f, 0, partner(y))
            for f, x, y in places
        }
        turned = {
            (f, last, y): (1 - f, 0, BY - 1 - partner(y) if aligned(y) else y)
            for f in range(2)
            for y in range(BY)
        }

        def eastward(value, pairs):
            return lax.ppermute(value, both, [(rank(*a), rank(*b)) for a, b in pairs.items()])

        def westward(value, pairs):
            return lax.ppermute(value, both, [(rank(*b), rank(*a)) for a, b in pairs.items()])

        if block_cols == 1:
            return eastward(value0, straight), eastward(value1, turned)
        flipped = (seam_rows[:, 1] - seam_rows[:, 0]) % seam_rows.shape[1] != 1
        face = lax.axis_index("face")
        block_x = lax.axis_index("blk") // BY
        return (
            jnp.where(
                (block_x == last) & flipped[face],
                westward(value1, turned),
                westward(value1, straight),
            ),
            jnp.where(
                (block_x == 0) & flipped[1 - face],
                eastward(value0, turned),
                eastward(value0, straight),
            ),
        )

    halo0, halo1 = across(strip0, strip1, same)
    far0, far1 = across(far0, far1, next_pair)
    from_next = swapped(to_next, next_pair)
    own, hot = call(
        own_kernel,
        [(vmem, x) for x in (stored, slot_of, lanes)],
        [((ROWS, MID), f32), ((MID, ELEMENTS), bf16)],
        10**8,
        name="own",
    )
    (to_pair,) = call(
        corners_kernel,
        [(vmem, x) for x in (flags, halo0, halo1, to_pair, hot)],
        [((ALL_ROWS, LANES), f32)],
        10**8,
        name="corners",
    )
    from_pair = swapped(to_pair, in_pair)
    tile = ((11 * NODES, LANES), f32)
    low, centre, high = call(
        middle_kernel,
        [(vmem, x) for x in (flags, halo0, halo1, own, lanes, table, weight)],
        [tile, tile, tile],
        10**8,
        name="middle",
    )
    (far,) = call(
        far_kernel,
        [(vmem, x) for x in (far1, far0, from_next, low)],
        [((2 * CORNER_ROWS, LANES), f32)],
        10**11,
        name="far",
    )
    (stepped,) = call(
        functools.partial(steps_kernel, block_cols),
        [
            (vmem, x)
            for x in (
                flags, from_pair, from_next, far, low, centre, high, hot, table, weight, lanes
            )
        ],
        [(fields.shape, f32)],
        10**8,
        scratch=[pltpu.VMEM((EXT // LANES, 4 * NODES, LANES), f32)],
        name="steps",
    )
    return stepped


def solution(mesh):
    return jax.shard_map(
        on_device,
        mesh=mesh,
        in_specs=(
            P(None, None, None, ("face", "blk")),
            P(None, None, ("face", "blk")),
            P(None, None, ("face", "blk")),
            P(None, None, ("face", "blk")),
            P(None, None, ("face", "blk")),
            P(("face", "blk"), None),
            P(),
        ),
        out_specs=P(None, None, None, ("face", "blk")),
        check_vma=False,
    )
```

```python
import functools
import math

import jax
import jax.numpy as jnp
import ml_dtypes
import numpy as np
from jax import lax
from jax.experimental import pallas as pl
from jax.experimental.pallas import tpu as pltpu
from jax.sharding import PartitionSpec as P

BY = 16
GX = 16
GY = 16
NP = 8
NODES = NP * NP
ARRAYS = 7
ROWS = ARRAYS * NODES
MOVED = 6 * NODES
EDGE_ROWS = 4 * NP
ALL_ROWS = ROWS + EDGE_ROWS
HALF_ROWS = (MOVED + NODES // 2 + 2 * NP) // 2
RING = 4
RIM_ROWS = ROWS + 2 * EDGE_ROWS
CORNER_ROWS = (MOVED + NODES // 2 + 4 * NP) // 8
PITCH = GX + 2 * RING
MID = GY * PITCH
LANES = 128
EXT = MID + 2 * LANES
LEAD = LANES - RING * PITCH
ELEMENTS = GX * GY

time_step = 0.03
hyper_coeff = 0.0002

f32 = jnp.float32
bf16 = jnp.bfloat16
i32 = jnp.int32


def legendre_pair(location, degree):
    lower_value = 1.0
    upper_value = location
    for polynomial_order in range(2, degree + 1):
        lower_value, upper_value = (
            upper_value,
            (
                (2 * polynomial_order - 1) * location * upper_value
                - (polynomial_order - 1) * lower_value
            )
            / polynomial_order,
        )
    return (lower_value, upper_value)


def gll_tables(points):
    degree = points - 1
    locations = [-math.cos(math.pi * position / degree) for position in range(points)]
    for iteration in range(100):
        updated = []
        for location in locations:
            lower_value, upper_value = legendre_pair(location, degree)
            updated.append(
                location - (location * upper_value - lower_value) / ((degree + 1) * upper_value)
            )
        locations = updated
    locations[0] = -1.0
    locations[degree] = 1.0
    legendre_at = [legendre_pair(location, degree)[1] for location in locations]
    weights = [2.0 / (degree * (degree + 1) * value * value) for value in legendre_at]
    corner_value = degree * (degree + 1) / 4.0
    derivative = []
    for row_index in range(points):
        row_values = []
        for column_index in range(points):
            if row_index != column_index:
                row_values.append(
                    legendre_at[row_index]
                    / (legendre_at[column_index] * (locations[row_index] - locations[column_index]))
                )
            elif row_index == 0:
                row_values.append(-corner_value)
            elif row_index == degree:
                row_values.append(corner_value)
            else:
                row_values.append(0.0)
        derivative.append(row_values)
    return np.asarray(weights, np.float64), np.asarray(derivative, np.float64)


def in_three(matrix):
    high = matrix.astype(ml_dtypes.bfloat16)
    low = (matrix - high.astype(np.float64)).astype(ml_dtypes.bfloat16)
    return np.concatenate([high, high, low], 1)


def operator_table():
    weights, derivative = gll_tables(NP)
    eye = np.eye(NP)
    node_weight = np.outer(weights, weights).reshape(NODES, 1)
    along_x = node_weight * np.kron(derivative, eye)
    along_y = node_weight * np.kron(eye, derivative)
    second = derivative @ derivative
    both = node_weight * (np.kron(second, eye) + np.kron(eye, second))
    table = np.zeros((5 * NODES, 4 * NODES), ml_dtypes.bfloat16)
    table[:NODES, : 3 * NODES] = in_three(along_x)
    table[NODES : 2 * NODES, : 3 * NODES] = in_three(along_y)
    flux = [in_three(along_x), in_three(along_y)]
    for k, part in enumerate(flux):
        at = 2 * k * NODES
        table[2 * NODES : 3 * NODES, at : at + 2 * NODES] = part[:, : 2 * NODES]
        table[3 * NODES : 4 * NODES, at : at + NODES] = part[:, 2 * NODES :]
    table[4 * NODES :, : 3 * NODES] = in_three(both)
    spread = np.broadcast_to(node_weight, (NODES, LANES)).astype(np.float32)
    return table.astype(np.float32), np.ascontiguousarray(spread)


def lane_tables():
    table = np.zeros((24, MID), np.int32)
    for lane in range(MID):
        row, col = divmod(lane, PITCH)
        x = col - RING
        own = 0 <= x < GX
        table[0:8, lane] = x * GY + row if own else -1
        if not own:
            table[8:16, lane] = row * RING + (col if x < 0 else x - GX)
        table[16:24, lane] = 0 if own else (1 if x < 0 else 2)
    ext = np.zeros((8, EXT), np.int32)
    outer = np.zeros((32, 2 * LANES), np.int32)
    for lane in range(EXT):
        row, col = divmod(lane - LEAD, PITCH)
        y = row - RING
        x = col - RING
        ext[0, lane] = x in (-RING, GX + RING - 1)
        ext[1, lane] = y == GY - 1
        ext[2, lane] = y == 0
        ext[3, lane] = 0 <= y < GY and 0 <= x < GX
        ext[4, lane] = y == -RING
        ext[5, lane] = y == GY + RING - 1
        if -RING - 1 <= y < 0 or GY <= y <= GY + RING:
            place = lane if y < 0 else lane - MID
            step = y + RING if y < 0 else y - GY
            near = step + 1 if y < 0 else step
            far = 0 <= step < RING
            if 0 <= x < GX:
                outer[0:8, place] = near * GX + x
                outer[8:16, place] = 1
                outer[24:32, place] = LANES + step * GX + x if far else -1
            else:
                across = x + RING if x < 0 else x - GX
                outer[0:8, place] = (RING + 1) * GX + near * RING + across
                outer[8:16, place] = 2 if x < 0 else 3
                outer[24:32, place] = LANES + RING * GX + step * RING + across if far else -1
            outer[16:24, place] = y > 0
    whole = np.zeros((64, EXT), np.int32)
    whole[0:24, :MID] = table
    whole[24:32] = ext
    whole[32:64, : 2 * LANES] = outer
    return whole


def dot(a, b):
    return jnp.dot(a, b, preferred_element_type=f32)


def picked(values, one_hot):
    high = values.astype(bf16)
    low = (values - high.astype(f32)).astype(bf16)
    both = dot(jnp.concatenate([high, low], 0), one_hot)
    return both[: values.shape[0]] + both[values.shape[0] :]


def as_one_hot(row_of_lane, depth):
    index = lax.broadcasted_iota(i32, (depth, row_of_lane.shape[1]), 0)
    return jnp.where(index == row_of_lane[0:1], 1.0, 0.0).astype(bf16)


def high_low_high(values):
    high = values.astype(bf16)
    low = (values - high.astype(f32)).astype(bf16)
    return [high, low, high]


def by_slot(halves, cell_of_lane):
    size = cell_of_lane.shape[1]
    halves = [jnp.broadcast_to(half, (8, LANES)) for half in halves]
    chosen = []
    for k in range(size // LANES):
        cell = cell_of_lane[:, k * LANES : (k + 1) * LANES]
        low, high = (jnp.take_along_axis(half, cell & (LANES - 1), axis=1) for half in halves)
        chosen.append(jnp.where(cell < 0, -1, jnp.where(cell < LANES, low, high)))
    return as_one_hot(jnp.concatenate(chosen, 1), ELEMENTS)


def stored_rows(fields_ref, others):
    fields = fields_ref[...].reshape(3 * NODES, ELEMENTS)
    others = [ref[...].reshape(NODES, ELEMENTS) for ref in others]
    return jnp.concatenate([fields[:NODES] - others[-1], fields[NODES:]] + others, 0)


def mass_tendency(table, p, u, v, area_depth, weighted_area, spin):
    slopes = dot(table[: 2 * NODES, : 3 * NODES], jnp.concatenate(high_low_high(p), 0))
    flux = high_low_high(area_depth * u)[:2] + high_low_high(area_depth * v)[:2]
    spread = dot(table[2 * NODES : 4 * NODES], jnp.concatenate(flux, 0))
    return [
        -(spread[:NODES] + spread[NODES:]),
        spin * v - weighted_area * slopes[:NODES],
        -spin * u - weighted_area * slopes[NODES:],
    ]


def edge_values(table_ref, weight_ref, p, u, v, area, depth, spin):
    root = jnp.sqrt(area)
    mass = jnp.concatenate([weight_ref[...]] * (area.shape[1] // LANES), 1) * area
    table = table_ref[...].astype(bf16)
    return mass_tendency(table, p, u, v, root * depth, root, mass * spin) + [mass]


def row_edges(sums):
    return tuple(sums[0, pl.ds(j, EDGE_ROWS, stride=NP)] for j in (NP - 1, 0))


def beside(left, right):
    return jnp.concatenate([left, right], 1)


def one_of_four(parts, index):
    out = parts[0]
    for k in range(1, 4):
        out = jnp.where(index == k, parts[k], out)
    return out


def folded(tide, kept, late, step):
    half = NODES // 2
    back = pltpu.roll(tide[half:], LANES - step, 1)
    onward = pltpu.roll(tide[half:], step, 1)
    return jnp.where(kept, tide[:half], jnp.where(late, back, onward))


def unfolded(rows, late, step):
    back = pltpu.roll(rows, LANES - step, 1)
    onward = pltpu.roll(rows, step, 1)
    return jnp.concatenate([rows, jnp.where(late, onward, back)], 0)


def strip_rows(parts, late, shift, rims):
    lane = lax.broadcasted_iota(i32, (1, LANES), 1)
    index = (lane >> shift) & 3
    kept = jnp.where(late, index // 2, 1 - index // 2) != 0
    tide = folded(parts[6], kept, late, 2 << shift)
    rim = one_of_four(rims, index)
    return jnp.concatenate(parts[:6] + [tide, rim, jnp.zeros_like(rim)], 0)


def placed_rows(whole, late, shift):
    half = NODES // 2
    tide = unfolded(whole[MOVED : MOVED + half], late, 2 << shift)
    rim = whole[MOVED + half : MOVED + half + NP]
    return jnp.concatenate([whole[:MOVED], tide] + spread_out(rim, late, shift), 0)


def spread_out(rim, late, shift):
    parts = []
    for k in range(4):
        first = pltpu.roll(rim, (LANES - (k << shift)) % LANES, 1) if k else rim
        last = pltpu.roll(rim, (3 - k) << shift, 1) if k < 3 else rim
        parts.append(jnp.where(late, first, last))
    return parts


def with_row_rim(whole, sums, top):
    north, south = row_edges(sums)
    rim = jnp.where(top, pltpu.roll(north, RING, 1), pltpu.roll(south, LANES - RING, 1))
    parts = [rim[k * NP : (k + 1) * NP] for k in range(4)]
    lane = lax.broadcasted_iota(i32, (1, LANES), 1)
    spots = []
    for k, part in enumerate(parts):
        first = pltpu.roll(part, k * RING, 1) if k else part
        last = pltpu.roll(part, (LANES - (3 - k) * RING) % LANES, 1) if k < 3 else part
        spots.append(jnp.where(top, first, last))
    rim = one_of_four(spots, (lane >> 2) & 3)
    return jnp.concatenate([whole[: MOVED + NODES // 2 + NP], rim], 0)


def in_eight(whole):
    whole = jnp.concatenate([whole, jnp.zeros((8 * CORNER_ROWS - whole.shape[0], LANES), f32)], 0)
    return [whole[k * CORNER_ROWS : (k + 1) * CORNER_ROWS] for k in range(8)]


def corner_of(whole, start, top):
    lane = lax.broadcasted_iota(i32, (1, LANES), 1)
    out = None
    for k, part in enumerate(in_eight(whole)):
        last = pltpu.roll(part, (LANES - start - 48 + 16 * k) % LANES, 1)
        first = pltpu.roll(part, (LANES - start + 16 * k) % LANES, 1)
        part = jnp.where(top != 0, last, first)
        out = part if k == 0 else jnp.where(lane >= 16 * k, part, out)
    return out


def both_corners(whole, odd):
    group = lax.broadcasted_iota(i32, (1, LANES), 1) >> 4
    other_group = (group + jnp.where(odd != 0, 7, 1)) & 7
    first, other = None, None
    for k, part in enumerate(in_eight(whole)):
        part = pltpu.roll(part, (LANES + 16 * k - 48 * odd) & (LANES - 1), 1)
        first = part if k == 0 else jnp.where(group == k, part, first)
        other = part if k == 0 else jnp.where(other_group == k, part, other)
    return first, other


def arrived_corners(far0, far1, block_cols, odd):
    lane = lax.broadcasted_iota(i32, (1, LANES), 1)
    corners = []
    for k in range(8):
        if block_cols == 1:
            part = jnp.where((lane >> 4) == k, far0, far1)
            part = pltpu.roll(part, (LANES + 64 + 16 * (1 - odd) - 16 * k) & (LANES - 1), 1)
        else:
            first = pltpu.roll(far0, (64 - 16 * k) % LANES, 1)
            other = pltpu.roll(far1, (80 - 16 * k) % LANES, 1)
            part = jnp.where((lane & 16) == 0, first, other)
        corners.append(part)
    return jnp.concatenate(corners, 0), ((lane >> 4) & 1) ^ (1 - odd if block_cols == 1 else 0)


def packed(whole):
    second = lax.broadcasted_iota(i32, (1, LANES), 1) >= 64
    top, bottom = whole[:HALF_ROWS], whole[HALF_ROWS:]
    return (
        jnp.where(second, pltpu.roll(bottom, 64, 1), top),
        jnp.where(second, bottom, pltpu.roll(top, 64, 1)),
    )


def unpacked(in0, in1):
    second = lax.broadcasted_iota(i32, (1, LANES), 1) >= 64
    top = jnp.where(second, pltpu.roll(in1, 64, 1), in0)
    bottom = jnp.where(second, in1, pltpu.roll(in0, 64, 1))
    return jnp.concatenate([top, bottom], 0)


def seam_flags(seam_ref, block_cols):
    size_y = seam_ref.shape[1]
    face = lax.axis_index("face")
    blk = lax.axis_index("blk")
    block_x = blk // BY

    def flipped(k):
        return jnp.where(lax.rem(seam_ref[k, 1] - seam_ref[k, 0] + size_y, size_y) != 1, 1, 0)

    first, second = flipped(0), flipped(1)
    east_flip = jnp.where(face == 0, first, second)
    west_flip = jnp.where(face == 0, second, first)
    if block_cols == 1:
        return 1 - east_flip, 0, east_flip, 1
    at_east = jnp.where(block_x == block_cols - 1, east_flip, 0)
    at_west = jnp.where(block_x == 0, west_flip, 0)
    return 1, at_east, 0, at_west


def slots_in(flags_ref):
    return flags_ref[4:5], flags_ref[5:6]


def flags_in(flags_ref, tiles=1):
    return [jnp.concatenate([flags_ref[k : k + 1]] * tiles, 1) for k in range(4)]


def strips_kernel(block_cols, *refs):
    sources, (out1_ref, out0_ref, stored_ref, flags_ref) = refs[:9], refs[9:13]
    buffers, sems = refs[13:22], refs[22]
    copies = [
        pltpu.make_async_copy(source, buffer, sems.at[k])
        for k, (source, buffer) in enumerate(zip(sources, buffers))
    ]
    for copy in copies:
        copy.start()
    seam_ref, slot_ref, fields_ref, area_ref, depth_ref, spin_ref, tide_ref = buffers[:7]
    table_ref, weight_ref = buffers[7:]
    for copy in copies[:2]:
        copy.wait()
    east0, flip0, east1, flip1 = flags = seam_flags(seam_ref, block_cols)
    index = lax.broadcasted_iota(i32, (8, LANES), 0)
    flags_ref[...] = sum(jnp.where(index == k, flag, 0) for k, flag in enumerate(flags))
    slots = slot_ref[:, :LANES], slot_ref[:, LANES:]
    flags_ref[4:5], flags_ref[5:6] = slots
    lane = lax.broadcasted_iota(i32, (8, 2 * LANES), 1)
    second = (lane & 64) != 0
    place = lane & 63
    row = place >> 2
    row = jnp.where(jnp.where(second, flip1, flip0) != 0, GY - 1 - row, row)
    east = jnp.where(second, east1, east0) != 0
    col = jnp.where(east, GX - RING, 0) + (place & 3)
    col = jnp.where(lane >= LANES, jnp.where(east, GX - RING - 1, RING), col)
    one_hot = by_slot(slots, col * GY + row)
    for copy in copies[2:7]:
        copy.wait()
    stored = stored_rows(fields_ref, (area_ref, depth_ref, spin_ref, tide_ref))
    both = picked(stored, one_hot)

    lane = lax.broadcasted_iota(i32, (1, LANES), 1)
    second = lane >= 64
    flip = jnp.where(second, flip1, flip0) != 0
    sign = jnp.where(flip, -1.0, 1.0)
    node = lax.broadcasted_iota(i32, (1, NP, 1), 1)

    def turned(values):
        shaped = values.reshape(-1, NP, LANES)
        shaped = pltpu.roll(shaped, 4, 1)
        shaped = jnp.where((node & 2) == 0, pltpu.roll(shaped, 6, 1), pltpu.roll(shaped, 2, 1))
        shaped = jnp.where((node & 1) == 0, pltpu.roll(shaped, 7, 1), pltpu.roll(shaped, 1, 1))
        return shaped.reshape(values.shape)

    strip, ring = (
        [part[k * NODES : (k + 1) * NODES] for k in range(ARRAYS)]
        for part in (both[:, :LANES], both[:, LANES:])
    )
    for copy in copies[7:]:
        copy.wait()
    edges = edge_values(table_ref, weight_ref, *ring[:6])
    east = jnp.where(second, east1, east0) != 0
    ends = [jnp.where(east, part[NODES - NP :], part[:NP]) for part in edges]
    ends[2] = ends[2] * sign
    strip[2] = strip[2] * sign
    strip[5] = strip[5] * sign
    for ref, part, flip in zip(
        (out0_ref, out1_ref), packed(strip_rows(strip, east, 0, ends)), (flip0, flip1)
    ):
        if isinstance(flip, int):
            ref[...] = turned(part) if flip else part
        else:
            ref[...] = jnp.where(flip != 0, turned(part), part)
    stored_ref[...] = stored


def rows_kernel(
    block_cols, flags_ref, stored_ref, strip1_ref, strip0_ref, table_ref, weight_ref,
    next_ref, far0_ref, far1_ref, pair_ref, sums,
):
    east0, flip0, east1, flip1 = flags_in(flags_ref)
    odd = lax.axis_index("blk") & 1
    lane = lax.broadcasted_iota(i32, (8, 2 * LANES), 1)
    row = jnp.where(odd != 0, GY - RING, 0) + ((lane & 63) >> 4)
    row = jnp.where((lane & 64) != 0, jnp.where(odd != 0, GY - RING - 1, RING), row)
    five = jnp.where(odd != 0, 0, GY - RING - 1) + jnp.minimum((lane & (LANES - 1)) >> 4, RING)
    row = jnp.where(lane >= LANES, five, row)
    both = picked(stored_ref[...], by_slot(slots_in(flags_ref), (lane & 15) * GY + row))
    pair_ref[...] = both[:, LANES:]
    rows = [both[k * NODES : (k + 1) * NODES, :LANES] for k in range(ARRAYS)]
    whole = unpacked(strip0_ref[...], strip1_ref[...])
    strip = [whole[k * NODES : (k + 1) * NODES] for k in range(6)]
    edges = edge_values(table_ref, weight_ref, *map(beside, strip, rows[:6]))
    sums[0] = jnp.concatenate([part[:, :LANES] for part in edges], 0)
    lane = lax.broadcasted_iota(i32, (1, LANES), 1)
    top0, top1 = odd ^ flip0, odd ^ flip1
    whole = with_row_rim(whole, sums, jnp.where(lane >= 64, top1, top0) != 0)
    if block_cols == 1:
        far0_ref[...], far1_ref[...] = both_corners(whole, odd)
    else:
        far0_ref[...] = corner_of(whole, 0, top0)
        far1_ref[...] = corner_of(whole, 64, top1)
    sums[0] = jnp.concatenate([part[:, LANES:] for part in edges], 0)
    up = jnp.broadcast_to(odd != 0, (1, LANES))
    rim = pltpu.roll(jnp.where(up, *row_edges(sums)), 64, 1)
    rim = [rim[k * NP : (k + 1) * NP] for k in range(4)]
    whole = strip_rows(rows, up, 4, rim)
    top, bottom = whole[:HALF_ROWS], whole[HALF_ROWS:]
    next_ref[...] = jnp.where(lane >= 64, pltpu.roll(bottom, 64, 1), top)


def corners_kernel(flags_ref, in0_ref, in1_ref, pair_ref, _, out_ref):
    east0, flip0, east1, flip1 = flags_in(flags_ref)
    top = 1 - (lax.axis_index("blk") & 1)
    lane = lax.broadcasted_iota(i32, (1, LANES), 1)
    halves = []
    for start in (0, 64):
        at0 = jnp.where(top != 0, 36, 80)
        at1 = jnp.where(top != 0, 56, 100)
        first = pltpu.roll(in0_ref[...], (at0 - start) & (LANES - 1), 1)
        other = pltpu.roll(in1_ref[...], (at1 - start) & (LANES - 1), 1)
        halves.append(jnp.where(lane < 100, first, other))
    late = jnp.where(lane < 100, east0, east1) == 0
    whole = placed_rows(jnp.concatenate(halves, 0), late, 0)
    out_ref[:ROWS] = jnp.where(lane < 80, pair_ref[...], whole[:ROWS])
    out_ref[ROWS:] = whole[ROWS:]


def own_kernel(flags_ref, stored_ref, lanes_ref, own_ref, hot_ref):
    one_hot = by_slot(slots_in(flags_ref), lanes_ref[0:8, :MID])
    own_ref[...] = picked(stored_ref[...], one_hot)
    hot_ref[...] = one_hot.astype(f32).T.astype(bf16)


def first_sums(table, weight, parts, rims, at_rim):
    p, u, v, area, depth, spin, tide = parts
    size = area.shape[1]
    root = jnp.sqrt(area)
    mass = jnp.concatenate([weight] * (size // LANES), 1) * area
    used = [p, u, v, root * depth, root, mass * spin, tide]
    for part, rim in zip(mass_tendency(table, p, u, v, *used[3:6]) + [mass], rims):
        west, east = part[:NP], part[NODES - NP :]
        at_east = jnp.where(at_rim, rim, pltpu.roll(west, size - 1, 1))
        at_west = jnp.where(at_rim, rim, pltpu.roll(east, 1, 1))
        used.append(
            jnp.concatenate([west + at_west, part[NP : NODES - NP], east + at_east], 0)
        )
    return used


def middle_kernel(
    flags_ref, in0_ref, in1_ref, own_ref, lanes_ref, table_ref, weight_ref,
    low_ref, centre_ref, high_ref,
):
    east0, flip0, east1, flip1 = flags_in(flags_ref)
    second = lax.broadcasted_iota(i32, (1, LANES), 1) >= 64
    late = jnp.where(second, east1, east0) == 0
    whole = placed_rows(unpacked(in0_ref[...], in1_ref[...]), late, 0)
    side = lanes_ref[16:24, :MID]
    east = flags_in(flags_ref, MID // LANES)[0]
    first_at = jnp.where(side == 2, 64 * (1 - east), 64 * east)
    place = jnp.where(side == 0, -1, lanes_ref[8:16, :MID] + first_at)
    placed = picked(whole, as_one_hot(place, LANES))
    parts = [
        placed[k * NODES : (k + 1) * NODES] + own_ref[k * NODES : (k + 1) * NODES]
        for k in range(ARRAYS)
    ]
    rims = [placed[ROWS + c * NP : ROWS + (c + 1) * NP] for c in range(4)]
    at_rim = lanes_ref[24:25, LANES : LANES + MID] != 0
    used = first_sums(table_ref[...].astype(bf16), weight_ref[...], parts, rims, at_rim)
    for k, ref in enumerate((low_ref, centre_ref, high_ref)):
        for n, part in enumerate(used):
            ref[n * NODES : (n + 1) * NODES] = part[:, k * LANES : (k + 1) * LANES]


def far_kernel(block_cols, flags_ref, far1_ref, far0_ref, next_ref, _, out_ref):
    east0, flip0, east1, flip1 = flags_in(flags_ref)
    odd = lax.axis_index("blk") & 1
    lane = lax.broadcasted_iota(i32, (1, LANES), 1)
    below = jnp.broadcast_to(odd == 0, (1, LANES))
    strip = jnp.concatenate([next_ref[...], pltpu.roll(next_ref[...], 64, 1)], 0)
    strip = placed_rows(strip, below, 4)
    corners, strip_of = arrived_corners(far0_ref[...], far1_ref[...], block_cols, odd)
    late = jnp.where(strip_of != 0, east1, east0) == 0
    rim = MOVED + NODES // 2 + NP
    rim = jnp.concatenate(spread_out(corners[rim : rim + NP], below, 2), 0)
    corners = placed_rows(corners, late, 0)
    own = lane < 64
    out_ref[:ROWS] = jnp.where(own, strip[:ROWS], corners[:ROWS])
    out_ref[ROWS:ALL_ROWS] = corners[ROWS:]
    out_ref[ALL_ROWS:] = jnp.where(own, strip[ROWS:], rim)


def steps_kernel(
    block_cols, flags_ref, pair_ref, next_ref, low_ref, centre_ref,
    high_ref, hot_ref, table_ref, weight_ref, lanes_ref, out_ref, sums,
):
    east0, flip0, east1, flip1 = flags_in(flags_ref)
    odd = lax.axis_index("blk") & 1
    block_y = lax.rem(lax.axis_index("blk"), BY)

    lane = lax.broadcasted_iota(i32, (1, LANES), 1)
    pair = jnp.concatenate([pair_ref[...], jnp.zeros((EDGE_ROWS, LANES), f32)], 0)
    around = beside(pair, next_ref[...])
    outer_at = [lanes_ref[32 + 8 * k : 40 + 8 * k, : 2 * LANES] for k in range(4)]
    kind = outer_at[1]
    from_pair = jnp.where(outer_at[2] != 0, 1 - odd, odd) != 0
    east = flags_in(flags_ref, 2)[0]
    strip_at = jnp.where(kind == 3, 1 - east, east)
    far_at = strip_at ^ (1 - odd) if block_cols == 1 else strip_at
    strip_at, far_at = (jnp.where(kind > 1, at, 0) for at in (strip_at, far_at))
    place = jnp.where(
        from_pair,
        outer_at[0] + (RING + 1) * RING * strip_at,
        jnp.where(outer_at[3] < 0, -1, outer_at[3] + RING * RING * far_at),
    )
    outer = picked(around, as_one_hot(jnp.where(kind == 0, -1, place), 2 * LANES))
    table = table_ref[...].astype(bf16)
    tiles = (None, low_ref, centre_ref, high_ref, None)
    count = len(tiles)
    masks = [lanes_ref[24:32, k * LANES : (k + 1) * LANES] for k in range(count)]
    closed_above = jnp.where(block_y == BY - 1, masks[-2][1:2], 0) != 0
    closed_below = jnp.where(block_y == 0, masks[1][2:3], 0) != 0
    first_row = jnp.where(odd == 0, masks[0][4:5], 0) != 0
    last_row = jnp.where(odd != 0, masks[-1][5:6], 0) != 0
    outer_used = first_sums(
        table,
        weight_ref[...],
        [outer[k * NODES : (k + 1) * NODES] for k in range(ARRAYS)],
        [outer[ROWS + c * NP : ROWS + (c + 1) * NP] for c in range(4)],
        beside(masks[0][0:1], masks[-1][0:1]) != 0,
    )

    def shifted(parts, by, ring):
        turned = [pltpu.roll(part, -by % LANES, 1) for part in parts]
        size = len(parts)
        step = 1 if by > 0 else -1
        others = [(k + step) % size if ring else min(max(k + step, 0), size - 1) for k in range(size)]
        from_other = lane >= LANES - by if by > 0 else lane < -by
        return [jnp.where(from_other, turned[others[k]], turned[k]) for k in range(size)]

    def put_x_sums(groups, components):
        slots = [k for group in groups for k in group]
        ring = len(slots) < count
        per_tile = [
            [part[:, n * LANES : (n + 1) * LANES] for part in parts]
            for group, parts in zip(groups, components)
            for n in range(len(group))
        ]
        for c in range(3):
            parts = [tile[c] for tile in per_tile]
            west = [part[:NP] for part in parts]
            east = [part[NODES - NP :] for part in parts]
            at_east, at_west = shifted(west, 1, ring), shifted(east, -1, ring)
            for n, k in enumerate(slots):
                sums[k, c * NODES : c * NODES + NP] = west[n] + at_west[n]
                sums[k, c * NODES + NP : (c + 1) * NODES - NP] = parts[n][NP : NODES - NP]
                sums[k, (c + 1) * NODES - NP : (c + 1) * NODES] = east[n] + at_east[n]

    def edge_y(components, slots, rows=None):
        ring = len(slots) < count
        south_at = pl.ds(0, components * NP, stride=NP)
        north_at = pl.ds(NP - 1, components * NP, stride=NP)
        south = [sums[k, south_at] for k in slots]
        north = [sums[k, north_at] for k in slots]
        at_north, at_south = shifted(south, PITCH, ring), shifted(north, -PITCH, ring)
        for n, k in enumerate(slots):
            if k == count - 2:
                at_north[n] = jnp.where(closed_above, 0.0, at_north[n])
            if k == 1:
                at_south[n] = jnp.where(closed_below, 0.0, at_south[n])
        if rows is not None:
            at_south[0] = jnp.where(first_row, rows[0], at_south[0])
            at_north[-1] = jnp.where(last_row, rows[1], at_north[-1])
        for n, k in enumerate(slots):
            sums[k, south_at] = south[n] + at_south[n]
            sums[k, north_at] = north[n] + at_north[n]

    node = lax.broadcasted_iota(i32, (1, NP, 1), 1)
    rows = []
    for rim in (outer[ALL_ROWS:, :LANES], outer[ALL_ROWS:, LANES:]):
        east = pltpu.roll(rim, LANES - 1, 1).reshape(4, NP, LANES)
        west = pltpu.roll(rim, 1, 1).reshape(4, NP, LANES)
        rim = (
            rim.reshape(4, NP, LANES)
            + jnp.where(node == NP - 1, pltpu.roll(east, NP - 1, 1), 0.0)
            + jnp.where(node == 0, pltpu.roll(west, 1, 1), 0.0)
        )
        rows.append(rim.reshape(EDGE_ROWS, LANES))

    every = tuple(range(count))
    groups = (every[0:2], every[2:4], every[4:])

    def tile_part(k, n):
        if tiles[k] is None:
            return outer_used[n][:, :LANES] if k == 0 else outer_used[n][:, LANES:]
        return tiles[k][n * NODES : (n + 1) * NODES]

    def part_of(group, n):
        return jnp.concatenate([tile_part(k, n) for k in group], 1)

    def summed(group, c):
        return jnp.concatenate([sums[k, c * NODES : (c + 1) * NODES] for k in group], 1)

    def average(group, per_mass):
        return [summed(group, c) * per_mass for c in range(3)]

    def laplace(s):
        return [
            dot(table[4 * NODES :, : 3 * NODES], jnp.concatenate(high_low_high(part), 0))
            for part in s
        ]

    start = [[part_of(group, n) for n in range(3)] for group in groups]
    fixed = [[part_of(group, n) for n in range(3, 6)] for group in groups]
    for k in every:
        for c in range(4):
            sums[k, c * NODES : (c + 1) * NODES] = tile_part(k, 7 + c)
    edge_y(4, every, rows)
    per_mass = [1.0 / summed(group, 3) for group in groups]
    one = []
    for n, group in enumerate(groups):
        change = average(group, per_mass[n])
        one.append([s + time_step * c for s, c in zip(start[n], change)])
    put_x_sums(groups, [mass_tendency(table, *s, *f) for s, f in zip(one, fixed)])
    edge_y(3, every)
    two = []
    for n, group in enumerate(groups):
        change = average(group, per_mass[n])
        two.append(
            [0.75 * s + 0.25 * (o + time_step * c) for s, o, c in zip(start[n], one[n], change)]
        )
    put_x_sums(groups, [mass_tendency(table, *s, *f) for s, f in zip(two, fixed)])
    edge_y(3, every)

    def regrouped(per_group):
        (outer_low, high_above) = per_group[0], per_group[1]
        below, low = outer_low[:, :LANES], outer_low[:, LANES:]
        centre, high = high_above[:, :LANES], high_above[:, LANES:]
        near = jnp.where(lane < LANES // 2, per_group[2], below)
        return [beside(low, centre), beside(high, near)]

    def of_groups(values):
        return [list(parts) for parts in zip(*(regrouped(part) for part in zip(*values)))]

    for c in range(3):
        rows_at = slice(c * NODES, (c + 1) * NODES)
        sums[count - 1, rows_at] = jnp.where(
            lane < LANES // 2, sums[count - 1, rows_at], sums[0, rows_at]
        )
    slots = every[1:]
    groups = (slots[0:2], slots[2:4])
    start, two = of_groups(start), of_groups(two)
    tide = regrouped([part_of(every[0:2], 6), part_of(every[2:4], 6), part_of(every[4:], 6)])
    per_mass = regrouped(per_mass)
    three = []
    for n, group in enumerate(groups):
        change = average(group, per_mass[n])
        now = [
            s / 3.0 + 2.0 / 3.0 * (o + time_step * c)
            for s, o, c in zip(start[n], two[n], change)
        ]
        now[0] = now[0] + tide[n]
        three.append(now)
    put_x_sums(groups, [laplace(s) for s in three])
    edge_y(3, slots)
    change = [average(group, per_mass[n]) for n, group in enumerate(groups)]
    put_x_sums(groups, [laplace(s) for s in change])
    edge_y(3, slots)
    stepped = []
    for n, group in enumerate(groups):
        change = average(group, per_mass[n])
        now = [s - time_step * hyper_coeff * b for s, b in zip(three[n], change)]
        stepped.append(jnp.concatenate(now, 0))
    stepped = jnp.concatenate(stepped, 1)[:, :MID]
    own = lanes_ref[27:28, LANES : LANES + MID] != 0
    stored = picked(jnp.where(own, stepped, 0.0), hot_ref[...])
    out_ref[...] = stored.reshape(out_ref.shape)


def on_device(fields, jacobian, water_depth, coriolis, tide_height, slot_of, seam_rows):
    block_cols = lax.axis_size("blk") // BY
    table, weight = operator_table()
    table, weight, lanes = map(jnp.asarray, (table, weight, lane_tables()))
    vmem = pl.BlockSpec(memory_space=pltpu.VMEM)
    hbm = pl.BlockSpec(memory_space=pltpu.HBM)
    params = pltpu.CompilerParams(vmem_limit_bytes=48 * 2**20)
    held = (fields, jacobian, water_depth, coriolis, tide_height)

    def call(kernel, ins, outs, cost, scratch=(), name=None):
        return pl.pallas_call(
            kernel,
            out_shape=[jax.ShapeDtypeStruct(*out) for out in outs],
            in_specs=[spec for spec, value in ins],
            out_specs=[vmem] * len(outs),
            scratch_shapes=list(scratch),
            compiler_params=params,
            cost_estimate=pl.CostEstimate(
                flops=cost, bytes_accessed=2 * 2**20, transcendentals=0
            ),
            name=name,
        )(
            *[
                pltpu.with_memory_space_constraint(value, pltpu.HBM) if spec is hbm else value
                for spec, value in ins
            ]
        )

    strip = ((HALF_ROWS, LANES), f32)
    def room(values, spaces=None):
        spaces = spaces or [pltpu.VMEM] * len(values)
        buffers = [space(x.shape, x.dtype) for space, x in zip(spaces, values)]
        return buffers + [pltpu.SemaphoreType.DMA((len(values),))]

    needed = (seam_rows, slot_of, *held, table, weight)
    corner = ((CORNER_ROWS, LANES), f32)
    scratch = [pltpu.VMEM((1, 4 * NODES, LANES), f32)]
    strip1, strip0, stored, flags = call(
        functools.partial(strips_kernel, block_cols),
        [(hbm, x) for x in needed],
        [strip, strip, ((ROWS, ELEMENTS), f32), ((8, LANES), i32)],
        10**8,
        scratch=room(needed, [pltpu.SMEM] + [pltpu.VMEM] * (len(needed) - 1)),
        name="strips",
    )
    to_next, far0, far1, to_pair = call(
        functools.partial(rows_kernel, block_cols),
        [(vmem, x) for x in (flags, stored, strip1, strip0, table, weight)],
        [strip, corner, corner, ((ROWS, LANES), f32)],
        10**8,
        scratch=scratch,
        name="rows",
    )
    span = block_cols * BY
    both = ("face", "blk")
    places = [(f, x, y) for f in range(2) for x in range(block_cols) for y in range(BY)]

    def rank(face, block_x, block_y):
        return face * span + block_x * BY + block_y

    def same(y):
        return y

    def in_pair(y):
        return y ^ 1

    def next_pair(y):
        other = y + 1 if y % 2 else y - 1
        return other if 0 <= other < BY else y

    def swapped(value, partner):
        pairs = [
            (rank(f, x, y), rank(f if partner(y) != y else 1 - f, x, partner(y)))
            for f, x, y in places
        ]
        return lax.ppermute(value, both, pairs)

    def across(value0, value1, partner):
        last = block_cols - 1

        def aligned(y):
            return partner is same or partner(y) != y

        straight = {
            (f, x, y): (f, x + 1, partner(y)) if x < last else (1 - f, 0, partner(y))
            for f, x, y in places
        }
        turned = {
            (f, last, y): (1 - f, 0, BY - 1 - partner(y) if aligned(y) else y)
            for f in range(2)
            for y in range(BY)
        }

        def eastward(value, pairs):
            return lax.ppermute(value, both, [(rank(*a), rank(*b)) for a, b in pairs.items()])

        def westward(value, pairs):
            return lax.ppermute(value, both, [(rank(*b), rank(*a)) for a, b in pairs.items()])

        if block_cols == 1:
            return eastward(value0, straight), eastward(value1, turned)
        flipped = (seam_rows[:, 1] - seam_rows[:, 0]) % seam_rows.shape[1] != 1
        face = lax.axis_index("face")
        block_x = lax.axis_index("blk") // BY
        return (
            jnp.where(
                (block_x == last) & flipped[face],
                westward(value1, turned),
                westward(value1, straight),
            ),
            jnp.where(
                (block_x == 0) & flipped[1 - face],
                eastward(value0, turned),
                eastward(value0, straight),
            ),
        )

    halo0, halo1 = across(strip0, strip1, same)
    far0, far1 = across(far0, far1, next_pair)
    from_next = swapped(to_next, next_pair)
    own, hot = call(
        own_kernel,
        [(vmem, x) for x in (flags, stored, lanes)],
        [((ROWS, MID), f32), ((MID, ELEMENTS), bf16)],
        10**8,
        name="own",
    )
    (to_pair,) = call(
        corners_kernel,
        [(vmem, x) for x in (flags, halo0, halo1, to_pair, hot)],
        [((ALL_ROWS, LANES), f32)],
        10**8,
        name="corners",
    )
    from_pair = swapped(to_pair, in_pair)
    tile = ((11 * NODES, LANES), f32)
    low, centre, high = call(
        middle_kernel,
        [(vmem, x) for x in (flags, halo0, halo1, own, lanes, table, weight)],
        [tile, tile, tile],
        10**8,
        name="middle",
    )
    (from_next,) = call(
        functools.partial(far_kernel, block_cols),
        [(vmem, x) for x in (flags, far1, far0, from_next, low)],
        [((RIM_ROWS, LANES), f32)],
        10**11,
        name="far",
    )
    (stepped,) = call(
        functools.partial(steps_kernel, block_cols),
        [
            (vmem, x)
            for x in (
                flags, from_pair, from_next, low, centre, high, hot, table, weight, lanes
            )
        ],
        [(fields.shape, f32)],
        10**8,
        scratch=[pltpu.VMEM((EXT // LANES, 4 * NODES, LANES), f32)],
        name="steps",
    )
    return stepped


def solution(mesh):
    return jax.shard_map(
        on_device,
        mesh=mesh,
        in_specs=(
            P(None, None, None, ("face", "blk")),
            P(None, None, ("face", "blk")),
            P(None, None, ("face", "blk")),
            P(None, None, ("face", "blk")),
            P(None, None, ("face", "blk")),
            P(("face", "blk"), None),
            P(),
        ),
        out_specs=P(None, None, None, ("face", "blk")),
        check_vma=False,
    )
```

```python
import functools
import math

import jax
import jax.numpy as jnp
import ml_dtypes
import numpy as np
from jax import lax
from jax.experimental import pallas as pl
from jax.experimental.pallas import tpu as pltpu
from jax.sharding import PartitionSpec as P

BY = 16
GX = 16
GY = 16
NP = 8
NODES = NP * NP
ARRAYS = 7
ROWS = ARRAYS * NODES
MOVED = 6 * NODES
EDGE_ROWS = 4 * NP
ALL_ROWS = ROWS + EDGE_ROWS
HALF_ROWS = (MOVED + NODES // 2 + 2 * NP) // 2
RING = 4
RIM_ROWS = ROWS + 2 * EDGE_ROWS
CORNER_ROWS = (MOVED + NODES // 2 + 4 * NP) // 8
PITCH = GX + 2 * RING
MID = GY * PITCH
LANES = 128
EXT = MID + 2 * LANES
LEAD = LANES - RING * PITCH
ELEMENTS = GX * GY

time_step = 0.03
hyper_coeff = 0.0002

f32 = jnp.float32
bf16 = jnp.bfloat16
i32 = jnp.int32


def legendre_pair(location, degree):
    lower_value = 1.0
    upper_value = location
    for polynomial_order in range(2, degree + 1):
        lower_value, upper_value = (
            upper_value,
            (
                (2 * polynomial_order - 1) * location * upper_value
                - (polynomial_order - 1) * lower_value
            )
            / polynomial_order,
        )
    return (lower_value, upper_value)


def gll_tables(points):
    degree = points - 1
    locations = [-math.cos(math.pi * position / degree) for position in range(points)]
    for iteration in range(100):
        updated = []
        for location in locations:
            lower_value, upper_value = legendre_pair(location, degree)
            updated.append(
                location - (location * upper_value - lower_value) / ((degree + 1) * upper_value)
            )
        locations = updated
    locations[0] = -1.0
    locations[degree] = 1.0
    legendre_at = [legendre_pair(location, degree)[1] for location in locations]
    weights = [2.0 / (degree * (degree + 1) * value * value) for value in legendre_at]
    corner_value = degree * (degree + 1) / 4.0
    derivative = []
    for row_index in range(points):
        row_values = []
        for column_index in range(points):
            if row_index != column_index:
                row_values.append(
                    legendre_at[row_index]
                    / (legendre_at[column_index] * (locations[row_index] - locations[column_index]))
                )
            elif row_index == 0:
                row_values.append(-corner_value)
            elif row_index == degree:
                row_values.append(corner_value)
            else:
                row_values.append(0.0)
        derivative.append(row_values)
    return np.asarray(weights, np.float64), np.asarray(derivative, np.float64)


def in_three(matrix):
    high = matrix.astype(ml_dtypes.bfloat16)
    low = (matrix - high.astype(np.float64)).astype(ml_dtypes.bfloat16)
    return np.concatenate([high, high, low], 1)


def operator_table():
    weights, derivative = gll_tables(NP)
    eye = np.eye(NP)
    node_weight = np.outer(weights, weights).reshape(NODES, 1)
    along_x = node_weight * np.kron(derivative, eye)
    along_y = node_weight * np.kron(eye, derivative)
    second = derivative @ derivative
    both = node_weight * (np.kron(second, eye) + np.kron(eye, second))
    table = np.zeros((5 * NODES, 4 * NODES), ml_dtypes.bfloat16)
    table[:NODES, : 3 * NODES] = in_three(along_x)
    table[NODES : 2 * NODES, : 3 * NODES] = in_three(along_y)
    flux = [in_three(along_x), in_three(along_y)]
    for k, part in enumerate(flux):
        at = 2 * k * NODES
        table[2 * NODES : 3 * NODES, at : at + 2 * NODES] = part[:, : 2 * NODES]
        table[3 * NODES : 4 * NODES, at : at + NODES] = part[:, 2 * NODES :]
    table[4 * NODES :, : 3 * NODES] = in_three(both)
    table = table.astype(np.float32)
    spread = np.broadcast_to(node_weight, (NODES, LANES)).astype(np.float32)
    ends = np.r_[:NP, NODES - NP : NODES]
    edge_table = np.zeros((10 * NP, 4 * NODES), np.float32)
    for k in range(4):
        edge_table[2 * k * NP : 2 * (k + 1) * NP] = table[k * NODES + ends]
    edge_table[8 * NP :, :LANES] = spread[ends]
    return table, np.ascontiguousarray(spread), edge_table


def lane_tables():
    table = np.zeros((24, MID), np.int32)
    for lane in range(MID):
        row, col = divmod(lane, PITCH)
        x = col - RING
        own = 0 <= x < GX
        table[0:8, lane] = x * GY + row if own else -1
        if not own:
            table[8:16, lane] = row * RING + (col if x < 0 else x - GX)
        table[16:24, lane] = 0 if own else (1 if x < 0 else 2)
    ext = np.zeros((8, EXT), np.int32)
    outer = np.zeros((32, 2 * LANES), np.int32)
    for lane in range(EXT):
        row, col = divmod(lane - LEAD, PITCH)
        y = row - RING
        x = col - RING
        ext[0, lane] = x in (-RING, GX + RING - 1)
        ext[1, lane] = y == GY - 1
        ext[2, lane] = y == 0
        ext[3, lane] = 0 <= y < GY and 0 <= x < GX
        ext[4, lane] = y == -RING
        ext[5, lane] = y == GY + RING - 1
        if -RING - 1 <= y < 0 or GY <= y <= GY + RING:
            place = lane if y < 0 else lane - MID
            step = y + RING if y < 0 else y - GY
            near = step + 1 if y < 0 else step
            far = 0 <= step < RING
            if 0 <= x < GX:
                outer[0:8, place] = near * GX + x
                outer[8:16, place] = 1
                outer[24:32, place] = LANES + step * GX + x if far else -1
            else:
                across = x + RING if x < 0 else x - GX
                outer[0:8, place] = (RING + 1) * GX + near * RING + across
                outer[8:16, place] = 2 if x < 0 else 3
                outer[24:32, place] = LANES + RING * GX + step * RING + across if far else -1
            outer[16:24, place] = y > 0
    whole = np.zeros((64, EXT), np.int32)
    whole[0:24, :MID] = table
    whole[24:32] = ext
    whole[32:64, : 2 * LANES] = outer
    return whole


def dot(a, b):
    return jnp.dot(a, b, preferred_element_type=f32)


def picked(values, one_hot):
    high = values.astype(bf16)
    low = (values - high.astype(f32)).astype(bf16)
    both = dot(jnp.concatenate([high, low], 0), one_hot)
    return both[: values.shape[0]] + both[values.shape[0] :]


def as_one_hot(row_of_lane, depth):
    index = lax.broadcasted_iota(i32, (depth, row_of_lane.shape[1]), 0)
    return jnp.where(index == row_of_lane[0:1], 1.0, 0.0).astype(bf16)


def high_low_high(values):
    high = values.astype(bf16)
    low = (values - high.astype(f32)).astype(bf16)
    return [high, low, high]


def by_slot(halves, cell_of_lane):
    size = cell_of_lane.shape[1]
    halves = [jnp.broadcast_to(half, (8, LANES)) for half in halves]
    chosen = []
    for k in range(size // LANES):
        cell = cell_of_lane[:, k * LANES : (k + 1) * LANES]
        low, high = (jnp.take_along_axis(half, cell & (LANES - 1), axis=1) for half in halves)
        chosen.append(jnp.where(cell < 0, -1, jnp.where(cell < LANES, low, high)))
    return as_one_hot(jnp.concatenate(chosen, 1), ELEMENTS)


def stored_rows(fields_ref, others):
    fields = fields_ref[...].reshape(3 * NODES, ELEMENTS)
    others = [ref[...].reshape(NODES, ELEMENTS) for ref in others]
    return jnp.concatenate([fields[:NODES] - others[-1], fields[NODES:]] + others, 0)


def mass_tendency(table, p, u, v, area_depth, weighted_area, spin):
    slopes = dot(table[: 2 * NODES, : 3 * NODES], jnp.concatenate(high_low_high(p), 0))
    flux = high_low_high(area_depth * u)[:2] + high_low_high(area_depth * v)[:2]
    spread = dot(table[2 * NODES : 4 * NODES], jnp.concatenate(flux, 0))
    return [
        -(spread[:NODES] + spread[NODES:]),
        spin * v - weighted_area * slopes[:NODES],
        -spin * u - weighted_area * slopes[NODES:],
    ]


def edge_values(table_ref, weight_ref, p, u, v, area, depth, spin):
    root = jnp.sqrt(area)
    mass = jnp.concatenate([weight_ref[...]] * (area.shape[1] // LANES), 1) * area
    table = table_ref[...].astype(bf16)
    return mass_tendency(table, p, u, v, root * depth, root, mass * spin) + [mass]


def column_edges(table, weight, p, u, v, area, depth, spin):
    def ends(part):
        return jnp.concatenate([part[:NP], part[NODES - NP :]], 0)

    root = jnp.sqrt(area)
    area_depth = root * depth
    root, mass = ends(root), weight * ends(area)
    weighted_spin = mass * ends(spin)
    slopes = dot(table[: 4 * NP, : 3 * NODES], jnp.concatenate(high_low_high(p), 0))
    flux = high_low_high(area_depth * u)[:2] + high_low_high(area_depth * v)[:2]
    spread = dot(table[4 * NP :], jnp.concatenate(flux, 0))
    return [
        -(spread[: 2 * NP] + spread[2 * NP :]),
        weighted_spin * ends(v) - root * slopes[: 2 * NP],
        -weighted_spin * ends(u) - root * slopes[2 * NP :],
        mass,
    ]


def row_edges(sums):
    return tuple(sums[0, pl.ds(j, EDGE_ROWS, stride=NP)] for j in (NP - 1, 0))


def beside(left, right):
    return jnp.concatenate([left, right], 1)


def one_of_four(parts, index):
    out = parts[0]
    for k in range(1, 4):
        out = jnp.where(index == k, parts[k], out)
    return out


def folded(tide, kept, late, step):
    half = NODES // 2
    back = pltpu.roll(tide[half:], LANES - step, 1)
    onward = pltpu.roll(tide[half:], step, 1)
    return jnp.where(kept, tide[:half], jnp.where(late, back, onward))


def unfolded(rows, late, step):
    back = pltpu.roll(rows, LANES - step, 1)
    onward = pltpu.roll(rows, step, 1)
    return jnp.concatenate([rows, jnp.where(late, onward, back)], 0)


def strip_rows(parts, late, shift, rims):
    lane = lax.broadcasted_iota(i32, (1, LANES), 1)
    index = (lane >> shift) & 3
    kept = jnp.where(late, index // 2, 1 - index // 2) != 0
    tide = folded(parts[6], kept, late, 2 << shift)
    rim = one_of_four(rims, index)
    return jnp.concatenate(parts[:6] + [tide, rim, jnp.zeros_like(rim)], 0)


def placed_rows(whole, late, shift):
    half = NODES // 2
    tide = unfolded(whole[MOVED : MOVED + half], late, 2 << shift)
    rim = whole[MOVED + half : MOVED + half + NP]
    return jnp.concatenate([whole[:MOVED], tide] + spread_out(rim, late, shift), 0)


def spread_out(rim, late, shift):
    parts = []
    for k in range(4):
        first = pltpu.roll(rim, (LANES - (k << shift)) % LANES, 1) if k else rim
        last = pltpu.roll(rim, (3 - k) << shift, 1) if k < 3 else rim
        parts.append(jnp.where(late, first, last))
    return parts


def with_row_rim(whole, sums, top):
    north, south = row_edges(sums)
    rim = jnp.where(top, pltpu.roll(north, RING, 1), pltpu.roll(south, LANES - RING, 1))
    parts = [rim[k * NP : (k + 1) * NP] for k in range(4)]
    lane = lax.broadcasted_iota(i32, (1, LANES), 1)
    spots = []
    for k, part in enumerate(parts):
        first = pltpu.roll(part, k * RING, 1) if k else part
        last = pltpu.roll(part, (LANES - (3 - k) * RING) % LANES, 1) if k < 3 else part
        spots.append(jnp.where(top, first, last))
    rim = one_of_four(spots, (lane >> 2) & 3)
    return jnp.concatenate([whole[: MOVED + NODES // 2 + NP], rim], 0)


def in_eight(whole):
    whole = jnp.concatenate([whole, jnp.zeros((8 * CORNER_ROWS - whole.shape[0], LANES), f32)], 0)
    return [whole[k * CORNER_ROWS : (k + 1) * CORNER_ROWS] for k in range(8)]


def corner_of(whole, start, top):
    lane = lax.broadcasted_iota(i32, (1, LANES), 1)
    out = None
    for k, part in enumerate(in_eight(whole)):
        last = pltpu.roll(part, (LANES - start - 48 + 16 * k) % LANES, 1)
        first = pltpu.roll(part, (LANES - start + 16 * k) % LANES, 1)
        part = jnp.where(top != 0, last, first)
        out = part if k == 0 else jnp.where(lane >= 16 * k, part, out)
    return out


def both_corners(whole, odd):
    group = lax.broadcasted_iota(i32, (1, LANES), 1) >> 4
    other_group = (group + jnp.where(odd != 0, 7, 1)) & 7
    first, other = None, None
    for k, part in enumerate(in_eight(whole)):
        part = pltpu.roll(part, (LANES + 16 * k - 48 * odd) & (LANES - 1), 1)
        first = part if k == 0 else jnp.where(group == k, part, first)
        other = part if k == 0 else jnp.where(other_group == k, part, other)
    return first, other


def arrived_corners(far0, far1, block_cols, odd):
    lane = lax.broadcasted_iota(i32, (1, LANES), 1)
    corners = []
    for k in range(8):
        if block_cols == 1:
            part = jnp.where((lane >> 4) == k, far0, far1)
            part = pltpu.roll(part, (LANES + 64 + 16 * (1 - odd) - 16 * k) & (LANES - 1), 1)
        else:
            first = pltpu.roll(far0, (64 - 16 * k) % LANES, 1)
            other = pltpu.roll(far1, (80 - 16 * k) % LANES, 1)
            part = jnp.where((lane & 16) == 0, first, other)
        corners.append(part)
    return jnp.concatenate(corners, 0), ((lane >> 4) & 1) ^ (1 - odd if block_cols == 1 else 0)


def packed(whole):
    second = lax.broadcasted_iota(i32, (1, LANES), 1) >= 64
    top, bottom = whole[:HALF_ROWS], whole[HALF_ROWS:]
    return (
        jnp.where(second, pltpu.roll(bottom, 64, 1), top),
        jnp.where(second, bottom, pltpu.roll(top, 64, 1)),
    )


def unpacked(in0, in1):
    second = lax.broadcasted_iota(i32, (1, LANES), 1) >= 64
    top = jnp.where(second, pltpu.roll(in1, 64, 1), in0)
    bottom = jnp.where(second, in1, pltpu.roll(in0, 64, 1))
    return jnp.concatenate([top, bottom], 0)


def seam_flags(seam_ref, block_cols):
    size_y = seam_ref.shape[1]
    face = lax.axis_index("face")
    blk = lax.axis_index("blk")
    block_x = blk // BY

    def flipped(k):
        return jnp.where(lax.rem(seam_ref[k, 1] - seam_ref[k, 0] + size_y, size_y) != 1, 1, 0)

    first, second = flipped(0), flipped(1)
    east_flip = jnp.where(face == 0, first, second)
    west_flip = jnp.where(face == 0, second, first)
    if block_cols == 1:
        return 1 - east_flip, 0, east_flip, 1
    at_east = jnp.where(block_x == block_cols - 1, east_flip, 0)
    at_west = jnp.where(block_x == 0, west_flip, 0)
    return 1, at_east, 0, at_west


def slots_in(flags_ref):
    return flags_ref[4:5], flags_ref[5:6]


def flags_in(flags_ref, tiles=1):
    return [jnp.concatenate([flags_ref[k : k + 1]] * tiles, 1) for k in range(4)]


def strips_kernel(block_cols, *refs):
    sources, (out1_ref, out0_ref, stored_ref, flags_ref) = refs[:8], refs[8:12]
    buffers, sems = refs[12:20], refs[20]
    copies = [
        pltpu.make_async_copy(source, buffer, sems.at[k])
        for k, (source, buffer) in enumerate(zip(sources, buffers))
    ]
    for copy in copies:
        copy.start()
    seam_ref, slot_ref, fields_ref, area_ref, depth_ref, spin_ref, tide_ref = buffers[:7]
    table_ref = buffers[7]
    for copy in copies[:2]:
        copy.wait()
    east0, flip0, east1, flip1 = flags = seam_flags(seam_ref, block_cols)
    index = lax.broadcasted_iota(i32, (8, LANES), 0)
    flags_ref[...] = sum(jnp.where(index == k, flag, 0) for k, flag in enumerate(flags))
    slots = slot_ref[:, :LANES], slot_ref[:, LANES:]
    flags_ref[4:5], flags_ref[5:6] = slots
    lane = lax.broadcasted_iota(i32, (8, 2 * LANES), 1)
    second = (lane & 64) != 0
    place = lane & 63
    row = place >> 2
    row = jnp.where(jnp.where(second, flip1, flip0) != 0, GY - 1 - row, row)
    east = jnp.where(second, east1, east0) != 0
    col = jnp.where(east, GX - RING, 0) + (place & 3)
    col = jnp.where(lane >= LANES, jnp.where(east, GX - RING - 1, RING), col)
    one_hot = by_slot(slots, col * GY + row)
    for copy in copies[2:7]:
        copy.wait()
    stored = stored_rows(fields_ref, (area_ref, depth_ref, spin_ref, tide_ref))
    both = picked(stored, one_hot)

    lane = lax.broadcasted_iota(i32, (1, LANES), 1)
    second = lane >= 64
    flip = jnp.where(second, flip1, flip0) != 0
    sign = jnp.where(flip, -1.0, 1.0)
    node = lax.broadcasted_iota(i32, (1, NP, 1), 1)

    def turned(values):
        shaped = values.reshape(-1, NP, LANES)
        shaped = pltpu.roll(shaped, 4, 1)
        shaped = jnp.where((node & 2) == 0, pltpu.roll(shaped, 6, 1), pltpu.roll(shaped, 2, 1))
        shaped = jnp.where((node & 1) == 0, pltpu.roll(shaped, 7, 1), pltpu.roll(shaped, 1, 1))
        return shaped.reshape(values.shape)

    strip, ring = (
        [part[k * NODES : (k + 1) * NODES] for k in range(ARRAYS)]
        for part in (both[:, :LANES], both[:, LANES:])
    )
    for copy in copies[7:]:
        copy.wait()
    table, weight = table_ref[: 8 * NP].astype(bf16), table_ref[8 * NP :, :LANES]
    edges = column_edges(table, weight, *ring[:6])
    east = jnp.where(second, east1, east0) != 0
    ends = [jnp.where(east, part[NP:], part[:NP]) for part in edges]
    ends[2] = ends[2] * sign
    strip[2] = strip[2] * sign
    strip[5] = strip[5] * sign
    for ref, part, flip in zip(
        (out0_ref, out1_ref), packed(strip_rows(strip, east, 0, ends)), (flip0, flip1)
    ):
        if isinstance(flip, int):
            ref[...] = turned(part) if flip else part
        else:
            ref[...] = jnp.where(flip != 0, turned(part), part)
    stored_ref[...] = stored


def rows_kernel(
    block_cols, flags_ref, stored_ref, strip1_ref, strip0_ref, table_ref, weight_ref,
    next_ref, far0_ref, far1_ref, pair_ref, sums,
):
    east0, flip0, east1, flip1 = flags_in(flags_ref)
    odd = lax.axis_index("blk") & 1
    lane = lax.broadcasted_iota(i32, (8, 2 * LANES), 1)
    row = jnp.where(odd != 0, GY - RING, 0) + ((lane & 63) >> 4)
    row = jnp.where((lane & 64) != 0, jnp.where(odd != 0, GY - RING - 1, RING), row)
    five = jnp.where(odd != 0, 0, GY - RING - 1) + jnp.minimum((lane & (LANES - 1)) >> 4, RING)
    row = jnp.where(lane >= LANES, five, row)
    both = picked(stored_ref[...], by_slot(slots_in(flags_ref), (lane & 15) * GY + row))
    pair_ref[...] = both[:, LANES:]
    rows = [both[k * NODES : (k + 1) * NODES, :LANES] for k in range(ARRAYS)]
    whole = unpacked(strip0_ref[...], strip1_ref[...])
    strip = [whole[k * NODES : (k + 1) * NODES] for k in range(6)]
    edges = edge_values(table_ref, weight_ref, *map(beside, strip, rows[:6]))
    sums[0] = jnp.concatenate([part[:, :LANES] for part in edges], 0)
    lane = lax.broadcasted_iota(i32, (1, LANES), 1)
    top0, top1 = odd ^ flip0, odd ^ flip1
    whole = with_row_rim(whole, sums, jnp.where(lane >= 64, top1, top0) != 0)
    if block_cols == 1:
        far0_ref[...], far1_ref[...] = both_corners(whole, odd)
    else:
        far0_ref[...] = corner_of(whole, 0, top0)
        far1_ref[...] = corner_of(whole, 64, top1)
    sums[0] = jnp.concatenate([part[:, LANES:] for part in edges], 0)
    up = jnp.broadcast_to(odd != 0, (1, LANES))
    rim = pltpu.roll(jnp.where(up, *row_edges(sums)), 64, 1)
    rim = [rim[k * NP : (k + 1) * NP] for k in range(4)]
    whole = strip_rows(rows, up, 4, rim)
    top, bottom = whole[:HALF_ROWS], whole[HALF_ROWS:]
    next_ref[...] = jnp.where(lane >= 64, pltpu.roll(bottom, 64, 1), top)


def corners_kernel(flags_ref, in0_ref, in1_ref, pair_ref, _, out_ref):
    east0, flip0, east1, flip1 = flags_in(flags_ref)
    top = 1 - (lax.axis_index("blk") & 1)
    lane = lax.broadcasted_iota(i32, (1, LANES), 1)
    halves = []
    for start in (0, 64):
        at0 = jnp.where(top != 0, 36, 80)
        at1 = jnp.where(top != 0, 56, 100)
        first = pltpu.roll(in0_ref[...], (at0 - start) & (LANES - 1), 1)
        other = pltpu.roll(in1_ref[...], (at1 - start) & (LANES - 1), 1)
        halves.append(jnp.where(lane < 100, first, other))
    late = jnp.where(lane < 100, east0, east1) == 0
    whole = placed_rows(jnp.concatenate(halves, 0), late, 0)
    out_ref[:ROWS] = jnp.where(lane < 80, pair_ref[...], whole[:ROWS])
    out_ref[ROWS:] = whole[ROWS:]


def own_kernel(flags_ref, stored_ref, lanes_ref, own_ref, hot_ref):
    one_hot = by_slot(slots_in(flags_ref), lanes_ref[0:8, :MID])
    own_ref[...] = picked(stored_ref[...], one_hot)
    hot_ref[...] = one_hot.astype(f32).T.astype(bf16)


def first_sums(table, weight, parts, rims, at_rim):
    p, u, v, area, depth, spin, tide = parts
    size = area.shape[1]
    root = jnp.sqrt(area)
    mass = jnp.concatenate([weight] * (size // LANES), 1) * area
    used = [p, u, v, root * depth, root, mass * spin, tide]
    for part, rim in zip(mass_tendency(table, p, u, v, *used[3:6]) + [mass], rims):
        west, east = part[:NP], part[NODES - NP :]
        at_east = jnp.where(at_rim, rim, pltpu.roll(west, size - 1, 1))
        at_west = jnp.where(at_rim, rim, pltpu.roll(east, 1, 1))
        used.append(
            jnp.concatenate([west + at_west, part[NP : NODES - NP], east + at_east], 0)
        )
    return used


def middle_kernel(
    flags_ref, in0_ref, in1_ref, own_ref, lanes_ref, table_ref, weight_ref,
    low_ref, centre_ref, high_ref,
):
    east0, flip0, east1, flip1 = flags_in(flags_ref)
    second = lax.broadcasted_iota(i32, (1, LANES), 1) >= 64
    late = jnp.where(second, east1, east0) == 0
    whole = placed_rows(unpacked(in0_ref[...], in1_ref[...]), late, 0)
    side = lanes_ref[16:24, :MID]
    east = flags_in(flags_ref, MID // LANES)[0]
    first_at = jnp.where(side == 2, 64 * (1 - east), 64 * east)
    place = jnp.where(side == 0, -1, lanes_ref[8:16, :MID] + first_at)
    placed = picked(whole, as_one_hot(place, LANES))
    parts = [
        placed[k * NODES : (k + 1) * NODES] + own_ref[k * NODES : (k + 1) * NODES]
        for k in range(ARRAYS)
    ]
    rims = [placed[ROWS + c * NP : ROWS + (c + 1) * NP] for c in range(4)]
    at_rim = lanes_ref[24:25, LANES : LANES + MID] != 0
    used = first_sums(table_ref[...].astype(bf16), weight_ref[...], parts, rims, at_rim)
    for k, ref in enumerate((low_ref, centre_ref, high_ref)):
        for n, part in enumerate(used):
            ref[n * NODES : (n + 1) * NODES] = part[:, k * LANES : (k + 1) * LANES]


def far_kernel(block_cols, flags_ref, far1_ref, far0_ref, next_ref, _, out_ref):
    east0, flip0, east1, flip1 = flags_in(flags_ref)
    odd = lax.axis_index("blk") & 1
    lane = lax.broadcasted_iota(i32, (1, LANES), 1)
    below = jnp.broadcast_to(odd == 0, (1, LANES))
    strip = jnp.concatenate([next_ref[...], pltpu.roll(next_ref[...], 64, 1)], 0)
    strip = placed_rows(strip, below, 4)
    corners, strip_of = arrived_corners(far0_ref[...], far1_ref[...], block_cols, odd)
    late = jnp.where(strip_of != 0, east1, east0) == 0
    rim = MOVED + NODES // 2 + NP
    rim = jnp.concatenate(spread_out(corners[rim : rim + NP], below, 2), 0)
    corners = placed_rows(corners, late, 0)
    own = lane < 64
    out_ref[:ROWS] = jnp.where(own, strip[:ROWS], corners[:ROWS])
    out_ref[ROWS:ALL_ROWS] = corners[ROWS:]
    out_ref[ALL_ROWS:] = jnp.where(own, strip[ROWS:], rim)


def steps_kernel(
    block_cols, flags_ref, pair_ref, next_ref, low_ref, centre_ref,
    high_ref, hot_ref, table_ref, weight_ref, lanes_ref, out_ref, sums,
):
    east0, flip0, east1, flip1 = flags_in(flags_ref)
    odd = lax.axis_index("blk") & 1
    block_y = lax.rem(lax.axis_index("blk"), BY)

    lane = lax.broadcasted_iota(i32, (1, LANES), 1)
    pair = jnp.concatenate([pair_ref[...], jnp.zeros((EDGE_ROWS, LANES), f32)], 0)
    around = beside(pair, next_ref[...])
    outer_at = [lanes_ref[32 + 8 * k : 40 + 8 * k, : 2 * LANES] for k in range(4)]
    kind = outer_at[1]
    from_pair = jnp.where(outer_at[2] != 0, 1 - odd, odd) != 0
    east = flags_in(flags_ref, 2)[0]
    strip_at = jnp.where(kind == 3, 1 - east, east)
    far_at = strip_at ^ (1 - odd) if block_cols == 1 else strip_at
    strip_at, far_at = (jnp.where(kind > 1, at, 0) for at in (strip_at, far_at))
    place = jnp.where(
        from_pair,
        outer_at[0] + (RING + 1) * RING * strip_at,
        jnp.where(outer_at[3] < 0, -1, outer_at[3] + RING * RING * far_at),
    )
    outer = picked(around, as_one_hot(jnp.where(kind == 0, -1, place), 2 * LANES))
    table = table_ref[...].astype(bf16)
    tiles = (None, low_ref, centre_ref, high_ref, None)
    count = len(tiles)
    masks = [lanes_ref[24:32, k * LANES : (k + 1) * LANES] for k in range(count)]
    closed_above = jnp.where(block_y == BY - 1, masks[-2][1:2], 0) != 0
    closed_below = jnp.where(block_y == 0, masks[1][2:3], 0) != 0
    first_row = jnp.where(odd == 0, masks[0][4:5], 0) != 0
    last_row = jnp.where(odd != 0, masks[-1][5:6], 0) != 0
    outer_used = first_sums(
        table,
        weight_ref[...],
        [outer[k * NODES : (k + 1) * NODES] for k in range(ARRAYS)],
        [outer[ROWS + c * NP : ROWS + (c + 1) * NP] for c in range(4)],
        beside(masks[0][0:1], masks[-1][0:1]) != 0,
    )

    def shifted(parts, by, ring):
        turned = [pltpu.roll(part, -by % LANES, 1) for part in parts]
        size = len(parts)
        step = 1 if by > 0 else -1
        others = [(k + step) % size if ring else min(max(k + step, 0), size - 1) for k in range(size)]
        from_other = lane >= LANES - by if by > 0 else lane < -by
        return [jnp.where(from_other, turned[others[k]], turned[k]) for k in range(size)]

    def put_x_sums(groups, components):
        slots = [k for group in groups for k in group]
        ring = len(slots) < count
        per_tile = [
            [part[:, n * LANES : (n + 1) * LANES] for part in parts]
            for group, parts in zip(groups, components)
            for n in range(len(group))
        ]
        for c in range(3):
            parts = [tile[c] for tile in per_tile]
            west = [part[:NP] for part in parts]
            east = [part[NODES - NP :] for part in parts]
            at_east, at_west = shifted(west, 1, ring), shifted(east, -1, ring)
            for n, k in enumerate(slots):
                sums[k, c * NODES : c * NODES + NP] = west[n] + at_west[n]
                sums[k, c * NODES + NP : (c + 1) * NODES - NP] = parts[n][NP : NODES - NP]
                sums[k, (c + 1) * NODES - NP : (c + 1) * NODES] = east[n] + at_east[n]

    def edge_y(components, slots, rows=None):
        ring = len(slots) < count
        south_at = pl.ds(0, components * NP, stride=NP)
        north_at = pl.ds(NP - 1, components * NP, stride=NP)
        south = [sums[k, south_at] for k in slots]
        north = [sums[k, north_at] for k in slots]
        at_north, at_south = shifted(south, PITCH, ring), shifted(north, -PITCH, ring)
        for n, k in enumerate(slots):
            if k == count - 2:
                at_north[n] = jnp.where(closed_above, 0.0, at_north[n])
            if k == 1:
                at_south[n] = jnp.where(closed_below, 0.0, at_south[n])
        if rows is not None:
            at_south[0] = jnp.where(first_row, rows[0], at_south[0])
            at_north[-1] = jnp.where(last_row, rows[1], at_north[-1])
        for n, k in enumerate(slots):
            sums[k, south_at] = south[n] + at_south[n]
            sums[k, north_at] = north[n] + at_north[n]

    node = lax.broadcasted_iota(i32, (1, NP, 1), 1)
    rows = []
    for rim in (outer[ALL_ROWS:, :LANES], outer[ALL_ROWS:, LANES:]):
        east = pltpu.roll(rim, LANES - 1, 1).reshape(4, NP, LANES)
        west = pltpu.roll(rim, 1, 1).reshape(4, NP, LANES)
        rim = (
            rim.reshape(4, NP, LANES)
            + jnp.where(node == NP - 1, pltpu.roll(east, NP - 1, 1), 0.0)
            + jnp.where(node == 0, pltpu.roll(west, 1, 1), 0.0)
        )
        rows.append(rim.reshape(EDGE_ROWS, LANES))

    every = tuple(range(count))
    groups = (every[0:2], every[2:4], every[4:])

    def tile_part(k, n):
        if tiles[k] is None:
            return outer_used[n][:, :LANES] if k == 0 else outer_used[n][:, LANES:]
        return tiles[k][n * NODES : (n + 1) * NODES]

    def part_of(group, n):
        return jnp.concatenate([tile_part(k, n) for k in group], 1)

    def summed(group, c):
        return jnp.concatenate([sums[k, c * NODES : (c + 1) * NODES] for k in group], 1)

    def average(group, per_mass):
        return [summed(group, c) * per_mass for c in range(3)]

    def laplace(s):
        return [
            dot(table[4 * NODES :, : 3 * NODES], jnp.concatenate(high_low_high(part), 0))
            for part in s
        ]

    start = [[part_of(group, n) for n in range(3)] for group in groups]
    fixed = [[part_of(group, n) for n in range(3, 6)] for group in groups]
    for k in every:
        for c in range(4):
            sums[k, c * NODES : (c + 1) * NODES] = tile_part(k, 7 + c)
    edge_y(4, every, rows)
    per_mass = [1.0 / summed(group, 3) for group in groups]
    one = []
    for n, group in enumerate(groups):
        change = average(group, per_mass[n])
        one.append([s + time_step * c for s, c in zip(start[n], change)])
    put_x_sums(groups, [mass_tendency(table, *s, *f) for s, f in zip(one, fixed)])
    edge_y(3, every)
    two = []
    for n, group in enumerate(groups):
        change = average(group, per_mass[n])
        two.append(
            [0.75 * s + 0.25 * (o + time_step * c) for s, o, c in zip(start[n], one[n], change)]
        )
    put_x_sums(groups, [mass_tendency(table, *s, *f) for s, f in zip(two, fixed)])
    edge_y(3, every)

    def regrouped(per_group):
        (outer_low, high_above) = per_group[0], per_group[1]
        below, low = outer_low[:, :LANES], outer_low[:, LANES:]
        centre, high = high_above[:, :LANES], high_above[:, LANES:]
        near = jnp.where(lane < LANES // 2, per_group[2], below)
        return [beside(low, centre), beside(high, near)]

    def of_groups(values):
        return [list(parts) for parts in zip(*(regrouped(part) for part in zip(*values)))]

    for c in range(3):
        rows_at = slice(c * NODES, (c + 1) * NODES)
        sums[count - 1, rows_at] = jnp.where(
            lane < LANES // 2, sums[count - 1, rows_at], sums[0, rows_at]
        )
    slots = every[1:]
    groups = (slots[0:2], slots[2:4])
    start, two = of_groups(start), of_groups(two)
    tide = regrouped([part_of(every[0:2], 6), part_of(every[2:4], 6), part_of(every[4:], 6)])
    per_mass = regrouped(per_mass)
    three = []
    for n, group in enumerate(groups):
        change = average(group, per_mass[n])
        now = [
            s / 3.0 + 2.0 / 3.0 * (o + time_step * c)
            for s, o, c in zip(start[n], two[n], change)
        ]
        now[0] = now[0] + tide[n]
        three.append(now)
    put_x_sums(groups, [laplace(s) for s in three])
    edge_y(3, slots)
    change = [average(group, per_mass[n]) for n, group in enumerate(groups)]
    put_x_sums(groups, [laplace(s) for s in change])
    edge_y(3, slots)
    stepped = []
    for n, group in enumerate(groups):
        change = average(group, per_mass[n])
        now = [s - time_step * hyper_coeff * b for s, b in zip(three[n], change)]
        stepped.append(jnp.concatenate(now, 0))
    stepped = jnp.concatenate(stepped, 1)[:, :MID]
    own = lanes_ref[27:28, LANES : LANES + MID] != 0
    stored = picked(jnp.where(own, stepped, 0.0), hot_ref[...])
    out_ref[...] = stored.reshape(out_ref.shape)


def on_device(fields, jacobian, water_depth, coriolis, tide_height, slot_of, seam_rows):
    block_cols = lax.axis_size("blk") // BY
    table, weight, edge_table, lanes = map(jnp.asarray, (*operator_table(), lane_tables()))
    vmem = pl.BlockSpec(memory_space=pltpu.VMEM)
    hbm = pl.BlockSpec(memory_space=pltpu.HBM)
    params = pltpu.CompilerParams(vmem_limit_bytes=48 * 2**20)
    held = (fields, jacobian, water_depth, coriolis, tide_height)

    def call(kernel, ins, outs, cost, scratch=(), name=None):
        return pl.pallas_call(
            kernel,
            out_shape=[jax.ShapeDtypeStruct(*out) for out in outs],
            in_specs=[spec for spec, value in ins],
            out_specs=[vmem] * len(outs),
            scratch_shapes=list(scratch),
            compiler_params=params,
            cost_estimate=pl.CostEstimate(
                flops=cost, bytes_accessed=2 * 2**20, transcendentals=0
            ),
            name=name,
        )(
            *[
                pltpu.with_memory_space_constraint(value, pltpu.HBM) if spec is hbm else value
                for spec, value in ins
            ]
        )

    strip = ((HALF_ROWS, LANES), f32)
    def room(values, spaces=None):
        spaces = spaces or [pltpu.VMEM] * len(values)
        buffers = [space(x.shape, x.dtype) for space, x in zip(spaces, values)]
        return buffers + [pltpu.SemaphoreType.DMA((len(values),))]

    needed = (seam_rows, slot_of, *held, edge_table)
    corner = ((CORNER_ROWS, LANES), f32)
    scratch = [pltpu.VMEM((1, 4 * NODES, LANES), f32)]
    strip1, strip0, stored, flags = call(
        functools.partial(strips_kernel, block_cols),
        [(hbm, x) for x in needed],
        [strip, strip, ((ROWS, ELEMENTS), f32), ((8, LANES), i32)],
        10**8,
        scratch=room(needed, [pltpu.SMEM] + [pltpu.VMEM] * (len(needed) - 1)),
        name="strips",
    )
    to_next, far0, far1, to_pair = call(
        functools.partial(rows_kernel, block_cols),
        [(vmem, x) for x in (flags, stored, strip1, strip0, table, weight)],
        [strip, corner, corner, ((ROWS, LANES), f32)],
        10**8,
        scratch=scratch,
        name="rows",
    )
    span = block_cols * BY
    both = ("face", "blk")
    places = [(f, x, y) for f in range(2) for x in range(block_cols) for y in range(BY)]

    def rank(face, block_x, block_y):
        return face * span + block_x * BY + block_y

    def same(y):
        return y

    def in_pair(y):
        return y ^ 1

    def next_pair(y):
        other = y + 1 if y % 2 else y - 1
        return other if 0 <= other < BY else y

    def swapped(value, partner):
        pairs = [
            (rank(f, x, y), rank(f if partner(y) != y else 1 - f, x, partner(y)))
            for f, x, y in places
        ]
        return lax.ppermute(value, both, pairs)

    def across(value0, value1, partner):
        last = block_cols - 1

        def aligned(y):
            return partner is same or partner(y) != y

        straight = {
            (f, x, y): (f, x + 1, partner(y)) if x < last else (1 - f, 0, partner(y))
            for f, x, y in places
        }
        turned = {
            (f, last, y): (1 - f, 0, BY - 1 - partner(y) if aligned(y) else y)
            for f in range(2)
            for y in range(BY)
        }

        def eastward(value, pairs):
            return lax.ppermute(value, both, [(rank(*a), rank(*b)) for a, b in pairs.items()])

        def westward(value, pairs):
            return lax.ppermute(value, both, [(rank(*b), rank(*a)) for a, b in pairs.items()])

        if block_cols == 1:
            return eastward(value0, straight), eastward(value1, turned)
        flipped = (seam_rows[:, 1] - seam_rows[:, 0]) % seam_rows.shape[1] != 1
        face = lax.axis_index("face")
        block_x = lax.axis_index("blk") // BY
        return (
            jnp.where(
                (block_x == last) & flipped[face],
                westward(value1, turned),
                westward(value1, straight),
            ),
            jnp.where(
                (block_x == 0) & flipped[1 - face],
                eastward(value0, turned),
                eastward(value0, straight),
            ),
        )

    halo0, halo1 = across(strip0, strip1, same)
    far0, far1 = across(far0, far1, next_pair)
    from_next = swapped(to_next, next_pair)
    own, hot = call(
        own_kernel,
        [(vmem, x) for x in (flags, stored, lanes)],
        [((ROWS, MID), f32), ((MID, ELEMENTS), bf16)],
        10**8,
        name="own",
    )
    (to_pair,) = call(
        corners_kernel,
        [(vmem, x) for x in (flags, halo0, halo1, to_pair, hot)],
        [((ALL_ROWS, LANES), f32)],
        10**8,
        name="corners",
    )
    from_pair = swapped(to_pair, in_pair)
    tile = ((11 * NODES, LANES), f32)
    low, centre, high = call(
        middle_kernel,
        [(vmem, x) for x in (flags, halo0, halo1, own, lanes, table, weight)],
        [tile, tile, tile],
        10**8,
        name="middle",
    )
    (from_next,) = call(
        functools.partial(far_kernel, block_cols),
        [(vmem, x) for x in (flags, far1, far0, from_next, low)],
        [((RIM_ROWS, LANES), f32)],
        10**11,
        name="far",
    )
    (stepped,) = call(
        functools.partial(steps_kernel, block_cols),
        [
            (vmem, x)
            for x in (
                flags, from_pair, from_next, low, centre, high, hot, table, weight, lanes
            )
        ],
        [(fields.shape, f32)],
        10**8,
        scratch=[pltpu.VMEM((EXT // LANES, 4 * NODES, LANES), f32)],
        name="steps",
    )
    return stepped


def solution(mesh):
    return jax.shard_map(
        on_device,
        mesh=mesh,
        in_specs=(
            P(None, None, None, ("face", "blk")),
            P(None, None, ("face", "blk")),
            P(None, None, ("face", "blk")),
            P(None, None, ("face", "blk")),
            P(None, None, ("face", "blk")),
            P(("face", "blk"), None),
            P(),
        ),
        out_specs=P(None, None, None, ("face", "blk")),
        check_vma=False,
    )
```

```python
import functools
import math

import jax
import jax.numpy as jnp
import ml_dtypes
import numpy as np
from jax import lax
from jax.experimental import pallas as pl
from jax.experimental.pallas import tpu as pltpu
from jax.sharding import PartitionSpec as P

BY = 16
GX = 16
GY = 16
NP = 8
NODES = NP * NP
ARRAYS = 7
ROWS = ARRAYS * NODES
MOVED = 6 * NODES
EDGE_ROWS = 4 * NP
ALL_ROWS = ROWS + EDGE_ROWS
HALF_ROWS = (MOVED + NODES // 2 + 2 * NP) // 2
RING = 4
RIM_ROWS = ROWS + 2 * EDGE_ROWS
CORNER_ROWS = (MOVED + NODES // 2 + 4 * NP) // 8
PITCH = GX + 2 * RING
MID = GY * PITCH
LANES = 128
EXT = MID + 2 * LANES
LEAD = LANES - RING * PITCH
ELEMENTS = GX * GY

time_step = 0.03
hyper_coeff = 0.0002

f32 = jnp.float32
bf16 = jnp.bfloat16
i32 = jnp.int32


def legendre_pair(location, degree):
    lower_value = 1.0
    upper_value = location
    for polynomial_order in range(2, degree + 1):
        lower_value, upper_value = (
            upper_value,
            (
                (2 * polynomial_order - 1) * location * upper_value
                - (polynomial_order - 1) * lower_value
            )
            / polynomial_order,
        )
    return (lower_value, upper_value)


def gll_tables(points):
    degree = points - 1
    locations = [-math.cos(math.pi * position / degree) for position in range(points)]
    for iteration in range(100):
        updated = []
        for location in locations:
            lower_value, upper_value = legendre_pair(location, degree)
            updated.append(
                location - (location * upper_value - lower_value) / ((degree + 1) * upper_value)
            )
        locations = updated
    locations[0] = -1.0
    locations[degree] = 1.0
    legendre_at = [legendre_pair(location, degree)[1] for location in locations]
    weights = [2.0 / (degree * (degree + 1) * value * value) for value in legendre_at]
    corner_value = degree * (degree + 1) / 4.0
    derivative = []
    for row_index in range(points):
        row_values = []
        for column_index in range(points):
            if row_index != column_index:
                row_values.append(
                    legendre_at[row_index]
                    / (legendre_at[column_index] * (locations[row_index] - locations[column_index]))
                )
            elif row_index == 0:
                row_values.append(-corner_value)
            elif row_index == degree:
                row_values.append(corner_value)
            else:
                row_values.append(0.0)
        derivative.append(row_values)
    return np.asarray(weights, np.float64), np.asarray(derivative, np.float64)


def in_three(matrix):
    high = matrix.astype(ml_dtypes.bfloat16)
    low = (matrix - high.astype(np.float64)).astype(ml_dtypes.bfloat16)
    return np.concatenate([high, high, low], 1)


def operator_table():
    weights, derivative = gll_tables(NP)
    eye = np.eye(NP)
    node_weight = np.outer(weights, weights).reshape(NODES, 1)
    along_x = node_weight * np.kron(derivative, eye)
    along_y = node_weight * np.kron(eye, derivative)
    second = derivative @ derivative
    both = node_weight * (np.kron(second, eye) + np.kron(eye, second))
    table = np.zeros((5 * NODES, 4 * NODES), ml_dtypes.bfloat16)
    table[:NODES, : 3 * NODES] = in_three(along_x)
    table[NODES : 2 * NODES, : 3 * NODES] = in_three(along_y)
    flux = [in_three(along_x), in_three(along_y)]
    for k, part in enumerate(flux):
        at = 2 * k * NODES
        table[2 * NODES : 3 * NODES, at : at + 2 * NODES] = part[:, : 2 * NODES]
        table[3 * NODES : 4 * NODES, at : at + NODES] = part[:, 2 * NODES :]
    table[4 * NODES :, : 3 * NODES] = in_three(both)
    table = table.astype(np.float32)
    spread = np.broadcast_to(node_weight, (NODES, LANES)).astype(np.float32)
    ends = np.r_[:NP, NODES - NP : NODES]
    edge_table = np.zeros((10 * NP, 4 * NODES), np.float32)
    for k in range(4):
        edge_table[2 * k * NP : 2 * (k + 1) * NP] = table[k * NODES + ends]
    edge_table[8 * NP :, :LANES] = spread[ends]
    return table, np.ascontiguousarray(spread), edge_table


def lane_tables():
    table = np.zeros((24, MID), np.int32)
    for lane in range(MID):
        row, col = divmod(lane, PITCH)
        x = col - RING
        own = 0 <= x < GX
        table[0:8, lane] = x * GY + row if own else -1
        if not own:
            table[8:16, lane] = row * RING + (col if x < 0 else x - GX)
        table[16:24, lane] = 0 if own else (1 if x < 0 else 2)
    ext = np.zeros((8, EXT), np.int32)
    outer = np.zeros((32, 2 * LANES), np.int32)
    for lane in range(EXT):
        row, col = divmod(lane - LEAD, PITCH)
        y = row - RING
        x = col - RING
        ext[0, lane] = x in (-RING, GX + RING - 1)
        ext[1, lane] = y == GY - 1
        ext[2, lane] = y == 0
        ext[3, lane] = 0 <= y < GY and 0 <= x < GX
        ext[4, lane] = y == -RING
        ext[5, lane] = y == GY + RING - 1
        if -RING - 1 <= y < 0 or GY <= y <= GY + RING:
            place = lane if y < 0 else lane - MID
            step = y + RING if y < 0 else y - GY
            near = step + 1 if y < 0 else step
            far = 0 <= step < RING
            if 0 <= x < GX:
                outer[0:8, place] = near * GX + x
                outer[8:16, place] = 1
                outer[24:32, place] = LANES + step * GX + x if far else -1
            else:
                across = x + RING if x < 0 else x - GX
                outer[0:8, place] = (RING + 1) * GX + near * RING + across
                outer[8:16, place] = 2 if x < 0 else 3
                outer[24:32, place] = LANES + RING * GX + step * RING + across if far else -1
            outer[16:24, place] = y > 0
    whole = np.zeros((64, EXT), np.int32)
    whole[0:24, :MID] = table
    whole[24:32] = ext
    whole[32:64, : 2 * LANES] = outer
    return whole


def dot(a, b):
    return jnp.dot(a, b, preferred_element_type=f32)


def picked(values, one_hot):
    high = values.astype(bf16)
    low = (values - high.astype(f32)).astype(bf16)
    both = dot(jnp.concatenate([high, low], 0), one_hot)
    return both[: values.shape[0]] + both[values.shape[0] :]


def as_one_hot(row_of_lane, depth):
    index = lax.broadcasted_iota(i32, (depth, row_of_lane.shape[1]), 0)
    return jnp.where(index == row_of_lane[0:1], 1.0, 0.0).astype(bf16)


def high_low_high(values):
    high = values.astype(bf16)
    low = (values - high.astype(f32)).astype(bf16)
    return [high, low, high]


def by_slot(halves, cell_of_lane):
    size = cell_of_lane.shape[1]
    halves = [jnp.broadcast_to(half, (8, LANES)) for half in halves]
    chosen = []
    for k in range(size // LANES):
        cell = cell_of_lane[:, k * LANES : (k + 1) * LANES]
        low, high = (jnp.take_along_axis(half, cell & (LANES - 1), axis=1) for half in halves)
        chosen.append(jnp.where(cell < 0, -1, jnp.where(cell < LANES, low, high)))
    return as_one_hot(jnp.concatenate(chosen, 1), ELEMENTS)


def stored_rows(fields_ref, others):
    fields = fields_ref[...].reshape(3 * NODES, ELEMENTS)
    others = [ref[...].reshape(NODES, ELEMENTS) for ref in others]
    return jnp.concatenate([fields[:NODES] - others[-1], fields[NODES:]] + others, 0)


def mass_tendency(table, p, u, v, area_depth, weighted_area, spin):
    slopes = dot(table[: 2 * NODES, : 3 * NODES], jnp.concatenate(high_low_high(p), 0))
    flux = high_low_high(area_depth * u)[:2] + high_low_high(area_depth * v)[:2]
    spread = dot(table[2 * NODES : 4 * NODES], jnp.concatenate(flux, 0))
    return [
        -(spread[:NODES] + spread[NODES:]),
        spin * v - weighted_area * slopes[:NODES],
        -spin * u - weighted_area * slopes[NODES:],
    ]


def edge_values(table_ref, weight_ref, p, u, v, area, depth, spin):
    root = jnp.sqrt(area)
    mass = jnp.concatenate([weight_ref[...]] * (area.shape[1] // LANES), 1) * area
    table = table_ref[...].astype(bf16)
    return mass_tendency(table, p, u, v, root * depth, root, mass * spin) + [mass]


def column_edges(table, weight, p, u, v, area, depth, spin):
    def ends(part):
        return jnp.concatenate([part[:NP], part[NODES - NP :]], 0)

    root = jnp.sqrt(area)
    area_depth = root * depth
    root, mass = ends(root), weight * ends(area)
    weighted_spin = mass * ends(spin)
    slopes = dot(table[: 4 * NP, : 3 * NODES], jnp.concatenate(high_low_high(p), 0))
    flux = high_low_high(area_depth * u)[:2] + high_low_high(area_depth * v)[:2]
    spread = dot(table[4 * NP :], jnp.concatenate(flux, 0))
    return [
        -(spread[: 2 * NP] + spread[2 * NP :]),
        weighted_spin * ends(v) - root * slopes[: 2 * NP],
        -weighted_spin * ends(u) - root * slopes[2 * NP :],
        mass,
    ]


def row_edges(sums):
    return tuple(sums[0, pl.ds(j, EDGE_ROWS, stride=NP)] for j in (NP - 1, 0))


def beside(left, right):
    return jnp.concatenate([left, right], 1)


def one_of_four(parts, index):
    out = parts[0]
    for k in range(1, 4):
        out = jnp.where(index == k, parts[k], out)
    return out


def folded(tide, kept, late, step):
    half = NODES // 2
    back = pltpu.roll(tide[half:], LANES - step, 1)
    onward = pltpu.roll(tide[half:], step, 1)
    return jnp.where(kept, tide[:half], jnp.where(late, back, onward))


def unfolded(rows, late, step):
    back = pltpu.roll(rows, LANES - step, 1)
    onward = pltpu.roll(rows, step, 1)
    return jnp.concatenate([rows, jnp.where(late, onward, back)], 0)


def strip_rows(parts, late, shift, rims):
    lane = lax.broadcasted_iota(i32, (1, LANES), 1)
    index = (lane >> shift) & 3
    kept = jnp.where(late, index // 2, 1 - index // 2) != 0
    tide = folded(parts[6], kept, late, 2 << shift)
    rim = one_of_four(rims, index)
    return jnp.concatenate(parts[:6] + [tide, rim, jnp.zeros_like(rim)], 0)


def placed_rows(whole, late, shift):
    half = NODES // 2
    tide = unfolded(whole[MOVED : MOVED + half], late, 2 << shift)
    rim = whole[MOVED + half : MOVED + half + NP]
    return jnp.concatenate([whole[:MOVED], tide] + spread_out(rim, late, shift), 0)


def spread_out(rim, late, shift):
    parts = []
    for k in range(4):
        first = pltpu.roll(rim, (LANES - (k << shift)) % LANES, 1) if k else rim
        last = pltpu.roll(rim, (3 - k) << shift, 1) if k < 3 else rim
        parts.append(jnp.where(late, first, last))
    return parts


def with_row_rim(whole, sums, top):
    north, south = row_edges(sums)
    rim = jnp.where(top, pltpu.roll(north, RING, 1), pltpu.roll(south, LANES - RING, 1))
    parts = [rim[k * NP : (k + 1) * NP] for k in range(4)]
    lane = lax.broadcasted_iota(i32, (1, LANES), 1)
    spots = []
    for k, part in enumerate(parts):
        first = pltpu.roll(part, k * RING, 1) if k else part
        last = pltpu.roll(part, (LANES - (3 - k) * RING) % LANES, 1) if k < 3 else part
        spots.append(jnp.where(top, first, last))
    rim = one_of_four(spots, (lane >> 2) & 3)
    return jnp.concatenate([whole[: MOVED + NODES // 2 + NP], rim], 0)


def in_eight(whole):
    whole = jnp.concatenate([whole, jnp.zeros((8 * CORNER_ROWS - whole.shape[0], LANES), f32)], 0)
    return [whole[k * CORNER_ROWS : (k + 1) * CORNER_ROWS] for k in range(8)]


def corner_of(whole, start, top):
    lane = lax.broadcasted_iota(i32, (1, LANES), 1)
    out = None
    for k, part in enumerate(in_eight(whole)):
        last = pltpu.roll(part, (LANES - start - 48 + 16 * k) % LANES, 1)
        first = pltpu.roll(part, (LANES - start + 16 * k) % LANES, 1)
        part = jnp.where(top != 0, last, first)
        out = part if k == 0 else jnp.where(lane >= 16 * k, part, out)
    return out


def both_corners(whole, odd):
    group = lax.broadcasted_iota(i32, (1, LANES), 1) >> 4
    other_group = (group + jnp.where(odd != 0, 7, 1)) & 7
    first, other = None, None
    for k, part in enumerate(in_eight(whole)):
        part = pltpu.roll(part, (LANES + 16 * k - 48 * odd) & (LANES - 1), 1)
        first = part if k == 0 else jnp.where(group == k, part, first)
        other = part if k == 0 else jnp.where(other_group == k, part, other)
    return first, other


def arrived_corners(far0, far1, block_cols, odd):
    lane = lax.broadcasted_iota(i32, (1, LANES), 1)
    corners = []
    for k in range(8):
        if block_cols == 1:
            part = jnp.where((lane >> 4) == k, far0, far1)
            part = pltpu.roll(part, (LANES + 64 + 16 * (1 - odd) - 16 * k) & (LANES - 1), 1)
        else:
            first = pltpu.roll(far0, (64 - 16 * k) % LANES, 1)
            other = pltpu.roll(far1, (80 - 16 * k) % LANES, 1)
            part = jnp.where((lane & 16) == 0, first, other)
        corners.append(part)
    return jnp.concatenate(corners, 0), ((lane >> 4) & 1) ^ (1 - odd if block_cols == 1 else 0)


def packed(whole):
    second = lax.broadcasted_iota(i32, (1, LANES), 1) >= 64
    top, bottom = whole[:HALF_ROWS], whole[HALF_ROWS:]
    return (
        jnp.where(second, pltpu.roll(bottom, 64, 1), top),
        jnp.where(second, bottom, pltpu.roll(top, 64, 1)),
    )


def unpacked(in0, in1):
    second = lax.broadcasted_iota(i32, (1, LANES), 1) >= 64
    top = jnp.where(second, pltpu.roll(in1, 64, 1), in0)
    bottom = jnp.where(second, in1, pltpu.roll(in0, 64, 1))
    return jnp.concatenate([top, bottom], 0)


def seam_flags(seam_ref, block_cols):
    size_y = seam_ref.shape[1]
    face = lax.axis_index("face")
    blk = lax.axis_index("blk")
    block_x = blk // BY

    def flipped(k):
        return jnp.where(lax.rem(seam_ref[k, 1] - seam_ref[k, 0] + size_y, size_y) != 1, 1, 0)

    first, second = flipped(0), flipped(1)
    east_flip = jnp.where(face == 0, first, second)
    west_flip = jnp.where(face == 0, second, first)
    if block_cols == 1:
        return 1 - east_flip, 0, east_flip, 1
    at_east = jnp.where(block_x == block_cols - 1, east_flip, 0)
    at_west = jnp.where(block_x == 0, west_flip, 0)
    return 1, at_east, 0, at_west


def slots_in(flags_ref):
    return flags_ref[4:5], flags_ref[5:6]


def flags_in(flags_ref, tiles=1):
    return [jnp.concatenate([flags_ref[k : k + 1]] * tiles, 1) for k in range(4)]


def mirrored_first(block_y):
    return (block_y >= BY // 4) & (block_y < BY - BY // 4)


def in_order(block_cols, first, second):
    if block_cols > 1:
        return first, second
    swap = mirrored_first(lax.rem(lax.axis_index("blk"), BY))
    return jnp.where(swap, second, first), jnp.where(swap, first, second)


def strips_kernel(block_cols, *refs):
    sources, (first_ref, then_ref, stored_ref, flags_ref) = refs[:8], refs[8:12]
    buffers, sems = refs[12:20], refs[20]
    copies = [
        pltpu.make_async_copy(source, buffer, sems.at[k])
        for k, (source, buffer) in enumerate(zip(sources, buffers))
    ]
    for copy in copies:
        copy.start()
    seam_ref, slot_ref, fields_ref, area_ref, depth_ref, spin_ref, tide_ref = buffers[:7]
    table_ref = buffers[7]
    for copy in copies[:2]:
        copy.wait()
    east0, flip0, east1, flip1 = flags = seam_flags(seam_ref, block_cols)
    index = lax.broadcasted_iota(i32, (8, LANES), 0)
    flags_ref[...] = sum(jnp.where(index == k, flag, 0) for k, flag in enumerate(flags))
    slots = slot_ref[:, :LANES], slot_ref[:, LANES:]
    flags_ref[4:5], flags_ref[5:6] = slots
    lane = lax.broadcasted_iota(i32, (8, 2 * LANES), 1)
    second = (lane & 64) != 0
    place = lane & 63
    row = place >> 2
    row = jnp.where(jnp.where(second, flip1, flip0) != 0, GY - 1 - row, row)
    east = jnp.where(second, east1, east0) != 0
    col = jnp.where(east, GX - RING, 0) + (place & 3)
    col = jnp.where(lane >= LANES, jnp.where(east, GX - RING - 1, RING), col)
    one_hot = by_slot(slots, col * GY + row)
    for copy in copies[2:7]:
        copy.wait()
    stored = stored_rows(fields_ref, (area_ref, depth_ref, spin_ref, tide_ref))
    both = picked(stored, one_hot)

    lane = lax.broadcasted_iota(i32, (1, LANES), 1)
    second = lane >= 64
    flip = jnp.where(second, flip1, flip0) != 0
    sign = jnp.where(flip, -1.0, 1.0)
    node = lax.broadcasted_iota(i32, (1, NP, 1), 1)

    def turned(values):
        shaped = values.reshape(-1, NP, LANES)
        shaped = pltpu.roll(shaped, 4, 1)
        shaped = jnp.where((node & 2) == 0, pltpu.roll(shaped, 6, 1), pltpu.roll(shaped, 2, 1))
        shaped = jnp.where((node & 1) == 0, pltpu.roll(shaped, 7, 1), pltpu.roll(shaped, 1, 1))
        return shaped.reshape(values.shape)

    strip, ring = (
        [part[k * NODES : (k + 1) * NODES] for k in range(ARRAYS)]
        for part in (both[:, :LANES], both[:, LANES:])
    )
    for copy in copies[7:]:
        copy.wait()
    table, weight = table_ref[: 8 * NP].astype(bf16), table_ref[8 * NP :, :LANES]
    edges = column_edges(table, weight, *ring[:6])
    east = jnp.where(second, east1, east0) != 0
    ends = [jnp.where(east, part[NP:], part[:NP]) for part in edges]
    ends[2] = ends[2] * sign
    strip[2] = strip[2] * sign
    strip[5] = strip[5] * sign
    strips = []
    for part, flip in zip(packed(strip_rows(strip, east, 0, ends)), (flip0, flip1)):
        if isinstance(flip, int):
            strips.append(turned(part) if flip else part)
        else:
            strips.append(jnp.where(flip != 0, turned(part), part))
    first_ref[...], then_ref[...] = in_order(block_cols, *strips)
    stored_ref[...] = stored


def rows_kernel(
    block_cols, flags_ref, stored_ref, first_ref, then_ref, table_ref, weight_ref,
    next_ref, far0_ref, far1_ref, pair_ref, sums,
):
    east0, flip0, east1, flip1 = flags_in(flags_ref)
    odd = lax.axis_index("blk") & 1
    lane = lax.broadcasted_iota(i32, (8, 2 * LANES), 1)
    row = jnp.where(odd != 0, GY - RING, 0) + ((lane & 63) >> 4)
    row = jnp.where((lane & 64) != 0, jnp.where(odd != 0, GY - RING - 1, RING), row)
    five = jnp.where(odd != 0, 0, GY - RING - 1) + jnp.minimum((lane & (LANES - 1)) >> 4, RING)
    row = jnp.where(lane >= LANES, five, row)
    both = picked(stored_ref[...], by_slot(slots_in(flags_ref), (lane & 15) * GY + row))
    pair_ref[...] = both[:, LANES:]
    rows = [both[k * NODES : (k + 1) * NODES, :LANES] for k in range(ARRAYS)]
    whole = unpacked(*in_order(block_cols, first_ref[...], then_ref[...]))
    strip = [whole[k * NODES : (k + 1) * NODES] for k in range(6)]
    edges = edge_values(table_ref, weight_ref, *map(beside, strip, rows[:6]))
    sums[0] = jnp.concatenate([part[:, :LANES] for part in edges], 0)
    lane = lax.broadcasted_iota(i32, (1, LANES), 1)
    top0, top1 = odd ^ flip0, odd ^ flip1
    whole = with_row_rim(whole, sums, jnp.where(lane >= 64, top1, top0) != 0)
    if block_cols == 1:
        far0_ref[...], far1_ref[...] = both_corners(whole, odd)
    else:
        far0_ref[...] = corner_of(whole, 0, top0)
        far1_ref[...] = corner_of(whole, 64, top1)
    sums[0] = jnp.concatenate([part[:, LANES:] for part in edges], 0)
    up = jnp.broadcast_to(odd != 0, (1, LANES))
    rim = pltpu.roll(jnp.where(up, *row_edges(sums)), 64, 1)
    rim = [rim[k * NP : (k + 1) * NP] for k in range(4)]
    whole = strip_rows(rows, up, 4, rim)
    top, bottom = whole[:HALF_ROWS], whole[HALF_ROWS:]
    next_ref[...] = jnp.where(lane >= 64, pltpu.roll(bottom, 64, 1), top)


def corners_kernel(block_cols, flags_ref, first_ref, then_ref, pair_ref, _, out_ref):
    east0, flip0, east1, flip1 = flags_in(flags_ref)
    in0, in1 = in_order(block_cols, first_ref[...], then_ref[...])
    top = 1 - (lax.axis_index("blk") & 1)
    lane = lax.broadcasted_iota(i32, (1, LANES), 1)
    halves = []
    for start in (0, 64):
        at0 = jnp.where(top != 0, 36, 80)
        at1 = jnp.where(top != 0, 56, 100)
        first = pltpu.roll(in0, (at0 - start) & (LANES - 1), 1)
        other = pltpu.roll(in1, (at1 - start) & (LANES - 1), 1)
        halves.append(jnp.where(lane < 100, first, other))
    late = jnp.where(lane < 100, east0, east1) == 0
    whole = placed_rows(jnp.concatenate(halves, 0), late, 0)
    out_ref[:ROWS] = jnp.where(lane < 80, pair_ref[...], whole[:ROWS])
    out_ref[ROWS:] = whole[ROWS:]


def own_kernel(flags_ref, stored_ref, lanes_ref, own_ref, hot_ref):
    one_hot = by_slot(slots_in(flags_ref), lanes_ref[0:8, :MID])
    own_ref[...] = picked(stored_ref[...], one_hot)
    hot_ref[...] = one_hot.astype(f32).T.astype(bf16)


def first_sums(table, weight, parts, rims, at_rim):
    p, u, v, area, depth, spin, tide = parts
    size = area.shape[1]
    root = jnp.sqrt(area)
    mass = jnp.concatenate([weight] * (size // LANES), 1) * area
    used = [p, u, v, root * depth, root, mass * spin, tide]
    for part, rim in zip(mass_tendency(table, p, u, v, *used[3:6]) + [mass], rims):
        west, east = part[:NP], part[NODES - NP :]
        at_east = jnp.where(at_rim, rim, pltpu.roll(west, size - 1, 1))
        at_west = jnp.where(at_rim, rim, pltpu.roll(east, 1, 1))
        used.append(
            jnp.concatenate([west + at_west, part[NP : NODES - NP], east + at_east], 0)
        )
    return used


def middle_kernel(
    block_cols, flags_ref, first_ref, then_ref, own_ref, lanes_ref, table_ref, weight_ref,
    low_ref, centre_ref, high_ref,
):
    east0, flip0, east1, flip1 = flags_in(flags_ref)
    second = lax.broadcasted_iota(i32, (1, LANES), 1) >= 64
    late = jnp.where(second, east1, east0) == 0
    whole = unpacked(*in_order(block_cols, first_ref[...], then_ref[...]))
    whole = placed_rows(whole, late, 0)
    side = lanes_ref[16:24, :MID]
    east = flags_in(flags_ref, MID // LANES)[0]
    first_at = jnp.where(side == 2, 64 * (1 - east), 64 * east)
    place = jnp.where(side == 0, -1, lanes_ref[8:16, :MID] + first_at)
    placed = picked(whole, as_one_hot(place, LANES))
    parts = [
        placed[k * NODES : (k + 1) * NODES] + own_ref[k * NODES : (k + 1) * NODES]
        for k in range(ARRAYS)
    ]
    rims = [placed[ROWS + c * NP : ROWS + (c + 1) * NP] for c in range(4)]
    at_rim = lanes_ref[24:25, LANES : LANES + MID] != 0
    used = first_sums(table_ref[...].astype(bf16), weight_ref[...], parts, rims, at_rim)
    for k, ref in enumerate((low_ref, centre_ref, high_ref)):
        for n, part in enumerate(used):
            ref[n * NODES : (n + 1) * NODES] = part[:, k * LANES : (k + 1) * LANES]


def far_kernel(block_cols, flags_ref, far1_ref, far0_ref, next_ref, _, out_ref):
    east0, flip0, east1, flip1 = flags_in(flags_ref)
    odd = lax.axis_index("blk") & 1
    lane = lax.broadcasted_iota(i32, (1, LANES), 1)
    below = jnp.broadcast_to(odd == 0, (1, LANES))
    strip = jnp.concatenate([next_ref[...], pltpu.roll(next_ref[...], 64, 1)], 0)
    strip = placed_rows(strip, below, 4)
    corners, strip_of = arrived_corners(far0_ref[...], far1_ref[...], block_cols, odd)
    late = jnp.where(strip_of != 0, east1, east0) == 0
    rim = MOVED + NODES // 2 + NP
    rim = jnp.concatenate(spread_out(corners[rim : rim + NP], below, 2), 0)
    corners = placed_rows(corners, late, 0)
    own = lane < 64
    out_ref[:ROWS] = jnp.where(own, strip[:ROWS], corners[:ROWS])
    out_ref[ROWS:ALL_ROWS] = corners[ROWS:]
    out_ref[ALL_ROWS:] = jnp.where(own, strip[ROWS:], rim)


def steps_kernel(
    block_cols, flags_ref, pair_ref, next_ref, low_ref, centre_ref,
    high_ref, hot_ref, table_ref, weight_ref, lanes_ref, out_ref, sums,
):
    east0, flip0, east1, flip1 = flags_in(flags_ref)
    odd = lax.axis_index("blk") & 1
    block_y = lax.rem(lax.axis_index("blk"), BY)

    lane = lax.broadcasted_iota(i32, (1, LANES), 1)
    pair = jnp.concatenate([pair_ref[...], jnp.zeros((EDGE_ROWS, LANES), f32)], 0)
    around = beside(pair, next_ref[...])
    outer_at = [lanes_ref[32 + 8 * k : 40 + 8 * k, : 2 * LANES] for k in range(4)]
    kind = outer_at[1]
    from_pair = jnp.where(outer_at[2] != 0, 1 - odd, odd) != 0
    east = flags_in(flags_ref, 2)[0]
    strip_at = jnp.where(kind == 3, 1 - east, east)
    far_at = strip_at ^ (1 - odd) if block_cols == 1 else strip_at
    strip_at, far_at = (jnp.where(kind > 1, at, 0) for at in (strip_at, far_at))
    place = jnp.where(
        from_pair,
        outer_at[0] + (RING + 1) * RING * strip_at,
        jnp.where(outer_at[3] < 0, -1, outer_at[3] + RING * RING * far_at),
    )
    outer = picked(around, as_one_hot(jnp.where(kind == 0, -1, place), 2 * LANES))
    table = table_ref[...].astype(bf16)
    tiles = (None, low_ref, centre_ref, high_ref, None)
    count = len(tiles)
    masks = [lanes_ref[24:32, k * LANES : (k + 1) * LANES] for k in range(count)]
    closed_above = jnp.where(block_y == BY - 1, masks[-2][1:2], 0) != 0
    closed_below = jnp.where(block_y == 0, masks[1][2:3], 0) != 0
    first_row = jnp.where(odd == 0, masks[0][4:5], 0) != 0
    last_row = jnp.where(odd != 0, masks[-1][5:6], 0) != 0
    outer_used = first_sums(
        table,
        weight_ref[...],
        [outer[k * NODES : (k + 1) * NODES] for k in range(ARRAYS)],
        [outer[ROWS + c * NP : ROWS + (c + 1) * NP] for c in range(4)],
        beside(masks[0][0:1], masks[-1][0:1]) != 0,
    )

    def shifted(parts, by, ring):
        turned = [pltpu.roll(part, -by % LANES, 1) for part in parts]
        size = len(parts)
        step = 1 if by > 0 else -1
        others = [(k + step) % size if ring else min(max(k + step, 0), size - 1) for k in range(size)]
        from_other = lane >= LANES - by if by > 0 else lane < -by
        return [jnp.where(from_other, turned[others[k]], turned[k]) for k in range(size)]

    def put_x_sums(groups, components):
        slots = [k for group in groups for k in group]
        ring = len(slots) < count
        per_tile = [
            [part[:, n * LANES : (n + 1) * LANES] for part in parts]
            for group, parts in zip(groups, components)
            for n in range(len(group))
        ]
        for c in range(3):
            parts = [tile[c] for tile in per_tile]
            west = [part[:NP] for part in parts]
            east = [part[NODES - NP :] for part in parts]
            at_east, at_west = shifted(west, 1, ring), shifted(east, -1, ring)
            for n, k in enumerate(slots):
                sums[k, c * NODES : c * NODES + NP] = west[n] + at_west[n]
                sums[k, c * NODES + NP : (c + 1) * NODES - NP] = parts[n][NP : NODES - NP]
                sums[k, (c + 1) * NODES - NP : (c + 1) * NODES] = east[n] + at_east[n]

    def edge_y(components, slots, rows=None):
        ring = len(slots) < count
        south_at = pl.ds(0, components * NP, stride=NP)
        north_at = pl.ds(NP - 1, components * NP, stride=NP)
        south = [sums[k, south_at] for k in slots]
        north = [sums[k, north_at] for k in slots]
        at_north, at_south = shifted(south, PITCH, ring), shifted(north, -PITCH, ring)
        for n, k in enumerate(slots):
            if k == count - 2:
                at_north[n] = jnp.where(closed_above, 0.0, at_north[n])
            if k == 1:
                at_south[n] = jnp.where(closed_below, 0.0, at_south[n])
        if rows is not None:
            at_south[0] = jnp.where(first_row, rows[0], at_south[0])
            at_north[-1] = jnp.where(last_row, rows[1], at_north[-1])
        for n, k in enumerate(slots):
            sums[k, south_at] = south[n] + at_south[n]
            sums[k, north_at] = north[n] + at_north[n]

    node = lax.broadcasted_iota(i32, (1, NP, 1), 1)
    rows = []
    for rim in (outer[ALL_ROWS:, :LANES], outer[ALL_ROWS:, LANES:]):
        east = pltpu.roll(rim, LANES - 1, 1).reshape(4, NP, LANES)
        west = pltpu.roll(rim, 1, 1).reshape(4, NP, LANES)
        rim = (
            rim.reshape(4, NP, LANES)
            + jnp.where(node == NP - 1, pltpu.roll(east, NP - 1, 1), 0.0)
            + jnp.where(node == 0, pltpu.roll(west, 1, 1), 0.0)
        )
        rows.append(rim.reshape(EDGE_ROWS, LANES))

    every = tuple(range(count))
    groups = (every[0:2], every[2:4], every[4:])

    def tile_part(k, n):
        if tiles[k] is None:
            return outer_used[n][:, :LANES] if k == 0 else outer_used[n][:, LANES:]
        return tiles[k][n * NODES : (n + 1) * NODES]

    def part_of(group, n):
        return jnp.concatenate([tile_part(k, n) for k in group], 1)

    def summed(group, c):
        return jnp.concatenate([sums[k, c * NODES : (c + 1) * NODES] for k in group], 1)

    def average(group, per_mass):
        return [summed(group, c) * per_mass for c in range(3)]

    def laplace(s):
        return [
            dot(table[4 * NODES :, : 3 * NODES], jnp.concatenate(high_low_high(part), 0))
            for part in s
        ]

    start = [[part_of(group, n) for n in range(3)] for group in groups]
    fixed = [[part_of(group, n) for n in range(3, 6)] for group in groups]
    for k in every:
        for c in range(4):
            sums[k, c * NODES : (c + 1) * NODES] = tile_part(k, 7 + c)
    edge_y(4, every, rows)
    per_mass = [1.0 / summed(group, 3) for group in groups]
    one = []
    for n, group in enumerate(groups):
        change = average(group, per_mass[n])
        one.append([s + time_step * c for s, c in zip(start[n], change)])
    put_x_sums(groups, [mass_tendency(table, *s, *f) for s, f in zip(one, fixed)])
    edge_y(3, every)
    two = []
    for n, group in enumerate(groups):
        change = average(group, per_mass[n])
        two.append(
            [0.75 * s + 0.25 * (o + time_step * c) for s, o, c in zip(start[n], one[n], change)]
        )
    put_x_sums(groups, [mass_tendency(table, *s, *f) for s, f in zip(two, fixed)])
    edge_y(3, every)

    def regrouped(per_group):
        (outer_low, high_above) = per_group[0], per_group[1]
        below, low = outer_low[:, :LANES], outer_low[:, LANES:]
        centre, high = high_above[:, :LANES], high_above[:, LANES:]
        near = jnp.where(lane < LANES // 2, per_group[2], below)
        return [beside(low, centre), beside(high, near)]

    def of_groups(values):
        return [list(parts) for parts in zip(*(regrouped(part) for part in zip(*values)))]

    for c in range(3):
        rows_at = slice(c * NODES, (c + 1) * NODES)
        sums[count - 1, rows_at] = jnp.where(
            lane < LANES // 2, sums[count - 1, rows_at], sums[0, rows_at]
        )
    slots = every[1:]
    groups = (slots[0:2], slots[2:4])
    start, two = of_groups(start), of_groups(two)
    tide = regrouped([part_of(every[0:2], 6), part_of(every[2:4], 6), part_of(every[4:], 6)])
    per_mass = regrouped(per_mass)
    three = []
    for n, group in enumerate(groups):
        change = average(group, per_mass[n])
        now = [
            s / 3.0 + 2.0 / 3.0 * (o + time_step * c)
            for s, o, c in zip(start[n], two[n], change)
        ]
        now[0] = now[0] + tide[n]
        three.append(now)
    put_x_sums(groups, [laplace(s) for s in three])
    edge_y(3, slots)
    change = [average(group, per_mass[n]) for n, group in enumerate(groups)]
    put_x_sums(groups, [laplace(s) for s in change])
    edge_y(3, slots)
    stepped = []
    for n, group in enumerate(groups):
        change = average(group, per_mass[n])
        now = [s - time_step * hyper_coeff * b for s, b in zip(three[n], change)]
        stepped.append(jnp.concatenate(now, 0))
    stepped = jnp.concatenate(stepped, 1)[:, :MID]
    own = lanes_ref[27:28, LANES : LANES + MID] != 0
    stored = picked(jnp.where(own, stepped, 0.0), hot_ref[...])
    out_ref[...] = stored.reshape(out_ref.shape)


def on_device(fields, jacobian, water_depth, coriolis, tide_height, slot_of, seam_rows):
    block_cols = lax.axis_size("blk") // BY
    table, weight, edge_table, lanes = map(jnp.asarray, (*operator_table(), lane_tables()))
    vmem = pl.BlockSpec(memory_space=pltpu.VMEM)
    hbm = pl.BlockSpec(memory_space=pltpu.HBM)
    params = pltpu.CompilerParams(vmem_limit_bytes=48 * 2**20)
    held = (fields, jacobian, water_depth, coriolis, tide_height)

    def call(kernel, ins, outs, cost, scratch=(), name=None):
        return pl.pallas_call(
            kernel,
            out_shape=[jax.ShapeDtypeStruct(*out) for out in outs],
            in_specs=[spec for spec, value in ins],
            out_specs=[vmem] * len(outs),
            scratch_shapes=list(scratch),
            compiler_params=params,
            cost_estimate=pl.CostEstimate(
                flops=cost, bytes_accessed=2 * 2**20, transcendentals=0
            ),
            name=name,
        )(
            *[
                pltpu.with_memory_space_constraint(value, pltpu.HBM) if spec is hbm else value
                for spec, value in ins
            ]
        )

    strip = ((HALF_ROWS, LANES), f32)
    def room(values, spaces=None):
        spaces = spaces or [pltpu.VMEM] * len(values)
        buffers = [space(x.shape, x.dtype) for space, x in zip(spaces, values)]
        return buffers + [pltpu.SemaphoreType.DMA((len(values),))]

    needed = (seam_rows, slot_of, *held, edge_table)
    corner = ((CORNER_ROWS, LANES), f32)
    scratch = [pltpu.VMEM((1, 4 * NODES, LANES), f32)]
    first, then, stored, flags = call(
        functools.partial(strips_kernel, block_cols),
        [(hbm, x) for x in needed],
        [strip, strip, ((ROWS, ELEMENTS), f32), ((8, LANES), i32)],
        10**8,
        scratch=room(needed, [pltpu.SMEM] + [pltpu.VMEM] * (len(needed) - 1)),
        name="strips",
    )
    to_next, far0, far1, to_pair = call(
        functools.partial(rows_kernel, block_cols),
        [(vmem, x) for x in (flags, stored, first, then, table, weight)],
        [strip, corner, corner, ((ROWS, LANES), f32)],
        10**8,
        scratch=scratch,
        name="rows",
    )
    span = block_cols * BY
    both = ("face", "blk")
    places = [(f, x, y) for f in range(2) for x in range(block_cols) for y in range(BY)]

    def rank(face, block_x, block_y):
        return face * span + block_x * BY + block_y

    def same(y):
        return y

    def in_pair(y):
        return y ^ 1

    def next_pair(y):
        other = y + 1 if y % 2 else y - 1
        return other if 0 <= other < BY else y

    def swapped(value, partner):
        pairs = [
            (rank(f, x, y), rank(f if partner(y) != y else 1 - f, x, partner(y)))
            for f, x, y in places
        ]
        return lax.ppermute(value, both, pairs)

    def across(value0, value1, partner):
        last = block_cols - 1

        def aligned(y):
            return partner is same or partner(y) != y

        straight = {
            (f, x, y): (f, x + 1, partner(y)) if x < last else (1 - f, 0, partner(y))
            for f, x, y in places
        }
        turned = {
            (f, last, y): (1 - f, 0, BY - 1 - partner(y) if aligned(y) else y)
            for f in range(2)
            for y in range(BY)
        }

        def eastward(value, pairs):
            return lax.ppermute(value, both, [(rank(*a), rank(*b)) for a, b in pairs.items()])

        def westward(value, pairs):
            return lax.ppermute(value, both, [(rank(*b), rank(*a)) for a, b in pairs.items()])

        if block_cols == 1:
            return eastward(value0, straight), eastward(value1, turned)
        flipped = (seam_rows[:, 1] - seam_rows[:, 0]) % seam_rows.shape[1] != 1
        face = lax.axis_index("face")
        block_x = lax.axis_index("blk") // BY
        return (
            jnp.where(
                (block_x == last) & flipped[face],
                westward(value1, turned),
                westward(value1, straight),
            ),
            jnp.where(
                (block_x == 0) & flipped[1 - face],
                eastward(value0, turned),
                eastward(value0, straight),
            ),
        )

    if block_cols == 1:
        halos = []
        for value, mirrored in ((first, mirrored_first), (then, lambda y: not mirrored_first(y))):
            pairs = [
                (rank(f, x, y), rank(1 - f, x, BY - 1 - y if mirrored(y) else y))
                for f, x, y in places
            ]
            halos.append(lax.ppermute(value, both, pairs))
        halo0, halo1 = halos
    else:
        halo0, halo1 = across(first, then, same)
    far0, far1 = across(far0, far1, next_pair)
    from_next = swapped(to_next, next_pair)
    own, hot = call(
        own_kernel,
        [(vmem, x) for x in (flags, stored, lanes)],
        [((ROWS, MID), f32), ((MID, ELEMENTS), bf16)],
        10**8,
        name="own",
    )
    (to_pair,) = call(
        functools.partial(corners_kernel, block_cols),
        [(vmem, x) for x in (flags, halo0, halo1, to_pair, hot)],
        [((ALL_ROWS, LANES), f32)],
        10**8,
        name="corners",
    )
    from_pair = swapped(to_pair, in_pair)
    tile = ((11 * NODES, LANES), f32)
    low, centre, high = call(
        functools.partial(middle_kernel, block_cols),
        [(vmem, x) for x in (flags, halo0, halo1, own, lanes, table, weight)],
        [tile, tile, tile],
        10**8,
        name="middle",
    )
    (from_next,) = call(
        functools.partial(far_kernel, block_cols),
        [(vmem, x) for x in (flags, far1, far0, from_next, low)],
        [((RIM_ROWS, LANES), f32)],
        10**11,
        name="far",
    )
    (stepped,) = call(
        functools.partial(steps_kernel, block_cols),
        [
            (vmem, x)
            for x in (
                flags, from_pair, from_next, low, centre, high, hot, table, weight, lanes
            )
        ],
        [(fields.shape, f32)],
        10**8,
        scratch=[pltpu.VMEM((EXT // LANES, 4 * NODES, LANES), f32)],
        name="steps",
    )
    return stepped


def solution(mesh):
    return jax.shard_map(
        on_device,
        mesh=mesh,
        in_specs=(
            P(None, None, None, ("face", "blk")),
            P(None, None, ("face", "blk")),
            P(None, None, ("face", "blk")),
            P(None, None, ("face", "blk")),
            P(None, None, ("face", "blk")),
            P(("face", "blk"), None),
            P(),
        ),
        out_specs=P(None, None, None, ("face", "blk")),
        check_vma=False,
    )
```

```python
import functools
import math

import jax
import jax.numpy as jnp
import ml_dtypes
import numpy as np
from jax import lax
from jax.experimental import pallas as pl
from jax.experimental.pallas import tpu as pltpu
from jax.sharding import PartitionSpec as P

BY = 16
GX = 16
GY = 16
NP = 8
NODES = NP * NP
ARRAYS = 7
ROWS = ARRAYS * NODES
MOVED = 6 * NODES
EDGE_ROWS = 4 * NP
ALL_ROWS = ROWS + EDGE_ROWS
HALF_ROWS = (MOVED + NODES // 2 + 2 * NP) // 2
RING = 4
RIM_ROWS = ROWS + 2 * EDGE_ROWS
CORNER_ROWS = (MOVED + NODES // 2 + 4 * NP) // 8
PITCH = GX + 2 * RING
MID = GY * PITCH
LANES = 128
EXT = MID + 2 * LANES
LEAD = LANES - RING * PITCH
ELEMENTS = GX * GY

time_step = 0.03
hyper_coeff = 0.0002

f32 = jnp.float32
bf16 = jnp.bfloat16
i32 = jnp.int32


def legendre_pair(location, degree):
    lower_value = 1.0
    upper_value = location
    for polynomial_order in range(2, degree + 1):
        lower_value, upper_value = (
            upper_value,
            (
                (2 * polynomial_order - 1) * location * upper_value
                - (polynomial_order - 1) * lower_value
            )
            / polynomial_order,
        )
    return (lower_value, upper_value)


def gll_tables(points):
    degree = points - 1
    locations = [-math.cos(math.pi * position / degree) for position in range(points)]
    for iteration in range(100):
        updated = []
        for location in locations:
            lower_value, upper_value = legendre_pair(location, degree)
            updated.append(
                location - (location * upper_value - lower_value) / ((degree + 1) * upper_value)
            )
        locations = updated
    locations[0] = -1.0
    locations[degree] = 1.0
    legendre_at = [legendre_pair(location, degree)[1] for location in locations]
    weights = [2.0 / (degree * (degree + 1) * value * value) for value in legendre_at]
    corner_value = degree * (degree + 1) / 4.0
    derivative = []
    for row_index in range(points):
        row_values = []
        for column_index in range(points):
            if row_index != column_index:
                row_values.append(
                    legendre_at[row_index]
                    / (legendre_at[column_index] * (locations[row_index] - locations[column_index]))
                )
            elif row_index == 0:
                row_values.append(-corner_value)
            elif row_index == degree:
                row_values.append(corner_value)
            else:
                row_values.append(0.0)
        derivative.append(row_values)
    return np.asarray(weights, np.float64), np.asarray(derivative, np.float64)


def in_three(matrix):
    high = matrix.astype(ml_dtypes.bfloat16)
    low = (matrix - high.astype(np.float64)).astype(ml_dtypes.bfloat16)
    return np.concatenate([high, high, low], 1)


def operator_table():
    weights, derivative = gll_tables(NP)
    eye = np.eye(NP)
    node_weight = np.outer(weights, weights).reshape(NODES, 1)
    along_x = node_weight * np.kron(derivative, eye)
    along_y = node_weight * np.kron(eye, derivative)
    second = derivative @ derivative
    both = node_weight * (np.kron(second, eye) + np.kron(eye, second))
    table = np.zeros((5 * NODES, 4 * NODES), ml_dtypes.bfloat16)
    table[:NODES, : 3 * NODES] = in_three(along_x)
    table[NODES : 2 * NODES, : 3 * NODES] = in_three(along_y)
    flux = [in_three(along_x), in_three(along_y)]
    for k, part in enumerate(flux):
        at = 2 * k * NODES
        table[2 * NODES : 3 * NODES, at : at + 2 * NODES] = part[:, : 2 * NODES]
        table[3 * NODES : 4 * NODES, at : at + NODES] = part[:, 2 * NODES :]
    table[4 * NODES :, : 3 * NODES] = in_three(both)
    table = table.astype(np.float32)
    spread = np.broadcast_to(node_weight, (NODES, LANES)).astype(np.float32)
    ends = np.r_[:NP, NODES - NP : NODES]
    edge_table = np.zeros((10 * NP, 4 * NODES), np.float32)
    for k in range(4):
        edge_table[2 * k * NP : 2 * (k + 1) * NP] = table[k * NODES + ends]
    edge_table[8 * NP :, :LANES] = spread[ends]
    return table, np.ascontiguousarray(spread), edge_table


def lane_tables():
    table = np.zeros((24, MID), np.int32)
    for lane in range(MID):
        row, col = divmod(lane, PITCH)
        x = col - RING
        own = 0 <= x < GX
        table[0:8, lane] = x * GY + row if own else -1
        if not own:
            table[8:16, lane] = row * RING + (col if x < 0 else x - GX)
        table[16:24, lane] = 0 if own else (1 if x < 0 else 2)
    ext = np.zeros((8, EXT), np.int32)
    outer = np.zeros((32, 2 * LANES), np.int32)
    for lane in range(EXT):
        row, col = divmod(lane - LEAD, PITCH)
        y = row - RING
        x = col - RING
        ext[0, lane] = x in (-RING, GX + RING - 1)
        ext[1, lane] = y == GY - 1
        ext[2, lane] = y == 0
        ext[3, lane] = 0 <= y < GY and 0 <= x < GX
        ext[4, lane] = y == -RING
        ext[5, lane] = y == GY + RING - 1
        if -RING - 1 <= y < 0 or GY <= y <= GY + RING:
            place = lane if y < 0 else lane - MID
            step = y + RING if y < 0 else y - GY
            near = step + 1 if y < 0 else step
            far = 0 <= step < RING
            if 0 <= x < GX:
                outer[0:8, place] = near * GX + x
                outer[8:16, place] = 1
                outer[24:32, place] = LANES + step * GX + x if far else -1
            else:
                across = x + RING if x < 0 else x - GX
                outer[0:8, place] = (RING + 1) * GX + near * RING + across
                outer[8:16, place] = 2 if x < 0 else 3
                outer[24:32, place] = LANES + RING * GX + step * RING + across if far else -1
            outer[16:24, place] = y > 0
    whole = np.zeros((64, EXT), np.int32)
    whole[0:24, :MID] = table
    whole[24:32] = ext
    whole[32:64, : 2 * LANES] = outer
    return whole


def dot(a, b):
    return jnp.dot(a, b, preferred_element_type=f32)


def picked(values, one_hot):
    high = values.astype(bf16)
    low = (values - high.astype(f32)).astype(bf16)
    both = dot(jnp.concatenate([high, low], 0), one_hot)
    return both[: values.shape[0]] + both[values.shape[0] :]


def as_one_hot(row_of_lane, depth):
    index = lax.broadcasted_iota(i32, (depth, row_of_lane.shape[1]), 0)
    return jnp.where(index == row_of_lane[0:1], 1.0, 0.0).astype(bf16)


def high_low_high(values):
    high = values.astype(bf16)
    low = (values - high.astype(f32)).astype(bf16)
    return [high, low, high]


def by_slot(halves, cell_of_lane):
    size = cell_of_lane.shape[1]
    halves = [jnp.broadcast_to(half, (8, LANES)) for half in halves]
    chosen = []
    for k in range(size // LANES):
        cell = cell_of_lane[:, k * LANES : (k + 1) * LANES]
        low, high = (jnp.take_along_axis(half, cell & (LANES - 1), axis=1) for half in halves)
        chosen.append(jnp.where(cell < 0, -1, jnp.where(cell < LANES, low, high)))
    return as_one_hot(jnp.concatenate(chosen, 1), ELEMENTS)


def stored_rows(fields_ref, others):
    fields = fields_ref[...].reshape(3 * NODES, ELEMENTS)
    others = [ref[...].reshape(NODES, ELEMENTS) for ref in others]
    return jnp.concatenate([fields[:NODES] - others[-1], fields[NODES:]] + others, 0)


def mass_tendency(table, p, u, v, area_depth, weighted_area, spin):
    slopes = dot(table[: 2 * NODES, : 3 * NODES], jnp.concatenate(high_low_high(p), 0))
    flux = high_low_high(area_depth * u)[:2] + high_low_high(area_depth * v)[:2]
    spread = dot(table[2 * NODES : 4 * NODES], jnp.concatenate(flux, 0))
    return [
        -(spread[:NODES] + spread[NODES:]),
        spin * v - weighted_area * slopes[:NODES],
        -spin * u - weighted_area * slopes[NODES:],
    ]


def edge_values(table_ref, weight_ref, p, u, v, area, depth, spin):
    root = jnp.sqrt(area)
    mass = jnp.concatenate([weight_ref[...]] * (area.shape[1] // LANES), 1) * area
    table = table_ref[...].astype(bf16)
    return mass_tendency(table, p, u, v, root * depth, root, mass * spin) + [mass]


def column_edges(table, weight, p, u, v, area, depth, spin):
    def ends(part):
        return jnp.concatenate([part[:NP], part[NODES - NP :]], 0)

    root = jnp.sqrt(area)
    area_depth = root * depth
    root, mass = ends(root), weight * ends(area)
    weighted_spin = mass * ends(spin)
    slopes = dot(table[: 4 * NP, : 3 * NODES], jnp.concatenate(high_low_high(p), 0))
    flux = high_low_high(area_depth * u)[:2] + high_low_high(area_depth * v)[:2]
    spread = dot(table[4 * NP :], jnp.concatenate(flux, 0))
    return [
        -(spread[: 2 * NP] + spread[2 * NP :]),
        weighted_spin * ends(v) - root * slopes[: 2 * NP],
        -weighted_spin * ends(u) - root * slopes[2 * NP :],
        mass,
    ]


def row_edges(sums):
    return tuple(sums[0, pl.ds(j, EDGE_ROWS, stride=NP)] for j in (NP - 1, 0))


def beside(left, right):
    return jnp.concatenate([left, right], 1)


def one_of_four(parts, index):
    out = parts[0]
    for k in range(1, 4):
        out = jnp.where(index == k, parts[k], out)
    return out


def folded(tide, kept, late, step):
    half = NODES // 2
    back = pltpu.roll(tide[half:], LANES - step, 1)
    onward = pltpu.roll(tide[half:], step, 1)
    return jnp.where(kept, tide[:half], jnp.where(late, back, onward))


def unfolded(rows, late, step):
    back = pltpu.roll(rows, LANES - step, 1)
    onward = pltpu.roll(rows, step, 1)
    return jnp.concatenate([rows, jnp.where(late, onward, back)], 0)


def strip_rows(parts, late, shift, rims):
    lane = lax.broadcasted_iota(i32, (1, LANES), 1)
    index = (lane >> shift) & 3
    kept = jnp.where(late, index // 2, 1 - index // 2) != 0
    tide = folded(parts[6], kept, late, 2 << shift)
    rim = one_of_four(rims, index)
    return jnp.concatenate(parts[:6] + [tide, rim, jnp.zeros_like(rim)], 0)


def placed_rows(whole, late, shift):
    half = NODES // 2
    tide = unfolded(whole[MOVED : MOVED + half], late, 2 << shift)
    rim = whole[MOVED + half : MOVED + half + NP]
    return jnp.concatenate([whole[:MOVED], tide] + spread_out(rim, late, shift), 0)


def spread_out(rim, late, shift):
    parts = []
    for k in range(4):
        first = pltpu.roll(rim, (LANES - (k << shift)) % LANES, 1) if k else rim
        last = pltpu.roll(rim, (3 - k) << shift, 1) if k < 3 else rim
        parts.append(jnp.where(late, first, last))
    return parts


def with_row_rim(whole, sums, top):
    north, south = row_edges(sums)
    rim = jnp.where(top, pltpu.roll(north, RING, 1), pltpu.roll(south, LANES - RING, 1))
    parts = [rim[k * NP : (k + 1) * NP] for k in range(4)]
    lane = lax.broadcasted_iota(i32, (1, LANES), 1)
    spots = []
    for k, part in enumerate(parts):
        first = pltpu.roll(part, k * RING, 1) if k else part
        last = pltpu.roll(part, (LANES - (3 - k) * RING) % LANES, 1) if k < 3 else part
        spots.append(jnp.where(top, first, last))
    rim = one_of_four(spots, (lane >> 2) & 3)
    return jnp.concatenate([whole[: MOVED + NODES // 2 + NP], rim], 0)


def in_eight(whole):
    whole = jnp.concatenate([whole, jnp.zeros((8 * CORNER_ROWS - whole.shape[0], LANES), f32)], 0)
    return [whole[k * CORNER_ROWS : (k + 1) * CORNER_ROWS] for k in range(8)]


def corner_of(whole, start, top):
    lane = lax.broadcasted_iota(i32, (1, LANES), 1)
    out = None
    for k, part in enumerate(in_eight(whole)):
        last = pltpu.roll(part, (LANES - start - 48 + 16 * k) % LANES, 1)
        first = pltpu.roll(part, (LANES - start + 16 * k) % LANES, 1)
        part = jnp.where(top != 0, last, first)
        out = part if k == 0 else jnp.where(lane >= 16 * k, part, out)
    return out


def both_corners(whole, odd):
    group = lax.broadcasted_iota(i32, (1, LANES), 1) >> 4
    other_group = (group + jnp.where(odd != 0, 7, 1)) & 7
    first, other = None, None
    for k, part in enumerate(in_eight(whole)):
        part = pltpu.roll(part, (LANES + 16 * k - 48 * odd) & (LANES - 1), 1)
        first = part if k == 0 else jnp.where(group == k, part, first)
        other = part if k == 0 else jnp.where(other_group == k, part, other)
    return first, other


def arrived_corners(far0, far1, block_cols, odd):
    lane = lax.broadcasted_iota(i32, (1, LANES), 1)
    corners = []
    for k in range(8):
        if block_cols == 1:
            part = jnp.where((lane >> 4) == k, far0, far1)
            part = pltpu.roll(part, (LANES + 64 + 16 * (1 - odd) - 16 * k) & (LANES - 1), 1)
        else:
            first = pltpu.roll(far0, (64 - 16 * k) % LANES, 1)
            other = pltpu.roll(far1, (80 - 16 * k) % LANES, 1)
            part = jnp.where((lane & 16) == 0, first, other)
        corners.append(part)
    return jnp.concatenate(corners, 0), ((lane >> 4) & 1) ^ (1 - odd if block_cols == 1 else 0)


def packed(whole):
    second = lax.broadcasted_iota(i32, (1, LANES), 1) >= 64
    top, bottom = whole[:HALF_ROWS], whole[HALF_ROWS:]
    return (
        jnp.where(second, pltpu.roll(bottom, 64, 1), top),
        jnp.where(second, bottom, pltpu.roll(top, 64, 1)),
    )


def unpacked(in0, in1):
    second = lax.broadcasted_iota(i32, (1, LANES), 1) >= 64
    top = jnp.where(second, pltpu.roll(in1, 64, 1), in0)
    bottom = jnp.where(second, in1, pltpu.roll(in0, 64, 1))
    return jnp.concatenate([top, bottom], 0)


def seam_flags(seam_ref, block_cols):
    size_y = seam_ref.shape[1]
    face = lax.axis_index("face")
    blk = lax.axis_index("blk")
    block_x = blk // BY

    def flipped(k):
        return jnp.where(lax.rem(seam_ref[k, 1] - seam_ref[k, 0] + size_y, size_y) != 1, 1, 0)

    first, second = flipped(0), flipped(1)
    east_flip = jnp.where(face == 0, first, second)
    west_flip = jnp.where(face == 0, second, first)
    if block_cols == 1:
        return 1 - east_flip, 0, east_flip, 1
    at_east = jnp.where(block_x == block_cols - 1, east_flip, 0)
    at_west = jnp.where(block_x == 0, west_flip, 0)
    return 1, at_east, 0, at_west


def slots_in(flags_ref):
    return flags_ref[4:5], flags_ref[5:6]


def flags_in(flags_ref, tiles=1):
    return [jnp.concatenate([flags_ref[k : k + 1]] * tiles, 1) for k in range(4)]


def mirrored_first(block_y):
    return (block_y >= BY // 4) & (block_y < BY - BY // 4)


def in_order(block_cols, first, second):
    if block_cols > 1:
        return first, second
    swap = mirrored_first(lax.rem(lax.axis_index("blk"), BY))
    return jnp.where(swap, second, first), jnp.where(swap, first, second)


def strips_kernel(block_cols, *refs):
    sources, (first_ref, then_ref, stored_ref, flags_ref) = refs[:8], refs[8:12]
    buffers, sems = refs[12:20], refs[20]
    copies = [
        pltpu.make_async_copy(source, buffer, sems.at[k])
        for k, (source, buffer) in enumerate(zip(sources, buffers))
    ]
    for copy in copies:
        copy.start()
    seam_ref, slot_ref, fields_ref, area_ref, depth_ref, spin_ref, tide_ref = buffers[:7]
    table_ref = buffers[7]
    for copy in copies[:2]:
        copy.wait()
    east0, flip0, east1, flip1 = flags = seam_flags(seam_ref, block_cols)
    index = lax.broadcasted_iota(i32, (8, LANES), 0)
    flags_ref[...] = sum(jnp.where(index == k, flag, 0) for k, flag in enumerate(flags))
    slots = slot_ref[:, :LANES], slot_ref[:, LANES:]
    flags_ref[4:5], flags_ref[5:6] = slots
    lane = lax.broadcasted_iota(i32, (8, 2 * LANES), 1)
    second = (lane & 64) != 0
    place = lane & 63
    row = place >> 2
    row = jnp.where(jnp.where(second, flip1, flip0) != 0, GY - 1 - row, row)
    east = jnp.where(second, east1, east0) != 0
    col = jnp.where(east, GX - RING, 0) + (place & 3)
    col = jnp.where(lane >= LANES, jnp.where(east, GX - RING - 1, RING), col)
    one_hot = by_slot(slots, col * GY + row)
    for copy in copies[2:7]:
        copy.wait()
    stored = stored_rows(fields_ref, (area_ref, depth_ref, spin_ref, tide_ref))
    both = picked(stored, one_hot)

    lane = lax.broadcasted_iota(i32, (1, LANES), 1)
    second = lane >= 64
    flip = jnp.where(second, flip1, flip0) != 0
    sign = jnp.where(flip, -1.0, 1.0)
    node = lax.broadcasted_iota(i32, (1, NP, 1), 1)

    def turned(values):
        shaped = values.reshape(-1, NP, LANES)
        shaped = pltpu.roll(shaped, 4, 1)
        shaped = jnp.where((node & 2) == 0, pltpu.roll(shaped, 6, 1), pltpu.roll(shaped, 2, 1))
        shaped = jnp.where((node & 1) == 0, pltpu.roll(shaped, 7, 1), pltpu.roll(shaped, 1, 1))
        return shaped.reshape(values.shape)

    strip, ring = (
        [part[k * NODES : (k + 1) * NODES] for k in range(ARRAYS)]
        for part in (both[:, :LANES], both[:, LANES:])
    )
    for copy in copies[7:]:
        copy.wait()
    table, weight = table_ref[: 8 * NP].astype(bf16), table_ref[8 * NP :, :LANES]
    edges = column_edges(table, weight, *ring[:6])
    east = jnp.where(second, east1, east0) != 0
    ends = [jnp.where(east, part[NP:], part[:NP]) for part in edges]
    ends[2] = ends[2] * sign
    strip[2] = strip[2] * sign
    strip[5] = strip[5] * sign
    strips = []
    for part, flip in zip(packed(strip_rows(strip, east, 0, ends)), (flip0, flip1)):
        if isinstance(flip, int):
            strips.append(turned(part) if flip else part)
        else:
            strips.append(jnp.where(flip != 0, turned(part), part))
    first_ref[...], then_ref[...] = in_order(block_cols, *strips)
    stored_ref[...] = stored


def rows_kernel(
    block_cols, flags_ref, stored_ref, first_ref, then_ref, table_ref, weight_ref,
    next_ref, far0_ref, far1_ref, pair_ref, sums,
):
    east0, flip0, east1, flip1 = flags_in(flags_ref)
    odd = lax.axis_index("blk") & 1
    lane = lax.broadcasted_iota(i32, (8, 2 * LANES), 1)
    row = jnp.where(odd != 0, GY - RING, 0) + ((lane & 63) >> 4)
    row = jnp.where((lane & 64) != 0, jnp.where(odd != 0, GY - RING - 1, RING), row)
    five = jnp.where(odd != 0, 0, GY - RING - 1) + jnp.minimum((lane & (LANES - 1)) >> 4, RING)
    row = jnp.where(lane >= LANES, five, row)
    both = picked(stored_ref[...], by_slot(slots_in(flags_ref), (lane & 15) * GY + row))
    pair_ref[...] = both[:, LANES:]
    rows = [both[k * NODES : (k + 1) * NODES, :LANES] for k in range(ARRAYS)]
    whole = unpacked(*in_order(block_cols, first_ref[...], then_ref[...]))
    strip = [whole[k * NODES : (k + 1) * NODES] for k in range(6)]
    edges = edge_values(table_ref, weight_ref, *map(beside, strip, rows[:6]))
    sums[0] = jnp.concatenate([part[:, :LANES] for part in edges], 0)
    lane = lax.broadcasted_iota(i32, (1, LANES), 1)
    top0, top1 = odd ^ flip0, odd ^ flip1
    whole = with_row_rim(whole, sums, jnp.where(lane >= 64, top1, top0) != 0)
    if block_cols == 1:
        far0_ref[...], far1_ref[...] = both_corners(whole, odd)
    else:
        far0_ref[...] = corner_of(whole, 0, top0)
        far1_ref[...] = corner_of(whole, 64, top1)
    sums[0] = jnp.concatenate([part[:, LANES:] for part in edges], 0)
    up = jnp.broadcast_to(odd != 0, (1, LANES))
    rim = pltpu.roll(jnp.where(up, *row_edges(sums)), 64, 1)
    rim = [rim[k * NP : (k + 1) * NP] for k in range(4)]
    whole = strip_rows(rows, up, 4, rim)
    top, bottom = whole[:HALF_ROWS], whole[HALF_ROWS:]
    next_ref[...] = jnp.where(lane >= 64, pltpu.roll(bottom, 64, 1), top)


def corners_kernel(block_cols, flags_ref, first_ref, then_ref, pair_ref, _, out_ref):
    east0, flip0, east1, flip1 = flags_in(flags_ref)
    in0, in1 = in_order(block_cols, first_ref[...], then_ref[...])
    top = 1 - (lax.axis_index("blk") & 1)
    lane = lax.broadcasted_iota(i32, (1, LANES), 1)
    halves = []
    for start in (0, 64):
        at0 = jnp.where(top != 0, 36, 80)
        at1 = jnp.where(top != 0, 56, 100)
        first = pltpu.roll(in0, (at0 - start) & (LANES - 1), 1)
        other = pltpu.roll(in1, (at1 - start) & (LANES - 1), 1)
        halves.append(jnp.where(lane < 100, first, other))
    late = jnp.where(lane < 100, east0, east1) == 0
    whole = placed_rows(jnp.concatenate(halves, 0), late, 0)
    out_ref[:ROWS] = jnp.where(lane < 80, pair_ref[...], whole[:ROWS])
    out_ref[ROWS:] = whole[ROWS:]


def own_kernel(flags_ref, stored_ref, lanes_ref, own_ref, hot_ref):
    one_hot = by_slot(slots_in(flags_ref), lanes_ref[0:8, :MID])
    own_ref[...] = picked(stored_ref[...], one_hot)
    hot_ref[...] = one_hot.astype(f32).T.astype(bf16)


def first_sums(table, weight, parts, rims, at_rim):
    p, u, v, area, depth, spin, tide = parts
    size = area.shape[1]
    root = jnp.sqrt(area)
    mass = jnp.concatenate([weight] * (size // LANES), 1) * area
    used = [p, u, v, root * depth, root, mass * spin, tide]
    for part, rim in zip(mass_tendency(table, p, u, v, *used[3:6]) + [mass], rims):
        west, east = part[:NP], part[NODES - NP :]
        at_east = jnp.where(at_rim, rim, pltpu.roll(west, size - 1, 1))
        at_west = jnp.where(at_rim, rim, pltpu.roll(east, 1, 1))
        used.append(
            jnp.concatenate([west + at_west, part[NP : NODES - NP], east + at_east], 0)
        )
    return used


def middle_kernel(
    block_cols, flags_ref, first_ref, then_ref, own_ref, lanes_ref, table_ref, weight_ref,
    low_ref, centre_ref, high_ref,
):
    east0, flip0, east1, flip1 = flags_in(flags_ref)
    second = lax.broadcasted_iota(i32, (1, LANES), 1) >= 64
    late = jnp.where(second, east1, east0) == 0
    whole = unpacked(*in_order(block_cols, first_ref[...], then_ref[...]))
    whole = placed_rows(whole, late, 0)
    side = lanes_ref[16:24, :MID]
    east = flags_in(flags_ref, MID // LANES)[0]
    first_at = jnp.where(side == 2, 64 * (1 - east), 64 * east)
    place = jnp.where(side == 0, -1, lanes_ref[8:16, :MID] + first_at)
    placed = picked(whole, as_one_hot(place, LANES))
    parts = [
        placed[k * NODES : (k + 1) * NODES] + own_ref[k * NODES : (k + 1) * NODES]
        for k in range(ARRAYS)
    ]
    rims = [placed[ROWS + c * NP : ROWS + (c + 1) * NP] for c in range(4)]
    at_rim = lanes_ref[24:25, LANES : LANES + MID] != 0
    used = first_sums(table_ref[...].astype(bf16), weight_ref[...], parts, rims, at_rim)
    for k, ref in enumerate((low_ref, centre_ref, high_ref)):
        for n, part in enumerate(used):
            ref[n * NODES : (n + 1) * NODES] = part[:, k * LANES : (k + 1) * LANES]


def far_kernel(block_cols, flags_ref, far1_ref, far0_ref, _, out_ref):
    east0, flip0, east1, flip1 = flags_in(flags_ref)
    odd = lax.axis_index("blk") & 1
    below = jnp.broadcast_to(odd == 0, (1, LANES))
    corners, strip_of = arrived_corners(far0_ref[...], far1_ref[...], block_cols, odd)
    late = jnp.where(strip_of != 0, east1, east0) == 0
    rim = MOVED + NODES // 2 + NP
    out_ref[:ALL_ROWS] = placed_rows(corners, late, 0)
    out_ref[ALL_ROWS:] = jnp.concatenate(spread_out(corners[rim : rim + NP], below, 2), 0)


def next_kernel(next_ref, corners_ref, out_ref):
    below = jnp.broadcast_to((lax.axis_index("blk") & 1) == 0, (1, LANES))
    own = lax.broadcasted_iota(i32, (1, LANES), 1) < 64
    strip = jnp.concatenate([next_ref[...], pltpu.roll(next_ref[...], 64, 1)], 0)
    strip = placed_rows(strip, below, 4)
    out_ref[:ROWS] = jnp.where(own, strip[:ROWS], corners_ref[:ROWS])
    out_ref[ROWS:ALL_ROWS] = corners_ref[ROWS:ALL_ROWS]
    out_ref[ALL_ROWS:] = jnp.where(own, strip[ROWS:], corners_ref[ALL_ROWS:])


def steps_kernel(
    block_cols, flags_ref, pair_ref, next_ref, low_ref, centre_ref,
    high_ref, hot_ref, table_ref, weight_ref, lanes_ref, out_ref, sums,
):
    east0, flip0, east1, flip1 = flags_in(flags_ref)
    odd = lax.axis_index("blk") & 1
    block_y = lax.rem(lax.axis_index("blk"), BY)

    lane = lax.broadcasted_iota(i32, (1, LANES), 1)
    pair = jnp.concatenate([pair_ref[...], jnp.zeros((EDGE_ROWS, LANES), f32)], 0)
    around = beside(pair, next_ref[...])
    outer_at = [lanes_ref[32 + 8 * k : 40 + 8 * k, : 2 * LANES] for k in range(4)]
    kind = outer_at[1]
    from_pair = jnp.where(outer_at[2] != 0, 1 - odd, odd) != 0
    east = flags_in(flags_ref, 2)[0]
    strip_at = jnp.where(kind == 3, 1 - east, east)
    far_at = strip_at ^ (1 - odd) if block_cols == 1 else strip_at
    strip_at, far_at = (jnp.where(kind > 1, at, 0) for at in (strip_at, far_at))
    place = jnp.where(
        from_pair,
        outer_at[0] + (RING + 1) * RING * strip_at,
        jnp.where(outer_at[3] < 0, -1, outer_at[3] + RING * RING * far_at),
    )
    outer = picked(around, as_one_hot(jnp.where(kind == 0, -1, place), 2 * LANES))
    table = table_ref[...].astype(bf16)
    tiles = (None, low_ref, centre_ref, high_ref, None)
    count = len(tiles)
    masks = [lanes_ref[24:32, k * LANES : (k + 1) * LANES] for k in range(count)]
    closed_above = jnp.where(block_y == BY - 1, masks[-2][1:2], 0) != 0
    closed_below = jnp.where(block_y == 0, masks[1][2:3], 0) != 0
    first_row = jnp.where(odd == 0, masks[0][4:5], 0) != 0
    last_row = jnp.where(odd != 0, masks[-1][5:6], 0) != 0
    outer_used = first_sums(
        table,
        weight_ref[...],
        [outer[k * NODES : (k + 1) * NODES] for k in range(ARRAYS)],
        [outer[ROWS + c * NP : ROWS + (c + 1) * NP] for c in range(4)],
        beside(masks[0][0:1], masks[-1][0:1]) != 0,
    )

    def shifted(parts, by, ring):
        turned = [pltpu.roll(part, -by % LANES, 1) for part in parts]
        size = len(parts)
        step = 1 if by > 0 else -1
        others = [(k + step) % size if ring else min(max(k + step, 0), size - 1) for k in range(size)]
        from_other = lane >= LANES - by if by > 0 else lane < -by
        return [jnp.where(from_other, turned[others[k]], turned[k]) for k in range(size)]

    def put_x_sums(groups, components):
        slots = [k for group in groups for k in group]
        ring = len(slots) < count
        per_tile = [
            [part[:, n * LANES : (n + 1) * LANES] for part in parts]
            for group, parts in zip(groups, components)
            for n in range(len(group))
        ]
        for c in range(3):
            parts = [tile[c] for tile in per_tile]
            west = [part[:NP] for part in parts]
            east = [part[NODES - NP :] for part in parts]
            at_east, at_west = shifted(west, 1, ring), shifted(east, -1, ring)
            for n, k in enumerate(slots):
                sums[k, c * NODES : c * NODES + NP] = west[n] + at_west[n]
                sums[k, c * NODES + NP : (c + 1) * NODES - NP] = parts[n][NP : NODES - NP]
                sums[k, (c + 1) * NODES - NP : (c + 1) * NODES] = east[n] + at_east[n]

    def edge_y(components, slots, rows=None):
        ring = len(slots) < count
        south_at = pl.ds(0, components * NP, stride=NP)
        north_at = pl.ds(NP - 1, components * NP, stride=NP)
        south = [sums[k, south_at] for k in slots]
        north = [sums[k, north_at] for k in slots]
        at_north, at_south = shifted(south, PITCH, ring), shifted(north, -PITCH, ring)
        for n, k in enumerate(slots):
            if k == count - 2:
                at_north[n] = jnp.where(closed_above, 0.0, at_north[n])
            if k == 1:
                at_south[n] = jnp.where(closed_below, 0.0, at_south[n])
        if rows is not None:
            at_south[0] = jnp.where(first_row, rows[0], at_south[0])
            at_north[-1] = jnp.where(last_row, rows[1], at_north[-1])
        for n, k in enumerate(slots):
            sums[k, south_at] = south[n] + at_south[n]
            sums[k, north_at] = north[n] + at_north[n]

    node = lax.broadcasted_iota(i32, (1, NP, 1), 1)
    rows = []
    for rim in (outer[ALL_ROWS:, :LANES], outer[ALL_ROWS:, LANES:]):
        east = pltpu.roll(rim, LANES - 1, 1).reshape(4, NP, LANES)
        west = pltpu.roll(rim, 1, 1).reshape(4, NP, LANES)
        rim = (
            rim.reshape(4, NP, LANES)
            + jnp.where(node == NP - 1, pltpu.roll(east, NP - 1, 1), 0.0)
            + jnp.where(node == 0, pltpu.roll(west, 1, 1), 0.0)
        )
        rows.append(rim.reshape(EDGE_ROWS, LANES))

    every = tuple(range(count))
    groups = (every[0:2], every[2:4], every[4:])

    def tile_part(k, n):
        if tiles[k] is None:
            return outer_used[n][:, :LANES] if k == 0 else outer_used[n][:, LANES:]
        return tiles[k][n * NODES : (n + 1) * NODES]

    def part_of(group, n):
        return jnp.concatenate([tile_part(k, n) for k in group], 1)

    def summed(group, c):
        return jnp.concatenate([sums[k, c * NODES : (c + 1) * NODES] for k in group], 1)

    def average(group, per_mass):
        return [summed(group, c) * per_mass for c in range(3)]

    def laplace(s):
        return [
            dot(table[4 * NODES :, : 3 * NODES], jnp.concatenate(high_low_high(part), 0))
            for part in s
        ]

    start = [[part_of(group, n) for n in range(3)] for group in groups]
    fixed = [[part_of(group, n) for n in range(3, 6)] for group in groups]
    for k in every:
        for c in range(4):
            sums[k, c * NODES : (c + 1) * NODES] = tile_part(k, 7 + c)
    edge_y(4, every, rows)
    per_mass = [1.0 / summed(group, 3) for group in groups]
    one = []
    for n, group in enumerate(groups):
        change = average(group, per_mass[n])
        one.append([s + time_step * c for s, c in zip(start[n], change)])
    put_x_sums(groups, [mass_tendency(table, *s, *f) for s, f in zip(one, fixed)])
    edge_y(3, every)
    two = []
    for n, group in enumerate(groups):
        change = average(group, per_mass[n])
        two.append(
            [0.75 * s + 0.25 * (o + time_step * c) for s, o, c in zip(start[n], one[n], change)]
        )
    put_x_sums(groups, [mass_tendency(table, *s, *f) for s, f in zip(two, fixed)])
    edge_y(3, every)

    def regrouped(per_group):
        (outer_low, high_above) = per_group[0], per_group[1]
        below, low = outer_low[:, :LANES], outer_low[:, LANES:]
        centre, high = high_above[:, :LANES], high_above[:, LANES:]
        near = jnp.where(lane < LANES // 2, per_group[2], below)
        return [beside(low, centre), beside(high, near)]

    def of_groups(values):
        return [list(parts) for parts in zip(*(regrouped(part) for part in zip(*values)))]

    for c in range(3):
        rows_at = slice(c * NODES, (c + 1) * NODES)
        sums[count - 1, rows_at] = jnp.where(
            lane < LANES // 2, sums[count - 1, rows_at], sums[0, rows_at]
        )
    slots = every[1:]
    groups = (slots[0:2], slots[2:4])
    start, two = of_groups(start), of_groups(two)
    tide = regrouped([part_of(every[0:2], 6), part_of(every[2:4], 6), part_of(every[4:], 6)])
    per_mass = regrouped(per_mass)
    three = []
    for n, group in enumerate(groups):
        change = average(group, per_mass[n])
        now = [
            s / 3.0 + 2.0 / 3.0 * (o + time_step * c)
            for s, o, c in zip(start[n], two[n], change)
        ]
        now[0] = now[0] + tide[n]
        three.append(now)
    put_x_sums(groups, [laplace(s) for s in three])
    edge_y(3, slots)
    change = [average(group, per_mass[n]) for n, group in enumerate(groups)]
    put_x_sums(groups, [laplace(s) for s in change])
    edge_y(3, slots)
    stepped = []
    for n, group in enumerate(groups):
        change = average(group, per_mass[n])
        now = [s - time_step * hyper_coeff * b for s, b in zip(three[n], change)]
        stepped.append(jnp.concatenate(now, 0))
    stepped = jnp.concatenate(stepped, 1)[:, :MID]
    own = lanes_ref[27:28, LANES : LANES + MID] != 0
    stored = picked(jnp.where(own, stepped, 0.0), hot_ref[...])
    out_ref[...] = stored.reshape(out_ref.shape)


def on_device(fields, jacobian, water_depth, coriolis, tide_height, slot_of, seam_rows):
    block_cols = lax.axis_size("blk") // BY
    table, weight, edge_table, lanes = map(jnp.asarray, (*operator_table(), lane_tables()))
    vmem = pl.BlockSpec(memory_space=pltpu.VMEM)
    hbm = pl.BlockSpec(memory_space=pltpu.HBM)
    params = pltpu.CompilerParams(vmem_limit_bytes=48 * 2**20)
    held = (fields, jacobian, water_depth, coriolis, tide_height)

    def call(kernel, ins, outs, cost, scratch=(), name=None):
        return pl.pallas_call(
            kernel,
            out_shape=[jax.ShapeDtypeStruct(*out) for out in outs],
            in_specs=[spec for spec, value in ins],
            out_specs=[vmem] * len(outs),
            scratch_shapes=list(scratch),
            compiler_params=params,
            cost_estimate=pl.CostEstimate(
                flops=cost, bytes_accessed=2 * 2**20, transcendentals=0
            ),
            name=name,
        )(
            *[
                pltpu.with_memory_space_constraint(value, pltpu.HBM) if spec is hbm else value
                for spec, value in ins
            ]
        )

    strip = ((HALF_ROWS, LANES), f32)
    def room(values, spaces=None):
        spaces = spaces or [pltpu.VMEM] * len(values)
        buffers = [space(x.shape, x.dtype) for space, x in zip(spaces, values)]
        return buffers + [pltpu.SemaphoreType.DMA((len(values),))]

    needed = (seam_rows, slot_of, *held, edge_table)
    corner = ((CORNER_ROWS, LANES), f32)
    scratch = [pltpu.VMEM((1, 4 * NODES, LANES), f32)]
    first, then, stored, flags = call(
        functools.partial(strips_kernel, block_cols),
        [(hbm, x) for x in needed],
        [strip, strip, ((ROWS, ELEMENTS), f32), ((8, LANES), i32)],
        10**8,
        scratch=room(needed, [pltpu.SMEM] + [pltpu.VMEM] * (len(needed) - 1)),
        name="strips",
    )
    to_next, far0, far1, to_pair = call(
        functools.partial(rows_kernel, block_cols),
        [(vmem, x) for x in (flags, stored, first, then, table, weight)],
        [strip, corner, corner, ((ROWS, LANES), f32)],
        10**8,
        scratch=scratch,
        name="rows",
    )
    span = block_cols * BY
    both = ("face", "blk")
    places = [(f, x, y) for f in range(2) for x in range(block_cols) for y in range(BY)]

    def rank(face, block_x, block_y):
        return face * span + block_x * BY + block_y

    def same(y):
        return y

    def in_pair(y):
        return y ^ 1

    def next_pair(y):
        other = y + 1 if y % 2 else y - 1
        return other if 0 <= other < BY else y

    def swapped(value, partner):
        pairs = [
            (rank(f, x, y), rank(f if partner(y) != y else 1 - f, x, partner(y)))
            for f, x, y in places
        ]
        return lax.ppermute(value, both, pairs)

    def across(value0, value1, partner):
        last = block_cols - 1

        def aligned(y):
            return partner is same or partner(y) != y

        straight = {
            (f, x, y): (f, x + 1, partner(y)) if x < last else (1 - f, 0, partner(y))
            for f, x, y in places
        }
        turned = {
            (f, last, y): (1 - f, 0, BY - 1 - partner(y) if aligned(y) else y)
            for f in range(2)
            for y in range(BY)
        }

        def eastward(value, pairs):
            return lax.ppermute(value, both, [(rank(*a), rank(*b)) for a, b in pairs.items()])

        def westward(value, pairs):
            return lax.ppermute(value, both, [(rank(*b), rank(*a)) for a, b in pairs.items()])

        if block_cols == 1:
            return eastward(value0, straight), eastward(value1, turned)
        flipped = (seam_rows[:, 1] - seam_rows[:, 0]) % seam_rows.shape[1] != 1
        face = lax.axis_index("face")
        block_x = lax.axis_index("blk") // BY
        return (
            jnp.where(
                (block_x == last) & flipped[face],
                westward(value1, turned),
                westward(value1, straight),
            ),
            jnp.where(
                (block_x == 0) & flipped[1 - face],
                eastward(value0, turned),
                eastward(value0, straight),
            ),
        )

    if block_cols == 1:
        halos = []
        for value, mirrored in ((first, mirrored_first), (then, lambda y: not mirrored_first(y))):
            pairs = [
                (rank(f, x, y), rank(1 - f, x, BY - 1 - y if mirrored(y) else y))
                for f, x, y in places
            ]
            halos.append(lax.ppermute(value, both, pairs))
        halo0, halo1 = halos
    else:
        halo0, halo1 = across(first, then, same)
    far0, far1 = across(far0, far1, next_pair)
    from_next = swapped(to_next, next_pair)
    own, hot = call(
        own_kernel,
        [(vmem, x) for x in (flags, stored, lanes)],
        [((ROWS, MID), f32), ((MID, ELEMENTS), bf16)],
        10**8,
        name="own",
    )
    (to_pair,) = call(
        functools.partial(corners_kernel, block_cols),
        [(vmem, x) for x in (flags, halo0, halo1, to_pair, hot)],
        [((ALL_ROWS, LANES), f32)],
        10**8,
        name="corners",
    )
    from_pair = swapped(to_pair, in_pair)
    tile = ((11 * NODES, LANES), f32)
    low, centre, high = call(
        functools.partial(middle_kernel, block_cols),
        [(vmem, x) for x in (flags, halo0, halo1, own, lanes, table, weight)],
        [tile, tile, tile],
        10**8,
        name="middle",
    )
    outer = ((RIM_ROWS, LANES), f32)
    (corners,) = call(
        functools.partial(far_kernel, block_cols),
        [(vmem, x) for x in (flags, far1, far0, low)],
        [outer],
        10**11,
        name="far",
    )
    (from_next,) = call(
        next_kernel, [(vmem, x) for x in (from_next, corners)], [outer], 10**10, name="next"
    )
    (stepped,) = call(
        functools.partial(steps_kernel, block_cols),
        [
            (vmem, x)
            for x in (
                flags, from_pair, from_next, low, centre, high, hot, table, weight, lanes
            )
        ],
        [(fields.shape, f32)],
        10**8,
        scratch=[pltpu.VMEM((EXT // LANES, 4 * NODES, LANES), f32)],
        name="steps",
    )
    return stepped


def solution(mesh):
    return jax.shard_map(
        on_device,
        mesh=mesh,
        in_specs=(
            P(None, None, None, ("face", "blk")),
            P(None, None, ("face", "blk")),
            P(None, None, ("face", "blk")),
            P(None, None, ("face", "blk")),
            P(None, None, ("face", "blk")),
            P(("face", "blk"), None),
            P(),
        ),
        out_specs=P(None, None, None, ("face", "blk")),
        check_vma=False,
    )
```

```python
import functools
import math

import jax
import jax.numpy as jnp
import ml_dtypes
import numpy as np
from jax import lax
from jax.experimental import pallas as pl
from jax.experimental.pallas import tpu as pltpu
from jax.sharding import PartitionSpec as P

BY = 16
GX = 16
GY = 16
NP = 8
NODES = NP * NP
ARRAYS = 7
ROWS = ARRAYS * NODES
MOVED = 6 * NODES
EDGE_ROWS = 4 * NP
ALL_ROWS = ROWS + EDGE_ROWS
HALF_ROWS = (MOVED + NODES // 2 + 2 * NP) // 2
RING = 4
RIM_ROWS = ROWS + 2 * EDGE_ROWS
CORNER_ROWS = (MOVED + NODES // 2 + 4 * NP) // 8
PITCH = GX + 2 * RING
MID = GY * PITCH
LANES = 128
EXT = MID + 2 * LANES
LEAD = LANES - RING * PITCH
ELEMENTS = GX * GY

time_step = 0.03
hyper_coeff = 0.0002

f32 = jnp.float32
bf16 = jnp.bfloat16
i32 = jnp.int32


def legendre_pair(location, degree):
    lower_value = 1.0
    upper_value = location
    for polynomial_order in range(2, degree + 1):
        lower_value, upper_value = (
            upper_value,
            (
                (2 * polynomial_order - 1) * location * upper_value
                - (polynomial_order - 1) * lower_value
            )
            / polynomial_order,
        )
    return (lower_value, upper_value)


def gll_tables(points):
    degree = points - 1
    locations = [-math.cos(math.pi * position / degree) for position in range(points)]
    for iteration in range(100):
        updated = []
        for location in locations:
            lower_value, upper_value = legendre_pair(location, degree)
            updated.append(
                location - (location * upper_value - lower_value) / ((degree + 1) * upper_value)
            )
        locations = updated
    locations[0] = -1.0
    locations[degree] = 1.0
    legendre_at = [legendre_pair(location, degree)[1] for location in locations]
    weights = [2.0 / (degree * (degree + 1) * value * value) for value in legendre_at]
    corner_value = degree * (degree + 1) / 4.0
    derivative = []
    for row_index in range(points):
        row_values = []
        for column_index in range(points):
            if row_index != column_index:
                row_values.append(
                    legendre_at[row_index]
                    / (legendre_at[column_index] * (locations[row_index] - locations[column_index]))
                )
            elif row_index == 0:
                row_values.append(-corner_value)
            elif row_index == degree:
                row_values.append(corner_value)
            else:
                row_values.append(0.0)
        derivative.append(row_values)
    return np.asarray(weights, np.float64), np.asarray(derivative, np.float64)


def in_three(matrix):
    high = matrix.astype(ml_dtypes.bfloat16)
    low = (matrix - high.astype(np.float64)).astype(ml_dtypes.bfloat16)
    return np.concatenate([high, high, low], 1)


def operator_table():
    weights, derivative = gll_tables(NP)
    eye = np.eye(NP)
    node_weight = np.outer(weights, weights).reshape(NODES, 1)
    along_x = node_weight * np.kron(derivative, eye)
    along_y = node_weight * np.kron(eye, derivative)
    second = derivative @ derivative
    both = node_weight * (np.kron(second, eye) + np.kron(eye, second))
    table = np.zeros((5 * NODES, 4 * NODES), ml_dtypes.bfloat16)
    table[:NODES, : 3 * NODES] = in_three(along_x)
    table[NODES : 2 * NODES, : 3 * NODES] = in_three(along_y)
    flux = [in_three(along_x), in_three(along_y)]
    for k, part in enumerate(flux):
        at = 2 * k * NODES
        table[2 * NODES : 3 * NODES, at : at + 2 * NODES] = part[:, : 2 * NODES]
        table[3 * NODES : 4 * NODES, at : at + NODES] = part[:, 2 * NODES :]
    table[4 * NODES :, : 3 * NODES] = in_three(both)
    table = table.astype(np.float32)
    spread = np.broadcast_to(node_weight, (NODES, LANES)).astype(np.float32)
    ends = np.r_[:NP, NODES - NP : NODES]
    edge_table = np.zeros((10 * NP, 4 * NODES), np.float32)
    for k in range(4):
        edge_table[2 * k * NP : 2 * (k + 1) * NP] = table[k * NODES + ends]
    edge_table[8 * NP :, :LANES] = spread[ends]
    return table, np.ascontiguousarray(spread), edge_table


def lane_tables():
    table = np.zeros((24, MID), np.int32)
    for lane in range(MID):
        row, col = divmod(lane, PITCH)
        x = col - RING
        own = 0 <= x < GX
        table[0:8, lane] = x * GY + row if own else -1
        if not own:
            table[8:16, lane] = row * RING + (col if x < 0 else x - GX)
        table[16:24, lane] = 0 if own else (1 if x < 0 else 2)
    ext = np.zeros((8, EXT), np.int32)
    outer = np.zeros((32, 2 * LANES), np.int32)
    for lane in range(EXT):
        row, col = divmod(lane - LEAD, PITCH)
        y = row - RING
        x = col - RING
        ext[0, lane] = x in (-RING, GX + RING - 1)
        ext[1, lane] = y == GY - 1
        ext[2, lane] = y == 0
        ext[3, lane] = 0 <= y < GY and 0 <= x < GX
        ext[4, lane] = y == -RING
        ext[5, lane] = y == GY + RING - 1
        if -RING - 1 <= y < 0 or GY <= y <= GY + RING:
            place = lane if y < 0 else lane - MID
            step = y + RING if y < 0 else y - GY
            near = step + 1 if y < 0 else step
            far = 0 <= step < RING
            if 0 <= x < GX:
                outer[0:8, place] = near * GX + x
                outer[8:16, place] = 1
                outer[24:32, place] = LANES + step * GX + x if far else -1
            else:
                across = x + RING if x < 0 else x - GX
                outer[0:8, place] = (RING + 1) * GX + near * RING + across
                outer[8:16, place] = 2 if x < 0 else 3
                outer[24:32, place] = LANES + RING * GX + step * RING + across if far else -1
            outer[16:24, place] = y > 0
    whole = np.zeros((64, EXT), np.int32)
    whole[0:24, :MID] = table
    whole[24:32] = ext
    whole[32:64, : 2 * LANES] = outer
    return whole


def dot(a, b):
    return jnp.dot(a, b, preferred_element_type=f32)


def picked(values, one_hot):
    high = values.astype(bf16)
    low = (values - high.astype(f32)).astype(bf16)
    both = dot(jnp.concatenate([high, low], 0), one_hot)
    return both[: values.shape[0]] + both[values.shape[0] :]


def as_one_hot(row_of_lane, depth):
    index = lax.broadcasted_iota(i32, (depth, row_of_lane.shape[1]), 0)
    return jnp.where(index == row_of_lane[0:1], 1.0, 0.0).astype(bf16)


def high_low_high(values):
    high = values.astype(bf16)
    low = (values - high.astype(f32)).astype(bf16)
    return [high, low, high]


def by_slot(halves, cell_of_lane):
    size = cell_of_lane.shape[1]
    halves = [jnp.broadcast_to(half, (8, LANES)) for half in halves]
    chosen = []
    for k in range(size // LANES):
        cell = cell_of_lane[:, k * LANES : (k + 1) * LANES]
        low, high = (jnp.take_along_axis(half, cell & (LANES - 1), axis=1) for half in halves)
        chosen.append(jnp.where(cell < 0, -1, jnp.where(cell < LANES, low, high)))
    return as_one_hot(jnp.concatenate(chosen, 1), ELEMENTS)


def stored_rows(fields_ref, others):
    fields = fields_ref[...].reshape(3 * NODES, ELEMENTS)
    others = [ref[...].reshape(NODES, ELEMENTS) for ref in others]
    return jnp.concatenate([fields[:NODES] - others[-1], fields[NODES:]] + others, 0)


def mass_tendency(table, p, u, v, area_depth, weighted_area, spin):
    slopes = dot(table[: 2 * NODES, : 3 * NODES], jnp.concatenate(high_low_high(p), 0))
    flux = high_low_high(area_depth * u)[:2] + high_low_high(area_depth * v)[:2]
    spread = dot(table[2 * NODES : 4 * NODES], jnp.concatenate(flux, 0))
    return [
        -(spread[:NODES] + spread[NODES:]),
        spin * v - weighted_area * slopes[:NODES],
        -spin * u - weighted_area * slopes[NODES:],
    ]


def edge_values(table_ref, weight_ref, p, u, v, area, depth, spin):
    root = jnp.sqrt(area)
    mass = jnp.concatenate([weight_ref[...]] * (area.shape[1] // LANES), 1) * area
    table = table_ref[...].astype(bf16)
    return mass_tendency(table, p, u, v, root * depth, root, mass * spin) + [mass]


def column_edges(table, weight, p, u, v, area, depth, spin):
    def ends(part):
        return jnp.concatenate([part[:NP], part[NODES - NP :]], 0)

    root = jnp.sqrt(area)
    area_depth = root * depth
    root, mass = ends(root), weight * ends(area)
    weighted_spin = mass * ends(spin)
    slopes = dot(table[: 4 * NP, : 3 * NODES], jnp.concatenate(high_low_high(p), 0))
    flux = high_low_high(area_depth * u)[:2] + high_low_high(area_depth * v)[:2]
    spread = dot(table[4 * NP :], jnp.concatenate(flux, 0))
    return [
        -(spread[: 2 * NP] + spread[2 * NP :]),
        weighted_spin * ends(v) - root * slopes[: 2 * NP],
        -weighted_spin * ends(u) - root * slopes[2 * NP :],
        mass,
    ]


def row_edges(sums):
    return tuple(sums[0, pl.ds(j, EDGE_ROWS, stride=NP)] for j in (NP - 1, 0))


def beside(left, right):
    return jnp.concatenate([left, right], 1)


def one_of_four(parts, index):
    out = parts[0]
    for k in range(1, 4):
        out = jnp.where(index == k, parts[k], out)
    return out


def folded(tide, kept, late, step):
    half = NODES // 2
    back = pltpu.roll(tide[half:], LANES - step, 1)
    onward = pltpu.roll(tide[half:], step, 1)
    return jnp.where(kept, tide[:half], jnp.where(late, back, onward))


def unfolded(rows, late, step):
    back = pltpu.roll(rows, LANES - step, 1)
    onward = pltpu.roll(rows, step, 1)
    return jnp.concatenate([rows, jnp.where(late, onward, back)], 0)


def strip_rows(parts, late, shift, rims):
    lane = lax.broadcasted_iota(i32, (1, LANES), 1)
    index = (lane >> shift) & 3
    kept = jnp.where(late, index // 2, 1 - index // 2) != 0
    tide = folded(parts[6], kept, late, 2 << shift)
    rim = one_of_four(rims, index)
    return jnp.concatenate(parts[:6] + [tide, rim, jnp.zeros_like(rim)], 0)


def placed_rows(whole, late, shift):
    half = NODES // 2
    tide = unfolded(whole[MOVED : MOVED + half], late, 2 << shift)
    rim = whole[MOVED + half : MOVED + half + NP]
    return jnp.concatenate([whole[:MOVED], tide] + spread_out(rim, late, shift), 0)


def spread_out(rim, late, shift):
    parts = []
    for k in range(4):
        first = pltpu.roll(rim, (LANES - (k << shift)) % LANES, 1) if k else rim
        last = pltpu.roll(rim, (3 - k) << shift, 1) if k < 3 else rim
        parts.append(jnp.where(late, first, last))
    return parts


def with_row_rim(whole, sums, top):
    north, south = row_edges(sums)
    rim = jnp.where(top, pltpu.roll(north, RING, 1), pltpu.roll(south, LANES - RING, 1))
    parts = [rim[k * NP : (k + 1) * NP] for k in range(4)]
    lane = lax.broadcasted_iota(i32, (1, LANES), 1)
    spots = []
    for k, part in enumerate(parts):
        first = pltpu.roll(part, k * RING, 1) if k else part
        last = pltpu.roll(part, (LANES - (3 - k) * RING) % LANES, 1) if k < 3 else part
        spots.append(jnp.where(top, first, last))
    rim = one_of_four(spots, (lane >> 2) & 3)
    return jnp.concatenate([whole[: MOVED + NODES // 2 + NP], rim], 0)


def in_eight(whole):
    whole = jnp.concatenate([whole, jnp.zeros((8 * CORNER_ROWS - whole.shape[0], LANES), f32)], 0)
    return [whole[k * CORNER_ROWS : (k + 1) * CORNER_ROWS] for k in range(8)]


def corner_of(whole, start, top):
    lane = lax.broadcasted_iota(i32, (1, LANES), 1)
    out = None
    for k, part in enumerate(in_eight(whole)):
        last = pltpu.roll(part, (LANES - start - 48 + 16 * k) % LANES, 1)
        first = pltpu.roll(part, (LANES - start + 16 * k) % LANES, 1)
        part = jnp.where(top != 0, last, first)
        out = part if k == 0 else jnp.where(lane >= 16 * k, part, out)
    return out


def both_corners(whole, odd):
    group = lax.broadcasted_iota(i32, (1, LANES), 1) >> 4
    other_group = (group + jnp.where(odd != 0, 7, 1)) & 7
    first, other = None, None
    for k, part in enumerate(in_eight(whole)):
        part = pltpu.roll(part, (LANES + 16 * k - 48 * odd) & (LANES - 1), 1)
        first = part if k == 0 else jnp.where(group == k, part, first)
        other = part if k == 0 else jnp.where(other_group == k, part, other)
    return first, other


def arrived_corners(far0, far1, block_cols, odd):
    lane = lax.broadcasted_iota(i32, (1, LANES), 1)
    corners = []
    for k in range(8):
        if block_cols == 1:
            part = jnp.where((lane >> 4) == k, far0, far1)
            part = pltpu.roll(part, (LANES + 64 + 16 * (1 - odd) - 16 * k) & (LANES - 1), 1)
        else:
            first = pltpu.roll(far0, (64 - 16 * k) % LANES, 1)
            other = pltpu.roll(far1, (80 - 16 * k) % LANES, 1)
            part = jnp.where((lane & 16) == 0, first, other)
        corners.append(part)
    return jnp.concatenate(corners, 0), ((lane >> 4) & 1) ^ (1 - odd if block_cols == 1 else 0)


def packed(whole):
    second = lax.broadcasted_iota(i32, (1, LANES), 1) >= 64
    top, bottom = whole[:HALF_ROWS], whole[HALF_ROWS:]
    return (
        jnp.where(second, pltpu.roll(bottom, 64, 1), top),
        jnp.where(second, bottom, pltpu.roll(top, 64, 1)),
    )


def unpacked(in0, in1):
    second = lax.broadcasted_iota(i32, (1, LANES), 1) >= 64
    top = jnp.where(second, pltpu.roll(in1, 64, 1), in0)
    bottom = jnp.where(second, in1, pltpu.roll(in0, 64, 1))
    return jnp.concatenate([top, bottom], 0)


def seam_flags(seam_ref, block_cols):
    size_y = seam_ref.shape[1]
    face = lax.axis_index("face")
    blk = lax.axis_index("blk")
    block_x = blk // BY

    def flipped(k):
        return jnp.where(lax.rem(seam_ref[k, 1] - seam_ref[k, 0] + size_y, size_y) != 1, 1, 0)

    first, second = flipped(0), flipped(1)
    east_flip = jnp.where(face == 0, first, second)
    west_flip = jnp.where(face == 0, second, first)
    if block_cols == 1:
        return 1 - east_flip, 0, east_flip, 1
    at_east = jnp.where(block_x == block_cols - 1, east_flip, 0)
    at_west = jnp.where(block_x == 0, west_flip, 0)
    return 1, at_east, 0, at_west


def slots_in(flags_ref):
    return flags_ref[4:5], flags_ref[5:6]


def flags_in(flags_ref, tiles=1):
    return [jnp.concatenate([flags_ref[k : k + 1]] * tiles, 1) for k in range(4)]


def mirrored_first(block_y):
    return (block_y >= BY // 4) & (block_y < BY - BY // 4)


def in_order(block_cols, first, second):
    if block_cols > 1:
        return first, second
    swap = mirrored_first(lax.rem(lax.axis_index("blk"), BY))
    return jnp.where(swap, second, first), jnp.where(swap, first, second)


def strips_kernel(block_cols, *refs):
    sources, (first_ref, then_ref, stored_ref, flags_ref) = refs[:8], refs[8:12]
    buffers, sems = refs[12:20], refs[20]
    pieces = list(zip(sources, buffers))
    pieces[2:3] = [(sources[2].at[c], buffers[2].at[c]) for c in range(3)]
    copies = [
        pltpu.make_async_copy(source, buffer, sems.at[k])
        for k, (source, buffer) in enumerate(pieces)
    ]
    for copy in copies:
        copy.start()
    seam_ref, slot_ref, fields_ref, area_ref, depth_ref, spin_ref, tide_ref = buffers[:7]
    table_ref = buffers[7]
    for copy in copies[:2]:
        copy.wait()
    east0, flip0, east1, flip1 = flags = seam_flags(seam_ref, block_cols)
    index = lax.broadcasted_iota(i32, (8, LANES), 0)
    flags_ref[...] = sum(jnp.where(index == k, flag, 0) for k, flag in enumerate(flags))
    slots = slot_ref[:, :LANES], slot_ref[:, LANES:]
    flags_ref[4:5], flags_ref[5:6] = slots
    lane = lax.broadcasted_iota(i32, (8, 2 * LANES), 1)
    second = (lane & 64) != 0
    place = lane & 63
    row = place >> 2
    row = jnp.where(jnp.where(second, flip1, flip0) != 0, GY - 1 - row, row)
    east = jnp.where(second, east1, east0) != 0
    col = jnp.where(east, GX - RING, 0) + (place & 3)
    col = jnp.where(lane >= LANES, jnp.where(east, GX - RING - 1, RING), col)
    one_hot = by_slot(slots, col * GY + row)
    for copy in copies[2:9]:
        copy.wait()
    stored = stored_rows(fields_ref, (area_ref, depth_ref, spin_ref, tide_ref))
    both = picked(stored, one_hot)

    lane = lax.broadcasted_iota(i32, (1, LANES), 1)
    second = lane >= 64
    flip = jnp.where(second, flip1, flip0) != 0
    sign = jnp.where(flip, -1.0, 1.0)
    node = lax.broadcasted_iota(i32, (1, NP, 1), 1)

    def turned(values):
        shaped = values.reshape(-1, NP, LANES)
        shaped = pltpu.roll(shaped, 4, 1)
        shaped = jnp.where((node & 2) == 0, pltpu.roll(shaped, 6, 1), pltpu.roll(shaped, 2, 1))
        shaped = jnp.where((node & 1) == 0, pltpu.roll(shaped, 7, 1), pltpu.roll(shaped, 1, 1))
        return shaped.reshape(values.shape)

    strip, ring = (
        [part[k * NODES : (k + 1) * NODES] for k in range(ARRAYS)]
        for part in (both[:, :LANES], both[:, LANES:])
    )
    for copy in copies[9:]:
        copy.wait()
    table, weight = table_ref[: 8 * NP].astype(bf16), table_ref[8 * NP :, :LANES]
    edges = column_edges(table, weight, *ring[:6])
    east = jnp.where(second, east1, east0) != 0
    ends = [jnp.where(east, part[NP:], part[:NP]) for part in edges]
    ends[2] = ends[2] * sign
    strip[2] = strip[2] * sign
    strip[5] = strip[5] * sign
    strips = []
    for part, flip in zip(packed(strip_rows(strip, east, 0, ends)), (flip0, flip1)):
        if isinstance(flip, int):
            strips.append(turned(part) if flip else part)
        else:
            strips.append(jnp.where(flip != 0, turned(part), part))
    first_ref[...], then_ref[...] = in_order(block_cols, *strips)
    stored_ref[...] = stored


def rows_kernel(
    block_cols, flags_ref, stored_ref, first_ref, then_ref, table_ref, weight_ref,
    next_ref, far0_ref, far1_ref, pair_ref, sums,
):
    east0, flip0, east1, flip1 = flags_in(flags_ref)
    odd = lax.axis_index("blk") & 1
    lane = lax.broadcasted_iota(i32, (8, 2 * LANES), 1)
    row = jnp.where(odd != 0, GY - RING, 0) + ((lane & 63) >> 4)
    row = jnp.where((lane & 64) != 0, jnp.where(odd != 0, GY - RING - 1, RING), row)
    five = jnp.where(odd != 0, 0, GY - RING - 1) + jnp.minimum((lane & (LANES - 1)) >> 4, RING)
    row = jnp.where(lane >= LANES, five, row)
    both = picked(stored_ref[...], by_slot(slots_in(flags_ref), (lane & 15) * GY + row))
    pair_ref[...] = both[:, LANES:]
    rows = [both[k * NODES : (k + 1) * NODES, :LANES] for k in range(ARRAYS)]
    whole = unpacked(*in_order(block_cols, first_ref[...], then_ref[...]))
    strip = [whole[k * NODES : (k + 1) * NODES] for k in range(6)]
    edges = edge_values(table_ref, weight_ref, *map(beside, strip, rows[:6]))
    sums[0] = jnp.concatenate([part[:, :LANES] for part in edges], 0)
    lane = lax.broadcasted_iota(i32, (1, LANES), 1)
    top0, top1 = odd ^ flip0, odd ^ flip1
    whole = with_row_rim(whole, sums, jnp.where(lane >= 64, top1, top0) != 0)
    if block_cols == 1:
        far0_ref[...], far1_ref[...] = both_corners(whole, odd)
    else:
        far0_ref[...] = corner_of(whole, 0, top0)
        far1_ref[...] = corner_of(whole, 64, top1)
    sums[0] = jnp.concatenate([part[:, LANES:] for part in edges], 0)
    up = jnp.broadcast_to(odd != 0, (1, LANES))
    rim = pltpu.roll(jnp.where(up, *row_edges(sums)), 64, 1)
    rim = [rim[k * NP : (k + 1) * NP] for k in range(4)]
    whole = strip_rows(rows, up, 4, rim)
    top, bottom = whole[:HALF_ROWS], whole[HALF_ROWS:]
    next_ref[...] = jnp.where(lane >= 64, pltpu.roll(bottom, 64, 1), top)


def corners_kernel(block_cols, flags_ref, first_ref, then_ref, pair_ref, _, out_ref):
    east0, flip0, east1, flip1 = flags_in(flags_ref)
    in0, in1 = in_order(block_cols, first_ref[...], then_ref[...])
    top = 1 - (lax.axis_index("blk") & 1)
    lane = lax.broadcasted_iota(i32, (1, LANES), 1)
    halves = []
    for start in (0, 64):
        at0 = jnp.where(top != 0, 36, 80)
        at1 = jnp.where(top != 0, 56, 100)
        first = pltpu.roll(in0, (at0 - start) & (LANES - 1), 1)
        other = pltpu.roll(in1, (at1 - start) & (LANES - 1), 1)
        halves.append(jnp.where(lane < 100, first, other))
    late = jnp.where(lane < 100, east0, east1) == 0
    whole = placed_rows(jnp.concatenate(halves, 0), late, 0)
    out_ref[:ROWS] = jnp.where(lane < 80, pair_ref[...], whole[:ROWS])
    out_ref[ROWS:] = whole[ROWS:]


def own_kernel(flags_ref, stored_ref, lanes_ref, own_ref, hot_ref):
    one_hot = by_slot(slots_in(flags_ref), lanes_ref[0:8, :MID])
    own_ref[...] = picked(stored_ref[...], one_hot)
    hot_ref[...] = one_hot.astype(f32).T.astype(bf16)


def first_sums(table, weight, parts, rims, at_rim):
    p, u, v, area, depth, spin, tide = parts
    size = area.shape[1]
    root = jnp.sqrt(area)
    mass = jnp.concatenate([weight] * (size // LANES), 1) * area
    used = [p, u, v, root * depth, root, mass * spin, tide]
    for part, rim in zip(mass_tendency(table, p, u, v, *used[3:6]) + [mass], rims):
        west, east = part[:NP], part[NODES - NP :]
        at_east = jnp.where(at_rim, rim, pltpu.roll(west, size - 1, 1))
        at_west = jnp.where(at_rim, rim, pltpu.roll(east, 1, 1))
        used.append(
            jnp.concatenate([west + at_west, part[NP : NODES - NP], east + at_east], 0)
        )
    return used


def middle_kernel(
    block_cols, flags_ref, first_ref, then_ref, own_ref, lanes_ref, table_ref, weight_ref,
    low_ref, centre_ref, high_ref,
):
    east0, flip0, east1, flip1 = flags_in(flags_ref)
    second = lax.broadcasted_iota(i32, (1, LANES), 1) >= 64
    late = jnp.where(second, east1, east0) == 0
    whole = unpacked(*in_order(block_cols, first_ref[...], then_ref[...]))
    whole = placed_rows(whole, late, 0)
    side = lanes_ref[16:24, :MID]
    east = flags_in(flags_ref, MID // LANES)[0]
    first_at = jnp.where(side == 2, 64 * (1 - east), 64 * east)
    place = jnp.where(side == 0, -1, lanes_ref[8:16, :MID] + first_at)
    placed = picked(whole, as_one_hot(place, LANES))
    parts = [
        placed[k * NODES : (k + 1) * NODES] + own_ref[k * NODES : (k + 1) * NODES]
        for k in range(ARRAYS)
    ]
    rims = [placed[ROWS + c * NP : ROWS + (c + 1) * NP] for c in range(4)]
    at_rim = lanes_ref[24:25, LANES : LANES + MID] != 0
    used = first_sums(table_ref[...].astype(bf16), weight_ref[...], parts, rims, at_rim)
    for k, ref in enumerate((low_ref, centre_ref, high_ref)):
        for n, part in enumerate(used):
            ref[n * NODES : (n + 1) * NODES] = part[:, k * LANES : (k + 1) * LANES]


def far_kernel(block_cols, flags_ref, far1_ref, far0_ref, next_ref, _, out_ref):
    east0, flip0, east1, flip1 = flags_in(flags_ref)
    odd = lax.axis_index("blk") & 1
    lane = lax.broadcasted_iota(i32, (1, LANES), 1)
    below = jnp.broadcast_to(odd == 0, (1, LANES))
    strip = jnp.concatenate([next_ref[...], pltpu.roll(next_ref[...], 64, 1)], 0)
    strip = placed_rows(strip, below, 4)
    corners, strip_of = arrived_corners(far0_ref[...], far1_ref[...], block_cols, odd)
    late = jnp.where(strip_of != 0, east1, east0) == 0
    rim = MOVED + NODES // 2 + NP
    rim = jnp.concatenate(spread_out(corners[rim : rim + NP], below, 2), 0)
    corners = placed_rows(corners, late, 0)
    own = lane < 64
    out_ref[:ROWS] = jnp.where(own, strip[:ROWS], corners[:ROWS])
    out_ref[ROWS:ALL_ROWS] = corners[ROWS:]
    out_ref[ALL_ROWS:] = jnp.where(own, strip[ROWS:], rim)


def steps_kernel(
    block_cols, flags_ref, pair_ref, next_ref, low_ref, centre_ref,
    high_ref, hot_ref, table_ref, weight_ref, lanes_ref, out_ref, sums, leaving, sems,
):
    east0, flip0, east1, flip1 = flags_in(flags_ref)
    odd = lax.axis_index("blk") & 1
    block_y = lax.rem(lax.axis_index("blk"), BY)

    lane = lax.broadcasted_iota(i32, (1, LANES), 1)
    pair = jnp.concatenate([pair_ref[...], jnp.zeros((EDGE_ROWS, LANES), f32)], 0)
    around = beside(pair, next_ref[...])
    outer_at = [lanes_ref[32 + 8 * k : 40 + 8 * k, : 2 * LANES] for k in range(4)]
    kind = outer_at[1]
    from_pair = jnp.where(outer_at[2] != 0, 1 - odd, odd) != 0
    east = flags_in(flags_ref, 2)[0]
    strip_at = jnp.where(kind == 3, 1 - east, east)
    far_at = strip_at ^ (1 - odd) if block_cols == 1 else strip_at
    strip_at, far_at = (jnp.where(kind > 1, at, 0) for at in (strip_at, far_at))
    place = jnp.where(
        from_pair,
        outer_at[0] + (RING + 1) * RING * strip_at,
        jnp.where(outer_at[3] < 0, -1, outer_at[3] + RING * RING * far_at),
    )
    outer = picked(around, as_one_hot(jnp.where(kind == 0, -1, place), 2 * LANES))
    table = table_ref[...].astype(bf16)
    tiles = (None, low_ref, centre_ref, high_ref, None)
    count = len(tiles)
    masks = [lanes_ref[24:32, k * LANES : (k + 1) * LANES] for k in range(count)]
    closed_above = jnp.where(block_y == BY - 1, masks[-2][1:2], 0) != 0
    closed_below = jnp.where(block_y == 0, masks[1][2:3], 0) != 0
    first_row = jnp.where(odd == 0, masks[0][4:5], 0) != 0
    last_row = jnp.where(odd != 0, masks[-1][5:6], 0) != 0
    outer_used = first_sums(
        table,
        weight_ref[...],
        [outer[k * NODES : (k + 1) * NODES] for k in range(ARRAYS)],
        [outer[ROWS + c * NP : ROWS + (c + 1) * NP] for c in range(4)],
        beside(masks[0][0:1], masks[-1][0:1]) != 0,
    )

    def shifted(parts, by, ring):
        turned = [pltpu.roll(part, -by % LANES, 1) for part in parts]
        size = len(parts)
        step = 1 if by > 0 else -1
        others = [(k + step) % size if ring else min(max(k + step, 0), size - 1) for k in range(size)]
        from_other = lane >= LANES - by if by > 0 else lane < -by
        return [jnp.where(from_other, turned[others[k]], turned[k]) for k in range(size)]

    def put_x_sums(groups, components):
        slots = [k for group in groups for k in group]
        ring = len(slots) < count
        per_tile = [
            [part[:, n * LANES : (n + 1) * LANES] for part in parts]
            for group, parts in zip(groups, components)
            for n in range(len(group))
        ]
        for c in range(3):
            parts = [tile[c] for tile in per_tile]
            west = [part[:NP] for part in parts]
            east = [part[NODES - NP :] for part in parts]
            at_east, at_west = shifted(west, 1, ring), shifted(east, -1, ring)
            for n, k in enumerate(slots):
                sums[k, c * NODES : c * NODES + NP] = west[n] + at_west[n]
                sums[k, c * NODES + NP : (c + 1) * NODES - NP] = parts[n][NP : NODES - NP]
                sums[k, (c + 1) * NODES - NP : (c + 1) * NODES] = east[n] + at_east[n]

    def edge_y(components, slots, rows=None):
        ring = len(slots) < count
        south_at = pl.ds(0, components * NP, stride=NP)
        north_at = pl.ds(NP - 1, components * NP, stride=NP)
        south = [sums[k, south_at] for k in slots]
        north = [sums[k, north_at] for k in slots]
        at_north, at_south = shifted(south, PITCH, ring), shifted(north, -PITCH, ring)
        for n, k in enumerate(slots):
            if k == count - 2:
                at_north[n] = jnp.where(closed_above, 0.0, at_north[n])
            if k == 1:
                at_south[n] = jnp.where(closed_below, 0.0, at_south[n])
        if rows is not None:
            at_south[0] = jnp.where(first_row, rows[0], at_south[0])
            at_north[-1] = jnp.where(last_row, rows[1], at_north[-1])
        for n, k in enumerate(slots):
            sums[k, south_at] = south[n] + at_south[n]
            sums[k, north_at] = north[n] + at_north[n]

    node = lax.broadcasted_iota(i32, (1, NP, 1), 1)
    rows = []
    for rim in (outer[ALL_ROWS:, :LANES], outer[ALL_ROWS:, LANES:]):
        east = pltpu.roll(rim, LANES - 1, 1).reshape(4, NP, LANES)
        west = pltpu.roll(rim, 1, 1).reshape(4, NP, LANES)
        rim = (
            rim.reshape(4, NP, LANES)
            + jnp.where(node == NP - 1, pltpu.roll(east, NP - 1, 1), 0.0)
            + jnp.where(node == 0, pltpu.roll(west, 1, 1), 0.0)
        )
        rows.append(rim.reshape(EDGE_ROWS, LANES))

    every = tuple(range(count))
    groups = (every[0:2], every[2:4], every[4:])

    def tile_part(k, n):
        if tiles[k] is None:
            return outer_used[n][:, :LANES] if k == 0 else outer_used[n][:, LANES:]
        return tiles[k][n * NODES : (n + 1) * NODES]

    def part_of(group, n):
        return jnp.concatenate([tile_part(k, n) for k in group], 1)

    def summed(group, c):
        return jnp.concatenate([sums[k, c * NODES : (c + 1) * NODES] for k in group], 1)

    def average(group, per_mass):
        return [summed(group, c) * per_mass for c in range(3)]

    def laplace(s):
        return [
            dot(table[4 * NODES :, : 3 * NODES], jnp.concatenate(high_low_high(part), 0))
            for part in s
        ]

    start = [[part_of(group, n) for n in range(3)] for group in groups]
    fixed = [[part_of(group, n) for n in range(3, 6)] for group in groups]
    for k in every:
        for c in range(4):
            sums[k, c * NODES : (c + 1) * NODES] = tile_part(k, 7 + c)
    edge_y(4, every, rows)
    per_mass = [1.0 / summed(group, 3) for group in groups]
    one = []
    for n, group in enumerate(groups):
        change = average(group, per_mass[n])
        one.append([s + time_step * c for s, c in zip(start[n], change)])
    put_x_sums(groups, [mass_tendency(table, *s, *f) for s, f in zip(one, fixed)])
    edge_y(3, every)
    two = []
    for n, group in enumerate(groups):
        change = average(group, per_mass[n])
        two.append(
            [0.75 * s + 0.25 * (o + time_step * c) for s, o, c in zip(start[n], one[n], change)]
        )
    put_x_sums(groups, [mass_tendency(table, *s, *f) for s, f in zip(two, fixed)])
    edge_y(3, every)

    def regrouped(per_group):
        (outer_low, high_above) = per_group[0], per_group[1]
        below, low = outer_low[:, :LANES], outer_low[:, LANES:]
        centre, high = high_above[:, :LANES], high_above[:, LANES:]
        near = jnp.where(lane < LANES // 2, per_group[2], below)
        return [beside(low, centre), beside(high, near)]

    def of_groups(values):
        return [list(parts) for parts in zip(*(regrouped(part) for part in zip(*values)))]

    for c in range(3):
        rows_at = slice(c * NODES, (c + 1) * NODES)
        sums[count - 1, rows_at] = jnp.where(
            lane < LANES // 2, sums[count - 1, rows_at], sums[0, rows_at]
        )
    slots = every[1:]
    groups = (slots[0:2], slots[2:4])
    start, two = of_groups(start), of_groups(two)
    tide = regrouped([part_of(every[0:2], 6), part_of(every[2:4], 6), part_of(every[4:], 6)])
    per_mass = regrouped(per_mass)
    three = []
    for n, group in enumerate(groups):
        change = average(group, per_mass[n])
        now = [
            s / 3.0 + 2.0 / 3.0 * (o + time_step * c)
            for s, o, c in zip(start[n], two[n], change)
        ]
        now[0] = now[0] + tide[n]
        three.append(now)
    put_x_sums(groups, [laplace(s) for s in three])
    edge_y(3, slots)
    change = [average(group, per_mass[n]) for n, group in enumerate(groups)]
    put_x_sums(groups, [laplace(s) for s in change])
    edge_y(3, slots)
    stepped = []
    for n, group in enumerate(groups):
        change = average(group, per_mass[n])
        now = [s - time_step * hyper_coeff * b for s, b in zip(three[n], change)]
        stepped.append(jnp.concatenate(now, 0))
    stepped = jnp.concatenate(stepped, 1)[:, :MID]
    own = lanes_ref[27:28, LANES : LANES + MID] != 0
    stored = picked(jnp.where(own, stepped, 0.0), hot_ref[...])
    copies = []
    for c in range(3):
        leaving[c] = stored[c * NODES : (c + 1) * NODES].reshape(leaving.shape[1:])
        copies.append(pltpu.make_async_copy(leaving.at[c], out_ref.at[c], sems.at[c]))
        copies[c].start()
    for copy in copies:
        copy.wait()


def on_device(fields, jacobian, water_depth, coriolis, tide_height, slot_of, seam_rows):
    block_cols = lax.axis_size("blk") // BY
    table, weight, edge_table, lanes = map(jnp.asarray, (*operator_table(), lane_tables()))
    vmem = pl.BlockSpec(memory_space=pltpu.VMEM)
    hbm = pl.BlockSpec(memory_space=pltpu.HBM)
    params = pltpu.CompilerParams(vmem_limit_bytes=48 * 2**20)
    held = (fields, jacobian, water_depth, coriolis, tide_height)

    def call(kernel, ins, outs, cost, scratch=(), name=None, out_spec=vmem):
        return pl.pallas_call(
            kernel,
            out_shape=[jax.ShapeDtypeStruct(*out) for out in outs],
            in_specs=[spec for spec, value in ins],
            out_specs=[out_spec] * len(outs),
            scratch_shapes=list(scratch),
            compiler_params=params,
            cost_estimate=pl.CostEstimate(
                flops=cost, bytes_accessed=2 * 2**20, transcendentals=0
            ),
            name=name,
        )(
            *[
                pltpu.with_memory_space_constraint(value, pltpu.HBM) if spec is hbm else value
                for spec, value in ins
            ]
        )

    strip = ((HALF_ROWS, LANES), f32)
    def room(values, spaces=None):
        spaces = spaces or [pltpu.VMEM] * len(values)
        buffers = [space(x.shape, x.dtype) for space, x in zip(spaces, values)]
        return buffers + [pltpu.SemaphoreType.DMA((len(values) + 2,))]

    needed = (seam_rows, slot_of, *held, edge_table)
    corner = ((CORNER_ROWS, LANES), f32)
    scratch = [pltpu.VMEM((1, 4 * NODES, LANES), f32)]
    first, then, stored, flags = call(
        functools.partial(strips_kernel, block_cols),
        [(hbm, x) for x in needed],
        [strip, strip, ((ROWS, ELEMENTS), f32), ((8, LANES), i32)],
        10**8,
        scratch=room(needed, [pltpu.SMEM] + [pltpu.VMEM] * (len(needed) - 1)),
        name="strips",
    )
    to_next, far0, far1, to_pair = call(
        functools.partial(rows_kernel, block_cols),
        [(vmem, x) for x in (flags, stored, first, then, table, weight)],
        [strip, corner, corner, ((ROWS, LANES), f32)],
        10**8,
        scratch=scratch,
        name="rows",
    )
    span = block_cols * BY
    both = ("face", "blk")
    places = [(f, x, y) for f in range(2) for x in range(block_cols) for y in range(BY)]

    def rank(face, block_x, block_y):
        return face * span + block_x * BY + block_y

    def same(y):
        return y

    def in_pair(y):
        return y ^ 1

    def next_pair(y):
        other = y + 1 if y % 2 else y - 1
        return other if 0 <= other < BY else y

    def swapped(value, partner):
        pairs = [
            (rank(f, x, y), rank(f if partner(y) != y else 1 - f, x, partner(y)))
            for f, x, y in places
        ]
        return lax.ppermute(value, both, pairs)

    def across(value0, value1, partner):
        last = block_cols - 1

        def aligned(y):
            return partner is same or partner(y) != y

        straight = {
            (f, x, y): (f, x + 1, partner(y)) if x < last else (1 - f, 0, partner(y))
            for f, x, y in places
        }
        turned = {
            (f, last, y): (1 - f, 0, BY - 1 - partner(y) if aligned(y) else y)
            for f in range(2)
            for y in range(BY)
        }

        def eastward(value, pairs):
            return lax.ppermute(value, both, [(rank(*a), rank(*b)) for a, b in pairs.items()])

        def westward(value, pairs):
            return lax.ppermute(value, both, [(rank(*b), rank(*a)) for a, b in pairs.items()])

        if block_cols == 1:
            return eastward(value0, straight), eastward(value1, turned)
        flipped = (seam_rows[:, 1] - seam_rows[:, 0]) % seam_rows.shape[1] != 1
        face = lax.axis_index("face")
        block_x = lax.axis_index("blk") // BY
        return (
            jnp.where(
                (block_x == last) & flipped[face],
                westward(value1, turned),
                westward(value1, straight),
            ),
            jnp.where(
                (block_x == 0) & flipped[1 - face],
                eastward(value0, turned),
                eastward(value0, straight),
            ),
        )

    if block_cols == 1:
        halos = []
        for value, mirrored in ((first, mirrored_first), (then, lambda y: not mirrored_first(y))):
            pairs = [
                (rank(f, x, y), rank(1 - f, x, BY - 1 - y if mirrored(y) else y))
                for f, x, y in places
            ]
            halos.append(lax.ppermute(value, both, pairs))
        halo0, halo1 = halos
    else:
        halo0, halo1 = across(first, then, same)
    far0, far1 = across(far0, far1, next_pair)
    from_next = swapped(to_next, next_pair)
    own, hot = call(
        own_kernel,
        [(vmem, x) for x in (flags, stored, lanes)],
        [((ROWS, MID), f32), ((MID, ELEMENTS), bf16)],
        10**8,
        name="own",
    )
    (to_pair,) = call(
        functools.partial(corners_kernel, block_cols),
        [(vmem, x) for x in (flags, halo0, halo1, to_pair, hot)],
        [((ALL_ROWS, LANES), f32)],
        10**8,
        name="corners",
    )
    from_pair = swapped(to_pair, in_pair)
    tile = ((11 * NODES, LANES), f32)
    low, centre, high = call(
        functools.partial(middle_kernel, block_cols),
        [(vmem, x) for x in (flags, halo0, halo1, own, lanes, table, weight)],
        [tile, tile, tile],
        10**8,
        name="middle",
    )
    (from_next,) = call(
        functools.partial(far_kernel, block_cols),
        [(vmem, x) for x in (flags, far1, far0, from_next, low)],
        [((RIM_ROWS, LANES), f32)],
        10**11,
        name="far",
    )
    (stepped,) = call(
        functools.partial(steps_kernel, block_cols),
        [
            (vmem, x)
            for x in (
                flags, from_pair, from_next, low, centre, high, hot, table, weight, lanes
            )
        ],
        [(fields.shape, f32)],
        10**8,
        scratch=[
            pltpu.VMEM((EXT // LANES, 4 * NODES, LANES), f32),
            pltpu.VMEM(fields.shape, f32),
            pltpu.SemaphoreType.DMA((3,)),
        ],
        out_spec=hbm,
        name="steps",
    )
    return stepped


def solution(mesh):
    return jax.shard_map(
        on_device,
        mesh=mesh,
        in_specs=(
            P(None, None, None, ("face", "blk")),
            P(None, None, ("face", "blk")),
            P(None, None, ("face", "blk")),
            P(None, None, ("face", "blk")),
            P(None, None, ("face", "blk")),
            P(("face", "blk"), None),
            P(),
        ),
        out_specs=P(None, None, None, ("face", "blk")),
        check_vma=False,
    )
```

```python
import functools
import math

import jax
import jax.numpy as jnp
import ml_dtypes
import numpy as np
from jax import lax
from jax.experimental import pallas as pl
from jax.experimental.pallas import tpu as pltpu
from jax.sharding import PartitionSpec as P

BY = 16
GX = 16
GY = 16
NP = 8
NODES = NP * NP
ARRAYS = 7
ROWS = ARRAYS * NODES
MOVED = 6 * NODES
EDGE_ROWS = 4 * NP
ALL_ROWS = ROWS + EDGE_ROWS
HALF_ROWS = (MOVED + NODES // 2 + 2 * NP) // 2
RING = 4
RIM_ROWS = ROWS + 2 * EDGE_ROWS
CORNER_ROWS = (MOVED + NODES // 2 + 4 * NP) // 8
PITCH = GX + 2 * RING
MID = GY * PITCH
LANES = 128
EXT = MID + 2 * LANES
LEAD = LANES - RING * PITCH
ELEMENTS = GX * GY

time_step = 0.03
hyper_coeff = 0.0002

f32 = jnp.float32
bf16 = jnp.bfloat16
i32 = jnp.int32


def legendre_pair(location, degree):
    lower_value = 1.0
    upper_value = location
    for polynomial_order in range(2, degree + 1):
        lower_value, upper_value = (
            upper_value,
            (
                (2 * polynomial_order - 1) * location * upper_value
                - (polynomial_order - 1) * lower_value
            )
            / polynomial_order,
        )
    return (lower_value, upper_value)


def gll_tables(points):
    degree = points - 1
    locations = [-math.cos(math.pi * position / degree) for position in range(points)]
    for iteration in range(100):
        updated = []
        for location in locations:
            lower_value, upper_value = legendre_pair(location, degree)
            updated.append(
                location - (location * upper_value - lower_value) / ((degree + 1) * upper_value)
            )
        locations = updated
    locations[0] = -1.0
    locations[degree] = 1.0
    legendre_at = [legendre_pair(location, degree)[1] for location in locations]
    weights = [2.0 / (degree * (degree + 1) * value * value) for value in legendre_at]
    corner_value = degree * (degree + 1) / 4.0
    derivative = []
    for row_index in range(points):
        row_values = []
        for column_index in range(points):
            if row_index != column_index:
                row_values.append(
                    legendre_at[row_index]
                    / (legendre_at[column_index] * (locations[row_index] - locations[column_index]))
                )
            elif row_index == 0:
                row_values.append(-corner_value)
            elif row_index == degree:
                row_values.append(corner_value)
            else:
                row_values.append(0.0)
        derivative.append(row_values)
    return np.asarray(weights, np.float64), np.asarray(derivative, np.float64)


def in_three(matrix):
    high = matrix.astype(ml_dtypes.bfloat16)
    low = (matrix - high.astype(np.float64)).astype(ml_dtypes.bfloat16)
    return np.concatenate([high, high, low], 1)


def operator_table():
    weights, derivative = gll_tables(NP)
    eye = np.eye(NP)
    node_weight = np.outer(weights, weights).reshape(NODES, 1)
    along_x = node_weight * np.kron(derivative, eye)
    along_y = node_weight * np.kron(eye, derivative)
    second = derivative @ derivative
    both = node_weight * (np.kron(second, eye) + np.kron(eye, second))
    table = np.zeros((5 * NODES, 4 * NODES), ml_dtypes.bfloat16)
    table[:NODES, : 3 * NODES] = in_three(along_x)
    table[NODES : 2 * NODES, : 3 * NODES] = in_three(along_y)
    flux = [in_three(along_x), in_three(along_y)]
    for k, part in enumerate(flux):
        at = 2 * k * NODES
        table[2 * NODES : 3 * NODES, at : at + 2 * NODES] = part[:, : 2 * NODES]
        table[3 * NODES : 4 * NODES, at : at + NODES] = part[:, 2 * NODES :]
    table[4 * NODES :, : 3 * NODES] = in_three(both)
    table = table.astype(np.float32)
    spread = np.broadcast_to(node_weight, (NODES, LANES)).astype(np.float32)
    ends = np.r_[:NP, NODES - NP : NODES]
    edge_table = np.zeros((10 * NP, 4 * NODES), np.float32)
    for k in range(4):
        edge_table[2 * k * NP : 2 * (k + 1) * NP] = table[k * NODES + ends]
    edge_table[8 * NP :, :LANES] = spread[ends]
    return table, np.ascontiguousarray(spread), edge_table


def lane_tables():
    table = np.zeros((24, MID), np.int32)
    for lane in range(MID):
        row, col = divmod(lane, PITCH)
        x = col - RING
        own = 0 <= x < GX
        table[0:8, lane] = x * GY + row if own else -1
        if not own:
            table[8:16, lane] = row * RING + (col if x < 0 else x - GX)
        table[16:24, lane] = 0 if own else (1 if x < 0 else 2)
    ext = np.zeros((8, EXT), np.int32)
    outer = np.zeros((32, 2 * LANES), np.int32)
    for lane in range(EXT):
        row, col = divmod(lane - LEAD, PITCH)
        y = row - RING
        x = col - RING
        ext[0, lane] = x in (-RING, GX + RING - 1)
        ext[1, lane] = y == GY - 1
        ext[2, lane] = y == 0
        ext[3, lane] = 0 <= y < GY and 0 <= x < GX
        ext[4, lane] = y == -RING
        ext[5, lane] = y == GY + RING - 1
        if -RING - 1 <= y < 0 or GY <= y <= GY + RING:
            place = lane if y < 0 else lane - MID
            step = y + RING if y < 0 else y - GY
            near = step + 1 if y < 0 else step
            far = 0 <= step < RING
            if 0 <= x < GX:
                outer[0:8, place] = near * GX + x
                outer[8:16, place] = 1
                outer[24:32, place] = LANES + step * GX + x if far else -1
            else:
                across = x + RING if x < 0 else x - GX
                outer[0:8, place] = (RING + 1) * GX + near * RING + across
                outer[8:16, place] = 2 if x < 0 else 3
                outer[24:32, place] = LANES + RING * GX + step * RING + across if far else -1
            outer[16:24, place] = y > 0
    whole = np.zeros((64, EXT), np.int32)
    whole[0:24, :MID] = table
    whole[24:32] = ext
    whole[32:64, : 2 * LANES] = outer
    return whole


def dot(a, b):
    return jnp.dot(a, b, preferred_element_type=f32)


def picked(values, one_hot):
    high = values.astype(bf16)
    low = (values - high.astype(f32)).astype(bf16)
    both = dot(jnp.concatenate([high, low], 0), one_hot)
    return both[: values.shape[0]] + both[values.shape[0] :]


def as_one_hot(row_of_lane, depth):
    index = lax.broadcasted_iota(i32, (depth, row_of_lane.shape[1]), 0)
    return jnp.where(index == row_of_lane[0:1], 1.0, 0.0).astype(bf16)


def high_low_high(values):
    high = values.astype(bf16)
    low = (values - high.astype(f32)).astype(bf16)
    return [high, low, high]


def by_slot(halves, cell_of_lane):
    size = cell_of_lane.shape[1]
    halves = [jnp.broadcast_to(half, (8, LANES)) for half in halves]
    chosen = []
    for k in range(size // LANES):
        cell = cell_of_lane[:, k * LANES : (k + 1) * LANES]
        low, high = (jnp.take_along_axis(half, cell & (LANES - 1), axis=1) for half in halves)
        chosen.append(jnp.where(cell < 0, -1, jnp.where(cell < LANES, low, high)))
    return as_one_hot(jnp.concatenate(chosen, 1), ELEMENTS)


def stored_rows(fields_ref, others):
    fields = fields_ref[...].reshape(3 * NODES, ELEMENTS)
    others = [ref[...].reshape(NODES, ELEMENTS) for ref in others]
    return jnp.concatenate([fields[:NODES] - others[-1], fields[NODES:]] + others, 0)


def mass_tendency(table, p, u, v, area_depth, weighted_area, spin):
    slopes = dot(table[: 2 * NODES, : 3 * NODES], jnp.concatenate(high_low_high(p), 0))
    flux = high_low_high(area_depth * u)[:2] + high_low_high(area_depth * v)[:2]
    spread = dot(table[2 * NODES : 4 * NODES], jnp.concatenate(flux, 0))
    return [
        -(spread[:NODES] + spread[NODES:]),
        spin * v - weighted_area * slopes[:NODES],
        -spin * u - weighted_area * slopes[NODES:],
    ]


def edge_values(table_ref, weight_ref, p, u, v, area, depth, spin):
    root = jnp.sqrt(area)
    mass = jnp.concatenate([weight_ref[...]] * (area.shape[1] // LANES), 1) * area
    table = table_ref[...].astype(bf16)
    return mass_tendency(table, p, u, v, root * depth, root, mass * spin) + [mass]


def column_edges(table, weight, p, u, v, area, depth, spin):
    def ends(part):
        return jnp.concatenate([part[:NP], part[NODES - NP :]], 0)

    root = jnp.sqrt(area)
    area_depth = root * depth
    root, mass = ends(root), weight * ends(area)
    weighted_spin = mass * ends(spin)
    slopes = dot(table[: 4 * NP, : 3 * NODES], jnp.concatenate(high_low_high(p), 0))
    flux = high_low_high(area_depth * u)[:2] + high_low_high(area_depth * v)[:2]
    spread = dot(table[4 * NP :], jnp.concatenate(flux, 0))
    return [
        -(spread[: 2 * NP] + spread[2 * NP :]),
        weighted_spin * ends(v) - root * slopes[: 2 * NP],
        -weighted_spin * ends(u) - root * slopes[2 * NP :],
        mass,
    ]


def row_edges(sums):
    return tuple(sums[0, pl.ds(j, EDGE_ROWS, stride=NP)] for j in (NP - 1, 0))


def beside(left, right):
    return jnp.concatenate([left, right], 1)


def one_of_four(parts, index):
    out = parts[0]
    for k in range(1, 4):
        out = jnp.where(index == k, parts[k], out)
    return out


def folded(tide, kept, late, step):
    half = NODES // 2
    back = pltpu.roll(tide[half:], LANES - step, 1)
    onward = pltpu.roll(tide[half:], step, 1)
    return jnp.where(kept, tide[:half], jnp.where(late, back, onward))


def unfolded(rows, late, step):
    back = pltpu.roll(rows, LANES - step, 1)
    onward = pltpu.roll(rows, step, 1)
    return jnp.concatenate([rows, jnp.where(late, onward, back)], 0)


def strip_rows(parts, late, shift, rims):
    lane = lax.broadcasted_iota(i32, (1, LANES), 1)
    index = (lane >> shift) & 3
    kept = jnp.where(late, index // 2, 1 - index // 2) != 0
    tide = folded(parts[6], kept, late, 2 << shift)
    rim = one_of_four(rims, index)
    return jnp.concatenate(parts[:6] + [tide, rim, jnp.zeros_like(rim)], 0)


def placed_rows(whole, late, shift):
    half = NODES // 2
    tide = unfolded(whole[MOVED : MOVED + half], late, 2 << shift)
    rim = whole[MOVED + half : MOVED + half + NP]
    return jnp.concatenate([whole[:MOVED], tide] + spread_out(rim, late, shift), 0)


def spread_out(rim, late, shift):
    parts = []
    for k in range(4):
        first = pltpu.roll(rim, (LANES - (k << shift)) % LANES, 1) if k else rim
        last = pltpu.roll(rim, (3 - k) << shift, 1) if k < 3 else rim
        parts.append(jnp.where(late, first, last))
    return parts


def with_row_rim(whole, sums, top):
    north, south = row_edges(sums)
    rim = jnp.where(top, pltpu.roll(north, RING, 1), pltpu.roll(south, LANES - RING, 1))
    parts = [rim[k * NP : (k + 1) * NP] for k in range(4)]
    lane = lax.broadcasted_iota(i32, (1, LANES), 1)
    spots = []
    for k, part in enumerate(parts):
        first = pltpu.roll(part, k * RING, 1) if k else part
        last = pltpu.roll(part, (LANES - (3 - k) * RING) % LANES, 1) if k < 3 else part
        spots.append(jnp.where(top, first, last))
    rim = one_of_four(spots, (lane >> 2) & 3)
    return jnp.concatenate([whole[: MOVED + NODES // 2 + NP], rim], 0)


def in_eight(whole):
    whole = jnp.concatenate([whole, jnp.zeros((8 * CORNER_ROWS - whole.shape[0], LANES), f32)], 0)
    return [whole[k * CORNER_ROWS : (k + 1) * CORNER_ROWS] for k in range(8)]


def corner_of(whole, start, top):
    lane = lax.broadcasted_iota(i32, (1, LANES), 1)
    out = None
    for k, part in enumerate(in_eight(whole)):
        last = pltpu.roll(part, (LANES - start - 48 + 16 * k) % LANES, 1)
        first = pltpu.roll(part, (LANES - start + 16 * k) % LANES, 1)
        part = jnp.where(top != 0, last, first)
        out = part if k == 0 else jnp.where(lane >= 16 * k, part, out)
    return out


def both_corners(whole, odd):
    group = lax.broadcasted_iota(i32, (1, LANES), 1) >> 4
    other_group = (group + jnp.where(odd != 0, 7, 1)) & 7
    first, other = None, None
    for k, part in enumerate(in_eight(whole)):
        part = pltpu.roll(part, (LANES + 16 * k - 48 * odd) & (LANES - 1), 1)
        first = part if k == 0 else jnp.where(group == k, part, first)
        other = part if k == 0 else jnp.where(other_group == k, part, other)
    return first, other


def arrived_corners(far0, far1, block_cols, odd):
    lane = lax.broadcasted_iota(i32, (1, LANES), 1)
    corners = []
    for k in range(8):
        if block_cols == 1:
            part = jnp.where((lane >> 4) == k, far0, far1)
            part = pltpu.roll(part, (LANES + 64 + 16 * (1 - odd) - 16 * k) & (LANES - 1), 1)
        else:
            first = pltpu.roll(far0, (64 - 16 * k) % LANES, 1)
            other = pltpu.roll(far1, (80 - 16 * k) % LANES, 1)
            part = jnp.where((lane & 16) == 0, first, other)
        corners.append(part)
    return jnp.concatenate(corners, 0), ((lane >> 4) & 1) ^ (1 - odd if block_cols == 1 else 0)


def packed(whole):
    second = lax.broadcasted_iota(i32, (1, LANES), 1) >= 64
    top, bottom = whole[:HALF_ROWS], whole[HALF_ROWS:]
    return (
        jnp.where(second, pltpu.roll(bottom, 64, 1), top),
        jnp.where(second, bottom, pltpu.roll(top, 64, 1)),
    )


def unpacked(in0, in1):
    second = lax.broadcasted_iota(i32, (1, LANES), 1) >= 64
    top = jnp.where(second, pltpu.roll(in1, 64, 1), in0)
    bottom = jnp.where(second, in1, pltpu.roll(in0, 64, 1))
    return jnp.concatenate([top, bottom], 0)


def seam_flags(seam_ref, block_cols):
    size_y = seam_ref.shape[1]
    face = lax.axis_index("face")
    blk = lax.axis_index("blk")
    block_x = blk // BY

    def flipped(k):
        return jnp.where(lax.rem(seam_ref[k, 1] - seam_ref[k, 0] + size_y, size_y) != 1, 1, 0)

    first, second = flipped(0), flipped(1)
    east_flip = jnp.where(face == 0, first, second)
    west_flip = jnp.where(face == 0, second, first)
    if block_cols == 1:
        return 1 - east_flip, 0, east_flip, 1
    at_east = jnp.where(block_x == block_cols - 1, east_flip, 0)
    at_west = jnp.where(block_x == 0, west_flip, 0)
    return 1, at_east, 0, at_west


def slots_in(flags_ref):
    return flags_ref[4:5], flags_ref[5:6]


def flags_in(flags_ref, tiles=1):
    return [jnp.concatenate([flags_ref[k : k + 1]] * tiles, 1) for k in range(4)]


def mirrored_first(block_y):
    return (block_y >= BY // 8) & (block_y < BY - BY // 8)


def in_order(block_cols, first, second):
    if block_cols > 1:
        return first, second
    swap = mirrored_first(lax.rem(lax.axis_index("blk"), BY))
    return jnp.where(swap, second, first), jnp.where(swap, first, second)


def strips_kernel(block_cols, *refs):
    sources, (first_ref, then_ref, stored_ref, flags_ref) = refs[:8], refs[8:12]
    buffers, sems = refs[12:20], refs[20]
    copies = [
        pltpu.make_async_copy(source, buffer, sems.at[k])
        for k, (source, buffer) in enumerate(zip(sources, buffers))
    ]
    for copy in copies:
        copy.start()
    seam_ref, slot_ref, fields_ref, area_ref, depth_ref, spin_ref, tide_ref = buffers[:7]
    table_ref = buffers[7]
    for copy in copies[:2]:
        copy.wait()
    east0, flip0, east1, flip1 = flags = seam_flags(seam_ref, block_cols)
    index = lax.broadcasted_iota(i32, (8, LANES), 0)
    flags_ref[...] = sum(jnp.where(index == k, flag, 0) for k, flag in enumerate(flags))
    slots = slot_ref[:, :LANES], slot_ref[:, LANES:]
    flags_ref[4:5], flags_ref[5:6] = slots
    lane = lax.broadcasted_iota(i32, (8, 2 * LANES), 1)
    second = (lane & 64) != 0
    place = lane & 63
    row = place >> 2
    row = jnp.where(jnp.where(second, flip1, flip0) != 0, GY - 1 - row, row)
    east = jnp.where(second, east1, east0) != 0
    col = jnp.where(east, GX - RING, 0) + (place & 3)
    col = jnp.where(lane >= LANES, jnp.where(east, GX - RING - 1, RING), col)
    one_hot = by_slot(slots, col * GY + row)
    for copy in copies[2:7]:
        copy.wait()
    stored = stored_rows(fields_ref, (area_ref, depth_ref, spin_ref, tide_ref))
    both = picked(stored, one_hot)

    lane = lax.broadcasted_iota(i32, (1, LANES), 1)
    second = lane >= 64
    flip = jnp.where(second, flip1, flip0) != 0
    sign = jnp.where(flip, -1.0, 1.0)
    node = lax.broadcasted_iota(i32, (1, NP, 1), 1)

    def turned(values):
        shaped = values.reshape(-1, NP, LANES)
        shaped = pltpu.roll(shaped, 4, 1)
        shaped = jnp.where((node & 2) == 0, pltpu.roll(shaped, 6, 1), pltpu.roll(shaped, 2, 1))
        shaped = jnp.where((node & 1) == 0, pltpu.roll(shaped, 7, 1), pltpu.roll(shaped, 1, 1))
        return shaped.reshape(values.shape)

    strip, ring = (
        [part[k * NODES : (k + 1) * NODES] for k in range(ARRAYS)]
        for part in (both[:, :LANES], both[:, LANES:])
    )
    for copy in copies[7:]:
        copy.wait()
    table, weight = table_ref[: 8 * NP].astype(bf16), table_ref[8 * NP :, :LANES]
    edges = column_edges(table, weight, *ring[:6])
    east = jnp.where(second, east1, east0) != 0
    ends = [jnp.where(east, part[NP:], part[:NP]) for part in edges]
    ends[2] = ends[2] * sign
    strip[2] = strip[2] * sign
    strip[5] = strip[5] * sign
    strips = []
    for part, flip in zip(packed(strip_rows(strip, east, 0, ends)), (flip0, flip1)):
        if isinstance(flip, int):
            strips.append(turned(part) if flip else part)
        else:
            strips.append(jnp.where(flip != 0, turned(part), part))
    first_ref[...], then_ref[...] = in_order(block_cols, *strips)
    stored_ref[...] = stored


def rows_kernel(
    block_cols, flags_ref, stored_ref, first_ref, then_ref, table_ref, weight_ref,
    next_ref, far0_ref, far1_ref, pair_ref, sums,
):
    east0, flip0, east1, flip1 = flags_in(flags_ref)
    odd = lax.axis_index("blk") & 1
    lane = lax.broadcasted_iota(i32, (8, 2 * LANES), 1)
    row = jnp.where(odd != 0, GY - RING, 0) + ((lane & 63) >> 4)
    row = jnp.where((lane & 64) != 0, jnp.where(odd != 0, GY - RING - 1, RING), row)
    five = jnp.where(odd != 0, 0, GY - RING - 1) + jnp.minimum((lane & (LANES - 1)) >> 4, RING)
    row = jnp.where(lane >= LANES, five, row)
    both = picked(stored_ref[...], by_slot(slots_in(flags_ref), (lane & 15) * GY + row))
    pair_ref[...] = both[:, LANES:]
    rows = [both[k * NODES : (k + 1) * NODES, :LANES] for k in range(ARRAYS)]
    whole = unpacked(*in_order(block_cols, first_ref[...], then_ref[...]))
    strip = [whole[k * NODES : (k + 1) * NODES] for k in range(6)]
    edges = edge_values(table_ref, weight_ref, *map(beside, strip, rows[:6]))
    sums[0] = jnp.concatenate([part[:, :LANES] for part in edges], 0)
    lane = lax.broadcasted_iota(i32, (1, LANES), 1)
    top0, top1 = odd ^ flip0, odd ^ flip1
    whole = with_row_rim(whole, sums, jnp.where(lane >= 64, top1, top0) != 0)
    if block_cols == 1:
        far0_ref[...], far1_ref[...] = both_corners(whole, odd)
    else:
        far0_ref[...] = corner_of(whole, 0, top0)
        far1_ref[...] = corner_of(whole, 64, top1)
    sums[0] = jnp.concatenate([part[:, LANES:] for part in edges], 0)
    up = jnp.broadcast_to(odd != 0, (1, LANES))
    rim = pltpu.roll(jnp.where(up, *row_edges(sums)), 64, 1)
    rim = [rim[k * NP : (k + 1) * NP] for k in range(4)]
    whole = strip_rows(rows, up, 4, rim)
    top, bottom = whole[:HALF_ROWS], whole[HALF_ROWS:]
    next_ref[...] = jnp.where(lane >= 64, pltpu.roll(bottom, 64, 1), top)


def corners_kernel(block_cols, flags_ref, first_ref, then_ref, pair_ref, _, out_ref):
    east0, flip0, east1, flip1 = flags_in(flags_ref)
    in0, in1 = in_order(block_cols, first_ref[...], then_ref[...])
    top = 1 - (lax.axis_index("blk") & 1)
    lane = lax.broadcasted_iota(i32, (1, LANES), 1)
    halves = []
    for start in (0, 64):
        at0 = jnp.where(top != 0, 36, 80)
        at1 = jnp.where(top != 0, 56, 100)
        first = pltpu.roll(in0, (at0 - start) & (LANES - 1), 1)
        other = pltpu.roll(in1, (at1 - start) & (LANES - 1), 1)
        halves.append(jnp.where(lane < 100, first, other))
    late = jnp.where(lane < 100, east0, east1) == 0
    whole = placed_rows(jnp.concatenate(halves, 0), late, 0)
    out_ref[:ROWS] = jnp.where(lane < 80, pair_ref[...], whole[:ROWS])
    out_ref[ROWS:] = whole[ROWS:]


def own_kernel(flags_ref, stored_ref, lanes_ref, own_ref, hot_ref):
    one_hot = by_slot(slots_in(flags_ref), lanes_ref[0:8, :MID])
    own_ref[...] = picked(stored_ref[...], one_hot)
    hot_ref[...] = one_hot.astype(f32).T.astype(bf16)


def first_sums(table, weight, parts, rims, at_rim):
    p, u, v, area, depth, spin, tide = parts
    size = area.shape[1]
    root = jnp.sqrt(area)
    mass = jnp.concatenate([weight] * (size // LANES), 1) * area
    used = [p, u, v, root * depth, root, mass * spin, tide]
    for part, rim in zip(mass_tendency(table, p, u, v, *used[3:6]) + [mass], rims):
        west, east = part[:NP], part[NODES - NP :]
        at_east = jnp.where(at_rim, rim, pltpu.roll(west, size - 1, 1))
        at_west = jnp.where(at_rim, rim, pltpu.roll(east, 1, 1))
        used.append(
            jnp.concatenate([west + at_west, part[NP : NODES - NP], east + at_east], 0)
        )
    return used


def middle_kernel(
    block_cols, flags_ref, first_ref, then_ref, own_ref, lanes_ref, table_ref, weight_ref,
    low_ref, centre_ref, high_ref,
):
    east0, flip0, east1, flip1 = flags_in(flags_ref)
    second = lax.broadcasted_iota(i32, (1, LANES), 1) >= 64
    late = jnp.where(second, east1, east0) == 0
    whole = unpacked(*in_order(block_cols, first_ref[...], then_ref[...]))
    whole = placed_rows(whole, late, 0)
    side = lanes_ref[16:24, :MID]
    east = flags_in(flags_ref, MID // LANES)[0]
    first_at = jnp.where(side == 2, 64 * (1 - east), 64 * east)
    place = jnp.where(side == 0, -1, lanes_ref[8:16, :MID] + first_at)
    placed = picked(whole, as_one_hot(place, LANES))
    parts = [
        placed[k * NODES : (k + 1) * NODES] + own_ref[k * NODES : (k + 1) * NODES]
        for k in range(ARRAYS)
    ]
    rims = [placed[ROWS + c * NP : ROWS + (c + 1) * NP] for c in range(4)]
    at_rim = lanes_ref[24:25, LANES : LANES + MID] != 0
    used = first_sums(table_ref[...].astype(bf16), weight_ref[...], parts, rims, at_rim)
    for k, ref in enumerate((low_ref, centre_ref, high_ref)):
        for n, part in enumerate(used):
            ref[n * NODES : (n + 1) * NODES] = part[:, k * LANES : (k + 1) * LANES]


def far_kernel(block_cols, flags_ref, far1_ref, far0_ref, next_ref, _, out_ref):
    east0, flip0, east1, flip1 = flags_in(flags_ref)
    odd = lax.axis_index("blk") & 1
    lane = lax.broadcasted_iota(i32, (1, LANES), 1)
    below = jnp.broadcast_to(odd == 0, (1, LANES))
    strip = jnp.concatenate([next_ref[...], pltpu.roll(next_ref[...], 64, 1)], 0)
    strip = placed_rows(strip, below, 4)
    corners, strip_of = arrived_corners(far0_ref[...], far1_ref[...], block_cols, odd)
    late = jnp.where(strip_of != 0, east1, east0) == 0
    rim = MOVED + NODES // 2 + NP
    rim = jnp.concatenate(spread_out(corners[rim : rim + NP], below, 2), 0)
    corners = placed_rows(corners, late, 0)
    own = lane < 64
    out_ref[:ROWS] = jnp.where(own, strip[:ROWS], corners[:ROWS])
    out_ref[ROWS:ALL_ROWS] = corners[ROWS:]
    out_ref[ALL_ROWS:] = jnp.where(own, strip[ROWS:], rim)


def steps_kernel(
    block_cols, flags_ref, pair_ref, next_ref, low_ref, centre_ref,
    high_ref, hot_ref, table_ref, weight_ref, lanes_ref, out_ref, sums,
):
    east0, flip0, east1, flip1 = flags_in(flags_ref)
    odd = lax.axis_index("blk") & 1
    block_y = lax.rem(lax.axis_index("blk"), BY)

    lane = lax.broadcasted_iota(i32, (1, LANES), 1)
    pair = jnp.concatenate([pair_ref[...], jnp.zeros((EDGE_ROWS, LANES), f32)], 0)
    around = beside(pair, next_ref[...])
    outer_at = [lanes_ref[32 + 8 * k : 40 + 8 * k, : 2 * LANES] for k in range(4)]
    kind = outer_at[1]
    from_pair = jnp.where(outer_at[2] != 0, 1 - odd, odd) != 0
    east = flags_in(flags_ref, 2)[0]
    strip_at = jnp.where(kind == 3, 1 - east, east)
    far_at = strip_at ^ (1 - odd) if block_cols == 1 else strip_at
    strip_at, far_at = (jnp.where(kind > 1, at, 0) for at in (strip_at, far_at))
    place = jnp.where(
        from_pair,
        outer_at[0] + (RING + 1) * RING * strip_at,
        jnp.where(outer_at[3] < 0, -1, outer_at[3] + RING * RING * far_at),
    )
    outer = picked(around, as_one_hot(jnp.where(kind == 0, -1, place), 2 * LANES))
    table = table_ref[...].astype(bf16)
    tiles = (None, low_ref, centre_ref, high_ref, None)
    count = len(tiles)
    masks = [lanes_ref[24:32, k * LANES : (k + 1) * LANES] for k in range(count)]
    closed_above = jnp.where(block_y == BY - 1, masks[-2][1:2], 0) != 0
    closed_below = jnp.where(block_y == 0, masks[1][2:3], 0) != 0
    first_row = jnp.where(odd == 0, masks[0][4:5], 0) != 0
    last_row = jnp.where(odd != 0, masks[-1][5:6], 0) != 0
    outer_used = first_sums(
        table,
        weight_ref[...],
        [outer[k * NODES : (k + 1) * NODES] for k in range(ARRAYS)],
        [outer[ROWS + c * NP : ROWS + (c + 1) * NP] for c in range(4)],
        beside(masks[0][0:1], masks[-1][0:1]) != 0,
    )

    def shifted(parts, by, ring):
        turned = [pltpu.roll(part, -by % LANES, 1) for part in parts]
        size = len(parts)
        step = 1 if by > 0 else -1
        others = [(k + step) % size if ring else min(max(k + step, 0), size - 1) for k in range(size)]
        from_other = lane >= LANES - by if by > 0 else lane < -by
        return [jnp.where(from_other, turned[others[k]], turned[k]) for k in range(size)]

    def put_x_sums(groups, components):
        slots = [k for group in groups for k in group]
        ring = len(slots) < count
        per_tile = [
            [part[:, n * LANES : (n + 1) * LANES] for part in parts]
            for group, parts in zip(groups, components)
            for n in range(len(group))
        ]
        for c in range(3):
            parts = [tile[c] for tile in per_tile]
            west = [part[:NP] for part in parts]
            east = [part[NODES - NP :] for part in parts]
            at_east, at_west = shifted(west, 1, ring), shifted(east, -1, ring)
            for n, k in enumerate(slots):
                sums[k, c * NODES : c * NODES + NP] = west[n] + at_west[n]
                sums[k, c * NODES + NP : (c + 1) * NODES - NP] = parts[n][NP : NODES - NP]
                sums[k, (c + 1) * NODES - NP : (c + 1) * NODES] = east[n] + at_east[n]

    def edge_y(components, slots, rows=None):
        ring = len(slots) < count
        south_at = pl.ds(0, components * NP, stride=NP)
        north_at = pl.ds(NP - 1, components * NP, stride=NP)
        south = [sums[k, south_at] for k in slots]
        north = [sums[k, north_at] for k in slots]
        at_north, at_south = shifted(south, PITCH, ring), shifted(north, -PITCH, ring)
        for n, k in enumerate(slots):
            if k == count - 2:
                at_north[n] = jnp.where(closed_above, 0.0, at_north[n])
            if k == 1:
                at_south[n] = jnp.where(closed_below, 0.0, at_south[n])
        if rows is not None:
            at_south[0] = jnp.where(first_row, rows[0], at_south[0])
            at_north[-1] = jnp.where(last_row, rows[1], at_north[-1])
        for n, k in enumerate(slots):
            sums[k, south_at] = south[n] + at_south[n]
            sums[k, north_at] = north[n] + at_north[n]

    node = lax.broadcasted_iota(i32, (1, NP, 1), 1)
    rows = []
    for rim in (outer[ALL_ROWS:, :LANES], outer[ALL_ROWS:, LANES:]):
        east = pltpu.roll(rim, LANES - 1, 1).reshape(4, NP, LANES)
        west = pltpu.roll(rim, 1, 1).reshape(4, NP, LANES)
        rim = (
            rim.reshape(4, NP, LANES)
            + jnp.where(node == NP - 1, pltpu.roll(east, NP - 1, 1), 0.0)
            + jnp.where(node == 0, pltpu.roll(west, 1, 1), 0.0)
        )
        rows.append(rim.reshape(EDGE_ROWS, LANES))

    every = tuple(range(count))
    groups = (every[0:2], every[2:4], every[4:])

    def tile_part(k, n):
        if tiles[k] is None:
            return outer_used[n][:, :LANES] if k == 0 else outer_used[n][:, LANES:]
        return tiles[k][n * NODES : (n + 1) * NODES]

    def part_of(group, n):
        return jnp.concatenate([tile_part(k, n) for k in group], 1)

    def summed(group, c):
        return jnp.concatenate([sums[k, c * NODES : (c + 1) * NODES] for k in group], 1)

    def average(group, per_mass):
        return [summed(group, c) * per_mass for c in range(3)]

    def laplace(s):
        return [
            dot(table[4 * NODES :, : 3 * NODES], jnp.concatenate(high_low_high(part), 0))
            for part in s
        ]

    start = [[part_of(group, n) for n in range(3)] for group in groups]
    fixed = [[part_of(group, n) for n in range(3, 6)] for group in groups]
    for k in every:
        for c in range(4):
            sums[k, c * NODES : (c + 1) * NODES] = tile_part(k, 7 + c)
    edge_y(4, every, rows)
    per_mass = [1.0 / summed(group, 3) for group in groups]
    one = []
    for n, group in enumerate(groups):
        change = average(group, per_mass[n])
        one.append([s + time_step * c for s, c in zip(start[n], change)])
    put_x_sums(groups, [mass_tendency(table, *s, *f) for s, f in zip(one, fixed)])
    edge_y(3, every)
    two = []
    for n, group in enumerate(groups):
        change = average(group, per_mass[n])
        two.append(
            [0.75 * s + 0.25 * (o + time_step * c) for s, o, c in zip(start[n], one[n], change)]
        )
    put_x_sums(groups, [mass_tendency(table, *s, *f) for s, f in zip(two, fixed)])
    edge_y(3, every)

    def regrouped(per_group):
        (outer_low, high_above) = per_group[0], per_group[1]
        below, low = outer_low[:, :LANES], outer_low[:, LANES:]
        centre, high = high_above[:, :LANES], high_above[:, LANES:]
        near = jnp.where(lane < LANES // 2, per_group[2], below)
        return [beside(low, centre), beside(high, near)]

    def of_groups(values):
        return [list(parts) for parts in zip(*(regrouped(part) for part in zip(*values)))]

    for c in range(3):
        rows_at = slice(c * NODES, (c + 1) * NODES)
        sums[count - 1, rows_at] = jnp.where(
            lane < LANES // 2, sums[count - 1, rows_at], sums[0, rows_at]
        )
    slots = every[1:]
    groups = (slots[0:2], slots[2:4])
    start, two = of_groups(start), of_groups(two)
    tide = regrouped([part_of(every[0:2], 6), part_of(every[2:4], 6), part_of(every[4:], 6)])
    per_mass = regrouped(per_mass)
    three = []
    for n, group in enumerate(groups):
        change = average(group, per_mass[n])
        now = [
            s / 3.0 + 2.0 / 3.0 * (o + time_step * c)
            for s, o, c in zip(start[n], two[n], change)
        ]
        now[0] = now[0] + tide[n]
        three.append(now)
    put_x_sums(groups, [laplace(s) for s in three])
    edge_y(3, slots)
    change = [average(group, per_mass[n]) for n, group in enumerate(groups)]
    put_x_sums(groups, [laplace(s) for s in change])
    edge_y(3, slots)
    stepped = []
    for n, group in enumerate(groups):
        change = average(group, per_mass[n])
        now = [s - time_step * hyper_coeff * b for s, b in zip(three[n], change)]
        stepped.append(jnp.concatenate(now, 0))
    stepped = jnp.concatenate(stepped, 1)[:, :MID]
    own = lanes_ref[27:28, LANES : LANES + MID] != 0
    stored = picked(jnp.where(own, stepped, 0.0), hot_ref[...])
    out_ref[...] = stored.reshape(out_ref.shape)


def on_device(fields, jacobian, water_depth, coriolis, tide_height, slot_of, seam_rows):
    block_cols = lax.axis_size("blk") // BY
    table, weight, edge_table, lanes = map(jnp.asarray, (*operator_table(), lane_tables()))
    vmem = pl.BlockSpec(memory_space=pltpu.VMEM)
    hbm = pl.BlockSpec(memory_space=pltpu.HBM)
    params = pltpu.CompilerParams(vmem_limit_bytes=48 * 2**20)
    held = (fields, jacobian, water_depth, coriolis, tide_height)

    def call(kernel, ins, outs, cost, scratch=(), name=None):
        return pl.pallas_call(
            kernel,
            out_shape=[jax.ShapeDtypeStruct(*out) for out in outs],
            in_specs=[spec for spec, value in ins],
            out_specs=[vmem] * len(outs),
            scratch_shapes=list(scratch),
            compiler_params=params,
            cost_estimate=pl.CostEstimate(
                flops=cost, bytes_accessed=2 * 2**20, transcendentals=0
            ),
            name=name,
        )(
            *[
                pltpu.with_memory_space_constraint(value, pltpu.HBM) if spec is hbm else value
                for spec, value in ins
            ]
        )

    strip = ((HALF_ROWS, LANES), f32)
    def room(values, spaces=None):
        spaces = spaces or [pltpu.VMEM] * len(values)
        buffers = [space(x.shape, x.dtype) for space, x in zip(spaces, values)]
        return buffers + [pltpu.SemaphoreType.DMA((len(values),))]

    needed = (seam_rows, slot_of, *held, edge_table)
    corner = ((CORNER_ROWS, LANES), f32)
    scratch = [pltpu.VMEM((1, 4 * NODES, LANES), f32)]
    first, then, stored, flags = call(
        functools.partial(strips_kernel, block_cols),
        [(hbm, x) for x in needed],
        [strip, strip, ((ROWS, ELEMENTS), f32), ((8, LANES), i32)],
        10**8,
        scratch=room(needed, [pltpu.SMEM] + [pltpu.VMEM] * (len(needed) - 1)),
        name="strips",
    )
    to_next, far0, far1, to_pair = call(
        functools.partial(rows_kernel, block_cols),
        [(vmem, x) for x in (flags, stored, first, then, table, weight)],
        [strip, corner, corner, ((ROWS, LANES), f32)],
        10**8,
        scratch=scratch,
        name="rows",
    )
    span = block_cols * BY
    both = ("face", "blk")
    places = [(f, x, y) for f in range(2) for x in range(block_cols) for y in range(BY)]

    def rank(face, block_x, block_y):
        return face * span + block_x * BY + block_y

    def same(y):
        return y

    def in_pair(y):
        return y ^ 1

    def next_pair(y):
        other = y + 1 if y % 2 else y - 1
        return other if 0 <= other < BY else y

    def swapped(value, partner):
        pairs = [
            (rank(f, x, y), rank(f if partner(y) != y else 1 - f, x, partner(y)))
            for f, x, y in places
        ]
        return lax.ppermute(value, both, pairs)

    def across(value0, value1, partner):
        last = block_cols - 1

        def aligned(y):
            return partner is same or partner(y) != y

        straight = {
            (f, x, y): (f, x + 1, partner(y)) if x < last else (1 - f, 0, partner(y))
            for f, x, y in places
        }
        turned = {
            (f, last, y): (1 - f, 0, BY - 1 - partner(y) if aligned(y) else y)
            for f in range(2)
            for y in range(BY)
        }

        def eastward(value, pairs):
            return lax.ppermute(value, both, [(rank(*a), rank(*b)) for a, b in pairs.items()])

        def westward(value, pairs):
            return lax.ppermute(value, both, [(rank(*b), rank(*a)) for a, b in pairs.items()])

        if block_cols == 1:
            return eastward(value0, straight), eastward(value1, turned)
        flipped = (seam_rows[:, 1] - seam_rows[:, 0]) % seam_rows.shape[1] != 1
        face = lax.axis_index("face")
        block_x = lax.axis_index("blk") // BY
        return (
            jnp.where(
                (block_x == last) & flipped[face],
                westward(value1, turned),
                westward(value1, straight),
            ),
            jnp.where(
                (block_x == 0) & flipped[1 - face],
                eastward(value0, turned),
                eastward(value0, straight),
            ),
        )

    if block_cols == 1:
        halos = []
        for value, mirrored in ((first, mirrored_first), (then, lambda y: not mirrored_first(y))):
            pairs = [
                (rank(f, x, y), rank(1 - f, x, BY - 1 - y if mirrored(y) else y))
                for f, x, y in places
            ]
            halos.append(lax.ppermute(value, both, pairs))
        halo0, halo1 = halos
    else:
        halo0, halo1 = across(first, then, same)
    far0, far1 = across(far0, far1, next_pair)
    from_next = swapped(to_next, next_pair)
    own, hot = call(
        own_kernel,
        [(vmem, x) for x in (flags, stored, lanes)],
        [((ROWS, MID), f32), ((MID, ELEMENTS), bf16)],
        10**8,
        name="own",
    )
    (to_pair,) = call(
        functools.partial(corners_kernel, block_cols),
        [(vmem, x) for x in (flags, halo0, halo1, to_pair, hot)],
        [((ALL_ROWS, LANES), f32)],
        10**8,
        name="corners",
    )
    from_pair = swapped(to_pair, in_pair)
    tile = ((11 * NODES, LANES), f32)
    low, centre, high = call(
        functools.partial(middle_kernel, block_cols),
        [(vmem, x) for x in (flags, halo0, halo1, own, lanes, table, weight)],
        [tile, tile, tile],
        10**8,
        name="middle",
    )
    (from_next,) = call(
        functools.partial(far_kernel, block_cols),
        [(vmem, x) for x in (flags, far1, far0, from_next, low)],
        [((RIM_ROWS, LANES), f32)],
        10**11,
        name="far",
    )
    (stepped,) = call(
        functools.partial(steps_kernel, block_cols),
        [
            (vmem, x)
            for x in (
                flags, from_pair, from_next, low, centre, high, hot, table, weight, lanes
            )
        ],
        [(fields.shape, f32)],
        10**8,
        scratch=[pltpu.VMEM((EXT // LANES, 4 * NODES, LANES), f32)],
        name="steps",
    )
    return stepped


def solution(mesh):
    return jax.shard_map(
        on_device,
        mesh=mesh,
        in_specs=(
            P(None, None, None, ("face", "blk")),
            P(None, None, ("face", "blk")),
            P(None, None, ("face", "blk")),
            P(None, None, ("face", "blk")),
            P(None, None, ("face", "blk")),
            P(("face", "blk"), None),
            P(),
        ),
        out_specs=P(None, None, None, ("face", "blk")),
        check_vma=False,
    )
```

```python
import functools
import math

import jax
import jax.numpy as jnp
import ml_dtypes
import numpy as np
from jax import lax
from jax.experimental import pallas as pl
from jax.experimental.pallas import tpu as pltpu
from jax.sharding import PartitionSpec as P

BY = 16
GX = 16
GY = 16
NP = 8
NODES = NP * NP
ARRAYS = 7
ROWS = ARRAYS * NODES
MOVED = 6 * NODES
EDGE_ROWS = 4 * NP
ALL_ROWS = ROWS + EDGE_ROWS
HALF_ROWS = (MOVED + NODES // 2 + 2 * NP) // 2
RING = 4
RIM_ROWS = ROWS + 2 * EDGE_ROWS
CORNER_ROWS = (MOVED + NODES // 2 + 4 * NP) // 8
PITCH = GX + 2 * RING
MID = GY * PITCH
LANES = 128
EXT = MID + 2 * LANES
LEAD = LANES - RING * PITCH
ELEMENTS = GX * GY

time_step = 0.03
hyper_coeff = 0.0002

f32 = jnp.float32
bf16 = jnp.bfloat16
i32 = jnp.int32


def legendre_pair(location, degree):
    lower_value = 1.0
    upper_value = location
    for polynomial_order in range(2, degree + 1):
        lower_value, upper_value = (
            upper_value,
            (
                (2 * polynomial_order - 1) * location * upper_value
                - (polynomial_order - 1) * lower_value
            )
            / polynomial_order,
        )
    return (lower_value, upper_value)


def gll_tables(points):
    degree = points - 1
    locations = [-math.cos(math.pi * position / degree) for position in range(points)]
    for iteration in range(100):
        updated = []
        for location in locations:
            lower_value, upper_value = legendre_pair(location, degree)
            updated.append(
                location - (location * upper_value - lower_value) / ((degree + 1) * upper_value)
            )
        locations = updated
    locations[0] = -1.0
    locations[degree] = 1.0
    legendre_at = [legendre_pair(location, degree)[1] for location in locations]
    weights = [2.0 / (degree * (degree + 1) * value * value) for value in legendre_at]
    corner_value = degree * (degree + 1) / 4.0
    derivative = []
    for row_index in range(points):
        row_values = []
        for column_index in range(points):
            if row_index != column_index:
                row_values.append(
                    legendre_at[row_index]
                    / (legendre_at[column_index] * (locations[row_index] - locations[column_index]))
                )
            elif row_index == 0:
                row_values.append(-corner_value)
            elif row_index == degree:
                row_values.append(corner_value)
            else:
                row_values.append(0.0)
        derivative.append(row_values)
    return np.asarray(weights, np.float64), np.asarray(derivative, np.float64)


def in_three(matrix):
    high = matrix.astype(ml_dtypes.bfloat16)
    low = (matrix - high.astype(np.float64)).astype(ml_dtypes.bfloat16)
    return np.concatenate([high, high, low], 1)


def operator_table():
    weights, derivative = gll_tables(NP)
    eye = np.eye(NP)
    node_weight = np.outer(weights, weights).reshape(NODES, 1)
    along_x = node_weight * np.kron(derivative, eye)
    along_y = node_weight * np.kron(eye, derivative)
    second = derivative @ derivative
    both = node_weight * (np.kron(second, eye) + np.kron(eye, second))
    table = np.zeros((5 * NODES, 4 * NODES), ml_dtypes.bfloat16)
    table[:NODES, : 3 * NODES] = in_three(along_x)
    table[NODES : 2 * NODES, : 3 * NODES] = in_three(along_y)
    flux = [in_three(along_x), in_three(along_y)]
    for k, part in enumerate(flux):
        at = 2 * k * NODES
        table[2 * NODES : 3 * NODES, at : at + 2 * NODES] = part[:, : 2 * NODES]
        table[3 * NODES : 4 * NODES, at : at + NODES] = part[:, 2 * NODES :]
    table[4 * NODES :, : 3 * NODES] = in_three(both)
    table = table.astype(np.float32)
    spread = np.broadcast_to(node_weight, (NODES, LANES)).astype(np.float32)
    ends = np.r_[:NP, NODES - NP : NODES]
    edge_table = np.zeros((10 * NP, 4 * NODES), np.float32)
    for k in range(4):
        edge_table[2 * k * NP : 2 * (k + 1) * NP] = table[k * NODES + ends]
    edge_table[8 * NP :, :LANES] = spread[ends]
    return table, np.ascontiguousarray(spread), edge_table


def lane_tables():
    table = np.zeros((24, MID), np.int32)
    for lane in range(MID):
        row, col = divmod(lane, PITCH)
        x = col - RING
        own = 0 <= x < GX
        table[0:8, lane] = x * GY + row if own else -1
        if not own:
            table[8:16, lane] = row * RING + (col if x < 0 else x - GX)
        table[16:24, lane] = 0 if own else (1 if x < 0 else 2)
    ext = np.zeros((8, EXT), np.int32)
    outer = np.zeros((32, 2 * LANES), np.int32)
    for lane in range(EXT):
        row, col = divmod(lane - LEAD, PITCH)
        y = row - RING
        x = col - RING
        ext[0, lane] = x in (-RING, GX + RING - 1)
        ext[1, lane] = y == GY - 1
        ext[2, lane] = y == 0
        ext[3, lane] = 0 <= y < GY and 0 <= x < GX
        ext[4, lane] = y == -RING
        ext[5, lane] = y == GY + RING - 1
        if -RING - 1 <= y < 0 or GY <= y <= GY + RING:
            place = lane if y < 0 else lane - MID
            step = y + RING if y < 0 else y - GY
            near = step + 1 if y < 0 else step
            far = 0 <= step < RING
            if 0 <= x < GX:
                outer[0:8, place] = near * GX + x
                outer[8:16, place] = 1
                outer[24:32, place] = LANES + step * GX + x if far else -1
            else:
                across = x + RING if x < 0 else x - GX
                outer[0:8, place] = (RING + 1) * GX + near * RING + across
                outer[8:16, place] = 2 if x < 0 else 3
                outer[24:32, place] = LANES + RING * GX + step * RING + across if far else -1
            outer[16:24, place] = y > 0
    whole = np.zeros((64, EXT), np.int32)
    whole[0:24, :MID] = table
    whole[24:32] = ext
    whole[32:64, : 2 * LANES] = outer
    return whole


def dot(a, b):
    return jnp.dot(a, b, preferred_element_type=f32)


def picked(values, one_hot):
    high = values.astype(bf16)
    low = (values - high.astype(f32)).astype(bf16)
    both = dot(jnp.concatenate([high, low], 0), one_hot)
    return both[: values.shape[0]] + both[values.shape[0] :]


def as_one_hot(row_of_lane, depth):
    index = lax.broadcasted_iota(i32, (depth, row_of_lane.shape[1]), 0)
    return jnp.where(index == row_of_lane[0:1], 1.0, 0.0).astype(bf16)


def high_low_high(values):
    high = values.astype(bf16)
    low = (values - high.astype(f32)).astype(bf16)
    return [high, low, high]


def by_slot(halves, cell_of_lane):
    size = cell_of_lane.shape[1]
    halves = [jnp.broadcast_to(half, (8, LANES)) for half in halves]
    chosen = []
    for k in range(size // LANES):
        cell = cell_of_lane[:, k * LANES : (k + 1) * LANES]
        low, high = (jnp.take_along_axis(half, cell & (LANES - 1), axis=1) for half in halves)
        chosen.append(jnp.where(cell < 0, -1, jnp.where(cell < LANES, low, high)))
    return as_one_hot(jnp.concatenate(chosen, 1), ELEMENTS)


def stored_rows(fields_ref, others):
    fields = fields_ref[...].reshape(3 * NODES, ELEMENTS)
    others = [ref[...].reshape(NODES, ELEMENTS) for ref in others]
    return jnp.concatenate([fields[:NODES] - others[-1], fields[NODES:]] + others, 0)


def mass_tendency(table, p, u, v, area_depth, weighted_area, spin):
    slopes = dot(table[: 2 * NODES, : 3 * NODES], jnp.concatenate(high_low_high(p), 0))
    flux = high_low_high(area_depth * u)[:2] + high_low_high(area_depth * v)[:2]
    spread = dot(table[2 * NODES : 4 * NODES], jnp.concatenate(flux, 0))
    return [
        -(spread[:NODES] + spread[NODES:]),
        spin * v - weighted_area * slopes[:NODES],
        -spin * u - weighted_area * slopes[NODES:],
    ]


def edge_values(table_ref, weight_ref, p, u, v, area, depth, spin):
    root = jnp.sqrt(area)
    mass = jnp.concatenate([weight_ref[...]] * (area.shape[1] // LANES), 1) * area
    table = table_ref[...].astype(bf16)
    return mass_tendency(table, p, u, v, root * depth, root, mass * spin) + [mass]


def column_edges(table, weight, p, u, v, area, depth, spin):
    def ends(part):
        return jnp.concatenate([part[:NP], part[NODES - NP :]], 0)

    root = jnp.sqrt(area)
    area_depth = root * depth
    root, mass = ends(root), weight * ends(area)
    weighted_spin = mass * ends(spin)
    slopes = dot(table[: 4 * NP, : 3 * NODES], jnp.concatenate(high_low_high(p), 0))
    flux = high_low_high(area_depth * u)[:2] + high_low_high(area_depth * v)[:2]
    spread = dot(table[4 * NP :], jnp.concatenate(flux, 0))
    return [
        -(spread[: 2 * NP] + spread[2 * NP :]),
        weighted_spin * ends(v) - root * slopes[: 2 * NP],
        -weighted_spin * ends(u) - root * slopes[2 * NP :],
        mass,
    ]


def row_edges(sums):
    return tuple(sums[0, pl.ds(j, EDGE_ROWS, stride=NP)] for j in (NP - 1, 0))


def beside(left, right):
    return jnp.concatenate([left, right], 1)


def one_of_four(parts, index):
    out = parts[0]
    for k in range(1, 4):
        out = jnp.where(index == k, parts[k], out)
    return out


def folded(tide, kept, late, step):
    half = NODES // 2
    back = pltpu.roll(tide[half:], LANES - step, 1)
    onward = pltpu.roll(tide[half:], step, 1)
    return jnp.where(kept, tide[:half], jnp.where(late, back, onward))


def unfolded(rows, late, step):
    back = pltpu.roll(rows, LANES - step, 1)
    onward = pltpu.roll(rows, step, 1)
    return jnp.concatenate([rows, jnp.where(late, onward, back)], 0)


def strip_rows(parts, late, shift, rims):
    lane = lax.broadcasted_iota(i32, (1, LANES), 1)
    index = (lane >> shift) & 3
    kept = jnp.where(late, index // 2, 1 - index // 2) != 0
    tide = folded(parts[6], kept, late, 2 << shift)
    rim = one_of_four(rims, index)
    return jnp.concatenate(parts[:6] + [tide, rim, jnp.zeros_like(rim)], 0)


def placed_rows(whole, late, shift):
    half = NODES // 2
    tide = unfolded(whole[MOVED : MOVED + half], late, 2 << shift)
    rim = whole[MOVED + half : MOVED + half + NP]
    return jnp.concatenate([whole[:MOVED], tide] + spread_out(rim, late, shift), 0)


def spread_out(rim, late, shift):
    parts = []
    for k in range(4):
        first = pltpu.roll(rim, (LANES - (k << shift)) % LANES, 1) if k else rim
        last = pltpu.roll(rim, (3 - k) << shift, 1) if k < 3 else rim
        parts.append(jnp.where(late, first, last))
    return parts


def with_row_rim(whole, sums, top):
    north, south = row_edges(sums)
    rim = jnp.where(top, pltpu.roll(north, RING, 1), pltpu.roll(south, LANES - RING, 1))
    parts = [rim[k * NP : (k + 1) * NP] for k in range(4)]
    lane = lax.broadcasted_iota(i32, (1, LANES), 1)
    spots = []
    for k, part in enumerate(parts):
        first = pltpu.roll(part, k * RING, 1) if k else part
        last = pltpu.roll(part, (LANES - (3 - k) * RING) % LANES, 1) if k < 3 else part
        spots.append(jnp.where(top, first, last))
    rim = one_of_four(spots, (lane >> 2) & 3)
    return jnp.concatenate([whole[: MOVED + NODES // 2 + NP], rim], 0)


def in_eight(whole):
    whole = jnp.concatenate([whole, jnp.zeros((8 * CORNER_ROWS - whole.shape[0], LANES), f32)], 0)
    return [whole[k * CORNER_ROWS : (k + 1) * CORNER_ROWS] for k in range(8)]


def corner_of(whole, start, top):
    lane = lax.broadcasted_iota(i32, (1, LANES), 1)
    out = None
    for k, part in enumerate(in_eight(whole)):
        last = pltpu.roll(part, (LANES - start - 48 + 16 * k) % LANES, 1)
        first = pltpu.roll(part, (LANES - start + 16 * k) % LANES, 1)
        part = jnp.where(top != 0, last, first)
        out = part if k == 0 else jnp.where(lane >= 16 * k, part, out)
    return out


def both_corners(whole, odd):
    group = lax.broadcasted_iota(i32, (1, LANES), 1) >> 4
    other_group = (group + jnp.where(odd != 0, 7, 1)) & 7
    first, other = None, None
    for k, part in enumerate(in_eight(whole)):
        part = pltpu.roll(part, (LANES + 16 * k - 48 * odd) & (LANES - 1), 1)
        first = part if k == 0 else jnp.where(group == k, part, first)
        other = part if k == 0 else jnp.where(other_group == k, part, other)
    return first, other


def arrived_corners(far0, far1, block_cols, odd):
    lane = lax.broadcasted_iota(i32, (1, LANES), 1)
    corners = []
    for k in range(8):
        if block_cols == 1:
            part = jnp.where((lane >> 4) == k, far0, far1)
            part = pltpu.roll(part, (LANES + 64 + 16 * (1 - odd) - 16 * k) & (LANES - 1), 1)
        else:
            first = pltpu.roll(far0, (64 - 16 * k) % LANES, 1)
            other = pltpu.roll(far1, (80 - 16 * k) % LANES, 1)
            part = jnp.where((lane & 16) == 0, first, other)
        corners.append(part)
    return jnp.concatenate(corners, 0), ((lane >> 4) & 1) ^ (1 - odd if block_cols == 1 else 0)


def packed(whole):
    second = lax.broadcasted_iota(i32, (1, LANES), 1) >= 64
    top, bottom = whole[:HALF_ROWS], whole[HALF_ROWS:]
    return (
        jnp.where(second, pltpu.roll(bottom, 64, 1), top),
        jnp.where(second, bottom, pltpu.roll(top, 64, 1)),
    )


def unpacked(in0, in1):
    second = lax.broadcasted_iota(i32, (1, LANES), 1) >= 64
    top = jnp.where(second, pltpu.roll(in1, 64, 1), in0)
    bottom = jnp.where(second, in1, pltpu.roll(in0, 64, 1))
    return jnp.concatenate([top, bottom], 0)


def seam_flags(seam_ref, block_cols):
    size_y = seam_ref.shape[1]
    face = lax.axis_index("face")
    blk = lax.axis_index("blk")
    block_x = blk // BY

    def flipped(k):
        return jnp.where(lax.rem(seam_ref[k, 1] - seam_ref[k, 0] + size_y, size_y) != 1, 1, 0)

    first, second = flipped(0), flipped(1)
    east_flip = jnp.where(face == 0, first, second)
    west_flip = jnp.where(face == 0, second, first)
    if block_cols == 1:
        return 1 - east_flip, 0, east_flip, 1
    at_east = jnp.where(block_x == block_cols - 1, east_flip, 0)
    at_west = jnp.where(block_x == 0, west_flip, 0)
    return 1, at_east, 0, at_west


def slots_in(flags_ref):
    return flags_ref[4:5], flags_ref[5:6]


def flags_in(flags_ref, tiles=1):
    return [jnp.concatenate([flags_ref[k : k + 1]] * tiles, 1) for k in range(4)]


def mirrored_first(block_y):
    return (block_y >= BY // 4) & (block_y < BY - BY // 4)


def in_order(block_cols, first, second):
    if block_cols > 1:
        return first, second
    swap = mirrored_first(lax.rem(lax.axis_index("blk"), BY))
    return jnp.where(swap, second, first), jnp.where(swap, first, second)


def strips_kernel(block_cols, *refs):
    sources, (first_ref, then_ref, stored_ref, flags_ref) = refs[:8], refs[8:12]
    buffers, sems = refs[12:20], refs[20]
    copies = [
        pltpu.make_async_copy(source, buffer, sems.at[k])
        for k, (source, buffer) in enumerate(zip(sources, buffers))
    ]
    for copy in copies:
        copy.start()
    seam_ref, slot_ref, fields_ref, area_ref, depth_ref, spin_ref, tide_ref = buffers[:7]
    table_ref = buffers[7]
    for copy in copies[:2]:
        copy.wait()
    east0, flip0, east1, flip1 = flags = seam_flags(seam_ref, block_cols)
    index = lax.broadcasted_iota(i32, (8, LANES), 0)
    flags_ref[...] = sum(jnp.where(index == k, flag, 0) for k, flag in enumerate(flags))
    slots = slot_ref[:, :LANES], slot_ref[:, LANES:]
    flags_ref[4:5], flags_ref[5:6] = slots
    lane = lax.broadcasted_iota(i32, (8, 2 * LANES), 1)
    second = (lane & 64) != 0
    place = lane & 63
    row = place >> 2
    row = jnp.where(jnp.where(second, flip1, flip0) != 0, GY - 1 - row, row)
    east = jnp.where(second, east1, east0) != 0
    col = jnp.where(east, GX - RING, 0) + (place & 3)
    col = jnp.where(lane >= LANES, jnp.where(east, GX - RING - 1, RING), col)
    one_hot = by_slot(slots, col * GY + row)
    for copy in copies[2:7]:
        copy.wait()
    stored = stored_rows(fields_ref, (area_ref, depth_ref, spin_ref, tide_ref))
    both = picked(stored, one_hot)

    lane = lax.broadcasted_iota(i32, (1, LANES), 1)
    second = lane >= 64
    flip = jnp.where(second, flip1, flip0) != 0
    sign = jnp.where(flip, -1.0, 1.0)
    node = lax.broadcasted_iota(i32, (1, NP, 1), 1)

    def turned(values):
        shaped = values.reshape(-1, NP, LANES)
        shaped = pltpu.roll(shaped, 4, 1)
        shaped = jnp.where((node & 2) == 0, pltpu.roll(shaped, 6, 1), pltpu.roll(shaped, 2, 1))
        shaped = jnp.where((node & 1) == 0, pltpu.roll(shaped, 7, 1), pltpu.roll(shaped, 1, 1))
        return shaped.reshape(values.shape)

    strip, ring = (
        [part[k * NODES : (k + 1) * NODES] for k in range(ARRAYS)]
        for part in (both[:, :LANES], both[:, LANES:])
    )
    for copy in copies[7:]:
        copy.wait()
    table, weight = table_ref[: 8 * NP].astype(bf16), table_ref[8 * NP :, :LANES]
    edges = column_edges(table, weight, *ring[:6])
    east = jnp.where(second, east1, east0) != 0
    ends = [jnp.where(east, part[NP:], part[:NP]) for part in edges]
    ends[2] = ends[2] * sign
    strip[2] = strip[2] * sign
    strip[5] = strip[5] * sign
    strips = []
    for part, flip in zip(packed(strip_rows(strip, east, 0, ends)), (flip0, flip1)):
        if isinstance(flip, int):
            strips.append(turned(part) if flip else part)
        else:
            strips.append(jnp.where(flip != 0, turned(part), part))
    first_ref[...], then_ref[...] = in_order(block_cols, *strips)
    stored_ref[...] = stored


def rows_kernel(
    block_cols, flags_ref, stored_ref, first_ref, then_ref, table_ref, weight_ref,
    next_ref, far0_ref, far1_ref, pair_ref, sums,
):
    east0, flip0, east1, flip1 = flags_in(flags_ref)
    odd = lax.axis_index("blk") & 1
    lane = lax.broadcasted_iota(i32, (8, 2 * LANES), 1)
    row = jnp.where(odd != 0, GY - RING, 0) + ((lane & 63) >> 4)
    row = jnp.where((lane & 64) != 0, jnp.where(odd != 0, GY - RING - 1, RING), row)
    five = jnp.where(odd != 0, 0, GY - RING - 1) + jnp.minimum((lane & (LANES - 1)) >> 4, RING)
    row = jnp.where(lane >= LANES, five, row)
    both = picked(stored_ref[...], by_slot(slots_in(flags_ref), (lane & 15) * GY + row))
    pair_ref[...] = both[:, LANES:]
    rows = [both[k * NODES : (k + 1) * NODES, :LANES] for k in range(ARRAYS)]
    whole = unpacked(*in_order(block_cols, first_ref[...], then_ref[...]))
    strip = [whole[k * NODES : (k + 1) * NODES] for k in range(6)]
    edges = edge_values(table_ref, weight_ref, *map(beside, strip, rows[:6]))
    sums[0] = jnp.concatenate([part[:, :LANES] for part in edges], 0)
    lane = lax.broadcasted_iota(i32, (1, LANES), 1)
    top0, top1 = odd ^ flip0, odd ^ flip1
    whole = with_row_rim(whole, sums, jnp.where(lane >= 64, top1, top0) != 0)
    if block_cols == 1:
        far0_ref[...], far1_ref[...] = both_corners(whole, odd)
    else:
        far0_ref[...] = corner_of(whole, 0, top0)
        far1_ref[...] = corner_of(whole, 64, top1)
    sums[0] = jnp.concatenate([part[:, LANES:] for part in edges], 0)
    up = jnp.broadcast_to(odd != 0, (1, LANES))
    rim = pltpu.roll(jnp.where(up, *row_edges(sums)), 64, 1)
    rim = [rim[k * NP : (k + 1) * NP] for k in range(4)]
    whole = strip_rows(rows, up, 4, rim)
    top, bottom = whole[:HALF_ROWS], whole[HALF_ROWS:]
    next_ref[...] = jnp.where(lane >= 64, pltpu.roll(bottom, 64, 1), top)


def corners_kernel(block_cols, flags_ref, first_ref, then_ref, pair_ref, _, out_ref):
    east0, flip0, east1, flip1 = flags_in(flags_ref)
    in0, in1 = in_order(block_cols, first_ref[...], then_ref[...])
    top = 1 - (lax.axis_index("blk") & 1)
    lane = lax.broadcasted_iota(i32, (1, LANES), 1)
    halves = []
    for start in (0, 64):
        at0 = jnp.where(top != 0, 36, 80)
        at1 = jnp.where(top != 0, 56, 100)
        first = pltpu.roll(in0, (at0 - start) & (LANES - 1), 1)
        other = pltpu.roll(in1, (at1 - start) & (LANES - 1), 1)
        halves.append(jnp.where(lane < 100, first, other))
    late = jnp.where(lane < 100, east0, east1) == 0
    whole = placed_rows(jnp.concatenate(halves, 0), late, 0)
    out_ref[:ROWS] = jnp.where(lane < 80, pair_ref[...], whole[:ROWS])
    out_ref[ROWS:] = whole[ROWS:]


def own_kernel(flags_ref, stored_ref, lanes_ref, own_ref, hot_ref):
    one_hot = by_slot(slots_in(flags_ref), lanes_ref[0:8, :MID])
    own_ref[...] = picked(stored_ref[...], one_hot)
    hot_ref[...] = one_hot.astype(f32).T.astype(bf16)


def first_sums(table, weight, parts, rims, at_rim):
    p, u, v, area, depth, spin, tide = parts
    size = area.shape[1]
    root = jnp.sqrt(area)
    mass = jnp.concatenate([weight] * (size // LANES), 1) * area
    used = [p, u, v, root * depth, root, mass * spin, tide]
    for part, rim in zip(mass_tendency(table, p, u, v, *used[3:6]) + [mass], rims):
        west, east = part[:NP], part[NODES - NP :]
        at_east = jnp.where(at_rim, rim, pltpu.roll(west, size - 1, 1))
        at_west = jnp.where(at_rim, rim, pltpu.roll(east, 1, 1))
        used.append(
            jnp.concatenate([west + at_west, part[NP : NODES - NP], east + at_east], 0)
        )
    return used


def middle_kernel(
    block_cols, flags_ref, first_ref, then_ref, own_ref, lanes_ref, table_ref, weight_ref,
    low_ref, centre_ref, high_ref,
):
    east0, flip0, east1, flip1 = flags_in(flags_ref)
    second = lax.broadcasted_iota(i32, (1, LANES), 1) >= 64
    late = jnp.where(second, east1, east0) == 0
    whole = unpacked(*in_order(block_cols, first_ref[...], then_ref[...]))
    whole = placed_rows(whole, late, 0)
    side = lanes_ref[16:24, :MID]
    east = flags_in(flags_ref, MID // LANES)[0]
    first_at = jnp.where(side == 2, 64 * (1 - east), 64 * east)
    place = jnp.where(side == 0, -1, lanes_ref[8:16, :MID] + first_at)
    placed = picked(whole, as_one_hot(place, LANES))
    parts = [
        placed[k * NODES : (k + 1) * NODES] + own_ref[k * NODES : (k + 1) * NODES]
        for k in range(ARRAYS)
    ]
    rims = [placed[ROWS + c * NP : ROWS + (c + 1) * NP] for c in range(4)]
    at_rim = lanes_ref[24:25, LANES : LANES + MID] != 0
    used = first_sums(table_ref[...].astype(bf16), weight_ref[...], parts, rims, at_rim)
    for k, ref in enumerate((low_ref, centre_ref, high_ref)):
        for n, part in enumerate(used):
            ref[n * NODES : (n + 1) * NODES] = part[:, k * LANES : (k + 1) * LANES]


def next_kernel(next_ref, _, out_ref):
    below = jnp.broadcast_to((lax.axis_index("blk") & 1) == 0, (1, LANES))
    strip = jnp.concatenate([next_ref[...], pltpu.roll(next_ref[...], 64, 1)], 0)
    out_ref[...] = placed_rows(strip, below, 4)


def far_kernel(block_cols, flags_ref, far1_ref, far0_ref, strip_ref, out_ref):
    east0, flip0, east1, flip1 = flags_in(flags_ref)
    odd = lax.axis_index("blk") & 1
    own = lax.broadcasted_iota(i32, (1, LANES), 1) < 64
    below = jnp.broadcast_to(odd == 0, (1, LANES))
    corners, strip_of = arrived_corners(far0_ref[...], far1_ref[...], block_cols, odd)
    late = jnp.where(strip_of != 0, east1, east0) == 0
    rim = MOVED + NODES // 2 + NP
    rim = jnp.concatenate(spread_out(corners[rim : rim + NP], below, 2), 0)
    corners = placed_rows(corners, late, 0)
    out_ref[:ROWS] = jnp.where(own, strip_ref[:ROWS], corners[:ROWS])
    out_ref[ROWS:ALL_ROWS] = corners[ROWS:]
    out_ref[ALL_ROWS:] = jnp.where(own, strip_ref[ROWS:], rim)


def steps_kernel(
    block_cols, flags_ref, pair_ref, next_ref, low_ref, centre_ref,
    high_ref, hot_ref, table_ref, weight_ref, lanes_ref, out_ref, sums,
):
    east0, flip0, east1, flip1 = flags_in(flags_ref)
    odd = lax.axis_index("blk") & 1
    block_y = lax.rem(lax.axis_index("blk"), BY)

    lane = lax.broadcasted_iota(i32, (1, LANES), 1)
    pair = jnp.concatenate([pair_ref[...], jnp.zeros((EDGE_ROWS, LANES), f32)], 0)
    around = beside(pair, next_ref[...])
    outer_at = [lanes_ref[32 + 8 * k : 40 + 8 * k, : 2 * LANES] for k in range(4)]
    kind = outer_at[1]
    from_pair = jnp.where(outer_at[2] != 0, 1 - odd, odd) != 0
    east = flags_in(flags_ref, 2)[0]
    strip_at = jnp.where(kind == 3, 1 - east, east)
    far_at = strip_at ^ (1 - odd) if block_cols == 1 else strip_at
    strip_at, far_at = (jnp.where(kind > 1, at, 0) for at in (strip_at, far_at))
    place = jnp.where(
        from_pair,
        outer_at[0] + (RING + 1) * RING * strip_at,
        jnp.where(outer_at[3] < 0, -1, outer_at[3] + RING * RING * far_at),
    )
    outer = picked(around, as_one_hot(jnp.where(kind == 0, -1, place), 2 * LANES))
    table = table_ref[...].astype(bf16)
    tiles = (None, low_ref, centre_ref, high_ref, None)
    count = len(tiles)
    masks = [lanes_ref[24:32, k * LANES : (k + 1) * LANES] for k in range(count)]
    closed_above = jnp.where(block_y == BY - 1, masks[-2][1:2], 0) != 0
    closed_below = jnp.where(block_y == 0, masks[1][2:3], 0) != 0
    first_row = jnp.where(odd == 0, masks[0][4:5], 0) != 0
    last_row = jnp.where(odd != 0, masks[-1][5:6], 0) != 0
    outer_used = first_sums(
        table,
        weight_ref[...],
        [outer[k * NODES : (k + 1) * NODES] for k in range(ARRAYS)],
        [outer[ROWS + c * NP : ROWS + (c + 1) * NP] for c in range(4)],
        beside(masks[0][0:1], masks[-1][0:1]) != 0,
    )

    def shifted(parts, by, ring):
        turned = [pltpu.roll(part, -by % LANES, 1) for part in parts]
        size = len(parts)
        step = 1 if by > 0 else -1
        others = [(k + step) % size if ring else min(max(k + step, 0), size - 1) for k in range(size)]
        from_other = lane >= LANES - by if by > 0 else lane < -by
        return [jnp.where(from_other, turned[others[k]], turned[k]) for k in range(size)]

    def put_x_sums(groups, components):
        slots = [k for group in groups for k in group]
        ring = len(slots) < count
        per_tile = [
            [part[:, n * LANES : (n + 1) * LANES] for part in parts]
            for group, parts in zip(groups, components)
            for n in range(len(group))
        ]
        for c in range(3):
            parts = [tile[c] for tile in per_tile]
            west = [part[:NP] for part in parts]
            east = [part[NODES - NP :] for part in parts]
            at_east, at_west = shifted(west, 1, ring), shifted(east, -1, ring)
            for n, k in enumerate(slots):
                sums[k, c * NODES : c * NODES + NP] = west[n] + at_west[n]
                sums[k, c * NODES + NP : (c + 1) * NODES - NP] = parts[n][NP : NODES - NP]
                sums[k, (c + 1) * NODES - NP : (c + 1) * NODES] = east[n] + at_east[n]

    def edge_y(components, slots, rows=None):
        ring = len(slots) < count
        south_at = pl.ds(0, components * NP, stride=NP)
        north_at = pl.ds(NP - 1, components * NP, stride=NP)
        south = [sums[k, south_at] for k in slots]
        north = [sums[k, north_at] for k in slots]
        at_north, at_south = shifted(south, PITCH, ring), shifted(north, -PITCH, ring)
        for n, k in enumerate(slots):
            if k == count - 2:
                at_north[n] = jnp.where(closed_above, 0.0, at_north[n])
            if k == 1:
                at_south[n] = jnp.where(closed_below, 0.0, at_south[n])
        if rows is not None:
            at_south[0] = jnp.where(first_row, rows[0], at_south[0])
            at_north[-1] = jnp.where(last_row, rows[1], at_north[-1])
        for n, k in enumerate(slots):
            sums[k, south_at] = south[n] + at_south[n]
            sums[k, north_at] = north[n] + at_north[n]

    node = lax.broadcasted_iota(i32, (1, NP, 1), 1)
    rows = []
    for rim in (outer[ALL_ROWS:, :LANES], outer[ALL_ROWS:, LANES:]):
        east = pltpu.roll(rim, LANES - 1, 1).reshape(4, NP, LANES)
        west = pltpu.roll(rim, 1, 1).reshape(4, NP, LANES)
        rim = (
            rim.reshape(4, NP, LANES)
            + jnp.where(node == NP - 1, pltpu.roll(east, NP - 1, 1), 0.0)
            + jnp.where(node == 0, pltpu.roll(west, 1, 1), 0.0)
        )
        rows.append(rim.reshape(EDGE_ROWS, LANES))

    every = tuple(range(count))
    groups = (every[0:2], every[2:4], every[4:])

    def tile_part(k, n):
        if tiles[k] is None:
            return outer_used[n][:, :LANES] if k == 0 else outer_used[n][:, LANES:]
        return tiles[k][n * NODES : (n + 1) * NODES]

    def part_of(group, n):
        return jnp.concatenate([tile_part(k, n) for k in group], 1)

    def summed(group, c):
        return jnp.concatenate([sums[k, c * NODES : (c + 1) * NODES] for k in group], 1)

    def average(group, per_mass):
        return [summed(group, c) * per_mass for c in range(3)]

    def laplace(s):
        return [
            dot(table[4 * NODES :, : 3 * NODES], jnp.concatenate(high_low_high(part), 0))
            for part in s
        ]

    start = [[part_of(group, n) for n in range(3)] for group in groups]
    fixed = [[part_of(group, n) for n in range(3, 6)] for group in groups]
    for k in every:
        for c in range(4):
            sums[k, c * NODES : (c + 1) * NODES] = tile_part(k, 7 + c)
    edge_y(4, every, rows)
    per_mass = [1.0 / summed(group, 3) for group in groups]
    one = []
    for n, group in enumerate(groups):
        change = average(group, per_mass[n])
        one.append([s + time_step * c for s, c in zip(start[n], change)])
    put_x_sums(groups, [mass_tendency(table, *s, *f) for s, f in zip(one, fixed)])
    edge_y(3, every)
    two = []
    for n, group in enumerate(groups):
        change = average(group, per_mass[n])
        two.append(
            [0.75 * s + 0.25 * (o + time_step * c) for s, o, c in zip(start[n], one[n], change)]
        )
    put_x_sums(groups, [mass_tendency(table, *s, *f) for s, f in zip(two, fixed)])
    edge_y(3, every)

    def regrouped(per_group):
        (outer_low, high_above) = per_group[0], per_group[1]
        below, low = outer_low[:, :LANES], outer_low[:, LANES:]
        centre, high = high_above[:, :LANES], high_above[:, LANES:]
        near = jnp.where(lane < LANES // 2, per_group[2], below)
        return [beside(low, centre), beside(high, near)]

    def of_groups(values):
        return [list(parts) for parts in zip(*(regrouped(part) for part in zip(*values)))]

    for c in range(3):
        rows_at = slice(c * NODES, (c + 1) * NODES)
        sums[count - 1, rows_at] = jnp.where(
            lane < LANES // 2, sums[count - 1, rows_at], sums[0, rows_at]
        )
    slots = every[1:]
    groups = (slots[0:2], slots[2:4])
    start, two = of_groups(start), of_groups(two)
    tide = regrouped([part_of(every[0:2], 6), part_of(every[2:4], 6), part_of(every[4:], 6)])
    per_mass = regrouped(per_mass)
    three = []
    for n, group in enumerate(groups):
        change = average(group, per_mass[n])
        now = [
            s / 3.0 + 2.0 / 3.0 * (o + time_step * c)
            for s, o, c in zip(start[n], two[n], change)
        ]
        now[0] = now[0] + tide[n]
        three.append(now)
    put_x_sums(groups, [laplace(s) for s in three])
    edge_y(3, slots)
    change = [average(group, per_mass[n]) for n, group in enumerate(groups)]
    put_x_sums(groups, [laplace(s) for s in change])
    edge_y(3, slots)
    stepped = []
    for n, group in enumerate(groups):
        change = average(group, per_mass[n])
        now = [s - time_step * hyper_coeff * b for s, b in zip(three[n], change)]
        stepped.append(jnp.concatenate(now, 0))
    stepped = jnp.concatenate(stepped, 1)[:, :MID]
    own = lanes_ref[27:28, LANES : LANES + MID] != 0
    stored = picked(jnp.where(own, stepped, 0.0), hot_ref[...])
    out_ref[...] = stored.reshape(out_ref.shape)


def on_device(fields, jacobian, water_depth, coriolis, tide_height, slot_of, seam_rows):
    block_cols = lax.axis_size("blk") // BY
    table, weight, edge_table, lanes = map(jnp.asarray, (*operator_table(), lane_tables()))
    vmem = pl.BlockSpec(memory_space=pltpu.VMEM)
    hbm = pl.BlockSpec(memory_space=pltpu.HBM)
    params = pltpu.CompilerParams(vmem_limit_bytes=48 * 2**20)
    held = (fields, jacobian, water_depth, coriolis, tide_height)

    def call(kernel, ins, outs, cost, scratch=(), name=None):
        return pl.pallas_call(
            kernel,
            out_shape=[jax.ShapeDtypeStruct(*out) for out in outs],
            in_specs=[spec for spec, value in ins],
            out_specs=[vmem] * len(outs),
            scratch_shapes=list(scratch),
            compiler_params=params,
            cost_estimate=pl.CostEstimate(
                flops=cost, bytes_accessed=2 * 2**20, transcendentals=0
            ),
            name=name,
        )(
            *[
                pltpu.with_memory_space_constraint(value, pltpu.HBM) if spec is hbm else value
                for spec, value in ins
            ]
        )

    strip = ((HALF_ROWS, LANES), f32)
    def room(values, spaces=None):
        spaces = spaces or [pltpu.VMEM] * len(values)
        buffers = [space(x.shape, x.dtype) for space, x in zip(spaces, values)]
        return buffers + [pltpu.SemaphoreType.DMA((len(values),))]

    needed = (seam_rows, slot_of, *held, edge_table)
    corner = ((CORNER_ROWS, LANES), f32)
    scratch = [pltpu.VMEM((1, 4 * NODES, LANES), f32)]
    first, then, stored, flags = call(
        functools.partial(strips_kernel, block_cols),
        [(hbm, x) for x in needed],
        [strip, strip, ((ROWS, ELEMENTS), f32), ((8, LANES), i32)],
        10**8,
        scratch=room(needed, [pltpu.SMEM] + [pltpu.VMEM] * (len(needed) - 1)),
        name="strips",
    )
    to_next, far0, far1, to_pair = call(
        functools.partial(rows_kernel, block_cols),
        [(vmem, x) for x in (flags, stored, first, then, table, weight)],
        [strip, corner, corner, ((ROWS, LANES), f32)],
        10**8,
        scratch=scratch,
        name="rows",
    )
    span = block_cols * BY
    both = ("face", "blk")
    places = [(f, x, y) for f in range(2) for x in range(block_cols) for y in range(BY)]

    def rank(face, block_x, block_y):
        return face * span + block_x * BY + block_y

    def same(y):
        return y

    def in_pair(y):
        return y ^ 1

    def next_pair(y):
        other = y + 1 if y % 2 else y - 1
        return other if 0 <= other < BY else y

    def swapped(value, partner):
        pairs = [
            (rank(f, x, y), rank(f if partner(y) != y else 1 - f, x, partner(y)))
            for f, x, y in places
        ]
        return lax.ppermute(value, both, pairs)

    def across(value0, value1, partner):
        last = block_cols - 1

        def aligned(y):
            return partner is same or partner(y) != y

        straight = {
            (f, x, y): (f, x + 1, partner(y)) if x < last else (1 - f, 0, partner(y))
            for f, x, y in places
        }
        turned = {
            (f, last, y): (1 - f, 0, BY - 1 - partner(y) if aligned(y) else y)
            for f in range(2)
            for y in range(BY)
        }

        def eastward(value, pairs):
            return lax.ppermute(value, both, [(rank(*a), rank(*b)) for a, b in pairs.items()])

        def westward(value, pairs):
            return lax.ppermute(value, both, [(rank(*b), rank(*a)) for a, b in pairs.items()])

        if block_cols == 1:
            return eastward(value0, straight), eastward(value1, turned)
        flipped = (seam_rows[:, 1] - seam_rows[:, 0]) % seam_rows.shape[1] != 1
        face = lax.axis_index("face")
        block_x = lax.axis_index("blk") // BY
        return (
            jnp.where(
                (block_x == last) & flipped[face],
                westward(value1, turned),
                westward(value1, straight),
            ),
            jnp.where(
                (block_x == 0) & flipped[1 - face],
                eastward(value0, turned),
                eastward(value0, straight),
            ),
        )

    if block_cols == 1:
        halos = []
        for value, mirrored in ((first, mirrored_first), (then, lambda y: not mirrored_first(y))):
            pairs = [
                (rank(f, x, y), rank(1 - f, x, BY - 1 - y if mirrored(y) else y))
                for f, x, y in places
            ]
            halos.append(lax.ppermute(value, both, pairs))
        halo0, halo1 = halos
    else:
        halo0, halo1 = across(first, then, same)
    far0, far1 = across(far0, far1, next_pair)
    from_next = swapped(to_next, next_pair)
    own, hot = call(
        own_kernel,
        [(vmem, x) for x in (flags, stored, lanes)],
        [((ROWS, MID), f32), ((MID, ELEMENTS), bf16)],
        10**8,
        name="own",
    )
    (to_pair,) = call(
        functools.partial(corners_kernel, block_cols),
        [(vmem, x) for x in (flags, halo0, halo1, to_pair, hot)],
        [((ALL_ROWS, LANES), f32)],
        10**8,
        name="corners",
    )
    from_pair = swapped(to_pair, in_pair)
    tile = ((11 * NODES, LANES), f32)
    low, centre, high = call(
        functools.partial(middle_kernel, block_cols),
        [(vmem, x) for x in (flags, halo0, halo1, own, lanes, table, weight)],
        [tile, tile, tile],
        10**8,
        name="middle",
    )
    (from_next,) = call(
        next_kernel,
        [(vmem, x) for x in (from_next, low)],
        [((ALL_ROWS, LANES), f32)],
        10**11,
        name="next",
    )
    (from_next,) = call(
        functools.partial(far_kernel, block_cols),
        [(vmem, x) for x in (flags, far1, far0, from_next)],
        [((RIM_ROWS, LANES), f32)],
        10**10,
        name="far",
    )
    (stepped,) = call(
        functools.partial(steps_kernel, block_cols),
        [
            (vmem, x)
            for x in (
                flags, from_pair, from_next, low, centre, high, hot, table, weight, lanes
            )
        ],
        [(fields.shape, f32)],
        10**8,
        scratch=[pltpu.VMEM((EXT // LANES, 4 * NODES, LANES), f32)],
        name="steps",
    )
    return stepped


def solution(mesh):
    return jax.shard_map(
        on_device,
        mesh=mesh,
        in_specs=(
            P(None, None, None, ("face", "blk")),
            P(None, None, ("face", "blk")),
            P(None, None, ("face", "blk")),
            P(None, None, ("face", "blk")),
            P(None, None, ("face", "blk")),
            P(("face", "blk"), None),
            P(),
        ),
        out_specs=P(None, None, None, ("face", "blk")),
        check_vma=False,
    )
```

```python
import functools
import math

import jax
import jax.numpy as jnp
import ml_dtypes
import numpy as np
from jax import lax
from jax.experimental import pallas as pl
from jax.experimental.pallas import tpu as pltpu
from jax.sharding import PartitionSpec as P

BY = 16
GX = 16
GY = 16
NP = 8
NODES = NP * NP
ARRAYS = 7
ROWS = ARRAYS * NODES
MOVED = 6 * NODES
EDGE_ROWS = 4 * NP
ALL_ROWS = ROWS + EDGE_ROWS
HALF_ROWS = (MOVED + NODES // 2 + 2 * NP) // 2
RING = 4
RIM_ROWS = ROWS + 2 * EDGE_ROWS
CORNER_ROWS = (MOVED + NODES // 2 + 4 * NP) // 8
PITCH = GX + 2 * RING
MID = GY * PITCH
LANES = 128
EXT = MID + 2 * LANES
LEAD = LANES - RING * PITCH
ELEMENTS = GX * GY

time_step = 0.03
hyper_coeff = 0.0002

f32 = jnp.float32
bf16 = jnp.bfloat16
i32 = jnp.int32


def legendre_pair(location, degree):
    lower_value = 1.0
    upper_value = location
    for polynomial_order in range(2, degree + 1):
        lower_value, upper_value = (
            upper_value,
            (
                (2 * polynomial_order - 1) * location * upper_value
                - (polynomial_order - 1) * lower_value
            )
            / polynomial_order,
        )
    return (lower_value, upper_value)


def gll_tables(points):
    degree = points - 1
    locations = [-math.cos(math.pi * position / degree) for position in range(points)]
    for iteration in range(100):
        updated = []
        for location in locations:
            lower_value, upper_value = legendre_pair(location, degree)
            updated.append(
                location - (location * upper_value - lower_value) / ((degree + 1) * upper_value)
            )
        locations = updated
    locations[0] = -1.0
    locations[degree] = 1.0
    legendre_at = [legendre_pair(location, degree)[1] for location in locations]
    weights = [2.0 / (degree * (degree + 1) * value * value) for value in legendre_at]
    corner_value = degree * (degree + 1) / 4.0
    derivative = []
    for row_index in range(points):
        row_values = []
        for column_index in range(points):
            if row_index != column_index:
                row_values.append(
                    legendre_at[row_index]
                    / (legendre_at[column_index] * (locations[row_index] - locations[column_index]))
                )
            elif row_index == 0:
                row_values.append(-corner_value)
            elif row_index == degree:
                row_values.append(corner_value)
            else:
                row_values.append(0.0)
        derivative.append(row_values)
    return np.asarray(weights, np.float64), np.asarray(derivative, np.float64)


def in_three(matrix):
    high = matrix.astype(ml_dtypes.bfloat16)
    low = (matrix - high.astype(np.float64)).astype(ml_dtypes.bfloat16)
    return np.concatenate([high, high, low], 1)


def operator_table():
    weights, derivative = gll_tables(NP)
    eye = np.eye(NP)
    node_weight = np.outer(weights, weights).reshape(NODES, 1)
    along_x = node_weight * np.kron(derivative, eye)
    along_y = node_weight * np.kron(eye, derivative)
    second = derivative @ derivative
    both = node_weight * (np.kron(second, eye) + np.kron(eye, second))
    table = np.zeros((5 * NODES, 4 * NODES), ml_dtypes.bfloat16)
    table[:NODES, : 3 * NODES] = in_three(along_x)
    table[NODES : 2 * NODES, : 3 * NODES] = in_three(along_y)
    flux = [in_three(along_x), in_three(along_y)]
    for k, part in enumerate(flux):
        at = 2 * k * NODES
        table[2 * NODES : 3 * NODES, at : at + 2 * NODES] = part[:, : 2 * NODES]
        table[3 * NODES : 4 * NODES, at : at + NODES] = part[:, 2 * NODES :]
    table[4 * NODES :, : 3 * NODES] = in_three(both)
    table = table.astype(np.float32)
    spread = np.broadcast_to(node_weight, (NODES, LANES)).astype(np.float32)
    ends = np.r_[:NP, NODES - NP : NODES]
    edge_table = np.zeros((10 * NP, 4 * NODES), np.float32)
    for k in range(4):
        edge_table[2 * k * NP : 2 * (k + 1) * NP] = table[k * NODES + ends]
    edge_table[8 * NP :, :LANES] = spread[ends]
    return table.astype(ml_dtypes.bfloat16), np.ascontiguousarray(spread), edge_table


def lane_tables():
    table = np.zeros((24, MID), np.int32)
    for lane in range(MID):
        row, col = divmod(lane, PITCH)
        x = col - RING
        own = 0 <= x < GX
        table[0:8, lane] = x * GY + row if own else -1
        if not own:
            table[8:16, lane] = row * RING + (col if x < 0 else x - GX)
        table[16:24, lane] = 0 if own else (1 if x < 0 else 2)
    ext = np.zeros((8, EXT), np.int32)
    outer = np.zeros((32, 2 * LANES), np.int32)
    for lane in range(EXT):
        row, col = divmod(lane - LEAD, PITCH)
        y = row - RING
        x = col - RING
        ext[0, lane] = x in (-RING, GX + RING - 1)
        ext[1, lane] = y == GY - 1
        ext[2, lane] = y == 0
        ext[3, lane] = 0 <= y < GY and 0 <= x < GX
        ext[4, lane] = y == -RING
        ext[5, lane] = y == GY + RING - 1
        if -RING - 1 <= y < 0 or GY <= y <= GY + RING:
            place = lane if y < 0 else lane - MID
            step = y + RING if y < 0 else y - GY
            near = step + 1 if y < 0 else step
            far = 0 <= step < RING
            if 0 <= x < GX:
                outer[0:8, place] = near * GX + x
                outer[8:16, place] = 1
                outer[24:32, place] = LANES + step * GX + x if far else -1
            else:
                across = x + RING if x < 0 else x - GX
                outer[0:8, place] = (RING + 1) * GX + near * RING + across
                outer[8:16, place] = 2 if x < 0 else 3
                outer[24:32, place] = LANES + RING * GX + step * RING + across if far else -1
            outer[16:24, place] = y > 0
    whole = np.zeros((64, EXT), np.int32)
    whole[0:24, :MID] = table
    whole[24:32] = ext
    whole[32:64, : 2 * LANES] = outer
    return whole


def dot(a, b):
    return jnp.dot(a, b, preferred_element_type=f32)


def picked(values, one_hot):
    high = values.astype(bf16)
    low = (values - high.astype(f32)).astype(bf16)
    both = dot(jnp.concatenate([high, low], 0), one_hot)
    return both[: values.shape[0]] + both[values.shape[0] :]


def as_one_hot(row_of_lane, depth):
    index = lax.broadcasted_iota(i32, (depth, row_of_lane.shape[1]), 0)
    return jnp.where(index == row_of_lane[0:1], 1.0, 0.0).astype(bf16)


def high_low_high(values):
    high = values.astype(bf16)
    low = (values - high.astype(f32)).astype(bf16)
    return [high, low, high]


def by_slot(halves, cell_of_lane):
    size = cell_of_lane.shape[1]
    halves = [jnp.broadcast_to(half, (8, LANES)) for half in halves]
    chosen = []
    for k in range(size // LANES):
        cell = cell_of_lane[:, k * LANES : (k + 1) * LANES]
        low, high = (jnp.take_along_axis(half, cell & (LANES - 1), axis=1) for half in halves)
        chosen.append(jnp.where(cell < 0, -1, jnp.where(cell < LANES, low, high)))
    return as_one_hot(jnp.concatenate(chosen, 1), ELEMENTS)


def stored_rows(fields_ref, others):
    fields = fields_ref[...].reshape(3 * NODES, ELEMENTS)
    others = [ref[...].reshape(NODES, ELEMENTS) for ref in others]
    return jnp.concatenate([fields[:NODES] - others[-1], fields[NODES:]] + others, 0)


def mass_tendency(table, p, u, v, area_depth, weighted_area, spin):
    slopes = dot(table[: 2 * NODES, : 3 * NODES], jnp.concatenate(high_low_high(p), 0))
    flux = high_low_high(area_depth * u)[:2] + high_low_high(area_depth * v)[:2]
    spread = dot(table[2 * NODES : 4 * NODES], jnp.concatenate(flux, 0))
    return [
        -(spread[:NODES] + spread[NODES:]),
        spin * v - weighted_area * slopes[:NODES],
        -spin * u - weighted_area * slopes[NODES:],
    ]


def edge_values(table_ref, weight_ref, p, u, v, area, depth, spin):
    root = jnp.sqrt(area)
    mass = jnp.concatenate([weight_ref[...]] * (area.shape[1] // LANES), 1) * area
    table = table_ref[...]
    return mass_tendency(table, p, u, v, root * depth, root, mass * spin) + [mass]


def column_edges(table, weight, p, u, v, area, depth, spin):
    def ends(part):
        return jnp.concatenate([part[:NP], part[NODES - NP :]], 0)

    root = jnp.sqrt(area)
    area_depth = root * depth
    root, mass = ends(root), weight * ends(area)
    weighted_spin = mass * ends(spin)
    slopes = dot(table[: 4 * NP, : 3 * NODES], jnp.concatenate(high_low_high(p), 0))
    flux = high_low_high(area_depth * u)[:2] + high_low_high(area_depth * v)[:2]
    spread = dot(table[4 * NP :], jnp.concatenate(flux, 0))
    return [
        -(spread[: 2 * NP] + spread[2 * NP :]),
        weighted_spin * ends(v) - root * slopes[: 2 * NP],
        -weighted_spin * ends(u) - root * slopes[2 * NP :],
        mass,
    ]


def row_edges(sums):
    return tuple(sums[0, pl.ds(j, EDGE_ROWS, stride=NP)] for j in (NP - 1, 0))


def beside(left, right):
    return jnp.concatenate([left, right], 1)


def one_of_four(parts, index):
    out = parts[0]
    for k in range(1, 4):
        out = jnp.where(index == k, parts[k], out)
    return out


def folded(tide, kept, late, step):
    half = NODES // 2
    back = pltpu.roll(tide[half:], LANES - step, 1)
    onward = pltpu.roll(tide[half:], step, 1)
    return jnp.where(kept, tide[:half], jnp.where(late, back, onward))


def unfolded(rows, late, step):
    back = pltpu.roll(rows, LANES - step, 1)
    onward = pltpu.roll(rows, step, 1)
    return jnp.concatenate([rows, jnp.where(late, onward, back)], 0)


def strip_rows(parts, late, shift, rims):
    lane = lax.broadcasted_iota(i32, (1, LANES), 1)
    index = (lane >> shift) & 3
    kept = jnp.where(late, index // 2, 1 - index // 2) != 0
    tide = folded(parts[6], kept, late, 2 << shift)
    rim = one_of_four(rims, index)
    return jnp.concatenate(parts[:6] + [tide, rim, jnp.zeros_like(rim)], 0)


def placed_rows(whole, late, shift):
    half = NODES // 2
    tide = unfolded(whole[MOVED : MOVED + half], late, 2 << shift)
    rim = whole[MOVED + half : MOVED + half + NP]
    return jnp.concatenate([whole[:MOVED], tide] + spread_out(rim, late, shift), 0)


def spread_out(rim, late, shift):
    parts = []
    for k in range(4):
        first = pltpu.roll(rim, (LANES - (k << shift)) % LANES, 1) if k else rim
        last = pltpu.roll(rim, (3 - k) << shift, 1) if k < 3 else rim
        parts.append(jnp.where(late, first, last))
    return parts


def with_row_rim(whole, sums, top):
    north, south = row_edges(sums)
    rim = jnp.where(top, pltpu.roll(north, RING, 1), pltpu.roll(south, LANES - RING, 1))
    parts = [rim[k * NP : (k + 1) * NP] for k in range(4)]
    lane = lax.broadcasted_iota(i32, (1, LANES), 1)
    spots = []
    for k, part in enumerate(parts):
        first = pltpu.roll(part, k * RING, 1) if k else part
        last = pltpu.roll(part, (LANES - (3 - k) * RING) % LANES, 1) if k < 3 else part
        spots.append(jnp.where(top, first, last))
    rim = one_of_four(spots, (lane >> 2) & 3)
    return jnp.concatenate([whole[: MOVED + NODES // 2 + NP], rim], 0)


def in_eight(whole):
    whole = jnp.concatenate([whole, jnp.zeros((8 * CORNER_ROWS - whole.shape[0], LANES), f32)], 0)
    return [whole[k * CORNER_ROWS : (k + 1) * CORNER_ROWS] for k in range(8)]


def corner_of(whole, start, top):
    lane = lax.broadcasted_iota(i32, (1, LANES), 1)
    out = None
    for k, part in enumerate(in_eight(whole)):
        last = pltpu.roll(part, (LANES - start - 48 + 16 * k) % LANES, 1)
        first = pltpu.roll(part, (LANES - start + 16 * k) % LANES, 1)
        part = jnp.where(top != 0, last, first)
        out = part if k == 0 else jnp.where(lane >= 16 * k, part, out)
    return out


def both_corners(whole, odd):
    group = lax.broadcasted_iota(i32, (1, LANES), 1) >> 4
    other_group = (group + jnp.where(odd != 0, 7, 1)) & 7
    first, other = None, None
    for k, part in enumerate(in_eight(whole)):
        part = pltpu.roll(part, (LANES + 16 * k - 48 * odd) & (LANES - 1), 1)
        first = part if k == 0 else jnp.where(group == k, part, first)
        other = part if k == 0 else jnp.where(other_group == k, part, other)
    return first, other


def arrived_corners(far0, far1, block_cols, odd):
    lane = lax.broadcasted_iota(i32, (1, LANES), 1)
    corners = []
    for k in range(8):
        if block_cols == 1:
            part = jnp.where((lane >> 4) == k, far0, far1)
            part = pltpu.roll(part, (LANES + 64 + 16 * (1 - odd) - 16 * k) & (LANES - 1), 1)
        else:
            first = pltpu.roll(far0, (64 - 16 * k) % LANES, 1)
            other = pltpu.roll(far1, (80 - 16 * k) % LANES, 1)
            part = jnp.where((lane & 16) == 0, first, other)
        corners.append(part)
    return jnp.concatenate(corners, 0), ((lane >> 4) & 1) ^ (1 - odd if block_cols == 1 else 0)


def packed(whole):
    second = lax.broadcasted_iota(i32, (1, LANES), 1) >= 64
    top, bottom = whole[:HALF_ROWS], whole[HALF_ROWS:]
    return (
        jnp.where(second, pltpu.roll(bottom, 64, 1), top),
        jnp.where(second, bottom, pltpu.roll(top, 64, 1)),
    )


def unpacked(in0, in1):
    second = lax.broadcasted_iota(i32, (1, LANES), 1) >= 64
    top = jnp.where(second, pltpu.roll(in1, 64, 1), in0)
    bottom = jnp.where(second, in1, pltpu.roll(in0, 64, 1))
    return jnp.concatenate([top, bottom], 0)


def seam_flags(seam_ref, block_cols):
    size_y = seam_ref.shape[1]
    face = lax.axis_index("face")
    blk = lax.axis_index("blk")
    block_x = blk // BY

    def flipped(k):
        return jnp.where(lax.rem(seam_ref[k, 1] - seam_ref[k, 0] + size_y, size_y) != 1, 1, 0)

    first, second = flipped(0), flipped(1)
    east_flip = jnp.where(face == 0, first, second)
    west_flip = jnp.where(face == 0, second, first)
    if block_cols == 1:
        return 1 - east_flip, 0, east_flip, 1
    at_east = jnp.where(block_x == block_cols - 1, east_flip, 0)
    at_west = jnp.where(block_x == 0, west_flip, 0)
    return 1, at_east, 0, at_west


def slots_in(flags_ref):
    return flags_ref[4:5], flags_ref[5:6]


def flags_in(flags_ref, tiles=1):
    return [jnp.concatenate([flags_ref[k : k + 1]] * tiles, 1) for k in range(4)]


def mirrored_first(block_y):
    return (block_y >= BY // 4) & (block_y < BY - BY // 4)


def in_order(block_cols, first, second):
    if block_cols > 1:
        return first, second
    swap = mirrored_first(lax.rem(lax.axis_index("blk"), BY))
    return jnp.where(swap, second, first), jnp.where(swap, first, second)


def strips_kernel(block_cols, *refs):
    sources, (first_ref, then_ref, stored_ref, flags_ref) = refs[:8], refs[8:12]
    buffers, sems = refs[12:20], refs[20]
    copies = [
        pltpu.make_async_copy(source, buffer, sems.at[k])
        for k, (source, buffer) in enumerate(zip(sources, buffers))
    ]
    for copy in copies:
        copy.start()
    seam_ref, slot_ref, fields_ref, area_ref, depth_ref, spin_ref, tide_ref = buffers[:7]
    table_ref = buffers[7]
    for copy in copies[:2]:
        copy.wait()
    east0, flip0, east1, flip1 = flags = seam_flags(seam_ref, block_cols)
    index = lax.broadcasted_iota(i32, (8, LANES), 0)
    flags_ref[...] = sum(jnp.where(index == k, flag, 0) for k, flag in enumerate(flags))
    slots = slot_ref[:, :LANES], slot_ref[:, LANES:]
    flags_ref[4:5], flags_ref[5:6] = slots
    lane = lax.broadcasted_iota(i32, (8, 2 * LANES), 1)
    second = (lane & 64) != 0
    place = lane & 63
    row = place >> 2
    row = jnp.where(jnp.where(second, flip1, flip0) != 0, GY - 1 - row, row)
    east = jnp.where(second, east1, east0) != 0
    col = jnp.where(east, GX - RING, 0) + (place & 3)
    col = jnp.where(lane >= LANES, jnp.where(east, GX - RING - 1, RING), col)
    one_hot = by_slot(slots, col * GY + row)
    for copy in copies[2:7]:
        copy.wait()
    stored = stored_rows(fields_ref, (area_ref, depth_ref, spin_ref, tide_ref))
    both = picked(stored, one_hot)

    lane = lax.broadcasted_iota(i32, (1, LANES), 1)
    second = lane >= 64
    flip = jnp.where(second, flip1, flip0) != 0
    sign = jnp.where(flip, -1.0, 1.0)
    node = lax.broadcasted_iota(i32, (1, NP, 1), 1)

    def turned(values):
        shaped = values.reshape(-1, NP, LANES)
        shaped = pltpu.roll(shaped, 4, 1)
        shaped = jnp.where((node & 2) == 0, pltpu.roll(shaped, 6, 1), pltpu.roll(shaped, 2, 1))
        shaped = jnp.where((node & 1) == 0, pltpu.roll(shaped, 7, 1), pltpu.roll(shaped, 1, 1))
        return shaped.reshape(values.shape)

    strip, ring = (
        [part[k * NODES : (k + 1) * NODES] for k in range(ARRAYS)]
        for part in (both[:, :LANES], both[:, LANES:])
    )
    for copy in copies[7:]:
        copy.wait()
    table, weight = table_ref[: 8 * NP].astype(bf16), table_ref[8 * NP :, :LANES]
    edges = column_edges(table, weight, *ring[:6])
    east = jnp.where(second, east1, east0) != 0
    ends = [jnp.where(east, part[NP:], part[:NP]) for part in edges]
    ends[2] = ends[2] * sign
    strip[2] = strip[2] * sign
    strip[5] = strip[5] * sign
    strips = []
    for part, flip in zip(packed(strip_rows(strip, east, 0, ends)), (flip0, flip1)):
        if isinstance(flip, int):
            strips.append(turned(part) if flip else part)
        else:
            strips.append(jnp.where(flip != 0, turned(part), part))
    first_ref[...], then_ref[...] = in_order(block_cols, *strips)
    stored_ref[...] = stored


def rows_kernel(
    block_cols, flags_ref, stored_ref, first_ref, then_ref, table_ref, weight_ref,
    next_ref, far0_ref, far1_ref, pair_ref, sums,
):
    east0, flip0, east1, flip1 = flags_in(flags_ref)
    odd = lax.axis_index("blk") & 1
    lane = lax.broadcasted_iota(i32, (8, 2 * LANES), 1)
    row = jnp.where(odd != 0, GY - RING, 0) + ((lane & 63) >> 4)
    row = jnp.where((lane & 64) != 0, jnp.where(odd != 0, GY - RING - 1, RING), row)
    five = jnp.where(odd != 0, 0, GY - RING - 1) + jnp.minimum((lane & (LANES - 1)) >> 4, RING)
    row = jnp.where(lane >= LANES, five, row)
    both = picked(stored_ref[...], by_slot(slots_in(flags_ref), (lane & 15) * GY + row))
    pair_ref[...] = both[:, LANES:]
    rows = [both[k * NODES : (k + 1) * NODES, :LANES] for k in range(ARRAYS)]
    whole = unpacked(*in_order(block_cols, first_ref[...], then_ref[...]))
    strip = [whole[k * NODES : (k + 1) * NODES] for k in range(6)]
    edges = edge_values(table_ref, weight_ref, *map(beside, strip, rows[:6]))
    sums[0] = jnp.concatenate([part[:, :LANES] for part in edges], 0)
    lane = lax.broadcasted_iota(i32, (1, LANES), 1)
    top0, top1 = odd ^ flip0, odd ^ flip1
    whole = with_row_rim(whole, sums, jnp.where(lane >= 64, top1, top0) != 0)
    if block_cols == 1:
        far0_ref[...], far1_ref[...] = both_corners(whole, odd)
    else:
        far0_ref[...] = corner_of(whole, 0, top0)
        far1_ref[...] = corner_of(whole, 64, top1)
    sums[0] = jnp.concatenate([part[:, LANES:] for part in edges], 0)
    up = jnp.broadcast_to(odd != 0, (1, LANES))
    rim = pltpu.roll(jnp.where(up, *row_edges(sums)), 64, 1)
    rim = [rim[k * NP : (k + 1) * NP] for k in range(4)]
    whole = strip_rows(rows, up, 4, rim)
    top, bottom = whole[:HALF_ROWS], whole[HALF_ROWS:]
    next_ref[...] = jnp.where(lane >= 64, pltpu.roll(bottom, 64, 1), top)


def corners_kernel(block_cols, flags_ref, first_ref, then_ref, pair_ref, _, out_ref):
    east0, flip0, east1, flip1 = flags_in(flags_ref)
    in0, in1 = in_order(block_cols, first_ref[...], then_ref[...])
    top = 1 - (lax.axis_index("blk") & 1)
    lane = lax.broadcasted_iota(i32, (1, LANES), 1)
    halves = []
    for start in (0, 64):
        at0 = jnp.where(top != 0, 36, 80)
        at1 = jnp.where(top != 0, 56, 100)
        first = pltpu.roll(in0, (at0 - start) & (LANES - 1), 1)
        other = pltpu.roll(in1, (at1 - start) & (LANES - 1), 1)
        halves.append(jnp.where(lane < 100, first, other))
    late = jnp.where(lane < 100, east0, east1) == 0
    whole = placed_rows(jnp.concatenate(halves, 0), late, 0)
    out_ref[:ROWS] = jnp.where(lane < 80, pair_ref[...], whole[:ROWS])
    out_ref[ROWS:] = whole[ROWS:]


def own_kernel(flags_ref, stored_ref, lanes_ref, own_ref, hot_ref):
    one_hot = by_slot(slots_in(flags_ref), lanes_ref[0:8, :MID])
    own_ref[...] = picked(stored_ref[...], one_hot)
    hot_ref[...] = one_hot.astype(f32).T.astype(bf16)


def first_sums(table, weight, parts, rims, at_rim):
    p, u, v, area, depth, spin, tide = parts
    size = area.shape[1]
    root = jnp.sqrt(area)
    mass = jnp.concatenate([weight] * (size // LANES), 1) * area
    used = [p, u, v, root * depth, root, mass * spin, tide]
    for part, rim in zip(mass_tendency(table, p, u, v, *used[3:6]) + [mass], rims):
        west, east = part[:NP], part[NODES - NP :]
        at_east = jnp.where(at_rim, rim, pltpu.roll(west, size - 1, 1))
        at_west = jnp.where(at_rim, rim, pltpu.roll(east, 1, 1))
        used.append(
            jnp.concatenate([west + at_west, part[NP : NODES - NP], east + at_east], 0)
        )
    return used


def middle_kernel(
    block_cols, flags_ref, first_ref, then_ref, own_ref, lanes_ref, table_ref, weight_ref,
    low_ref, centre_ref, high_ref,
):
    east0, flip0, east1, flip1 = flags_in(flags_ref)
    second = lax.broadcasted_iota(i32, (1, LANES), 1) >= 64
    late = jnp.where(second, east1, east0) == 0
    whole = unpacked(*in_order(block_cols, first_ref[...], then_ref[...]))
    whole = placed_rows(whole, late, 0)
    side = lanes_ref[16:24, :MID]
    east = flags_in(flags_ref, MID // LANES)[0]
    first_at = jnp.where(side == 2, 64 * (1 - east), 64 * east)
    place = jnp.where(side == 0, -1, lanes_ref[8:16, :MID] + first_at)
    placed = picked(whole, as_one_hot(place, LANES))
    parts = [
        placed[k * NODES : (k + 1) * NODES] + own_ref[k * NODES : (k + 1) * NODES]
        for k in range(ARRAYS)
    ]
    rims = [placed[ROWS + c * NP : ROWS + (c + 1) * NP] for c in range(4)]
    at_rim = lanes_ref[24:25, LANES : LANES + MID] != 0
    used = first_sums(table_ref[...], weight_ref[...], parts, rims, at_rim)
    for k, ref in enumerate((low_ref, centre_ref, high_ref)):
        for n, part in enumerate(used):
            ref[n * NODES : (n + 1) * NODES] = part[:, k * LANES : (k + 1) * LANES]


def far_kernel(block_cols, flags_ref, far1_ref, far0_ref, next_ref, _, out_ref):
    east0, flip0, east1, flip1 = flags_in(flags_ref)
    odd = lax.axis_index("blk") & 1
    lane = lax.broadcasted_iota(i32, (1, LANES), 1)
    below = jnp.broadcast_to(odd == 0, (1, LANES))
    strip = jnp.concatenate([next_ref[...], pltpu.roll(next_ref[...], 64, 1)], 0)
    strip = placed_rows(strip, below, 4)
    corners, strip_of = arrived_corners(far0_ref[...], far1_ref[...], block_cols, odd)
    late = jnp.where(strip_of != 0, east1, east0) == 0
    rim = MOVED + NODES // 2 + NP
    rim = jnp.concatenate(spread_out(corners[rim : rim + NP], below, 2), 0)
    corners = placed_rows(corners, late, 0)
    own = lane < 64
    out_ref[:ROWS] = jnp.where(own, strip[:ROWS], corners[:ROWS])
    out_ref[ROWS:ALL_ROWS] = corners[ROWS:]
    out_ref[ALL_ROWS:] = jnp.where(own, strip[ROWS:], rim)


def steps_kernel(
    block_cols, flags_ref, pair_ref, next_ref, low_ref, centre_ref,
    high_ref, hot_ref, table_ref, weight_ref, lanes_ref, out_ref, sums,
):
    east0, flip0, east1, flip1 = flags_in(flags_ref)
    odd = lax.axis_index("blk") & 1
    block_y = lax.rem(lax.axis_index("blk"), BY)

    lane = lax.broadcasted_iota(i32, (1, LANES), 1)
    pair = jnp.concatenate([pair_ref[...], jnp.zeros((EDGE_ROWS, LANES), f32)], 0)
    around = beside(pair, next_ref[...])
    outer_at = [lanes_ref[32 + 8 * k : 40 + 8 * k, : 2 * LANES] for k in range(4)]
    kind = outer_at[1]
    from_pair = jnp.where(outer_at[2] != 0, 1 - odd, odd) != 0
    east = flags_in(flags_ref, 2)[0]
    strip_at = jnp.where(kind == 3, 1 - east, east)
    far_at = strip_at ^ (1 - odd) if block_cols == 1 else strip_at
    strip_at, far_at = (jnp.where(kind > 1, at, 0) for at in (strip_at, far_at))
    place = jnp.where(
        from_pair,
        outer_at[0] + (RING + 1) * RING * strip_at,
        jnp.where(outer_at[3] < 0, -1, outer_at[3] + RING * RING * far_at),
    )
    outer = picked(around, as_one_hot(jnp.where(kind == 0, -1, place), 2 * LANES))
    table = table_ref[...]
    tiles = (None, low_ref, centre_ref, high_ref, None)
    count = len(tiles)
    masks = [lanes_ref[24:32, k * LANES : (k + 1) * LANES] for k in range(count)]
    closed_above = jnp.where(block_y == BY - 1, masks[-2][1:2], 0) != 0
    closed_below = jnp.where(block_y == 0, masks[1][2:3], 0) != 0
    first_row = jnp.where(odd == 0, masks[0][4:5], 0) != 0
    last_row = jnp.where(odd != 0, masks[-1][5:6], 0) != 0
    outer_used = first_sums(
        table,
        weight_ref[...],
        [outer[k * NODES : (k + 1) * NODES] for k in range(ARRAYS)],
        [outer[ROWS + c * NP : ROWS + (c + 1) * NP] for c in range(4)],
        beside(masks[0][0:1], masks[-1][0:1]) != 0,
    )

    def shifted(parts, by, ring):
        turned = [pltpu.roll(part, -by % LANES, 1) for part in parts]
        size = len(parts)
        step = 1 if by > 0 else -1
        others = [(k + step) % size if ring else min(max(k + step, 0), size - 1) for k in range(size)]
        from_other = lane >= LANES - by if by > 0 else lane < -by
        return [jnp.where(from_other, turned[others[k]], turned[k]) for k in range(size)]

    def put_x_sums(groups, components):
        slots = [k for group in groups for k in group]
        ring = len(slots) < count
        per_tile = [
            [part[:, n * LANES : (n + 1) * LANES] for part in parts]
            for group, parts in zip(groups, components)
            for n in range(len(group))
        ]
        for c in range(3):
            parts = [tile[c] for tile in per_tile]
            west = [part[:NP] for part in parts]
            east = [part[NODES - NP :] for part in parts]
            at_east, at_west = shifted(west, 1, ring), shifted(east, -1, ring)
            for n, k in enumerate(slots):
                sums[k, c * NODES : c * NODES + NP] = west[n] + at_west[n]
                sums[k, c * NODES + NP : (c + 1) * NODES - NP] = parts[n][NP : NODES - NP]
                sums[k, (c + 1) * NODES - NP : (c + 1) * NODES] = east[n] + at_east[n]

    def edge_y(components, slots, rows=None):
        ring = len(slots) < count
        south_at = pl.ds(0, components * NP, stride=NP)
        north_at = pl.ds(NP - 1, components * NP, stride=NP)
        south = [sums[k, south_at] for k in slots]
        north = [sums[k, north_at] for k in slots]
        at_north, at_south = shifted(south, PITCH, ring), shifted(north, -PITCH, ring)
        for n, k in enumerate(slots):
            if k == count - 2:
                at_north[n] = jnp.where(closed_above, 0.0, at_north[n])
            if k == 1:
                at_south[n] = jnp.where(closed_below, 0.0, at_south[n])
        if rows is not None:
            at_south[0] = jnp.where(first_row, rows[0], at_south[0])
            at_north[-1] = jnp.where(last_row, rows[1], at_north[-1])
        for n, k in enumerate(slots):
            sums[k, south_at] = south[n] + at_south[n]
            sums[k, north_at] = north[n] + at_north[n]

    node = lax.broadcasted_iota(i32, (1, NP, 1), 1)
    rows = []
    for rim in (outer[ALL_ROWS:, :LANES], outer[ALL_ROWS:, LANES:]):
        east = pltpu.roll(rim, LANES - 1, 1).reshape(4, NP, LANES)
        west = pltpu.roll(rim, 1, 1).reshape(4, NP, LANES)
        rim = (
            rim.reshape(4, NP, LANES)
            + jnp.where(node == NP - 1, pltpu.roll(east, NP - 1, 1), 0.0)
            + jnp.where(node == 0, pltpu.roll(west, 1, 1), 0.0)
        )
        rows.append(rim.reshape(EDGE_ROWS, LANES))

    every = tuple(range(count))
    groups = (every[0:2], every[2:4], every[4:])

    def tile_part(k, n):
        if tiles[k] is None:
            return outer_used[n][:, :LANES] if k == 0 else outer_used[n][:, LANES:]
        return tiles[k][n * NODES : (n + 1) * NODES]

    def part_of(group, n):
        return jnp.concatenate([tile_part(k, n) for k in group], 1)

    def summed(group, c):
        return jnp.concatenate([sums[k, c * NODES : (c + 1) * NODES] for k in group], 1)

    def average(group, per_mass):
        return [summed(group, c) * per_mass for c in range(3)]

    def laplace(s):
        return [
            dot(table[4 * NODES :, : 3 * NODES], jnp.concatenate(high_low_high(part), 0))
            for part in s
        ]

    start = [[part_of(group, n) for n in range(3)] for group in groups]
    fixed = [[part_of(group, n) for n in range(3, 6)] for group in groups]
    for k in every:
        for c in range(4):
            sums[k, c * NODES : (c + 1) * NODES] = tile_part(k, 7 + c)
    edge_y(4, every, rows)
    per_mass = [1.0 / summed(group, 3) for group in groups]
    one = []
    for n, group in enumerate(groups):
        change = average(group, per_mass[n])
        one.append([s + time_step * c for s, c in zip(start[n], change)])
    put_x_sums(groups, [mass_tendency(table, *s, *f) for s, f in zip(one, fixed)])
    edge_y(3, every)
    two = []
    for n, group in enumerate(groups):
        change = average(group, per_mass[n])
        two.append(
            [0.75 * s + 0.25 * (o + time_step * c) for s, o, c in zip(start[n], one[n], change)]
        )
    put_x_sums(groups, [mass_tendency(table, *s, *f) for s, f in zip(two, fixed)])
    edge_y(3, every)

    def regrouped(per_group):
        (outer_low, high_above) = per_group[0], per_group[1]
        below, low = outer_low[:, :LANES], outer_low[:, LANES:]
        centre, high = high_above[:, :LANES], high_above[:, LANES:]
        near = jnp.where(lane < LANES // 2, per_group[2], below)
        return [beside(low, centre), beside(high, near)]

    def of_groups(values):
        return [list(parts) for parts in zip(*(regrouped(part) for part in zip(*values)))]

    for c in range(3):
        rows_at = slice(c * NODES, (c + 1) * NODES)
        sums[count - 1, rows_at] = jnp.where(
            lane < LANES // 2, sums[count - 1, rows_at], sums[0, rows_at]
        )
    slots = every[1:]
    groups = (slots[0:2], slots[2:4])
    start, two = of_groups(start), of_groups(two)
    tide = regrouped([part_of(every[0:2], 6), part_of(every[2:4], 6), part_of(every[4:], 6)])
    per_mass = regrouped(per_mass)
    three = []
    for n, group in enumerate(groups):
        change = average(group, per_mass[n])
        now = [
            s / 3.0 + 2.0 / 3.0 * (o + time_step * c)
            for s, o, c in zip(start[n], two[n], change)
        ]
        now[0] = now[0] + tide[n]
        three.append(now)
    put_x_sums(groups, [laplace(s) for s in three])
    edge_y(3, slots)
    change = [average(group, per_mass[n]) for n, group in enumerate(groups)]
    put_x_sums(groups, [laplace(s) for s in change])
    edge_y(3, slots)
    stepped = []
    for n, group in enumerate(groups):
        change = average(group, per_mass[n])
        now = [s - time_step * hyper_coeff * b for s, b in zip(three[n], change)]
        stepped.append(jnp.concatenate(now, 0))
    stepped = jnp.concatenate(stepped, 1)[:, :MID]
    own = lanes_ref[27:28, LANES : LANES + MID] != 0
    stored = picked(jnp.where(own, stepped, 0.0), hot_ref[...])
    out_ref[...] = stored.reshape(out_ref.shape)


def on_device(fields, jacobian, water_depth, coriolis, tide_height, slot_of, seam_rows):
    block_cols = lax.axis_size("blk") // BY
    table, weight, edge_table, lanes = map(jnp.asarray, (*operator_table(), lane_tables()))
    vmem = pl.BlockSpec(memory_space=pltpu.VMEM)
    hbm = pl.BlockSpec(memory_space=pltpu.HBM)
    params = pltpu.CompilerParams(vmem_limit_bytes=48 * 2**20)
    held = (fields, jacobian, water_depth, coriolis, tide_height)

    def call(kernel, ins, outs, cost, scratch=(), name=None):
        return pl.pallas_call(
            kernel,
            out_shape=[jax.ShapeDtypeStruct(*out) for out in outs],
            in_specs=[spec for spec, value in ins],
            out_specs=[vmem] * len(outs),
            scratch_shapes=list(scratch),
            compiler_params=params,
            cost_estimate=pl.CostEstimate(
                flops=cost, bytes_accessed=2 * 2**20, transcendentals=0
            ),
            name=name,
        )(
            *[
                pltpu.with_memory_space_constraint(value, pltpu.HBM) if spec is hbm else value
                for spec, value in ins
            ]
        )

    strip = ((HALF_ROWS, LANES), f32)
    def room(values, spaces=None):
        spaces = spaces or [pltpu.VMEM] * len(values)
        buffers = [space(x.shape, x.dtype) for space, x in zip(spaces, values)]
        return buffers + [pltpu.SemaphoreType.DMA((len(values),))]

    needed = (seam_rows, slot_of, *held, edge_table)
    corner = ((CORNER_ROWS, LANES), f32)
    scratch = [pltpu.VMEM((1, 4 * NODES, LANES), f32)]
    first, then, stored, flags = call(
        functools.partial(strips_kernel, block_cols),
        [(hbm, x) for x in needed],
        [strip, strip, ((ROWS, ELEMENTS), f32), ((8, LANES), i32)],
        10**8,
        scratch=room(needed, [pltpu.SMEM] + [pltpu.VMEM] * (len(needed) - 1)),
        name="strips",
    )
    to_next, far0, far1, to_pair = call(
        functools.partial(rows_kernel, block_cols),
        [(vmem, x) for x in (flags, stored, first, then, table, weight)],
        [strip, corner, corner, ((ROWS, LANES), f32)],
        10**8,
        scratch=scratch,
        name="rows",
    )
    span = block_cols * BY
    both = ("face", "blk")
    places = [(f, x, y) for f in range(2) for x in range(block_cols) for y in range(BY)]

    def rank(face, block_x, block_y):
        return face * span + block_x * BY + block_y

    def same(y):
        return y

    def in_pair(y):
        return y ^ 1

    def next_pair(y):
        other = y + 1 if y % 2 else y - 1
        return other if 0 <= other < BY else y

    def swapped(value, partner):
        pairs = [
            (rank(f, x, y), rank(f if partner(y) != y else 1 - f, x, partner(y)))
            for f, x, y in places
        ]
        return lax.ppermute(value, both, pairs)

    def across(value0, value1, partner):
        last = block_cols - 1

        def aligned(y):
            return partner is same or partner(y) != y

        straight = {
            (f, x, y): (f, x + 1, partner(y)) if x < last else (1 - f, 0, partner(y))
            for f, x, y in places
        }
        turned = {
            (f, last, y): (1 - f, 0, BY - 1 - partner(y) if aligned(y) else y)
            for f in range(2)
            for y in range(BY)
        }

        def eastward(value, pairs):
            return lax.ppermute(value, both, [(rank(*a), rank(*b)) for a, b in pairs.items()])

        def westward(value, pairs):
            return lax.ppermute(value, both, [(rank(*b), rank(*a)) for a, b in pairs.items()])

        if block_cols == 1:
            return eastward(value0, straight), eastward(value1, turned)
        flipped = (seam_rows[:, 1] - seam_rows[:, 0]) % seam_rows.shape[1] != 1
        face = lax.axis_index("face")
        block_x = lax.axis_index("blk") // BY
        return (
            jnp.where(
                (block_x == last) & flipped[face],
                westward(value1, turned),
                westward(value1, straight),
            ),
            jnp.where(
                (block_x == 0) & flipped[1 - face],
                eastward(value0, turned),
                eastward(value0, straight),
            ),
        )

    if block_cols == 1:
        halos = []
        for value, mirrored in ((first, mirrored_first), (then, lambda y: not mirrored_first(y))):
            pairs = [
                (rank(f, x, y), rank(1 - f, x, BY - 1 - y if mirrored(y) else y))
                for f, x, y in places
            ]
            halos.append(lax.ppermute(value, both, pairs))
        halo0, halo1 = halos
    else:
        halo0, halo1 = across(first, then, same)
    far0, far1 = across(far0, far1, next_pair)
    from_next = swapped(to_next, next_pair)
    own, hot = call(
        own_kernel,
        [(vmem, x) for x in (flags, stored, lanes)],
        [((ROWS, MID), f32), ((MID, ELEMENTS), bf16)],
        10**8,
        name="own",
    )
    (to_pair,) = call(
        functools.partial(corners_kernel, block_cols),
        [(vmem, x) for x in (flags, halo0, halo1, to_pair, hot)],
        [((ALL_ROWS, LANES), f32)],
        10**8,
        name="corners",
    )
    from_pair = swapped(to_pair, in_pair)
    tile = ((11 * NODES, LANES), f32)
    low, centre, high = call(
        functools.partial(middle_kernel, block_cols),
        [(vmem, x) for x in (flags, halo0, halo1, own, lanes, table, weight)],
        [tile, tile, tile],
        10**8,
        name="middle",
    )
    (from_next,) = call(
        functools.partial(far_kernel, block_cols),
        [(vmem, x) for x in (flags, far1, far0, from_next, low)],
        [((RIM_ROWS, LANES), f32)],
        10**11,
        name="far",
    )
    (stepped,) = call(
        functools.partial(steps_kernel, block_cols),
        [
            (vmem, x)
            for x in (
                flags, from_pair, from_next, low, centre, high, hot, table, weight, lanes
            )
        ],
        [(fields.shape, f32)],
        10**8,
        scratch=[pltpu.VMEM((EXT // LANES, 4 * NODES, LANES), f32)],
        name="steps",
    )
    return stepped


def solution(mesh):
    return jax.shard_map(
        on_device,
        mesh=mesh,
        in_specs=(
            P(None, None, None, ("face", "blk")),
            P(None, None, ("face", "blk")),
            P(None, None, ("face", "blk")),
            P(None, None, ("face", "blk")),
            P(None, None, ("face", "blk")),
            P(("face", "blk"), None),
            P(),
        ),
        out_specs=P(None, None, None, ("face", "blk")),
        check_vma=False,
    )
```

```python
import functools
import math

import jax
import jax.numpy as jnp
import ml_dtypes
import numpy as np
from jax import lax
from jax.experimental import pallas as pl
from jax.experimental.pallas import tpu as pltpu
from jax.sharding import PartitionSpec as P

BY = 16
GX = 16
GY = 16
NP = 8
NODES = NP * NP
ARRAYS = 7
ROWS = ARRAYS * NODES
MOVED = 6 * NODES
EDGE_ROWS = 4 * NP
ALL_ROWS = ROWS + EDGE_ROWS
HALF_ROWS = (MOVED + NODES // 2 + 2 * NP) // 2
RING = 4
RIM_ROWS = ROWS + 2 * EDGE_ROWS
CORNER_ROWS = (MOVED + NODES // 2 + 4 * NP) // 8
PITCH = GX + 2 * RING
MID = GY * PITCH
LANES = 128
EXT = MID + 2 * LANES
LEAD = LANES - RING * PITCH
ELEMENTS = GX * GY

time_step = 0.03
hyper_coeff = 0.0002

f32 = jnp.float32
bf16 = jnp.bfloat16
i32 = jnp.int32


def legendre_pair(location, degree):
    lower_value = 1.0
    upper_value = location
    for polynomial_order in range(2, degree + 1):
        lower_value, upper_value = (
            upper_value,
            (
                (2 * polynomial_order - 1) * location * upper_value
                - (polynomial_order - 1) * lower_value
            )
            / polynomial_order,
        )
    return (lower_value, upper_value)


def gll_tables(points):
    degree = points - 1
    locations = [-math.cos(math.pi * position / degree) for position in range(points)]
    for iteration in range(100):
        updated = []
        for location in locations:
            lower_value, upper_value = legendre_pair(location, degree)
            updated.append(
                location - (location * upper_value - lower_value) / ((degree + 1) * upper_value)
            )
        locations = updated
    locations[0] = -1.0
    locations[degree] = 1.0
    legendre_at = [legendre_pair(location, degree)[1] for location in locations]
    weights = [2.0 / (degree * (degree + 1) * value * value) for value in legendre_at]
    corner_value = degree * (degree + 1) / 4.0
    derivative = []
    for row_index in range(points):
        row_values = []
        for column_index in range(points):
            if row_index != column_index:
                row_values.append(
                    legendre_at[row_index]
                    / (legendre_at[column_index] * (locations[row_index] - locations[column_index]))
                )
            elif row_index == 0:
                row_values.append(-corner_value)
            elif row_index == degree:
                row_values.append(corner_value)
            else:
                row_values.append(0.0)
        derivative.append(row_values)
    return np.asarray(weights, np.float64), np.asarray(derivative, np.float64)


def in_three(matrix):
    high = matrix.astype(ml_dtypes.bfloat16)
    low = (matrix - high.astype(np.float64)).astype(ml_dtypes.bfloat16)
    return np.concatenate([high, high, low], 1)


def operator_table():
    weights, derivative = gll_tables(NP)
    eye = np.eye(NP)
    node_weight = np.outer(weights, weights).reshape(NODES, 1)
    along_x = node_weight * np.kron(derivative, eye)
    along_y = node_weight * np.kron(eye, derivative)
    second = derivative @ derivative
    both = node_weight * (np.kron(second, eye) + np.kron(eye, second))
    table = np.zeros((5 * NODES, 4 * NODES), ml_dtypes.bfloat16)
    table[:NODES, : 3 * NODES] = in_three(along_x)
    table[NODES : 2 * NODES, : 3 * NODES] = in_three(along_y)
    flux = [in_three(along_x), in_three(along_y)]
    for k, part in enumerate(flux):
        at = 2 * k * NODES
        table[2 * NODES : 3 * NODES, at : at + 2 * NODES] = part[:, : 2 * NODES]
        table[3 * NODES : 4 * NODES, at : at + NODES] = part[:, 2 * NODES :]
    table[4 * NODES :, : 3 * NODES] = in_three(both)
    table = table.astype(np.float32)
    spread = np.broadcast_to(node_weight, (NODES, LANES)).astype(np.float32)
    ends = np.r_[:NP, NODES - NP : NODES]
    edge_table = np.zeros((10 * NP, 4 * NODES), np.float32)
    for k in range(4):
        edge_table[2 * k * NP : 2 * (k + 1) * NP] = table[k * NODES + ends]
    edge_table[8 * NP :, :LANES] = spread[ends]
    return table, np.ascontiguousarray(spread), edge_table


def lane_tables():
    table = np.zeros((24, MID), np.int32)
    for lane in range(MID):
        row, col = divmod(lane, PITCH)
        x = col - RING
        own = 0 <= x < GX
        table[0:8, lane] = x * GY + row if own else -1
        if not own:
            table[8:16, lane] = row * RING + (col if x < 0 else x - GX)
        table[16:24, lane] = 0 if own else (1 if x < 0 else 2)
    ext = np.zeros((8, EXT), np.int32)
    outer = np.zeros((32, 2 * LANES), np.int32)
    for lane in range(EXT):
        row, col = divmod(lane - LEAD, PITCH)
        y = row - RING
        x = col - RING
        ext[0, lane] = x in (-RING, GX + RING - 1)
        ext[1, lane] = y == GY - 1
        ext[2, lane] = y == 0
        ext[3, lane] = 0 <= y < GY and 0 <= x < GX
        ext[4, lane] = y == -RING
        ext[5, lane] = y == GY + RING - 1
        if -RING - 1 <= y < 0 or GY <= y <= GY + RING:
            place = lane if y < 0 else lane - MID
            step = y + RING if y < 0 else y - GY
            near = step + 1 if y < 0 else step
            far = 0 <= step < RING
            if 0 <= x < GX:
                outer[0:8, place] = near * GX + x
                outer[8:16, place] = 1
                outer[24:32, place] = LANES + step * GX + x if far else -1
            else:
                across = x + RING if x < 0 else x - GX
                outer[0:8, place] = (RING + 1) * GX + near * RING + across
                outer[8:16, place] = 2 if x < 0 else 3
                outer[24:32, place] = LANES + RING * GX + step * RING + across if far else -1
            outer[16:24, place] = y > 0
    whole = np.zeros((64, EXT), np.int32)
    whole[0:24, :MID] = table
    whole[24:32] = ext
    whole[32:64, : 2 * LANES] = outer
    return whole


def dot(a, b):
    return jnp.dot(a, b, preferred_element_type=f32)


def picked(values, one_hot):
    high = values.astype(bf16)
    low = (values - high.astype(f32)).astype(bf16)
    both = dot(jnp.concatenate([high, low], 0), one_hot)
    return both[: values.shape[0]] + both[values.shape[0] :]


def as_one_hot(row_of_lane, depth):
    index = lax.broadcasted_iota(i32, (depth, row_of_lane.shape[1]), 0)
    return jnp.where(index == row_of_lane[0:1], 1.0, 0.0).astype(bf16)


def high_low_high(values):
    high = values.astype(bf16)
    low = (values - high.astype(f32)).astype(bf16)
    return [high, low, high]


def by_slot(halves, cell_of_lane):
    size = cell_of_lane.shape[1]
    halves = [jnp.broadcast_to(half, (8, LANES)) for half in halves]
    chosen = []
    for k in range(size // LANES):
        cell = cell_of_lane[:, k * LANES : (k + 1) * LANES]
        low, high = (jnp.take_along_axis(half, cell & (LANES - 1), axis=1) for half in halves)
        chosen.append(jnp.where(cell < 0, -1, jnp.where(cell < LANES, low, high)))
    return as_one_hot(jnp.concatenate(chosen, 1), ELEMENTS)


def stored_rows(fields_ref, others):
    fields = fields_ref[...].reshape(3 * NODES, ELEMENTS)
    others = [ref[...].reshape(NODES, ELEMENTS) for ref in others]
    return jnp.concatenate([fields[:NODES] - others[-1], fields[NODES:]] + others, 0)


def mass_tendency(table, p, u, v, area_depth, weighted_area, spin):
    slopes = dot(table[: 2 * NODES, : 3 * NODES], jnp.concatenate(high_low_high(p), 0))
    flux = high_low_high(area_depth * u)[:2] + high_low_high(area_depth * v)[:2]
    spread = dot(table[2 * NODES : 4 * NODES], jnp.concatenate(flux, 0))
    return [
        -(spread[:NODES] + spread[NODES:]),
        spin * v - weighted_area * slopes[:NODES],
        -spin * u - weighted_area * slopes[NODES:],
    ]


def edge_values(table_ref, weight_ref, p, u, v, area, depth, spin):
    root = jnp.sqrt(area)
    mass = jnp.concatenate([weight_ref[...]] * (area.shape[1] // LANES), 1) * area
    table = table_ref[...].astype(bf16)
    return mass_tendency(table, p, u, v, root * depth, root, mass * spin) + [mass]


def column_edges(table, weight, p, u, v, area, depth, spin):
    def ends(part):
        return jnp.concatenate([part[:NP], part[NODES - NP :]], 0)

    root = jnp.sqrt(area)
    area_depth = root * depth
    root, mass = ends(root), weight * ends(area)
    weighted_spin = mass * ends(spin)
    slopes = dot(table[: 4 * NP, : 3 * NODES], jnp.concatenate(high_low_high(p), 0))
    flux = high_low_high(area_depth * u)[:2] + high_low_high(area_depth * v)[:2]
    spread = dot(table[4 * NP :], jnp.concatenate(flux, 0))
    return [
        -(spread[: 2 * NP] + spread[2 * NP :]),
        weighted_spin * ends(v) - root * slopes[: 2 * NP],
        -weighted_spin * ends(u) - root * slopes[2 * NP :],
        mass,
    ]


def row_edges(sums):
    return tuple(sums[0, pl.ds(j, EDGE_ROWS, stride=NP)] for j in (NP - 1, 0))


def beside(left, right):
    return jnp.concatenate([left, right], 1)


def one_of_four(parts, index):
    out = parts[0]
    for k in range(1, 4):
        out = jnp.where(index == k, parts[k], out)
    return out


def folded(tide, kept, late, step):
    half = NODES // 2
    back = pltpu.roll(tide[half:], LANES - step, 1)
    onward = pltpu.roll(tide[half:], step, 1)
    return jnp.where(kept, tide[:half], jnp.where(late, back, onward))


def unfolded(rows, late, step):
    back = pltpu.roll(rows, LANES - step, 1)
    onward = pltpu.roll(rows, step, 1)
    return jnp.concatenate([rows, jnp.where(late, onward, back)], 0)


def strip_rows(parts, late, shift, rims):
    lane = lax.broadcasted_iota(i32, (1, LANES), 1)
    index = (lane >> shift) & 3
    kept = jnp.where(late, index // 2, 1 - index // 2) != 0
    tide = folded(parts[6], kept, late, 2 << shift)
    rim = one_of_four(rims, index)
    return jnp.concatenate(parts[:6] + [tide, rim, jnp.zeros_like(rim)], 0)


def placed_rows(whole, late, shift):
    half = NODES // 2
    tide = unfolded(whole[MOVED : MOVED + half], late, 2 << shift)
    rim = whole[MOVED + half : MOVED + half + NP]
    return jnp.concatenate([whole[:MOVED], tide] + spread_out(rim, late, shift), 0)


def spread_out(rim, late, shift):
    parts = []
    for k in range(4):
        first = pltpu.roll(rim, (LANES - (k << shift)) % LANES, 1) if k else rim
        last = pltpu.roll(rim, (3 - k) << shift, 1) if k < 3 else rim
        parts.append(jnp.where(late, first, last))
    return parts


def with_row_rim(whole, sums, top):
    north, south = row_edges(sums)
    rim = jnp.where(top, pltpu.roll(north, RING, 1), pltpu.roll(south, LANES - RING, 1))
    parts = [rim[k * NP : (k + 1) * NP] for k in range(4)]
    lane = lax.broadcasted_iota(i32, (1, LANES), 1)
    spots = []
    for k, part in enumerate(parts):
        first = pltpu.roll(part, k * RING, 1) if k else part
        last = pltpu.roll(part, (LANES - (3 - k) * RING) % LANES, 1) if k < 3 else part
        spots.append(jnp.where(top, first, last))
    rim = one_of_four(spots, (lane >> 2) & 3)
    return jnp.concatenate([whole[: MOVED + NODES // 2 + NP], rim], 0)


def in_eight(whole):
    whole = jnp.concatenate([whole, jnp.zeros((8 * CORNER_ROWS - whole.shape[0], LANES), f32)], 0)
    return [whole[k * CORNER_ROWS : (k + 1) * CORNER_ROWS] for k in range(8)]


def corner_of(whole, start, top):
    lane = lax.broadcasted_iota(i32, (1, LANES), 1)
    out = None
    for k, part in enumerate(in_eight(whole)):
        last = pltpu.roll(part, (LANES - start - 48 + 16 * k) % LANES, 1)
        first = pltpu.roll(part, (LANES - start + 16 * k) % LANES, 1)
        part = jnp.where(top != 0, last, first)
        out = part if k == 0 else jnp.where(lane >= 16 * k, part, out)
    return out


def both_corners(whole, odd):
    group = lax.broadcasted_iota(i32, (1, LANES), 1) >> 4
    other_group = (group + jnp.where(odd != 0, 7, 1)) & 7
    first, other = None, None
    for k, part in enumerate(in_eight(whole)):
        part = pltpu.roll(part, (LANES + 16 * k - 48 * odd) & (LANES - 1), 1)
        first = part if k == 0 else jnp.where(group == k, part, first)
        other = part if k == 0 else jnp.where(other_group == k, part, other)
    return first, other


def arrived_corners(far0, far1, block_cols, odd):
    lane = lax.broadcasted_iota(i32, (1, LANES), 1)
    corners = []
    for k in range(8):
        if block_cols == 1:
            part = jnp.where((lane >> 4) == k, far0, far1)
            part = pltpu.roll(part, (LANES + 64 + 16 * (1 - odd) - 16 * k) & (LANES - 1), 1)
        else:
            first = pltpu.roll(far0, (64 - 16 * k) % LANES, 1)
            other = pltpu.roll(far1, (80 - 16 * k) % LANES, 1)
            part = jnp.where((lane & 16) == 0, first, other)
        corners.append(part)
    return jnp.concatenate(corners, 0), ((lane >> 4) & 1) ^ (1 - odd if block_cols == 1 else 0)


def packed(whole):
    second = lax.broadcasted_iota(i32, (1, LANES), 1) >= 64
    top, bottom = whole[:HALF_ROWS], whole[HALF_ROWS:]
    return (
        jnp.where(second, pltpu.roll(bottom, 64, 1), top),
        jnp.where(second, bottom, pltpu.roll(top, 64, 1)),
    )


def unpacked(in0, in1):
    second = lax.broadcasted_iota(i32, (1, LANES), 1) >= 64
    top = jnp.where(second, pltpu.roll(in1, 64, 1), in0)
    bottom = jnp.where(second, in1, pltpu.roll(in0, 64, 1))
    return jnp.concatenate([top, bottom], 0)


def seam_flags(seam_ref, block_cols):
    size_y = seam_ref.shape[1]
    face = lax.axis_index("face")
    blk = lax.axis_index("blk")
    block_x = blk // BY

    def flipped(k):
        return jnp.where(lax.rem(seam_ref[k, 1] - seam_ref[k, 0] + size_y, size_y) != 1, 1, 0)

    first, second = flipped(0), flipped(1)
    east_flip = jnp.where(face == 0, first, second)
    west_flip = jnp.where(face == 0, second, first)
    if block_cols == 1:
        return 1 - east_flip, 0, east_flip, 1
    at_east = jnp.where(block_x == block_cols - 1, east_flip, 0)
    at_west = jnp.where(block_x == 0, west_flip, 0)
    return 1, at_east, 0, at_west


def slots_in(flags_ref):
    return flags_ref[4:5], flags_ref[5:6]


def flags_in(flags_ref, tiles=1):
    return [jnp.concatenate([flags_ref[k : k + 1]] * tiles, 1) for k in range(4)]


def mirrored_first(block_y):
    return (block_y >= BY // 4) & (block_y < BY - BY // 4)


def in_order(block_cols, first, second):
    if block_cols > 1:
        return first, second
    swap = mirrored_first(lax.rem(lax.axis_index("blk"), BY))
    return jnp.where(swap, second, first), jnp.where(swap, first, second)


def strips_kernel(block_cols, *refs):
    sources, (first_ref, then_ref, stored_ref, flags_ref) = refs[:8], refs[8:12]
    buffers, sems = refs[12:20], refs[20]
    copies = [
        pltpu.make_async_copy(source, buffer, sems.at[k])
        for k, (source, buffer) in enumerate(zip(sources, buffers))
    ]
    for copy in copies:
        copy.start()
    seam_ref, slot_ref, fields_ref, area_ref, depth_ref, spin_ref, tide_ref = buffers[:7]
    table_ref = buffers[7]
    for copy in copies[:2]:
        copy.wait()
    east0, flip0, east1, flip1 = flags = seam_flags(seam_ref, block_cols)
    index = lax.broadcasted_iota(i32, (8, LANES), 0)
    flags_ref[...] = sum(jnp.where(index == k, flag, 0) for k, flag in enumerate(flags))
    slots = slot_ref[:, :LANES], slot_ref[:, LANES:]
    flags_ref[4:5], flags_ref[5:6] = slots
    lane = lax.broadcasted_iota(i32, (8, 2 * LANES), 1)
    second = (lane & 64) != 0
    place = lane & 63
    row = place >> 2
    row = jnp.where(jnp.where(second, flip1, flip0) != 0, GY - 1 - row, row)
    east = jnp.where(second, east1, east0) != 0
    col = jnp.where(east, GX - RING, 0) + (place & 3)
    col = jnp.where(lane >= LANES, jnp.where(east, GX - RING - 1, RING), col)
    one_hot = by_slot(slots, col * GY + row)
    for copy in copies[2:7]:
        copy.wait()
    stored = stored_rows(fields_ref, (area_ref, depth_ref, spin_ref, tide_ref))
    both = picked(stored, one_hot)

    lane = lax.broadcasted_iota(i32, (1, LANES), 1)
    second = lane >= 64
    flip = jnp.where(second, flip1, flip0) != 0
    sign = jnp.where(flip, -1.0, 1.0)
    node = lax.broadcasted_iota(i32, (1, NP, 1), 1)

    def turned(values):
        shaped = values.reshape(-1, NP, LANES)
        shaped = pltpu.roll(shaped, 4, 1)
        shaped = jnp.where((node & 2) == 0, pltpu.roll(shaped, 6, 1), pltpu.roll(shaped, 2, 1))
        shaped = jnp.where((node & 1) == 0, pltpu.roll(shaped, 7, 1), pltpu.roll(shaped, 1, 1))
        return shaped.reshape(values.shape)

    strip, ring = (
        [part[k * NODES : (k + 1) * NODES] for k in range(ARRAYS)]
        for part in (both[:, :LANES], both[:, LANES:])
    )
    for copy in copies[7:]:
        copy.wait()
    table, weight = table_ref[: 8 * NP].astype(bf16), table_ref[8 * NP :, :LANES]
    edges = column_edges(table, weight, *ring[:6])
    east = jnp.where(second, east1, east0) != 0
    ends = [jnp.where(east, part[NP:], part[:NP]) for part in edges]
    ends[2] = ends[2] * sign
    strip[2] = strip[2] * sign
    strip[5] = strip[5] * sign
    strips = []
    for part, flip in zip(packed(strip_rows(strip, east, 0, ends)), (flip0, flip1)):
        if isinstance(flip, int):
            strips.append(turned(part) if flip else part)
        else:
            strips.append(jnp.where(flip != 0, turned(part), part))
    first_ref[...], then_ref[...] = in_order(block_cols, *strips)
    stored_ref[...] = stored


def rows_kernel(
    block_cols, flags_ref, stored_ref, first_ref, then_ref, table_ref, weight_ref,
    next_ref, far0_ref, far1_ref, pair_ref, sums,
):
    east0, flip0, east1, flip1 = flags_in(flags_ref)
    odd = lax.axis_index("blk") & 1
    lane = lax.broadcasted_iota(i32, (8, 2 * LANES), 1)
    row = jnp.where(odd != 0, GY - RING, 0) + ((lane & 63) >> 4)
    row = jnp.where((lane & 64) != 0, jnp.where(odd != 0, GY - RING - 1, RING), row)
    five = jnp.where(odd != 0, 0, GY - RING - 1) + jnp.minimum((lane & (LANES - 1)) >> 4, RING)
    row = jnp.where(lane >= LANES, five, row)
    both = picked(stored_ref[...], by_slot(slots_in(flags_ref), (lane & 15) * GY + row))
    pair_ref[...] = both[:, LANES:]
    rows = [both[k * NODES : (k + 1) * NODES, :LANES] for k in range(ARRAYS)]
    whole = unpacked(*in_order(block_cols, first_ref[...], then_ref[...]))
    strip = [whole[k * NODES : (k + 1) * NODES] for k in range(6)]
    edges = edge_values(table_ref, weight_ref, *map(beside, strip, rows[:6]))
    sums[0] = jnp.concatenate([part[:, :LANES] for part in edges], 0)
    lane = lax.broadcasted_iota(i32, (1, LANES), 1)
    top0, top1 = odd ^ flip0, odd ^ flip1
    whole = with_row_rim(whole, sums, jnp.where(lane >= 64, top1, top0) != 0)
    if block_cols == 1:
        far0_ref[...], far1_ref[...] = both_corners(whole, odd)
    else:
        far0_ref[...] = corner_of(whole, 0, top0)
        far1_ref[...] = corner_of(whole, 64, top1)
    sums[0] = jnp.concatenate([part[:, LANES:] for part in edges], 0)
    up = jnp.broadcast_to(odd != 0, (1, LANES))
    rim = pltpu.roll(jnp.where(up, *row_edges(sums)), 64, 1)
    rim = [rim[k * NP : (k + 1) * NP] for k in range(4)]
    whole = strip_rows(rows, up, 4, rim)
    top, bottom = whole[:HALF_ROWS], whole[HALF_ROWS:]
    next_ref[...] = jnp.where(lane >= 64, pltpu.roll(bottom, 64, 1), top)


def corners_kernel(block_cols, flags_ref, first_ref, then_ref, pair_ref, _, out_ref):
    east0, flip0, east1, flip1 = flags_in(flags_ref)
    in0, in1 = in_order(block_cols, first_ref[...], then_ref[...])
    top = 1 - (lax.axis_index("blk") & 1)
    lane = lax.broadcasted_iota(i32, (1, LANES), 1)
    halves = []
    for start in (0, 64):
        at0 = jnp.where(top != 0, 36, 80)
        at1 = jnp.where(top != 0, 56, 100)
        first = pltpu.roll(in0, (at0 - start) & (LANES - 1), 1)
        other = pltpu.roll(in1, (at1 - start) & (LANES - 1), 1)
        halves.append(jnp.where(lane < 100, first, other))
    late = jnp.where(lane < 100, east0, east1) == 0
    whole = placed_rows(jnp.concatenate(halves, 0), late, 0)
    out_ref[:ROWS] = jnp.where(lane < 80, pair_ref[...], whole[:ROWS])
    out_ref[ROWS:] = whole[ROWS:]


def own_kernel(flags_ref, stored_ref, lanes_ref, own_ref, hot_ref):
    one_hot = by_slot(slots_in(flags_ref), lanes_ref[0:8, :MID])
    own_ref[...] = picked(stored_ref[...], one_hot)
    hot_ref[...] = one_hot.astype(f32).T.astype(bf16)


def first_sums(table, weight, parts, rims, at_rim):
    p, u, v, area, depth, spin, tide = parts
    size = area.shape[1]
    root = jnp.sqrt(area)
    mass = jnp.concatenate([weight] * (size // LANES), 1) * area
    used = [p, u, v, root * depth, root, mass * spin, tide]
    for part, rim in zip(mass_tendency(table, p, u, v, *used[3:6]) + [mass], rims):
        west, east = part[:NP], part[NODES - NP :]
        at_east = jnp.where(at_rim, rim, pltpu.roll(west, size - 1, 1))
        at_west = jnp.where(at_rim, rim, pltpu.roll(east, 1, 1))
        used.append(
            jnp.concatenate([west + at_west, part[NP : NODES - NP], east + at_east], 0)
        )
    return used


def middle_kernel(
    block_cols, flags_ref, first_ref, then_ref, own_ref, lanes_ref, table_ref, weight_ref,
    low_ref, centre_ref, high_ref,
):
    east0, flip0, east1, flip1 = flags_in(flags_ref)
    second = lax.broadcasted_iota(i32, (1, LANES), 1) >= 64
    late = jnp.where(second, east1, east0) == 0
    whole = unpacked(*in_order(block_cols, first_ref[...], then_ref[...]))
    whole = placed_rows(whole, late, 0)
    side = lanes_ref[16:24, :MID]
    east = flags_in(flags_ref, MID // LANES)[0]
    first_at = jnp.where(side == 2, 64 * (1 - east), 64 * east)
    place = jnp.where(side == 0, -1, lanes_ref[8:16, :MID] + first_at)
    placed = picked(whole, as_one_hot(place, LANES))
    parts = [
        placed[k * NODES : (k + 1) * NODES] + own_ref[k * NODES : (k + 1) * NODES]
        for k in range(ARRAYS)
    ]
    rims = [placed[ROWS + c * NP : ROWS + (c + 1) * NP] for c in range(4)]
    at_rim = lanes_ref[24:25, LANES : LANES + MID] != 0
    used = first_sums(table_ref[...].astype(bf16), weight_ref[...], parts, rims, at_rim)
    for k, ref in enumerate((low_ref, centre_ref, high_ref)):
        for n, part in enumerate(used):
            ref[n * NODES : (n + 1) * NODES] = part[:, k * LANES : (k + 1) * LANES]


def far_kernel(block_cols, flags_ref, far0_ref, far1_ref, next_ref, _, out_ref):
    east0, flip0, east1, flip1 = flags_in(flags_ref)
    odd = lax.axis_index("blk") & 1
    lane = lax.broadcasted_iota(i32, (1, LANES), 1)
    below = jnp.broadcast_to(odd == 0, (1, LANES))
    strip = jnp.concatenate([next_ref[...], pltpu.roll(next_ref[...], 64, 1)], 0)
    strip = placed_rows(strip, below, 4)
    corners, strip_of = arrived_corners(far0_ref[...], far1_ref[...], block_cols, odd)
    late = jnp.where(strip_of != 0, east1, east0) == 0
    rim = MOVED + NODES // 2 + NP
    rim = jnp.concatenate(spread_out(corners[rim : rim + NP], below, 2), 0)
    corners = placed_rows(corners, late, 0)
    own = lane < 64
    out_ref[:ROWS] = jnp.where(own, strip[:ROWS], corners[:ROWS])
    out_ref[ROWS:ALL_ROWS] = corners[ROWS:]
    out_ref[ALL_ROWS:] = jnp.where(own, strip[ROWS:], rim)


def steps_kernel(
    block_cols, flags_ref, pair_ref, next_ref, low_ref, centre_ref,
    high_ref, hot_ref, table_ref, weight_ref, lanes_ref, out_ref, sums,
):
    east0, flip0, east1, flip1 = flags_in(flags_ref)
    odd = lax.axis_index("blk") & 1
    block_y = lax.rem(lax.axis_index("blk"), BY)

    lane = lax.broadcasted_iota(i32, (1, LANES), 1)
    pair = jnp.concatenate([pair_ref[...], jnp.zeros((EDGE_ROWS, LANES), f32)], 0)
    around = beside(pair, next_ref[...])
    outer_at = [lanes_ref[32 + 8 * k : 40 + 8 * k, : 2 * LANES] for k in range(4)]
    kind = outer_at[1]
    from_pair = jnp.where(outer_at[2] != 0, 1 - odd, odd) != 0
    east = flags_in(flags_ref, 2)[0]
    strip_at = jnp.where(kind == 3, 1 - east, east)
    far_at = strip_at ^ (1 - odd) if block_cols == 1 else strip_at
    strip_at, far_at = (jnp.where(kind > 1, at, 0) for at in (strip_at, far_at))
    place = jnp.where(
        from_pair,
        outer_at[0] + (RING + 1) * RING * strip_at,
        jnp.where(outer_at[3] < 0, -1, outer_at[3] + RING * RING * far_at),
    )
    outer = picked(around, as_one_hot(jnp.where(kind == 0, -1, place), 2 * LANES))
    table = table_ref[...].astype(bf16)
    tiles = (None, low_ref, centre_ref, high_ref, None)
    count = len(tiles)
    masks = [lanes_ref[24:32, k * LANES : (k + 1) * LANES] for k in range(count)]
    closed_above = jnp.where(block_y == BY - 1, masks[-2][1:2], 0) != 0
    closed_below = jnp.where(block_y == 0, masks[1][2:3], 0) != 0
    first_row = jnp.where(odd == 0, masks[0][4:5], 0) != 0
    last_row = jnp.where(odd != 0, masks[-1][5:6], 0) != 0
    outer_used = first_sums(
        table,
        weight_ref[...],
        [outer[k * NODES : (k + 1) * NODES] for k in range(ARRAYS)],
        [outer[ROWS + c * NP : ROWS + (c + 1) * NP] for c in range(4)],
        beside(masks[0][0:1], masks[-1][0:1]) != 0,
    )

    def shifted(parts, by, ring):
        turned = [pltpu.roll(part, -by % LANES, 1) for part in parts]
        size = len(parts)
        step = 1 if by > 0 else -1
        others = [(k + step) % size if ring else min(max(k + step, 0), size - 1) for k in range(size)]
        from_other = lane >= LANES - by if by > 0 else lane < -by
        return [jnp.where(from_other, turned[others[k]], turned[k]) for k in range(size)]

    def put_x_sums(groups, components):
        slots = [k for group in groups for k in group]
        ring = len(slots) < count
        per_tile = [
            [part[:, n * LANES : (n + 1) * LANES] for part in parts]
            for group, parts in zip(groups, components)
            for n in range(len(group))
        ]
        for c in range(3):
            parts = [tile[c] for tile in per_tile]
            west = [part[:NP] for part in parts]
            east = [part[NODES - NP :] for part in parts]
            at_east, at_west = shifted(west, 1, ring), shifted(east, -1, ring)
            for n, k in enumerate(slots):
                sums[k, c * NODES : c * NODES + NP] = west[n] + at_west[n]
                sums[k, c * NODES + NP : (c + 1) * NODES - NP] = parts[n][NP : NODES - NP]
                sums[k, (c + 1) * NODES - NP : (c + 1) * NODES] = east[n] + at_east[n]

    def edge_y(components, slots, rows=None):
        ring = len(slots) < count
        south_at = pl.ds(0, components * NP, stride=NP)
        north_at = pl.ds(NP - 1, components * NP, stride=NP)
        south = [sums[k, south_at] for k in slots]
        north = [sums[k, north_at] for k in slots]
        at_north, at_south = shifted(south, PITCH, ring), shifted(north, -PITCH, ring)
        for n, k in enumerate(slots):
            if k == count - 2:
                at_north[n] = jnp.where(closed_above, 0.0, at_north[n])
            if k == 1:
                at_south[n] = jnp.where(closed_below, 0.0, at_south[n])
        if rows is not None:
            at_south[0] = jnp.where(first_row, rows[0], at_south[0])
            at_north[-1] = jnp.where(last_row, rows[1], at_north[-1])
        for n, k in enumerate(slots):
            sums[k, south_at] = south[n] + at_south[n]
            sums[k, north_at] = north[n] + at_north[n]

    node = lax.broadcasted_iota(i32, (1, NP, 1), 1)
    rows = []
    for rim in (outer[ALL_ROWS:, :LANES], outer[ALL_ROWS:, LANES:]):
        east = pltpu.roll(rim, LANES - 1, 1).reshape(4, NP, LANES)
        west = pltpu.roll(rim, 1, 1).reshape(4, NP, LANES)
        rim = (
            rim.reshape(4, NP, LANES)
            + jnp.where(node == NP - 1, pltpu.roll(east, NP - 1, 1), 0.0)
            + jnp.where(node == 0, pltpu.roll(west, 1, 1), 0.0)
        )
        rows.append(rim.reshape(EDGE_ROWS, LANES))

    every = tuple(range(count))
    groups = (every[0:2], every[2:4], every[4:])

    def tile_part(k, n):
        if tiles[k] is None:
            return outer_used[n][:, :LANES] if k == 0 else outer_used[n][:, LANES:]
        return tiles[k][n * NODES : (n + 1) * NODES]

    def part_of(group, n):
        return jnp.concatenate([tile_part(k, n) for k in group], 1)

    def summed(group, c):
        return jnp.concatenate([sums[k, c * NODES : (c + 1) * NODES] for k in group], 1)

    def average(group, per_mass):
        return [summed(group, c) * per_mass for c in range(3)]

    def laplace(s):
        return [
            dot(table[4 * NODES :, : 3 * NODES], jnp.concatenate(high_low_high(part), 0))
            for part in s
        ]

    start = [[part_of(group, n) for n in range(3)] for group in groups]
    fixed = [[part_of(group, n) for n in range(3, 6)] for group in groups]
    for k in every:
        for c in range(4):
            sums[k, c * NODES : (c + 1) * NODES] = tile_part(k, 7 + c)
    edge_y(4, every, rows)
    per_mass = [1.0 / summed(group, 3) for group in groups]
    one = []
    for n, group in enumerate(groups):
        change = average(group, per_mass[n])
        one.append([s + time_step * c for s, c in zip(start[n], change)])
    put_x_sums(groups, [mass_tendency(table, *s, *f) for s, f in zip(one, fixed)])
    edge_y(3, every)
    two = []
    for n, group in enumerate(groups):
        change = average(group, per_mass[n])
        two.append(
            [0.75 * s + 0.25 * (o + time_step * c) for s, o, c in zip(start[n], one[n], change)]
        )
    put_x_sums(groups, [mass_tendency(table, *s, *f) for s, f in zip(two, fixed)])
    edge_y(3, every)

    def regrouped(per_group):
        (outer_low, high_above) = per_group[0], per_group[1]
        below, low = outer_low[:, :LANES], outer_low[:, LANES:]
        centre, high = high_above[:, :LANES], high_above[:, LANES:]
        near = jnp.where(lane < LANES // 2, per_group[2], below)
        return [beside(low, centre), beside(high, near)]

    def of_groups(values):
        return [list(parts) for parts in zip(*(regrouped(part) for part in zip(*values)))]

    for c in range(3):
        rows_at = slice(c * NODES, (c + 1) * NODES)
        sums[count - 1, rows_at] = jnp.where(
            lane < LANES // 2, sums[count - 1, rows_at], sums[0, rows_at]
        )
    slots = every[1:]
    groups = (slots[0:2], slots[2:4])
    start, two = of_groups(start), of_groups(two)
    tide = regrouped([part_of(every[0:2], 6), part_of(every[2:4], 6), part_of(every[4:], 6)])
    per_mass = regrouped(per_mass)
    three = []
    for n, group in enumerate(groups):
        change = average(group, per_mass[n])
        now = [
            s / 3.0 + 2.0 / 3.0 * (o + time_step * c)
            for s, o, c in zip(start[n], two[n], change)
        ]
        now[0] = now[0] + tide[n]
        three.append(now)
    put_x_sums(groups, [laplace(s) for s in three])
    edge_y(3, slots)
    change = [average(group, per_mass[n]) for n, group in enumerate(groups)]
    put_x_sums(groups, [laplace(s) for s in change])
    edge_y(3, slots)
    stepped = []
    for n, group in enumerate(groups):
        change = average(group, per_mass[n])
        now = [s - time_step * hyper_coeff * b for s, b in zip(three[n], change)]
        stepped.append(jnp.concatenate(now, 0))
    stepped = jnp.concatenate(stepped, 1)[:, :MID]
    own = lanes_ref[27:28, LANES : LANES + MID] != 0
    stored = picked(jnp.where(own, stepped, 0.0), hot_ref[...])
    out_ref[...] = stored.reshape(out_ref.shape)


def on_device(fields, jacobian, water_depth, coriolis, tide_height, slot_of, seam_rows):
    block_cols = lax.axis_size("blk") // BY
    table, weight, edge_table, lanes = map(jnp.asarray, (*operator_table(), lane_tables()))
    vmem = pl.BlockSpec(memory_space=pltpu.VMEM)
    hbm = pl.BlockSpec(memory_space=pltpu.HBM)
    params = pltpu.CompilerParams(vmem_limit_bytes=48 * 2**20)
    held = (fields, jacobian, water_depth, coriolis, tide_height)

    def call(kernel, ins, outs, cost, scratch=(), name=None):
        return pl.pallas_call(
            kernel,
            out_shape=[jax.ShapeDtypeStruct(*out) for out in outs],
            in_specs=[spec for spec, value in ins],
            out_specs=[vmem] * len(outs),
            scratch_shapes=list(scratch),
            compiler_params=params,
            cost_estimate=pl.CostEstimate(
                flops=cost, bytes_accessed=2 * 2**20, transcendentals=0
            ),
            name=name,
        )(
            *[
                pltpu.with_memory_space_constraint(value, pltpu.HBM) if spec is hbm else value
                for spec, value in ins
            ]
        )

    strip = ((HALF_ROWS, LANES), f32)
    def room(values, spaces=None):
        spaces = spaces or [pltpu.VMEM] * len(values)
        buffers = [space(x.shape, x.dtype) for space, x in zip(spaces, values)]
        return buffers + [pltpu.SemaphoreType.DMA((len(values),))]

    needed = (seam_rows, slot_of, *held, edge_table)
    corner = ((CORNER_ROWS, LANES), f32)
    scratch = [pltpu.VMEM((1, 4 * NODES, LANES), f32)]
    first, then, stored, flags = call(
        functools.partial(strips_kernel, block_cols),
        [(hbm, x) for x in needed],
        [strip, strip, ((ROWS, ELEMENTS), f32), ((8, LANES), i32)],
        10**8,
        scratch=room(needed, [pltpu.SMEM] + [pltpu.VMEM] * (len(needed) - 1)),
        name="strips",
    )
    to_next, far0, far1, to_pair = call(
        functools.partial(rows_kernel, block_cols),
        [(vmem, x) for x in (flags, stored, first, then, table, weight)],
        [strip, corner, corner, ((ROWS, LANES), f32)],
        10**8,
        scratch=scratch,
        name="rows",
    )
    span = block_cols * BY
    both = ("face", "blk")
    places = [(f, x, y) for f in range(2) for x in range(block_cols) for y in range(BY)]

    def rank(face, block_x, block_y):
        return face * span + block_x * BY + block_y

    def same(y):
        return y

    def in_pair(y):
        return y ^ 1

    def next_pair(y):
        other = y + 1 if y % 2 else y - 1
        return other if 0 <= other < BY else y

    def swapped(value, partner):
        pairs = [
            (rank(f, x, y), rank(f if partner(y) != y else 1 - f, x, partner(y)))
            for f, x, y in places
        ]
        return lax.ppermute(value, both, pairs)

    def across(value0, value1, partner):
        last = block_cols - 1

        def aligned(y):
            return partner is same or partner(y) != y

        straight = {
            (f, x, y): (f, x + 1, partner(y)) if x < last else (1 - f, 0, partner(y))
            for f, x, y in places
        }
        turned = {
            (f, last, y): (1 - f, 0, BY - 1 - partner(y) if aligned(y) else y)
            for f in range(2)
            for y in range(BY)
        }

        def eastward(value, pairs):
            return lax.ppermute(value, both, [(rank(*a), rank(*b)) for a, b in pairs.items()])

        def westward(value, pairs):
            return lax.ppermute(value, both, [(rank(*b), rank(*a)) for a, b in pairs.items()])

        if block_cols == 1:
            return eastward(value0, straight), eastward(value1, turned)
        flipped = (seam_rows[:, 1] - seam_rows[:, 0]) % seam_rows.shape[1] != 1
        face = lax.axis_index("face")
        block_x = lax.axis_index("blk") // BY
        return (
            jnp.where(
                (block_x == last) & flipped[face],
                westward(value1, turned),
                westward(value1, straight),
            ),
            jnp.where(
                (block_x == 0) & flipped[1 - face],
                eastward(value0, turned),
                eastward(value0, straight),
            ),
        )

    if block_cols == 1:
        halos = []
        for value, mirrored in ((first, mirrored_first), (then, lambda y: not mirrored_first(y))):
            pairs = [
                (rank(f, x, y), rank(1 - f, x, BY - 1 - y if mirrored(y) else y))
                for f, x, y in places
            ]
            halos.append(lax.ppermute(value, both, pairs))
        halo0, halo1 = halos
    else:
        halo0, halo1 = across(first, then, same)
    far0, far1 = across(far0, far1, next_pair)
    from_next = swapped(to_next, next_pair)
    own, hot = call(
        own_kernel,
        [(vmem, x) for x in (flags, stored, lanes)],
        [((ROWS, MID), f32), ((MID, ELEMENTS), bf16)],
        10**8,
        name="own",
    )
    (to_pair,) = call(
        functools.partial(corners_kernel, block_cols),
        [(vmem, x) for x in (flags, halo0, halo1, to_pair, hot)],
        [((ALL_ROWS, LANES), f32)],
        10**8,
        name="corners",
    )
    from_pair = swapped(to_pair, in_pair)
    tile = ((11 * NODES, LANES), f32)
    low, centre, high = call(
        functools.partial(middle_kernel, block_cols),
        [(vmem, x) for x in (flags, halo0, halo1, own, lanes, table, weight)],
        [tile, tile, tile],
        10**8,
        name="middle",
    )
    (from_next,) = call(
        functools.partial(far_kernel, block_cols),
        [(vmem, x) for x in (flags, far0, far1, from_next, low)],
        [((RIM_ROWS, LANES), f32)],
        10**11,
        name="far",
    )
    (stepped,) = call(
        functools.partial(steps_kernel, block_cols),
        [
            (vmem, x)
            for x in (
                flags, from_pair, from_next, low, centre, high, hot, table, weight, lanes
            )
        ],
        [(fields.shape, f32)],
        10**8,
        scratch=[pltpu.VMEM((EXT // LANES, 4 * NODES, LANES), f32)],
        name="steps",
    )
    return stepped


def solution(mesh):
    return jax.shard_map(
        on_device,
        mesh=mesh,
        in_specs=(
            P(None, None, None, ("face", "blk")),
            P(None, None, ("face", "blk")),
            P(None, None, ("face", "blk")),
            P(None, None, ("face", "blk")),
            P(None, None, ("face", "blk")),
            P(("face", "blk"), None),
            P(),
        ),
        out_specs=P(None, None, None, ("face", "blk")),
        check_vma=False,
    )
```

```python
import functools
import math

import jax
import jax.numpy as jnp
import ml_dtypes
import numpy as np
from jax import lax
from jax.experimental import pallas as pl
from jax.experimental.pallas import tpu as pltpu
from jax.sharding import PartitionSpec as P

BY = 16
GX = 16
GY = 16
NP = 8
NODES = NP * NP
ARRAYS = 7
ROWS = ARRAYS * NODES
MOVED = 6 * NODES
EDGE_ROWS = 4 * NP
ALL_ROWS = ROWS + EDGE_ROWS
HALF_ROWS = (MOVED + NODES // 2 + 2 * NP) // 2
RING = 4
RIM_ROWS = ROWS + 2 * EDGE_ROWS
CORNER_ROWS = (MOVED + NODES // 2 + 4 * NP) // 8
PITCH = GX + 2 * RING
MID = GY * PITCH
LANES = 128
EXT = MID + 2 * LANES
LEAD = LANES - RING * PITCH
ELEMENTS = GX * GY

time_step = 0.03
hyper_coeff = 0.0002

f32 = jnp.float32
bf16 = jnp.bfloat16
i32 = jnp.int32


def legendre_pair(location, degree):
    lower_value = 1.0
    upper_value = location
    for polynomial_order in range(2, degree + 1):
        lower_value, upper_value = (
            upper_value,
            (
                (2 * polynomial_order - 1) * location * upper_value
                - (polynomial_order - 1) * lower_value
            )
            / polynomial_order,
        )
    return (lower_value, upper_value)


def gll_tables(points):
    degree = points - 1
    locations = [-math.cos(math.pi * position / degree) for position in range(points)]
    for iteration in range(100):
        updated = []
        for location in locations:
            lower_value, upper_value = legendre_pair(location, degree)
            updated.append(
                location - (location * upper_value - lower_value) / ((degree + 1) * upper_value)
            )
        locations = updated
    locations[0] = -1.0
    locations[degree] = 1.0
    legendre_at = [legendre_pair(location, degree)[1] for location in locations]
    weights = [2.0 / (degree * (degree + 1) * value * value) for value in legendre_at]
    corner_value = degree * (degree + 1) / 4.0
    derivative = []
    for row_index in range(points):
        row_values = []
        for column_index in range(points):
            if row_index != column_index:
                row_values.append(
                    legendre_at[row_index]
                    / (legendre_at[column_index] * (locations[row_index] - locations[column_index]))
                )
            elif row_index == 0:
                row_values.append(-corner_value)
            elif row_index == degree:
                row_values.append(corner_value)
            else:
                row_values.append(0.0)
        derivative.append(row_values)
    return np.asarray(weights, np.float64), np.asarray(derivative, np.float64)


def in_three(matrix):
    high = matrix.astype(ml_dtypes.bfloat16)
    low = (matrix - high.astype(np.float64)).astype(ml_dtypes.bfloat16)
    return np.concatenate([high, high, low], 1)


def operator_table():
    weights, derivative = gll_tables(NP)
    eye = np.eye(NP)
    node_weight = np.outer(weights, weights).reshape(NODES, 1)
    along_x = node_weight * np.kron(derivative, eye)
    along_y = node_weight * np.kron(eye, derivative)
    second = derivative @ derivative
    both = node_weight * (np.kron(second, eye) + np.kron(eye, second))
    table = np.zeros((5 * NODES, 4 * NODES), ml_dtypes.bfloat16)
    table[:NODES, : 3 * NODES] = in_three(along_x)
    table[NODES : 2 * NODES, : 3 * NODES] = in_three(along_y)
    flux = [in_three(along_x), in_three(along_y)]
    for k, part in enumerate(flux):
        at = 2 * k * NODES
        table[2 * NODES : 3 * NODES, at : at + 2 * NODES] = part[:, : 2 * NODES]
        table[3 * NODES : 4 * NODES, at : at + NODES] = part[:, 2 * NODES :]
    table[4 * NODES :, : 3 * NODES] = in_three(both)
    table = table.astype(np.float32)
    spread = np.broadcast_to(node_weight, (NODES, LANES)).astype(np.float32)
    ends = np.r_[:NP, NODES - NP : NODES]
    edge_table = np.zeros((10 * NP, 4 * NODES), np.float32)
    for k in range(4):
        edge_table[2 * k * NP : 2 * (k + 1) * NP] = table[k * NODES + ends]
    edge_table[8 * NP :, :LANES] = spread[ends]
    return table, np.ascontiguousarray(spread), edge_table


def lane_tables():
    table = np.zeros((24, MID), np.int32)
    for lane in range(MID):
        row, col = divmod(lane, PITCH)
        x = col - RING
        own = 0 <= x < GX
        table[0:8, lane] = x * GY + row if own else -1
        if not own:
            table[8:16, lane] = row * RING + (col if x < 0 else x - GX)
        table[16:24, lane] = 0 if own else (1 if x < 0 else 2)
    ext = np.zeros((8, EXT), np.int32)
    outer = np.zeros((32, 2 * LANES), np.int32)
    for lane in range(EXT):
        row, col = divmod(lane - LEAD, PITCH)
        y = row - RING
        x = col - RING
        ext[0, lane] = x in (-RING, GX + RING - 1)
        ext[1, lane] = y == GY - 1
        ext[2, lane] = y == 0
        ext[3, lane] = 0 <= y < GY and 0 <= x < GX
        ext[4, lane] = y == -RING
        ext[5, lane] = y == GY + RING - 1
        if -RING - 1 <= y < 0 or GY <= y <= GY + RING:
            place = lane if y < 0 else lane - MID
            step = y + RING if y < 0 else y - GY
            near = step + 1 if y < 0 else step
            far = 0 <= step < RING
            if 0 <= x < GX:
                outer[0:8, place] = near * GX + x
                outer[8:16, place] = 1
                outer[24:32, place] = LANES + step * GX + x if far else -1
            else:
                across = x + RING if x < 0 else x - GX
                outer[0:8, place] = (RING + 1) * GX + near * RING + across
                outer[8:16, place] = 2 if x < 0 else 3
                outer[24:32, place] = LANES + RING * GX + step * RING + across if far else -1
            outer[16:24, place] = y > 0
    whole = np.zeros((64, EXT), np.int32)
    whole[0:24, :MID] = table
    whole[24:32] = ext
    whole[32:64, : 2 * LANES] = outer
    return whole


def dot(a, b):
    return jnp.dot(a, b, preferred_element_type=f32)


def picked(values, one_hot):
    high = values.astype(bf16)
    low = (values - high.astype(f32)).astype(bf16)
    both = dot(jnp.concatenate([high, low], 0), one_hot)
    return both[: values.shape[0]] + both[values.shape[0] :]


def as_one_hot(row_of_lane, depth):
    index = lax.broadcasted_iota(i32, (depth, row_of_lane.shape[1]), 0)
    return jnp.where(index == row_of_lane[0:1], 1.0, 0.0).astype(bf16)


def high_low_high(values):
    high = values.astype(bf16)
    low = (values - high.astype(f32)).astype(bf16)
    return [high, low, high]


def by_slot(halves, cell_of_lane):
    size = cell_of_lane.shape[1]
    halves = [jnp.broadcast_to(half, (8, LANES)) for half in halves]
    chosen = []
    for k in range(size // LANES):
        cell = cell_of_lane[:, k * LANES : (k + 1) * LANES]
        low, high = (jnp.take_along_axis(half, cell & (LANES - 1), axis=1) for half in halves)
        chosen.append(jnp.where(cell < 0, -1, jnp.where(cell < LANES, low, high)))
    return as_one_hot(jnp.concatenate(chosen, 1), ELEMENTS)


def stored_rows(fields_ref, others):
    fields = fields_ref[...].reshape(3 * NODES, ELEMENTS)
    others = [ref[...].reshape(NODES, ELEMENTS) for ref in others]
    return jnp.concatenate([fields[:NODES] - others[-1], fields[NODES:]] + others, 0)


def mass_tendency(table, p, u, v, area_depth, weighted_area, spin):
    slopes = dot(table[: 2 * NODES, : 3 * NODES], jnp.concatenate(high_low_high(p), 0))
    flux = high_low_high(area_depth * u)[:2] + high_low_high(area_depth * v)[:2]
    spread = dot(table[2 * NODES : 4 * NODES], jnp.concatenate(flux, 0))
    return [
        -(spread[:NODES] + spread[NODES:]),
        spin * v - weighted_area * slopes[:NODES],
        -spin * u - weighted_area * slopes[NODES:],
    ]


def edge_values(table_ref, weight_ref, p, u, v, area, depth, spin):
    root = jnp.sqrt(area)
    mass = jnp.concatenate([weight_ref[...]] * (area.shape[1] // LANES), 1) * area
    table = table_ref[...].astype(bf16)
    return mass_tendency(table, p, u, v, root * depth, root, mass * spin) + [mass]


def column_edges(table, weight, p, u, v, area, depth, spin):
    def ends(part):
        return jnp.concatenate([part[:NP], part[NODES - NP :]], 0)

    root = jnp.sqrt(area)
    area_depth = root * depth
    root, mass = ends(root), weight * ends(area)
    weighted_spin = mass * ends(spin)
    slopes = dot(table[: 4 * NP, : 3 * NODES], jnp.concatenate(high_low_high(p), 0))
    flux = high_low_high(area_depth * u)[:2] + high_low_high(area_depth * v)[:2]
    spread = dot(table[4 * NP :], jnp.concatenate(flux, 0))
    return [
        -(spread[: 2 * NP] + spread[2 * NP :]),
        weighted_spin * ends(v) - root * slopes[: 2 * NP],
        -weighted_spin * ends(u) - root * slopes[2 * NP :],
        mass,
    ]


def row_edges(sums):
    return tuple(sums[0, pl.ds(j, EDGE_ROWS, stride=NP)] for j in (NP - 1, 0))


def beside(left, right):
    return jnp.concatenate([left, right], 1)


def one_of_four(parts, index):
    out = parts[0]
    for k in range(1, 4):
        out = jnp.where(index == k, parts[k], out)
    return out


def folded(tide, kept, late, step):
    half = NODES // 2
    back = pltpu.roll(tide[half:], LANES - step, 1)
    onward = pltpu.roll(tide[half:], step, 1)
    return jnp.where(kept, tide[:half], jnp.where(late, back, onward))


def unfolded(rows, late, step):
    back = pltpu.roll(rows, LANES - step, 1)
    onward = pltpu.roll(rows, step, 1)
    return jnp.concatenate([rows, jnp.where(late, onward, back)], 0)


def strip_rows(parts, late, shift, rims):
    lane = lax.broadcasted_iota(i32, (1, LANES), 1)
    index = (lane >> shift) & 3
    kept = jnp.where(late, index // 2, 1 - index // 2) != 0
    tide = folded(parts[6], kept, late, 2 << shift)
    rim = one_of_four(rims, index)
    return jnp.concatenate(parts[:6] + [tide, rim, jnp.zeros_like(rim)], 0)


def placed_rows(whole, late, shift):
    half = NODES // 2
    tide = unfolded(whole[MOVED : MOVED + half], late, 2 << shift)
    rim = whole[MOVED + half : MOVED + half + NP]
    return jnp.concatenate([whole[:MOVED], tide] + spread_out(rim, late, shift), 0)


def spread_out(rim, late, shift):
    parts = []
    for k in range(4):
        first = pltpu.roll(rim, (LANES - (k << shift)) % LANES, 1) if k else rim
        last = pltpu.roll(rim, (3 - k) << shift, 1) if k < 3 else rim
        parts.append(jnp.where(late, first, last))
    return parts


def with_row_rim(whole, sums, top):
    north, south = row_edges(sums)
    rim = jnp.where(top, pltpu.roll(north, RING, 1), pltpu.roll(south, LANES - RING, 1))
    parts = [rim[k * NP : (k + 1) * NP] for k in range(4)]
    lane = lax.broadcasted_iota(i32, (1, LANES), 1)
    spots = []
    for k, part in enumerate(parts):
        first = pltpu.roll(part, k * RING, 1) if k else part
        last = pltpu.roll(part, (LANES - (3 - k) * RING) % LANES, 1) if k < 3 else part
        spots.append(jnp.where(top, first, last))
    rim = one_of_four(spots, (lane >> 2) & 3)
    return jnp.concatenate([whole[: MOVED + NODES // 2 + NP], rim], 0)


def in_eight(whole):
    whole = jnp.concatenate([whole, jnp.zeros((8 * CORNER_ROWS - whole.shape[0], LANES), f32)], 0)
    return [whole[k * CORNER_ROWS : (k + 1) * CORNER_ROWS] for k in range(8)]


def corner_of(whole, start, top):
    lane = lax.broadcasted_iota(i32, (1, LANES), 1)
    out = None
    for k, part in enumerate(in_eight(whole)):
        last = pltpu.roll(part, (LANES - start - 48 + 16 * k) % LANES, 1)
        first = pltpu.roll(part, (LANES - start + 16 * k) % LANES, 1)
        part = jnp.where(top != 0, last, first)
        out = part if k == 0 else jnp.where(lane >= 16 * k, part, out)
    return out


def both_corners(whole, odd):
    group = lax.broadcasted_iota(i32, (1, LANES), 1) >> 4
    other_group = (group + jnp.where(odd != 0, 7, 1)) & 7
    first, other = None, None
    for k, part in enumerate(in_eight(whole)):
        part = pltpu.roll(part, (LANES + 16 * k - 48 * odd) & (LANES - 1), 1)
        first = part if k == 0 else jnp.where(group == k, part, first)
        other = part if k == 0 else jnp.where(other_group == k, part, other)
    return first, other


def arrived_corners(far0, far1, block_cols, odd):
    lane = lax.broadcasted_iota(i32, (1, LANES), 1)
    corners = []
    for k in range(8):
        if block_cols == 1:
            part = jnp.where((lane >> 4) == k, far0, far1)
            part = pltpu.roll(part, (LANES + 64 + 16 * (1 - odd) - 16 * k) & (LANES - 1), 1)
        else:
            first = pltpu.roll(far0, (64 - 16 * k) % LANES, 1)
            other = pltpu.roll(far1, (80 - 16 * k) % LANES, 1)
            part = jnp.where((lane & 16) == 0, first, other)
        corners.append(part)
    return jnp.concatenate(corners, 0), ((lane >> 4) & 1) ^ (1 - odd if block_cols == 1 else 0)


def packed(whole):
    second = lax.broadcasted_iota(i32, (1, LANES), 1) >= 64
    top, bottom = whole[:HALF_ROWS], whole[HALF_ROWS:]
    return (
        jnp.where(second, pltpu.roll(bottom, 64, 1), top),
        jnp.where(second, bottom, pltpu.roll(top, 64, 1)),
    )


def unpacked(in0, in1):
    second = lax.broadcasted_iota(i32, (1, LANES), 1) >= 64
    top = jnp.where(second, pltpu.roll(in1, 64, 1), in0)
    bottom = jnp.where(second, in1, pltpu.roll(in0, 64, 1))
    return jnp.concatenate([top, bottom], 0)


def seam_flags(seam_ref, block_cols):
    size_y = seam_ref.shape[1]
    face = lax.axis_index("face")
    blk = lax.axis_index("blk")
    block_x = blk // BY

    def flipped(k):
        return jnp.where(lax.rem(seam_ref[k, 1] - seam_ref[k, 0] + size_y, size_y) != 1, 1, 0)

    first, second = flipped(0), flipped(1)
    east_flip = jnp.where(face == 0, first, second)
    west_flip = jnp.where(face == 0, second, first)
    if block_cols == 1:
        return 1 - east_flip, 0, east_flip, 1
    at_east = jnp.where(block_x == block_cols - 1, east_flip, 0)
    at_west = jnp.where(block_x == 0, west_flip, 0)
    return 1, at_east, 0, at_west


def slots_in(flags_ref):
    return flags_ref[4:5], flags_ref[5:6]


def flags_in(flags_ref, tiles=1):
    return [jnp.concatenate([flags_ref[k : k + 1]] * tiles, 1) for k in range(4)]


def mirrored_first(block_y):
    return (block_y >= BY // 4 - 1) & (block_y < BY - BY // 4 + 1)


def in_order(block_cols, first, second):
    if block_cols > 1:
        return first, second
    swap = mirrored_first(lax.rem(lax.axis_index("blk"), BY))
    return jnp.where(swap, second, first), jnp.where(swap, first, second)


def strips_kernel(block_cols, *refs):
    sources, (first_ref, then_ref, stored_ref, flags_ref) = refs[:8], refs[8:12]
    buffers, sems = refs[12:20], refs[20]
    copies = [
        pltpu.make_async_copy(source, buffer, sems.at[k])
        for k, (source, buffer) in enumerate(zip(sources, buffers))
    ]
    for copy in copies:
        copy.start()
    seam_ref, slot_ref, fields_ref, area_ref, depth_ref, spin_ref, tide_ref = buffers[:7]
    table_ref = buffers[7]
    for copy in copies[:2]:
        copy.wait()
    east0, flip0, east1, flip1 = flags = seam_flags(seam_ref, block_cols)
    index = lax.broadcasted_iota(i32, (8, LANES), 0)
    flags_ref[...] = sum(jnp.where(index == k, flag, 0) for k, flag in enumerate(flags))
    slots = slot_ref[:, :LANES], slot_ref[:, LANES:]
    flags_ref[4:5], flags_ref[5:6] = slots
    lane = lax.broadcasted_iota(i32, (8, 2 * LANES), 1)
    second = (lane & 64) != 0
    place = lane & 63
    row = place >> 2
    row = jnp.where(jnp.where(second, flip1, flip0) != 0, GY - 1 - row, row)
    east = jnp.where(second, east1, east0) != 0
    col = jnp.where(east, GX - RING, 0) + (place & 3)
    col = jnp.where(lane >= LANES, jnp.where(east, GX - RING - 1, RING), col)
    one_hot = by_slot(slots, col * GY + row)
    for copy in copies[2:7]:
        copy.wait()
    stored = stored_rows(fields_ref, (area_ref, depth_ref, spin_ref, tide_ref))
    both = picked(stored, one_hot)

    lane = lax.broadcasted_iota(i32, (1, LANES), 1)
    second = lane >= 64
    flip = jnp.where(second, flip1, flip0) != 0
    sign = jnp.where(flip, -1.0, 1.0)
    node = lax.broadcasted_iota(i32, (1, NP, 1), 1)

    def turned(values):
        shaped = values.reshape(-1, NP, LANES)
        shaped = pltpu.roll(shaped, 4, 1)
        shaped = jnp.where((node & 2) == 0, pltpu.roll(shaped, 6, 1), pltpu.roll(shaped, 2, 1))
        shaped = jnp.where((node & 1) == 0, pltpu.roll(shaped, 7, 1), pltpu.roll(shaped, 1, 1))
        return shaped.reshape(values.shape)

    strip, ring = (
        [part[k * NODES : (k + 1) * NODES] for k in range(ARRAYS)]
        for part in (both[:, :LANES], both[:, LANES:])
    )
    for copy in copies[7:]:
        copy.wait()
    table, weight = table_ref[: 8 * NP].astype(bf16), table_ref[8 * NP :, :LANES]
    edges = column_edges(table, weight, *ring[:6])
    east = jnp.where(second, east1, east0) != 0
    ends = [jnp.where(east, part[NP:], part[:NP]) for part in edges]
    ends[2] = ends[2] * sign
    strip[2] = strip[2] * sign
    strip[5] = strip[5] * sign
    strips = []
    for part, flip in zip(packed(strip_rows(strip, east, 0, ends)), (flip0, flip1)):
        if isinstance(flip, int):
            strips.append(turned(part) if flip else part)
        else:
            strips.append(jnp.where(flip != 0, turned(part), part))
    first_ref[...], then_ref[...] = in_order(block_cols, *strips)
    stored_ref[...] = stored


def rows_kernel(
    block_cols, flags_ref, stored_ref, first_ref, then_ref, table_ref, weight_ref,
    next_ref, far0_ref, far1_ref, pair_ref, sums,
):
    east0, flip0, east1, flip1 = flags_in(flags_ref)
    odd = lax.axis_index("blk") & 1
    lane = lax.broadcasted_iota(i32, (8, 2 * LANES), 1)
    row = jnp.where(odd != 0, GY - RING, 0) + ((lane & 63) >> 4)
    row = jnp.where((lane & 64) != 0, jnp.where(odd != 0, GY - RING - 1, RING), row)
    five = jnp.where(odd != 0, 0, GY - RING - 1) + jnp.minimum((lane & (LANES - 1)) >> 4, RING)
    row = jnp.where(lane >= LANES, five, row)
    both = picked(stored_ref[...], by_slot(slots_in(flags_ref), (lane & 15) * GY + row))
    pair_ref[...] = both[:, LANES:]
    rows = [both[k * NODES : (k + 1) * NODES, :LANES] for k in range(ARRAYS)]
    whole = unpacked(*in_order(block_cols, first_ref[...], then_ref[...]))
    strip = [whole[k * NODES : (k + 1) * NODES] for k in range(6)]
    edges = edge_values(table_ref, weight_ref, *map(beside, strip, rows[:6]))
    sums[0] = jnp.concatenate([part[:, :LANES] for part in edges], 0)
    lane = lax.broadcasted_iota(i32, (1, LANES), 1)
    top0, top1 = odd ^ flip0, odd ^ flip1
    whole = with_row_rim(whole, sums, jnp.where(lane >= 64, top1, top0) != 0)
    if block_cols == 1:
        far0_ref[...], far1_ref[...] = both_corners(whole, odd)
    else:
        far0_ref[...] = corner_of(whole, 0, top0)
        far1_ref[...] = corner_of(whole, 64, top1)
    sums[0] = jnp.concatenate([part[:, LANES:] for part in edges], 0)
    up = jnp.broadcast_to(odd != 0, (1, LANES))
    rim = pltpu.roll(jnp.where(up, *row_edges(sums)), 64, 1)
    rim = [rim[k * NP : (k + 1) * NP] for k in range(4)]
    whole = strip_rows(rows, up, 4, rim)
    top, bottom = whole[:HALF_ROWS], whole[HALF_ROWS:]
    next_ref[...] = jnp.where(lane >= 64, pltpu.roll(bottom, 64, 1), top)


def corners_kernel(block_cols, flags_ref, first_ref, then_ref, pair_ref, _, out_ref):
    east0, flip0, east1, flip1 = flags_in(flags_ref)
    in0, in1 = in_order(block_cols, first_ref[...], then_ref[...])
    top = 1 - (lax.axis_index("blk") & 1)
    lane = lax.broadcasted_iota(i32, (1, LANES), 1)
    halves = []
    for start in (0, 64):
        at0 = jnp.where(top != 0, 36, 80)
        at1 = jnp.where(top != 0, 56, 100)
        first = pltpu.roll(in0, (at0 - start) & (LANES - 1), 1)
        other = pltpu.roll(in1, (at1 - start) & (LANES - 1), 1)
        halves.append(jnp.where(lane < 100, first, other))
    late = jnp.where(lane < 100, east0, east1) == 0
    whole = placed_rows(jnp.concatenate(halves, 0), late, 0)
    out_ref[:ROWS] = jnp.where(lane < 80, pair_ref[...], whole[:ROWS])
    out_ref[ROWS:] = whole[ROWS:]


def own_kernel(flags_ref, stored_ref, lanes_ref, own_ref, hot_ref):
    one_hot = by_slot(slots_in(flags_ref), lanes_ref[0:8, :MID])
    own_ref[...] = picked(stored_ref[...], one_hot)
    hot_ref[...] = one_hot.astype(f32).T.astype(bf16)


def first_sums(table, weight, parts, rims, at_rim):
    p, u, v, area, depth, spin, tide = parts
    size = area.shape[1]
    root = jnp.sqrt(area)
    mass = jnp.concatenate([weight] * (size // LANES), 1) * area
    used = [p, u, v, root * depth, root, mass * spin, tide]
    for part, rim in zip(mass_tendency(table, p, u, v, *used[3:6]) + [mass], rims):
        west, east = part[:NP], part[NODES - NP :]
        at_east = jnp.where(at_rim, rim, pltpu.roll(west, size - 1, 1))
        at_west = jnp.where(at_rim, rim, pltpu.roll(east, 1, 1))
        used.append(
            jnp.concatenate([west + at_west, part[NP : NODES - NP], east + at_east], 0)
        )
    return used


def middle_kernel(
    block_cols, flags_ref, first_ref, then_ref, own_ref, lanes_ref, table_ref, weight_ref,
    low_ref, centre_ref, high_ref,
):
    east0, flip0, east1, flip1 = flags_in(flags_ref)
    second = lax.broadcasted_iota(i32, (1, LANES), 1) >= 64
    late = jnp.where(second, east1, east0) == 0
    whole = unpacked(*in_order(block_cols, first_ref[...], then_ref[...]))
    whole = placed_rows(whole, late, 0)
    side = lanes_ref[16:24, :MID]
    east = flags_in(flags_ref, MID // LANES)[0]
    first_at = jnp.where(side == 2, 64 * (1 - east), 64 * east)
    place = jnp.where(side == 0, -1, lanes_ref[8:16, :MID] + first_at)
    placed = picked(whole, as_one_hot(place, LANES))
    parts = [
        placed[k * NODES : (k + 1) * NODES] + own_ref[k * NODES : (k + 1) * NODES]
        for k in range(ARRAYS)
    ]
    rims = [placed[ROWS + c * NP : ROWS + (c + 1) * NP] for c in range(4)]
    at_rim = lanes_ref[24:25, LANES : LANES + MID] != 0
    used = first_sums(table_ref[...].astype(bf16), weight_ref[...], parts, rims, at_rim)
    for k, ref in enumerate((low_ref, centre_ref, high_ref)):
        for n, part in enumerate(used):
            ref[n * NODES : (n + 1) * NODES] = part[:, k * LANES : (k + 1) * LANES]


def far_kernel(block_cols, flags_ref, far1_ref, far0_ref, next_ref, _, out_ref):
    east0, flip0, east1, flip1 = flags_in(flags_ref)
    odd = lax.axis_index("blk") & 1
    lane = lax.broadcasted_iota(i32, (1, LANES), 1)
    below = jnp.broadcast_to(odd == 0, (1, LANES))
    strip = jnp.concatenate([next_ref[...], pltpu.roll(next_ref[...], 64, 1)], 0)
    strip = placed_rows(strip, below, 4)
    corners, strip_of = arrived_corners(far0_ref[...], far1_ref[...], block_cols, odd)
    late = jnp.where(strip_of != 0, east1, east0) == 0
    rim = MOVED + NODES // 2 + NP
    rim = jnp.concatenate(spread_out(corners[rim : rim + NP], below, 2), 0)
    corners = placed_rows(corners, late, 0)
    own = lane < 64
    out_ref[:ROWS] = jnp.where(own, strip[:ROWS], corners[:ROWS])
    out_ref[ROWS:ALL_ROWS] = corners[ROWS:]
    out_ref[ALL_ROWS:] = jnp.where(own, strip[ROWS:], rim)


def steps_kernel(
    block_cols, flags_ref, pair_ref, next_ref, low_ref, centre_ref,
    high_ref, hot_ref, table_ref, weight_ref, lanes_ref, out_ref, sums,
):
    east0, flip0, east1, flip1 = flags_in(flags_ref)
    odd = lax.axis_index("blk") & 1
    block_y = lax.rem(lax.axis_index("blk"), BY)

    lane = lax.broadcasted_iota(i32, (1, LANES), 1)
    pair = jnp.concatenate([pair_ref[...], jnp.zeros((EDGE_ROWS, LANES), f32)], 0)
    around = beside(pair, next_ref[...])
    outer_at = [lanes_ref[32 + 8 * k : 40 + 8 * k, : 2 * LANES] for k in range(4)]
    kind = outer_at[1]
    from_pair = jnp.where(outer_at[2] != 0, 1 - odd, odd) != 0
    east = flags_in(flags_ref, 2)[0]
    strip_at = jnp.where(kind == 3, 1 - east, east)
    far_at = strip_at ^ (1 - odd) if block_cols == 1 else strip_at
    strip_at, far_at = (jnp.where(kind > 1, at, 0) for at in (strip_at, far_at))
    place = jnp.where(
        from_pair,
        outer_at[0] + (RING + 1) * RING * strip_at,
        jnp.where(outer_at[3] < 0, -1, outer_at[3] + RING * RING * far_at),
    )
    outer = picked(around, as_one_hot(jnp.where(kind == 0, -1, place), 2 * LANES))
    table = table_ref[...].astype(bf16)
    tiles = (None, low_ref, centre_ref, high_ref, None)
    count = len(tiles)
    masks = [lanes_ref[24:32, k * LANES : (k + 1) * LANES] for k in range(count)]
    closed_above = jnp.where(block_y == BY - 1, masks[-2][1:2], 0) != 0
    closed_below = jnp.where(block_y == 0, masks[1][2:3], 0) != 0
    first_row = jnp.where(odd == 0, masks[0][4:5], 0) != 0
    last_row = jnp.where(odd != 0, masks[-1][5:6], 0) != 0
    outer_used = first_sums(
        table,
        weight_ref[...],
        [outer[k * NODES : (k + 1) * NODES] for k in range(ARRAYS)],
        [outer[ROWS + c * NP : ROWS + (c + 1) * NP] for c in range(4)],
        beside(masks[0][0:1], masks[-1][0:1]) != 0,
    )

    def shifted(parts, by, ring):
        turned = [pltpu.roll(part, -by % LANES, 1) for part in parts]
        size = len(parts)
        step = 1 if by > 0 else -1
        others = [(k + step) % size if ring else min(max(k + step, 0), size - 1) for k in range(size)]
        from_other = lane >= LANES - by if by > 0 else lane < -by
        return [jnp.where(from_other, turned[others[k]], turned[k]) for k in range(size)]

    def put_x_sums(groups, components):
        slots = [k for group in groups for k in group]
        ring = len(slots) < count
        per_tile = [
            [part[:, n * LANES : (n + 1) * LANES] for part in parts]
            for group, parts in zip(groups, components)
            for n in range(len(group))
        ]
        for c in range(3):
            parts = [tile[c] for tile in per_tile]
            west = [part[:NP] for part in parts]
            east = [part[NODES - NP :] for part in parts]
            at_east, at_west = shifted(west, 1, ring), shifted(east, -1, ring)
            for n, k in enumerate(slots):
                sums[k, c * NODES : c * NODES + NP] = west[n] + at_west[n]
                sums[k, c * NODES + NP : (c + 1) * NODES - NP] = parts[n][NP : NODES - NP]
                sums[k, (c + 1) * NODES - NP : (c + 1) * NODES] = east[n] + at_east[n]

    def edge_y(components, slots, rows=None):
        ring = len(slots) < count
        south_at = pl.ds(0, components * NP, stride=NP)
        north_at = pl.ds(NP - 1, components * NP, stride=NP)
        south = [sums[k, south_at] for k in slots]
        north = [sums[k, north_at] for k in slots]
        at_north, at_south = shifted(south, PITCH, ring), shifted(north, -PITCH, ring)
        for n, k in enumerate(slots):
            if k == count - 2:
                at_north[n] = jnp.where(closed_above, 0.0, at_north[n])
            if k == 1:
                at_south[n] = jnp.where(closed_below, 0.0, at_south[n])
        if rows is not None:
            at_south[0] = jnp.where(first_row, rows[0], at_south[0])
            at_north[-1] = jnp.where(last_row, rows[1], at_north[-1])
        for n, k in enumerate(slots):
            sums[k, south_at] = south[n] + at_south[n]
            sums[k, north_at] = north[n] + at_north[n]

    node = lax.broadcasted_iota(i32, (1, NP, 1), 1)
    rows = []
    for rim in (outer[ALL_ROWS:, :LANES], outer[ALL_ROWS:, LANES:]):
        east = pltpu.roll(rim, LANES - 1, 1).reshape(4, NP, LANES)
        west = pltpu.roll(rim, 1, 1).reshape(4, NP, LANES)
        rim = (
            rim.reshape(4, NP, LANES)
            + jnp.where(node == NP - 1, pltpu.roll(east, NP - 1, 1), 0.0)
            + jnp.where(node == 0, pltpu.roll(west, 1, 1), 0.0)
        )
        rows.append(rim.reshape(EDGE_ROWS, LANES))

    every = tuple(range(count))
    groups = (every[0:2], every[2:4], every[4:])

    def tile_part(k, n):
        if tiles[k] is None:
            return outer_used[n][:, :LANES] if k == 0 else outer_used[n][:, LANES:]
        return tiles[k][n * NODES : (n + 1) * NODES]

    def part_of(group, n):
        return jnp.concatenate([tile_part(k, n) for k in group], 1)

    def summed(group, c):
        return jnp.concatenate([sums[k, c * NODES : (c + 1) * NODES] for k in group], 1)

    def average(group, per_mass):
        return [summed(group, c) * per_mass for c in range(3)]

    def laplace(s):
        return [
            dot(table[4 * NODES :, : 3 * NODES], jnp.concatenate(high_low_high(part), 0))
            for part in s
        ]

    start = [[part_of(group, n) for n in range(3)] for group in groups]
    fixed = [[part_of(group, n) for n in range(3, 6)] for group in groups]
    for k in every:
        for c in range(4):
            sums[k, c * NODES : (c + 1) * NODES] = tile_part(k, 7 + c)
    edge_y(4, every, rows)
    per_mass = [1.0 / summed(group, 3) for group in groups]
    one = []
    for n, group in enumerate(groups):
        change = average(group, per_mass[n])
        one.append([s + time_step * c for s, c in zip(start[n], change)])
    put_x_sums(groups, [mass_tendency(table, *s, *f) for s, f in zip(one, fixed)])
    edge_y(3, every)
    two = []
    for n, group in enumerate(groups):
        change = average(group, per_mass[n])
        two.append(
            [0.75 * s + 0.25 * (o + time_step * c) for s, o, c in zip(start[n], one[n], change)]
        )
    put_x_sums(groups, [mass_tendency(table, *s, *f) for s, f in zip(two, fixed)])
    edge_y(3, every)

    def regrouped(per_group):
        (outer_low, high_above) = per_group[0], per_group[1]
        below, low = outer_low[:, :LANES], outer_low[:, LANES:]
        centre, high = high_above[:, :LANES], high_above[:, LANES:]
        near = jnp.where(lane < LANES // 2, per_group[2], below)
        return [beside(low, centre), beside(high, near)]

    def of_groups(values):
        return [list(parts) for parts in zip(*(regrouped(part) for part in zip(*values)))]

    for c in range(3):
        rows_at = slice(c * NODES, (c + 1) * NODES)
        sums[count - 1, rows_at] = jnp.where(
            lane < LANES // 2, sums[count - 1, rows_at], sums[0, rows_at]
        )
    slots = every[1:]
    groups = (slots[0:2], slots[2:4])
    start, two = of_groups(start), of_groups(two)
    tide = regrouped([part_of(every[0:2], 6), part_of(every[2:4], 6), part_of(every[4:], 6)])
    per_mass = regrouped(per_mass)
    three = []
    for n, group in enumerate(groups):
        change = average(group, per_mass[n])
        now = [
            s / 3.0 + 2.0 / 3.0 * (o + time_step * c)
            for s, o, c in zip(start[n], two[n], change)
        ]
        now[0] = now[0] + tide[n]
        three.append(now)
    put_x_sums(groups, [laplace(s) for s in three])
    edge_y(3, slots)
    change = [average(group, per_mass[n]) for n, group in enumerate(groups)]
    put_x_sums(groups, [laplace(s) for s in change])
    edge_y(3, slots)
    stepped = []
    for n, group in enumerate(groups):
        change = average(group, per_mass[n])
        now = [s - time_step * hyper_coeff * b for s, b in zip(three[n], change)]
        stepped.append(jnp.concatenate(now, 0))
    stepped = jnp.concatenate(stepped, 1)[:, :MID]
    own = lanes_ref[27:28, LANES : LANES + MID] != 0
    stored = picked(jnp.where(own, stepped, 0.0), hot_ref[...])
    out_ref[...] = stored.reshape(out_ref.shape)


def on_device(fields, jacobian, water_depth, coriolis, tide_height, slot_of, seam_rows):
    block_cols = lax.axis_size("blk") // BY
    table, weight, edge_table, lanes = map(jnp.asarray, (*operator_table(), lane_tables()))
    vmem = pl.BlockSpec(memory_space=pltpu.VMEM)
    hbm = pl.BlockSpec(memory_space=pltpu.HBM)
    params = pltpu.CompilerParams(vmem_limit_bytes=48 * 2**20)
    held = (fields, jacobian, water_depth, coriolis, tide_height)

    def call(kernel, ins, outs, cost, scratch=(), name=None):
        return pl.pallas_call(
            kernel,
            out_shape=[jax.ShapeDtypeStruct(*out) for out in outs],
            in_specs=[spec for spec, value in ins],
            out_specs=[vmem] * len(outs),
            scratch_shapes=list(scratch),
            compiler_params=params,
            cost_estimate=pl.CostEstimate(
                flops=cost, bytes_accessed=2 * 2**20, transcendentals=0
            ),
            name=name,
        )(
            *[
                pltpu.with_memory_space_constraint(value, pltpu.HBM) if spec is hbm else value
                for spec, value in ins
            ]
        )

    strip = ((HALF_ROWS, LANES), f32)
    def room(values, spaces=None):
        spaces = spaces or [pltpu.VMEM] * len(values)
        buffers = [space(x.shape, x.dtype) for space, x in zip(spaces, values)]
        return buffers + [pltpu.SemaphoreType.DMA((len(values),))]

    needed = (seam_rows, slot_of, *held, edge_table)
    corner = ((CORNER_ROWS, LANES), f32)
    scratch = [pltpu.VMEM((1, 4 * NODES, LANES), f32)]
    first, then, stored, flags = call(
        functools.partial(strips_kernel, block_cols),
        [(hbm, x) for x in needed],
        [strip, strip, ((ROWS, ELEMENTS), f32), ((8, LANES), i32)],
        10**8,
        scratch=room(needed, [pltpu.SMEM] + [pltpu.VMEM] * (len(needed) - 1)),
        name="strips",
    )
    to_next, far0, far1, to_pair = call(
        functools.partial(rows_kernel, block_cols),
        [(vmem, x) for x in (flags, stored, first, then, table, weight)],
        [strip, corner, corner, ((ROWS, LANES), f32)],
        10**8,
        scratch=scratch,
        name="rows",
    )
    span = block_cols * BY
    both = ("face", "blk")
    places = [(f, x, y) for f in range(2) for x in range(block_cols) for y in range(BY)]

    def rank(face, block_x, block_y):
        return face * span + block_x * BY + block_y

    def same(y):
        return y

    def in_pair(y):
        return y ^ 1

    def next_pair(y):
        other = y + 1 if y % 2 else y - 1
        return other if 0 <= other < BY else y

    def swapped(value, partner):
        pairs = [
            (rank(f, x, y), rank(f if partner(y) != y else 1 - f, x, partner(y)))
            for f, x, y in places
        ]
        return lax.ppermute(value, both, pairs)

    def across(value0, value1, partner):
        last = block_cols - 1

        def aligned(y):
            return partner is same or partner(y) != y

        straight = {
            (f, x, y): (f, x + 1, partner(y)) if x < last else (1 - f, 0, partner(y))
            for f, x, y in places
        }
        turned = {
            (f, last, y): (1 - f, 0, BY - 1 - partner(y) if aligned(y) else y)
            for f in range(2)
            for y in range(BY)
        }

        def eastward(value, pairs):
            return lax.ppermute(value, both, [(rank(*a), rank(*b)) for a, b in pairs.items()])

        def westward(value, pairs):
            return lax.ppermute(value, both, [(rank(*b), rank(*a)) for a, b in pairs.items()])

        if block_cols == 1:
            return eastward(value0, straight), eastward(value1, turned)
        flipped = (seam_rows[:, 1] - seam_rows[:, 0]) % seam_rows.shape[1] != 1
        face = lax.axis_index("face")
        block_x = lax.axis_index("blk") // BY
        return (
            jnp.where(
                (block_x == last) & flipped[face],
                westward(value1, turned),
                westward(value1, straight),
            ),
            jnp.where(
                (block_x == 0) & flipped[1 - face],
                eastward(value0, turned),
                eastward(value0, straight),
            ),
        )

    if block_cols == 1:
        halos = []
        for value, mirrored in ((first, mirrored_first), (then, lambda y: not mirrored_first(y))):
            pairs = [
                (rank(f, x, y), rank(1 - f, x, BY - 1 - y if mirrored(y) else y))
                for f, x, y in places
            ]
            halos.append(lax.ppermute(value, both, pairs))
        halo0, halo1 = halos
    else:
        halo0, halo1 = across(first, then, same)
    far0, far1 = across(far0, far1, next_pair)
    from_next = swapped(to_next, next_pair)
    own, hot = call(
        own_kernel,
        [(vmem, x) for x in (flags, stored, lanes)],
        [((ROWS, MID), f32), ((MID, ELEMENTS), bf16)],
        10**8,
        name="own",
    )
    (to_pair,) = call(
        functools.partial(corners_kernel, block_cols),
        [(vmem, x) for x in (flags, halo0, halo1, to_pair, hot)],
        [((ALL_ROWS, LANES), f32)],
        10**8,
        name="corners",
    )
    from_pair = swapped(to_pair, in_pair)
    tile = ((11 * NODES, LANES), f32)
    low, centre, high = call(
        functools.partial(middle_kernel, block_cols),
        [(vmem, x) for x in (flags, halo0, halo1, own, lanes, table, weight)],
        [tile, tile, tile],
        10**8,
        name="middle",
    )
    (from_next,) = call(
        functools.partial(far_kernel, block_cols),
        [(vmem, x) for x in (flags, far1, far0, from_next, low)],
        [((RIM_ROWS, LANES), f32)],
        10**11,
        name="far",
    )
    (stepped,) = call(
        functools.partial(steps_kernel, block_cols),
        [
            (vmem, x)
            for x in (
                flags, from_pair, from_next, low, centre, high, hot, table, weight, lanes
            )
        ],
        [(fields.shape, f32)],
        10**8,
        scratch=[pltpu.VMEM((EXT // LANES, 4 * NODES, LANES), f32)],
        name="steps",
    )
    return stepped


def solution(mesh):
    return jax.shard_map(
        on_device,
        mesh=mesh,
        in_specs=(
            P(None, None, None, ("face", "blk")),
            P(None, None, ("face", "blk")),
            P(None, None, ("face", "blk")),
            P(None, None, ("face", "blk")),
            P(None, None, ("face", "blk")),
            P(("face", "blk"), None),
            P(),
        ),
        out_specs=P(None, None, None, ("face", "blk")),
        check_vma=False,
    )
```
